32 devices in a mesh: dp: 8 (over y, x, core), fsdp: 4 (over z).
Axes of the slice: x: 2, y: 2, z: 4, core: 2. Of those that a mesh axis runs over, the one named last changes fastest.
Arguments:
- frames: bfloat16 [49152, 512], P(('dp', 'fsdp'))
- seq_lengths: int32 [32, 3], P(('dp', 'fsdp')), may hold values from 512 to 1536, as said below
- seq_offsets: int32 [32, 3], P(('dp', 'fsdp')), may hold values from 0 to 1024, as said below
- seq_counts: int32 [32], P(('dp', 'fsdp')), may hold values from 1 to 3, as said below
- ffn_up: bfloat16 [2, 512, 2048], P(None, ('dp', 'fsdp')), may hold values from -0.25 to 0.25
- ffn_down: bfloat16 [2, 2048, 512], P(None, ('dp', 'fsdp')), may hold values from -0.125 to 0.125
- ffn_bias_up: bfloat16 [2, 2048], P(None, ('dp', 'fsdp')), may hold values from -3 to 3
- mix_in: bfloat16 [512, 1024], P(('dp', 'fsdp')), may hold values from -0.25 to 0.25
- mix_out: bfloat16 [512, 512], P(('dp', 'fsdp')), may hold values from -0.25 to 0.25
- conv_in: bfloat16 [512, 1024], P(('dp', 'fsdp')), may hold values from -0.25 to 0.25
- conv_out: bfloat16 [512, 512], P(('dp', 'fsdp')), may hold values from -0.25 to 0.25
- conv_out_bias: bfloat16 [512], P(('dp', 'fsdp')), may hold values from -3 to 3
- ssm_rate: bfloat16 [32, 512], P(None, ('dp', 'fsdp')), may hold values from -8 to -3
- ssm_map: bfloat16 [2, 32, 512], P(None, None, ('dp', 'fsdp')), may hold values from -4 to 4
- conv_kernel: bfloat16 [15, 512], P(None, ('dp', 'fsdp')), may hold values from -1.5 to 1.5
- gains: bfloat16 [6, 512], P(None, ('dp', 'fsdp')), may hold values from 0.099609375 to 1.8984375
- shifts: bfloat16 [12, 512], P(None, ('dp', 'fsdp')), may hold values from -3 to 3
- cotangent: bfloat16 [49152, 512], P(('dp', 'fsdp')), may hold values from -6 to 6
Outputs:
- output: bfloat16 [49152, 512], P(('dp', 'fsdp'))
- frames_grad: float32 [49152, 512], P(('dp', 'fsdp'))
- ffn_up_grad: float32 [2, 512, 2048], P(None, ('dp', 'fsdp'))
- ffn_down_grad: float32 [2, 2048, 512], P(None, ('dp', 'fsdp'))
- ffn_bias_up_grad: float32 [2, 2048], P(None, ('dp', 'fsdp'))
- mix_in_grad: float32 [512, 1024], P(('dp', 'fsdp'))
- mix_out_grad: float32 [512, 512], P(('dp', 'fsdp'))
- conv_in_grad: float32 [512, 1024], P(('dp', 'fsdp'))
- conv_out_grad: float32 [512, 512], P(('dp', 'fsdp'))
- conv_out_bias_grad: float32 [512], P(('dp', 'fsdp'))
- ssm_rate_grad: float32 [32, 512], P(None, ('dp', 'fsdp'))
- ssm_map_grad: float32 [2, 32, 512], P(None, None, ('dp', 'fsdp'))
- conv_kernel_grad: float32 [15, 512], P(None, ('dp', 'fsdp'))
- gains_grad: float32 [6, 512], P(None, ('dp', 'fsdp'))
- shifts_grad: float32 [12, 512], P(None, ('dp', 'fsdp'))
The draws below stay inside these ranges and needn't reach their ends.
Inputs may be any that keep to these rules, and one draw needn't show every extreme that they name: `seq_lengths`: each device's lengths are multiples of 512, and those of its first seq_counts slots sum to 1536; slots at or past seq_counts repeat the last used slot. Some device holds one sequence of 1536 frames and some device three sequences. `seq_offsets`: each used slot's offset is the sum of the lengths of the device's earlier slots; slots at or past seq_counts repeat the last used slot. `seq_counts`: the number of used slots of each device.
All inputs are finite; a program needn't handle non-finite values.
Results may differ from the reference program's by a relative error of at most 0.013.
Values may be sent and summed in bfloat16 or wider, within the bound.
A program may use at most 320 MiB of HBM per device.

```python
import math
from functools import partial
import jax
import jax.numpy as jnp
import numpy as np
from jax import lax

D = 512
FF = 2048
STATE = 32
KW = 15
BLOCK = 32
SEG = 512
TOK_DEV = 1536
TOKENS = 49152
N_DP = 8
N_FSDP = 4


LENGTH_TABLE = np.array([[3, 3, 3], [2, 1, 1], [1, 2, 2], [1, 1, 1]], dtype=np.int32)


OFFSET_TABLE = np.array([[0, 0, 0], [0, 2, 2], [0, 1, 1], [0, 1, 2]], dtype=np.int32)


COUNT_TABLE = np.array([1, 2, 2, 3], dtype=np.int32)


def pattern_draw(key):
    places = jnp.arange(N_DP * N_FSDP, dtype=jnp.int32)
    chosen = jax.random.randint(jax.random.fold_in(key, 17), (N_DP * N_FSDP,), 0, 4, dtype=jnp.int32)
    chosen = jnp.where(places == 0, 0, jnp.where(places == 1, 3, chosen))
    return chosen.astype(jnp.int32)


def draw_seq_lengths(key, part):
    return (jnp.asarray(LENGTH_TABLE)[pattern_draw(key)] * SEG).astype(jnp.int32)


def draw_seq_offsets(key, part):
    return (jnp.asarray(OFFSET_TABLE)[pattern_draw(key)] * SEG).astype(jnp.int32)


def draw_seq_counts(key, part):
    return jnp.asarray(COUNT_TABLE)[pattern_draw(key)].astype(jnp.int32)


def draw_frames(key, part):
    noise_key = jax.random.fold_in(key, 23)
    common_key = jax.random.fold_in(key, 29)
    rows = TOK_DEV * N_DP * N_FSDP
    device_index = (jnp.arange(rows, dtype=jnp.int32) // TOK_DEV).astype(jnp.float32)
    ramp = device_index / (N_DP * N_FSDP - 1)
    common = jax.random.normal(common_key, (D,), jnp.float32)
    noise = jax.random.normal(noise_key, (rows, D), jnp.float32)
    weight = 0.5 * jnp.exp(ramp * math.log(6.0))
    return (noise + weight[:, None] * common[None, :]).astype(jnp.bfloat16)


def block_levels(key, dims, split, low, top_value):
    level, own = 1.0, jax.random.fold_in(key, 6)
    for axis_at, blocks in split:
        steps = jnp.exp(jax.random.uniform(jax.random.fold_in(own, axis_at), (blocks,), jnp.float32, low / len(split), top_value / len(split)))
        level = level * jnp.repeat(steps, dims[axis_at] // blocks).reshape([-1 if axis == axis_at else 1 for axis in range(len(dims))])
    return level


def normal_values(own_key, shape, scale, limit, cuts=(), held_as=jnp.bfloat16):
    entries = jax.random.normal(own_key, shape, jnp.float32) * scale
    if len(cuts) > 0:
        entries = block_levels(own_key, shape, cuts, -0.22, 0.18) * entries
    return jnp.clip(entries, min=-limit, max=limit).astype(held_as)


def setup_inputs(seed: int = 0) -> dict:
    splits = jax.random.split(jax.random.key(seed), 19)
    return {
        "frames": draw_frames(jax.random.fold_in(splits[18], 71), 0),
        "seq_lengths": draw_seq_lengths(jax.random.fold_in(splits[18], 71), 0),
        "seq_offsets": draw_seq_offsets(jax.random.fold_in(splits[18], 71), 0),
        "seq_counts": draw_seq_counts(jax.random.fold_in(splits[18], 71), 0),
        "ffn_up": normal_values(splits[4], (2, D, FF), D ** -0.5, 0.25, ((1, 32),)),
        "ffn_down": normal_values(splits[5], (2, FF, D), FF ** -0.5, 0.125, ((1, 32),)),
        "ffn_bias_up": normal_values(splits[6], (2, FF), 0.5, 3.0, ((1, 32),)),
        "mix_in": normal_values(splits[7], (D, 2 * D), D ** -0.5, 0.25, ((0, 32),)),
        "mix_out": normal_values(splits[8], (D, D), D ** -0.5, 0.25, ((0, 32),)),
        "conv_in": normal_values(splits[9], (D, 2 * D), D ** -0.5, 0.25, ((0, 32),)),
        "conv_out": normal_values(splits[10], (D, D), D ** -0.5, 0.25, ((0, 32),)),
        "conv_out_bias": normal_values(splits[11], (D,), 0.5, 3.0, ((0, 32),)),
        "ssm_rate": jnp.clip(-8.0 + 5.0 * jax.random.uniform(splits[12], (STATE, D), jnp.float32) ** block_levels(splits[12], (STATE, D), ((1, 32),), -0.2, 0.2), -8.0, -3.0).astype(jnp.bfloat16),
        "ssm_map": normal_values(splits[13], (2, STATE, D), (STATE ** -0.25), 4.0, ((2, 32),)),
        "conv_kernel": normal_values(splits[14], (KW, D), KW ** -0.5, 1.5, ((1, 32),)),
        "gains": jnp.clip(1.0 + 0.18 * jax.random.normal(splits[15], (6, D), jnp.float32), 0.099609375, 1.8984375).astype(jnp.bfloat16),
        "shifts": normal_values(splits[16], (12, D), 0.5, 3.0, ((1, 32),)),
        "cotangent": normal_values(splits[17], (TOKENS, D), 1.0, 6.0, ((0, 32),)),
    }


@jax.custom_vjp
def low(v):
    return lax.optimization_barrier(v.astype(jnp.bfloat16)).astype(jnp.float32)

@jax.custom_vjp
def low_back(v):
    return v

def low_keep(v):
    return (low(v), None)

def low_pass(kept, grad):
    return (grad,)

def back_keep(v):
    return (v, None)

def back_low(kept, grad):
    return (low(grad),)
low.defvjp(low_keep, low_pass)
low_back.defvjp(back_keep, back_low)
EPSILON = 1e-05
HIGHEST = lax.Precision.HIGHEST

def layer_norm(values, gain_row, shift_row):
    average = lax.optimization_barrier(jnp.mean(values, axis=-1, keepdims=True))
    centered = values - average
    variance = lax.optimization_barrier(jnp.mean(centered * centered, axis=-1, keepdims=True))
    return centered * lax.rsqrt(variance + EPSILON) * gain_row + shift_row

def swish(values):
    return values * jax.nn.sigmoid(values)

def combine(earlier, latter):
    return (earlier[0] * latter[0], latter[0] * earlier[1] + latter[1])

def state_space(driving, log_rate, coupling, skip_gain, carry_on):
    frames_dev, channels = driving.shape
    blocks = frames_dev // BLOCK
    log_decay = -jnp.exp(log_rate)
    input_map = coupling[0] * jnp.sqrt(-jnp.expm1(2.0 * log_decay))
    output_map = coupling[1]
    step_index = jnp.arange(BLOCK, dtype=jnp.int32)
    step_float = step_index.astype(jnp.float32)
    kernel = lax.optimization_barrier(jnp.sum(jnp.exp(step_float[:, None, None] * log_decay[None]) * (input_map * output_map)[None], axis=1))
    lag_steps = step_index[:, None] - step_index[None, :]
    select = (lag_steps[:, :, None] == step_index[None, None, :]).astype(jnp.float32)
    toeplitz = jnp.einsum('tsl,lc->tsc', select, kernel, precision=HIGHEST)
    pieces = driving.reshape(blocks, BLOCK, channels)
    within_block = jnp.einsum('tsc,bsc->btc', toeplitz, pieces, precision=HIGHEST)
    tail_weights = jnp.exp((BLOCK - 1.0 - step_float)[:, None, None] * log_decay[None]) * input_map[None]
    end_states = jnp.einsum('snc,bsc->bnc', tail_weights, pieces, precision=HIGHEST)
    block_links = carry_on[:, None, None] * jnp.exp(BLOCK * log_decay)[None]
    totals = lax.associative_scan(combine, (block_links, end_states))[1]
    incoming = carry_on[:, None, None] * jnp.concatenate([jnp.zeros_like(totals[:1]), totals[:-1]], axis=0)
    lead_weights = jnp.exp((step_float + 1.0)[:, None, None] * log_decay[None]) * output_map[None]
    from_before = jnp.einsum('tnc,bnc->btc', lead_weights, incoming, precision=HIGHEST)
    return (within_block + from_before).reshape(frames_dev, channels) + skip_gain * driving

def mixer(carry_on, mixed_in, log_rate, coupling, skip_gain):
    channels = mixed_in.shape[1] // 2
    driving = mixed_in[:, :channels]
    gate_in = mixed_in[:, channels:]
    return state_space(driving, log_rate, coupling, skip_gain, carry_on) * swish(gate_in)

def glu_conv(position, extent, projected, conv_taps):
    channels = projected.shape[1] // 2
    glu_out = projected[:, :channels] * jax.nn.sigmoid(projected[:, channels:])
    half_span = conv_taps.shape[0] // 2
    padded = jnp.pad(glu_out, ((half_span, half_span), (0, 0)))
    result = jnp.zeros_like(glu_out)
    for tap_index in range(conv_taps.shape[0]):
        source = position + (tap_index - half_span)
        inside = ((source >= 0) & (source < extent)).astype(jnp.float32)[:, None]
        result = result + conv_taps[tap_index][None, :] * padded[tap_index:tap_index + glu_out.shape[0]] * inside
    return result

def layout(lengths, offsets, used_slots, frames_dev):
    slot_index = jnp.arange(lengths.shape[0], dtype=jnp.int32)[None, :]
    frame_index = jnp.arange(frames_dev, dtype=jnp.int32)[:, None]
    inside = ((frame_index >= offsets[None, :]) & (frame_index < offsets[None, :] + lengths[None, :]) & (slot_index < used_slots)).astype(jnp.int32)
    position = lax.optimization_barrier(jnp.sum(inside * (frame_index - offsets[None, :]), axis=1))
    extent = lax.optimization_barrier(jnp.sum(inside * lengths[None, :], axis=1))
    starts = position.reshape(frames_dev // BLOCK, BLOCK)[:, 0]
    carry_on = (starts > 0).astype(jnp.float32)
    return (position, extent, carry_on)

def matmul(left, right):
    return jnp.dot(left, right, precision=HIGHEST, preferred_element_type=jnp.float32)

def feed_forward(values, params, index):
    gains = params[10]
    shifts = params[11]
    normed = layer_norm(values, gains[3 * index], shifts[3 * index])
    hidden = low_back(matmul(low(normed), params[0][index]) + params[2][index])
    branch = low_back(matmul(low(swish(hidden)), params[1][index]) + shifts[6 + index])
    return values + 0.5 * branch

def forward_one(params, values, position, extent, carry_on):
    gains = params[10]
    shifts = params[11]
    after_one = feed_forward(values, params, 0)
    normed_two = layer_norm(after_one, gains[1], shifts[1])
    mixed_in = low_back(matmul(low(normed_two), params[3]))
    gated_out = mixer(carry_on, mixed_in, params[7], params[8], shifts[11])
    after_two = after_one + low_back(matmul(low(gated_out), params[4]) + shifts[8])
    normed_three = layer_norm(after_two, gains[2], shifts[2])
    projected = low_back(matmul(low(normed_three), params[5]) + jnp.concatenate([shifts[9], shifts[10]]))
    return (after_two, glu_conv(position, extent, projected, params[9]))

def forward_two(params, after_two, normed_bn):
    conv_branch = low_back(matmul(low(swish(normed_bn)), params[6]) + params[12])
    after_four = feed_forward(after_two + conv_branch, params, 1)
    return layer_norm(after_four, params[10][4], params[11][4])

def whole_forward(inputs, params, position, extent, carry_on):
    places = position.shape[0]
    gains = params[10]
    shifts = params[11]

    def first_section(packed):
        return forward_one(params, packed[0], packed[1], packed[2], packed[3])

    def second_section(packed):
        return forward_two(params, packed[0], packed[1])
    grouped = inputs.reshape(places, inputs.shape[0] // places, inputs.shape[1])
    after_two, convolved = lax.map(jax.checkpoint(first_section), (grouped, position, extent, carry_on))
    center = lax.optimization_barrier(jnp.mean(convolved, axis=(0, 1)))
    deviation = convolved - center
    spread = lax.optimization_barrier(jnp.mean(deviation * deviation, axis=(0, 1)))
    normed_bn = deviation * lax.rsqrt(spread + EPSILON) * gains[5] + shifts[5]
    result = lax.map(jax.checkpoint(second_section), (after_two, normed_bn))
    return result.reshape(inputs.shape)

def reference(frames, seq_lengths, seq_offsets, seq_counts, ffn_up, ffn_down, ffn_bias_up, mix_in, mix_out, conv_in, conv_out, conv_out_bias, ssm_rate, ssm_map, conv_kernel, gains, shifts, cotangent):
    params = (ffn_up.astype(jnp.float32), ffn_down.astype(jnp.float32), ffn_bias_up.astype(jnp.float32), mix_in.astype(jnp.float32), mix_out.astype(jnp.float32), conv_in.astype(jnp.float32), conv_out.astype(jnp.float32), ssm_rate.astype(jnp.float32), ssm_map.astype(jnp.float32), conv_kernel.astype(jnp.float32), gains.astype(jnp.float32), shifts.astype(jnp.float32), conv_out_bias.astype(jnp.float32))
    position, extent, carry_on = jax.vmap(partial(layout, frames_dev=TOK_DEV))(seq_lengths, seq_offsets, seq_counts)
    inputs = frames.astype(jnp.float32)

    def forward_fn(values, weights):
        return whole_forward(values, weights, position, extent, carry_on)
    result, pullback = jax.vjp(forward_fn, inputs, params)
    frames_grad, weight_grads = pullback(cotangent.astype(jnp.float32))
    return (result.astype(jnp.bfloat16), frames_grad, weight_grads[0], weight_grads[1], weight_grads[2], weight_grads[3], weight_grads[4], weight_grads[5], weight_grads[6], weight_grads[12], weight_grads[7], weight_grads[8], weight_grads[9], weight_grads[10], weight_grads[11])
```

```python
import itertools
from functools import partial

import jax
import jax.numpy as jnp
from jax import lax
from jax.experimental import pallas as pl
from jax.experimental.pallas import tpu as pltpu
from jax.sharding import PartitionSpec as P

MESH = pl.DeviceIdType.MESH
BF16 = jnp.bfloat16
F32 = jnp.float32


def flip(index, bit):
    return index + bit * (1 - 2 * lax.rem(lax.div(index, bit), 2))


def flip_all(index, bits):
    for bit in bits:
        index = flip(index, bit)
    return index


def combos(bits):
    found = [()]
    for bit in bits:
        found = found + [entry + (bit,) for entry in found]
    return found


def plan_bits(n_dp):
    bits, bit = [], 2
    while bit < n_dp:
        bits.append(bit)
        bit *= 2
    return tuple(bits)


def greet(dp, fs, n_dp, n_fs):
    barrier = pltpu.get_barrier_semaphore()
    bits = (1,) + plan_bits(n_dp)
    for bit in bits:
        pl.semaphore_signal(barrier, inc=1, device_id=(flip(dp, bit), fs), device_id_type=MESH)
    for step in range(1, n_fs):
        pl.semaphore_signal(
            barrier, inc=1, device_id=(dp, lax.rem(fs + step, n_fs)), device_id_type=MESH
        )
    pl.semaphore_wait(barrier, len(bits) + n_fs - 1)


def gather_kernel(n_dp, n_fs, layers, *refs):
    n_in = len(layers)
    n_out = sum(layers)
    ins, outs = refs[:n_in], refs[n_in : n_in + n_out]
    send_sem, recv_sem, local_sem = refs[n_in + n_out :]
    sources = []
    for ref, count in zip(ins, layers):
        sources += [ref.at[layer] for layer in range(count)]
    dp, fs = lax.axis_index("dp"), lax.axis_index("fsdp")
    bits = plan_bits(n_dp)
    orders = (bits, bits[::-1])
    half = n_fs // 2
    greet(dp, fs, n_dp, n_fs)
    sends = []

    def remote(chunk, slot, src, dst, device):
        return pltpu.make_async_remote_copy(
            src_ref=src,
            dst_ref=dst,
            send_sem=send_sem.at[chunk, slot],
            recv_sem=recv_sem.at[chunk, slot],
            device_id=device,
            device_id_type=MESH,
        )

    def stages(chunk):
        src, out = sources[chunk], outs[chunk]
        mine = dp * n_fs + fs
        slots = itertools.count()

        def zone(where, part):
            if part is None:
                return out.at[pl.ds(where * n_fs, n_fs)]
            return out.at[pl.ds(where * n_fs + part * half, half)]

        steps = []
        z_slots = [next(slots) for _ in range(1, n_fs)]
        local = pltpu.make_async_copy(src, out.at[mine], local_sem.at[chunk])

        def start():
            local.start()
            for step in range(1, n_fs):
                to = (dp, lax.rem(fs + step, n_fs))
                copy = remote(chunk, z_slots[step - 1], src, out.at[mine], to)
                copy.start()
                sends.append(copy)

        steps.append(start)

        def wait_z():
            local.wait()
            for step in range(1, n_fs):
                origin = dp * n_fs + lax.rem(fs + n_fs - step, n_fs)
                remote(chunk, z_slots[step - 1], src, out.at[origin], (dp, fs)).wait_recv()

        waits = [wait_z]
        for depth in range(len(bits)):
            plan = []
            for part, order in enumerate(orders):
                for entry in combos(order[:depth]):
                    plan.append((next(slots), part, order[depth], entry))

            def go(plan=plan, before=tuple(waits)):
                for wait in before:
                    wait()
                for slot, part, bit, entry in plan:
                    view = zone(flip_all(dp, entry), part)
                    copy = remote(chunk, slot, view, view, (flip(dp, bit), fs))
                    copy.start()
                    sends.append(copy)

            def arrive(plan=plan):
                for slot, part, bit, entry in plan:
                    view = zone(flip_all(flip(dp, bit), entry), part)
                    remote(chunk, slot, view, view, (flip(dp, bit), fs)).wait_recv()

            steps.append(go)
            waits = [arrive]
        last = [(next(slots), entry) for entry in combos(bits)]

        def cross(before=tuple(waits)):
            for wait in before:
                wait()
            for slot, entry in last:
                view = zone(flip_all(dp, entry), None)
                copy = remote(chunk, slot, view, view, (flip(dp, 1), fs))
                copy.start()
                sends.append(copy)

        def finish():
            for slot, entry in last:
                view = zone(flip_all(flip(dp, 1), entry), None)
                remote(chunk, slot, view, view, (flip(dp, 1), fs)).wait_recv()

        steps += [cross, finish]
        return steps

    plans = [stages(chunk) for chunk in range(n_out)]
    depth = len(plans[0])
    for wave in range(n_out + depth - 1):
        for chunk in range(n_out):
            stage = wave - chunk
            if 0 <= stage < depth:
                plans[chunk][stage]()
    for copy in sends:
        copy.wait_send()


def slot_count(n_dp, n_fs):
    nb = len(plan_bits(n_dp))
    return n_fs - 1 + 2 * (2**nb - 1) + 2**nb


def gather_all(n_dp, n_fs, arrays, collective_id):
    layers = tuple(a.shape[0] for a in arrays)
    outs = []
    for a in arrays:
        outs += [jax.ShapeDtypeStruct((n_dp * n_fs,) + a.shape[1:], a.dtype)] * a.shape[0]
    count = slot_count(n_dp, n_fs)
    return pl.pallas_call(
        partial(gather_kernel, n_dp, n_fs, layers),
        out_shape=outs,
        in_specs=[pl.BlockSpec(memory_space=pltpu.HBM)] * len(arrays),
        out_specs=[pl.BlockSpec(memory_space=pltpu.HBM)] * len(outs),
        scratch_shapes=[
            pltpu.SemaphoreType.DMA((len(outs), count)),
            pltpu.SemaphoreType.DMA((len(outs), count)),
            pltpu.SemaphoreType.DMA((len(outs),)),
        ],
        compiler_params=pltpu.CompilerParams(collective_id=collective_id, has_side_effects=True),
        name="gather_parameters",
    )(*arrays)


def scatter_kernel(n_dp, n_fs, n_chunks, *refs):
    ins, outs = refs[:n_chunks], refs[n_chunks : 2 * n_chunks]
    per = 4
    scratch = refs[2 * n_chunks : 2 * n_chunks + per * n_chunks]
    send_sem, recv_sem, local_sem = refs[2 * n_chunks + per * n_chunks :]
    dp, fs = lax.axis_index("dp"), lax.axis_index("fsdp")
    bits = plan_bits(n_dp)
    nb = len(bits)
    orders = (bits[::-1], bits)
    half = n_fs // 2
    index = {entry: at for at, entry in enumerate(combos(bits))}
    greet(dp, fs, n_dp, n_fs)
    sends = []

    def remote(chunk, slot, src, dst, device):
        return pltpu.make_async_remote_copy(
            src_ref=src,
            dst_ref=dst,
            send_sem=send_sem.at[chunk, slot],
            recv_sem=recv_sem.at[chunk, slot],
            device_id=device,
            device_id_type=MESH,
        )

    def add_into(kept, other):
        count = kept.shape[0]

        def body(at, _):
            total = kept[at].astype(F32) + other[at].astype(F32)
            kept[at] = total.astype(BF16)
            return 0

        lax.fori_loop(0, count, body, 0)

    def stages(chunk):
        src, out = ins[chunk], outs[chunk]
        first, own, later, last = scratch[per * chunk : per * chunk + per]
        slots = itertools.count()
        pieces = [(next(slots), entry, index[entry]) for entry in combos(bits)]
        loads = [
            pltpu.make_async_copy(
                src.at[pl.ds(flip_all(dp, entry) * n_fs, n_fs)], own.at[at], local_sem.at[chunk, at]
            )
            for _, entry, at in pieces
        ]

        def start():
            for slot, entry, at in pieces:
                view = src.at[pl.ds(flip_all(flip(dp, 1), entry) * n_fs, n_fs)]
                copy = remote(chunk, slot, view, first.at[at], (flip(dp, 1), fs))
                copy.start()
                sends.append(copy)
            for load in loads:
                load.start()

        def fold_first():
            for load, (slot, entry, at) in zip(loads, pieces):
                load.wait()
                remote(chunk, slot, first.at[at], first.at[at], (flip(dp, 1), fs)).wait_recv()
                add_into(own.at[at], first.at[at])

        steps = [start]
        folds = [fold_first]
        used = 0
        for depth in range(nb):
            plan = []
            for part, order in enumerate(orders):
                bit, gone = order[depth], order[:depth]
                keep = [e for e in combos(bits) if not (set(e) & set(gone)) and bit not in e]
                for entry in keep:
                    away = tuple(sorted(entry + (bit,)))
                    plan.append((next(slots), part, bit, index[away], index[entry], used))
                    used += 1

            def go(plan=plan, before=tuple(folds)):
                for fold in before:
                    fold()
                for slot, part, bit, away, kept, place in plan:
                    copy = remote(
                        chunk,
                        slot,
                        own.at[away, pl.ds(part * half, half)],
                        later.at[place],
                        (flip(dp, bit), fs),
                    )
                    copy.start()
                    sends.append(copy)

            def fold(plan=plan):
                for slot, part, bit, away, kept, place in plan:
                    view = later.at[place]
                    remote(chunk, slot, view, view, (flip(dp, bit), fs)).wait_recv()
                    add_into(own.at[kept, pl.ds(part * half, half)], view)

            steps.append(go)
            folds = [fold]
        z_slots = [next(slots) for _ in range(1, n_fs)]

        def cross(before=tuple(folds)):
            for fold in before:
                fold()
            for step in range(1, n_fs):
                to = lax.rem(fs + step, n_fs)
                copy = remote(chunk, z_slots[step - 1], own.at[0, to], last.at[step - 1], (dp, to))
                copy.start()
                sends.append(copy)

        def finish():
            total = own[0, fs].astype(F32)
            for step in range(1, n_fs):
                view = last.at[step - 1]
                remote(chunk, z_slots[step - 1], view, view, (dp, fs)).wait_recv()
                total = total + last[step - 1].astype(F32)
            out[...] = total

        steps += [cross, finish]
        return steps

    plans = [stages(chunk) for chunk in range(n_chunks)]
    depth = len(plans[0])
    for wave in range(n_chunks + depth - 1):
        for chunk in range(n_chunks):
            stage = wave - chunk
            if 0 <= stage < depth:
                plans[chunk][stage]()
    for copy in sends:
        copy.wait_send()


def scatter_all(n_dp, n_fs, arrays, collective_id):
    nb = len(plan_bits(n_dp))
    pieces = 2**nb
    scratch = []
    for a in arrays:
        tail = a.shape[1:]
        scratch += [
            pltpu.VMEM((pieces, n_fs) + tail, BF16),
            pltpu.VMEM((pieces, n_fs) + tail, BF16),
            pltpu.VMEM((2 * (pieces - 1), n_fs // 2) + tail, BF16),
            pltpu.VMEM((n_fs - 1,) + tail, BF16),
        ]
    count = slot_count(n_dp, n_fs)
    n = len(arrays)
    return pl.pallas_call(
        partial(scatter_kernel, n_dp, n_fs, n),
        out_shape=[jax.ShapeDtypeStruct(a.shape[1:], F32) for a in arrays],
        in_specs=[pl.BlockSpec(memory_space=pltpu.HBM)] * n,
        out_specs=[pl.BlockSpec(memory_space=pltpu.VMEM)] * n,
        scratch_shapes=scratch
        + [
            pltpu.SemaphoreType.DMA((n, count)),
            pltpu.SemaphoreType.DMA((n, count)),
            pltpu.SemaphoreType.DMA((n, pieces)),
        ],
        compiler_params=pltpu.CompilerParams(
            collective_id=collective_id, has_side_effects=True, vmem_limit_bytes=48 << 20
        ),
        name="scatter_gradients",
    )(*arrays)


def exchange_kernel(n_dp, n_fs, x_ref, out_ref, octet, line, send_sem, recv_sem):
    dp, fs = lax.axis_index("dp"), lax.axis_index("fsdp")
    barrier = pltpu.get_barrier_semaphore()
    for step in range(1, n_dp):
        pl.semaphore_signal(
            barrier, inc=1, device_id=(lax.rem(dp + step, n_dp), fs), device_id_type=MESH
        )
    for step in range(1, n_fs):
        pl.semaphore_signal(
            barrier, inc=1, device_id=(dp, lax.rem(fs + step, n_fs)), device_id_type=MESH
        )
    pl.semaphore_wait(barrier, n_dp + n_fs - 2)
    sends = []
    octet[0] = x_ref[...]
    for step in range(1, n_dp):
        copy = pltpu.make_async_remote_copy(
            src_ref=octet.at[0],
            dst_ref=octet.at[step],
            send_sem=send_sem.at[step],
            recv_sem=recv_sem.at[step],
            device_id=(lax.rem(dp + step, n_dp), fs),
            device_id_type=MESH,
        )
        copy.start()
        sends.append(copy)
    for copy in sends:
        copy.wait_recv()
    total = octet[0]
    for step in range(1, n_dp):
        total = total + octet[step]
    line[0] = total
    more = []
    for step in range(1, n_fs):
        copy = pltpu.make_async_remote_copy(
            src_ref=line.at[0],
            dst_ref=line.at[step],
            send_sem=send_sem.at[n_dp + step],
            recv_sem=recv_sem.at[n_dp + step],
            device_id=(dp, lax.rem(fs + step, n_fs)),
            device_id_type=MESH,
        )
        copy.start()
        more.append(copy)
    for copy in more:
        copy.wait_recv()
    total = line[0]
    for step in range(1, n_fs):
        total = total + line[step]
    out_ref[...] = total
    for copy in sends + more:
        copy.wait_send()


def exchange_sum(n_dp, n_fs, x, collective_id):
    return pl.pallas_call(
        partial(exchange_kernel, n_dp, n_fs),
        out_shape=jax.ShapeDtypeStruct(x.shape, F32),
        in_specs=[pl.BlockSpec(memory_space=pltpu.VMEM)],
        out_specs=pl.BlockSpec(memory_space=pltpu.VMEM),
        scratch_shapes=[
            pltpu.VMEM((n_dp,) + x.shape, F32),
            pltpu.VMEM((n_fs,) + x.shape, F32),
            pltpu.SemaphoreType.DMA((n_dp + n_fs,)),
            pltpu.SemaphoreType.DMA((n_dp + n_fs,)),
        ],
        compiler_params=pltpu.CompilerParams(collective_id=collective_id, has_side_effects=True),
        name="exchange_sums",
    )(x)


BLOCK = 32


EPSILON = 1e-05
HIGHEST = lax.Precision.HIGHEST


def layer_norm(values, gain_row, shift_row):
    average = jnp.mean(values, axis=-1, keepdims=True)
    centered = values - average
    variance = jnp.mean(centered * centered, axis=-1, keepdims=True)
    return centered * lax.rsqrt(variance + EPSILON) * gain_row + shift_row


def swish(values):
    return values * jax.nn.sigmoid(values)


def combine(earlier, latter):
    return (earlier[0] * latter[0], latter[0] * earlier[1] + latter[1])


def state_space(driving, log_rate, coupling, skip_gain, carry_on):
    frames_dev, channels = driving.shape
    blocks = frames_dev // BLOCK
    log_decay = -jnp.exp(log_rate)
    input_map = coupling[0] * jnp.sqrt(-jnp.expm1(2.0 * log_decay))
    output_map = coupling[1]
    step_index = jnp.arange(BLOCK, dtype=jnp.int32)
    step_float = step_index.astype(jnp.float32)
    kernel = jnp.sum(
        jnp.exp(step_float[:, None, None] * log_decay[None]) * (input_map * output_map)[None],
        axis=1,
    )
    lag_steps = step_index[:, None] - step_index[None, :]
    select = (lag_steps[:, :, None] == step_index[None, None, :]).astype(jnp.float32)
    toeplitz = jnp.einsum("tsl,lc->tsc", select, kernel, precision=HIGHEST)
    pieces = driving.reshape(blocks, BLOCK, channels)
    within_block = jnp.einsum("tsc,bsc->btc", toeplitz, pieces, precision=HIGHEST)
    tail_weights = (
        jnp.exp((BLOCK - 1.0 - step_float)[:, None, None] * log_decay[None]) * input_map[None]
    )
    end_states = jnp.einsum("snc,bsc->bnc", tail_weights, pieces, precision=HIGHEST)
    block_links = carry_on[:, None, None] * jnp.exp(BLOCK * log_decay)[None]
    totals = lax.associative_scan(combine, (block_links, end_states))[1]
    incoming = carry_on[:, None, None] * jnp.concatenate(
        [jnp.zeros_like(totals[:1]), totals[:-1]], axis=0
    )
    lead_weights = jnp.exp((step_float + 1.0)[:, None, None] * log_decay[None]) * output_map[None]
    from_before = jnp.einsum("tnc,bnc->btc", lead_weights, incoming, precision=HIGHEST)
    return (within_block + from_before).reshape(frames_dev, channels) + skip_gain * driving


def mixer(carry_on, mixed_in, log_rate, coupling, skip_gain):
    channels = mixed_in.shape[1] // 2
    driving = mixed_in[:, :channels]
    gate_in = mixed_in[:, channels:]
    return state_space(driving, log_rate, coupling, skip_gain, carry_on) * swish(gate_in)


def glu_conv(position, extent, projected, conv_taps):
    channels = projected.shape[1] // 2
    glu_out = projected[:, :channels] * jax.nn.sigmoid(projected[:, channels:])
    half_span = conv_taps.shape[0] // 2
    padded = jnp.pad(glu_out, ((half_span, half_span), (0, 0)))
    result = jnp.zeros_like(glu_out)
    for tap_index in range(conv_taps.shape[0]):
        source = position + (tap_index - half_span)
        inside = ((source >= 0) & (source < extent)).astype(jnp.float32)[:, None]
        result = (
            result
            + conv_taps[tap_index][None, :]
            * padded[tap_index : tap_index + glu_out.shape[0]]
            * inside
        )
    return result


def layout(lengths, offsets, used_slots, frames_dev):
    slot_index = jnp.arange(lengths.shape[0], dtype=jnp.int32)[None, :]
    frame_index = jnp.arange(frames_dev, dtype=jnp.int32)[:, None]
    inside = (
        (frame_index >= offsets[None, :])
        & (frame_index < offsets[None, :] + lengths[None, :])
        & (slot_index < used_slots)
    ).astype(jnp.int32)
    position = jnp.sum(inside * (frame_index - offsets[None, :]), axis=1)
    extent = jnp.sum(inside * lengths[None, :], axis=1)
    starts = position.reshape(frames_dev // BLOCK, BLOCK)[:, 0]
    carry_on = (starts > 0).astype(jnp.float32)
    return (position, extent, carry_on)


def product(left, right):
    return jnp.dot(left, right, preferred_element_type=jnp.float32)


def left_product(left, right):
    return lax.dot_general(
        left, right, (((0,), (0,)), ((), ())), preferred_element_type=jnp.float32
    )


def right_product(left, right):
    return lax.dot_general(
        left, right, (((1,), (1,)), ((), ())), preferred_element_type=jnp.float32
    )


def dense_back(grad_out, saved_low, weight):
    grad_low = grad_out.astype(jnp.bfloat16)
    return (left_product(saved_low, grad_low), right_product(grad_low, weight), grad_low)


def column_sum(grad_low):
    return jnp.sum(grad_low, axis=0, dtype=jnp.float32)


def ffn_forward(values, up_weight, down_weight, bias_up, gain_row, shift_row, bias_down):
    normed, norm_back = jax.vjp(layer_norm, values, gain_row, shift_row)
    normed_low = normed.astype(jnp.bfloat16)
    hidden = product(normed_low, up_weight) + bias_up
    active, swish_back = jax.vjp(swish, hidden)
    active_low = active.astype(jnp.bfloat16)
    branch = product(active_low, down_weight) + bias_down
    return (values + 0.5 * branch, (norm_back, normed_low, swish_back, active_low))


def ffn_backward(grad_values, saved, up_weight, down_weight):
    norm_back, normed_low, swish_back, active_low = saved
    down_grad, grad_active, down_low = dense_back(0.5 * grad_values, active_low, down_weight)
    up_grad, grad_normed, up_low = dense_back(swish_back(grad_active)[0], normed_low, up_weight)
    grad_input, gain_grad, shift_grad = norm_back(grad_normed)
    return (
        grad_values + grad_input,
        (up_grad, down_grad, column_sum(up_low), column_sum(down_low), gain_grad, shift_grad),
    )


def pack_small(bias_up, conv_bias, rate, maps, taps, gains, shifts, devices=1):
    layers, hidden = bias_up.shape
    channels = conv_bias.shape[0]
    ratio = hidden // channels
    bias = bias_up.reshape((layers, devices, ratio, channels // devices))
    bias = bias.transpose((0, 2, 1, 3)).reshape((layers * ratio, channels))
    rows = jnp.concatenate(
        [bias, conv_bias[None], rate, maps.reshape((-1, channels)), taps, gains, shifts], axis=0
    )
    rows = jnp.pad(rows, ((0, 256 - rows.shape[0]), (0, 0)))
    return rows.T


def unpack_small(small, devices, layers=2, ratio=4, states=32, width=15):
    rows = small.T
    channels = rows.shape[1]
    at = layers * ratio
    bias = rows[:at].reshape((layers, ratio, devices, channels // devices))
    bias = bias.transpose((0, 2, 1, 3)).reshape((layers, ratio * channels))
    out = [bias, rows[at]]
    at += 1
    for count in (states, 2 * states, width, 6, 12):
        out.append(rows[at : at + count])
        at += count
    out[3] = out[3].reshape((2, states, channels))
    return tuple(out)


def on_device(
    n_dp,
    n_fs,
    frames,
    seq_lengths,
    seq_offsets,
    seq_counts,
    ffn_up,
    ffn_down,
    ffn_bias_up,
    mix_in,
    mix_out,
    conv_in,
    conv_out,
    conv_out_bias,
    ssm_rate,
    ssm_map,
    conv_kernel,
    gains,
    shifts,
    cotangent,
):
    gathered = gather_all(
        n_dp,
        n_fs,
        [
            pack_small(ffn_bias_up, conv_out_bias, ssm_rate, ssm_map, conv_kernel, gains, shifts)[None],
            ffn_up,
            ffn_down,
            mix_in[None],
            mix_out[None],
            conv_in[None],
            conv_out[None],
        ],
        1,
    )
    small, up0, up1, down0, down1, mixin_full, mixout_full, convin_full, convout_full = [
        g.reshape((-1, g.shape[-1])) for g in gathered
    ]
    up_full, down_full = (up0, up1), (down0, down1)
    (
        bias_full,
        convbias_full,
        rate_full,
        map_full,
        taps_full,
        gains_full,
        shifts_full,
    ) = unpack_small(small.astype(jnp.float32), gathered[0].shape[0])
    bias_set = bias_full.astype(jnp.float32)
    gain_set = gains_full.astype(jnp.float32)
    shift_set = shifts_full.astype(jnp.float32)
    convbias_set = convbias_full.astype(jnp.float32)
    rate_set = rate_full.astype(jnp.float32)
    map_set = map_full.astype(jnp.float32)
    taps_set = taps_full.astype(jnp.float32)
    position, extent, carry_on = layout(
        seq_lengths[0], seq_offsets[0], seq_counts[0], frames.shape[0]
    )
    inputs = frames.astype(jnp.float32)
    channels = inputs.shape[1]
    after_one, saved_one = ffn_forward(
        inputs, up_full[0], down_full[0], bias_set[0], gain_set[0], shift_set[0], shift_set[6]
    )
    normed_two, norm_two_back = jax.vjp(layer_norm, after_one, gain_set[1], shift_set[1])
    normed_two_low = normed_two.astype(jnp.bfloat16)
    mixed_in = product(normed_two_low, mixin_full)
    gated_out, mixer_back = jax.vjp(
        partial(mixer, carry_on), mixed_in, rate_set, map_set, shift_set[11]
    )
    gated_low = gated_out.astype(jnp.bfloat16)
    after_two = after_one + (product(gated_low, mixout_full) + shift_set[8])
    normed_three, norm_three_back = jax.vjp(layer_norm, after_two, gain_set[2], shift_set[2])
    normed_three_low = normed_three.astype(jnp.bfloat16)
    projected = product(normed_three_low, convin_full) + jnp.concatenate(
        [shift_set[9], shift_set[10]]
    )
    convolved, conv_back = jax.vjp(partial(glu_conv, position, extent), projected, taps_set)
    count_all = float(frames.shape[0] * n_dp * n_fs)
    center = exchange_sum(n_dp, n_fs, jnp.sum(convolved, axis=0)[None], 2)[0] / count_all
    deviation = convolved - center
    spread = exchange_sum(n_dp, n_fs, jnp.sum(deviation * deviation, axis=0)[None], 3)[0] / count_all
    scale_inv = lax.rsqrt(spread + EPSILON)
    standard = deviation * scale_inv
    normed_bn = standard * gain_set[5] + shift_set[5]
    active_bn, swish_bn_back = jax.vjp(swish, normed_bn)
    active_bn_low = active_bn.astype(jnp.bfloat16)
    after_three = after_two + (product(active_bn_low, convout_full) + convbias_set)
    after_four, saved_four = ffn_forward(
        after_three, up_full[1], down_full[1], bias_set[1], gain_set[3], shift_set[3], shift_set[7]
    )
    result, norm_last_back = jax.vjp(layer_norm, after_four, gain_set[4], shift_set[4])
    grad_four, gain_grad_last, shift_grad_last = norm_last_back(cotangent.astype(jnp.float32))
    grad_three, ffn_grads_four = ffn_backward(grad_four, saved_four, up_full[1], down_full[1])
    convout_grad, grad_active_bn, conv_out_low = dense_back(grad_three, active_bn_low, convout_full)
    convbias_grad = column_sum(conv_out_low)
    grad_normed_bn = swish_bn_back(grad_active_bn)[0]
    bn_gain_grad = jnp.sum(grad_normed_bn * standard, axis=0)
    bn_shift_grad = jnp.sum(grad_normed_bn, axis=0)
    grad_standard = grad_normed_bn * gain_set[5]
    plain_sum, cross_sum = exchange_sum(
        n_dp,
        n_fs,
        jnp.stack([jnp.sum(grad_standard, axis=0), jnp.sum(grad_standard * standard, axis=0)]),
        4,
    )
    grad_convolved = scale_inv * (
        grad_standard - plain_sum / count_all - standard * (cross_sum / count_all)
    )
    grad_projected, taps_grad = conv_back(grad_convolved)
    convin_grad, grad_normed_three, proj_low = dense_back(
        grad_projected, normed_three_low, convin_full
    )
    convin_bias_grad = column_sum(proj_low)
    grad_two_part, gain_grad_three, shift_grad_three = norm_three_back(grad_normed_three)
    grad_two = grad_three + grad_two_part
    mixout_grad, grad_gated, mix_low = dense_back(grad_two, gated_low, mixout_full)
    grad_mixed, rate_grad, map_grad, skip_grad = mixer_back(grad_gated)
    mixin_grad, grad_normed_two = dense_back(grad_mixed, normed_two_low, mixin_full)[:2]
    grad_one_part, gain_grad_two, shift_grad_two = norm_two_back(grad_normed_two)
    grad_one = grad_two + grad_one_part
    grad_input, ffn_grads_one = ffn_backward(grad_one, saved_one, up_full[0], down_full[0])
    gain_stack = jnp.stack(
        [
            ffn_grads_one[4],
            gain_grad_two,
            gain_grad_three,
            ffn_grads_four[4],
            gain_grad_last,
            bn_gain_grad,
        ]
    )
    shift_stack = jnp.stack(
        [
            ffn_grads_one[5],
            shift_grad_two,
            shift_grad_three,
            ffn_grads_four[5],
            shift_grad_last,
            bn_shift_grad,
            ffn_grads_one[3],
            ffn_grads_four[3],
            column_sum(mix_low),
            convin_bias_grad[:channels],
            convin_bias_grad[channels:],
            skip_grad,
        ]
    )
    devices = n_dp * n_fs
    small_grad = pack_small(
        jnp.stack([ffn_grads_one[2], ffn_grads_four[2]]),
        convbias_grad,
        rate_grad,
        map_grad,
        taps_grad,
        gain_stack,
        shift_stack,
        devices,
    )
    reduced = scatter_all(
        n_dp,
        n_fs,
        [
            g.astype(BF16).reshape((devices, g.shape[0] // devices, g.shape[1]))
            for g in (
                ffn_grads_four[0],
                ffn_grads_four[1],
                convout_grad,
                convin_grad,
                mixout_grad,
                mixin_grad,
                ffn_grads_one[0],
                ffn_grads_one[1],
                small_grad,
            )
        ],
        5,
    )
    small = unpack_small(reduced[8], 1)
    return (
        result.astype(jnp.bfloat16),
        grad_input,
        jnp.stack([reduced[6], reduced[0]]),
        jnp.stack([reduced[7], reduced[1]]),
        small[0],
        reduced[5],
        reduced[4],
        reduced[3],
        reduced[2],
    ) + small[1:]


def solution(mesh):
    in_specs = (
        P(("dp", "fsdp"), None),
        P(("dp", "fsdp"), None),
        P(("dp", "fsdp"), None),
        P(("dp", "fsdp")),
        P(None, ("dp", "fsdp"), None),
        P(None, ("dp", "fsdp"), None),
        P(None, ("dp", "fsdp")),
        P(("dp", "fsdp"), None),
        P(("dp", "fsdp"), None),
        P(("dp", "fsdp"), None),
        P(("dp", "fsdp"), None),
        P(("dp", "fsdp")),
        P(None, ("dp", "fsdp")),
        P(None, None, ("dp", "fsdp")),
        P(None, ("dp", "fsdp")),
        P(None, ("dp", "fsdp")),
        P(None, ("dp", "fsdp")),
        P(("dp", "fsdp"), None),
    )
    out_specs = (
        P(("dp", "fsdp"), None),
        P(("dp", "fsdp"), None),
        P(None, ("dp", "fsdp"), None),
        P(None, ("dp", "fsdp"), None),
        P(None, ("dp", "fsdp")),
        P(("dp", "fsdp"), None),
        P(("dp", "fsdp"), None),
        P(("dp", "fsdp"), None),
        P(("dp", "fsdp"), None),
        P(("dp", "fsdp")),
        P(None, ("dp", "fsdp")),
        P(None, None, ("dp", "fsdp")),
        P(None, ("dp", "fsdp")),
        P(None, ("dp", "fsdp")),
        P(None, ("dp", "fsdp")),
    )
    return jax.shard_map(
        partial(on_device, mesh.shape["dp"], mesh.shape["fsdp"]), mesh=mesh, in_specs=in_specs, out_specs=out_specs, check_vma=False
    )
```

```python
import itertools
from functools import partial

import jax
import jax.numpy as jnp
from jax import lax
from jax.experimental import pallas as pl
from jax.experimental.pallas import tpu as pltpu
from jax.sharding import PartitionSpec as P

MESH = pl.DeviceIdType.MESH
BF16 = jnp.bfloat16
F32 = jnp.float32


def flip(index, bit):
    return index + bit * (1 - 2 * lax.rem(lax.div(index, bit), 2))


def flip_all(index, bits):
    for bit in bits:
        index = flip(index, bit)
    return index


def combos(bits):
    found = [()]
    for bit in bits:
        found = found + [entry + (bit,) for entry in found]
    return found


def plan_bits(n_dp):
    bits, bit = [], 2
    while bit < n_dp:
        bits.append(bit)
        bit *= 2
    return tuple(bits)


def greet(dp, fs, n_dp, n_fs):
    barrier = pltpu.get_barrier_semaphore()
    bits = (1,) + plan_bits(n_dp)
    for bit in bits:
        pl.semaphore_signal(barrier, inc=1, device_id=(flip(dp, bit), fs), device_id_type=MESH)
    for step in range(1, n_fs):
        pl.semaphore_signal(
            barrier, inc=1, device_id=(dp, lax.rem(fs + step, n_fs)), device_id_type=MESH
        )
    pl.semaphore_wait(barrier, len(bits) + n_fs - 1)


def gather_kernel(n_dp, n_fs, layers, *refs):
    n_in = len(layers)
    n_out = sum(layers)
    ins, outs = refs[:n_in], refs[n_in : n_in + n_out]
    send_sem, recv_sem, local_sem = refs[n_in + n_out :]
    sources = []
    for ref, count in zip(ins, layers):
        sources += [ref.at[layer] for layer in range(count)]
    dp, fs = lax.axis_index("dp"), lax.axis_index("fsdp")
    bits = plan_bits(n_dp)
    orders = (bits, bits[::-1])
    half = n_fs // 2
    greet(dp, fs, n_dp, n_fs)
    sends = []

    def remote(chunk, slot, src, dst, device):
        return pltpu.make_async_remote_copy(
            src_ref=src,
            dst_ref=dst,
            send_sem=send_sem.at[chunk, slot],
            recv_sem=recv_sem.at[chunk, slot],
            device_id=device,
            device_id_type=MESH,
        )

    def stages(chunk):
        src, out = sources[chunk], outs[chunk]
        mine = dp * n_fs + fs
        slots = itertools.count()

        def zone(where, part):
            if part is None:
                return out.at[pl.ds(where * n_fs, n_fs)]
            return out.at[pl.ds(where * n_fs + part * half, half)]

        steps = []
        z_slots = [next(slots) for _ in range(1, n_fs)]
        local = pltpu.make_async_copy(src, out.at[mine], local_sem.at[chunk])

        def start():
            local.start()
            for step in range(1, n_fs):
                to = (dp, lax.rem(fs + step, n_fs))
                copy = remote(chunk, z_slots[step - 1], src, out.at[mine], to)
                copy.start()
                sends.append(copy)

        steps.append(start)

        def wait_z():
            local.wait()
            for step in range(1, n_fs):
                origin = dp * n_fs + lax.rem(fs + n_fs - step, n_fs)
                remote(chunk, z_slots[step - 1], src, out.at[origin], (dp, fs)).wait_recv()

        waits = [wait_z]
        for depth in range(len(bits)):
            plan = []
            for part, order in enumerate(orders):
                for entry in combos(order[:depth]):
                    plan.append((next(slots), part, order[depth], entry))

            def go(plan=plan, before=tuple(waits)):
                for wait in before:
                    wait()
                for slot, part, bit, entry in plan:
                    view = zone(flip_all(dp, entry), part)
                    copy = remote(chunk, slot, view, view, (flip(dp, bit), fs))
                    copy.start()
                    sends.append(copy)

            def arrive(plan=plan):
                for slot, part, bit, entry in plan:
                    view = zone(flip_all(flip(dp, bit), entry), part)
                    remote(chunk, slot, view, view, (flip(dp, bit), fs)).wait_recv()

            steps.append(go)
            waits = [arrive]
        last = [(next(slots), entry) for entry in combos(bits)]

        def cross(before=tuple(waits)):
            for wait in before:
                wait()
            for slot, entry in last:
                view = zone(flip_all(dp, entry), None)
                copy = remote(chunk, slot, view, view, (flip(dp, 1), fs))
                copy.start()
                sends.append(copy)

        def finish():
            for slot, entry in last:
                view = zone(flip_all(flip(dp, 1), entry), None)
                remote(chunk, slot, view, view, (flip(dp, 1), fs)).wait_recv()

        steps += [cross, finish]
        return steps

    plans = [stages(chunk) for chunk in range(n_out)]
    depth = len(plans[0])
    for wave in range(n_out + depth - 1):
        for chunk in range(n_out):
            stage = wave - chunk
            if 0 <= stage < depth:
                plans[chunk][stage]()
    for copy in sends:
        copy.wait_send()


def slot_count(n_dp, n_fs):
    nb = len(plan_bits(n_dp))
    return n_fs - 1 + 2 * (2**nb - 1) + 2**nb


def gather_all(n_dp, n_fs, arrays, collective_id):
    layers = tuple(a.shape[0] for a in arrays)
    outs = []
    for a in arrays:
        outs += [jax.ShapeDtypeStruct((n_dp * n_fs,) + a.shape[1:], a.dtype)] * a.shape[0]
    count = slot_count(n_dp, n_fs)
    return pl.pallas_call(
        partial(gather_kernel, n_dp, n_fs, layers),
        out_shape=outs,
        in_specs=[pl.BlockSpec(memory_space=pltpu.HBM)] * len(arrays),
        out_specs=[pl.BlockSpec(memory_space=pltpu.HBM)] * len(outs),
        scratch_shapes=[
            pltpu.SemaphoreType.DMA((len(outs), count)),
            pltpu.SemaphoreType.DMA((len(outs), count)),
            pltpu.SemaphoreType.DMA((len(outs),)),
        ],
        compiler_params=pltpu.CompilerParams(collective_id=collective_id, has_side_effects=True),
        name="gather_parameters",
    )(*arrays)


def scatter_kernel(n_dp, n_fs, n_chunks, *refs):
    ins, outs = refs[:n_chunks], refs[n_chunks : 2 * n_chunks]
    per = 4
    scratch = refs[2 * n_chunks : 2 * n_chunks + per * n_chunks]
    send_sem, recv_sem, local_sem = refs[2 * n_chunks + per * n_chunks :]
    dp, fs = lax.axis_index("dp"), lax.axis_index("fsdp")
    bits = plan_bits(n_dp)
    nb = len(bits)
    orders = (bits[::-1], bits)
    half = n_fs // 2
    index = {entry: at for at, entry in enumerate(combos(bits))}
    greet(dp, fs, n_dp, n_fs)
    sends = []

    def remote(chunk, slot, src, dst, device):
        return pltpu.make_async_remote_copy(
            src_ref=src,
            dst_ref=dst,
            send_sem=send_sem.at[chunk, slot],
            recv_sem=recv_sem.at[chunk, slot],
            device_id=device,
            device_id_type=MESH,
        )

    def add_into(kept, other):
        count = kept.shape[0]

        def body(at, _):
            total = kept[at].astype(F32) + other[at].astype(F32)
            kept[at] = total.astype(BF16)
            return 0

        lax.fori_loop(0, count, body, 0)

    def stages(chunk):
        src, out = ins[chunk], outs[chunk]
        first, own, later, last = scratch[per * chunk : per * chunk + per]
        slots = itertools.count()
        pieces = [(next(slots), entry, index[entry]) for entry in combos(bits)]
        loads = [
            pltpu.make_async_copy(
                src.at[pl.ds(flip_all(dp, entry) * n_fs, n_fs)], own.at[at], local_sem.at[chunk, at]
            )
            for _, entry, at in pieces
        ]

        def start():
            for slot, entry, at in pieces:
                view = src.at[pl.ds(flip_all(flip(dp, 1), entry) * n_fs, n_fs)]
                copy = remote(chunk, slot, view, first.at[at], (flip(dp, 1), fs))
                copy.start()
                sends.append(copy)
            for load in loads:
                load.start()

        def fold_first():
            for load, (slot, entry, at) in zip(loads, pieces):
                load.wait()
                remote(chunk, slot, first.at[at], first.at[at], (flip(dp, 1), fs)).wait_recv()
                add_into(own.at[at], first.at[at])

        steps = [start]
        folds = [fold_first]
        used = 0
        for depth in range(nb):
            plan = []
            for part, order in enumerate(orders):
                bit, gone = order[depth], order[:depth]
                keep = [e for e in combos(bits) if not (set(e) & set(gone)) and bit not in e]
                for entry in keep:
                    away = tuple(sorted(entry + (bit,)))
                    plan.append((next(slots), part, bit, index[away], index[entry], used))
                    used += 1

            def go(plan=plan, before=tuple(folds)):
                for fold in before:
                    fold()
                for slot, part, bit, away, kept, place in plan:
                    copy = remote(
                        chunk,
                        slot,
                        own.at[away, pl.ds(part * half, half)],
                        later.at[place],
                        (flip(dp, bit), fs),
                    )
                    copy.start()
                    sends.append(copy)

            def fold(plan=plan):
                for slot, part, bit, away, kept, place in plan:
                    view = later.at[place]
                    remote(chunk, slot, view, view, (flip(dp, bit), fs)).wait_recv()
                    add_into(own.at[kept, pl.ds(part * half, half)], view)

            steps.append(go)
            folds = [fold]
        z_slots = [next(slots) for _ in range(1, n_fs)]

        def cross(before=tuple(folds)):
            for fold in before:
                fold()
            for step in range(1, n_fs):
                to = lax.rem(fs + step, n_fs)
                copy = remote(chunk, z_slots[step - 1], own.at[0, to], last.at[step - 1], (dp, to))
                copy.start()
                sends.append(copy)

        def finish():
            total = own[0, fs].astype(F32)
            for step in range(1, n_fs):
                view = last.at[step - 1]
                remote(chunk, z_slots[step - 1], view, view, (dp, fs)).wait_recv()
                total = total + last[step - 1].astype(F32)
            out[...] = total

        steps += [cross, finish]
        return steps

    plans = [stages(chunk) for chunk in range(n_chunks)]
    depth = len(plans[0])
    for wave in range(n_chunks + depth - 1):
        for chunk in range(n_chunks):
            stage = wave - chunk
            if 0 <= stage < depth:
                plans[chunk][stage]()
    for copy in sends:
        copy.wait_send()


def scatter_all(n_dp, n_fs, arrays, collective_id):
    nb = len(plan_bits(n_dp))
    pieces = 2**nb
    scratch = []
    for a in arrays:
        tail = a.shape[1:]
        scratch += [
            pltpu.VMEM((pieces, n_fs) + tail, BF16),
            pltpu.VMEM((pieces, n_fs) + tail, BF16),
            pltpu.VMEM((2 * (pieces - 1), n_fs // 2) + tail, BF16),
            pltpu.VMEM((n_fs - 1,) + tail, BF16),
        ]
    count = slot_count(n_dp, n_fs)
    n = len(arrays)
    return pl.pallas_call(
        partial(scatter_kernel, n_dp, n_fs, n),
        out_shape=[jax.ShapeDtypeStruct(a.shape[1:], F32) for a in arrays],
        in_specs=[pl.BlockSpec(memory_space=pltpu.HBM)] * n,
        out_specs=[pl.BlockSpec(memory_space=pltpu.VMEM)] * n,
        scratch_shapes=scratch
        + [
            pltpu.SemaphoreType.DMA((n, count)),
            pltpu.SemaphoreType.DMA((n, count)),
            pltpu.SemaphoreType.DMA((n, pieces)),
        ],
        compiler_params=pltpu.CompilerParams(
            collective_id=collective_id, has_side_effects=True, vmem_limit_bytes=48 << 20
        ),
        name="scatter_gradients",
    )(*arrays)


def exchange_kernel(n_dp, n_fs, x_ref, out_ref, octet, line, send_sem, recv_sem):
    dp, fs = lax.axis_index("dp"), lax.axis_index("fsdp")
    barrier = pltpu.get_barrier_semaphore()
    for step in range(1, n_dp):
        pl.semaphore_signal(
            barrier, inc=1, device_id=(lax.rem(dp + step, n_dp), fs), device_id_type=MESH
        )
    for step in range(1, n_fs):
        pl.semaphore_signal(
            barrier, inc=1, device_id=(dp, lax.rem(fs + step, n_fs)), device_id_type=MESH
        )
    pl.semaphore_wait(barrier, n_dp + n_fs - 2)
    sends = []
    octet[0] = x_ref[...]
    for step in range(1, n_dp):
        copy = pltpu.make_async_remote_copy(
            src_ref=octet.at[0],
            dst_ref=octet.at[step],
            send_sem=send_sem.at[step],
            recv_sem=recv_sem.at[step],
            device_id=(lax.rem(dp + step, n_dp), fs),
            device_id_type=MESH,
        )
        copy.start()
        sends.append(copy)
    for copy in sends:
        copy.wait_recv()
    total = octet[0]
    for step in range(1, n_dp):
        total = total + octet[step]
    line[0] = total
    more = []
    for step in range(1, n_fs):
        copy = pltpu.make_async_remote_copy(
            src_ref=line.at[0],
            dst_ref=line.at[step],
            send_sem=send_sem.at[n_dp + step],
            recv_sem=recv_sem.at[n_dp + step],
            device_id=(dp, lax.rem(fs + step, n_fs)),
            device_id_type=MESH,
        )
        copy.start()
        more.append(copy)
    for copy in more:
        copy.wait_recv()
    total = line[0]
    for step in range(1, n_fs):
        total = total + line[step]
    out_ref[...] = total
    for copy in sends + more:
        copy.wait_send()


def exchange(n_dp, n_fs, x, collective_id):
    return pl.pallas_call(
        partial(exchange_kernel, n_dp, n_fs),
        out_shape=jax.ShapeDtypeStruct(x.shape, F32),
        in_specs=[pl.BlockSpec(memory_space=pltpu.VMEM)],
        out_specs=pl.BlockSpec(memory_space=pltpu.VMEM),
        scratch_shapes=[
            pltpu.VMEM((n_dp,) + x.shape, F32),
            pltpu.VMEM((n_fs,) + x.shape, F32),
            pltpu.SemaphoreType.DMA((n_dp + n_fs,)),
            pltpu.SemaphoreType.DMA((n_dp + n_fs,)),
        ],
        compiler_params=pltpu.CompilerParams(collective_id=collective_id, has_side_effects=True),
        name="exchange_sums",
    )(x)


TILE = 512
STATES = 32
TAPS = 15
REACH = 8
EPSILON = 1e-05
CHUNK = 256
ROWS = 128
SPAN = 32
VMEM_LIMIT = 60 << 20


def sigmoid(v):
    return 0.5 * jnp.tanh(0.5 * v) + 0.5


def dot_nn(a, b):
    return jnp.dot(a, b, preferred_element_type=F32)


def dot_nt(a, b):
    return lax.dot_general(a, b, (((1,), (1,)), ((), ())), preferred_element_type=F32)


def dot_tn(a, b):
    return lax.dot_general(a, b, (((0,), (0,)), ((), ())), preferred_element_type=F32)


def norm_parts(v):
    centered = v - jnp.mean(v, axis=-1, keepdims=True)
    inv = lax.rsqrt(jnp.mean(centered * centered, axis=-1, keepdims=True) + EPSILON)
    return centered * inv, inv


def norm_back(grad, e, inv, gain):
    d = grad * gain
    return (
        d - jnp.mean(d, axis=-1, keepdims=True) - e * jnp.mean(d * e, axis=-1, keepdims=True)
    ) * inv


def fold8(v):
    return jnp.sum(v.reshape((v.shape[0] // 8, 8, v.shape[1])), axis=0)


def by_rows(body, rows=TILE, step=ROWS):
    def run(at, _):
        body(pl.ds(pl.multiple_of(at * step, step), step))
        return 0

    lax.fori_loop(0, rows // step, run, 0)


def columns(at, width=CHUNK):
    return pl.ds(pl.multiple_of(at * width, width), width)


def merge_rows(parts, low_half):
    for distance in (1, 2, 4):
        low = low_half[distance]
        parts = [
            jnp.where(low, a, b) + pltpu.roll(jnp.where(low, b, a), distance, 0)
            for a, b in zip(parts[0::2], parts[1::2])
        ]
    return parts[0]


def half_masks(width):
    row = lax.broadcasted_iota(jnp.int32, (8, width), 0)
    return {d: (row // d) % 2 == 0 for d in (4, 2, 1)}


def fold_states(v):
    return jnp.sum(v.reshape((STATES // 8, 8, v.shape[1])), axis=0)


def fill_halo(padded, flags_ref, tiles):
    pitch = TILE + 2 * REACH
    for at in range(tiles):
        base = at * pitch
        if at == 0:
            padded[:, base : base + REACH, :] = jnp.zeros_like(padded[:, base : base + REACH, :])
        if at == tiles - 1:
            end = base + REACH + TILE
            padded[:, end : end + REACH, :] = jnp.zeros_like(padded[:, end : end + REACH, :])
        else:
            keep = flags_ref[at + 1].astype(F32)
            end = base + REACH + TILE
            padded[:, end : end + REACH, :] = (
                padded[:, base + pitch + REACH : base + pitch + 2 * REACH, :] * keep
            )
            padded[:, base + pitch : base + pitch + REACH, :] = (
                padded[:, end - REACH : end, :] * keep
            )


def taps_over(padded, taps_ref, store, tiles, reverse, block=64):
    pitch = TILE + 2 * REACH
    per = TILE // block
    lanes = padded.shape[0]
    for lane in range(lanes):
        weights = [
            jnp.broadcast_to(taps_ref[k : k + 1, lane * 128 : lane * 128 + 128], (block, 128))
            for k in range(TAPS)
        ]

        def run(at, _):
            tile, inner = at // per, at % per
            base = tile * pitch + inner * block
            total = jnp.zeros((block, 128), F32)
            for k in range(TAPS):
                shift = REACH + (TAPS // 2 - k if reverse else k - TAPS // 2)
                total = total + weights[k] * padded[lane, pl.ds(base + shift, block), :]
            store(lane, tile * TILE + inner * block, base, total)
            return 0

        lax.fori_loop(0, tiles * per, run, 0)


def front_kernel(
    flags_ref,
    x_ref,
    up_ref,
    down_ref,
    mixin_ref,
    mixout_ref,
    convin_ref,
    bias_ref,
    vec_ref,
    taps_ref,
    decay_ref,
    map_ref,
    h_out,
    x1_out,
    u_out,
    v_out,
    y_out,
    gated_out,
    x2_out,
    p_out,
    hold_out,
    w_out,
    stat_out,
    low_scr,
    sum_scr,
    state_scr,
    padded,
):
    at = pl.program_id(0)
    tiles = pl.num_programs(0)
    channels = x_ref.shape[1]
    lanes = channels // 128
    gain = lambda k: vec_ref[k : k + 1, :]
    shift = lambda k: vec_ref[6 + k : 7 + k, :]

    def first(rows):
        e, _ = norm_parts(x_ref[rows, :].astype(F32))
        low_scr[rows, :] = (e * gain(0) + shift(0)).astype(BF16)
        sum_scr[rows, :] = jnp.zeros((ROWS, channels), F32)

    by_rows(first)

    def hidden(c, _):
        cols = columns(c)
        h = dot_nn(low_scr[...], up_ref[:, cols]) + bias_ref[0:1, cols]
        h_out[:, cols] = h.astype(BF16)
        active = (h * sigmoid(h)).astype(BF16)
        sum_scr[...] += dot_nn(active, down_ref[cols, :])
        return 0

    lax.fori_loop(0, up_ref.shape[1] // CHUNK, hidden, 0)

    def second(rows):
        x1 = x_ref[rows, :].astype(F32) + 0.5 * (sum_scr[rows, :] + shift(6))
        x1_out[rows, :] = x1
        e, _ = norm_parts(x1)
        low_scr[rows, :] = (e * gain(1) + shift(1)).astype(BF16)

    by_rows(second)

    def project(c, _):
        cols = columns(c)
        right = columns(c + channels // CHUNK)
        u_out[:, cols] = dot_nn(low_scr[...], mixin_ref[:, cols])
        v_out[:, cols] = dot_nn(low_scr[...], mixin_ref[:, right]).astype(BF16)
        return 0

    lax.fori_loop(0, channels // CHUNK, project, 0)

    low_half = half_masks(128)
    keep = flags_ref[at].astype(F32)

    @pl.when(at == 0)
    def _():
        state_scr[...] = jnp.zeros_like(state_scr)

    state_scr[...] = state_scr[...] * keep

    def scan_span(span, _):
        hold_out[span] = state_scr[...]

        def scan(step, _):
            start = pl.multiple_of(span * SPAN + step * 8, 8)
            for lane in range(lanes):
                cols = slice(lane * 128, lane * 128 + 128)
                state = state_scr[:, cols]
                decay = decay_ref[:, cols]
                maps = map_ref[:, cols]
                drive = u_out[pl.ds(start, 8), cols]
                parts = []
                for j in range(8):
                    state = decay * state + jnp.broadcast_to(drive[j : j + 1, :], (STATES, 128))
                    parts.append(fold_states(maps * state))
                state_scr[:, cols] = state
                sum_scr[pl.ds(start, 8), cols] = merge_rows(parts, low_half)
            return 0

        lax.fori_loop(0, SPAN // 8, scan, 0)
        return 0

    lax.fori_loop(0, TILE // SPAN, scan_span, 0)

    def gate(rows):
        y = sum_scr[rows, :] + shift(11) * u_out[rows, :]
        v = v_out[rows, :].astype(F32)
        y_out[rows, :] = y.astype(BF16)
        gated = (y * (v * sigmoid(v))).astype(BF16)
        gated_out[rows, :] = gated

    by_rows(gate)
    sum_scr[...] = dot_nn(gated_out[...], mixout_ref[...])

    def third(rows):
        x2 = x1_out[rows, :] + (sum_scr[rows, :] + shift(8))
        x2_out[rows, :] = x2
        e, _ = norm_parts(x2)
        low_scr[rows, :] = (e * gain(2) + shift(2)).astype(BF16)

    by_rows(third)
    pitch = TILE + 2 * REACH

    def widen(c, _):
        cols = columns(c)
        right = columns(c + channels // CHUNK)
        left_part = dot_nn(low_scr[...], convin_ref[:, cols]) + vec_ref[15:16, cols]
        right_part = dot_nn(low_scr[...], convin_ref[:, right]) + vec_ref[16:17, cols]
        p_out[:, cols] = left_part.astype(BF16)
        p_out[:, right] = right_part.astype(BF16)
        g = left_part * sigmoid(right_part)
        place = pl.ds(pl.multiple_of(at * pitch + REACH, 8), TILE)
        for k in range(CHUNK // 128):
            padded[c * (CHUNK // 128) + k, place, :] = g[:, k * 128 : k * 128 + 128]
        return 0

    lax.fori_loop(0, channels // CHUNK, widen, 0)

    @pl.when(at == tiles - 1)
    def _():
        count = w_out.shape[0] // TILE
        fill_halo(padded, flags_ref, count)

        def store(lane, row, base, total):
            w_out[pl.ds(pl.multiple_of(row, 64), 64), lane * 128 : lane * 128 + 128] = total

        taps_over(padded, taps_ref, store, count, False)
        stat_out[...] = jnp.zeros_like(stat_out)

        def total(at, _):
            rows = pl.ds(pl.multiple_of(at * ROWS, ROWS), ROWS)
            stat_out[0:8, :] += fold8(w_out[rows, :])
            return 0

        lax.fori_loop(0, w_out.shape[0] // ROWS, total, 0)
        center = jnp.sum(stat_out[0:8, :], axis=0, keepdims=True) * (1.0 / w_out.shape[0])

        def spread(at, _):
            rows = pl.ds(pl.multiple_of(at * ROWS, ROWS), ROWS)
            off = w_out[rows, :] - center
            stat_out[8:16, :] += fold8(off * off)
            return 0

        lax.fori_loop(0, w_out.shape[0] // ROWS, spread, 0)
        stat_out[0:8, :] = jnp.broadcast_to(center, (8, channels))
        stat_out[8:16, :] = jnp.broadcast_to(
            jnp.sum(stat_out[8:16, :], axis=0, keepdims=True), (8, channels)
        )


def whole(shape):
    zeros = (0,) * len(shape)
    return pl.BlockSpec(shape, lambda *_: zeros)


def params():
    return pltpu.CompilerParams(
        dimension_semantics=("arbitrary",), vmem_limit_bytes=VMEM_LIMIT
    )


def front(flags, x, up, down, mixin, mixout, convin, bias, vec, taps, decay, maps):
    frames, channels = x.shape
    hidden = up.shape[1]
    tiles = frames // TILE
    row = lambda width: pl.BlockSpec((TILE, width), lambda i, *_: (i, 0))
    shape = lambda width, kind: jax.ShapeDtypeStruct((frames, width), kind)
    spans = TILE // SPAN
    return pl.pallas_call(
        front_kernel,
        grid_spec=pltpu.PrefetchScalarGridSpec(
            num_scalar_prefetch=1,
            grid=(tiles,),
            in_specs=[row(channels)]
            + [whole(a.shape) for a in (up, down, mixin, mixout, convin, bias, vec, taps, decay, maps)],
            out_specs=[
                row(hidden),
                row(channels),
                row(channels),
                row(channels),
                row(channels),
                row(channels),
                row(channels),
                row(2 * channels),
                pl.BlockSpec((spans, STATES, channels), lambda i, *_: (i, 0, 0)),
                whole((frames, channels)),
                whole((16, channels)),
            ],
            scratch_shapes=[
                pltpu.VMEM((TILE, channels), BF16),
                pltpu.VMEM((TILE, channels), F32),
                pltpu.VMEM((STATES, channels), F32),
                pltpu.VMEM((channels // 128, tiles * (TILE + 2 * REACH), 128), F32),
            ],
        ),
        out_shape=[
            shape(hidden, BF16),
            shape(channels, F32),
            shape(channels, F32),
            shape(channels, BF16),
            shape(channels, BF16),
            shape(channels, BF16),
            shape(channels, F32),
            shape(2 * channels, BF16),
            jax.ShapeDtypeStruct((frames // SPAN, STATES, channels), F32),
            shape(channels, F32),
            jax.ShapeDtypeStruct((16, channels), F32),
        ],
        compiler_params=params(),
        name="front",
    )(flags, x, up, down, mixin, mixout, convin, bias, vec, taps, decay, maps)


def ffn_back(low_t, grad_t, grad_ref, h_load, up_ref, down_ref, up_acc, down_acc, bias_acc, back_scr, hidden):
    def chunk(c, _):
        cols = columns(c)
        h = h_load(cols)
        sig = sigmoid(h)
        active = h * sig
        gate = dot_nt(grad_ref[...], down_ref[cols, :])
        grad_h = (gate * (sig * (1.0 + h - active))).astype(BF16)
        bias_acc[:, cols] += fold8(grad_h.astype(F32))
        down_acc[cols, :] += dot_tn(active.astype(BF16), grad_ref[...])
        up_acc[:, cols] += dot_nn(low_t[...], grad_h)
        back_scr[...] += dot_nt(grad_h, up_ref[:, cols])
        return 0

    lax.fori_loop(0, hidden // CHUNK, chunk, 0)


def middle_kernel(
    x2_ref,
    w_ref,
    cot_ref,
    up_ref,
    down_ref,
    convout_ref,
    bias_ref,
    vec_ref,
    stat_ref,
    out_ref,
    gx3_ref,
    gnb_ref,
    gup_out,
    gdown_out,
    gconvout_out,
    gbias_out,
    gvec_out,
    up_acc,
    down_acc,
    convout_acc,
    bias_acc,
    vec_acc,
    h_scr,
    low_scr,
    turn_scr,
    act_scr,
    grad_scr,
    sum_scr,
    x3_scr,
):
    at = pl.program_id(0)
    tiles = pl.num_programs(0)
    channels = x2_ref.shape[1]
    hidden = up_ref.shape[1]
    gain = lambda k: vec_ref[k : k + 1, :]
    shift = lambda k: vec_ref[6 + k : 7 + k, :]
    center, scale = stat_ref[0:1, :], stat_ref[1:2, :]

    @pl.when(at == 0)
    def _():
        for ref in (up_acc, down_acc, convout_acc, bias_acc, vec_acc):
            ref[...] = jnp.zeros_like(ref)

    def normed(rows):
        e = (w_ref[rows, :] - center) * scale
        return e, e * gain(5) + shift(5)

    def first(rows):
        _, nb = normed(rows)
        act_scr[rows, :] = (nb * sigmoid(nb)).astype(BF16)

    by_rows(first)
    sum_scr[...] = dot_nn(act_scr[...], convout_ref[...])

    def second(rows):
        x3 = x2_ref[rows, :] + (sum_scr[rows, :] + vec_ref[18:19, :])
        x3_scr[rows, :] = x3
        e, _ = norm_parts(x3)
        low_scr[rows, :] = (e * gain(3) + shift(3)).astype(BF16)
        sum_scr[rows, :] = jnp.zeros((ROWS, channels), F32)

    by_rows(second)

    def forward(c, _):
        cols = columns(c)
        h = dot_nn(low_scr[...], up_ref[:, cols]) + bias_ref[1:2, cols]
        h_scr[:, cols] = h
        active = (h * sigmoid(h)).astype(BF16)
        sum_scr[...] += dot_nn(active, down_ref[cols, :])
        return 0

    lax.fori_loop(0, hidden // CHUNK, forward, 0)
    turn_scr[...] = low_scr[...].T

    def last(rows):
        x4 = x3_scr[rows, :] + 0.5 * (sum_scr[rows, :] + shift(7))
        e, inv = norm_parts(x4)
        out_ref[rows, :] = (e * gain(4) + shift(4)).astype(BF16)
        cot = cot_ref[rows, :].astype(F32)
        vec_acc[0] += fold8(cot * e)
        vec_acc[1] += fold8(cot)
        gx4 = norm_back(cot, e, inv, gain(4))
        gx3_ref[rows, :] = gx4
        low = (0.5 * gx4).astype(BF16)
        grad_scr[rows, :] = low
        vec_acc[2] += fold8(low.astype(F32))
        sum_scr[rows, :] = jnp.zeros((ROWS, channels), F32)

    by_rows(last)
    ffn_back(
        turn_scr,
        None,
        grad_scr,
        lambda cols: h_scr[:, cols],
        up_ref,
        down_ref,
        up_acc,
        down_acc,
        bias_acc,
        sum_scr,
        hidden,
    )

    def fourth(rows):
        e, inv = norm_parts(x3_scr[rows, :])
        grad = sum_scr[rows, :]
        vec_acc[3] += fold8(grad * e)
        vec_acc[4] += fold8(grad)
        gx3 = gx3_ref[rows, :] + norm_back(grad, e, inv, gain(3))
        gx3_ref[rows, :] = gx3
        low = gx3.astype(BF16)
        grad_scr[rows, :] = low
        vec_acc[5] += fold8(low.astype(F32))

    by_rows(fourth)
    convout_acc[...] += dot_tn(act_scr[...], grad_scr[...])
    sum_scr[...] = dot_nt(grad_scr[...], convout_ref[...])

    def fifth(rows):
        e, nb = normed(rows)
        sig = sigmoid(nb)
        gnb = sum_scr[rows, :] * (sig * (1.0 + nb * (1.0 - sig)))
        gnb_ref[rows, :] = gnb
        vec_acc[6] += fold8(gnb * e)
        vec_acc[7] += fold8(gnb)

    by_rows(fifth)

    @pl.when(at == tiles - 1)
    def _():
        by_rows(lambda rows: gup_out.__setitem__((rows, slice(None)), up_acc[rows, :].astype(BF16)), channels)
        by_rows(lambda rows: gdown_out.__setitem__((rows, slice(None)), down_acc[rows, :].astype(BF16)), hidden)
        by_rows(lambda rows: gconvout_out.__setitem__((rows, slice(None)), convout_acc[rows, :].astype(BF16)), channels)
        gbias_out[...] = jnp.broadcast_to(jnp.sum(bias_acc[...], axis=0, keepdims=True), gbias_out.shape)
        for k in range(8):
            gvec_out[k : k + 1, :] = jnp.sum(vec_acc[k], axis=0, keepdims=True)


def middle(x2, w, cot, up, down, convout, bias, vec, stat):
    frames, channels = x2.shape
    hidden = up.shape[1]
    tiles = frames // TILE
    row = lambda width: pl.BlockSpec((TILE, width), lambda i: (i, 0))
    big = lambda a: pltpu.VMEM(a.shape, F32)
    shapes = [
        jax.ShapeDtypeStruct((frames, channels), BF16),
        jax.ShapeDtypeStruct((frames, channels), F32),
        jax.ShapeDtypeStruct((frames, channels), F32),
        jax.ShapeDtypeStruct(up.shape, BF16),
        jax.ShapeDtypeStruct(down.shape, BF16),
        jax.ShapeDtypeStruct(convout.shape, BF16),
        jax.ShapeDtypeStruct((8, hidden), F32),
        jax.ShapeDtypeStruct((8, channels), F32),
    ]
    return pl.pallas_call(
        middle_kernel,
        grid=(tiles,),
        in_specs=[row(channels)] * 3
        + [whole(a.shape) for a in (up, down, convout, bias, vec, stat)],
        out_specs=[row(channels)] * 3 + [whole(s.shape) for s in shapes[3:]],
        out_shape=shapes,
        scratch_shapes=[
            big(up),
            big(down),
            big(convout),
            pltpu.VMEM((8, hidden), F32),
            pltpu.VMEM((8, 8, channels), F32),
            pltpu.VMEM((TILE, hidden), F32),
            pltpu.VMEM((TILE, channels), BF16),
            pltpu.VMEM((channels, TILE), BF16),
            pltpu.VMEM((TILE, channels), BF16),
            pltpu.VMEM((TILE, channels), BF16),
            pltpu.VMEM((TILE, channels), F32),
            pltpu.VMEM((TILE, channels), F32),
        ],
        compiler_params=params(),
        name="middle",
    )(x2, w, cot, up, down, convout, bias, vec, stat)


def conv_back_kernel(flags_ref, w_ref, gnb_ref, p_ref, taps_ref, vec_ref, stat_ref, gg_ref, gtaps_ref, padded, gpad):
    frames, channels = w_ref.shape
    tiles = frames // TILE
    pitch = TILE + 2 * REACH
    center, scale = stat_ref[0:1, :], stat_ref[1:2, :]
    plain, cross = stat_ref[2:3, :], stat_ref[3:4, :]

    for tile in range(tiles):

        def fill(at, _, tile=tile):
            rows = pl.ds(pl.multiple_of(tile * TILE + at * 64, 64), 64)
            place = pl.ds(pl.multiple_of(tile * pitch + REACH + at * 64, 8), 64)
            e = (w_ref[rows, :] - center) * scale
            d = gnb_ref[rows, :] * vec_ref[5:6, :]
            gw = scale * (d - plain - e * cross)
            g = p_ref[rows, :channels].astype(F32) * sigmoid(p_ref[rows, channels:].astype(F32))
            for lane in range(channels // 128):
                cols = slice(lane * 128, lane * 128 + 128)
                padded[lane, place, :] = gw[:, cols]
                gpad[lane, place, :] = g[:, cols]
            return 0

        lax.fori_loop(0, TILE // 64, fill, 0)
    fill_halo(padded, flags_ref, tiles)
    fill_halo(gpad, flags_ref, tiles)

    def store(lane, row, base, total):
        gg_ref[pl.ds(pl.multiple_of(row, 64), 64), lane * 128 : lane * 128 + 128] = total

    taps_over(padded, taps_ref, store, tiles, True)
    block = 64
    per = TILE // block
    for lane in range(channels // 128):

        def corr(at, sums, lane=lane):
            base = (at // per) * pitch + (at % per) * block
            here = padded[lane, pl.ds(pl.multiple_of(base + REACH, 8), block), :]
            return tuple(
                s + fold8(here * gpad[lane, pl.ds(base + REACH + k - TAPS // 2, block), :])
                for k, s in enumerate(sums)
            )

        sums = lax.fori_loop(0, tiles * per, corr, (jnp.zeros((8, 128), F32),) * TAPS)
        for k in range(TAPS):
            gtaps_ref[k : k + 1, lane * 128 : lane * 128 + 128] = jnp.sum(sums[k], axis=0, keepdims=True)


def conv_back(flags, w, gnb, p, taps, vec, stat):
    frames, channels = w.shape
    tiles = frames // TILE
    pad = pltpu.VMEM((channels // 128, tiles * (TILE + 2 * REACH), 128), F32)
    return pl.pallas_call(
        conv_back_kernel,
        in_specs=[pl.BlockSpec(memory_space=pltpu.SMEM)] + [pl.BlockSpec(memory_space=pltpu.VMEM)] * 6,
        out_specs=[pl.BlockSpec(memory_space=pltpu.VMEM)] * 2,
        out_shape=[
            jax.ShapeDtypeStruct((frames, channels), F32),
            jax.ShapeDtypeStruct((16, channels), F32),
        ],
        scratch_shapes=[pad, pad],
        compiler_params=pltpu.CompilerParams(vmem_limit_bytes=VMEM_LIMIT),
        name="conv_back",
    )(flags, w, gnb, p, taps, vec, stat)


def back_kernel(
    flags_ref,
    gg_ref,
    p_ref,
    x2_ref,
    gx3_ref,
    gated_ref,
    y_ref,
    v_ref,
    u_ref,
    x1_ref,
    hold_ref,
    convin_ref,
    mixout_ref,
    mixin_ref,
    vec_ref,
    decay_ref,
    map_ref,
    gx1_ref,
    gconvin_out,
    gmixout_out,
    gmixin_out,
    gvec_out,
    gmap_out,
    gdecay_out,
    convin_acc,
    mixout_acc,
    mixin_acc,
    vec_acc,
    map_acc,
    decay_acc,
    adj_scr,
    track,
    low_scr,
    wide_scr,
    sum_scr,
    gy_scr,
):
    step = pl.program_id(0)
    tiles = pl.num_programs(0)
    at = tiles - 1 - step
    channels = x2_ref.shape[1]
    lanes = channels // 128
    gain = lambda k: vec_ref[k : k + 1, :]
    shift = lambda k: vec_ref[6 + k : 7 + k, :]

    @pl.when(step == 0)
    def _():
        for ref in (convin_acc, mixout_acc, mixin_acc, vec_acc, map_acc, decay_acc, adj_scr):
            ref[...] = jnp.zeros_like(ref)

    left, right = slice(0, channels), slice(channels, 2 * channels)

    def first(rows):
        grad = gg_ref[rows, :]
        sig = sigmoid(p_ref[rows, right].astype(F32))
        gl = (grad * sig).astype(BF16)
        gr = (grad * p_ref[rows, left].astype(F32) * (sig * (1.0 - sig))).astype(BF16)
        wide_scr[rows, left] = gl
        wide_scr[rows, right] = gr
        vec_acc[0] += fold8(gl.astype(F32))
        vec_acc[1] += fold8(gr.astype(F32))
        e, _ = norm_parts(x2_ref[rows, :])
        low_scr[rows, :] = (e * gain(2) + shift(2)).astype(BF16)

    by_rows(first)
    turned = low_scr[...].T
    convin_acc[...] += dot_nn(turned, wide_scr[...])
    sum_scr[...] = dot_nt(wide_scr[...], convin_ref[...])

    def second(rows):
        e, inv = norm_parts(x2_ref[rows, :])
        grad = sum_scr[rows, :]
        vec_acc[2] += fold8(grad * e)
        vec_acc[3] += fold8(grad)
        gx2 = gx3_ref[rows, :] + norm_back(grad, e, inv, gain(2))
        gx1_ref[rows, :] = gx2
        low = gx2.astype(BF16)
        low_scr[rows, :] = low
        vec_acc[4] += fold8(low.astype(F32))

    by_rows(second)
    mixout_acc[...] += dot_tn(gated_ref[...], low_scr[...])
    sum_scr[...] = dot_nt(low_scr[...], mixout_ref[...])

    def third(rows):
        grad = sum_scr[rows, :]
        v = v_ref[rows, :].astype(F32)
        sig = sigmoid(v)
        swish = v * sig
        gy = grad * swish
        gy_scr[rows, :] = gy
        wide_scr[rows, right] = (
            grad * y_ref[rows, :].astype(F32) * (sig * (1.0 + v - swish))
        ).astype(BF16)
        vec_acc[5] += fold8(gy * u_ref[rows, :])

    by_rows(third)
    low_half = half_masks(128)
    later = jnp.minimum(at + 1, tiles - 1)
    adj_scr[...] = adj_scr[...] * flags_ref[later].astype(F32)

    def span_back(index, _):
        span = TILE // SPAN - 1 - index
        base = pl.multiple_of(span * SPAN, SPAN)
        for lane in range(lanes):
            cols = slice(lane * 128, lane * 128 + 128)
            decay = decay_ref[:, cols]

            def forward(block, state):
                drive = u_ref[pl.ds(pl.multiple_of(base + block * 8, 8), 8), cols]
                for j in range(8):
                    track[block * 8 + j, :, cols] = state
                    state = decay * state + jnp.broadcast_to(drive[j : j + 1, :], (STATES, 128))
                return state

            lax.fori_loop(0, SPAN // 8, forward, hold_ref[span, :, cols])

        def backward(index, _):
            block = SPAN // 8 - 1 - index
            start = pl.multiple_of(base + block * 8, 8)
            for lane in range(lanes):
                cols = slice(lane * 128, lane * 128 + 128)
                decay = decay_ref[:, cols]
                maps = map_ref[:, cols]
                adj = adj_scr[:, cols]
                drive = u_ref[pl.ds(start, 8), cols]
                grad = gy_scr[pl.ds(start, 8), cols]
                gmap = map_acc[:, cols]
                gdecay = decay_acc[:, cols]
                parts = [None] * 8
                for j in range(7, -1, -1):
                    adj = decay * adj + jnp.broadcast_to(grad[j : j + 1, :], (STATES, 128))
                    parts[j] = fold_states(maps * adj)
                    gmap = gmap + adj * jnp.broadcast_to(drive[j : j + 1, :], (STATES, 128))
                    gdecay = gdecay + adj * track[block * 8 + j, :, cols]
                adj_scr[:, cols] = adj
                map_acc[:, cols] = gmap
                decay_acc[:, cols] = gdecay
                sum_scr[pl.ds(start, 8), cols] = merge_rows(parts, low_half)
            return 0

        lax.fori_loop(0, SPAN // 8, backward, 0)
        return 0

    lax.fori_loop(0, TILE // SPAN, span_back, 0)

    def fourth(rows):
        gu = sum_scr[rows, :] + shift(11) * gy_scr[rows, :]
        wide_scr[rows, left] = gu.astype(BF16)
        e, _ = norm_parts(x1_ref[rows, :])
        low_scr[rows, :] = (e * gain(1) + shift(1)).astype(BF16)

    by_rows(fourth)
    turned = low_scr[...].T
    mixin_acc[...] += dot_nn(turned, wide_scr[...])
    sum_scr[...] = dot_nt(wide_scr[...], mixin_ref[...])

    def fifth(rows):
        e, inv = norm_parts(x1_ref[rows, :])
        grad = sum_scr[rows, :]
        vec_acc[6] += fold8(grad * e)
        vec_acc[7] += fold8(grad)
        gx1_ref[rows, :] = gx1_ref[rows, :] + norm_back(grad, e, inv, gain(1))

    by_rows(fifth)

    @pl.when(step == tiles - 1)
    def _():
        for out, acc in ((gconvin_out, convin_acc), (gmixout_out, mixout_acc), (gmixin_out, mixin_acc)):
            by_rows(
                lambda rows, out=out, acc=acc: out.__setitem__((rows, slice(None)), acc[rows, :].astype(BF16)),
                channels,
            )
        for k in range(8):
            gvec_out[k : k + 1, :] = jnp.sum(vec_acc[k], axis=0, keepdims=True)
        gmap_out[...] = map_acc[...]
        gdecay_out[...] = decay_acc[...] * map_ref[...]


def back(flags, gg, p, x2, gx3, gated, y, v, u, x1, hold, convin, mixout, mixin, vec, decay, maps):
    frames, channels = x2.shape
    tiles = frames // TILE
    row = lambda width: pl.BlockSpec((TILE, width), lambda i, *_: (tiles - 1 - i, 0))
    spans = TILE // SPAN
    big = lambda a: pltpu.VMEM(a.shape, F32)
    shapes = [
        jax.ShapeDtypeStruct((frames, channels), F32),
        jax.ShapeDtypeStruct(convin.shape, BF16),
        jax.ShapeDtypeStruct(mixout.shape, BF16),
        jax.ShapeDtypeStruct(mixin.shape, BF16),
        jax.ShapeDtypeStruct((8, channels), F32),
        jax.ShapeDtypeStruct((STATES, channels), F32),
        jax.ShapeDtypeStruct((STATES, channels), F32),
    ]
    return pl.pallas_call(
        back_kernel,
        grid_spec=pltpu.PrefetchScalarGridSpec(
            num_scalar_prefetch=1,
            grid=(tiles,),
            in_specs=[row(channels), row(2 * channels)]
            + [row(channels)] * 7
            + [pl.BlockSpec((spans, STATES, channels), lambda i, *_: (tiles - 1 - i, 0, 0))]
            + [whole(a.shape) for a in (convin, mixout, mixin, vec, decay, maps)],
            out_specs=[row(channels)] + [whole(s.shape) for s in shapes[1:]],
            scratch_shapes=[
                big(convin),
                big(mixout),
                big(mixin),
                pltpu.VMEM((8, 8, channels), F32),
                pltpu.VMEM((STATES, channels), F32),
                pltpu.VMEM((STATES, channels), F32),
                pltpu.VMEM((STATES, channels), F32),
                pltpu.VMEM((SPAN, STATES, channels), F32),
                pltpu.VMEM((TILE, channels), BF16),
                pltpu.VMEM((TILE, 2 * channels), BF16),
                pltpu.VMEM((TILE, channels), F32),
                pltpu.VMEM((TILE, channels), F32),
            ],
        ),
        out_shape=shapes,
        compiler_params=params(),
        name="back",
    )(flags, gg, p, x2, gx3, gated, y, v, u, x1, hold, convin, mixout, mixin, vec, decay, maps)


def tail_kernel(
    x_ref,
    h_ref,
    gx1_ref,
    up_ref,
    down_ref,
    vec_ref,
    gx_ref,
    gup_out,
    gdown_out,
    gbias_out,
    gvec_out,
    up_acc,
    down_acc,
    bias_acc,
    vec_acc,
    low_scr,
    turn_scr,
    grad_scr,
    sum_scr,
):
    at = pl.program_id(0)
    tiles = pl.num_programs(0)
    channels = x_ref.shape[1]
    hidden = up_ref.shape[1]

    @pl.when(at == 0)
    def _():
        for ref in (up_acc, down_acc, bias_acc, vec_acc):
            ref[...] = jnp.zeros_like(ref)

    def first(rows):
        e, _ = norm_parts(x_ref[rows, :].astype(F32))
        low_scr[rows, :] = (e * vec_ref[0:1, :] + vec_ref[6:7, :]).astype(BF16)
        low = (0.5 * gx1_ref[rows, :]).astype(BF16)
        grad_scr[rows, :] = low
        vec_acc[0] += fold8(low.astype(F32))
        sum_scr[rows, :] = jnp.zeros((ROWS, channels), F32)

    by_rows(first)
    turn_scr[...] = low_scr[...].T
    ffn_back(
        turn_scr,
        None,
        grad_scr,
        lambda cols: h_ref[:, cols].astype(F32),
        up_ref,
        down_ref,
        up_acc,
        down_acc,
        bias_acc,
        sum_scr,
        hidden,
    )

    def second(rows):
        e, inv = norm_parts(x_ref[rows, :].astype(F32))
        grad = sum_scr[rows, :]
        vec_acc[1] += fold8(grad * e)
        vec_acc[2] += fold8(grad)
        gx_ref[rows, :] = gx1_ref[rows, :] + norm_back(grad, e, inv, vec_ref[0:1, :])

    by_rows(second)

    @pl.when(at == tiles - 1)
    def _():
        by_rows(lambda rows: gup_out.__setitem__((rows, slice(None)), up_acc[rows, :].astype(BF16)), channels)
        by_rows(lambda rows: gdown_out.__setitem__((rows, slice(None)), down_acc[rows, :].astype(BF16)), hidden)
        gbias_out[...] = jnp.broadcast_to(jnp.sum(bias_acc[...], axis=0, keepdims=True), gbias_out.shape)
        for k in range(3):
            gvec_out[k : k + 1, :] = jnp.sum(vec_acc[k], axis=0, keepdims=True)


def tail(x, h, gx1, up, down, vec):
    frames, channels = x.shape
    hidden = up.shape[1]
    tiles = frames // TILE
    row = lambda width: pl.BlockSpec((TILE, width), lambda i: (i, 0))
    big = lambda a: pltpu.VMEM(a.shape, F32)
    shapes = [
        jax.ShapeDtypeStruct((frames, channels), F32),
        jax.ShapeDtypeStruct(up.shape, BF16),
        jax.ShapeDtypeStruct(down.shape, BF16),
        jax.ShapeDtypeStruct((8, hidden), F32),
        jax.ShapeDtypeStruct((8, channels), F32),
    ]
    return pl.pallas_call(
        tail_kernel,
        grid=(tiles,),
        in_specs=[row(channels), row(hidden), row(channels)]
        + [whole(a.shape) for a in (up, down, vec)],
        out_specs=[row(channels)] + [whole(s.shape) for s in shapes[1:]],
        out_shape=shapes,
        scratch_shapes=[
            big(up),
            big(down),
            pltpu.VMEM((8, hidden), F32),
            pltpu.VMEM((8, 8, channels), F32),
            pltpu.VMEM((TILE, channels), BF16),
            pltpu.VMEM((channels, TILE), BF16),
            pltpu.VMEM((TILE, channels), BF16),
            pltpu.VMEM((TILE, channels), F32),
        ],
        compiler_params=params(),
        name="tail",
    )(x, h, gx1, up, down, vec)


def pack_small(bias_up, conv_bias, rate, maps, taps, gains, shifts, devices=1):
    layers, hidden = bias_up.shape
    channels = conv_bias.shape[0]
    ratio = hidden // channels
    bias = bias_up.reshape((layers, devices, ratio, channels // devices))
    bias = bias.transpose((0, 2, 1, 3)).reshape((layers * ratio, channels))
    rows = jnp.concatenate(
        [bias, conv_bias[None], rate, maps.reshape((-1, channels)), taps, gains, shifts], axis=0
    )
    rows = jnp.pad(rows, ((0, 256 - rows.shape[0]), (0, 0)))
    return rows.T


def unpack_small(small, devices, layers=2, ratio=4, states=STATES, width=TAPS):
    rows = small.T
    channels = rows.shape[1]
    at = layers * ratio
    bias = rows[:at].reshape((layers, ratio, devices, channels // devices))
    bias = bias.transpose((0, 2, 1, 3)).reshape((layers, ratio * channels))
    out = [bias, rows[at]]
    at += 1
    for count in (states, 2 * states, width, 6, 12):
        out.append(rows[at : at + count])
        at += count
    out[3] = out[3].reshape((2, states, channels))
    return tuple(out)


def state_weights(log_rate, coupling):
    log_decay = -jnp.exp(log_rate)
    input_map = coupling[0] * jnp.sqrt(-jnp.expm1(2.0 * log_decay))
    return jnp.exp(log_decay), input_map * coupling[1]


def on_device(
    n_dp,
    n_fs,
    frames,
    seq_lengths,
    seq_offsets,
    seq_counts,
    ffn_up,
    ffn_down,
    ffn_bias_up,
    mix_in,
    mix_out,
    conv_in,
    conv_out,
    conv_out_bias,
    ssm_rate,
    ssm_map,
    conv_kernel,
    gains,
    shifts,
    cotangent,
):
    devices = n_dp * n_fs
    gathered = gather_all(
        n_dp,
        n_fs,
        [
            pack_small(ffn_bias_up, conv_out_bias, ssm_rate, ssm_map, conv_kernel, gains, shifts)[
                None
            ],
            ffn_up,
            ffn_down,
            mix_in[None],
            mix_out[None],
            conv_in[None],
            conv_out[None],
        ],
        1,
    )
    small, up0, up1, down0, down1, mixin, mixout, convin, convout = [
        g.reshape((-1, g.shape[-1])) for g in gathered
    ]
    bias, conv_bias, rate, maps, taps, gain_set, shift_set = unpack_small(
        small.astype(F32), devices
    )
    frames_dev, channels = frames.shape
    tiles = frames_dev // TILE
    slot = jnp.arange(seq_offsets.shape[1], dtype=jnp.int32)
    begins = (seq_offsets[0][None, :] == TILE * jnp.arange(tiles, dtype=jnp.int32)[:, None]) & (
        slot < seq_counts[0]
    )
    flags = 1 - jnp.max(begins.astype(jnp.int32), axis=1)
    vec = jnp.concatenate([gain_set, shift_set, conv_bias[None], jnp.zeros((5, channels), F32)])
    taps = jnp.pad(taps, ((0, 1), (0, 0)))
    (decay, coupling), weights_back = jax.vjp(state_weights, rate, maps)
    h0, x1, u, v, y, gated, x2, p, hold, w, stat = front(
        flags, frames, up0, down0, mixin, mixout, convin, bias, vec, taps, decay, coupling
    )
    count_all = float(frames_dev * devices)
    center = exchange(n_dp, n_fs, stat[0:1], 2) / devices
    shift_from = stat[0:1] - center
    spread = exchange(n_dp, n_fs, stat[8:9] + frames_dev * shift_from * shift_from, 3)
    scale = lax.rsqrt(spread / count_all + EPSILON)
    stat = jnp.concatenate([center, scale, jnp.zeros((6, channels), F32)])
    result, gx3, gnb, gup1, gdown1, gconvout, gbias1, gvec1 = middle(
        x2, w, cotangent, up1, down1, convout, bias, vec, stat
    )
    sums = exchange(n_dp, n_fs, gvec1[6:8], 4) * (gain_set[5:6] / count_all)
    stat = jnp.concatenate([center, scale, sums[1:2], sums[0:1], jnp.zeros((4, channels), F32)])
    gg, gtaps = conv_back(flags, w, gnb, p, taps, vec, stat)
    gx1, gconvin, gmixout, gmixin, gvec2, gmap, gdecay = back(
        flags, gg, p, x2, gx3, gated, y, v, u, x1, hold, convin, mixout, mixin, vec, decay, coupling
    )
    gx, gup0, gdown0, gbias0, gvec3 = tail(frames, h0, gx1, up0, down0, vec)
    rate_grad, map_grad = weights_back((gdecay, gmap))
    gain_grad = jnp.stack([gvec3[1], gvec2[6], gvec2[2], gvec1[3], gvec1[0], gvec1[6]])
    shift_grad = jnp.stack(
        [
            gvec3[2],
            gvec2[7],
            gvec2[3],
            gvec1[4],
            gvec1[1],
            gvec1[7],
            gvec3[0],
            gvec1[2],
            gvec2[4],
            gvec2[0],
            gvec2[1],
            gvec2[5],
        ]
    )
    small_grad = pack_small(
        jnp.concatenate([gbias0[:1], gbias1[:1]]),
        gvec1[5],
        rate_grad,
        map_grad,
        gtaps[:TAPS],
        gain_grad,
        shift_grad,
        devices,
    ).astype(BF16)
    reduced = scatter_all(
        n_dp,
        n_fs,
        [
            g.reshape((devices, g.shape[0] // devices, g.shape[1]))
            for g in (gup1, gdown1, gconvout, gconvin, gmixout, gmixin, gup0, gdown0, small_grad)
        ],
        5,
    )
    small = unpack_small(reduced[8], 1)
    return (
        result,
        gx,
        jnp.stack([reduced[6], reduced[0]]),
        jnp.stack([reduced[7], reduced[1]]),
        small[0],
        reduced[5],
        reduced[4],
        reduced[3],
        reduced[2],
    ) + small[1:]


def solution(mesh):
    both = ("dp", "fsdp")
    row, row1 = P(both, None), P(both)
    col, col3, mid = P(None, both), P(None, None, both), P(None, both, None)
    in_specs = (
        row,
        row,
        row,
        row1,
        mid,
        mid,
        col,
        row,
        row,
        row,
        row,
        row1,
        col,
        col3,
        col,
        col,
        col,
        row,
    )
    out_specs = (row, row, mid, mid, col, row, row, row, row, row1, col, col3, col, col, col)
    return jax.shard_map(
        partial(on_device, mesh.shape["dp"], mesh.shape["fsdp"]),
        mesh=mesh,
        in_specs=in_specs,
        out_specs=out_specs,
        check_vma=False,
    )
```

```python
import itertools
from functools import partial

import jax
import jax.numpy as jnp
from jax import lax
from jax.experimental import pallas as pl
from jax.experimental.pallas import tpu as pltpu
from jax.sharding import PartitionSpec as P

MESH = pl.DeviceIdType.MESH
BF16 = jnp.bfloat16
F32 = jnp.float32


def flip(index, bit):
    return index + bit * (1 - 2 * lax.rem(lax.div(index, bit), 2))


def flip_all(index, bits):
    for bit in bits:
        index = flip(index, bit)
    return index


def combos(bits):
    found = [()]
    for bit in bits:
        found = found + [entry + (bit,) for entry in found]
    return found


def plan_bits(n_dp):
    bits, bit = [], 2
    while bit < n_dp:
        bits.append(bit)
        bit *= 2
    return tuple(bits)


def greet(dp, fs, n_dp, n_fs):
    barrier = pltpu.get_barrier_semaphore()
    for step in range(1, n_dp):
        pl.semaphore_signal(
            barrier, inc=1, device_id=(lax.rem(dp + step, n_dp), fs), device_id_type=MESH
        )
    for step in range(1, n_fs):
        pl.semaphore_signal(
            barrier, inc=1, device_id=(dp, lax.rem(fs + step, n_fs)), device_id_type=MESH
        )
    pl.semaphore_wait(barrier, n_dp + n_fs - 2)


def gather_plan(dp, fs, n_dp, n_fs, sources, outs, send_sem, recv_sem, local_sem):
    bits = plan_bits(n_dp)
    orders = (bits, bits[::-1])
    half = n_fs // 2
    sends = []

    def stages(chunk):
        src, out = sources[chunk], outs[chunk]
        slots = itertools.count()

        def zone(where, part):
            if part is None:
                return out.at[pl.ds(where * n_fs, n_fs)]
            return out.at[pl.ds(where * n_fs + part * half, half)]

        def remote(slot, view_from, view_to, device):
            return pltpu.make_async_remote_copy(
                src_ref=view_from,
                dst_ref=view_to,
                send_sem=send_sem.at[chunk, slot],
                recv_sem=recv_sem.at[chunk, slot],
                device_id=device,
                device_id_type=MESH,
            )

        def launch(make):
            make().start()
            sends.append(lambda: make().wait_send())

        z_slots = [next(slots) for _ in range(1, n_fs)]

        def own_copy():
            return pltpu.make_async_copy(src, out.at[dp * n_fs + fs], local_sem.at[chunk])

        def start():
            own_copy().start()
            for step in range(1, n_fs):
                launch(
                    lambda step=step: remote(
                        z_slots[step - 1],
                        src,
                        out.at[dp * n_fs + fs],
                        (dp, lax.rem(fs + step, n_fs)),
                    )
                )

        def wait_z():
            own_copy().wait()
            for step in range(1, n_fs):
                origin = dp * n_fs + lax.rem(fs + n_fs - step, n_fs)
                remote(z_slots[step - 1], src, out.at[origin], (dp, fs)).wait_recv()

        steps, before = [start], wait_z
        for depth in range(len(bits)):
            plan = []
            for part, order in enumerate(orders):
                for entry in combos(order[:depth]):
                    plan.append((next(slots), part, order[depth], entry))

            def view(slot, part, bit, entry, arrived):
                where = flip_all(flip(dp, bit) if arrived else dp, entry)
                return remote(slot, zone(where, part), zone(where, part), (flip(dp, bit), fs))

            def go(plan=plan, before=before, view=view):
                before()
                for item in plan:
                    launch(lambda item=item: view(*item, False))

            def arrive(plan=plan, view=view):
                for item in plan:
                    view(*item, True).wait_recv()

            steps.append(go)
            before = arrive
        last = [(next(slots), entry) for entry in combos(bits)]

        def across(slot, entry, arrived):
            where = flip_all(flip(dp, 1) if arrived else dp, entry)
            return remote(slot, zone(where, None), zone(where, None), (flip(dp, 1), fs))

        def cross(before=before):
            before()
            for item in last:
                launch(lambda item=item: across(*item, False))

        def finish():
            for item in last:
                across(*item, True).wait_recv()

        return steps + [cross, finish]

    return [stages(chunk) for chunk in range(len(outs))], sends


def waves(plans):
    depth = len(plans[0])
    out = []
    for wave in range(len(plans) + depth - 1):
        out.append(
            [plans[c][wave - c] for c in range(len(plans)) if 0 <= wave - c < depth]
        )
    return out


def gather_kernel(n_dp, n_fs, layers, *refs):
    n_in = len(layers)
    n_out = sum(layers)
    ins, outs = refs[:n_in], refs[n_in : n_in + n_out]
    send_sem, recv_sem, local_sem = refs[n_in + n_out :]
    sources = []
    for ref, count in zip(ins, layers):
        sources += [ref.at[layer] for layer in range(count)]
    dp, fs = lax.axis_index("dp"), lax.axis_index("fsdp")
    greet(dp, fs, n_dp, n_fs)
    plans, sends = gather_plan(dp, fs, n_dp, n_fs, sources, outs, send_sem, recv_sem, local_sem)
    for wave in waves(plans):
        for stage in wave:
            stage()
    for wait in sends:
        wait()


def slot_count(n_dp, n_fs):
    nb = len(plan_bits(n_dp))
    return n_fs - 1 + 2 * (2**nb - 1) + 2**nb


def gather_all(n_dp, n_fs, arrays, collective_id):
    layers = tuple(a.shape[0] for a in arrays)
    outs = []
    for a in arrays:
        outs += [jax.ShapeDtypeStruct((n_dp * n_fs,) + a.shape[1:], a.dtype)] * a.shape[0]
    count = slot_count(n_dp, n_fs)
    return pl.pallas_call(
        partial(gather_kernel, n_dp, n_fs, layers),
        out_shape=outs,
        in_specs=[pl.BlockSpec(memory_space=pltpu.HBM)] * len(arrays),
        out_specs=[pl.BlockSpec(memory_space=pltpu.HBM)] * len(outs),
        scratch_shapes=[
            pltpu.SemaphoreType.DMA((len(outs), count)),
            pltpu.SemaphoreType.DMA((len(outs), count)),
            pltpu.SemaphoreType.DMA((len(outs),)),
        ],
        compiler_params=pltpu.CompilerParams(collective_id=collective_id, has_side_effects=True),
        name="gather_parameters",
    )(*arrays)


def scatter_plan(dp, fs, n_dp, n_fs, ins, emit, scratch, send_sem, recv_sem, local_sem, first=0):
    bits = plan_bits(n_dp)
    orders = (bits[::-1], bits)
    half = n_fs // 2
    index = {entry: at for at, entry in enumerate(combos(bits))}
    sends = []

    def add_into(kept, other):
        def body(at, _):
            kept[at] = (kept[at].astype(F32) + other[at].astype(F32)).astype(BF16)
            return 0

        lax.fori_loop(0, kept.shape[0], body, 0)

    def stages(chunk):
        src = ins[chunk]
        cross_in, own, later, last = scratch[4 * chunk : 4 * chunk + 4]
        slots = itertools.count()

        def remote(slot, view_from, view_to, device):
            return pltpu.make_async_remote_copy(
                src_ref=view_from,
                dst_ref=view_to,
                send_sem=send_sem.at[first + chunk, slot],
                recv_sem=recv_sem.at[first + chunk, slot],
                device_id=device,
                device_id_type=MESH,
            )

        def launch(make):
            make().start()
            sends.append(lambda: make().wait_send())

        def zone(entry, crossed):
            return src.at[pl.ds(flip_all(flip(dp, 1) if crossed else dp, entry) * n_fs, n_fs)]

        pieces = [(next(slots), entry, index[entry]) for entry in combos(bits)]

        def load(entry, at):
            return pltpu.make_async_copy(
                zone(entry, False), own.at[at], local_sem.at[first + chunk, at]
            )

        def across(slot, entry, at):
            return remote(slot, zone(entry, True), cross_in.at[at], (flip(dp, 1), fs))

        def start():
            for item in pieces:
                launch(lambda item=item: across(*item))
            for _, entry, at in pieces:
                load(entry, at).start()

        def fold_cross():
            for slot, entry, at in pieces:
                load(entry, at).wait()
                across(slot, entry, at).wait_recv()
                add_into(own.at[at], cross_in.at[at])

        steps, before = [start], fold_cross
        used = 0
        for depth in range(len(bits)):
            plan = []
            for part, order in enumerate(orders):
                bit, gone = order[depth], order[:depth]
                for entry in combos(bits):
                    if not (set(entry) & set(gone)) and bit not in entry:
                        away = tuple(sorted(entry + (bit,)))
                        plan.append((next(slots), part, bit, index[away], index[entry], used))
                        used += 1

            def move(slot, part, bit, away, kept, place):
                return remote(
                    slot,
                    own.at[away, pl.ds(part * half, half)],
                    later.at[place],
                    (flip(dp, bit), fs),
                )

            def go(plan=plan, before=before, move=move):
                before()
                for item in plan:
                    launch(lambda item=item: move(*item))

            def fold(plan=plan, move=move):
                for item in plan:
                    move(*item).wait_recv()
                    _, part, _, _, kept, place = item
                    add_into(own.at[kept, pl.ds(part * half, half)], later.at[place])

            steps.append(go)
            before = fold
        z_slots = [next(slots) for _ in range(1, n_fs)]

        def along(step):
            to = lax.rem(fs + step, n_fs)
            return remote(z_slots[step - 1], own.at[0, to], last.at[step - 1], (dp, to))

        def spread(before=before):
            before()
            for step in range(1, n_fs):
                launch(lambda step=step: along(step))

        def finish():
            total = own[0, fs].astype(F32)
            for step in range(1, n_fs):
                along(step).wait_recv()
                total = total + last[step - 1].astype(F32)
            emit(chunk, total)

        return steps + [spread, finish]

    return [stages(chunk) for chunk in range(len(ins))], sends


def scatter_scratch(n_dp, n_fs, tails):
    pieces = 2 ** len(plan_bits(n_dp))
    scratch = []
    for tail in tails:
        scratch += [
            pltpu.VMEM((pieces, n_fs) + tail, BF16),
            pltpu.VMEM((pieces, n_fs) + tail, BF16),
            pltpu.VMEM((2 * (pieces - 1), n_fs // 2) + tail, BF16),
            pltpu.VMEM((n_fs - 1,) + tail, BF16),
        ]
    return scratch


def scatter_sems(n_dp, n_fs, chunks):
    count = slot_count(n_dp, n_fs)
    return [
        pltpu.SemaphoreType.DMA((chunks, count)),
        pltpu.SemaphoreType.DMA((chunks, count)),
        pltpu.SemaphoreType.DMA((chunks, 2 ** len(plan_bits(n_dp)))),
    ]


def scatter_kernel(n_dp, n_fs, n_chunks, *refs):
    ins, outs = refs[:n_chunks], refs[n_chunks : 2 * n_chunks]
    scratch = refs[2 * n_chunks : 6 * n_chunks]
    dp, fs = lax.axis_index("dp"), lax.axis_index("fsdp")
    greet(dp, fs, n_dp, n_fs)

    def emit(chunk, total):
        outs[chunk][...] = total

    plans, sends = scatter_plan(dp, fs, n_dp, n_fs, ins, emit, scratch, *refs[6 * n_chunks :])
    for wave in waves(plans):
        for stage in wave:
            stage()
    for wait in sends:
        wait()


def scatter_all(n_dp, n_fs, arrays, collective_id):
    n = len(arrays)
    return pl.pallas_call(
        partial(scatter_kernel, n_dp, n_fs, n),
        out_shape=[jax.ShapeDtypeStruct(a.shape[1:], F32) for a in arrays],
        in_specs=[pl.BlockSpec(memory_space=pltpu.HBM)] * n,
        out_specs=[pl.BlockSpec(memory_space=pltpu.VMEM)] * n,
        scratch_shapes=scatter_scratch(n_dp, n_fs, [a.shape[1:] for a in arrays])
        + scatter_sems(n_dp, n_fs, n),
        compiler_params=pltpu.CompilerParams(
            collective_id=collective_id, has_side_effects=True, vmem_limit_bytes=48 << 20
        ),
        name="scatter_gradients",
    )(*arrays)


def swap_rows(axis, place, count, buffer, send_sem, recv_sem):
    def make(step):
        return pltpu.make_async_remote_copy(
            src_ref=buffer.at[0],
            dst_ref=buffer.at[step],
            send_sem=send_sem.at[step],
            recv_sem=recv_sem.at[step],
            device_id={axis: lax.rem(place + step, count)},
            device_id_type=MESH,
        )

    for step in range(1, count):
        make(step).start()
    for step in range(1, count):
        make(step).wait_recv()
    for step in range(1, count):
        make(step).wait_send()


def sum_over(x, dp, fs, n_dp, n_fs, octet, line, send_sem, recv_sem):
    octet[0] = x
    swap_rows("dp", dp, n_dp, octet, send_sem.at[0], recv_sem.at[0])
    total = octet[0]
    for step in range(1, n_dp):
        total = total + octet[step]
    line[0] = total
    swap_rows("fsdp", fs, n_fs, line, send_sem.at[1], recv_sem.at[1])
    total = line[0]
    for step in range(1, n_fs):
        total = total + line[step]
    return total


def pooled(buffer, count, weight):
    means = [buffer[k, 0:1, :] for k in range(count)]
    center = sum(means[1:], means[0]) * (1.0 / count)
    spread = buffer[0, 1:2, :]
    for k in range(1, count):
        spread = spread + buffer[k, 1:2, :]
    off = (means[0] - center) * (means[0] - center)
    for mean in means[1:]:
        off = off + (mean - center) * (mean - center)
    return center, spread + weight * off


def pool_over(center, spread, frames, dp, fs, n_dp, n_fs, octet, line, send_sem, recv_sem):
    octet[0] = jnp.zeros(octet.shape[1:], F32)
    line[0] = jnp.zeros(line.shape[1:], F32)
    octet[0, 0:1, :] = center
    octet[0, 1:2, :] = spread
    swap_rows("dp", dp, n_dp, octet, send_sem.at[0], recv_sem.at[0])
    center, spread = pooled(octet, n_dp, float(frames))
    line[0, 0:1, :] = center
    line[0, 1:2, :] = spread
    swap_rows("fsdp", fs, n_fs, line, send_sem.at[1], recv_sem.at[1])
    return pooled(line, n_fs, float(frames * n_dp))


def swap_scratch(n_dp, n_fs, channels):
    return [
        pltpu.VMEM((n_dp, 8, channels), F32),
        pltpu.VMEM((n_fs, 8, channels), F32),
        pltpu.SemaphoreType.DMA((2, max(n_dp, n_fs))),
        pltpu.SemaphoreType.DMA((2, max(n_dp, n_fs))),
    ]


def pool_kernel(n_dp, n_fs, frames, x_ref, out_ref, octet, line, send_sem, recv_sem):
    dp, fs = lax.axis_index("dp"), lax.axis_index("fsdp")
    greet(dp, fs, n_dp, n_fs)
    octet[0] = x_ref[...]
    center, spread = pool_over(
        x_ref[0:1, :], x_ref[1:2, :], frames, dp, fs, n_dp, n_fs, octet, line, send_sem, recv_sem
    )
    out_ref[...] = x_ref[...]
    out_ref[0:1, :] = center
    out_ref[1:2, :] = spread


def total_kernel(n_dp, n_fs, frames, x_ref, out_ref, octet, line, send_sem, recv_sem):
    dp, fs = lax.axis_index("dp"), lax.axis_index("fsdp")
    greet(dp, fs, n_dp, n_fs)
    out_ref[...] = sum_over(x_ref[...], dp, fs, n_dp, n_fs, octet, line, send_sem, recv_sem)


def exchange(n_dp, n_fs, x, frames, collective_id, kernel):
    return pl.pallas_call(
        partial(kernel, n_dp, n_fs, frames),
        out_shape=jax.ShapeDtypeStruct(x.shape, F32),
        in_specs=[pl.BlockSpec(memory_space=pltpu.VMEM)],
        out_specs=pl.BlockSpec(memory_space=pltpu.VMEM),
        scratch_shapes=swap_scratch(n_dp, n_fs, x.shape[1]),
        compiler_params=pltpu.CompilerParams(collective_id=collective_id, has_side_effects=True),
        name="exchange_rows",
    )(x)


TILE = 512
STATES = 32
TAPS = 15
REACH = 8
EPSILON = 1e-05
CHUNK = 256
ROWS = 128
SPAN = 32
VMEM_LIMIT = 60 << 20
TAP_ROW = 24
RATE = 40
MAP_IN = 72
MAP_OUT = 104
TABLE = 136


def sigmoid(v):
    return 0.5 * jnp.tanh(0.5 * v) + 0.5


def dot_nn(a, b):
    return jnp.dot(a, b, preferred_element_type=F32)


def dot_nt(a, b):
    return lax.dot_general(a, b, (((1,), (1,)), ((), ())), preferred_element_type=F32)


def dot_tn(a, b):
    return lax.dot_general(a, b, (((0,), (0,)), ((), ())), preferred_element_type=F32)


def norm_parts(v):
    centered = v - jnp.mean(v, axis=-1, keepdims=True)
    inv = lax.rsqrt(jnp.mean(centered * centered, axis=-1, keepdims=True) + EPSILON)
    return centered * inv, inv


def norm_back(grad, e, inv, gain):
    d = grad * gain
    return (
        d - jnp.mean(d, axis=-1, keepdims=True) - e * jnp.mean(d * e, axis=-1, keepdims=True)
    ) * inv


def fold8(v):
    return jnp.sum(v.reshape((v.shape[0] // 8, 8, v.shape[1])), axis=0)


def by_rows(body, rows=TILE, step=ROWS):
    def run(at, _):
        body(pl.ds(pl.multiple_of(at * step, step), step))
        return 0

    lax.fori_loop(0, rows // step, run, 0)


def columns(at, width=CHUNK):
    return pl.ds(pl.multiple_of(at * width, width), width)


def merge_rows(parts, low_half):
    for distance in (1, 2, 4):
        low = low_half[distance]
        parts = [
            jnp.where(low, a, b) + pltpu.roll(jnp.where(low, b, a), distance, 0)
            for a, b in zip(parts[0::2], parts[1::2])
        ]
    return parts[0]


def half_masks(width):
    row = lax.broadcasted_iota(jnp.int32, (8, width), 0)
    return {d: (row // d) % 2 == 0 for d in (4, 2, 1)}


def fold_states(v):
    return jnp.sum(v.reshape((STATES // 8, 8, v.shape[1])), axis=0)


def fill_halo(padded, flags_ref, tiles):
    pitch = TILE + 2 * REACH
    for at in range(tiles):
        base = at * pitch
        if at == 0:
            padded[:, base : base + REACH, :] = jnp.zeros_like(padded[:, base : base + REACH, :])
        if at == tiles - 1:
            end = base + REACH + TILE
            padded[:, end : end + REACH, :] = jnp.zeros_like(padded[:, end : end + REACH, :])
        else:
            keep = flags_ref[at + 1].astype(F32)
            end = base + REACH + TILE
            padded[:, end : end + REACH, :] = (
                padded[:, base + pitch + REACH : base + pitch + 2 * REACH, :] * keep
            )
            padded[:, base + pitch : base + pitch + REACH, :] = (
                padded[:, end - REACH : end, :] * keep
            )


def taps_over(padded, table_ref, store, tiles, reverse, block=64):
    pitch = TILE + 2 * REACH
    per = TILE // block
    lanes = padded.shape[0]
    for lane in range(lanes):
        weights = [
            jnp.broadcast_to(
                table_ref[TAP_ROW + k : TAP_ROW + k + 1, lane * 128 : lane * 128 + 128], (block, 128)
            )
            for k in range(TAPS)
        ]

        def run(at, _):
            tile, inner = at // per, at % per
            base = tile * pitch + inner * block
            total = jnp.zeros((block, 128), F32)
            for k in range(TAPS):
                shift = REACH + (TAPS // 2 - k if reverse else k - TAPS // 2)
                total = total + weights[k] * padded[lane, pl.ds(base + shift, block), :]
            store(lane, tile * TILE + inner * block, base, total)
            return 0

        lax.fori_loop(0, tiles * per, run, 0)


def small_exp(v):
    return 1.0 + v * (1.0 + v * (0.5 + v * (1.0 / 6 + v * (1.0 / 24 + v * (1.0 / 120)))))


def small_expm1_over(v):
    return 1.0 + v * (
        0.5 + v * (1.0 / 6 + v * (1.0 / 24 + v * (1.0 / 120 + v * (1.0 / 720 + v * (1.0 / 5040)))))
    )


def state_terms(table_ref):
    log_decay = -jnp.exp(table_ref[RATE : RATE + STATES, :])
    root = jnp.sqrt(-2.0 * log_decay * small_expm1_over(2.0 * log_decay))
    maps_in = table_ref[MAP_IN : MAP_IN + STATES, :]
    maps_out = table_ref[MAP_OUT : MAP_OUT + STATES, :]
    return log_decay, small_exp(log_decay), root, maps_in, maps_out


def ref_rows(ref):
    return ref.reshape((ref.shape[0] * ref.shape[1], ref.shape[2]))


WEIGHTS = 6


def front_kernel(mesh_size, *refs):
    fused = mesh_size is not None
    refs = list(refs)
    take = lambda count: [refs.pop(0) for _ in range(count)]
    flags_ref, x_ref = take(2)
    if fused:
        n_dp, n_fs = mesh_size
        shards = take(7)
    else:
        up_ref, down_ref, mixin_ref, mixout_ref, convin_ref, table_in, bias_in = take(7)
    (
        h_out,
        x1_out,
        u_out,
        v_out,
        y_out,
        gated_out,
        x2_out,
        p_out,
        hold_out,
        w_out,
        stat_out,
        table_ref,
        bias_ref,
        decay_ref,
        map_ref,
    ) = take(15)
    gathered = take(9) if fused else []
    x1_scr, low_all, low_scr, sum_scr, state_scr, padded = take(6)
    step = pl.program_id(0)
    channels = x_ref.shape[1]
    frames = w_out.shape[0]
    tiles = frames // TILE
    lanes = channels // 128
    gain = lambda k: table_ref[k : k + 1, :]
    shift = lambda k: table_ref[6 + k : 7 + k, :]
    here = lambda rows, tile: pl.ds(pl.multiple_of(tile * TILE + rows.start, ROWS), ROWS)
    if fused:
        small_v, up_v, down_v, mixin_v, mixout_v, convin_v = take(WEIGHTS)
        send_sem, recv_sem, local_sem, load_sem = take(4)
        swap = take(4)
        dp, fs = lax.axis_index("dp"), lax.axis_index("fsdp")
        small_s, up_s, down_s, mixin_s, mixout_s, convin_s, convout_s = shards
        sources = [
            small_s.at[0],
            up_s.at[0],
            down_s.at[0],
            mixin_s.at[0],
            mixout_s.at[0],
            convin_s.at[0],
            convout_s.at[0],
            up_s.at[1],
            down_s.at[1],
        ]
        plans, sends = gather_plan(
            dp, fs, n_dp, n_fs, sources, gathered, send_sem, recv_sem, local_sem
        )
        order = waves(plans)
        ready = len(plans[0]) + 2
        held = (small_v, up_v, down_v, mixin_v, mixout_v, convin_v)

        def load(chunk):
            return pltpu.make_async_copy(gathered[chunk], held[chunk], load_sem.at[chunk])

        up_ref, down_ref, mixin_ref, mixout_ref, convin_ref = [ref_rows(r) for r in held[1:]]

        @pl.when(step == 0)
        def _():
            greet(dp, fs, n_dp, n_fs)
            for wave in order[:ready]:
                for stage in wave:
                    stage()
            for chunk in range(3):
                load(chunk).start()
            load(0).wait()
            table_ref[...] = ref_rows(small_v)[:, :256].astype(F32).T[: table_ref.shape[0], :]
            total = small_v[0, :, 256:].astype(F32)
            for k in range(1, n_dp * n_fs):
                total = total + small_v[k, :, 256:].astype(F32)
            bias_ref[...] = total
            load(1).wait()
            load(2).wait()

        for k in range(1, tiles + 1):

            @pl.when(step == k)
            def _(k=k):
                for stage in order[ready + k - 1]:
                    stage()
                if k == tiles:
                    for chunk in range(3, 6):
                        load(chunk).start()
                    for chunk in range(3, 6):
                        load(chunk).wait()

        rest = order[ready + tiles :]
        for k in range(tiles):

            @pl.when(step == tiles + 1 + k)
            def _(k=k):
                for wave in rest[k :: tiles] if k < tiles - 1 else rest[k:]:
                    for stage in wave:
                        stage()
                if k == tiles - 1:
                    for wait in sends:
                        wait()

    else:

        @pl.when(step == 0)
        def _():
            table_ref[...] = table_in[...]
            bias_ref[...] = bias_in[...]

    @pl.when(step == 0)
    def _():
        _, decay, root, maps_in, maps_out = state_terms(table_ref)
        decay_ref[...] = decay
        map_ref[...] = maps_in * root * maps_out
        state_scr[...] = jnp.zeros_like(state_scr)

    @pl.when(step < tiles)
    def _():
        def first(rows):
            e, _ = norm_parts(x_ref[rows, :].astype(F32))
            low_scr[rows, :] = (e * gain(0) + shift(0)).astype(BF16)
            sum_scr[rows, :] = jnp.zeros((ROWS, channels), F32)

        by_rows(first)

        def hidden(c, _):
            cols = columns(c)
            h = dot_nn(low_scr[...], up_ref[:, cols]) + bias_ref[pl.ds(c, 1), :]
            h_out[:, cols] = h.astype(BF16)
            active = (h * sigmoid(h)).astype(BF16)
            sum_scr[...] += dot_nn(active, down_ref[cols, :])
            return 0

        lax.fori_loop(0, up_ref.shape[1] // CHUNK, hidden, 0)

        def second(rows):
            x1 = x_ref[rows, :].astype(F32) + 0.5 * (sum_scr[rows, :] + shift(6))
            x1_out[rows, :] = x1
            x1_scr[here(rows, step), :] = x1
            e, _ = norm_parts(x1)
            low_all[here(rows, step), :] = (e * gain(1) + shift(1)).astype(BF16)

        by_rows(second)

    @pl.when((step >= tiles) & (step < 2 * tiles))
    def _():
        at = step - tiles
        whole_tile = pl.ds(pl.multiple_of(at * TILE, TILE), TILE)

        def project(c, _):
            cols = columns(c)
            right = columns(c + channels // CHUNK)
            u_out[:, cols] = dot_nn(low_all[whole_tile, :], mixin_ref[:, cols])
            v_out[:, cols] = dot_nn(low_all[whole_tile, :], mixin_ref[:, right]).astype(BF16)
            return 0

        lax.fori_loop(0, channels // CHUNK, project, 0)
        low_half = half_masks(128)
        state_scr[...] = state_scr[...] * flags_ref[at].astype(F32)

        def scan_span(span, _):
            hold_out[span] = state_scr[...]

            def scan(block, _):
                start = pl.multiple_of(span * SPAN + block * 8, 8)
                for lane in range(lanes):
                    cols = slice(lane * 128, lane * 128 + 128)
                    state = state_scr[:, cols]
                    decay = decay_ref[:, cols]
                    maps = map_ref[:, cols]
                    drive = u_out[pl.ds(start, 8), cols]
                    parts = []
                    for j in range(8):
                        state = decay * state + jnp.broadcast_to(drive[j : j + 1, :], (STATES, 128))
                        parts.append(fold_states(maps * state))
                    state_scr[:, cols] = state
                    sum_scr[pl.ds(start, 8), cols] = merge_rows(parts, low_half)
                return 0

            lax.fori_loop(0, SPAN // 8, scan, 0)
            return 0

        lax.fori_loop(0, TILE // SPAN, scan_span, 0)

        def gate(rows):
            y = sum_scr[rows, :] + shift(11) * u_out[rows, :]
            v = v_out[rows, :].astype(F32)
            y_out[rows, :] = y.astype(BF16)
            gated_out[rows, :] = (y * (v * sigmoid(v))).astype(BF16)

        by_rows(gate)
        sum_scr[...] = dot_nn(gated_out[...], mixout_ref[...])

        def third(rows):
            x2 = x1_scr[here(rows, at), :] + (sum_scr[rows, :] + shift(8))
            x2_out[rows, :] = x2
            e, _ = norm_parts(x2)
            low_scr[rows, :] = (e * gain(2) + shift(2)).astype(BF16)

        by_rows(third)
        pitch = TILE + 2 * REACH

        def widen(c, _):
            cols = columns(c)
            right = columns(c + channels // CHUNK)
            left_part = dot_nn(low_scr[...], convin_ref[:, cols]) + table_ref[15:16, cols]
            right_part = dot_nn(low_scr[...], convin_ref[:, right]) + table_ref[16:17, cols]
            p_out[:, cols] = left_part.astype(BF16)
            p_out[:, right] = right_part.astype(BF16)
            g = left_part * sigmoid(right_part)
            place = pl.ds(pl.multiple_of(at * pitch + REACH, 8), TILE)
            for k in range(CHUNK // 128):
                padded[c * (CHUNK // 128) + k, place, :] = g[:, k * 128 : k * 128 + 128]
            return 0

        lax.fori_loop(0, channels // CHUNK, widen, 0)

    @pl.when(step == 2 * tiles)
    def _():
        fill_halo(padded, flags_ref, tiles)

        def store(lane, row, base, total):
            w_out[pl.ds(pl.multiple_of(row, 64), 64), lane * 128 : lane * 128 + 128] = total

        taps_over(padded, table_ref, store, tiles, False)
        stat_out[...] = jnp.zeros_like(stat_out)

        def total(at, _):
            rows = pl.ds(pl.multiple_of(at * ROWS, ROWS), ROWS)
            stat_out[...] += fold8(w_out[rows, :])
            return 0

        lax.fori_loop(0, frames // ROWS, total, 0)
        center = jnp.sum(stat_out[...], axis=0, keepdims=True) * (1.0 / frames)
        stat_out[...] = jnp.zeros_like(stat_out)

        def spread(at, _):
            rows = pl.ds(pl.multiple_of(at * ROWS, ROWS), ROWS)
            off = w_out[rows, :] - center
            stat_out[...] += fold8(off * off)
            return 0

        lax.fori_loop(0, frames // ROWS, spread, 0)
        around = jnp.sum(stat_out[...], axis=0, keepdims=True)
        if fused:
            center, around = pool_over(center, around, frames, dp, fs, n_dp, n_fs, *swap)
            around = lax.rsqrt(around * (1.0 / (frames * n_dp * n_fs)) + EPSILON)
        stat_out[...] = jnp.zeros_like(stat_out)
        stat_out[0:1, :] = center
        stat_out[1:2, :] = around


def whole(shape):
    zeros = (0,) * len(shape)
    return pl.BlockSpec(shape, lambda *_: zeros)


def params(collective_id=None):
    if collective_id is None:
        return pltpu.CompilerParams(
            dimension_semantics=("arbitrary",), vmem_limit_bytes=VMEM_LIMIT
        )
    return pltpu.CompilerParams(
        dimension_semantics=("arbitrary",),
        vmem_limit_bytes=VMEM_LIMIT,
        collective_id=collective_id,
        has_side_effects=True,
    )


def front(mesh_size, flags, x, weights, collective_id=None):
    fused = mesh_size is not None
    frames, channels = x.shape
    hidden = weights[1].shape[-1] if fused else weights[0].shape[1]
    tiles = frames // TILE
    early = lambda width: pl.BlockSpec((TILE, width), lambda i: (jnp.minimum(i, tiles - 1), 0))
    place = lambda i: jnp.clip(i - tiles, 0, tiles - 1)
    late = lambda width: pl.BlockSpec((TILE, width), lambda i: (place(i), 0))
    shape = lambda width, kind: jax.ShapeDtypeStruct((frames, width), kind)
    spans = TILE // SPAN
    state = jax.ShapeDtypeStruct((STATES, channels), F32)
    out_shape = [
        shape(hidden, BF16),
        shape(channels, F32),
        shape(channels, F32),
        shape(channels, BF16),
        shape(channels, BF16),
        shape(channels, BF16),
        shape(channels, F32),
        shape(2 * channels, BF16),
        jax.ShapeDtypeStruct((frames // SPAN, STATES, channels), F32),
        shape(channels, F32),
        jax.ShapeDtypeStruct((8, channels), F32),
        jax.ShapeDtypeStruct((TABLE, channels), F32),
        jax.ShapeDtypeStruct((16, CHUNK), F32),
        state,
        state,
    ]
    out_specs = [early(hidden), early(channels)]
    out_specs += [late(channels)] * 5
    out_specs += [
        late(2 * channels),
        pl.BlockSpec((spans, STATES, channels), lambda i: (place(i), 0, 0)),
    ]
    out_specs += [whole(s.shape) for s in out_shape[9:]]
    scratch = [
        pltpu.VMEM((frames, channels), F32),
        pltpu.VMEM((frames, channels), BF16),
        pltpu.VMEM((TILE, channels), BF16),
        pltpu.VMEM((TILE, channels), F32),
        pltpu.VMEM((STATES, channels), F32),
        pltpu.VMEM((channels // 128, tiles * (TILE + 2 * REACH), 128), F32),
    ]
    in_specs = [pl.BlockSpec(memory_space=pltpu.SMEM), early(channels)]
    if fused:
        n_dp, n_fs = mesh_size
        hbm = pl.BlockSpec(memory_space=pltpu.HBM)
        in_specs += [hbm] * len(weights)
        chunks = []
        for at in (0, 1, 2, 3, 4, 5, 6, 1, 2):
            chunks.append(jax.ShapeDtypeStruct((n_dp * n_fs,) + weights[at].shape[1:], BF16))
        out_shape += chunks
        out_specs += [hbm] * len(chunks)
        scratch += [pltpu.VMEM(c.shape, BF16) for c in chunks[:WEIGHTS]]
        count = slot_count(n_dp, n_fs)
        scratch += [
            pltpu.SemaphoreType.DMA((len(chunks), count)),
            pltpu.SemaphoreType.DMA((len(chunks), count)),
            pltpu.SemaphoreType.DMA((len(chunks),)),
            pltpu.SemaphoreType.DMA((WEIGHTS,)),
        ]
        scratch += swap_scratch(n_dp, n_fs, channels)
    else:
        in_specs += [whole(a.shape) for a in weights]
    return pl.pallas_call(
        partial(front_kernel, mesh_size),
        grid=(2 * tiles + 1,),
        in_specs=in_specs,
        out_specs=out_specs,
        out_shape=out_shape,
        scratch_shapes=scratch,
        compiler_params=params(collective_id),
        name="front",
    )(flags, x, *weights)


def ffn_back(low_t, grad_t, grad_ref, h_load, up_ref, down_ref, up_acc, down_acc, bias_acc, back_scr, hidden):
    def chunk(c, _):
        cols = columns(c)
        h = h_load(cols)
        sig = sigmoid(h)
        active = h * sig
        gate = dot_nt(grad_ref[...], down_ref[cols, :])
        grad_h = (gate * (sig * (1.0 + h - active))).astype(BF16)
        bias_acc[:, cols] += fold8(grad_h.astype(F32))
        down_acc[cols, :] += dot_tn(active.astype(BF16), grad_ref[...])
        up_acc[:, cols] += dot_nn(low_t[...], grad_h)
        back_scr[...] += dot_nt(grad_h, up_ref[:, cols])
        return 0

    lax.fori_loop(0, hidden // CHUNK, chunk, 0)


def middle_kernel(
    x2_ref,
    w_ref,
    cot_ref,
    up_ref,
    down_ref,
    convout_ref,
    bias_ref,
    vec_ref,
    stat_ref,
    out_ref,
    gx3_ref,
    gnb_ref,
    gup_out,
    gdown_out,
    gconvout_out,
    gbias_out,
    gvec_out,
    up_acc,
    down_acc,
    convout_acc,
    bias_acc,
    vec_acc,
    h_scr,
    low_scr,
    turn_scr,
    act_scr,
    grad_scr,
    sum_scr,
    x3_scr,
):
    at = pl.program_id(0)
    tiles = pl.num_programs(0)
    channels = x2_ref.shape[1]
    hidden = up_ref.shape[1]
    gain = lambda k: vec_ref[k : k + 1, :]
    shift = lambda k: vec_ref[6 + k : 7 + k, :]
    center, scale = stat_ref[0:1, :], stat_ref[1:2, :]

    @pl.when(at == 0)
    def _():
        for ref in (up_acc, down_acc, convout_acc, bias_acc, vec_acc):
            ref[...] = jnp.zeros_like(ref)

    def normed(rows):
        e = (w_ref[rows, :] - center) * scale
        return e, e * gain(5) + shift(5)

    def first(rows):
        _, nb = normed(rows)
        act_scr[rows, :] = (nb * sigmoid(nb)).astype(BF16)

    by_rows(first)
    sum_scr[...] = dot_nn(act_scr[...], convout_ref[...])

    def second(rows):
        x3 = x2_ref[rows, :] + (sum_scr[rows, :] + vec_ref[18:19, :])
        x3_scr[rows, :] = x3
        e, _ = norm_parts(x3)
        low_scr[rows, :] = (e * gain(3) + shift(3)).astype(BF16)
        sum_scr[rows, :] = jnp.zeros((ROWS, channels), F32)

    by_rows(second)

    def forward(c, _):
        cols = columns(c)
        h = dot_nn(low_scr[...], up_ref[:, cols]) + bias_ref[pl.ds(8 + c, 1), :]
        h_scr[:, cols] = h
        active = (h * sigmoid(h)).astype(BF16)
        sum_scr[...] += dot_nn(active, down_ref[cols, :])
        return 0

    lax.fori_loop(0, hidden // CHUNK, forward, 0)
    turn_scr[...] = low_scr[...].T

    def last(rows):
        x4 = x3_scr[rows, :] + 0.5 * (sum_scr[rows, :] + shift(7))
        e, inv = norm_parts(x4)
        out_ref[rows, :] = (e * gain(4) + shift(4)).astype(BF16)
        cot = cot_ref[rows, :].astype(F32)
        vec_acc[0] += fold8(cot * e)
        vec_acc[1] += fold8(cot)
        gx4 = norm_back(cot, e, inv, gain(4))
        gx3_ref[rows, :] = gx4
        low = (0.5 * gx4).astype(BF16)
        grad_scr[rows, :] = low
        vec_acc[2] += fold8(low.astype(F32))
        sum_scr[rows, :] = jnp.zeros((ROWS, channels), F32)

    by_rows(last)
    ffn_back(
        turn_scr,
        None,
        grad_scr,
        lambda cols: h_scr[:, cols],
        up_ref,
        down_ref,
        up_acc,
        down_acc,
        bias_acc,
        sum_scr,
        hidden,
    )

    def fourth(rows):
        e, inv = norm_parts(x3_scr[rows, :])
        grad = sum_scr[rows, :]
        vec_acc[3] += fold8(grad * e)
        vec_acc[4] += fold8(grad)
        gx3 = gx3_ref[rows, :] + norm_back(grad, e, inv, gain(3))
        gx3_ref[rows, :] = gx3
        low = gx3.astype(BF16)
        grad_scr[rows, :] = low
        vec_acc[5] += fold8(low.astype(F32))

    by_rows(fourth)
    convout_acc[...] += dot_tn(act_scr[...], grad_scr[...])
    sum_scr[...] = dot_nt(grad_scr[...], convout_ref[...])

    def fifth(rows):
        e, nb = normed(rows)
        sig = sigmoid(nb)
        gnb = sum_scr[rows, :] * (sig * (1.0 + nb * (1.0 - sig)))
        gnb_ref[rows, :] = gnb
        vec_acc[6] += fold8(gnb * e)
        vec_acc[7] += fold8(gnb)

    by_rows(fifth)

    @pl.when(at == tiles - 1)
    def _():
        by_rows(lambda rows: gup_out.__setitem__((rows, slice(None)), up_acc[rows, :].astype(BF16)), channels)
        by_rows(lambda rows: gdown_out.__setitem__((rows, slice(None)), down_acc[rows, :].astype(BF16)), hidden)
        by_rows(lambda rows: gconvout_out.__setitem__((rows, slice(None)), convout_acc[rows, :].astype(BF16)), channels)
        gbias_out[...] = jnp.broadcast_to(jnp.sum(bias_acc[...], axis=0, keepdims=True), gbias_out.shape)
        for k in range(8):
            gvec_out[k : k + 1, :] = jnp.sum(vec_acc[k], axis=0, keepdims=True)


def middle(x2, w, cot, up, down, convout, bias, vec, stat):
    frames, channels = x2.shape
    hidden = up.shape[1]
    tiles = frames // TILE
    row = lambda width: pl.BlockSpec((TILE, width), lambda i: (i, 0))
    big = lambda a: pltpu.VMEM(a.shape, F32)
    shapes = [
        jax.ShapeDtypeStruct((frames, channels), BF16),
        jax.ShapeDtypeStruct((frames, channels), F32),
        jax.ShapeDtypeStruct((frames, channels), F32),
        jax.ShapeDtypeStruct(up.shape, BF16),
        jax.ShapeDtypeStruct(down.shape, BF16),
        jax.ShapeDtypeStruct(convout.shape, BF16),
        jax.ShapeDtypeStruct((8, hidden), F32),
        jax.ShapeDtypeStruct((8, channels), F32),
    ]
    return pl.pallas_call(
        middle_kernel,
        grid=(tiles,),
        in_specs=[row(channels)] * 3
        + [whole(a.shape) for a in (up, down, convout, bias, vec, stat)],
        out_specs=[row(channels)] * 3 + [whole(s.shape) for s in shapes[3:]],
        out_shape=shapes,
        scratch_shapes=[
            big(up),
            big(down),
            big(convout),
            pltpu.VMEM((8, hidden), F32),
            pltpu.VMEM((8, 8, channels), F32),
            pltpu.VMEM((TILE, hidden), F32),
            pltpu.VMEM((TILE, channels), BF16),
            pltpu.VMEM((channels, TILE), BF16),
            pltpu.VMEM((TILE, channels), BF16),
            pltpu.VMEM((TILE, channels), BF16),
            pltpu.VMEM((TILE, channels), F32),
            pltpu.VMEM((TILE, channels), F32),
        ],
        compiler_params=params(),
        name="middle",
    )(x2, w, cot, up, down, convout, bias, vec, stat)


def conv_back_kernel(flags_ref, w_ref, gnb_ref, p_ref, vec_ref, stat_ref, gg_ref, gtaps_ref, padded, gpad):
    frames, channels = w_ref.shape
    tiles = frames // TILE
    pitch = TILE + 2 * REACH
    center, scale = stat_ref[0:1, :], stat_ref[1:2, :]
    plain, cross = stat_ref[2:3, :], stat_ref[3:4, :]

    for tile in range(tiles):

        def fill(at, _, tile=tile):
            rows = pl.ds(pl.multiple_of(tile * TILE + at * 64, 64), 64)
            place = pl.ds(pl.multiple_of(tile * pitch + REACH + at * 64, 8), 64)
            e = (w_ref[rows, :] - center) * scale
            d = gnb_ref[rows, :] * vec_ref[5:6, :]
            gw = scale * (d - plain - e * cross)
            g = p_ref[rows, :channels].astype(F32) * sigmoid(p_ref[rows, channels:].astype(F32))
            for lane in range(channels // 128):
                cols = slice(lane * 128, lane * 128 + 128)
                padded[lane, place, :] = gw[:, cols]
                gpad[lane, place, :] = g[:, cols]
            return 0

        lax.fori_loop(0, TILE // 64, fill, 0)
    fill_halo(padded, flags_ref, tiles)
    fill_halo(gpad, flags_ref, tiles)

    def store(lane, row, base, total):
        gg_ref[pl.ds(pl.multiple_of(row, 64), 64), lane * 128 : lane * 128 + 128] = total

    taps_over(padded, vec_ref, store, tiles, True)
    block = 64
    per = TILE // block
    for lane in range(channels // 128):

        def corr(at, sums, lane=lane):
            base = (at // per) * pitch + (at % per) * block
            here = padded[lane, pl.ds(pl.multiple_of(base + REACH, 8), block), :]
            return tuple(
                s + fold8(here * gpad[lane, pl.ds(base + REACH + k - TAPS // 2, block), :])
                for k, s in enumerate(sums)
            )

        sums = lax.fori_loop(0, tiles * per, corr, (jnp.zeros((8, 128), F32),) * TAPS)
        for k in range(TAPS):
            gtaps_ref[k : k + 1, lane * 128 : lane * 128 + 128] = jnp.sum(sums[k], axis=0, keepdims=True)


def conv_back(flags, w, gnb, p, vec, stat):
    frames, channels = w.shape
    tiles = frames // TILE
    pad = pltpu.VMEM((channels // 128, tiles * (TILE + 2 * REACH), 128), F32)
    return pl.pallas_call(
        conv_back_kernel,
        in_specs=[pl.BlockSpec(memory_space=pltpu.SMEM)] + [pl.BlockSpec(memory_space=pltpu.VMEM)] * 5,
        out_specs=[pl.BlockSpec(memory_space=pltpu.VMEM)] * 2,
        out_shape=[
            jax.ShapeDtypeStruct((frames, channels), F32),
            jax.ShapeDtypeStruct((16, channels), F32),
        ],
        scratch_shapes=[pad, pad],
        compiler_params=pltpu.CompilerParams(vmem_limit_bytes=VMEM_LIMIT),
        name="conv_back",
    )(flags, w, gnb, p, vec, stat)


def back_kernel(
    flags_ref,
    gg_ref,
    p_ref,
    x2_ref,
    gx3_ref,
    gated_ref,
    y_ref,
    v_ref,
    u_ref,
    x1_ref,
    hold_ref,
    convin_ref,
    mixout_ref,
    mixin_ref,
    vec_ref,
    decay_ref,
    map_ref,
    gx1_ref,
    gconvin_out,
    gmixout_out,
    gmixin_out,
    gvec_out,
    gmap_out,
    gdecay_out,
    convin_acc,
    mixout_acc,
    mixin_acc,
    vec_acc,
    map_acc,
    decay_acc,
    adj_scr,
    track,
    low_scr,
    wide_scr,
    sum_scr,
    gy_scr,
):
    step = pl.program_id(0)
    tiles = pl.num_programs(0)
    at = tiles - 1 - step
    channels = x2_ref.shape[1]
    lanes = channels // 128
    gain = lambda k: vec_ref[k : k + 1, :]
    shift = lambda k: vec_ref[6 + k : 7 + k, :]

    @pl.when(step == 0)
    def _():
        for ref in (convin_acc, mixout_acc, mixin_acc, vec_acc, map_acc, decay_acc, adj_scr):
            ref[...] = jnp.zeros_like(ref)

    left, right = slice(0, channels), slice(channels, 2 * channels)

    def first(rows):
        grad = gg_ref[rows, :]
        sig = sigmoid(p_ref[rows, right].astype(F32))
        gl = (grad * sig).astype(BF16)
        gr = (grad * p_ref[rows, left].astype(F32) * (sig * (1.0 - sig))).astype(BF16)
        wide_scr[rows, left] = gl
        wide_scr[rows, right] = gr
        vec_acc[0] += fold8(gl.astype(F32))
        vec_acc[1] += fold8(gr.astype(F32))
        e, _ = norm_parts(x2_ref[rows, :])
        low_scr[rows, :] = (e * gain(2) + shift(2)).astype(BF16)

    by_rows(first)
    turned = low_scr[...].T
    convin_acc[...] += dot_nn(turned, wide_scr[...])
    sum_scr[...] = dot_nt(wide_scr[...], convin_ref[...])

    def second(rows):
        e, inv = norm_parts(x2_ref[rows, :])
        grad = sum_scr[rows, :]
        vec_acc[2] += fold8(grad * e)
        vec_acc[3] += fold8(grad)
        gx2 = gx3_ref[rows, :] + norm_back(grad, e, inv, gain(2))
        gx1_ref[rows, :] = gx2
        low = gx2.astype(BF16)
        low_scr[rows, :] = low
        vec_acc[4] += fold8(low.astype(F32))

    by_rows(second)
    mixout_acc[...] += dot_tn(gated_ref[...], low_scr[...])
    sum_scr[...] = dot_nt(low_scr[...], mixout_ref[...])

    def third(rows):
        grad = sum_scr[rows, :]
        v = v_ref[rows, :].astype(F32)
        sig = sigmoid(v)
        swish = v * sig
        gy = grad * swish
        gy_scr[rows, :] = gy
        wide_scr[rows, right] = (
            grad * y_ref[rows, :].astype(F32) * (sig * (1.0 + v - swish))
        ).astype(BF16)
        vec_acc[5] += fold8(gy * u_ref[rows, :])

    by_rows(third)
    low_half = half_masks(128)
    later = jnp.minimum(at + 1, tiles - 1)
    adj_scr[...] = adj_scr[...] * flags_ref[later].astype(F32)

    def span_back(index, _):
        span = TILE // SPAN - 1 - index
        base = pl.multiple_of(span * SPAN, SPAN)
        for lane in range(lanes):
            cols = slice(lane * 128, lane * 128 + 128)
            decay = decay_ref[:, cols]

            def forward(block, state):
                drive = u_ref[pl.ds(pl.multiple_of(base + block * 8, 8), 8), cols]
                for j in range(8):
                    track[block * 8 + j, :, cols] = state
                    state = decay * state + jnp.broadcast_to(drive[j : j + 1, :], (STATES, 128))
                return state

            lax.fori_loop(0, SPAN // 8, forward, hold_ref[span, :, cols])

        def backward(index, _):
            block = SPAN // 8 - 1 - index
            start = pl.multiple_of(base + block * 8, 8)
            for lane in range(lanes):
                cols = slice(lane * 128, lane * 128 + 128)
                decay = decay_ref[:, cols]
                maps = map_ref[:, cols]
                adj = adj_scr[:, cols]
                drive = u_ref[pl.ds(start, 8), cols]
                grad = gy_scr[pl.ds(start, 8), cols]
                gmap = map_acc[:, cols]
                gdecay = decay_acc[:, cols]
                parts = [None] * 8
                for j in range(7, -1, -1):
                    adj = decay * adj + jnp.broadcast_to(grad[j : j + 1, :], (STATES, 128))
                    parts[j] = fold_states(maps * adj)
                    gmap = gmap + adj * jnp.broadcast_to(drive[j : j + 1, :], (STATES, 128))
                    gdecay = gdecay + adj * track[block * 8 + j, :, cols]
                adj_scr[:, cols] = adj
                map_acc[:, cols] = gmap
                decay_acc[:, cols] = gdecay
                sum_scr[pl.ds(start, 8), cols] = merge_rows(parts, low_half)
            return 0

        lax.fori_loop(0, SPAN // 8, backward, 0)
        return 0

    lax.fori_loop(0, TILE // SPAN, span_back, 0)

    def fourth(rows):
        gu = sum_scr[rows, :] + shift(11) * gy_scr[rows, :]
        wide_scr[rows, left] = gu.astype(BF16)
        e, _ = norm_parts(x1_ref[rows, :])
        low_scr[rows, :] = (e * gain(1) + shift(1)).astype(BF16)

    by_rows(fourth)
    turned = low_scr[...].T
    mixin_acc[...] += dot_nn(turned, wide_scr[...])
    sum_scr[...] = dot_nt(wide_scr[...], mixin_ref[...])

    def fifth(rows):
        e, inv = norm_parts(x1_ref[rows, :])
        grad = sum_scr[rows, :]
        vec_acc[6] += fold8(grad * e)
        vec_acc[7] += fold8(grad)
        gx1_ref[rows, :] = gx1_ref[rows, :] + norm_back(grad, e, inv, gain(1))

    by_rows(fifth)

    @pl.when(step == tiles - 1)
    def _():
        for out, acc in ((gconvin_out, convin_acc), (gmixout_out, mixout_acc), (gmixin_out, mixin_acc)):
            by_rows(
                lambda rows, out=out, acc=acc: out.__setitem__((rows, slice(None)), acc[rows, :].astype(BF16)),
                channels,
            )
        for k in range(8):
            gvec_out[k : k + 1, :] = jnp.sum(vec_acc[k], axis=0, keepdims=True)
        gmap_out[...] = map_acc[...]
        gdecay_out[...] = decay_acc[...] * map_ref[...]


def back(flags, gg, p, x2, gx3, gated, y, v, u, x1, hold, convin, mixout, mixin, vec, decay, maps):
    frames, channels = x2.shape
    tiles = frames // TILE
    row = lambda width: pl.BlockSpec((TILE, width), lambda i, *_: (tiles - 1 - i, 0))
    spans = TILE // SPAN
    big = lambda a: pltpu.VMEM(a.shape, F32)
    shapes = [
        jax.ShapeDtypeStruct((frames, channels), F32),
        jax.ShapeDtypeStruct(convin.shape, BF16),
        jax.ShapeDtypeStruct(mixout.shape, BF16),
        jax.ShapeDtypeStruct(mixin.shape, BF16),
        jax.ShapeDtypeStruct((8, channels), F32),
        jax.ShapeDtypeStruct((STATES, channels), F32),
        jax.ShapeDtypeStruct((STATES, channels), F32),
    ]
    return pl.pallas_call(
        back_kernel,
        grid_spec=pltpu.PrefetchScalarGridSpec(
            num_scalar_prefetch=1,
            grid=(tiles,),
            in_specs=[row(channels), row(2 * channels)]
            + [row(channels)] * 7
            + [pl.BlockSpec((spans, STATES, channels), lambda i, *_: (tiles - 1 - i, 0, 0))]
            + [whole(a.shape) for a in (convin, mixout, mixin, vec, decay, maps)],
            out_specs=[row(channels)] + [whole(s.shape) for s in shapes[1:]],
            scratch_shapes=[
                big(convin),
                big(mixout),
                big(mixin),
                pltpu.VMEM((8, 8, channels), F32),
                pltpu.VMEM((STATES, channels), F32),
                pltpu.VMEM((STATES, channels), F32),
                pltpu.VMEM((STATES, channels), F32),
                pltpu.VMEM((SPAN, STATES, channels), F32),
                pltpu.VMEM((TILE, channels), BF16),
                pltpu.VMEM((TILE, 2 * channels), BF16),
                pltpu.VMEM((TILE, channels), F32),
                pltpu.VMEM((TILE, channels), F32),
            ],
        ),
        out_shape=shapes,
        compiler_params=params(),
        name="back",
    )(flags, gg, p, x2, gx3, gated, y, v, u, x1, hold, convin, mixout, mixin, vec, decay, maps)


def tail_kernel(
    x_ref,
    h_ref,
    gx1_ref,
    up_ref,
    down_ref,
    vec_ref,
    gx_ref,
    gup_out,
    gdown_out,
    gbias_out,
    gvec_out,
    up_acc,
    down_acc,
    bias_acc,
    vec_acc,
    low_scr,
    turn_scr,
    grad_scr,
    sum_scr,
):
    at = pl.program_id(0)
    tiles = pl.num_programs(0)
    channels = x_ref.shape[1]
    hidden = up_ref.shape[1]

    @pl.when(at == 0)
    def _():
        for ref in (up_acc, down_acc, bias_acc, vec_acc):
            ref[...] = jnp.zeros_like(ref)

    def first(rows):
        e, _ = norm_parts(x_ref[rows, :].astype(F32))
        low_scr[rows, :] = (e * vec_ref[0:1, :] + vec_ref[6:7, :]).astype(BF16)
        low = (0.5 * gx1_ref[rows, :]).astype(BF16)
        grad_scr[rows, :] = low
        vec_acc[0] += fold8(low.astype(F32))
        sum_scr[rows, :] = jnp.zeros((ROWS, channels), F32)

    by_rows(first)
    turn_scr[...] = low_scr[...].T
    ffn_back(
        turn_scr,
        None,
        grad_scr,
        lambda cols: h_ref[:, cols].astype(F32),
        up_ref,
        down_ref,
        up_acc,
        down_acc,
        bias_acc,
        sum_scr,
        hidden,
    )

    def second(rows):
        e, inv = norm_parts(x_ref[rows, :].astype(F32))
        grad = sum_scr[rows, :]
        vec_acc[1] += fold8(grad * e)
        vec_acc[2] += fold8(grad)
        gx_ref[rows, :] = gx1_ref[rows, :] + norm_back(grad, e, inv, vec_ref[0:1, :])

    by_rows(second)

    @pl.when(at == tiles - 1)
    def _():
        by_rows(lambda rows: gup_out.__setitem__((rows, slice(None)), up_acc[rows, :].astype(BF16)), channels)
        by_rows(lambda rows: gdown_out.__setitem__((rows, slice(None)), down_acc[rows, :].astype(BF16)), hidden)
        gbias_out[...] = jnp.broadcast_to(jnp.sum(bias_acc[...], axis=0, keepdims=True), gbias_out.shape)
        for k in range(3):
            gvec_out[k : k + 1, :] = jnp.sum(vec_acc[k], axis=0, keepdims=True)


def tail(x, h, gx1, up, down, vec):
    frames, channels = x.shape
    hidden = up.shape[1]
    tiles = frames // TILE
    row = lambda width: pl.BlockSpec((TILE, width), lambda i: (i, 0))
    big = lambda a: pltpu.VMEM(a.shape, F32)
    shapes = [
        jax.ShapeDtypeStruct((frames, channels), F32),
        jax.ShapeDtypeStruct(up.shape, BF16),
        jax.ShapeDtypeStruct(down.shape, BF16),
        jax.ShapeDtypeStruct((8, hidden), F32),
        jax.ShapeDtypeStruct((8, channels), F32),
    ]
    return pl.pallas_call(
        tail_kernel,
        grid=(tiles,),
        in_specs=[row(channels), row(hidden), row(channels)]
        + [whole(a.shape) for a in (up, down, vec)],
        out_specs=[row(channels)] + [whole(s.shape) for s in shapes[1:]],
        out_shape=shapes,
        scratch_shapes=[
            big(up),
            big(down),
            pltpu.VMEM((8, hidden), F32),
            pltpu.VMEM((8, 8, channels), F32),
            pltpu.VMEM((TILE, channels), BF16),
            pltpu.VMEM((channels, TILE), BF16),
            pltpu.VMEM((TILE, channels), BF16),
            pltpu.VMEM((TILE, channels), F32),
        ],
        compiler_params=params(),
        name="tail",
    )(x, h, gx1, up, down, vec)


def pack_table(gains, shifts, conv_bias, taps, rate, maps):
    channels = gains.shape[1]
    blank = lambda rows: jnp.zeros((rows, channels), gains.dtype)
    parts = [gains, shifts, conv_bias[None], blank(TAP_ROW - 19), taps, blank(RATE - TAP_ROW - TAPS)]
    parts += [rate, maps[0], maps[1], blank(256 - TABLE)]
    return jnp.concatenate(parts, axis=0).T


def pack_bias(bias, place):
    layers, count = bias.shape
    hidden = 16 * CHUNK // layers
    wide = lax.dynamic_update_slice(
        jnp.zeros((layers, hidden), bias.dtype), bias, (0, place * count)
    )
    return wide.reshape((16, CHUNK))


def unpack_table(table):
    return (
        table[0:6],
        table[6:18],
        table[18],
        table[TAP_ROW : TAP_ROW + TAPS],
        table[RATE:MAP_IN],
        jnp.stack([table[MAP_IN:MAP_OUT], table[MAP_OUT:TABLE]]),
    )


def on_device(
    n_dp,
    n_fs,
    frames,
    seq_lengths,
    seq_offsets,
    seq_counts,
    ffn_up,
    ffn_down,
    ffn_bias_up,
    mix_in,
    mix_out,
    conv_in,
    conv_out,
    conv_out_bias,
    ssm_rate,
    ssm_map,
    conv_kernel,
    gains,
    shifts,
    cotangent,
):
    devices = n_dp * n_fs
    mine = lax.axis_index("dp") * n_fs + lax.axis_index("fsdp")
    frames_dev, channels = frames.shape
    tiles = frames_dev // TILE
    slot = jnp.arange(seq_offsets.shape[1], dtype=jnp.int32)
    begins = (seq_offsets[0][None, :] == TILE * jnp.arange(tiles, dtype=jnp.int32)[:, None]) & (
        slot < seq_counts[0]
    )
    flags = 1 - jnp.max(begins.astype(jnp.int32), axis=1)
    small = pack_table(gains, shifts, conv_out_bias, conv_kernel, ssm_rate, ssm_map)
    bias = pack_bias(ffn_bias_up, mine)
    fused = small.shape[0] % 16 == 0
    shards = [ffn_up, ffn_down, mix_in[None], mix_out[None], conv_in[None], conv_out[None]]
    if fused:
        small = jnp.concatenate([small, bias], axis=1)
        made = front((n_dp, n_fs), flags, frames, [small[None]] + shards, 1)
        _, up0, down0, mixin, mixout, convin, convout, up1, down1 = [
            g.reshape((-1, g.shape[-1])) for g in made[15:]
        ]
        stat = made[10]
    else:
        got = gather_all(n_dp, n_fs, [small[None], bias[None]] + shards, 1)
        small, _, up0, up1, down0, down1, mixin, mixout, convin, convout = [
            g.reshape((-1, g.shape[-1])) for g in got
        ]
        made = front(
            None,
            flags,
            frames,
            [
                up0,
                down0,
                mixin,
                mixout,
                convin,
                small.astype(F32).T[:TABLE],
                jnp.sum(got[1].astype(F32), axis=0),
            ],
        )
        pool = exchange(n_dp, n_fs, made[10], frames_dev, 2, pool_kernel)
        scale = lax.rsqrt(pool[1:2] / (frames_dev * devices) + EPSILON)
        stat = jnp.concatenate([pool[0:1], scale, jnp.zeros((6, channels), F32)])
    h0, x1, u, v, y, gated, x2, p, hold, w, _, table, bias, decay, coupling = made[:15]
    result, gx3, gnb, gup1, gdown1, gconvout, gbias1, gvec1 = middle(
        x2, w, cotangent, up1, down1, convout, bias, table, stat
    )
    sums = exchange(n_dp, n_fs, gvec1, 1, 4, total_kernel)[6:8]
    sums = sums * (table[5:6] / (frames_dev * devices))
    stat = jnp.concatenate([stat[0:2], sums[1:2], sums[0:1], jnp.zeros((4, channels), F32)])
    gg, gtaps = conv_back(flags, w, gnb, p, table, stat)
    gx1, gconvin, gmixout, gmixin, gvec2, gmap, gdecay = back(
        flags, gg, p, x2, gx3, gated, y, v, u, x1, hold, convin, mixout, mixin, table, decay, coupling
    )
    gx, gup0, gdown0, gbias0, gvec3 = tail(frames, h0, gx1, up0, down0, table)

    def weights_of(log_rate, maps):
        log_decay = -jnp.exp(log_rate)
        root = jnp.sqrt(-jnp.expm1(2.0 * log_decay))
        return jnp.exp(log_decay), maps[0] * root * maps[1]

    rate, maps = unpack_table(table)[4:]
    rate_grad, map_grad = jax.vjp(weights_of, rate, maps)[1]((gdecay, gmap))
    gain_grad = jnp.stack([gvec3[1], gvec2[6], gvec2[2], gvec1[3], gvec1[0], gvec1[6]])
    shift_grad = jnp.stack(
        [
            gvec3[2],
            gvec2[7],
            gvec2[3],
            gvec1[4],
            gvec1[1],
            gvec1[7],
            gvec3[0],
            gvec1[2],
            gvec2[4],
            gvec2[0],
            gvec2[1],
            gvec2[5],
        ]
    )
    small_grad = pack_table(gain_grad, shift_grad, gvec1[5], gtaps[:TAPS], rate_grad, map_grad)
    bias_grad = jnp.concatenate([gbias0[:1], gbias1[:1]]).reshape((16, CHUNK))
    wide = lambda g: g.reshape((devices, g.shape[0] // devices, g.shape[1]))
    reduced = scatter_all(
        n_dp,
        n_fs,
        [wide(g) for g in (gup1, gdown1, gconvout, gconvin, gmixout, gmixin, gup0, gdown0)]
        + [
            wide(small_grad.astype(BF16)),
            jnp.broadcast_to(bias_grad.astype(BF16), (devices, 16, CHUNK)),
        ],
        5,
    )
    gains_grad, shifts_grad, conv_bias_grad, taps_grad, rate_grad, map_grad = unpack_table(
        reduced[8].T
    )
    bias_grad = reduced[9].reshape((2, -1))
    count = bias_grad.shape[1] // devices
    bias_grad = lax.dynamic_slice(bias_grad, (0, mine * count), (2, count))
    return (
        result,
        gx,
        jnp.stack([reduced[6], reduced[0]]),
        jnp.stack([reduced[7], reduced[1]]),
        bias_grad,
        reduced[5],
        reduced[4],
        reduced[3],
        reduced[2],
        conv_bias_grad,
        rate_grad,
        map_grad,
        taps_grad,
        gains_grad,
        shifts_grad,
    )


def solution(mesh):
    both = ("dp", "fsdp")
    row, row1 = P(both, None), P(both)
    col, col3, mid = P(None, both), P(None, None, both), P(None, both, None)
    in_specs = (
        row,
        row,
        row,
        row1,
        mid,
        mid,
        col,
        row,
        row,
        row,
        row,
        row1,
        col,
        col3,
        col,
        col,
        col,
        row,
    )
    out_specs = (row, row, mid, mid, col, row, row, row, row, row1, col, col3, col, col, col)
    return jax.shard_map(
        partial(on_device, mesh.shape["dp"], mesh.shape["fsdp"]),
        mesh=mesh,
        in_specs=in_specs,
        out_specs=out_specs,
        check_vma=False,
    )
```

```python
import itertools
from functools import partial

import jax
import jax.numpy as jnp
from jax import lax
from jax.experimental import pallas as pl
from jax.experimental.pallas import tpu as pltpu
from jax.sharding import PartitionSpec as P

MESH = pl.DeviceIdType.MESH
BF16 = jnp.bfloat16
F32 = jnp.float32


def flip(index, bit):
    return index + bit * (1 - 2 * lax.rem(lax.div(index, bit), 2))


def flip_all(index, bits):
    for bit in bits:
        index = flip(index, bit)
    return index


def combos(bits):
    found = [()]
    for bit in bits:
        found = found + [entry + (bit,) for entry in found]
    return found


def plan_bits(n_dp):
    bits, bit = [], 2
    while bit < n_dp:
        bits.append(bit)
        bit *= 2
    return tuple(bits)


def greet(dp, fs, n_dp, n_fs):
    barrier = pltpu.get_barrier_semaphore()
    for step in range(1, n_dp):
        pl.semaphore_signal(
            barrier, inc=1, device_id=(lax.rem(dp + step, n_dp), fs), device_id_type=MESH
        )
    for step in range(1, n_fs):
        pl.semaphore_signal(
            barrier, inc=1, device_id=(dp, lax.rem(fs + step, n_fs)), device_id_type=MESH
        )
    pl.semaphore_wait(barrier, n_dp + n_fs - 2)


def gather_plan(dp, fs, n_dp, n_fs, sources, outs, send_sem, recv_sem, local_sem):
    bits = plan_bits(n_dp)
    orders = (bits, bits[::-1])
    half = n_fs // 2
    sends = []

    def stages(chunk):
        src, out = sources[chunk], outs[chunk]
        slots = itertools.count()

        def zone(where, part):
            if part is None:
                return out.at[pl.ds(where * n_fs, n_fs)]
            return out.at[pl.ds(where * n_fs + part * half, half)]

        def remote(slot, view_from, view_to, device):
            return pltpu.make_async_remote_copy(
                src_ref=view_from,
                dst_ref=view_to,
                send_sem=send_sem.at[chunk, slot],
                recv_sem=recv_sem.at[chunk, slot],
                device_id=device,
                device_id_type=MESH,
            )

        def launch(make):
            make().start()
            sends.append(lambda: make().wait_send())

        z_slots = [next(slots) for _ in range(1, n_fs)]

        def own_copy():
            return pltpu.make_async_copy(src, out.at[dp * n_fs + fs], local_sem.at[chunk])

        def start():
            own_copy().start()
            for step in range(1, n_fs):
                launch(
                    lambda step=step: remote(
                        z_slots[step - 1],
                        src,
                        out.at[dp * n_fs + fs],
                        (dp, lax.rem(fs + step, n_fs)),
                    )
                )

        def wait_z():
            own_copy().wait()
            for step in range(1, n_fs):
                origin = dp * n_fs + lax.rem(fs + n_fs - step, n_fs)
                remote(z_slots[step - 1], src, out.at[origin], (dp, fs)).wait_recv()

        steps, before = [start], wait_z
        for depth in range(len(bits)):
            plan = []
            for part, order in enumerate(orders):
                for entry in combos(order[:depth]):
                    plan.append((next(slots), part, order[depth], entry))

            def view(slot, part, bit, entry, arrived):
                where = flip_all(flip(dp, bit) if arrived else dp, entry)
                return remote(slot, zone(where, part), zone(where, part), (flip(dp, bit), fs))

            def go(plan=plan, before=before, view=view):
                before()
                for item in plan:
                    launch(lambda item=item: view(*item, False))

            def arrive(plan=plan, view=view):
                for item in plan:
                    view(*item, True).wait_recv()

            steps.append(go)
            before = arrive
        last = [(next(slots), entry) for entry in combos(bits)]

        def across(slot, entry, arrived):
            where = flip_all(flip(dp, 1) if arrived else dp, entry)
            return remote(slot, zone(where, None), zone(where, None), (flip(dp, 1), fs))

        def cross(before=before):
            before()
            for item in last:
                launch(lambda item=item: across(*item, False))

        def finish():
            for item in last:
                across(*item, True).wait_recv()

        return steps + [cross, finish]

    return [stages(chunk) for chunk in range(len(outs))], sends


def waves(plans):
    depth = len(plans[0])
    out = []
    for wave in range(len(plans) + depth - 1):
        out.append(
            [plans[c][wave - c] for c in range(len(plans)) if 0 <= wave - c < depth]
        )
    return out


def gather_kernel(n_dp, n_fs, layers, *refs):
    n_in = len(layers)
    n_out = sum(layers)
    ins, outs = refs[:n_in], refs[n_in : n_in + n_out]
    send_sem, recv_sem, local_sem = refs[n_in + n_out :]
    sources = []
    for ref, count in zip(ins, layers):
        sources += [ref.at[layer] for layer in range(count)]
    dp, fs = lax.axis_index("dp"), lax.axis_index("fsdp")
    greet(dp, fs, n_dp, n_fs)
    plans, sends = gather_plan(dp, fs, n_dp, n_fs, sources, outs, send_sem, recv_sem, local_sem)
    for wave in waves(plans):
        for stage in wave:
            stage()
    for wait in sends:
        wait()


def slot_count(n_dp, n_fs):
    nb = len(plan_bits(n_dp))
    return n_fs - 1 + 2 * (2**nb - 1) + 2**nb


def gather_all(n_dp, n_fs, arrays, collective_id):
    layers = tuple(a.shape[0] for a in arrays)
    outs = []
    for a in arrays:
        outs += [jax.ShapeDtypeStruct((n_dp * n_fs,) + a.shape[1:], a.dtype)] * a.shape[0]
    count = slot_count(n_dp, n_fs)
    return pl.pallas_call(
        partial(gather_kernel, n_dp, n_fs, layers),
        out_shape=outs,
        in_specs=[pl.BlockSpec(memory_space=pltpu.HBM)] * len(arrays),
        out_specs=[pl.BlockSpec(memory_space=pltpu.HBM)] * len(outs),
        scratch_shapes=[
            pltpu.SemaphoreType.DMA((len(outs), count)),
            pltpu.SemaphoreType.DMA((len(outs), count)),
            pltpu.SemaphoreType.DMA((len(outs),)),
        ],
        compiler_params=pltpu.CompilerParams(collective_id=collective_id, has_side_effects=True),
        name="gather_parameters",
    )(*arrays)


def scatter_plan(dp, fs, n_dp, n_fs, ins, emit, scratch, send_sem, recv_sem, local_sem, first=0):
    bits = plan_bits(n_dp)
    orders = (bits[::-1], bits)
    half = n_fs // 2
    index = {entry: at for at, entry in enumerate(combos(bits))}
    sends = []

    def add_into(kept, other):
        def body(at, _):
            kept[at] = (kept[at].astype(F32) + other[at].astype(F32)).astype(BF16)
            return 0

        lax.fori_loop(0, kept.shape[0], body, 0)

    def stages(chunk):
        src = ins[chunk]
        cross_in, own, later, last = scratch[4 * chunk : 4 * chunk + 4]
        slots = itertools.count()

        def remote(slot, view_from, view_to, device):
            return pltpu.make_async_remote_copy(
                src_ref=view_from,
                dst_ref=view_to,
                send_sem=send_sem.at[first + chunk, slot],
                recv_sem=recv_sem.at[first + chunk, slot],
                device_id=device,
                device_id_type=MESH,
            )

        def launch(make):
            make().start()
            sends.append(lambda: make().wait_send())

        def zone(entry, crossed):
            return src.at[pl.ds(flip_all(flip(dp, 1) if crossed else dp, entry) * n_fs, n_fs)]

        pieces = [(next(slots), entry, index[entry]) for entry in combos(bits)]

        def load(entry, at):
            return pltpu.make_async_copy(
                zone(entry, False), own.at[at], local_sem.at[first + chunk, at]
            )

        def across(slot, entry, at):
            return remote(slot, zone(entry, True), cross_in.at[at], (flip(dp, 1), fs))

        def start():
            for item in pieces:
                launch(lambda item=item: across(*item))
            for _, entry, at in pieces:
                load(entry, at).start()

        def fold_cross():
            for slot, entry, at in pieces:
                load(entry, at).wait()
                across(slot, entry, at).wait_recv()
                add_into(own.at[at], cross_in.at[at])

        steps, before = [start], fold_cross
        used = 0
        for depth in range(len(bits)):
            plan = []
            for part, order in enumerate(orders):
                bit, gone = order[depth], order[:depth]
                for entry in combos(bits):
                    if not (set(entry) & set(gone)) and bit not in entry:
                        away = tuple(sorted(entry + (bit,)))
                        plan.append((next(slots), part, bit, index[away], index[entry], used))
                        used += 1

            def move(slot, part, bit, away, kept, place):
                return remote(
                    slot,
                    own.at[away, pl.ds(part * half, half)],
                    later.at[place],
                    (flip(dp, bit), fs),
                )

            def go(plan=plan, before=before, move=move):
                before()
                for item in plan:
                    launch(lambda item=item: move(*item))

            def fold(plan=plan, move=move):
                for item in plan:
                    move(*item).wait_recv()
                    _, part, _, _, kept, place = item
                    add_into(own.at[kept, pl.ds(part * half, half)], later.at[place])

            steps.append(go)
            before = fold
        z_slots = [next(slots) for _ in range(1, n_fs)]

        def along(step):
            to = lax.rem(fs + step, n_fs)
            return remote(z_slots[step - 1], own.at[0, to], last.at[step - 1], (dp, to))

        def spread(before=before):
            before()
            for step in range(1, n_fs):
                launch(lambda step=step: along(step))

        def finish():
            total = own[0, fs].astype(F32)
            for step in range(1, n_fs):
                along(step).wait_recv()
                total = total + last[step - 1].astype(F32)
            emit(chunk, total)

        return steps + [spread, finish]

    return [stages(chunk) for chunk in range(len(ins))], sends


def scatter_scratch(n_dp, n_fs, tails):
    pieces = 2 ** len(plan_bits(n_dp))
    scratch = []
    for tail in tails:
        scratch += [
            pltpu.VMEM((pieces, n_fs) + tail, BF16),
            pltpu.VMEM((pieces, n_fs) + tail, BF16),
            pltpu.VMEM((2 * (pieces - 1), n_fs // 2) + tail, BF16),
            pltpu.VMEM((n_fs - 1,) + tail, BF16),
        ]
    return scratch


def scatter_sems(n_dp, n_fs, chunks):
    count = slot_count(n_dp, n_fs)
    return [
        pltpu.SemaphoreType.DMA((chunks, count)),
        pltpu.SemaphoreType.DMA((chunks, count)),
        pltpu.SemaphoreType.DMA((chunks, 2 ** len(plan_bits(n_dp)))),
    ]


def scatter_kernel(n_dp, n_fs, n_chunks, *refs):
    ins, outs = refs[:n_chunks], refs[n_chunks : 2 * n_chunks]
    scratch = refs[2 * n_chunks : 6 * n_chunks]
    dp, fs = lax.axis_index("dp"), lax.axis_index("fsdp")
    greet(dp, fs, n_dp, n_fs)

    def emit(chunk, total):
        outs[chunk][...] = total

    plans, sends = scatter_plan(dp, fs, n_dp, n_fs, ins, emit, scratch, *refs[6 * n_chunks :])
    for wave in waves(plans):
        for stage in wave:
            stage()
    for wait in sends:
        wait()


def scatter_all(n_dp, n_fs, arrays, collective_id):
    n = len(arrays)
    return pl.pallas_call(
        partial(scatter_kernel, n_dp, n_fs, n),
        out_shape=[jax.ShapeDtypeStruct(a.shape[1:], F32) for a in arrays],
        in_specs=[pl.BlockSpec(memory_space=pltpu.HBM)] * n,
        out_specs=[pl.BlockSpec(memory_space=pltpu.VMEM)] * n,
        scratch_shapes=scatter_scratch(n_dp, n_fs, [a.shape[1:] for a in arrays])
        + scatter_sems(n_dp, n_fs, n),
        compiler_params=pltpu.CompilerParams(
            collective_id=collective_id, has_side_effects=True, vmem_limit_bytes=48 << 20
        ),
        name="scatter_gradients",
    )(*arrays)


def swap_copy(axis, place, count, buffer, send_sem, recv_sem, step):
    return pltpu.make_async_remote_copy(
        src_ref=buffer.at[0],
        dst_ref=buffer.at[step],
        send_sem=send_sem.at[step],
        recv_sem=recv_sem.at[step],
        device_id={axis: lax.rem(place + step, count)},
        device_id_type=MESH,
    )


def swap_start(axis, place, count, *rest):
    for step in range(1, count):
        swap_copy(axis, place, count, *rest, step).start()


def swap_wait(axis, place, count, *rest):
    for step in range(1, count):
        swap_copy(axis, place, count, *rest, step).wait_recv()
    for step in range(1, count):
        swap_copy(axis, place, count, *rest, step).wait_send()


def swap_rows(*args):
    swap_start(*args)
    swap_wait(*args)


def sum_over(x, dp, fs, n_dp, n_fs, octet, line, send_sem, recv_sem, between=None):
    first = ("dp", dp, n_dp, octet, send_sem.at[0], recv_sem.at[0])
    octet[0] = x
    swap_start(*first)
    if between is not None:
        between()
    swap_wait(*first)
    total = octet[0]
    for step in range(1, n_dp):
        total = total + octet[step]
    line[0] = total
    swap_rows("fsdp", fs, n_fs, line, send_sem.at[1], recv_sem.at[1])
    total = line[0]
    for step in range(1, n_fs):
        total = total + line[step]
    return total


def pooled(buffer, count, weight):
    means = [buffer[k, 0:1, :] for k in range(count)]
    center = sum(means[1:], means[0]) * (1.0 / count)
    spread = buffer[0, 1:2, :]
    for k in range(1, count):
        spread = spread + buffer[k, 1:2, :]
    off = (means[0] - center) * (means[0] - center)
    for mean in means[1:]:
        off = off + (mean - center) * (mean - center)
    return center, spread + weight * off


def pool_over(center, spread, frames, dp, fs, n_dp, n_fs, octet, line, send_sem, recv_sem):
    octet[0] = jnp.zeros(octet.shape[1:], F32)
    line[0] = jnp.zeros(line.shape[1:], F32)
    octet[0, 0:1, :] = center
    octet[0, 1:2, :] = spread
    swap_rows("dp", dp, n_dp, octet, send_sem.at[0], recv_sem.at[0])
    center, spread = pooled(octet, n_dp, float(frames))
    line[0, 0:1, :] = center
    line[0, 1:2, :] = spread
    swap_rows("fsdp", fs, n_fs, line, send_sem.at[1], recv_sem.at[1])
    return pooled(line, n_fs, float(frames * n_dp))


def swap_scratch(n_dp, n_fs, channels):
    return [
        pltpu.VMEM((n_dp, 8, channels), F32),
        pltpu.VMEM((n_fs, 8, channels), F32),
        pltpu.SemaphoreType.DMA((2, max(n_dp, n_fs))),
        pltpu.SemaphoreType.DMA((2, max(n_dp, n_fs))),
    ]


def pool_kernel(n_dp, n_fs, frames, x_ref, out_ref, octet, line, send_sem, recv_sem):
    dp, fs = lax.axis_index("dp"), lax.axis_index("fsdp")
    greet(dp, fs, n_dp, n_fs)
    octet[0] = x_ref[...]
    center, spread = pool_over(
        x_ref[0:1, :], x_ref[1:2, :], frames, dp, fs, n_dp, n_fs, octet, line, send_sem, recv_sem
    )
    out_ref[...] = x_ref[...]
    out_ref[0:1, :] = center
    out_ref[1:2, :] = spread


def total_kernel(n_dp, n_fs, frames, x_ref, out_ref, octet, line, send_sem, recv_sem):
    dp, fs = lax.axis_index("dp"), lax.axis_index("fsdp")
    greet(dp, fs, n_dp, n_fs)
    out_ref[...] = sum_over(x_ref[...], dp, fs, n_dp, n_fs, octet, line, send_sem, recv_sem)


def exchange(n_dp, n_fs, x, frames, collective_id, kernel):
    return pl.pallas_call(
        partial(kernel, n_dp, n_fs, frames),
        out_shape=jax.ShapeDtypeStruct(x.shape, F32),
        in_specs=[pl.BlockSpec(memory_space=pltpu.VMEM)],
        out_specs=pl.BlockSpec(memory_space=pltpu.VMEM),
        scratch_shapes=swap_scratch(n_dp, n_fs, x.shape[1]),
        compiler_params=pltpu.CompilerParams(collective_id=collective_id, has_side_effects=True),
        name="exchange_rows",
    )(x)


TILE = 512
STATES = 32
TAPS = 15
REACH = 8
EPSILON = 1e-05
CHUNK = 256
ROWS = 128
SPAN = 32
VMEM_LIMIT = 60 << 20
TAP_ROW = 24
RATE = 40
MAP_IN = 72
MAP_OUT = 104
TABLE = 136


def sigmoid(v):
    return 0.5 * jnp.tanh(0.5 * v) + 0.5


def dot_nn(a, b):
    return jnp.dot(a, b, preferred_element_type=F32)


def dot_nt(a, b):
    return lax.dot_general(a, b, (((1,), (1,)), ((), ())), preferred_element_type=F32)


def dot_tn(a, b):
    return lax.dot_general(a, b, (((0,), (0,)), ((), ())), preferred_element_type=F32)


def norm_parts(v):
    centered = v - jnp.mean(v, axis=-1, keepdims=True)
    inv = lax.rsqrt(jnp.mean(centered * centered, axis=-1, keepdims=True) + EPSILON)
    return centered * inv, inv


def norm_back(grad, e, inv, gain):
    d = grad * gain
    return (
        d - jnp.mean(d, axis=-1, keepdims=True) - e * jnp.mean(d * e, axis=-1, keepdims=True)
    ) * inv


def fold8(v):
    return jnp.sum(v.reshape((v.shape[0] // 8, 8, v.shape[1])), axis=0)


def by_rows(body, rows=TILE, step=ROWS):
    def run(at, _):
        body(pl.ds(pl.multiple_of(at * step, step), step))
        return 0

    lax.fori_loop(0, rows // step, run, 0)


def columns(at, width=CHUNK):
    return pl.ds(pl.multiple_of(at * width, width), width)


def merge_rows(parts, low_half):
    for distance in (1, 2, 4):
        low = low_half[distance]
        parts = [
            jnp.where(low, a, b) + pltpu.roll(jnp.where(low, b, a), distance, 0)
            for a, b in zip(parts[0::2], parts[1::2])
        ]
    return parts[0]


def half_masks(width):
    row = lax.broadcasted_iota(jnp.int32, (8, width), 0)
    return {d: (row // d) % 2 == 0 for d in (4, 2, 1)}


def fold_states(v):
    return jnp.sum(v.reshape((STATES // 8, 8, v.shape[1])), axis=0)


def fill_halo(padded, flags_ref, tiles):
    pitch = TILE + 2 * REACH
    for at in range(tiles):
        base = at * pitch
        if at == 0:
            padded[:, base : base + REACH, :] = jnp.zeros_like(padded[:, base : base + REACH, :])
        if at == tiles - 1:
            end = base + REACH + TILE
            padded[:, end : end + REACH, :] = jnp.zeros_like(padded[:, end : end + REACH, :])
        else:
            keep = flags_ref[at + 1].astype(F32)
            end = base + REACH + TILE
            padded[:, end : end + REACH, :] = (
                padded[:, base + pitch + REACH : base + pitch + 2 * REACH, :] * keep
            )
            padded[:, base + pitch : base + pitch + REACH, :] = (
                padded[:, end - REACH : end, :] * keep
            )


def taps_over(padded, table_ref, store, tiles, reverse, block=64):
    pitch = TILE + 2 * REACH
    per = TILE // block
    lanes = padded.shape[0]
    for lane in range(lanes):
        weights = [
            jnp.broadcast_to(
                table_ref[TAP_ROW + k : TAP_ROW + k + 1, lane * 128 : lane * 128 + 128], (block, 128)
            )
            for k in range(TAPS)
        ]

        def run(at, _):
            tile, inner = at // per, at % per
            base = tile * pitch + inner * block
            total = jnp.zeros((block, 128), F32)
            for k in range(TAPS):
                shift = REACH + (TAPS // 2 - k if reverse else k - TAPS // 2)
                total = total + weights[k] * padded[lane, pl.ds(base + shift, block), :]
            store(lane, tile * TILE + inner * block, base, total)
            return 0

        lax.fori_loop(0, tiles * per, run, 0)


def small_exp(v):
    return 1.0 + v * (1.0 + v * (0.5 + v * (1.0 / 6 + v * (1.0 / 24 + v * (1.0 / 120)))))


def small_expm1_over(v):
    return 1.0 + v * (
        0.5 + v * (1.0 / 6 + v * (1.0 / 24 + v * (1.0 / 120 + v * (1.0 / 720 + v * (1.0 / 5040)))))
    )


def state_terms(table_ref):
    log_decay = -jnp.exp(table_ref[RATE : RATE + STATES, :])
    root = jnp.sqrt(-2.0 * log_decay * small_expm1_over(2.0 * log_decay))
    maps_in = table_ref[MAP_IN : MAP_IN + STATES, :]
    maps_out = table_ref[MAP_OUT : MAP_OUT + STATES, :]
    return log_decay, small_exp(log_decay), root, maps_in, maps_out


def ref_rows(ref):
    return ref.reshape((ref.shape[0] * ref.shape[1], ref.shape[2]))


WEIGHTS = 6


def front_kernel(mesh_size, *refs):
    fused = mesh_size is not None
    refs = list(refs)
    take = lambda count: [refs.pop(0) for _ in range(count)]
    flags_ref, x_ref = take(2)
    if fused:
        n_dp, n_fs = mesh_size
        shards = take(7)
    else:
        up_ref, down_ref, mixin_ref, mixout_ref, convin_ref, table_in, bias_in = take(7)
    (
        h_out,
        x1_out,
        u_out,
        v_out,
        y_out,
        gated_out,
        x2_out,
        p_out,
        hold_out,
        w_out,
        stat_out,
        table_ref,
        bias_ref,
        decay_ref,
        map_ref,
    ) = take(15)
    gathered = take(9) if fused else []
    x1_scr, low_all, low_scr, sum_scr, state_scr, padded = take(6)
    step = pl.program_id(0)
    channels = x_ref.shape[1]
    frames = w_out.shape[0]
    tiles = frames // TILE
    lanes = channels // 128
    gain = lambda k: table_ref[k : k + 1, :]
    shift = lambda k: table_ref[6 + k : 7 + k, :]
    here = lambda rows, tile: pl.ds(pl.multiple_of(tile * TILE + rows.start, ROWS), ROWS)
    if fused:
        small_v, up_v, down_v, mixin_v, mixout_v, convin_v = take(WEIGHTS)
        send_sem, recv_sem, local_sem, load_sem = take(4)
        swap = take(4)
        dp, fs = lax.axis_index("dp"), lax.axis_index("fsdp")
        small_s, up_s, down_s, mixin_s, mixout_s, convin_s, convout_s = shards
        sources = [
            small_s.at[0],
            up_s.at[0],
            down_s.at[0],
            mixin_s.at[0],
            mixout_s.at[0],
            convin_s.at[0],
            convout_s.at[0],
            up_s.at[1],
            down_s.at[1],
        ]
        plans, sends = gather_plan(
            dp, fs, n_dp, n_fs, sources, gathered, send_sem, recv_sem, local_sem
        )
        order = waves(plans)
        ready = len(plans[0]) + 2
        held = (small_v, up_v, down_v, mixin_v, mixout_v, convin_v)

        def load(chunk):
            return pltpu.make_async_copy(gathered[chunk], held[chunk], load_sem.at[chunk])

        up_ref, down_ref, mixin_ref, mixout_ref, convin_ref = [ref_rows(r) for r in held[1:]]

        @pl.when(step == 0)
        def _():
            greet(dp, fs, n_dp, n_fs)
            for wave in order[:ready]:
                for stage in wave:
                    stage()
            for chunk in range(3):
                load(chunk).start()
            load(0).wait()
            table_ref[...] = ref_rows(small_v)[:, :256].astype(F32).T[: table_ref.shape[0], :]
            total = small_v[0, :, 256:].astype(F32)
            for k in range(1, n_dp * n_fs):
                total = total + small_v[k, :, 256:].astype(F32)
            bias_ref[...] = total
            load(1).wait()
            load(2).wait()

        for k in range(1, tiles + 1):

            @pl.when(step == k)
            def _(k=k):
                for stage in order[ready + k - 1]:
                    stage()
                if k == tiles:
                    for chunk in range(3, 6):
                        load(chunk).start()
                    for chunk in range(3, 6):
                        load(chunk).wait()

        rest = order[ready + tiles :]
        for k in range(tiles):

            @pl.when(step == tiles + 1 + k)
            def _(k=k):
                for wave in rest[k :: tiles] if k < tiles - 1 else rest[k:]:
                    for stage in wave:
                        stage()
                if k == tiles - 1:
                    for wait in sends:
                        wait()

    else:

        @pl.when(step == 0)
        def _():
            table_ref[...] = table_in[...]
            bias_ref[...] = bias_in[...]

    @pl.when(step == 0)
    def _():
        _, decay, root, maps_in, maps_out = state_terms(table_ref)
        decay_ref[...] = decay
        map_ref[...] = maps_in * root * maps_out
        state_scr[...] = jnp.zeros_like(state_scr)

    @pl.when(step < tiles)
    def _():
        def first(rows):
            e, _ = norm_parts(x_ref[rows, :].astype(F32))
            low_scr[rows, :] = (e * gain(0) + shift(0)).astype(BF16)
            sum_scr[rows, :] = jnp.zeros((ROWS, channels), F32)

        by_rows(first)

        def hidden(c, _):
            cols = columns(c)
            h = dot_nn(low_scr[...], up_ref[:, cols]) + bias_ref[pl.ds(c, 1), :]
            h_out[:, cols] = h.astype(BF16)
            active = (h * sigmoid(h)).astype(BF16)
            sum_scr[...] += dot_nn(active, down_ref[cols, :])
            return 0

        lax.fori_loop(0, up_ref.shape[1] // CHUNK, hidden, 0)

        def second(rows):
            x1 = x_ref[rows, :].astype(F32) + 0.5 * (sum_scr[rows, :] + shift(6))
            x1_out[rows, :] = x1
            x1_scr[here(rows, step), :] = x1
            e, _ = norm_parts(x1)
            low_all[here(rows, step), :] = (e * gain(1) + shift(1)).astype(BF16)

        by_rows(second)

    @pl.when((step >= tiles) & (step < 2 * tiles))
    def _():
        at = step - tiles
        whole_tile = pl.ds(pl.multiple_of(at * TILE, TILE), TILE)

        def project(c, _):
            cols = columns(c)
            right = columns(c + channels // CHUNK)
            u_out[:, cols] = dot_nn(low_all[whole_tile, :], mixin_ref[:, cols])
            v_out[:, cols] = dot_nn(low_all[whole_tile, :], mixin_ref[:, right]).astype(BF16)
            return 0

        lax.fori_loop(0, channels // CHUNK, project, 0)
        low_half = half_masks(128)
        state_scr[...] = state_scr[...] * flags_ref[at].astype(F32)

        def scan_span(span, _):
            hold_out[span] = state_scr[...]

            def scan(block, _):
                start = pl.multiple_of(span * SPAN + block * 8, 8)
                for lane in range(lanes):
                    cols = slice(lane * 128, lane * 128 + 128)
                    state = state_scr[:, cols]
                    decay = decay_ref[:, cols]
                    maps = map_ref[:, cols]
                    drive = u_out[pl.ds(start, 8), cols]
                    parts = []
                    for j in range(8):
                        state = decay * state + jnp.broadcast_to(drive[j : j + 1, :], (STATES, 128))
                        parts.append(fold_states(maps * state))
                    state_scr[:, cols] = state
                    sum_scr[pl.ds(start, 8), cols] = merge_rows(parts, low_half)
                return 0

            lax.fori_loop(0, SPAN // 8, scan, 0)
            return 0

        lax.fori_loop(0, TILE // SPAN, scan_span, 0)

        def gate(rows):
            y = sum_scr[rows, :] + shift(11) * u_out[rows, :]
            v = v_out[rows, :].astype(F32)
            y_out[rows, :] = y.astype(BF16)
            gated_out[rows, :] = (y * (v * sigmoid(v))).astype(BF16)

        by_rows(gate)
        sum_scr[...] = dot_nn(gated_out[...], mixout_ref[...])

        def third(rows):
            x2 = x1_scr[here(rows, at), :] + (sum_scr[rows, :] + shift(8))
            x2_out[rows, :] = x2
            e, _ = norm_parts(x2)
            low_scr[rows, :] = (e * gain(2) + shift(2)).astype(BF16)

        by_rows(third)
        pitch = TILE + 2 * REACH

        def widen(c, _):
            cols = columns(c)
            right = columns(c + channels // CHUNK)
            left_part = dot_nn(low_scr[...], convin_ref[:, cols]) + table_ref[15:16, cols]
            right_part = dot_nn(low_scr[...], convin_ref[:, right]) + table_ref[16:17, cols]
            p_out[:, cols] = left_part.astype(BF16)
            p_out[:, right] = right_part.astype(BF16)
            g = left_part * sigmoid(right_part)
            place = pl.ds(pl.multiple_of(at * pitch + REACH, 8), TILE)
            for k in range(CHUNK // 128):
                padded[c * (CHUNK // 128) + k, place, :] = g[:, k * 128 : k * 128 + 128]
            return 0

        lax.fori_loop(0, channels // CHUNK, widen, 0)

    @pl.when(step == 2 * tiles)
    def _():
        fill_halo(padded, flags_ref, tiles)

        def store(lane, row, base, total):
            w_out[pl.ds(pl.multiple_of(row, 64), 64), lane * 128 : lane * 128 + 128] = total

        taps_over(padded, table_ref, store, tiles, False)
        stat_out[...] = jnp.zeros_like(stat_out)

        def total(at, _):
            rows = pl.ds(pl.multiple_of(at * ROWS, ROWS), ROWS)
            stat_out[...] += fold8(w_out[rows, :])
            return 0

        lax.fori_loop(0, frames // ROWS, total, 0)
        center = jnp.sum(stat_out[...], axis=0, keepdims=True) * (1.0 / frames)
        stat_out[...] = jnp.zeros_like(stat_out)

        def spread(at, _):
            rows = pl.ds(pl.multiple_of(at * ROWS, ROWS), ROWS)
            off = w_out[rows, :] - center
            stat_out[...] += fold8(off * off)
            return 0

        lax.fori_loop(0, frames // ROWS, spread, 0)
        around = jnp.sum(stat_out[...], axis=0, keepdims=True)
        if fused:
            center, around = pool_over(center, around, frames, dp, fs, n_dp, n_fs, *swap)
            around = lax.rsqrt(around * (1.0 / (frames * n_dp * n_fs)) + EPSILON)
        stat_out[...] = jnp.zeros_like(stat_out)
        stat_out[0:1, :] = center
        stat_out[1:2, :] = around


def whole(shape):
    zeros = (0,) * len(shape)
    return pl.BlockSpec(shape, lambda *_: zeros, pipeline_mode=pl.Buffered(1))


def params(collective_id=None):
    if collective_id is None:
        return pltpu.CompilerParams(
            dimension_semantics=("arbitrary",), vmem_limit_bytes=VMEM_LIMIT
        )
    return pltpu.CompilerParams(
        dimension_semantics=("arbitrary",),
        vmem_limit_bytes=VMEM_LIMIT,
        collective_id=collective_id,
        has_side_effects=True,
    )


def front(mesh_size, flags, x, weights, collective_id=None):
    fused = mesh_size is not None
    frames, channels = x.shape
    hidden = weights[1].shape[-1] if fused else weights[0].shape[1]
    tiles = frames // TILE
    early = lambda width: pl.BlockSpec((TILE, width), lambda i: (jnp.minimum(i, tiles - 1), 0))
    place = lambda i: jnp.clip(i - tiles, 0, tiles - 1)
    late = lambda width: pl.BlockSpec((TILE, width), lambda i: (place(i), 0))
    shape = lambda width, kind: jax.ShapeDtypeStruct((frames, width), kind)
    spans = TILE // SPAN
    state = jax.ShapeDtypeStruct((STATES, channels), F32)
    out_shape = [
        shape(hidden, BF16),
        shape(channels, F32),
        shape(channels, F32),
        shape(channels, BF16),
        shape(channels, BF16),
        shape(channels, BF16),
        shape(channels, F32),
        shape(2 * channels, BF16),
        jax.ShapeDtypeStruct((frames // SPAN, STATES, channels), F32),
        shape(channels, F32),
        jax.ShapeDtypeStruct((8, channels), F32),
        jax.ShapeDtypeStruct((TABLE, channels), F32),
        jax.ShapeDtypeStruct((16, CHUNK), F32),
        state,
        state,
    ]
    out_specs = [early(hidden), early(channels)]
    out_specs += [late(channels)] * 5
    out_specs += [
        late(2 * channels),
        pl.BlockSpec((spans, STATES, channels), lambda i: (place(i), 0, 0)),
    ]
    out_specs += [whole(s.shape) for s in out_shape[9:]]
    scratch = [
        pltpu.VMEM((frames, channels), F32),
        pltpu.VMEM((frames, channels), BF16),
        pltpu.VMEM((TILE, channels), BF16),
        pltpu.VMEM((TILE, channels), F32),
        pltpu.VMEM((STATES, channels), F32),
        pltpu.VMEM((channels // 128, tiles * (TILE + 2 * REACH), 128), F32),
    ]
    in_specs = [pl.BlockSpec(memory_space=pltpu.SMEM), early(channels)]
    if fused:
        n_dp, n_fs = mesh_size
        hbm = pl.BlockSpec(memory_space=pltpu.HBM)
        in_specs += [hbm] * len(weights)
        chunks = []
        for at in (0, 1, 2, 3, 4, 5, 6, 1, 2):
            chunks.append(jax.ShapeDtypeStruct((n_dp * n_fs,) + weights[at].shape[1:], BF16))
        out_shape += chunks
        out_specs += [hbm] * len(chunks)
        scratch += [pltpu.VMEM(c.shape, BF16) for c in chunks[:WEIGHTS]]
        count = slot_count(n_dp, n_fs)
        scratch += [
            pltpu.SemaphoreType.DMA((len(chunks), count)),
            pltpu.SemaphoreType.DMA((len(chunks), count)),
            pltpu.SemaphoreType.DMA((len(chunks),)),
            pltpu.SemaphoreType.DMA((WEIGHTS,)),
        ]
        scratch += swap_scratch(n_dp, n_fs, channels)
    else:
        in_specs += [whole(a.shape) for a in weights]
    return pl.pallas_call(
        partial(front_kernel, mesh_size),
        grid=(2 * tiles + 1,),
        in_specs=in_specs,
        out_specs=out_specs,
        out_shape=out_shape,
        scratch_shapes=scratch,
        compiler_params=params(collective_id),
        name="front",
    )(flags, x, *weights)


def ffn_back(low_t, grad_t, grad_ref, h_load, up_ref, down_ref, up_acc, down_acc, bias_acc, back_scr, hidden):
    def chunk(c, _):
        cols = columns(c)
        h = h_load(cols)
        sig = sigmoid(h)
        active = h * sig
        gate = dot_nt(grad_ref[...], down_ref[cols, :])
        grad_h = (gate * (sig * (1.0 + h - active))).astype(BF16)
        bias_acc[:, cols] += fold8(grad_h.astype(F32))
        down_acc[cols, :] += dot_tn(active.astype(BF16), grad_ref[...])
        up_acc[:, cols] += dot_nn(low_t[...], grad_h)
        back_scr[...] += dot_nt(grad_h, up_ref[:, cols])
        return 0

    lax.fori_loop(0, hidden // CHUNK, chunk, 0)


def convert_rows(out, acc, step=64):
    def run(at, _):
        rows = pl.ds(pl.multiple_of(at * step, step), step)
        out[rows, :] = acc[rows, :].astype(BF16)
        return 0

    lax.fori_loop(0, acc.shape[0] // step, run, 0)


def middle_kernel(
    mesh_size,
    x2_ref,
    w_ref,
    cot_ref,
    up_ref,
    down_ref,
    convout_ref,
    bias_ref,
    vec_ref,
    stat_ref,
    out_ref,
    gx3_ref,
    gnb_ref,
    gup_out,
    gdown_out,
    gconvout_out,
    gbias_out,
    gvec_out,
    stat_out,
    up_acc,
    down_acc,
    convout_acc,
    bias_acc,
    vec_acc,
    h_scr,
    low_scr,
    turn_scr,
    act_scr,
    grad_scr,
    sum_scr,
    x3_scr,
    *swap,
):
    at = pl.program_id(0)
    tiles = pl.num_programs(0)
    channels = x2_ref.shape[1]
    if mesh_size is not None:
        n_dp, n_fs = mesh_size
        dp, fs = lax.axis_index("dp"), lax.axis_index("fsdp")

        @pl.when(at == 0)
        def _():
            greet(dp, fs, n_dp, n_fs)

    hidden = up_ref.shape[1]
    gain = lambda k: vec_ref[k : k + 1, :]
    shift = lambda k: vec_ref[6 + k : 7 + k, :]
    center, scale = stat_ref[0:1, :], stat_ref[1:2, :]

    @pl.when(at == 0)
    def _():
        for ref in (up_acc, down_acc, convout_acc, bias_acc, vec_acc):
            ref[...] = jnp.zeros_like(ref)

    def normed(rows):
        e = (w_ref[rows, :] - center) * scale
        return e, e * gain(5) + shift(5)

    def first(rows):
        _, nb = normed(rows)
        act_scr[rows, :] = (nb * sigmoid(nb)).astype(BF16)

    by_rows(first)
    sum_scr[...] = dot_nn(act_scr[...], convout_ref[...])

    def second(rows):
        x3 = x2_ref[rows, :] + (sum_scr[rows, :] + vec_ref[18:19, :])
        x3_scr[rows, :] = x3
        e, _ = norm_parts(x3)
        low_scr[rows, :] = (e * gain(3) + shift(3)).astype(BF16)
        sum_scr[rows, :] = jnp.zeros((ROWS, channels), F32)

    by_rows(second)

    def forward(c, _):
        cols = columns(c)
        h = dot_nn(low_scr[...], up_ref[:, cols]) + bias_ref[pl.ds(8 + c, 1), :]
        h_scr[:, cols] = h
        active = (h * sigmoid(h)).astype(BF16)
        sum_scr[...] += dot_nn(active, down_ref[cols, :])
        return 0

    lax.fori_loop(0, hidden // CHUNK, forward, 0)
    turn_scr[...] = low_scr[...].T

    def last(rows):
        x4 = x3_scr[rows, :] + 0.5 * (sum_scr[rows, :] + shift(7))
        e, inv = norm_parts(x4)
        out_ref[rows, :] = (e * gain(4) + shift(4)).astype(BF16)
        cot = cot_ref[rows, :].astype(F32)
        vec_acc[0] += fold8(cot * e)
        vec_acc[1] += fold8(cot)
        gx4 = norm_back(cot, e, inv, gain(4))
        gx3_ref[rows, :] = gx4
        low = (0.5 * gx4).astype(BF16)
        grad_scr[rows, :] = low
        vec_acc[2] += fold8(low.astype(F32))
        sum_scr[rows, :] = jnp.zeros((ROWS, channels), F32)

    by_rows(last)
    ffn_back(
        turn_scr,
        None,
        grad_scr,
        lambda cols: h_scr[:, cols],
        up_ref,
        down_ref,
        up_acc,
        down_acc,
        bias_acc,
        sum_scr,
        hidden,
    )

    def fourth(rows):
        e, inv = norm_parts(x3_scr[rows, :])
        grad = sum_scr[rows, :]
        vec_acc[3] += fold8(grad * e)
        vec_acc[4] += fold8(grad)
        gx3 = gx3_ref[rows, :] + norm_back(grad, e, inv, gain(3))
        gx3_ref[rows, :] = gx3
        low = gx3.astype(BF16)
        grad_scr[rows, :] = low
        vec_acc[5] += fold8(low.astype(F32))

    by_rows(fourth)
    convout_acc[...] += dot_tn(act_scr[...], grad_scr[...])
    sum_scr[...] = dot_nt(grad_scr[...], convout_ref[...])

    def fifth(rows):
        e, nb = normed(rows)
        sig = sigmoid(nb)
        gnb = sum_scr[rows, :] * (sig * (1.0 + nb * (1.0 - sig)))
        gnb_ref[rows, :] = gnb
        vec_acc[6] += fold8(gnb * e)
        vec_acc[7] += fold8(gnb)

    by_rows(fifth)

    @pl.when(at == tiles - 1)
    def _():
        for k in range(8):
            gvec_out[k : k + 1, :] = jnp.sum(vec_acc[k], axis=0, keepdims=True)

        def convert():
            convert_rows(gup_out, up_acc)
            convert_rows(gdown_out, down_acc)
            convert_rows(gconvout_out, convout_acc)
            gbias_out[...] = jnp.broadcast_to(
                jnp.sum(bias_acc[...], axis=0, keepdims=True), gbias_out.shape
            )

        stat_out[...] = stat_ref[...]
        if mesh_size is None:
            convert()
        else:
            total = sum_over(gvec_out[...], dp, fs, n_dp, n_fs, *swap, between=convert)
            share = gain(5) * (1.0 / (TILE * tiles * n_dp * n_fs))
            stat_out[2:3, :] = total[7:8, :] * share
            stat_out[3:4, :] = total[6:7, :] * share


def middle(mesh_size, x2, w, cot, up, down, convout, bias, vec, stat, collective_id=None):
    frames, channels = x2.shape
    hidden = up.shape[1]
    tiles = frames // TILE
    row = lambda width: pl.BlockSpec((TILE, width), lambda i: (i, 0))
    big = lambda a: pltpu.VMEM(a.shape, F32)
    shapes = [
        jax.ShapeDtypeStruct((frames, channels), BF16),
        jax.ShapeDtypeStruct((frames, channels), F32),
        jax.ShapeDtypeStruct((frames, channels), F32),
        jax.ShapeDtypeStruct(up.shape, BF16),
        jax.ShapeDtypeStruct(down.shape, BF16),
        jax.ShapeDtypeStruct(convout.shape, BF16),
        jax.ShapeDtypeStruct((8, hidden), F32),
        jax.ShapeDtypeStruct((8, channels), F32),
        jax.ShapeDtypeStruct((8, channels), F32),
    ]
    swap = [] if mesh_size is None else swap_scratch(*mesh_size, channels)
    return pl.pallas_call(
        partial(middle_kernel, mesh_size),
        grid=(tiles,),
        in_specs=[row(channels)] * 3
        + [whole(a.shape) for a in (up, down, convout, bias, vec, stat)],
        out_specs=[row(channels)] * 3 + [whole(s.shape) for s in shapes[3:]],
        out_shape=shapes,
        scratch_shapes=[
            big(up),
            big(down),
            big(convout),
            pltpu.VMEM((8, hidden), F32),
            pltpu.VMEM((8, 8, channels), F32),
            pltpu.VMEM((TILE, hidden), F32),
            pltpu.VMEM((TILE, channels), BF16),
            pltpu.VMEM((channels, TILE), BF16),
            pltpu.VMEM((TILE, channels), BF16),
            pltpu.VMEM((TILE, channels), BF16),
            pltpu.VMEM((TILE, channels), F32),
            pltpu.VMEM((TILE, channels), F32),
        ]
        + swap,
        compiler_params=params(collective_id),
        name="middle",
    )(x2, w, cot, up, down, convout, bias, vec, stat)


def back_kernel(mesh_size, *refs):
    fused = mesh_size is not None
    refs = list(refs)
    take = lambda count: [refs.pop(0) for _ in range(count)]
    (
        flags_ref,
        w_ref,
        gnb_ref,
        p_all,
        x2_ref,
        gx3_ref,
        gated_ref,
        y_ref,
        v_ref,
        u_ref,
        x1_ref,
        hold_ref,
        convin_ref,
        mixout_ref,
        mixin_ref,
        vec_ref,
        stat_ref,
        decay_ref,
        map_ref,
    ) = take(19)
    sources = take(3) if fused else []
    (
        gx1_ref,
        gconvin_out,
        gmixout_out,
        gmixin_out,
        gvec_out,
        gtaps_ref,
        gmap_out,
        gdecay_out,
    ) = take(8)
    reduced = take(3) if fused else []
    (
        convin_acc,
        mixout_acc,
        mixin_acc,
        vec_acc,
        map_acc,
        decay_acc,
        adj_scr,
        track,
        low_scr,
        wide_scr,
        sum_scr,
        gy_scr,
        padded,
        gpad,
    ) = take(14)
    step = pl.program_id(0)
    tiles = pl.num_programs(0) - 1
    at = tiles - jnp.maximum(step, 1)
    channels = x2_ref.shape[1]
    lanes = channels // 128
    pitch = TILE + 2 * REACH
    gain = lambda k: vec_ref[k : k + 1, :]
    shift = lambda k: vec_ref[6 + k : 7 + k, :]
    left, right = slice(0, channels), slice(channels, 2 * channels)
    if fused:
        n_dp, n_fs = mesh_size
        scratch = take(12)
        dp, fs = lax.axis_index("dp"), lax.axis_index("fsdp")

        def emit(chunk, total):
            reduced[chunk][...] = total

        plans, sends = scatter_plan(dp, fs, n_dp, n_fs, sources, emit, scratch, *take(3))
        order = waves(plans)
        points = [(0, 0), (0, 1), (0, 2), (1, 0), (1, 3), (1, 4), (2, 0), (2, 3), (2, 4)]
        points += [(tiles, 4)] * (len(order) - len(points))

    def progress(point):
        if not fused:
            return
        for wave, place in zip(order, points):
            if place[1] == point:

                @pl.when(step == place[0])
                def _(wave=wave):
                    for stage in wave:
                        stage()

    @pl.when(step == 0)
    def _():
        for ref in (convin_acc, mixout_acc, mixin_acc, vec_acc, map_acc, decay_acc, adj_scr):
            ref[...] = jnp.zeros_like(ref)
        if fused:
            greet(dp, fs, n_dp, n_fs)

    progress(0)

    @pl.when(step == 0)
    def _():
        center, scale = stat_ref[0:1, :], stat_ref[1:2, :]
        plain, cross = stat_ref[2:3, :], stat_ref[3:4, :]
        per = TILE // 64

        def fill(index, _):
            tile, inner = index // per, index % per
            rows = pl.ds(pl.multiple_of(index * 64, 64), 64)
            place = pl.ds(pl.multiple_of(tile * pitch + REACH + inner * 64, 8), 64)
            e = (w_ref[rows, :] - center) * scale
            d = gnb_ref[rows, :] * gain(5)
            gw = scale * (d - plain - e * cross)
            g = p_all[rows, left].astype(F32) * sigmoid(p_all[rows, right].astype(F32))
            for lane in range(lanes):
                cols = slice(lane * 128, lane * 128 + 128)
                padded[lane, place, :] = gw[:, cols]
                gpad[lane, place, :] = g[:, cols]
            return 0

        lax.fori_loop(0, tiles * per, fill, 0)
        fill_halo(padded, flags_ref, tiles)
        fill_halo(gpad, flags_ref, tiles)

    progress(1)

    @pl.when(step == 0)
    def _():
        block = 64
        per = TILE // block
        gtaps_ref[...] = jnp.zeros_like(gtaps_ref)
        for lane in range(lanes):

            def corr(index, sums, lane=lane):
                base = (index // per) * pitch + (index % per) * block
                here = padded[lane, pl.ds(pl.multiple_of(base + REACH, 8), block), :]
                return tuple(
                    s + fold8(here * gpad[lane, pl.ds(base + REACH + k - TAPS // 2, block), :])
                    for k, s in enumerate(sums)
                )

            sums = lax.fori_loop(0, tiles * per, corr, (jnp.zeros((8, 128), F32),) * TAPS)
            for k in range(TAPS):
                gtaps_ref[k : k + 1, lane * 128 : lane * 128 + 128] = jnp.sum(
                    sums[k], axis=0, keepdims=True
                )

        def store(lane, row, base, total):
            gpad[lane, pl.ds(pl.multiple_of(base + REACH, 8), 64), :] = total

        taps_over(padded, vec_ref, store, tiles, True)

    progress(2)

    def back_tile():
        def first(rows):
            place = pl.ds(pl.multiple_of(at * pitch + REACH + rows.start, 8), ROWS)
            here = pl.ds(pl.multiple_of(at * TILE + rows.start, ROWS), ROWS)
            grad = jnp.concatenate([gpad[lane, place, :] for lane in range(lanes)], axis=1)
            sig = sigmoid(p_all[here, right].astype(F32))
            gl = (grad * sig).astype(BF16)
            gr = (grad * p_all[here, left].astype(F32) * (sig * (1.0 - sig))).astype(BF16)
            wide_scr[rows, left] = gl
            wide_scr[rows, right] = gr
            vec_acc[0] += fold8(gl.astype(F32))
            vec_acc[1] += fold8(gr.astype(F32))
            e, _ = norm_parts(x2_ref[rows, :])
            low_scr[rows, :] = (e * gain(2) + shift(2)).astype(BF16)

        by_rows(first)
        turned = low_scr[...].T
        convin_acc[...] += dot_nn(turned, wide_scr[...])
        sum_scr[...] = dot_nt(wide_scr[...], convin_ref[...])

        def second(rows):
            e, inv = norm_parts(x2_ref[rows, :])
            grad = sum_scr[rows, :]
            vec_acc[2] += fold8(grad * e)
            vec_acc[3] += fold8(grad)
            gx2 = gx3_ref[rows, :] + norm_back(grad, e, inv, gain(2))
            gx1_ref[rows, :] = gx2
            low = gx2.astype(BF16)
            low_scr[rows, :] = low
            vec_acc[4] += fold8(low.astype(F32))

        by_rows(second)
        progress(3)
        mixout_acc[...] += dot_tn(gated_ref[...], low_scr[...])
        sum_scr[...] = dot_nt(low_scr[...], mixout_ref[...])

        def third(rows):
            grad = sum_scr[rows, :]
            v = v_ref[rows, :].astype(F32)
            sig = sigmoid(v)
            swish = v * sig
            gy = grad * swish
            gy_scr[rows, :] = gy
            wide_scr[rows, right] = (
                grad * y_ref[rows, :].astype(F32) * (sig * (1.0 + v - swish))
            ).astype(BF16)
            vec_acc[5] += fold8(gy * u_ref[rows, :])

        by_rows(third)
        progress(4)
        low_half = half_masks(128)
        later = jnp.minimum(at + 1, tiles - 1)
        adj_scr[...] = adj_scr[...] * flags_ref[later].astype(F32)

        def span_back(index, _):
            span = TILE // SPAN - 1 - index
            base = pl.multiple_of(span * SPAN, SPAN)
            for lane in range(lanes):
                cols = slice(lane * 128, lane * 128 + 128)
                decay = decay_ref[:, cols]

                def forward(block, state):
                    drive = u_ref[pl.ds(pl.multiple_of(base + block * 8, 8), 8), cols]
                    for j in range(8):
                        track[block * 8 + j, :, cols] = state
                        state = decay * state + jnp.broadcast_to(drive[j : j + 1, :], (STATES, 128))
                    return state

                lax.fori_loop(0, SPAN // 8, forward, hold_ref[span, :, cols])

            def backward(index, _):
                block = SPAN // 8 - 1 - index
                start = pl.multiple_of(base + block * 8, 8)
                for lane in range(lanes):
                    cols = slice(lane * 128, lane * 128 + 128)
                    decay = decay_ref[:, cols]
                    maps = map_ref[:, cols]
                    adj = adj_scr[:, cols]
                    drive = u_ref[pl.ds(start, 8), cols]
                    grad = gy_scr[pl.ds(start, 8), cols]
                    gmap = map_acc[:, cols]
                    gdecay = decay_acc[:, cols]
                    parts = [None] * 8
                    for j in range(7, -1, -1):
                        adj = decay * adj + jnp.broadcast_to(grad[j : j + 1, :], (STATES, 128))
                        parts[j] = fold_states(maps * adj)
                        gmap = gmap + adj * jnp.broadcast_to(drive[j : j + 1, :], (STATES, 128))
                        gdecay = gdecay + adj * track[block * 8 + j, :, cols]
                    adj_scr[:, cols] = adj
                    map_acc[:, cols] = gmap
                    decay_acc[:, cols] = gdecay
                    sum_scr[pl.ds(start, 8), cols] = merge_rows(parts, low_half)
                return 0

            lax.fori_loop(0, SPAN // 8, backward, 0)
            return 0

        lax.fori_loop(0, TILE // SPAN, span_back, 0)

        def fourth(rows):
            gu = sum_scr[rows, :] + shift(11) * gy_scr[rows, :]
            wide_scr[rows, left] = gu.astype(BF16)
            e, _ = norm_parts(x1_ref[rows, :])
            low_scr[rows, :] = (e * gain(1) + shift(1)).astype(BF16)

        by_rows(fourth)
        turned = low_scr[...].T
        mixin_acc[...] += dot_nn(turned, wide_scr[...])
        sum_scr[...] = dot_nt(wide_scr[...], mixin_ref[...])

        def fifth(rows):
            e, inv = norm_parts(x1_ref[rows, :])
            grad = sum_scr[rows, :]
            vec_acc[6] += fold8(grad * e)
            vec_acc[7] += fold8(grad)
            gx1_ref[rows, :] = gx1_ref[rows, :] + norm_back(grad, e, inv, gain(1))

        by_rows(fifth)

        @pl.when(step == tiles)
        def _():
            convert_rows(gconvin_out, convin_acc)
            convert_rows(gmixout_out, mixout_acc)
            convert_rows(gmixin_out, mixin_acc)
            for k in range(8):
                gvec_out[k : k + 1, :] = jnp.sum(vec_acc[k], axis=0, keepdims=True)
            gmap_out[...] = map_acc[...]
            gdecay_out[...] = decay_acc[...] * map_ref[...]

    @pl.when(step > 0)
    def _():
        back_tile()

    if fused:

        @pl.when(step == tiles)
        def _():
            for wait in sends:
                wait()


def back(mesh_size, flags, w, gnb, p, x2, gx3, gated, y, v, u, x1, hold, convin, mixout, mixin, vec, stat, decay, maps, grads=(), collective_id=None):
    fused = mesh_size is not None
    frames, channels = x2.shape
    tiles = frames // TILE
    place = lambda i: tiles - jnp.maximum(i, 1)
    row = lambda width: pl.BlockSpec((TILE, width), lambda i: (place(i), 0))
    spans = TILE // SPAN
    big = lambda a: pltpu.VMEM(a.shape, F32)
    state = jax.ShapeDtypeStruct((STATES, channels), F32)
    shapes = [
        jax.ShapeDtypeStruct((frames, channels), F32),
        jax.ShapeDtypeStruct(convin.shape, BF16),
        jax.ShapeDtypeStruct(mixout.shape, BF16),
        jax.ShapeDtypeStruct(mixin.shape, BF16),
        jax.ShapeDtypeStruct((8, channels), F32),
        jax.ShapeDtypeStruct((16, channels), F32),
        state,
        state,
    ]
    pad = pltpu.VMEM((channels // 128, tiles * (TILE + 2 * REACH), 128), F32)
    scratch = [
        big(convin),
        big(mixout),
        big(mixin),
        pltpu.VMEM((8, 8, channels), F32),
        pltpu.VMEM((STATES, channels), F32),
        pltpu.VMEM((STATES, channels), F32),
        pltpu.VMEM((STATES, channels), F32),
        pltpu.VMEM((SPAN, STATES, channels), F32),
        pltpu.VMEM((TILE, channels), BF16),
        pltpu.VMEM((TILE, 2 * channels), BF16),
        pltpu.VMEM((TILE, channels), F32),
        pltpu.VMEM((TILE, channels), F32),
        pad,
        pad,
    ]
    if fused:
        tails = [g.shape[1:] for g in grads]
        shapes += [jax.ShapeDtypeStruct(t, F32) for t in tails]
        scratch += scatter_scratch(*mesh_size, tails) + scatter_sems(*mesh_size, len(tails))
    return pl.pallas_call(
        partial(back_kernel, mesh_size),
        grid=(tiles + 1,),
        in_specs=[pl.BlockSpec(memory_space=pltpu.SMEM)]
        + [whole(a.shape) for a in (w, gnb, p)]
        + [row(channels)] * 7
        + [pl.BlockSpec((spans, STATES, channels), lambda i: (place(i), 0, 0))]
        + [whole(a.shape) for a in (convin, mixout, mixin, vec, stat, decay, maps)]
        + [pl.BlockSpec(memory_space=pltpu.HBM)] * len(grads),
        out_specs=[row(channels)] + [whole(s.shape) for s in shapes[1:]],
        out_shape=shapes,
        scratch_shapes=scratch,
        compiler_params=params(collective_id),
        name="back",
    )(flags, w, gnb, p, x2, gx3, gated, y, v, u, x1, hold, convin, mixout, mixin, vec, stat, decay, maps, *grads)


def small_gradients(out, gvec1, gvec2, gvec3, gtaps, gmap, gdecay, table_ref):
    out[...] = jnp.zeros_like(out)
    gains = {1: (gvec2, 6), 2: (gvec2, 2), 3: (gvec1, 3), 4: (gvec1, 0), 5: (gvec1, 6)}
    shifts = {1: (gvec2, 7), 2: (gvec2, 3), 3: (gvec1, 4), 4: (gvec1, 1), 5: (gvec1, 7)}
    shifts.update({6: (gvec3, 0), 7: (gvec1, 2), 8: (gvec2, 4), 9: (gvec2, 0), 10: (gvec2, 1)})
    shifts.update({11: (gvec2, 5), 12: (gvec1, 5)})
    for at, (ref, row) in gains.items():
        out[at : at + 1, :] = ref[row : row + 1, :]
    for at, (ref, row) in shifts.items():
        out[6 + at : 7 + at, :] = ref[row : row + 1, :]
    out[TAP_ROW : TAP_ROW + TAPS, :] = gtaps[:TAPS, :]
    log_decay, decay, root, maps_in, maps_out = state_terms(table_ref)
    both = gmap[...] * root
    out[MAP_IN:MAP_OUT, :] = both * maps_out
    out[MAP_OUT:TABLE, :] = both * maps_in
    turn = (1.0 - root * root) / root
    out[RATE:MAP_IN, :] = log_decay * (
        gdecay[...] * decay - gmap[...] * maps_in * maps_out * turn
    )


def tail_kernel(mesh_size, *refs):
    fused = mesh_size is not None
    refs = list(refs)
    take = lambda count: [refs.pop(0) for _ in range(count)]
    x_ref, h_ref, gx1_ref, up_ref, down_ref, table_ref = take(6)
    if fused:
        gvec1, gvec2, gtaps, gmap, gdecay, gbias1 = take(6)
        sources = take(3)
        gx_ref, last_out = take(2)
        reduced = take(7)
    else:
        gx_ref, gvec_out, gbias_out, up_out, down_out = take(5)
    turn_scr, grad_scr, gh_scr, vec_acc, bias_scr = take(5)
    step = pl.program_id(0)
    frames, channels = x_ref.shape
    hidden = up_ref.shape[1]
    chunks = hidden // CHUNK
    tiles = frames // TILE
    first_b, first_c = 1 + chunks, 1 + 2 * chunks
    schedule = {}
    if fused:
        n_dp, n_fs = mesh_size
        down_src, left_src, right_src, small_src, small_scr, gvec3 = take(6)
        scratch = take(28)
        sems = take(3)
        swap = take(4)
        dp, fs = lax.axis_index("dp"), lax.axis_index("fsdp")
        down_out = ref_rows(down_src)
        halves = (ref_rows(left_src), ref_rows(right_src))

        def emit(chunk, total):
            reduced[chunk][...] = total

        plans, sends = scatter_plan(
            dp,
            fs,
            n_dp,
            n_fs,
            sources + [down_src, left_src, right_src, small_src],
            emit,
            scratch,
            *sems,
        )
        depth = len(plans[0])
        starts = [0, 0, 0, first_b, first_b + chunks // 2, first_c, first_c]
        for chunk, begin in enumerate(starts):
            for stage in range(depth):
                at = begin + 2 * stage if chunk < 5 else begin + stage
                schedule.setdefault(min(at, first_c + tiles), []).append((stage, chunk))
    last_step = first_c + tiles - 1

    def progress(at):
        for stage, chunk in sorted(schedule.get(at, [])):
            plans[chunk][stage]()

    @pl.when(step == 0)
    def _():
        if fused:
            greet(dp, fs, n_dp, n_fs)
        progress(0)
        vec_acc[...] = jnp.zeros_like(vec_acc)

        def first(rows):
            e, _ = norm_parts(x_ref[rows, :].astype(F32))
            low = (e * table_ref[0:1, :] + table_ref[6:7, :]).astype(BF16)
            turn_scr[:, rows] = low.T
            grad = (0.5 * gx1_ref[rows, :]).astype(BF16)
            grad_scr[rows, :] = grad
            vec_acc[0] += fold8(grad.astype(F32))

        by_rows(first, frames)

    if fused:
        for at in range(1, last_step + 1):
            if at in schedule and at != first_c:

                @pl.when(step == at)
                def _(at=at):
                    progress(at)

    @pl.when((step >= 1) & (step < first_b))
    def _():
        h = h_ref[...].astype(F32)
        active = (h * sigmoid(h)).astype(BF16)
        down_out[columns(step - 1), :] = dot_tn(active, grad_scr[...]).astype(BF16)

    def second_half(c, store):
        cols = columns(c)
        h = h_ref[...].astype(F32)
        sig = sigmoid(h)
        gate = dot_nt(grad_scr[...], down_ref[cols, :])
        grad_h = (gate * (sig * (1.0 + h * (1.0 - sig)))).astype(BF16)
        gh_scr[:, cols] = grad_h
        bias_scr[pl.ds(c, 1), :] = jnp.sum(fold8(grad_h.astype(F32)), axis=0, keepdims=True)
        store(dot_nn(turn_scr[...], grad_h).astype(BF16))

    if fused:
        for half in range(2):
            begin = first_b + half * (chunks // 2)

            @pl.when((step >= begin) & (step < begin + chunks // 2))
            def _(half=half, begin=begin):
                def store(value):
                    halves[half][:, columns(step - begin)] = value

                second_half(step - first_b, store)

    else:

        @pl.when((step >= first_b) & (step < first_c))
        def _():
            def store(value):
                up_out[:, columns(step - first_b)] = value

            second_half(step - first_b, store)

    if fused:

        @pl.when(step == first_c)
        def _():
            gvec3[0:1, :] = jnp.sum(vec_acc[0], axis=0, keepdims=True)
            small_gradients(small_scr, gvec1, gvec2, gvec3, gtaps, gmap, gdecay, table_ref)
            narrow = small_scr[...].T.astype(BF16)
            devices = small_src.shape[0]
            small_src[:, :, :256] = narrow.reshape((devices, 16, 256))
            for c in range(chunks):
                bias_scr[chunks + c : chunks + c + 1, :] = gbias1[0:1, c * CHUNK : c * CHUNK + CHUNK]
            bias = bias_scr[...].astype(BF16)
            small_src[:, :, 256:] = jnp.broadcast_to(bias[None], (devices, 16, CHUNK))
            progress(first_c)

    @pl.when(step >= first_c)
    def _():
        tile = step - first_c
        whole_tile = pl.ds(pl.multiple_of(tile * TILE, TILE), TILE)
        back = [
            dot_nt(gh_scr[whole_tile, :], up_ref[k * CHUNK : k * CHUNK + CHUNK, :])
            for k in range(channels // CHUNK)
        ]
        for k, value in enumerate(back):
            gx_ref[:, k * CHUNK : k * CHUNK + CHUNK] = value

        def second(rows):
            here = pl.ds(pl.multiple_of(tile * TILE + rows.start, ROWS), ROWS)
            e, inv = norm_parts(x_ref[here, :].astype(F32))
            grad = gx_ref[rows, :]
            vec_acc[1] += fold8(grad * e)
            vec_acc[2] += fold8(grad)
            gx_ref[rows, :] = gx1_ref[here, :] + norm_back(grad, e, inv, table_ref[0:1, :])

        by_rows(second)

    @pl.when(step == last_step)
    def _():
        if fused:
            last_out[...] = jnp.zeros_like(last_out)
            for k in range(2):
                last_out[k : k + 1, :] = jnp.sum(vec_acc[1 + k], axis=0, keepdims=True)
            ends = sorted(schedule.get(last_step + 1, []))

            def between():
                for stage, chunk in ends:
                    plans[chunk][stage]()

            last_out[...] = sum_over(last_out[...], dp, fs, n_dp, n_fs, *swap, between=between)
            for wait in sends:
                wait()
        else:
            gvec_out[...] = jnp.zeros_like(gvec_out)
            for k in range(3):
                gvec_out[k : k + 1, :] = jnp.sum(vec_acc[k], axis=0, keepdims=True)
            gbias_out[...] = bias_scr[...]


def tail(mesh_size, x, h, gx1, up, down, table, others=(), grads=(), collective_id=None):
    fused = mesh_size is not None
    frames, channels = x.shape
    hidden = up.shape[1]
    tiles, chunks = frames // TILE, hidden // CHUNK
    first_b, first_c = 1 + chunks, 1 + 2 * chunks
    place = lambda i: jnp.where(
        i < first_b, jnp.maximum(i - 1, 0), jnp.minimum(i - first_b, chunks - 1)
    )
    shapes = [jax.ShapeDtypeStruct((frames, channels), F32)]
    scratch = [
        pltpu.VMEM((channels, frames), BF16),
        pltpu.VMEM((frames, channels), BF16),
        pltpu.VMEM((frames, hidden), BF16),
        pltpu.VMEM((8, 8, channels), F32),
        pltpu.VMEM((2 * chunks, CHUNK), F32),
    ]
    if fused:
        devices = mesh_size[0] * mesh_size[1]
        tails = [g.shape[1:] for g in grads]
        own = [(hidden // devices, channels)] + [(channels // devices, hidden // 2)] * 2
        own.append((16, 2 * CHUNK))
        shapes.append(jax.ShapeDtypeStruct((8, channels), F32))
        shapes += [jax.ShapeDtypeStruct(t, F32) for t in tails + own]
        scratch += [pltpu.VMEM((devices,) + t, BF16) for t in own]
        scratch += [pltpu.VMEM((256, channels), F32), pltpu.VMEM((8, channels), F32)]
        scratch += scatter_scratch(*mesh_size, tails + own)
        scratch += scatter_sems(*mesh_size, len(tails + own))
        scratch += swap_scratch(*mesh_size, channels)
    else:
        shapes += [
            jax.ShapeDtypeStruct((8, channels), F32),
            jax.ShapeDtypeStruct((2 * chunks, CHUNK), F32),
            jax.ShapeDtypeStruct(up.shape, BF16),
            jax.ShapeDtypeStruct(down.shape, BF16),
        ]
    return pl.pallas_call(
        partial(tail_kernel, mesh_size),
        grid=(first_c + tiles,),
        in_specs=[whole(x.shape), pl.BlockSpec((frames, CHUNK), lambda i: (0, place(i)))]
        + [whole(a.shape) for a in (gx1, up, down, table) + tuple(others)]
        + [pl.BlockSpec(memory_space=pltpu.HBM)] * len(grads),
        out_specs=[
            pl.BlockSpec((TILE, channels), lambda i: (jnp.maximum(i - first_c, 0), 0))
        ]
        + [whole(s.shape) for s in shapes[1:]],
        out_shape=shapes,
        scratch_shapes=scratch,
        compiler_params=params(collective_id),
        name="tail",
    )(x, h, gx1, up, down, table, *others, *grads)


def unpack_kernel(
    place_ref,
    up1_ref,
    down1_ref,
    convout_ref,
    convin_ref,
    mixout_ref,
    mixin_ref,
    down0_ref,
    left_ref,
    right_ref,
    small_ref,
    last_ref,
    up_out,
    down_out,
    bias_out,
    mixin_out,
    mixout_out,
    convin_out,
    convout_out,
    convbias_out,
    rate_out,
    map_out,
    taps_out,
    gains_out,
    shifts_out,
):
    mine = place_ref[0]
    half = left_ref.shape[1]
    up_out[0, :, :half] = left_ref[...]
    up_out[0, :, half:] = right_ref[...]
    up_out[1] = up1_ref[...]
    down_out[0] = down0_ref[...]
    down_out[1] = down1_ref[...]
    mixin_out[...] = mixin_ref[...]
    mixout_out[...] = mixout_ref[...]
    convin_out[...] = convin_ref[...]
    convout_out[...] = convout_ref[...]
    count = bias_out.shape[1]
    row = (mine * count) // CHUNK
    inner = mine * count - row * CHUNK
    for layer in range(2):
        line = small_ref[pl.ds(8 * layer + row, 1), CHUNK:]
        line = pltpu.roll(jnp.broadcast_to(line, (8, CHUNK)), CHUNK - inner, 1)
        bias_out[layer : layer + 1, :] = line[0:1, :count]
    own = small_ref.shape[0]
    channels = last_ref.shape[1]
    first = pltpu.roll(last_ref[...], channels - mine * own, 1)[:, :128].T[:own, :]
    small = small_ref[:, :256]
    gains_out[...] = small[:, :6]
    gains_out[:, 0:1] = first[:, 0:1]
    shifts_out[...] = small[:, 6:18]
    shifts_out[:, 0:1] = first[:, 1:2]
    convbias_out[...] = small[:, 18:19]
    taps_out[...] = small[:, TAP_ROW : TAP_ROW + TAPS]
    rate_out[...] = small[:, RATE:MAP_IN]
    map_out[0] = small[:, MAP_IN:MAP_OUT]
    map_out[1] = small[:, MAP_OUT:TABLE]


def unpack(mine, up1, down1, convout, convin, mixout, mixin, down0, left, right, small, last, hidden):
    own = small.shape[0]
    devices = last.shape[1] // own
    f32 = lambda *shape: jax.ShapeDtypeStruct(shape, F32)
    vmem = pl.BlockSpec(memory_space=pltpu.VMEM)
    return pl.pallas_call(
        unpack_kernel,
        in_specs=[pl.BlockSpec(memory_space=pltpu.SMEM)] + [vmem] * 11,
        out_specs=[vmem] * 13,
        out_shape=[
            f32(2, *up1.shape),
            f32(2, *down1.shape),
            f32(2, hidden // devices),
            f32(*mixin.shape),
            f32(*mixout.shape),
            f32(*convin.shape),
            f32(*convout.shape),
            f32(own, 1),
            f32(own, STATES),
            f32(2, own, STATES),
            f32(own, TAPS),
            f32(own, 6),
            f32(own, 12),
        ],
        name="unpack",
    )(mine, up1, down1, convout, convin, mixout, mixin, down0, left, right, small, last)


def pack_table(gains, shifts, conv_bias, taps, rate, maps):
    channels = gains.shape[1]
    blank = lambda rows: jnp.zeros((rows, channels), gains.dtype)
    parts = [gains, shifts, conv_bias[None], blank(TAP_ROW - 19), taps, blank(RATE - TAP_ROW - TAPS)]
    parts += [rate, maps[0], maps[1], blank(256 - TABLE)]
    return jnp.concatenate(parts, axis=0).T


def pack_bias(bias, place):
    layers, count = bias.shape
    hidden = 16 * CHUNK // layers
    wide = lax.dynamic_update_slice(
        jnp.zeros((layers, hidden), bias.dtype), bias, (0, place * count)
    )
    return wide.reshape((16, CHUNK))


def unpack_table(table):
    return (
        table[0:6],
        table[6:18],
        table[18],
        table[TAP_ROW : TAP_ROW + TAPS],
        table[RATE:MAP_IN],
        jnp.stack([table[MAP_IN:MAP_OUT], table[MAP_OUT:TABLE]]),
    )


def on_device(
    n_dp,
    n_fs,
    frames,
    seq_lengths,
    seq_offsets,
    seq_counts,
    ffn_up,
    ffn_down,
    ffn_bias_up,
    mix_in,
    mix_out,
    conv_in,
    conv_out,
    conv_out_bias,
    ssm_rate,
    ssm_map,
    conv_kernel,
    gains,
    shifts,
    cotangent,
):
    devices = n_dp * n_fs
    mine = lax.axis_index("dp") * n_fs + lax.axis_index("fsdp")
    frames_dev, channels = frames.shape
    tiles = frames_dev // TILE
    slot = jnp.arange(seq_offsets.shape[1], dtype=jnp.int32)
    begins = (seq_offsets[0][None, :] == TILE * jnp.arange(tiles, dtype=jnp.int32)[:, None]) & (
        slot < seq_counts[0]
    )
    flags = 1 - jnp.max(begins.astype(jnp.int32), axis=1)
    small = pack_table(gains, shifts, conv_out_bias, conv_kernel, ssm_rate, ssm_map)
    bias = pack_bias(ffn_bias_up, mine)
    fused = small.shape[0] % 16 == 0
    shards = [ffn_up, ffn_down, mix_in[None], mix_out[None], conv_in[None], conv_out[None]]
    if fused:
        small = jnp.concatenate([small, bias], axis=1)
        made = front((n_dp, n_fs), flags, frames, [small[None]] + shards, 1)
        _, up0, down0, mixin, mixout, convin, convout, up1, down1 = [
            g.reshape((-1, g.shape[-1])) for g in made[15:]
        ]
        stat = made[10]
    else:
        got = gather_all(n_dp, n_fs, [small[None], bias[None]] + shards, 1)
        small, _, up0, up1, down0, down1, mixin, mixout, convin, convout = [
            g.reshape((-1, g.shape[-1])) for g in got
        ]
        made = front(
            None,
            flags,
            frames,
            [
                up0,
                down0,
                mixin,
                mixout,
                convin,
                small.astype(F32).T[:TABLE],
                jnp.sum(got[1].astype(F32), axis=0),
            ],
        )
        pool = exchange(n_dp, n_fs, made[10], frames_dev, 2, pool_kernel)
        scale = lax.rsqrt(pool[1:2] / (frames_dev * devices) + EPSILON)
        stat = jnp.concatenate([pool[0:1], scale, jnp.zeros((6, channels), F32)])
    h0, x1, u, v, y, gated, x2, p, hold, w, _, table, bias, decay, coupling = made[:15]
    size = (n_dp, n_fs) if fused else None
    result, gx3, gnb, gup1, gdown1, gconvout, gbias1, gvec1, stat = middle(
        size, x2, w, cotangent, up1, down1, convout, bias, table, stat, 2 if fused else None
    )
    if not fused:
        sums = exchange(n_dp, n_fs, gvec1, 1, 4, total_kernel)[6:8]
        sums = sums * (table[5:6] / (frames_dev * devices))
        stat = jnp.concatenate([stat[0:2], sums[1:2], sums[0:1], stat[4:8]])
    wide = lambda g: g.reshape((devices, g.shape[0] // devices, g.shape[1]))
    grads = tuple(wide(g) for g in (gup1, gdown1, gconvout))
    made = back(
        size,
        flags,
        w,
        gnb,
        p,
        x2,
        gx3,
        gated,
        y,
        v,
        u,
        x1,
        hold,
        convin,
        mixout,
        mixin,
        table,
        stat,
        decay,
        coupling,
        grads if fused else (),
        3 if fused else None,
    )
    gx1, gconvin, gmixout, gmixin, gvec2, gtaps, gmap, gdecay = made[:8]
    if fused:
        gx, last, *late = tail(
            size,
            frames,
            h0,
            gx1,
            up0,
            down0,
            table,
            (gvec1, gvec2, gtaps, gmap, gdecay, gbias1),
            tuple(wide(g) for g in (gconvin, gmixout, gmixin)),
            4,
        )
        (
            up_grad,
            down_grad,
            bias_grad,
            mixin_grad,
            mixout_grad,
            convin_grad,
            convout_grad,
            convbias_grad,
            rate_grad,
            map_grad,
            taps_grad,
            gains_grad,
            shifts_grad,
        ) = unpack(mine.reshape((1,)), *made[8:], *late, last, up0.shape[1])
        return (
            result,
            gx,
            up_grad,
            down_grad,
            bias_grad,
            mixin_grad,
            mixout_grad,
            convin_grad,
            convout_grad,
            convbias_grad.reshape((-1,)),
            rate_grad.T,
            map_grad.transpose((0, 2, 1)),
            taps_grad.T,
            gains_grad.T,
            shifts_grad.T,
        )
    gx, gvec3, gbias0, gup0, gdown0 = tail(None, frames, h0, gx1, up0, down0, table)

    def weights_of(log_rate, maps):
        log_decay = -jnp.exp(log_rate)
        root = jnp.sqrt(-jnp.expm1(2.0 * log_decay))
        return jnp.exp(log_decay), maps[0] * root * maps[1]

    rate, maps = unpack_table(table)[4:]
    rate_grad, map_grad = jax.vjp(weights_of, rate, maps)[1]((gdecay, gmap))
    gain_grad = jnp.stack([gvec3[1], gvec2[6], gvec2[2], gvec1[3], gvec1[0], gvec1[6]])
    rows = [gvec3[2], gvec2[7], gvec2[3], gvec1[4], gvec1[1], gvec1[7], gvec3[0], gvec1[2]]
    rows += [gvec2[4], gvec2[0], gvec2[1], gvec2[5]]
    small_grad = pack_table(
        gain_grad, jnp.stack(rows), gvec1[5], gtaps[:TAPS], rate_grad, map_grad
    )
    bias_grad = jnp.concatenate([gbias0[:8], gbias1[0].reshape((8, CHUNK))])
    reduced = scatter_all(
        n_dp,
        n_fs,
        list(grads)
        + [wide(g) for g in (gconvin, gmixout, gmixin, gup0, gdown0)]
        + [
            wide(small_grad.astype(BF16)),
            jnp.broadcast_to(bias_grad.astype(BF16), (devices, 16, CHUNK)),
        ],
        5,
    )
    gains_grad, shifts_grad, conv_bias_grad, taps_grad, rate_grad, map_grad = unpack_table(
        reduced[8].T
    )
    bias_grad = reduced[9].reshape((2, -1))
    count = bias_grad.shape[1] // devices
    bias_grad = lax.dynamic_slice(bias_grad, (0, mine * count), (2, count))
    return (
        result,
        gx,
        jnp.stack([reduced[6], reduced[0]]),
        jnp.stack([reduced[7], reduced[1]]),
        bias_grad,
        reduced[5],
        reduced[4],
        reduced[3],
        reduced[2],
        conv_bias_grad,
        rate_grad,
        map_grad,
        taps_grad,
        gains_grad,
        shifts_grad,
    )


def solution(mesh):
    both = ("dp", "fsdp")
    row, row1 = P(both, None), P(both)
    col, col3, mid = P(None, both), P(None, None, both), P(None, both, None)
    in_specs = (
        row,
        row,
        row,
        row1,
        mid,
        mid,
        col,
        row,
        row,
        row,
        row,
        row1,
        col,
        col3,
        col,
        col,
        col,
        row,
    )
    out_specs = (row, row, mid, mid, col, row, row, row, row, row1, col, col3, col, col, col)
    return jax.shard_map(
        partial(on_device, mesh.shape["dp"], mesh.shape["fsdp"]),
        mesh=mesh,
        in_specs=in_specs,
        out_specs=out_specs,
        check_vma=False,
    )
```

```python
import itertools
from functools import partial

import jax
import jax.numpy as jnp
from jax import lax
from jax.experimental import pallas as pl
from jax.experimental.pallas import tpu as pltpu
from jax.sharding import PartitionSpec as P

MESH = pl.DeviceIdType.MESH
BF16 = jnp.bfloat16
F32 = jnp.float32


def flip(index, bit):
    return index + bit * (1 - 2 * lax.rem(lax.div(index, bit), 2))


def flip_all(index, bits):
    for bit in bits:
        index = flip(index, bit)
    return index


def combos(bits):
    found = [()]
    for bit in bits:
        found = found + [entry + (bit,) for entry in found]
    return found


def plan_bits(n_dp):
    bits, bit = [], 2
    while bit < n_dp:
        bits.append(bit)
        bit *= 2
    return tuple(bits)


def greet(dp, fs, n_dp, n_fs):
    barrier = pltpu.get_barrier_semaphore()
    for step in range(1, n_dp):
        pl.semaphore_signal(
            barrier, inc=1, device_id=(lax.rem(dp + step, n_dp), fs), device_id_type=MESH
        )
    for step in range(1, n_fs):
        pl.semaphore_signal(
            barrier, inc=1, device_id=(dp, lax.rem(fs + step, n_fs)), device_id_type=MESH
        )
    pl.semaphore_wait(barrier, n_dp + n_fs - 2)


def gather_plan(dp, fs, n_dp, n_fs, sources, outs, send_sem, recv_sem, local_sem):
    bits = plan_bits(n_dp)
    orders = (bits, bits[::-1])
    half = n_fs // 2
    sends = []

    def stages(chunk):
        src, out = sources[chunk], outs[chunk]
        slots = itertools.count()

        def zone(where, part):
            if part is None:
                return out.at[pl.ds(where * n_fs, n_fs)]
            return out.at[pl.ds(where * n_fs + part * half, half)]

        def remote(slot, view_from, view_to, device):
            return pltpu.make_async_remote_copy(
                src_ref=view_from,
                dst_ref=view_to,
                send_sem=send_sem.at[chunk, slot],
                recv_sem=recv_sem.at[chunk, slot],
                device_id=device,
                device_id_type=MESH,
            )

        def launch(make):
            make().start()
            sends.append(lambda: make().wait_send())

        z_slots = [next(slots) for _ in range(1, n_fs)]

        def own_copy():
            return pltpu.make_async_copy(src, out.at[dp * n_fs + fs], local_sem.at[chunk])

        def start():
            own_copy().start()
            for step in range(1, n_fs):
                launch(
                    lambda step=step: remote(
                        z_slots[step - 1],
                        src,
                        out.at[dp * n_fs + fs],
                        (dp, lax.rem(fs + step, n_fs)),
                    )
                )

        def wait_z():
            own_copy().wait()
            for step in range(1, n_fs):
                origin = dp * n_fs + lax.rem(fs + n_fs - step, n_fs)
                remote(z_slots[step - 1], src, out.at[origin], (dp, fs)).wait_recv()

        steps, before = [start], wait_z
        for depth in range(len(bits)):
            plan = []
            for part, order in enumerate(orders):
                for entry in combos(order[:depth]):
                    plan.append((next(slots), part, order[depth], entry))

            def view(slot, part, bit, entry, arrived):
                where = flip_all(flip(dp, bit) if arrived else dp, entry)
                return remote(slot, zone(where, part), zone(where, part), (flip(dp, bit), fs))

            def go(plan=plan, before=before, view=view):
                before()
                for item in plan:
                    launch(lambda item=item: view(*item, False))

            def arrive(plan=plan, view=view):
                for item in plan:
                    view(*item, True).wait_recv()

            steps.append(go)
            before = arrive
        last = [(next(slots), entry) for entry in combos(bits)]

        def across(slot, entry, arrived):
            where = flip_all(flip(dp, 1) if arrived else dp, entry)
            return remote(slot, zone(where, None), zone(where, None), (flip(dp, 1), fs))

        def cross(before=before):
            before()
            for item in last:
                launch(lambda item=item: across(*item, False))

        def finish():
            for item in last:
                across(*item, True).wait_recv()

        return steps + [cross, finish]

    return [stages(chunk) for chunk in range(len(outs))], sends


def waves(plans):
    depth = len(plans[0])
    out = []
    for wave in range(len(plans) + depth - 1):
        out.append(
            [plans[c][wave - c] for c in range(len(plans)) if 0 <= wave - c < depth]
        )
    return out


def gather_kernel(n_dp, n_fs, layers, *refs):
    n_in = len(layers)
    n_out = sum(layers)
    ins, outs = refs[:n_in], refs[n_in : n_in + n_out]
    send_sem, recv_sem, local_sem = refs[n_in + n_out :]
    sources = []
    for ref, count in zip(ins, layers):
        sources += [ref.at[layer] for layer in range(count)]
    dp, fs = lax.axis_index("dp"), lax.axis_index("fsdp")
    greet(dp, fs, n_dp, n_fs)
    plans, sends = gather_plan(dp, fs, n_dp, n_fs, sources, outs, send_sem, recv_sem, local_sem)
    for wave in waves(plans):
        for stage in wave:
            stage()
    for wait in sends:
        wait()


def slot_count(n_dp, n_fs):
    nb = len(plan_bits(n_dp))
    return n_fs - 1 + 2 * (2**nb - 1) + 2**nb


def gather_all(n_dp, n_fs, arrays, collective_id):
    layers = tuple(a.shape[0] for a in arrays)
    outs = []
    for a in arrays:
        outs += [jax.ShapeDtypeStruct((n_dp * n_fs,) + a.shape[1:], a.dtype)] * a.shape[0]
    count = slot_count(n_dp, n_fs)
    return pl.pallas_call(
        partial(gather_kernel, n_dp, n_fs, layers),
        out_shape=outs,
        in_specs=[pl.BlockSpec(memory_space=pltpu.HBM)] * len(arrays),
        out_specs=[pl.BlockSpec(memory_space=pltpu.HBM)] * len(outs),
        scratch_shapes=[
            pltpu.SemaphoreType.DMA((len(outs), count)),
            pltpu.SemaphoreType.DMA((len(outs), count)),
            pltpu.SemaphoreType.DMA((len(outs),)),
        ],
        compiler_params=pltpu.CompilerParams(collective_id=collective_id, has_side_effects=True),
        name="gather_parameters",
    )(*arrays)


def scatter_plan(dp, fs, n_dp, n_fs, ins, emit, scratch, send_sem, recv_sem, local_sem, first=0):
    bits = plan_bits(n_dp)
    orders = (bits[::-1], bits)
    half = n_fs // 2
    index = {entry: at for at, entry in enumerate(combos(bits))}
    sends = []

    def add_into(kept, other):
        def body(at, _):
            kept[at] = (kept[at].astype(F32) + other[at].astype(F32)).astype(BF16)
            return 0

        lax.fori_loop(0, kept.shape[0], body, 0)

    def stages(chunk):
        src = ins[chunk]
        cross_in, own, later, last = scratch[4 * chunk : 4 * chunk + 4]
        slots = itertools.count()

        def remote(slot, view_from, view_to, device):
            return pltpu.make_async_remote_copy(
                src_ref=view_from,
                dst_ref=view_to,
                send_sem=send_sem.at[first + chunk, slot],
                recv_sem=recv_sem.at[first + chunk, slot],
                device_id=device,
                device_id_type=MESH,
            )

        def launch(make):
            make().start()
            sends.append(lambda: make().wait_send())

        def zone(entry, crossed):
            return src.at[pl.ds(flip_all(flip(dp, 1) if crossed else dp, entry) * n_fs, n_fs)]

        pieces = [(next(slots), entry, index[entry]) for entry in combos(bits)]

        def load(entry, at):
            return pltpu.make_async_copy(
                zone(entry, False), own.at[at], local_sem.at[first + chunk, at]
            )

        def across(slot, entry, at):
            return remote(slot, zone(entry, True), cross_in.at[at], (flip(dp, 1), fs))

        def start():
            for item in pieces:
                launch(lambda item=item: across(*item))
            for _, entry, at in pieces:
                load(entry, at).start()

        def fold_cross():
            for slot, entry, at in pieces:
                load(entry, at).wait()
                across(slot, entry, at).wait_recv()
                add_into(own.at[at], cross_in.at[at])

        steps, before = [start], fold_cross
        used = 0
        for depth in range(len(bits)):
            plan = []
            for part, order in enumerate(orders):
                bit, gone = order[depth], order[:depth]
                for entry in combos(bits):
                    if not (set(entry) & set(gone)) and bit not in entry:
                        away = tuple(sorted(entry + (bit,)))
                        plan.append((next(slots), part, bit, index[away], index[entry], used))
                        used += 1

            def move(slot, part, bit, away, kept, place):
                return remote(
                    slot,
                    own.at[away, pl.ds(part * half, half)],
                    later.at[place],
                    (flip(dp, bit), fs),
                )

            def go(plan=plan, before=before, move=move):
                before()
                for item in plan:
                    launch(lambda item=item: move(*item))

            def fold(plan=plan, move=move):
                for item in plan:
                    move(*item).wait_recv()
                    _, part, _, _, kept, place = item
                    add_into(own.at[kept, pl.ds(part * half, half)], later.at[place])

            steps.append(go)
            before = fold
        z_slots = [next(slots) for _ in range(1, n_fs)]

        def along(step):
            to = lax.rem(fs + step, n_fs)
            return remote(z_slots[step - 1], own.at[0, to], last.at[step - 1], (dp, to))

        def spread(before=before):
            before()
            for step in range(1, n_fs):
                launch(lambda step=step: along(step))

        def finish():
            total = own[0, fs].astype(F32)
            for step in range(1, n_fs):
                along(step).wait_recv()
                total = total + last[step - 1].astype(F32)
            emit(chunk, total)

        return steps + [spread, finish]

    return [stages(chunk) for chunk in range(len(ins))], sends


def scatter_scratch(n_dp, n_fs, tails):
    pieces = 2 ** len(plan_bits(n_dp))
    scratch = []
    for tail in tails:
        scratch += [
            pltpu.VMEM((pieces, n_fs) + tail, BF16),
            pltpu.VMEM((pieces, n_fs) + tail, BF16),
            pltpu.VMEM((2 * (pieces - 1), n_fs // 2) + tail, BF16),
            pltpu.VMEM((n_fs - 1,) + tail, BF16),
        ]
    return scratch


def scatter_sems(n_dp, n_fs, chunks):
    count = slot_count(n_dp, n_fs)
    return [
        pltpu.SemaphoreType.DMA((chunks, count)),
        pltpu.SemaphoreType.DMA((chunks, count)),
        pltpu.SemaphoreType.DMA((chunks, 2 ** len(plan_bits(n_dp)))),
    ]


def scatter_kernel(n_dp, n_fs, n_chunks, *refs):
    ins, outs = refs[:n_chunks], refs[n_chunks : 2 * n_chunks]
    scratch = refs[2 * n_chunks : 6 * n_chunks]
    dp, fs = lax.axis_index("dp"), lax.axis_index("fsdp")
    greet(dp, fs, n_dp, n_fs)

    def emit(chunk, total):
        outs[chunk][...] = total

    plans, sends = scatter_plan(dp, fs, n_dp, n_fs, ins, emit, scratch, *refs[6 * n_chunks :])
    for wave in waves(plans):
        for stage in wave:
            stage()
    for wait in sends:
        wait()


def scatter_all(n_dp, n_fs, arrays, collective_id):
    n = len(arrays)
    return pl.pallas_call(
        partial(scatter_kernel, n_dp, n_fs, n),
        out_shape=[jax.ShapeDtypeStruct(a.shape[1:], F32) for a in arrays],
        in_specs=[pl.BlockSpec(memory_space=pltpu.HBM)] * n,
        out_specs=[pl.BlockSpec(memory_space=pltpu.VMEM)] * n,
        scratch_shapes=scatter_scratch(n_dp, n_fs, [a.shape[1:] for a in arrays])
        + scatter_sems(n_dp, n_fs, n),
        compiler_params=pltpu.CompilerParams(
            collective_id=collective_id, has_side_effects=True, vmem_limit_bytes=48 << 20
        ),
        name="scatter_gradients",
    )(*arrays)


def swap_copy(axis, place, count, buffer, send_sem, recv_sem, step):
    return pltpu.make_async_remote_copy(
        src_ref=buffer.at[0],
        dst_ref=buffer.at[step],
        send_sem=send_sem.at[step],
        recv_sem=recv_sem.at[step],
        device_id={axis: lax.rem(place + step, count)},
        device_id_type=MESH,
    )


def swap_start(axis, place, count, *rest):
    for step in range(1, count):
        swap_copy(axis, place, count, *rest, step).start()


def swap_wait(axis, place, count, *rest):
    for step in range(1, count):
        swap_copy(axis, place, count, *rest, step).wait_recv()
    for step in range(1, count):
        swap_copy(axis, place, count, *rest, step).wait_send()


def swap_rows(*args):
    swap_start(*args)
    swap_wait(*args)


def sum_over(x, dp, fs, n_dp, n_fs, octet, line, send_sem, recv_sem, between=None):
    first = ("dp", dp, n_dp, octet, send_sem.at[0], recv_sem.at[0])
    octet[0] = x
    swap_start(*first)
    if between is not None:
        between()
    swap_wait(*first)
    total = octet[0]
    for step in range(1, n_dp):
        total = total + octet[step]
    line[0] = total
    swap_rows("fsdp", fs, n_fs, line, send_sem.at[1], recv_sem.at[1])
    total = line[0]
    for step in range(1, n_fs):
        total = total + line[step]
    return total


def pooled(buffer, count, weight):
    means = [buffer[k, 0:1, :] for k in range(count)]
    center = sum(means[1:], means[0]) * (1.0 / count)
    spread = buffer[0, 1:2, :]
    for k in range(1, count):
        spread = spread + buffer[k, 1:2, :]
    off = (means[0] - center) * (means[0] - center)
    for mean in means[1:]:
        off = off + (mean - center) * (mean - center)
    return center, spread + weight * off


def pool_over(center, spread, frames, dp, fs, n_dp, n_fs, octet, line, send_sem, recv_sem):
    octet[0] = jnp.zeros(octet.shape[1:], F32)
    line[0] = jnp.zeros(line.shape[1:], F32)
    octet[0, 0:1, :] = center
    octet[0, 1:2, :] = spread
    swap_rows("dp", dp, n_dp, octet, send_sem.at[0], recv_sem.at[0])
    center, spread = pooled(octet, n_dp, float(frames))
    line[0, 0:1, :] = center
    line[0, 1:2, :] = spread
    swap_rows("fsdp", fs, n_fs, line, send_sem.at[1], recv_sem.at[1])
    return pooled(line, n_fs, float(frames * n_dp))


def swap_scratch(n_dp, n_fs, channels):
    return [
        pltpu.VMEM((n_dp, 8, channels), F32),
        pltpu.VMEM((n_fs, 8, channels), F32),
        pltpu.SemaphoreType.DMA((2, max(n_dp, n_fs))),
        pltpu.SemaphoreType.DMA((2, max(n_dp, n_fs))),
    ]


def pool_kernel(n_dp, n_fs, frames, x_ref, out_ref, octet, line, send_sem, recv_sem):
    dp, fs = lax.axis_index("dp"), lax.axis_index("fsdp")
    greet(dp, fs, n_dp, n_fs)
    octet[0] = x_ref[...]
    center, spread = pool_over(
        x_ref[0:1, :], x_ref[1:2, :], frames, dp, fs, n_dp, n_fs, octet, line, send_sem, recv_sem
    )
    out_ref[...] = x_ref[...]
    out_ref[0:1, :] = center
    out_ref[1:2, :] = spread


def total_kernel(n_dp, n_fs, frames, x_ref, out_ref, octet, line, send_sem, recv_sem):
    dp, fs = lax.axis_index("dp"), lax.axis_index("fsdp")
    greet(dp, fs, n_dp, n_fs)
    out_ref[...] = sum_over(x_ref[...], dp, fs, n_dp, n_fs, octet, line, send_sem, recv_sem)


def exchange(n_dp, n_fs, x, frames, collective_id, kernel):
    return pl.pallas_call(
        partial(kernel, n_dp, n_fs, frames),
        out_shape=jax.ShapeDtypeStruct(x.shape, F32),
        in_specs=[pl.BlockSpec(memory_space=pltpu.VMEM)],
        out_specs=pl.BlockSpec(memory_space=pltpu.VMEM),
        scratch_shapes=swap_scratch(n_dp, n_fs, x.shape[1]),
        compiler_params=pltpu.CompilerParams(collective_id=collective_id, has_side_effects=True),
        name="exchange_rows",
    )(x)


class Place:
    def __init__(self, dp, fs, n_dp, n_fs):
        self.dp, self.fs, self.n_dp, self.n_fs = dp, fs, n_dp, n_fs
        self.count = (n_dp - 1).bit_length()
        self.bits = [lax.rem(lax.div(dp, 2**k), 2) for k in range(self.count)]
        self.half = n_fs // 2

    def peer(self, bit):
        return (flip(self.dp, 2**bit), self.fs)

    def view(self, ref, free=(), flipped=(), z=None, skip=()):
        index = []
        for bit in reversed(range(self.count)):
            if bit in skip:
                continue
            if bit in free:
                index.append(slice(None))
            else:
                index.append(1 - self.bits[bit] if bit in flipped else self.bits[bit])
        if z is not None:
            index.append(z)
        return ref.at[tuple(index)] if index else ref

    def part(self, which):
        return pl.ds(which * self.half, self.half)


def block_layout(n_dp, n_fs):
    return (2,) * ((n_dp - 1).bit_length()) + (n_fs,)


def hop_orders(place):
    bits = tuple(range(1, place.count))
    return (bits, bits[::-1])


def copy_count(n_dp, n_fs):
    return n_fs - 1 + 2 * ((n_dp - 1).bit_length() - 1) + 1


def block_gather(place, sources, outs, send_sem, recv_sem, local_sem):
    n_fs, fs = place.n_fs, place.fs
    sends = []

    def stages(chunk):
        src, out = sources[chunk], outs[chunk]

        def remote(slot, view_from, view_to, device):
            return pltpu.make_async_remote_copy(
                src_ref=view_from,
                dst_ref=view_to,
                send_sem=send_sem.at[chunk, slot],
                recv_sem=recv_sem.at[chunk, slot],
                device_id=device,
                device_id_type=MESH,
            )

        def launch(make):
            make().start()
            sends.append(lambda: make().wait_send())

        def own_copy():
            return pltpu.make_async_copy(src, place.view(out, z=fs), local_sem.at[chunk])

        def along(step):
            to = lax.rem(fs + step, n_fs)
            return remote(step - 1, src, place.view(out, z=fs), (place.dp, to))

        def start():
            own_copy().start()
            for step in range(1, n_fs):
                launch(lambda step=step: along(step))

        def wait_along():
            own_copy().wait()
            for step in range(1, n_fs):
                origin = lax.rem(fs + n_fs - step, n_fs)
                remote(
                    step - 1, src, place.view(out, z=origin), (place.dp, origin)
                ).wait_recv()

        steps, before = [start], wait_along
        slot = n_fs - 1
        orders = hop_orders(place)
        for depth in range(place.count - 1):
            plan = [(slot + part, part, order[depth], order[:depth]) for part, order in enumerate(orders)]
            slot += 2

            def hop(slot, part, bit, free, arrived):
                view = place.view(out, free, (bit,) if arrived else (), place.part(part))
                return remote(slot, view, view, place.peer(bit))

            def go(plan=plan, before=before, hop=hop):
                before()
                for item in plan:
                    launch(lambda item=item: hop(*item, False))

            def arrive(plan=plan, hop=hop):
                for item in plan:
                    hop(*item, True).wait_recv()

            steps.append(go)
            before = arrive

        def across(arrived, slot=slot):
            free = tuple(range(1, place.count))
            view = place.view(out, free, (0,) if arrived else ())
            return remote(slot, view, view, place.peer(0))

        def cross(before=before):
            before()
            launch(lambda: across(False))

        return steps + [cross, lambda: across(True).wait_recv()]

    return [stages(chunk) for chunk in range(len(outs))], sends


def block_scatter(place, sources, emit, scratch, send_sem, recv_sem, local_sem):
    n_fs, fs = place.n_fs, place.fs
    sends = []
    per = 3 + place.count - 1

    def add_into(kept, other):
        shape = kept.shape[:-3]
        for index in itertools.product(*[range(n) for n in shape]):
            kept[index] = (kept[index].astype(F32) + other[index].astype(F32)).astype(BF16)

    def stages(chunk):
        src = sources[chunk]
        own, cross_in, last, *later = scratch[per * chunk : per * chunk + per]

        def remote(slot, view_from, view_to, device):
            return pltpu.make_async_remote_copy(
                src_ref=view_from,
                dst_ref=view_to,
                send_sem=send_sem.at[chunk, slot],
                recv_sem=recv_sem.at[chunk, slot],
                device_id=device,
                device_id_type=MESH,
            )

        def launch(make):
            make().start()
            sends.append(lambda: make().wait_send())

        every = tuple(range(1, place.count))

        def load():
            return pltpu.make_async_copy(place.view(src, every), own, local_sem.at[chunk])

        def across():
            return remote(0, place.view(src, every, (0,)), cross_in, place.peer(0))

        def start():
            launch(across)
            load().start()

        def fold_cross():
            load().wait()
            across().wait_recv()
            add_into(own, cross_in)

        steps, before = [start], fold_cross
        slot = 1
        orders = [order[::-1] for order in hop_orders(place)]
        for depth in range(place.count - 1):
            plan = []
            for part, order in enumerate(orders):
                free = tuple(order[depth + 1 :])
                plan.append((slot + part, part, order[depth], free, later[depth]))
            slot += 2

            def hop(slot, part, bit, free, buffer):
                view = place.view(own, free, (bit,), place.part(part), skip=(0,))
                return remote(slot, view, buffer.at[part], place.peer(bit))

            def go(plan=plan, before=before, hop=hop):
                before()
                for item in plan:
                    launch(lambda item=item: hop(*item))

            def fold(plan=plan, hop=hop):
                for item in plan:
                    hop(*item).wait_recv()
                    _, part, _, free, buffer = item
                    kept = place.view(own, free, (), place.part(part), skip=(0,))
                    add_into(kept, buffer.at[part])

            steps.append(go)
            before = fold

        def along(step, slot=slot):
            to = lax.rem(fs + step, n_fs)
            view = place.view(own, z=to, skip=(0,))
            return remote(slot + step - 1, view, last.at[step - 1], (place.dp, to))

        def spread(before=before):
            before()
            for step in range(1, n_fs):
                launch(lambda step=step: along(step))

        def finish():
            total = place.view(own, z=fs, skip=(0,))[...].astype(F32)
            for step in range(1, n_fs):
                along(step).wait_recv()
                total = total + last[step - 1].astype(F32)
            emit(chunk, total)

        return steps + [spread, finish]

    return [stages(chunk) for chunk in range(len(sources))], sends


def block_scratch(n_dp, n_fs, blocks, tail):
    hops = (n_dp - 1).bit_length() - 1
    out = []
    for count in blocks:
        entry = (count,) + tail
        zone = (2,) * hops + (n_fs,) + entry
        out += [pltpu.VMEM(zone, BF16), pltpu.VMEM(zone, BF16), pltpu.VMEM((n_fs - 1,) + entry, BF16)]
        for depth in range(hops):
            out.append(pltpu.VMEM((2,) + (2,) * (hops - 1 - depth) + (n_fs // 2,) + entry, BF16))
    return out


def block_sems(n_dp, n_fs, chunks):
    count = copy_count(n_dp, n_fs)
    return [
        pltpu.SemaphoreType.DMA((chunks, count)),
        pltpu.SemaphoreType.DMA((chunks, count)),
        pltpu.SemaphoreType.DMA((chunks,)),
    ]


TILE = 512
STATES = 32
TAPS = 15
REACH = 8
EPSILON = 1e-05
CHUNK = 256
ROWS = 128
SPAN = 32
VMEM_LIMIT = 60 << 20
TAP_ROW = 24
RATE = 40
MAP_IN = 72
MAP_OUT = 104
TABLE = 136


def sigmoid(v):
    return 0.5 * jnp.tanh(0.5 * v) + 0.5


def dot_nn(a, b):
    return jnp.dot(a, b, preferred_element_type=F32)


def dot_nt(a, b):
    return lax.dot_general(a, b, (((1,), (1,)), ((), ())), preferred_element_type=F32)


def dot_tn(a, b):
    return lax.dot_general(a, b, (((0,), (0,)), ((), ())), preferred_element_type=F32)


def norm_parts(v):
    centered = v - jnp.mean(v, axis=-1, keepdims=True)
    inv = lax.rsqrt(jnp.mean(centered * centered, axis=-1, keepdims=True) + EPSILON)
    return centered * inv, inv


def norm_back(grad, e, inv, gain):
    d = grad * gain
    return (
        d - jnp.mean(d, axis=-1, keepdims=True) - e * jnp.mean(d * e, axis=-1, keepdims=True)
    ) * inv


def fold8(v):
    return jnp.sum(v.reshape((v.shape[0] // 8, 8, v.shape[1])), axis=0)


def by_rows(body, rows=TILE, step=ROWS):
    def run(at, _):
        body(pl.ds(pl.multiple_of(at * step, step), step))
        return 0

    lax.fori_loop(0, rows // step, run, 0)


def columns(at, width=CHUNK):
    return pl.ds(pl.multiple_of(at * width, width), width)


def merge_rows(parts, low_half):
    for distance in (1, 2, 4):
        low = low_half[distance]
        parts = [
            jnp.where(low, a, b) + pltpu.roll(jnp.where(low, b, a), distance, 0)
            for a, b in zip(parts[0::2], parts[1::2])
        ]
    return parts[0]


def half_masks(width):
    row = lax.broadcasted_iota(jnp.int32, (8, width), 0)
    return {d: (row // d) % 2 == 0 for d in (4, 2, 1)}


def fold_states(v):
    return jnp.sum(v.reshape((STATES // 8, 8, v.shape[1])), axis=0)


def fill_halo(padded, flags, tiles):
    pitch = TILE + 2 * REACH
    for at in range(tiles):
        base = at * pitch
        if at == 0:
            padded[:, base : base + REACH, :] = jnp.zeros_like(padded[:, base : base + REACH, :])
        if at == tiles - 1:
            end = base + REACH + TILE
            padded[:, end : end + REACH, :] = jnp.zeros_like(padded[:, end : end + REACH, :])
        else:
            keep = flags[at + 1]
            end = base + REACH + TILE
            padded[:, end : end + REACH, :] = (
                padded[:, base + pitch + REACH : base + pitch + 2 * REACH, :] * keep
            )
            padded[:, base + pitch : base + pitch + REACH, :] = (
                padded[:, end - REACH : end, :] * keep
            )


def taps_over(padded, table_ref, store, tiles, reverse, block=64):
    pitch = TILE + 2 * REACH
    per = TILE // block
    lanes = padded.shape[0]
    for lane in range(lanes):
        weights = [
            jnp.broadcast_to(
                table_ref[TAP_ROW + k : TAP_ROW + k + 1, lane * 128 : lane * 128 + 128], (block, 128)
            )
            for k in range(TAPS)
        ]

        def run(at, _):
            tile, inner = at // per, at % per
            base = tile * pitch + inner * block
            total = jnp.zeros((block, 128), F32)
            for k in range(TAPS):
                shift = REACH + (TAPS // 2 - k if reverse else k - TAPS // 2)
                total = total + weights[k] * padded[lane, pl.ds(base + shift, block), :]
            store(lane, tile * TILE + inner * block, base, total)
            return 0

        lax.fori_loop(0, tiles * per, run, 0)


def small_exp(v):
    return 1.0 + v * (1.0 + v * (0.5 + v * (1.0 / 6 + v * (1.0 / 24 + v * (1.0 / 120)))))


def small_expm1_over(v):
    return 1.0 + v * (
        0.5 + v * (1.0 / 6 + v * (1.0 / 24 + v * (1.0 / 120 + v * (1.0 / 720 + v * (1.0 / 5040)))))
    )


def state_terms(table_ref):
    log_decay = -jnp.exp(table_ref[RATE : RATE + STATES, :])
    root = jnp.sqrt(-2.0 * log_decay * small_expm1_over(2.0 * log_decay))
    maps_in = table_ref[MAP_IN : MAP_IN + STATES, :]
    maps_out = table_ref[MAP_OUT : MAP_OUT + STATES, :]
    return log_decay, small_exp(log_decay), root, maps_in, maps_out


def ref_rows(ref):
    return ref.reshape((ref.shape[0] * ref.shape[1], ref.shape[2]))


PIECE = 16
WIDTH = 512


def cols_of(ref, first, at):
    per = WIDTH // CHUNK
    part = ref[:, first + lax.div(at, per), :, columns(lax.rem(at, per))]
    return part.reshape((ref.shape[0] * PIECE, CHUNK))


def rows_of(ref, first, at):
    groups = CHUNK // (4 * PIECE)
    part = ref[pl.ds(at * groups, groups), first : first + 4]
    return part.reshape((CHUNK, WIDTH))


def square_of(ref, at):
    return ref[:, at].reshape((ref.shape[0] * PIECE, WIDTH))


def store_wide(out, first, acc):
    def run(group, _):
        rows = pl.ds(pl.multiple_of(group * PIECE, PIECE), PIECE)
        for k in range(acc.shape[1] // WIDTH):
            out[group, first + k] = acc[rows, k * WIDTH : k * WIDTH + WIDTH].astype(BF16)
        return 0

    lax.fori_loop(0, acc.shape[0] // PIECE, run, 0)


def store_tall(out, first, acc):
    def run(group, _):
        rows = pl.ds(pl.multiple_of(group * 4 * PIECE, 4 * PIECE), 4 * PIECE)
        out[group, first : first + 4] = acc[rows, :].astype(BF16).reshape((4, PIECE, WIDTH))
        return 0

    lax.fori_loop(0, acc.shape[0] // (4 * PIECE), run, 0)


def flat_groups(ref):
    count = 1
    for n in ref.shape[:-3]:
        count *= n
    return ref.reshape((count,) + ref.shape[-3:])


def carries(offsets_ref, counts_ref, tiles):
    out = []
    for tile in range(tiles):
        begins = jnp.int32(0)
        for slot in range(offsets_ref.shape[1]):
            here = (offsets_ref[0, slot] == tile * TILE) & (slot < counts_ref[0])
            begins = jnp.maximum(begins, here.astype(jnp.int32))
        out.append((1 - begins).astype(F32))
    return out


def pick(values, at):
    total = values[0] * (at == 0).astype(F32)
    for k in range(1, len(values)):
        total = total + values[k] * (at == k).astype(F32)
    return total


def pack_small(out, scr, place, bias_ref, gains, shifts, conv_bias, taps, rate, maps):
    own = gains.shape[1]
    scr[...] = jnp.zeros_like(scr)
    scr[0:6, :own] = gains[...].astype(F32)
    scr[6:18, :own] = shifts[...].astype(F32)
    scr[18:19, :own] = conv_bias[...].astype(F32)
    scr[TAP_ROW : TAP_ROW + TAPS, :own] = taps[...].astype(F32)
    out[:, :CHUNK] = scr[...].T[:own, :].astype(BF16)
    out[:, RATE:MAP_IN] = rate[...]
    out[:, MAP_IN:MAP_OUT] = maps[0]
    out[:, MAP_OUT:TABLE] = maps[1]
    count = bias_ref.shape[1]
    row = lax.div(place * count, CHUNK)
    inner = place * count - row * CHUNK
    at_row = lax.broadcasted_iota(jnp.int32, (PIECE, CHUNK), 0)
    wide = jnp.zeros((PIECE, CHUNK), F32)
    for layer in range(2):
        line = jnp.broadcast_to(bias_ref[layer : layer + 1, :].astype(F32), (8, count))
        line = jnp.concatenate([line, jnp.zeros((8, CHUNK - count), F32)], axis=1)
        line = pltpu.roll(line, inner, 1)
        wide = wide + jnp.where(at_row == 8 * layer + row, jnp.broadcast_to(line[0:1], wide.shape), 0.0)
    out[:, CHUNK:] = wide.astype(BF16)


def front_kernel(mesh_size, *refs):
    fused = mesh_size is not None
    refs = list(refs)
    take = lambda count: [refs.pop(0) for _ in range(count)]
    offsets_ref, counts_ref, x_ref = take(3)
    if fused:
        n_dp, n_fs = mesh_size
        small_in = take(7)
        up_s, down_s, mixin_s, mixout_s, convin_s, convout_s = take(6)
    else:
        first_v, second_v, third_v, table_in, bias_in = take(5)
    (
        h_out,
        x1_out,
        u_out,
        v_out,
        y_out,
        gated_out,
        x2_out,
        p_out,
        hold_out,
        w_out,
        stat_out,
        table_ref,
        bias_ref,
        decay_ref,
        map_ref,
    ) = take(15)
    gathered = take(4) if fused else []
    x1_scr, low_all, low_scr, sum_scr, state_scr, padded = take(6)
    step = pl.program_id(0)
    channels = x_ref.shape[1]
    frames = w_out.shape[0]
    tiles = frames // TILE
    lanes = channels // 128
    gain = lambda k: table_ref[k : k + 1, :]
    shift = lambda k: table_ref[6 + k : 7 + k, :]
    here = lambda rows, tile: pl.ds(pl.multiple_of(tile * TILE + rows.start, ROWS), ROWS)
    flags = carries(offsets_ref, counts_ref, tiles)
    if fused:
        first_c, second_c, third_c = take(3)
        sources = take(4)
        turn_scr = refs.pop(0)
        sems = take(3)
        load_sem = refs.pop(0)
        swap = take(4)
        dp, fs = lax.axis_index("dp"), lax.axis_index("fsdp")
        place = Place(dp, fs, n_dp, n_fs)
        landing = [first_c, second_c, third_c, gathered[3]]
        plans, sends = block_gather(place, sources, landing, *sems)
        first_v, second_v, third_v = [flat_groups(r) for r in landing[:3]]

        def keep_copy(chunk):
            return pltpu.make_async_copy(landing[chunk], gathered[chunk], load_sem.at[chunk])

        def run(*stages):
            for chunk, stage in stages:
                plans[chunk][stage]()

        @pl.when(step == 0)
        def _():
            pack_small(sources[0].at[0], turn_scr, dp * n_fs + fs, *small_in)
            for k in range(4):
                cols = slice(k * WIDTH, k * WIDTH + WIDTH)
                sources[0][1 + k] = up_s[0, :, cols]
                sources[3][1 + k] = up_s[1, :, cols]
                rows = slice(k * PIECE, k * PIECE + PIECE)
                sources[1][k] = down_s[0, rows, :]
                sources[3][5 + k] = down_s[1, rows, :]
            for k in range(2):
                cols = slice(k * WIDTH, k * WIDTH + WIDTH)
                sources[2][k] = mixin_s[:, cols]
                sources[2][3 + k] = convin_s[:, cols]
            sources[2][2] = mixout_s[...]
            sources[3][0] = convout_s[...]
            greet(dp, fs, n_dp, n_fs)
            run((0, 0), (1, 0), (0, 1), (1, 1), (2, 0), (0, 2), (1, 2), (0, 3), (2, 1), (1, 3), (0, 4))
            table_ref[...] = first_v[:, 0, :, :CHUNK].reshape((channels, CHUNK)).astype(F32).T[:TABLE, :]
            total = first_v[0, 0, :, CHUNK:].astype(F32)
            for k in range(1, n_dp * n_fs):
                total = total + first_v[k, 0, :, CHUNK:].astype(F32)
            bias_ref[...] = total
            run((1, 4))

        rest = {1: [(2, 2), (3, 0)], 2: [(2, 3)], tiles: [(2, 4), (3, 1)]}
        rest.update({tiles + 1: [(3, 2)], tiles + 2: [(3, 3)], 2 * tiles: [(3, 4)]})
        for at, stages in rest.items():

            @pl.when(step == at)
            def _(at=at, stages=stages):
                run(*stages)
                if at == tiles:
                    for chunk in range(3):
                        keep_copy(chunk).start()
                if at == 2 * tiles:
                    for chunk in range(3):
                        keep_copy(chunk).wait()
                    for wait in sends:
                        wait()

    else:

        @pl.when(step == 0)
        def _():
            table_ref[...] = table_in[...]
            bias_ref[...] = bias_in[...]

    @pl.when(step == 0)
    def _():
        _, decay, root, maps_in, maps_out = state_terms(table_ref)
        decay_ref[...] = decay
        map_ref[...] = maps_in * root * maps_out
        state_scr[...] = jnp.zeros_like(state_scr)

    @pl.when(step < tiles)
    def _():
        def first(rows):
            e, _ = norm_parts(x_ref[rows, :].astype(F32))
            low_scr[rows, :] = (e * gain(0) + shift(0)).astype(BF16)
            sum_scr[rows, :] = jnp.zeros((ROWS, channels), F32)

        by_rows(first)

        def hidden(c, _):
            cols = columns(c)
            h = dot_nn(low_scr[...], cols_of(first_v, 1, c)) + bias_ref[pl.ds(c, 1), :]
            h_out[:, cols] = h.astype(BF16)
            active = (h * sigmoid(h)).astype(BF16)
            sum_scr[...] += dot_nn(active, rows_of(second_v, 0, c))
            return 0

        lax.fori_loop(0, h_out.shape[1] // CHUNK, hidden, 0)

        def second(rows):
            x1 = x_ref[rows, :].astype(F32) + 0.5 * (sum_scr[rows, :] + shift(6))
            x1_out[rows, :] = x1
            x1_scr[here(rows, step), :] = x1
            e, _ = norm_parts(x1)
            low_all[here(rows, step), :] = (e * gain(1) + shift(1)).astype(BF16)

        by_rows(second)

    @pl.when((step >= tiles) & (step < 2 * tiles))
    def _():
        at = step - tiles
        whole_tile = pl.ds(pl.multiple_of(at * TILE, TILE), TILE)

        def project(c, _):
            cols = columns(c)
            low = low_all[whole_tile, :]
            u_out[:, cols] = dot_nn(low, cols_of(third_v, 0, c))
            v_out[:, cols] = dot_nn(low, cols_of(third_v, 1, c)).astype(BF16)
            return 0

        lax.fori_loop(0, channels // CHUNK, project, 0)
        low_half = half_masks(128)
        state_scr[...] = state_scr[...] * pick(flags, at)

        def scan_span(span, _):
            hold_out[span] = state_scr[...]

            def scan(block, _):
                start = pl.multiple_of(span * SPAN + block * 8, 8)
                for lane in range(lanes):
                    cols = slice(lane * 128, lane * 128 + 128)
                    state = state_scr[:, cols]
                    decay = decay_ref[:, cols]
                    maps = map_ref[:, cols]
                    drive = u_out[pl.ds(start, 8), cols]
                    parts = []
                    for j in range(8):
                        state = decay * state + jnp.broadcast_to(drive[j : j + 1, :], (STATES, 128))
                        parts.append(fold_states(maps * state))
                    state_scr[:, cols] = state
                    sum_scr[pl.ds(start, 8), cols] = merge_rows(parts, low_half)
                return 0

            lax.fori_loop(0, SPAN // 8, scan, 0)
            return 0

        lax.fori_loop(0, TILE // SPAN, scan_span, 0)

        def gate(rows):
            y = sum_scr[rows, :] + shift(11) * u_out[rows, :]
            v = v_out[rows, :].astype(F32)
            y_out[rows, :] = y.astype(BF16)
            gated_out[rows, :] = (y * (v * sigmoid(v))).astype(BF16)

        by_rows(gate)
        sum_scr[...] = dot_nn(gated_out[...], square_of(third_v, 2))

        def third(rows):
            x2 = x1_scr[here(rows, at), :] + (sum_scr[rows, :] + shift(8))
            x2_out[rows, :] = x2
            e, _ = norm_parts(x2)
            low_scr[rows, :] = (e * gain(2) + shift(2)).astype(BF16)

        by_rows(third)
        pitch = TILE + 2 * REACH

        def widen(c, _):
            cols = columns(c)
            right = columns(c + channels // CHUNK)
            left_part = dot_nn(low_scr[...], cols_of(third_v, 3, c)) + table_ref[15:16, cols]
            right_part = dot_nn(low_scr[...], cols_of(third_v, 4, c)) + table_ref[16:17, cols]
            p_out[:, cols] = left_part.astype(BF16)
            p_out[:, right] = right_part.astype(BF16)
            g = left_part * sigmoid(right_part)
            place = pl.ds(pl.multiple_of(at * pitch + REACH, 8), TILE)
            for k in range(CHUNK // 128):
                padded[c * (CHUNK // 128) + k, place, :] = g[:, k * 128 : k * 128 + 128]
            return 0

        lax.fori_loop(0, channels // CHUNK, widen, 0)

    @pl.when(step == 2 * tiles)
    def _():
        fill_halo(padded, flags, tiles)

        def store(lane, row, base, total):
            w_out[pl.ds(pl.multiple_of(row, 64), 64), lane * 128 : lane * 128 + 128] = total

        taps_over(padded, table_ref, store, tiles, False)
        stat_out[...] = jnp.zeros_like(stat_out)

        def total(at, _):
            rows = pl.ds(pl.multiple_of(at * ROWS, ROWS), ROWS)
            stat_out[...] += fold8(w_out[rows, :])
            return 0

        lax.fori_loop(0, frames // ROWS, total, 0)
        center = jnp.sum(stat_out[...], axis=0, keepdims=True) * (1.0 / frames)
        stat_out[...] = jnp.zeros_like(stat_out)

        def spread(at, _):
            rows = pl.ds(pl.multiple_of(at * ROWS, ROWS), ROWS)
            off = w_out[rows, :] - center
            stat_out[...] += fold8(off * off)
            return 0

        lax.fori_loop(0, frames // ROWS, spread, 0)
        around = jnp.sum(stat_out[...], axis=0, keepdims=True)
        if fused:
            center, around = pool_over(center, around, frames, dp, fs, n_dp, n_fs, *swap)
            around = lax.rsqrt(around * (1.0 / (frames * n_dp * n_fs)) + EPSILON)
        stat_out[...] = jnp.zeros_like(stat_out)
        stat_out[0:1, :] = center
        stat_out[1:2, :] = around


def whole(shape):
    zeros = (0,) * len(shape)
    return pl.BlockSpec(shape, lambda *_: zeros, pipeline_mode=pl.Buffered(1))


def params(collective_id=None):
    if collective_id is None:
        return pltpu.CompilerParams(
            dimension_semantics=("arbitrary",), vmem_limit_bytes=VMEM_LIMIT
        )
    return pltpu.CompilerParams(
        dimension_semantics=("arbitrary",),
        vmem_limit_bytes=VMEM_LIMIT,
        collective_id=collective_id,
        has_side_effects=True,
    )


SMEM_SPEC = pl.BlockSpec(memory_space=pltpu.SMEM)
HBM_SPEC = pl.BlockSpec(memory_space=pltpu.HBM)


def front(mesh_size, offsets, counts, x, small, weights, hidden, collective_id=None):
    fused = mesh_size is not None
    frames, channels = x.shape
    tiles = frames // TILE
    early = lambda width: pl.BlockSpec((TILE, width), lambda i: (jnp.minimum(i, tiles - 1), 0))
    place = lambda i: jnp.clip(i - tiles, 0, tiles - 1)
    late = lambda width: pl.BlockSpec((TILE, width), lambda i: (place(i), 0))
    shape = lambda width, kind: jax.ShapeDtypeStruct((frames, width), kind)
    spans = TILE // SPAN
    state = jax.ShapeDtypeStruct((STATES, channels), F32)
    out_shape = [
        shape(hidden, BF16),
        shape(channels, F32),
        shape(channels, F32),
        shape(channels, BF16),
        shape(channels, BF16),
        shape(channels, BF16),
        shape(channels, F32),
        shape(2 * channels, BF16),
        jax.ShapeDtypeStruct((frames // SPAN, STATES, channels), F32),
        shape(channels, F32),
        jax.ShapeDtypeStruct((8, channels), F32),
        jax.ShapeDtypeStruct((TABLE, channels), F32),
        jax.ShapeDtypeStruct((16, CHUNK), F32),
        state,
        state,
    ]
    out_specs = [early(hidden), early(channels)]
    out_specs += [late(channels)] * 5
    out_specs += [
        late(2 * channels),
        pl.BlockSpec((spans, STATES, channels), lambda i: (place(i), 0, 0)),
    ]
    out_specs += [whole(s.shape) for s in out_shape[9:]]
    scratch = [
        pltpu.VMEM((frames, channels), F32),
        pltpu.VMEM((frames, channels), BF16),
        pltpu.VMEM((TILE, channels), BF16),
        pltpu.VMEM((TILE, channels), F32),
        pltpu.VMEM((STATES, channels), F32),
        pltpu.VMEM((channels // 128, tiles * (TILE + 2 * REACH), 128), F32),
    ]
    operands = (weights if not fused else small + weights) + (small if not fused else [])
    if fused:
        layout = block_layout(*mesh_size)
        blocks = (5, 4, 5, 9)
        chunks = [jax.ShapeDtypeStruct(layout + (k, PIECE, WIDTH), BF16) for k in blocks]
        out_shape += chunks
        out_specs += [HBM_SPEC] * len(chunks)
        scratch += [pltpu.VMEM(c.shape, BF16) for c in chunks[:3]]
        scratch += [pltpu.VMEM((k, PIECE, WIDTH), BF16) for k in blocks]
        scratch += [pltpu.VMEM((CHUNK, 128), F32)]
        scratch += block_sems(*mesh_size, len(chunks)) + [pltpu.SemaphoreType.DMA((3,))]
        scratch += swap_scratch(*mesh_size, channels)
    return pl.pallas_call(
        partial(front_kernel, mesh_size),
        grid=(2 * tiles + 1,),
        in_specs=[SMEM_SPEC, SMEM_SPEC, early(channels)] + [whole(a.shape) for a in operands],
        out_specs=out_specs,
        out_shape=out_shape,
        scratch_shapes=scratch,
        compiler_params=params(collective_id),
        name="front",
    )(offsets, counts, x, *operands)


def middle_kernel(
    mesh_size,
    x2_ref,
    w_ref,
    cot_ref,
    blocks_ref,
    bias_ref,
    vec_ref,
    stat_ref,
    out_ref,
    gx3_ref,
    gnb_ref,
    gblocks_out,
    gbias_out,
    gvec_out,
    stat_out,
    up_acc,
    down_acc,
    convout_acc,
    bias_acc,
    vec_acc,
    h_scr,
    low_scr,
    turn_scr,
    act_scr,
    grad_scr,
    sum_scr,
    x3_scr,
    *swap,
):
    at = pl.program_id(0)
    tiles = pl.num_programs(0)
    channels = x2_ref.shape[1]
    if mesh_size is not None:
        n_dp, n_fs = mesh_size
        dp, fs = lax.axis_index("dp"), lax.axis_index("fsdp")

        @pl.when(at == 0)
        def _():
            greet(dp, fs, n_dp, n_fs)

    hidden = up_acc.shape[1]
    gain = lambda k: vec_ref[k : k + 1, :]
    shift = lambda k: vec_ref[6 + k : 7 + k, :]
    center, scale = stat_ref[0:1, :], stat_ref[1:2, :]

    @pl.when(at == 0)
    def _():
        for ref in (up_acc, down_acc, convout_acc, bias_acc, vec_acc):
            ref[...] = jnp.zeros_like(ref)

    def normed(rows):
        e = (w_ref[rows, :] - center) * scale
        return e, e * gain(5) + shift(5)

    def first(rows):
        _, nb = normed(rows)
        act_scr[rows, :] = (nb * sigmoid(nb)).astype(BF16)

    by_rows(first)
    sum_scr[...] = dot_nn(act_scr[...], square_of(blocks_ref, 0))

    def second(rows):
        x3 = x2_ref[rows, :] + (sum_scr[rows, :] + vec_ref[18:19, :])
        x3_scr[rows, :] = x3
        e, _ = norm_parts(x3)
        low_scr[rows, :] = (e * gain(3) + shift(3)).astype(BF16)
        sum_scr[rows, :] = jnp.zeros((ROWS, channels), F32)

    by_rows(second)

    def forward(c, _):
        cols = columns(c)
        h = dot_nn(low_scr[...], cols_of(blocks_ref, 1, c)) + bias_ref[pl.ds(8 + c, 1), :]
        h_scr[:, cols] = h
        active = (h * sigmoid(h)).astype(BF16)
        sum_scr[...] += dot_nn(active, rows_of(blocks_ref, 5, c))
        return 0

    lax.fori_loop(0, hidden // CHUNK, forward, 0)
    turn_scr[...] = low_scr[...].T

    def last(rows):
        x4 = x3_scr[rows, :] + 0.5 * (sum_scr[rows, :] + shift(7))
        e, inv = norm_parts(x4)
        out_ref[rows, :] = (e * gain(4) + shift(4)).astype(BF16)
        cot = cot_ref[rows, :].astype(F32)
        vec_acc[0] += fold8(cot * e)
        vec_acc[1] += fold8(cot)
        gx4 = norm_back(cot, e, inv, gain(4))
        gx3_ref[rows, :] = gx4
        low = (0.5 * gx4).astype(BF16)
        grad_scr[rows, :] = low
        vec_acc[2] += fold8(low.astype(F32))
        sum_scr[rows, :] = jnp.zeros((ROWS, channels), F32)

    by_rows(last)

    def backward(c, _):
        cols = columns(c)
        h = h_scr[:, cols]
        sig = sigmoid(h)
        active = h * sig
        gate = dot_nt(grad_scr[...], rows_of(blocks_ref, 5, c))
        grad_h = (gate * (sig * (1.0 + h - active))).astype(BF16)
        bias_acc[:, cols] += fold8(grad_h.astype(F32))
        down_acc[cols, :] += dot_tn(active.astype(BF16), grad_scr[...])
        up_acc[:, cols] += dot_nn(turn_scr[...], grad_h)
        sum_scr[...] += dot_nt(grad_h, cols_of(blocks_ref, 1, c))
        return 0

    lax.fori_loop(0, hidden // CHUNK, backward, 0)

    def fourth(rows):
        e, inv = norm_parts(x3_scr[rows, :])
        grad = sum_scr[rows, :]
        vec_acc[3] += fold8(grad * e)
        vec_acc[4] += fold8(grad)
        gx3 = gx3_ref[rows, :] + norm_back(grad, e, inv, gain(3))
        gx3_ref[rows, :] = gx3
        low = gx3.astype(BF16)
        grad_scr[rows, :] = low
        vec_acc[5] += fold8(low.astype(F32))

    by_rows(fourth)
    convout_acc[...] += dot_tn(act_scr[...], grad_scr[...])
    sum_scr[...] = dot_nt(grad_scr[...], square_of(blocks_ref, 0))

    def fifth(rows):
        e, nb = normed(rows)
        sig = sigmoid(nb)
        gnb = sum_scr[rows, :] * (sig * (1.0 + nb * (1.0 - sig)))
        gnb_ref[rows, :] = gnb
        vec_acc[6] += fold8(gnb * e)
        vec_acc[7] += fold8(gnb)

    by_rows(fifth)

    @pl.when(at == tiles - 1)
    def _():
        for k in range(8):
            gvec_out[k : k + 1, :] = jnp.sum(vec_acc[k], axis=0, keepdims=True)

        def convert():
            store_wide(gblocks_out, 0, convout_acc)
            store_wide(gblocks_out, 1, up_acc)
            store_tall(gblocks_out, 5, down_acc)
            gbias_out[...] = jnp.broadcast_to(
                jnp.sum(bias_acc[...], axis=0, keepdims=True), gbias_out.shape
            )

        stat_out[...] = stat_ref[...]
        if mesh_size is None:
            convert()
        else:
            total = sum_over(gvec_out[...], dp, fs, n_dp, n_fs, *swap, between=convert)
            share = gain(5) * (1.0 / (TILE * tiles * n_dp * n_fs))
            stat_out[2:3, :] = total[7:8, :] * share
            stat_out[3:4, :] = total[6:7, :] * share


def middle(mesh_size, x2, w, cot, blocks, bias, vec, stat, hidden, collective_id=None):
    frames, channels = x2.shape
    tiles = frames // TILE
    row = lambda width: pl.BlockSpec((TILE, width), lambda i: (i, 0))
    shapes = [
        jax.ShapeDtypeStruct((frames, channels), BF16),
        jax.ShapeDtypeStruct((frames, channels), F32),
        jax.ShapeDtypeStruct((frames, channels), F32),
        jax.ShapeDtypeStruct(blocks.shape, BF16),
        jax.ShapeDtypeStruct((8, hidden), F32),
        jax.ShapeDtypeStruct((8, channels), F32),
        jax.ShapeDtypeStruct((8, channels), F32),
    ]
    swap = [] if mesh_size is None else swap_scratch(*mesh_size, channels)
    return pl.pallas_call(
        partial(middle_kernel, mesh_size),
        grid=(tiles,),
        in_specs=[row(channels)] * 3
        + [whole(a.shape) for a in (blocks, bias, vec, stat)],
        out_specs=[row(channels)] * 3 + [whole(s.shape) for s in shapes[3:]],
        out_shape=shapes,
        scratch_shapes=[
            pltpu.VMEM((channels, hidden), F32),
            pltpu.VMEM((hidden, channels), F32),
            pltpu.VMEM((channels, channels), F32),
            pltpu.VMEM((8, hidden), F32),
            pltpu.VMEM((8, 8, channels), F32),
            pltpu.VMEM((TILE, hidden), F32),
            pltpu.VMEM((TILE, channels), BF16),
            pltpu.VMEM((channels, TILE), BF16),
            pltpu.VMEM((TILE, channels), BF16),
            pltpu.VMEM((TILE, channels), BF16),
            pltpu.VMEM((TILE, channels), F32),
            pltpu.VMEM((TILE, channels), F32),
        ]
        + swap,
        compiler_params=params(collective_id),
        name="middle",
    )(x2, w, cot, blocks, bias, vec, stat)


def back_kernel(mesh_size, *refs):
    fused = mesh_size is not None
    refs = list(refs)
    take = lambda count: [refs.pop(0) for _ in range(count)]
    (
        offsets_ref,
        counts_ref,
        w_ref,
        gnb_ref,
        p_all,
        x2_ref,
        gx3_ref,
        gated_ref,
        y_ref,
        v_ref,
        u_ref,
        x1_ref,
        hold_ref,
        blocks_ref,
        vec_ref,
        stat_ref,
        decay_ref,
        map_ref,
    ) = take(18)
    sources = take(1) if fused else []
    (
        gx1_ref,
        gblocks_out,
        gvec_out,
        gtaps_ref,
        gmap_out,
        gdecay_out,
    ) = take(6)
    reduced = take(1) if fused else []
    (
        convin_acc,
        mixout_acc,
        mixin_acc,
        vec_acc,
        map_acc,
        decay_acc,
        adj_scr,
        track,
        low_scr,
        wide_scr,
        sum_scr,
        gy_scr,
        padded,
        gpad,
    ) = take(14)
    step = pl.program_id(0)
    tiles = pl.num_programs(0) - 1
    at = tiles - jnp.maximum(step, 1)
    channels = x2_ref.shape[1]
    lanes = channels // 128
    pitch = TILE + 2 * REACH
    gain = lambda k: vec_ref[k : k + 1, :]
    shift = lambda k: vec_ref[6 + k : 7 + k, :]
    left, right = slice(0, channels), slice(channels, 2 * channels)
    flags = carries(offsets_ref, counts_ref, tiles)
    if fused:
        n_dp, n_fs = mesh_size
        place = Place(lax.axis_index("dp"), lax.axis_index("fsdp"), n_dp, n_fs)
        scratch = take(2 + place.count)

        def emit(chunk, total):
            reduced[chunk][...] = total

        plans, sends = block_scatter(place, sources, emit, scratch, *take(3))
        order = waves(plans)
        points = [(0, 0), (0, 2), (1, 0), (1, 3), (2, 0)]

    def progress(point):
        if not fused:
            return
        for wave, place in zip(order, points):
            if place[1] == point:

                @pl.when(step == place[0])
                def _(wave=wave):
                    for stage in wave:
                        stage()

    @pl.when(step == 0)
    def _():
        for ref in (convin_acc, mixout_acc, mixin_acc, vec_acc, map_acc, decay_acc, adj_scr):
            ref[...] = jnp.zeros_like(ref)
        if fused:
            greet(place.dp, place.fs, n_dp, n_fs)

    progress(0)

    @pl.when(step == 0)
    def _():
        center, scale = stat_ref[0:1, :], stat_ref[1:2, :]
        plain, cross = stat_ref[2:3, :], stat_ref[3:4, :]
        per = TILE // 64

        def fill(index, _):
            tile, inner = index // per, index % per
            rows = pl.ds(pl.multiple_of(index * 64, 64), 64)
            place = pl.ds(pl.multiple_of(tile * pitch + REACH + inner * 64, 8), 64)
            e = (w_ref[rows, :] - center) * scale
            d = gnb_ref[rows, :] * gain(5)
            gw = scale * (d - plain - e * cross)
            g = p_all[rows, left].astype(F32) * sigmoid(p_all[rows, right].astype(F32))
            for lane in range(lanes):
                cols = slice(lane * 128, lane * 128 + 128)
                padded[lane, place, :] = gw[:, cols]
                gpad[lane, place, :] = g[:, cols]
            return 0

        lax.fori_loop(0, tiles * per, fill, 0)
        fill_halo(padded, flags, tiles)
        fill_halo(gpad, flags, tiles)

    progress(1)

    @pl.when(step == 0)
    def _():
        block = 64
        per = TILE // block
        gtaps_ref[...] = jnp.zeros_like(gtaps_ref)
        for lane in range(lanes):

            def corr(index, sums, lane=lane):
                base = (index // per) * pitch + (index % per) * block
                here = padded[lane, pl.ds(pl.multiple_of(base + REACH, 8), block), :]
                return tuple(
                    s + fold8(here * gpad[lane, pl.ds(base + REACH + k - TAPS // 2, block), :])
                    for k, s in enumerate(sums)
                )

            sums = lax.fori_loop(0, tiles * per, corr, (jnp.zeros((8, 128), F32),) * TAPS)
            for k in range(TAPS):
                gtaps_ref[k : k + 1, lane * 128 : lane * 128 + 128] = jnp.sum(
                    sums[k], axis=0, keepdims=True
                )

        def store(lane, row, base, total):
            gpad[lane, pl.ds(pl.multiple_of(base + REACH, 8), 64), :] = total

        taps_over(padded, vec_ref, store, tiles, True)

    progress(2)

    def back_tile():
        def first(rows):
            place = pl.ds(pl.multiple_of(at * pitch + REACH + rows.start, 8), ROWS)
            here = pl.ds(pl.multiple_of(at * TILE + rows.start, ROWS), ROWS)
            grad = jnp.concatenate([gpad[lane, place, :] for lane in range(lanes)], axis=1)
            sig = sigmoid(p_all[here, right].astype(F32))
            gl = (grad * sig).astype(BF16)
            gr = (grad * p_all[here, left].astype(F32) * (sig * (1.0 - sig))).astype(BF16)
            wide_scr[rows, left] = gl
            wide_scr[rows, right] = gr
            vec_acc[0] += fold8(gl.astype(F32))
            vec_acc[1] += fold8(gr.astype(F32))
            e, _ = norm_parts(x2_ref[rows, :])
            low_scr[rows, :] = (e * gain(2) + shift(2)).astype(BF16)

        by_rows(first)
        turned = low_scr[...].T
        convin_acc[...] += dot_nn(turned, wide_scr[...])
        sum_scr[...] = dot_nt(wide_scr[:, left], square_of(blocks_ref, 3)) + dot_nt(
            wide_scr[:, right], square_of(blocks_ref, 4)
        )

        def second(rows):
            e, inv = norm_parts(x2_ref[rows, :])
            grad = sum_scr[rows, :]
            vec_acc[2] += fold8(grad * e)
            vec_acc[3] += fold8(grad)
            gx2 = gx3_ref[rows, :] + norm_back(grad, e, inv, gain(2))
            gx1_ref[rows, :] = gx2
            low = gx2.astype(BF16)
            low_scr[rows, :] = low
            vec_acc[4] += fold8(low.astype(F32))

        by_rows(second)
        progress(3)
        mixout_acc[...] += dot_tn(gated_ref[...], low_scr[...])
        sum_scr[...] = dot_nt(low_scr[...], square_of(blocks_ref, 2))

        def third(rows):
            grad = sum_scr[rows, :]
            v = v_ref[rows, :].astype(F32)
            sig = sigmoid(v)
            swish = v * sig
            gy = grad * swish
            gy_scr[rows, :] = gy
            wide_scr[rows, right] = (
                grad * y_ref[rows, :].astype(F32) * (sig * (1.0 + v - swish))
            ).astype(BF16)
            vec_acc[5] += fold8(gy * u_ref[rows, :])

        by_rows(third)
        progress(4)
        low_half = half_masks(128)
        later = jnp.minimum(at + 1, tiles - 1)
        adj_scr[...] = adj_scr[...] * pick(flags, later)

        def span_back(index, _):
            span = TILE // SPAN - 1 - index
            base = pl.multiple_of(span * SPAN, SPAN)
            for lane in range(lanes):
                cols = slice(lane * 128, lane * 128 + 128)
                decay = decay_ref[:, cols]

                def forward(block, state):
                    drive = u_ref[pl.ds(pl.multiple_of(base + block * 8, 8), 8), cols]
                    for j in range(8):
                        track[block * 8 + j, :, cols] = state
                        state = decay * state + jnp.broadcast_to(drive[j : j + 1, :], (STATES, 128))
                    return state

                lax.fori_loop(0, SPAN // 8, forward, hold_ref[span, :, cols])

            def backward(index, _):
                block = SPAN // 8 - 1 - index
                start = pl.multiple_of(base + block * 8, 8)
                for lane in range(lanes):
                    cols = slice(lane * 128, lane * 128 + 128)
                    decay = decay_ref[:, cols]
                    maps = map_ref[:, cols]
                    adj = adj_scr[:, cols]
                    drive = u_ref[pl.ds(start, 8), cols]
                    grad = gy_scr[pl.ds(start, 8), cols]
                    gmap = map_acc[:, cols]
                    gdecay = decay_acc[:, cols]
                    parts = [None] * 8
                    for j in range(7, -1, -1):
                        adj = decay * adj + jnp.broadcast_to(grad[j : j + 1, :], (STATES, 128))
                        parts[j] = fold_states(maps * adj)
                        gmap = gmap + adj * jnp.broadcast_to(drive[j : j + 1, :], (STATES, 128))
                        gdecay = gdecay + adj * track[block * 8 + j, :, cols]
                    adj_scr[:, cols] = adj
                    map_acc[:, cols] = gmap
                    decay_acc[:, cols] = gdecay
                    sum_scr[pl.ds(start, 8), cols] = merge_rows(parts, low_half)
                return 0

            lax.fori_loop(0, SPAN // 8, backward, 0)
            return 0

        lax.fori_loop(0, TILE // SPAN, span_back, 0)

        def fourth(rows):
            gu = sum_scr[rows, :] + shift(11) * gy_scr[rows, :]
            wide_scr[rows, left] = gu.astype(BF16)
            e, _ = norm_parts(x1_ref[rows, :])
            low_scr[rows, :] = (e * gain(1) + shift(1)).astype(BF16)

        by_rows(fourth)
        turned = low_scr[...].T
        mixin_acc[...] += dot_nn(turned, wide_scr[...])
        sum_scr[...] = dot_nt(wide_scr[:, left], square_of(blocks_ref, 0)) + dot_nt(
            wide_scr[:, right], square_of(blocks_ref, 1)
        )

        def fifth(rows):
            e, inv = norm_parts(x1_ref[rows, :])
            grad = sum_scr[rows, :]
            vec_acc[6] += fold8(grad * e)
            vec_acc[7] += fold8(grad)
            gx1_ref[rows, :] = gx1_ref[rows, :] + norm_back(grad, e, inv, gain(1))

        by_rows(fifth)

        @pl.when(step == tiles)
        def _():
            store_wide(gblocks_out, 0, mixin_acc)
            store_wide(gblocks_out, 2, mixout_acc)
            store_wide(gblocks_out, 3, convin_acc)
            for k in range(8):
                gvec_out[k : k + 1, :] = jnp.sum(vec_acc[k], axis=0, keepdims=True)
            gmap_out[...] = map_acc[...]
            gdecay_out[...] = decay_acc[...] * map_ref[...]

    @pl.when(step > 0)
    def _():
        back_tile()

    if fused:

        @pl.when(step == tiles)
        def _():
            for wait in sends:
                wait()


def back(mesh_size, offsets, counts, wholes, tiled, hold, blocks, vec, stat, decay, maps, grads=(), collective_id=None):
    fused = mesh_size is not None
    frames, channels = wholes[0].shape
    tiles = frames // TILE
    place = lambda i: tiles - jnp.maximum(i, 1)
    row = lambda width: pl.BlockSpec((TILE, width), lambda i: (place(i), 0))
    spans = TILE // SPAN
    state = jax.ShapeDtypeStruct((STATES, channels), F32)
    shapes = [
        jax.ShapeDtypeStruct((frames, channels), F32),
        jax.ShapeDtypeStruct(blocks.shape, BF16),
        jax.ShapeDtypeStruct((8, channels), F32),
        jax.ShapeDtypeStruct((16, channels), F32),
        state,
        state,
    ]
    pad = pltpu.VMEM((channels // 128, tiles * (TILE + 2 * REACH), 128), F32)
    scratch = [
        pltpu.VMEM((channels, 2 * channels), F32),
        pltpu.VMEM((channels, channels), F32),
        pltpu.VMEM((channels, 2 * channels), F32),
        pltpu.VMEM((8, 8, channels), F32),
        pltpu.VMEM((STATES, channels), F32),
        pltpu.VMEM((STATES, channels), F32),
        pltpu.VMEM((STATES, channels), F32),
        pltpu.VMEM((SPAN, STATES, channels), F32),
        pltpu.VMEM((TILE, channels), BF16),
        pltpu.VMEM((TILE, 2 * channels), BF16),
        pltpu.VMEM((TILE, channels), F32),
        pltpu.VMEM((TILE, channels), F32),
        pad,
        pad,
    ]
    if fused:
        counts_of = [g.shape[-3] for g in grads]
        shapes += [jax.ShapeDtypeStruct((k, PIECE, WIDTH), F32) for k in counts_of]
        scratch += block_scratch(*mesh_size, counts_of, (PIECE, WIDTH))
        scratch += block_sems(*mesh_size, len(grads))
    return pl.pallas_call(
        partial(back_kernel, mesh_size),
        grid=(tiles + 1,),
        in_specs=[SMEM_SPEC, SMEM_SPEC]
        + [whole(a.shape) for a in wholes]
        + [row(channels)] * len(tiled)
        + [pl.BlockSpec((spans, STATES, channels), lambda i: (place(i), 0, 0))]
        + [whole(a.shape) for a in (blocks, vec, stat, decay, maps)]
        + [HBM_SPEC] * len(grads),
        out_specs=[row(channels)] + [whole(s.shape) for s in shapes[1:]],
        out_shape=shapes,
        scratch_shapes=scratch,
        compiler_params=params(collective_id),
        name="back",
    )(offsets, counts, *wholes, *tiled, hold, blocks, vec, stat, decay, maps, *grads)


def small_gradients(out, gvec1, gvec2, gvec3, gtaps, gmap, gdecay, table_ref):
    out[...] = jnp.zeros_like(out)
    gains = {1: (gvec2, 6), 2: (gvec2, 2), 3: (gvec1, 3), 4: (gvec1, 0), 5: (gvec1, 6)}
    shifts = {1: (gvec2, 7), 2: (gvec2, 3), 3: (gvec1, 4), 4: (gvec1, 1), 5: (gvec1, 7)}
    shifts.update({6: (gvec3, 0), 7: (gvec1, 2), 8: (gvec2, 4), 9: (gvec2, 0), 10: (gvec2, 1)})
    shifts.update({11: (gvec2, 5), 12: (gvec1, 5)})
    for at, (ref, row) in gains.items():
        out[at : at + 1, :] = ref[row : row + 1, :]
    for at, (ref, row) in shifts.items():
        out[6 + at : 7 + at, :] = ref[row : row + 1, :]
    out[TAP_ROW : TAP_ROW + TAPS, :] = gtaps[:TAPS, :]
    log_decay, decay, root, maps_in, maps_out = state_terms(table_ref)
    both = gmap[...] * root
    out[MAP_IN:MAP_OUT, :] = both * maps_out
    out[MAP_OUT:TABLE, :] = both * maps_in
    turn = (1.0 - root * root) / root
    out[RATE:MAP_IN, :] = log_decay * (
        gdecay[...] * decay - gmap[...] * maps_in * maps_out * turn
    )


def store_cols(out, at, value):
    per = WIDTH // CHUNK
    groups = value.shape[0] // PIECE
    out[:, lax.div(at, per), :, columns(lax.rem(at, per))] = value.reshape((groups, PIECE, CHUNK))


def tail_kernel(mesh_size, *refs):
    fused = mesh_size is not None
    refs = list(refs)
    take = lambda count: [refs.pop(0) for _ in range(count)]
    x_ref, h_ref, gx1_ref, up_ref, down_ref, table_ref = take(6)
    hidden = 4 * WIDTH
    if fused:
        gvec1, gvec2, gtaps, gmap, gdecay, gbias1 = take(6)
        sources = take(1)
        gx_ref, last_out = take(2)
        reduced = take(5)
    else:
        gx_ref, gvec_out, gbias_out, up_out, down_out = take(5)
    turn_scr, grad_scr, gh_scr, vec_acc, bias_scr = take(5)
    step = pl.program_id(0)
    frames, channels = x_ref.shape
    chunks = hidden // CHUNK
    tiles = frames // TILE
    first_b, first_c = 1 + chunks, 1 + 2 * chunks
    schedule = {}
    if fused:
        n_dp, n_fs = mesh_size
        down_src, left_src, right_src, small_src, small_scr, gvec3 = take(6)
        dp, fs = lax.axis_index("dp"), lax.axis_index("fsdp")
        place = Place(dp, fs, n_dp, n_fs)
        scratch = take(5 * (2 + place.count))
        sems = take(3)
        swap = take(4)
        down_out = flat_groups(down_src)
        halves = (flat_groups(left_src), flat_groups(right_src))

        def emit(chunk, total):
            reduced[chunk][...] = total

        plans, sends = block_scatter(
            place, sources + [down_src, left_src, right_src, small_src], emit, scratch, *sems
        )
        begins = [
            (0, 3, 5, 7, 9),
            (first_b, first_b + 2, first_b + 4, first_b + 6, first_c),
            (first_b + 4, first_b + 6, first_c, first_c + 1, first_c + 2),
            (first_c, first_c + 1, first_c + 2, first_c + tiles, first_c + tiles),
            (first_c, first_c + 1, first_c + 2, first_c + tiles, first_c + tiles),
        ]
        for chunk, steps in enumerate(begins):
            for stage, at in enumerate(steps):
                schedule.setdefault(at, []).append((stage, chunk))
    last_step = first_c + tiles - 1

    def progress(at):
        for stage, chunk in sorted(schedule.get(at, [])):
            plans[chunk][stage]()

    @pl.when(step == 0)
    def _():
        if fused:
            greet(dp, fs, n_dp, n_fs)
        progress(0)
        vec_acc[...] = jnp.zeros_like(vec_acc)

        def first(rows):
            e, _ = norm_parts(x_ref[rows, :].astype(F32))
            low = (e * table_ref[0:1, :] + table_ref[6:7, :]).astype(BF16)
            turn_scr[:, rows] = low.T
            grad = (0.5 * gx1_ref[rows, :]).astype(BF16)
            grad_scr[rows, :] = grad
            vec_acc[0] += fold8(grad.astype(F32))

        by_rows(first, frames)

    if fused:
        for at in range(1, last_step + 1):
            if at in schedule and at != first_c:

                @pl.when(step == at)
                def _(at=at):
                    progress(at)

    @pl.when((step >= 1) & (step < first_b))
    def _():
        h = h_ref[...].astype(F32)
        active = (h * sigmoid(h)).astype(BF16)
        value = dot_tn(active, grad_scr[...]).astype(BF16)
        groups = CHUNK // (4 * PIECE)
        down_out[pl.ds((step - 1) * groups, groups)] = value.reshape((groups, 4, PIECE, WIDTH))

    def second_half(c, store):
        cols = columns(c)
        h = h_ref[...].astype(F32)
        sig = sigmoid(h)
        gate = dot_nt(grad_scr[...], rows_of(down_ref, 0, c))
        grad_h = (gate * (sig * (1.0 + h * (1.0 - sig)))).astype(BF16)
        gh_scr[:, cols] = grad_h
        bias_scr[pl.ds(c, 1), :] = jnp.sum(fold8(grad_h.astype(F32)), axis=0, keepdims=True)
        store(dot_nn(turn_scr[...], grad_h).astype(BF16))

    if fused:
        for half in range(2):
            begin = first_b + half * (chunks // 2)

            @pl.when((step >= begin) & (step < begin + chunks // 2))
            def _(half=half, begin=begin):
                def store(value):
                    store_cols(halves[half], step - begin, value)

                second_half(step - first_b, store)

    else:

        @pl.when((step >= first_b) & (step < first_c))
        def _():
            def store(value):
                store_cols(up_out, step - first_b, value)

            second_half(step - first_b, store)

    if fused:

        @pl.when(step == first_c)
        def _():
            gvec3[0:1, :] = jnp.sum(vec_acc[0], axis=0, keepdims=True)
            small_gradients(small_scr, gvec1, gvec2, gvec3, gtaps, gmap, gdecay, table_ref)
            narrow = small_scr[...].T.astype(BF16)
            devices = n_dp * n_fs
            small_out = flat_groups(small_src)
            small_out[:, 0, :, :CHUNK] = narrow.reshape((devices, PIECE, CHUNK))
            for c in range(chunks):
                bias_scr[chunks + c : chunks + c + 1, :] = gbias1[0:1, c * CHUNK : c * CHUNK + CHUNK]
            bias = bias_scr[...].astype(BF16)
            small_out[:, 0, :, CHUNK:] = jnp.broadcast_to(bias[None], (devices, PIECE, CHUNK))
            progress(first_c)

    @pl.when(step >= first_c)
    def _():
        tile = step - first_c
        whole_tile = pl.ds(pl.multiple_of(tile * TILE, TILE), TILE)
        total = dot_nt(gh_scr[whole_tile, :WIDTH], square_of(up_ref, 1))
        for k in range(1, hidden // WIDTH):
            cols = slice(k * WIDTH, k * WIDTH + WIDTH)
            total = total + dot_nt(gh_scr[whole_tile, cols], square_of(up_ref, 1 + k))
        gx_ref[...] = total

        def second(rows):
            here = pl.ds(pl.multiple_of(tile * TILE + rows.start, ROWS), ROWS)
            e, inv = norm_parts(x_ref[here, :].astype(F32))
            grad = gx_ref[rows, :]
            vec_acc[1] += fold8(grad * e)
            vec_acc[2] += fold8(grad)
            gx_ref[rows, :] = gx1_ref[here, :] + norm_back(grad, e, inv, table_ref[0:1, :])

        by_rows(second)

    @pl.when(step == last_step)
    def _():
        if fused:
            last_out[...] = jnp.zeros_like(last_out)
            for k in range(2):
                last_out[k : k + 1, :] = jnp.sum(vec_acc[1 + k], axis=0, keepdims=True)
            ends = sorted(schedule.get(last_step + 1, []))

            def between():
                for stage, chunk in ends:
                    plans[chunk][stage]()

            last_out[...] = sum_over(last_out[...], dp, fs, n_dp, n_fs, *swap, between=between)
            for wait in sends:
                wait()
        else:
            gvec_out[...] = jnp.zeros_like(gvec_out)
            for k in range(3):
                gvec_out[k : k + 1, :] = jnp.sum(vec_acc[k], axis=0, keepdims=True)
            gbias_out[...] = bias_scr[...]


def tail(mesh_size, x, h, gx1, up, down, table, others=(), grads=(), collective_id=None):
    fused = mesh_size is not None
    frames, channels = x.shape
    hidden = h.shape[1]
    tiles, chunks = frames // TILE, hidden // CHUNK
    first_b, first_c = 1 + chunks, 1 + 2 * chunks
    place = lambda i: jnp.where(
        i < first_b, jnp.maximum(i - 1, 0), jnp.minimum(i - first_b, chunks - 1)
    )
    shapes = [jax.ShapeDtypeStruct((frames, channels), F32)]
    scratch = [
        pltpu.VMEM((channels, frames), BF16),
        pltpu.VMEM((frames, channels), BF16),
        pltpu.VMEM((frames, hidden), BF16),
        pltpu.VMEM((8, 8, channels), F32),
        pltpu.VMEM((2 * chunks, CHUNK), F32),
    ]
    if fused:
        own = [4, 2, 2, 1]
        counts = [g.shape[-3] for g in grads] + own
        shapes.append(jax.ShapeDtypeStruct((8, channels), F32))
        shapes += [jax.ShapeDtypeStruct((k, PIECE, WIDTH), F32) for k in counts]
        layout = block_layout(*mesh_size)
        scratch += [pltpu.VMEM(layout + (k, PIECE, WIDTH), BF16) for k in own]
        scratch += [pltpu.VMEM((256, channels), F32), pltpu.VMEM((8, channels), F32)]
        scratch += block_scratch(*mesh_size, counts, (PIECE, WIDTH))
        scratch += block_sems(*mesh_size, len(counts))
        scratch += swap_scratch(*mesh_size, channels)
    else:
        shapes += [
            jax.ShapeDtypeStruct((8, channels), F32),
            jax.ShapeDtypeStruct((2 * chunks, CHUNK), F32),
            jax.ShapeDtypeStruct((channels // PIECE, 4, PIECE, WIDTH), BF16),
            jax.ShapeDtypeStruct((channels // PIECE, 4, PIECE, WIDTH), BF16),
        ]
    return pl.pallas_call(
        partial(tail_kernel, mesh_size),
        grid=(first_c + tiles,),
        in_specs=[whole(x.shape), pl.BlockSpec((frames, CHUNK), lambda i: (0, place(i)))]
        + [whole(a.shape) for a in (gx1, up, down, table) + tuple(others)]
        + [pl.BlockSpec(memory_space=pltpu.HBM)] * len(grads),
        out_specs=[
            pl.BlockSpec((TILE, channels), lambda i: (jnp.maximum(i - first_c, 0), 0))
        ]
        + [whole(s.shape) for s in shapes[1:]],
        out_shape=shapes,
        scratch_shapes=scratch,
        compiler_params=params(collective_id),
        name="tail",
    )(x, h, gx1, up, down, table, *others, *grads)


def unpack_kernel(
    place_ref,
    second_ref,
    mixer_ref,
    down_ref,
    left_ref,
    right_ref,
    small_ref,
    last_ref,
    up_out,
    down_out,
    bias_out,
    mixin_out,
    mixout_out,
    convin_out,
    convout_out,
    convbias_out,
    rate_out,
    map_out,
    taps_out,
    gains_out,
    shifts_out,
):
    mine = place_ref[0]
    for k in range(4):
        cols = slice(k * WIDTH, k * WIDTH + WIDTH)
        rows = slice(k * PIECE, k * PIECE + PIECE)
        up_out[0, :, cols] = (left_ref if k < 2 else right_ref)[k % 2]
        up_out[1, :, cols] = second_ref[1 + k]
        down_out[0, rows, :] = down_ref[k]
        down_out[1, rows, :] = second_ref[5 + k]
    convout_out[...] = second_ref[0]
    mixout_out[...] = mixer_ref[2]
    for k in range(2):
        cols = slice(k * WIDTH, k * WIDTH + WIDTH)
        mixin_out[:, cols] = mixer_ref[k]
        convin_out[:, cols] = mixer_ref[3 + k]
    count = bias_out.shape[1]
    row = (mine * count) // CHUNK
    inner = mine * count - row * CHUNK
    for layer in range(2):
        line = small_ref[0, pl.ds(8 * layer + row, 1), CHUNK:]
        line = pltpu.roll(jnp.broadcast_to(line, (8, CHUNK)), CHUNK - inner, 1)
        bias_out[layer : layer + 1, :] = line[0:1, :count]
    channels = last_ref.shape[1]
    first = pltpu.roll(last_ref[...], channels - mine * PIECE, 1)[:, :PIECE]
    small = small_ref[0, :, :CHUNK]
    turned = small.T
    gains_out[...] = turned[0:6, :]
    gains_out[0:1, :] = first[0:1, :]
    shifts_out[...] = turned[6:18, :]
    shifts_out[0:1, :] = first[1:2, :]
    convbias_out[...] = turned[18:19, :]
    taps_out[...] = turned[TAP_ROW : TAP_ROW + TAPS, :]
    rate_out[...] = small[:, RATE:MAP_IN]
    map_out[0] = small[:, MAP_IN:MAP_OUT]
    map_out[1] = small[:, MAP_OUT:TABLE]


def unpack(mine, arrays, hidden):
    channels = arrays[-1].shape[1]
    devices = channels // PIECE
    f32 = lambda *shape: jax.ShapeDtypeStruct(shape, F32)
    vmem = pl.BlockSpec(memory_space=pltpu.VMEM)
    return pl.pallas_call(
        unpack_kernel,
        in_specs=[SMEM_SPEC] + [vmem] * len(arrays),
        out_specs=[vmem] * 13,
        out_shape=[
            f32(2, PIECE, hidden),
            f32(2, hidden // devices, channels),
            f32(2, hidden // devices),
            f32(PIECE, 2 * WIDTH),
            f32(PIECE, WIDTH),
            f32(PIECE, 2 * WIDTH),
            f32(PIECE, WIDTH),
            f32(1, PIECE),
            f32(PIECE, STATES),
            f32(2, PIECE, STATES),
            f32(TAPS, PIECE),
            f32(6, PIECE),
            f32(12, PIECE),
        ],
        name="unpack",
    )(mine, *arrays)


def pack_table(gains, shifts, conv_bias, taps, rate, maps):
    channels = gains.shape[1]
    blank = lambda rows: jnp.zeros((rows, channels), gains.dtype)
    parts = [gains, shifts, conv_bias[None], blank(TAP_ROW - 19), taps, blank(RATE - TAP_ROW - TAPS)]
    parts += [rate, maps[0], maps[1], blank(256 - TABLE)]
    return jnp.concatenate(parts, axis=0).T


def pack_bias(bias, place):
    layers, count = bias.shape
    hidden = 16 * CHUNK // layers
    wide = lax.dynamic_update_slice(
        jnp.zeros((layers, hidden), bias.dtype), bias, (0, place * count)
    )
    return wide.reshape((16, CHUNK))


def unpack_table(table):
    return (
        table[0:6],
        table[6:18],
        table[18],
        table[TAP_ROW : TAP_ROW + TAPS],
        table[RATE:MAP_IN],
        jnp.stack([table[MAP_IN:MAP_OUT], table[MAP_OUT:TABLE]]),
    )


def on_device(
    n_dp,
    n_fs,
    frames,
    seq_lengths,
    seq_offsets,
    seq_counts,
    ffn_up,
    ffn_down,
    ffn_bias_up,
    mix_in,
    mix_out,
    conv_in,
    conv_out,
    conv_out_bias,
    ssm_rate,
    ssm_map,
    conv_kernel,
    gains,
    shifts,
    cotangent,
):
    devices = n_dp * n_fs
    mine = lax.axis_index("dp") * n_fs + lax.axis_index("fsdp")
    frames_dev, channels = frames.shape
    hidden = ffn_up.shape[2]
    if channels // devices == PIECE:
        size = (n_dp, n_fs)
        small = [
            ffn_bias_up,
            gains,
            shifts,
            conv_out_bias[None],
            conv_kernel,
            ssm_rate.T,
            ssm_map.transpose((0, 2, 1)),
        ]
        weights = [ffn_up, ffn_down, mix_in, mix_out, conv_in, conv_out]
        made = front(size, seq_offsets, seq_counts, frames, small, weights, hidden, 1)
        h0, x1, u, v, y, gated, x2, p, hold, w, stat, table, bias, decay, coupling = made[:15]
        groups = lambda g: g.reshape((devices,) + g.shape[-3:])
        places = lambda g: g.reshape(block_layout(n_dp, n_fs) + g.shape[1:])
        first, second, third, fourth = [groups(g) for g in made[15:]]
        result, gx3, gnb, grads, gbias1, gvec1, stat = middle(
            size, x2, w, cotangent, fourth, bias, table, stat, hidden, 2
        )
        gx1, grads2, gvec2, gtaps, gmap, gdecay, reduced = back(
            size,
            seq_offsets,
            seq_counts,
            [w, gnb, p],
            [x2, gx3, gated, y, v, u, x1],
            hold,
            third,
            table,
            stat,
            decay,
            coupling,
            (places(grads),),
            3,
        )
        others = (gvec1, gvec2, gtaps, gmap, gdecay, gbias1)
        gx, last, *late = tail(
            size, frames, h0, gx1, first, second, table, others, (places(grads2),), 4
        )
        made = unpack(mine.reshape((1,)), [reduced] + late + [last], hidden)
        made = list(made)
        made[7] = made[7].reshape((-1,))
        made[8] = made[8].T
        made[9] = made[9].transpose((0, 2, 1))
        return (result, gx) + tuple(made)

    small = pack_table(gains, shifts, conv_out_bias, conv_kernel, ssm_rate, ssm_map)
    got = gather_all(
        n_dp,
        n_fs,
        [
            small[None],
            pack_bias(ffn_bias_up, mine)[None],
            ffn_up,
            ffn_down,
            mix_in[None],
            mix_out[None],
            conv_in[None],
            conv_out[None],
        ],
        1,
    )
    matrix = lambda g: g.reshape((-1, g.shape[-1]))
    table, _, up0, up1, down0, down1, mixin, mixout, convin, convout = [matrix(g) for g in got]
    table = table.astype(F32).T[:TABLE]
    bias = jnp.sum(got[1].astype(F32), axis=0)
    group_count = channels // PIECE
    cut = lambda g: g.reshape((group_count, PIECE, -1, WIDTH)).transpose((0, 2, 1, 3))
    tall = lambda g: g.reshape((group_count, -1, PIECE, WIDTH))
    join = lambda g: g.transpose((0, 2, 1, 3)).reshape((channels, -1))
    blank = jnp.zeros((group_count, 1, PIECE, WIDTH), BF16)
    first = jnp.concatenate([blank, cut(up0)], axis=1)
    third = jnp.concatenate([cut(mixin), cut(mixout), cut(convin)], axis=1)
    fourth = jnp.concatenate([cut(convout), cut(up1), tall(down1)], axis=1)
    made = front(
        None, seq_offsets, seq_counts, frames, [table, bias], [first, tall(down0), third], hidden
    )
    h0, x1, u, v, y, gated, x2, p, hold, w, stat, table, bias, decay, coupling = made
    pool = exchange(n_dp, n_fs, stat, frames_dev, 2, pool_kernel)
    scale = lax.rsqrt(pool[1:2] / (frames_dev * devices) + EPSILON)
    stat = jnp.concatenate([pool[0:1], scale, jnp.zeros((6, channels), F32)])
    result, gx3, gnb, grads, gbias1, gvec1, stat = middle(
        None, x2, w, cotangent, fourth, bias, table, stat, hidden
    )
    sums = exchange(n_dp, n_fs, gvec1, 1, 4, total_kernel)[6:8]
    sums = sums * (table[5:6] / (frames_dev * devices))
    stat = jnp.concatenate([stat[0:2], sums[1:2], sums[0:1], stat[4:8]])
    gx1, grads2, gvec2, gtaps, gmap, gdecay = back(
        None,
        seq_offsets,
        seq_counts,
        [w, gnb, p],
        [x2, gx3, gated, y, v, u, x1],
        hold,
        third,
        table,
        stat,
        decay,
        coupling,
    )
    gx, gvec3, gbias0, gup0, gdown0 = tail(None, frames, h0, gx1, first, tall(down0), table)

    def weights_of(log_rate, maps):
        log_decay = -jnp.exp(log_rate)
        root = jnp.sqrt(-jnp.expm1(2.0 * log_decay))
        return jnp.exp(log_decay), maps[0] * root * maps[1]

    rate, maps = unpack_table(table)[4:]
    rate_grad, map_grad = jax.vjp(weights_of, rate, maps)[1]((gdecay, gmap))
    gain_grad = jnp.stack([gvec3[1], gvec2[6], gvec2[2], gvec1[3], gvec1[0], gvec1[6]])
    rows = [gvec3[2], gvec2[7], gvec2[3], gvec1[4], gvec1[1], gvec1[7], gvec3[0], gvec1[2]]
    rows += [gvec2[4], gvec2[0], gvec2[1], gvec2[5]]
    small_grad = pack_table(
        gain_grad, jnp.stack(rows), gvec1[5], gtaps[:TAPS], rate_grad, map_grad
    )
    bias_grad = jnp.concatenate([gbias0[:8], gbias1[0].reshape((8, CHUNK))])
    wide = lambda g: g.reshape((devices, g.shape[0] // devices, g.shape[1]))
    reduced = scatter_all(
        n_dp,
        n_fs,
        [
            wide(join(grads[:, 1:5])),
            wide(matrix(grads[:, 5:9])),
            wide(join(grads[:, 0:1])),
            wide(join(grads2[:, 3:5])),
            wide(join(grads2[:, 2:3])),
            wide(join(grads2[:, 0:2])),
            wide(join(gup0)),
            wide(matrix(gdown0)),
            wide(small_grad.astype(BF16)),
            jnp.broadcast_to(bias_grad.astype(BF16), (devices, PIECE, CHUNK)),
        ],
        5,
    )
    gains_grad, shifts_grad, conv_bias_grad, taps_grad, rate_grad, map_grad = unpack_table(
        reduced[8].T
    )
    bias_grad = reduced[9].reshape((2, -1))
    count = bias_grad.shape[1] // devices
    bias_grad = lax.dynamic_slice(bias_grad, (0, mine * count), (2, count))
    return (
        result,
        gx,
        jnp.stack([reduced[6], reduced[0]]),
        jnp.stack([reduced[7], reduced[1]]),
        bias_grad,
        reduced[5],
        reduced[4],
        reduced[3],
        reduced[2],
        conv_bias_grad,
        rate_grad,
        map_grad,
        taps_grad,
        gains_grad,
        shifts_grad,
    )


def solution(mesh):
    both = ("dp", "fsdp")
    row, row1 = P(both, None), P(both)
    col, col3, mid = P(None, both), P(None, None, both), P(None, both, None)
    in_specs = (
        row,
        row,
        row,
        row1,
        mid,
        mid,
        col,
        row,
        row,
        row,
        row,
        row1,
        col,
        col3,
        col,
        col,
        col,
        row,
    )
    out_specs = (row, row, mid, mid, col, row, row, row, row, row1, col, col3, col, col, col)
    return jax.shard_map(
        partial(on_device, mesh.shape["dp"], mesh.shape["fsdp"]),
        mesh=mesh,
        in_specs=in_specs,
        out_specs=out_specs,
        check_vma=False,
    )
```

```python
import itertools
from functools import partial

import jax
import jax.numpy as jnp
from jax import lax
from jax.experimental import pallas as pl
from jax.experimental.pallas import tpu as pltpu
from jax.sharding import PartitionSpec as P

MESH = pl.DeviceIdType.MESH
BF16 = jnp.bfloat16
F32 = jnp.float32


def flip(index, bit):
    return index + bit * (1 - 2 * lax.rem(lax.div(index, bit), 2))


def flip_all(index, bits):
    for bit in bits:
        index = flip(index, bit)
    return index


def combos(bits):
    found = [()]
    for bit in bits:
        found = found + [entry + (bit,) for entry in found]
    return found


def plan_bits(n_dp):
    bits, bit = [], 2
    while bit < n_dp:
        bits.append(bit)
        bit *= 2
    return tuple(bits)


def greet(dp, fs, n_dp, n_fs):
    barrier = pltpu.get_barrier_semaphore()
    for step in range(1, n_dp):
        pl.semaphore_signal(
            barrier, inc=1, device_id=(lax.rem(dp + step, n_dp), fs), device_id_type=MESH
        )
    for step in range(1, n_fs):
        pl.semaphore_signal(
            barrier, inc=1, device_id=(dp, lax.rem(fs + step, n_fs)), device_id_type=MESH
        )
    pl.semaphore_wait(barrier, n_dp + n_fs - 2)


def gather_plan(dp, fs, n_dp, n_fs, sources, outs, send_sem, recv_sem, local_sem):
    bits = plan_bits(n_dp)
    orders = (bits, bits[::-1])
    half = n_fs // 2
    sends = []

    def stages(chunk):
        src, out = sources[chunk], outs[chunk]
        slots = itertools.count()

        def zone(where, part):
            if part is None:
                return out.at[pl.ds(where * n_fs, n_fs)]
            return out.at[pl.ds(where * n_fs + part * half, half)]

        def remote(slot, view_from, view_to, device):
            return pltpu.make_async_remote_copy(
                src_ref=view_from,
                dst_ref=view_to,
                send_sem=send_sem.at[chunk, slot],
                recv_sem=recv_sem.at[chunk, slot],
                device_id=device,
                device_id_type=MESH,
            )

        def launch(make):
            make().start()
            sends.append(lambda: make().wait_send())

        z_slots = [next(slots) for _ in range(1, n_fs)]

        def own_copy():
            return pltpu.make_async_copy(src, out.at[dp * n_fs + fs], local_sem.at[chunk])

        def start():
            own_copy().start()
            for step in range(1, n_fs):
                launch(
                    lambda step=step: remote(
                        z_slots[step - 1],
                        src,
                        out.at[dp * n_fs + fs],
                        (dp, lax.rem(fs + step, n_fs)),
                    )
                )

        def wait_z():
            own_copy().wait()
            for step in range(1, n_fs):
                origin = dp * n_fs + lax.rem(fs + n_fs - step, n_fs)
                remote(z_slots[step - 1], src, out.at[origin], (dp, fs)).wait_recv()

        steps, before = [start], wait_z
        for depth in range(len(bits)):
            plan = []
            for part, order in enumerate(orders):
                for entry in combos(order[:depth]):
                    plan.append((next(slots), part, order[depth], entry))

            def view(slot, part, bit, entry, arrived):
                where = flip_all(flip(dp, bit) if arrived else dp, entry)
                return remote(slot, zone(where, part), zone(where, part), (flip(dp, bit), fs))

            def go(plan=plan, before=before, view=view):
                before()
                for item in plan:
                    launch(lambda item=item: view(*item, False))

            def arrive(plan=plan, view=view):
                for item in plan:
                    view(*item, True).wait_recv()

            steps.append(go)
            before = arrive
        last = [(next(slots), entry) for entry in combos(bits)]

        def across(slot, entry, arrived):
            where = flip_all(flip(dp, 1) if arrived else dp, entry)
            return remote(slot, zone(where, None), zone(where, None), (flip(dp, 1), fs))

        def cross(before=before):
            before()
            for item in last:
                launch(lambda item=item: across(*item, False))

        def finish():
            for item in last:
                across(*item, True).wait_recv()

        return steps + [cross, finish]

    return [stages(chunk) for chunk in range(len(outs))], sends


def waves(plans):
    depth = len(plans[0])
    out = []
    for wave in range(len(plans) + depth - 1):
        out.append(
            [plans[c][wave - c] for c in range(len(plans)) if 0 <= wave - c < depth]
        )
    return out


def gather_kernel(n_dp, n_fs, layers, *refs):
    n_in = len(layers)
    n_out = sum(layers)
    ins, outs = refs[:n_in], refs[n_in : n_in + n_out]
    send_sem, recv_sem, local_sem = refs[n_in + n_out :]
    sources = []
    for ref, count in zip(ins, layers):
        sources += [ref.at[layer] for layer in range(count)]
    dp, fs = lax.axis_index("dp"), lax.axis_index("fsdp")
    greet(dp, fs, n_dp, n_fs)
    plans, sends = gather_plan(dp, fs, n_dp, n_fs, sources, outs, send_sem, recv_sem, local_sem)
    for wave in waves(plans):
        for stage in wave:
            stage()
    for wait in sends:
        wait()


def slot_count(n_dp, n_fs):
    nb = len(plan_bits(n_dp))
    return n_fs - 1 + 2 * (2**nb - 1) + 2**nb


def gather_all(n_dp, n_fs, arrays, collective_id):
    layers = tuple(a.shape[0] for a in arrays)
    outs = []
    for a in arrays:
        outs += [jax.ShapeDtypeStruct((n_dp * n_fs,) + a.shape[1:], a.dtype)] * a.shape[0]
    count = slot_count(n_dp, n_fs)
    return pl.pallas_call(
        partial(gather_kernel, n_dp, n_fs, layers),
        out_shape=outs,
        in_specs=[pl.BlockSpec(memory_space=pltpu.HBM)] * len(arrays),
        out_specs=[pl.BlockSpec(memory_space=pltpu.HBM)] * len(outs),
        scratch_shapes=[
            pltpu.SemaphoreType.DMA((len(outs), count)),
            pltpu.SemaphoreType.DMA((len(outs), count)),
            pltpu.SemaphoreType.DMA((len(outs),)),
        ],
        compiler_params=pltpu.CompilerParams(collective_id=collective_id, has_side_effects=True),
        name="gather_parameters",
    )(*arrays)


def scatter_plan(dp, fs, n_dp, n_fs, ins, emit, scratch, send_sem, recv_sem, local_sem, first=0):
    bits = plan_bits(n_dp)
    orders = (bits[::-1], bits)
    half = n_fs // 2
    index = {entry: at for at, entry in enumerate(combos(bits))}
    sends = []

    def add_into(kept, other):
        def body(at, _):
            kept[at] = (kept[at].astype(F32) + other[at].astype(F32)).astype(BF16)
            return 0

        lax.fori_loop(0, kept.shape[0], body, 0)

    def stages(chunk):
        src = ins[chunk]
        cross_in, own, later, last = scratch[4 * chunk : 4 * chunk + 4]
        slots = itertools.count()

        def remote(slot, view_from, view_to, device):
            return pltpu.make_async_remote_copy(
                src_ref=view_from,
                dst_ref=view_to,
                send_sem=send_sem.at[first + chunk, slot],
                recv_sem=recv_sem.at[first + chunk, slot],
                device_id=device,
                device_id_type=MESH,
            )

        def launch(make):
            make().start()
            sends.append(lambda: make().wait_send())

        def zone(entry, crossed):
            return src.at[pl.ds(flip_all(flip(dp, 1) if crossed else dp, entry) * n_fs, n_fs)]

        pieces = [(next(slots), entry, index[entry]) for entry in combos(bits)]

        def load(entry, at):
            return pltpu.make_async_copy(
                zone(entry, False), own.at[at], local_sem.at[first + chunk, at]
            )

        def across(slot, entry, at):
            return remote(slot, zone(entry, True), cross_in.at[at], (flip(dp, 1), fs))

        def start():
            for item in pieces:
                launch(lambda item=item: across(*item))
            for _, entry, at in pieces:
                load(entry, at).start()

        def fold_cross():
            for slot, entry, at in pieces:
                load(entry, at).wait()
                across(slot, entry, at).wait_recv()
                add_into(own.at[at], cross_in.at[at])

        steps, before = [start], fold_cross
        used = 0
        for depth in range(len(bits)):
            plan = []
            for part, order in enumerate(orders):
                bit, gone = order[depth], order[:depth]
                for entry in combos(bits):
                    if not (set(entry) & set(gone)) and bit not in entry:
                        away = tuple(sorted(entry + (bit,)))
                        plan.append((next(slots), part, bit, index[away], index[entry], used))
                        used += 1

            def move(slot, part, bit, away, kept, place):
                return remote(
                    slot,
                    own.at[away, pl.ds(part * half, half)],
                    later.at[place],
                    (flip(dp, bit), fs),
                )

            def go(plan=plan, before=before, move=move):
                before()
                for item in plan:
                    launch(lambda item=item: move(*item))

            def fold(plan=plan, move=move):
                for item in plan:
                    move(*item).wait_recv()
                    _, part, _, _, kept, place = item
                    add_into(own.at[kept, pl.ds(part * half, half)], later.at[place])

            steps.append(go)
            before = fold
        z_slots = [next(slots) for _ in range(1, n_fs)]

        def along(step):
            to = lax.rem(fs + step, n_fs)
            return remote(z_slots[step - 1], own.at[0, to], last.at[step - 1], (dp, to))

        def spread(before=before):
            before()
            for step in range(1, n_fs):
                launch(lambda step=step: along(step))

        def finish():
            total = own[0, fs].astype(F32)
            for step in range(1, n_fs):
                along(step).wait_recv()
                total = total + last[step - 1].astype(F32)
            emit(chunk, total)

        return steps + [spread, finish]

    return [stages(chunk) for chunk in range(len(ins))], sends


def scatter_scratch(n_dp, n_fs, tails):
    pieces = 2 ** len(plan_bits(n_dp))
    scratch = []
    for tail in tails:
        scratch += [
            pltpu.VMEM((pieces, n_fs) + tail, BF16),
            pltpu.VMEM((pieces, n_fs) + tail, BF16),
            pltpu.VMEM((2 * (pieces - 1), n_fs // 2) + tail, BF16),
            pltpu.VMEM((n_fs - 1,) + tail, BF16),
        ]
    return scratch


def scatter_sems(n_dp, n_fs, chunks):
    count = slot_count(n_dp, n_fs)
    return [
        pltpu.SemaphoreType.DMA((chunks, count)),
        pltpu.SemaphoreType.DMA((chunks, count)),
        pltpu.SemaphoreType.DMA((chunks, 2 ** len(plan_bits(n_dp)))),
    ]


def scatter_kernel(n_dp, n_fs, n_chunks, *refs):
    ins, outs = refs[:n_chunks], refs[n_chunks : 2 * n_chunks]
    scratch = refs[2 * n_chunks : 6 * n_chunks]
    dp, fs = lax.axis_index("dp"), lax.axis_index("fsdp")
    greet(dp, fs, n_dp, n_fs)

    def emit(chunk, total):
        outs[chunk][...] = total

    plans, sends = scatter_plan(dp, fs, n_dp, n_fs, ins, emit, scratch, *refs[6 * n_chunks :])
    for wave in waves(plans):
        for stage in wave:
            stage()
    for wait in sends:
        wait()


def scatter_all(n_dp, n_fs, arrays, collective_id):
    n = len(arrays)
    return pl.pallas_call(
        partial(scatter_kernel, n_dp, n_fs, n),
        out_shape=[jax.ShapeDtypeStruct(a.shape[1:], F32) for a in arrays],
        in_specs=[pl.BlockSpec(memory_space=pltpu.HBM)] * n,
        out_specs=[pl.BlockSpec(memory_space=pltpu.VMEM)] * n,
        scratch_shapes=scatter_scratch(n_dp, n_fs, [a.shape[1:] for a in arrays])
        + scatter_sems(n_dp, n_fs, n),
        compiler_params=pltpu.CompilerParams(
            collective_id=collective_id, has_side_effects=True, vmem_limit_bytes=48 << 20
        ),
        name="scatter_gradients",
    )(*arrays)


def swap_copy(axis, place, count, buffer, send_sem, recv_sem, step):
    return pltpu.make_async_remote_copy(
        src_ref=buffer.at[0],
        dst_ref=buffer.at[step],
        send_sem=send_sem.at[step],
        recv_sem=recv_sem.at[step],
        device_id={axis: lax.rem(place + step, count)},
        device_id_type=MESH,
    )


def swap_start(axis, place, count, *rest):
    for step in range(1, count):
        swap_copy(axis, place, count, *rest, step).start()


def swap_wait(axis, place, count, *rest):
    for step in range(1, count):
        swap_copy(axis, place, count, *rest, step).wait_recv()
    for step in range(1, count):
        swap_copy(axis, place, count, *rest, step).wait_send()


def swap_rows(*args):
    swap_start(*args)
    swap_wait(*args)


def sum_over(x, dp, fs, n_dp, n_fs, octet, line, send_sem, recv_sem, between=None):
    first = ("dp", dp, n_dp, octet, send_sem.at[0], recv_sem.at[0])
    octet[0] = x
    swap_start(*first)
    if between is not None:
        between()
    swap_wait(*first)
    total = octet[0]
    for step in range(1, n_dp):
        total = total + octet[step]
    line[0] = total
    swap_rows("fsdp", fs, n_fs, line, send_sem.at[1], recv_sem.at[1])
    total = line[0]
    for step in range(1, n_fs):
        total = total + line[step]
    return total


def pooled(buffer, count, weight):
    means = [buffer[k, 0:1, :] for k in range(count)]
    center = sum(means[1:], means[0]) * (1.0 / count)
    spread = buffer[0, 1:2, :]
    for k in range(1, count):
        spread = spread + buffer[k, 1:2, :]
    off = (means[0] - center) * (means[0] - center)
    for mean in means[1:]:
        off = off + (mean - center) * (mean - center)
    return center, spread + weight * off


def pool_over(center, spread, frames, dp, fs, n_dp, n_fs, octet, line, send_sem, recv_sem):
    octet[0] = jnp.zeros(octet.shape[1:], F32)
    line[0] = jnp.zeros(line.shape[1:], F32)
    octet[0, 0:1, :] = center
    octet[0, 1:2, :] = spread
    swap_rows("dp", dp, n_dp, octet, send_sem.at[0], recv_sem.at[0])
    center, spread = pooled(octet, n_dp, float(frames))
    line[0, 0:1, :] = center
    line[0, 1:2, :] = spread
    swap_rows("fsdp", fs, n_fs, line, send_sem.at[1], recv_sem.at[1])
    return pooled(line, n_fs, float(frames * n_dp))


def swap_scratch(n_dp, n_fs, channels):
    return [
        pltpu.VMEM((n_dp, 8, channels), F32),
        pltpu.VMEM((n_fs, 8, channels), F32),
        pltpu.SemaphoreType.DMA((2, max(n_dp, n_fs))),
        pltpu.SemaphoreType.DMA((2, max(n_dp, n_fs))),
    ]


def pool_kernel(n_dp, n_fs, frames, x_ref, out_ref, octet, line, send_sem, recv_sem):
    dp, fs = lax.axis_index("dp"), lax.axis_index("fsdp")
    greet(dp, fs, n_dp, n_fs)
    octet[0] = x_ref[...]
    center, spread = pool_over(
        x_ref[0:1, :], x_ref[1:2, :], frames, dp, fs, n_dp, n_fs, octet, line, send_sem, recv_sem
    )
    out_ref[...] = x_ref[...]
    out_ref[0:1, :] = center
    out_ref[1:2, :] = spread


def total_kernel(n_dp, n_fs, frames, x_ref, out_ref, octet, line, send_sem, recv_sem):
    dp, fs = lax.axis_index("dp"), lax.axis_index("fsdp")
    greet(dp, fs, n_dp, n_fs)
    out_ref[...] = sum_over(x_ref[...], dp, fs, n_dp, n_fs, octet, line, send_sem, recv_sem)


def exchange(n_dp, n_fs, x, frames, collective_id, kernel):
    return pl.pallas_call(
        partial(kernel, n_dp, n_fs, frames),
        out_shape=jax.ShapeDtypeStruct(x.shape, F32),
        in_specs=[pl.BlockSpec(memory_space=pltpu.VMEM)],
        out_specs=pl.BlockSpec(memory_space=pltpu.VMEM),
        scratch_shapes=swap_scratch(n_dp, n_fs, x.shape[1]),
        compiler_params=pltpu.CompilerParams(collective_id=collective_id, has_side_effects=True),
        name="exchange_rows",
    )(x)


class Place:
    def __init__(self, dp, fs, n_dp, n_fs):
        self.dp, self.fs, self.n_dp, self.n_fs = dp, fs, n_dp, n_fs
        self.count = (n_dp - 1).bit_length()
        self.bits = [lax.rem(lax.div(dp, 2**k), 2) for k in range(self.count)]
        self.half = n_fs // 2

    def peer(self, bit):
        return (flip(self.dp, 2**bit), self.fs)

    def view(self, ref, free=(), flipped=(), z=None, skip=()):
        index = []
        for bit in reversed(range(self.count)):
            if bit in skip:
                continue
            if bit in free:
                index.append(slice(None))
            else:
                index.append(1 - self.bits[bit] if bit in flipped else self.bits[bit])
        if z is not None:
            index.append(z)
        return ref.at[tuple(index)] if index else ref

    def part(self, which):
        return pl.ds(which * self.half, self.half)


def block_layout(n_dp, n_fs):
    return (2,) * ((n_dp - 1).bit_length()) + (n_fs,)


def hop_orders(place):
    bits = tuple(range(1, place.count))
    return (bits, bits[::-1])


def copy_count(n_dp, n_fs):
    return n_fs - 1 + 2 * ((n_dp - 1).bit_length() - 1) + 1


def block_gather(place, sources, outs, send_sem, recv_sem, local_sem):
    n_fs, fs = place.n_fs, place.fs
    sends = []

    def stages(chunk):
        src, out = sources[chunk], outs[chunk]

        def remote(slot, view_from, view_to, device):
            return pltpu.make_async_remote_copy(
                src_ref=view_from,
                dst_ref=view_to,
                send_sem=send_sem.at[chunk, slot],
                recv_sem=recv_sem.at[chunk, slot],
                device_id=device,
                device_id_type=MESH,
            )

        def launch(make):
            make().start()
            sends.append(lambda: make().wait_send())

        def own_copy():
            return pltpu.make_async_copy(src, place.view(out, z=fs), local_sem.at[chunk])

        def along(step):
            to = lax.rem(fs + step, n_fs)
            return remote(step - 1, src, place.view(out, z=fs), (place.dp, to))

        def start():
            own_copy().start()
            for step in range(1, n_fs):
                launch(lambda step=step: along(step))

        def wait_along():
            own_copy().wait()
            for step in range(1, n_fs):
                origin = lax.rem(fs + n_fs - step, n_fs)
                remote(
                    step - 1, src, place.view(out, z=origin), (place.dp, origin)
                ).wait_recv()

        steps, before = [start], wait_along
        slot = n_fs - 1
        orders = hop_orders(place)
        for depth in range(place.count - 1):
            plan = [(slot + part, part, order[depth], order[:depth]) for part, order in enumerate(orders)]
            slot += 2

            def hop(slot, part, bit, free, arrived):
                view = place.view(out, free, (bit,) if arrived else (), place.part(part))
                return remote(slot, view, view, place.peer(bit))

            def go(plan=plan, before=before, hop=hop):
                before()
                for item in plan:
                    launch(lambda item=item: hop(*item, False))

            def arrive(plan=plan, hop=hop):
                for item in plan:
                    hop(*item, True).wait_recv()

            steps.append(go)
            before = arrive

        def across(arrived, slot=slot):
            free = tuple(range(1, place.count))
            view = place.view(out, free, (0,) if arrived else ())
            return remote(slot, view, view, place.peer(0))

        def cross(before=before):
            before()
            launch(lambda: across(False))

        return steps + [cross, lambda: across(True).wait_recv()]

    return [stages(chunk) for chunk in range(len(outs))], sends


def block_scatter(place, sources, emit, scratch, send_sem, recv_sem, local_sem):
    n_fs, fs = place.n_fs, place.fs
    sends = []
    per = 3 + place.count - 1

    def add_into(kept, other):
        shape = kept.shape[:-3]
        for index in itertools.product(*[range(n) for n in shape]):
            kept[index] = (kept[index].astype(F32) + other[index].astype(F32)).astype(BF16)

    def stages(chunk):
        src = sources[chunk]
        own, cross_in, last, *later = scratch[per * chunk : per * chunk + per]

        def remote(slot, view_from, view_to, device):
            return pltpu.make_async_remote_copy(
                src_ref=view_from,
                dst_ref=view_to,
                send_sem=send_sem.at[chunk, slot],
                recv_sem=recv_sem.at[chunk, slot],
                device_id=device,
                device_id_type=MESH,
            )

        def launch(make):
            make().start()
            sends.append(lambda: make().wait_send())

        every = tuple(range(1, place.count))

        def load():
            return pltpu.make_async_copy(place.view(src, every), own, local_sem.at[chunk])

        def across():
            return remote(0, place.view(src, every, (0,)), cross_in, place.peer(0))

        def start():
            launch(across)
            load().start()

        def fold_cross():
            load().wait()
            across().wait_recv()
            add_into(own, cross_in)

        steps, before = [start], fold_cross
        slot = 1
        orders = [order[::-1] for order in hop_orders(place)]
        for depth in range(place.count - 1):
            plan = []
            for part, order in enumerate(orders):
                free = tuple(order[depth + 1 :])
                plan.append((slot + part, part, order[depth], free, later[depth]))
            slot += 2

            def hop(slot, part, bit, free, buffer):
                view = place.view(own, free, (bit,), place.part(part), skip=(0,))
                return remote(slot, view, buffer.at[part], place.peer(bit))

            def go(plan=plan, before=before, hop=hop):
                before()
                for item in plan:
                    launch(lambda item=item: hop(*item))

            def fold(plan=plan, hop=hop):
                for item in plan:
                    hop(*item).wait_recv()
                    _, part, _, free, buffer = item
                    kept = place.view(own, free, (), place.part(part), skip=(0,))
                    add_into(kept, buffer.at[part])

            steps.append(go)
            before = fold

        def along(step, slot=slot):
            to = lax.rem(fs + step, n_fs)
            view = place.view(own, z=to, skip=(0,))
            return remote(slot + step - 1, view, last.at[step - 1], (place.dp, to))

        def spread(before=before):
            before()
            for step in range(1, n_fs):
                launch(lambda step=step: along(step))

        def finish():
            total = place.view(own, z=fs, skip=(0,))[...].astype(F32)
            for step in range(1, n_fs):
                along(step).wait_recv()
                total = total + last[step - 1].astype(F32)
            emit(chunk, total)

        return steps + [spread, finish]

    return [stages(chunk) for chunk in range(len(sources))], sends


def block_scratch(n_dp, n_fs, blocks, tail):
    hops = (n_dp - 1).bit_length() - 1
    out = []
    for count in blocks:
        entry = (count,) + tail
        zone = (2,) * hops + (n_fs,) + entry
        out += [pltpu.VMEM(zone, BF16), pltpu.VMEM(zone, BF16), pltpu.VMEM((n_fs - 1,) + entry, BF16)]
        for depth in range(hops):
            out.append(pltpu.VMEM((2,) + (2,) * (hops - 1 - depth) + (n_fs // 2,) + entry, BF16))
    return out


def block_sems(n_dp, n_fs, chunks):
    count = copy_count(n_dp, n_fs)
    return [
        pltpu.SemaphoreType.DMA((chunks, count)),
        pltpu.SemaphoreType.DMA((chunks, count)),
        pltpu.SemaphoreType.DMA((chunks,)),
    ]


TILE = 512
STATES = 32
TAPS = 15
REACH = 8
EPSILON = 1e-05
CHUNK = 256
ROWS = 128
VMEM_LIMIT = 60 << 20
TAP_ROW = 24
RATE = 40
MAP_IN = 72
MAP_OUT = 104
TABLE = 136


def sigmoid(v):
    return 0.5 * jnp.tanh(0.5 * v) + 0.5


def dot_nn(a, b):
    return jnp.dot(a, b, preferred_element_type=F32)


def dot_nt(a, b):
    return lax.dot_general(a, b, (((1,), (1,)), ((), ())), preferred_element_type=F32)


def dot_tn(a, b):
    return lax.dot_general(a, b, (((0,), (0,)), ((), ())), preferred_element_type=F32)


def norm_parts(v):
    centered = v - jnp.mean(v, axis=-1, keepdims=True)
    inv = lax.rsqrt(jnp.mean(centered * centered, axis=-1, keepdims=True) + EPSILON)
    return centered * inv, inv


def norm_back(grad, e, inv, gain):
    d = grad * gain
    return (
        d - jnp.mean(d, axis=-1, keepdims=True) - e * jnp.mean(d * e, axis=-1, keepdims=True)
    ) * inv


def fold8(v):
    return jnp.sum(v.reshape((v.shape[0] // 8, 8, v.shape[1])), axis=0)


def by_rows(body, rows=TILE, step=ROWS):
    def run(at, _):
        body(pl.ds(pl.multiple_of(at * step, step), step))
        return 0

    lax.fori_loop(0, rows // step, run, 0)


def columns(at, width=CHUNK):
    return pl.ds(pl.multiple_of(at * width, width), width)


def fill_halo(padded, flags, tiles):
    pitch = TILE + 2 * REACH
    for at in range(tiles):
        base = at * pitch
        if at == 0:
            padded[:, base : base + REACH, :] = jnp.zeros_like(padded[:, base : base + REACH, :])
        if at == tiles - 1:
            end = base + REACH + TILE
            padded[:, end : end + REACH, :] = jnp.zeros_like(padded[:, end : end + REACH, :])
        else:
            keep = flags[at + 1]
            end = base + REACH + TILE
            padded[:, end : end + REACH, :] = (
                padded[:, base + pitch + REACH : base + pitch + 2 * REACH, :] * keep
            )
            padded[:, base + pitch : base + pitch + REACH, :] = (
                padded[:, end - REACH : end, :] * keep
            )


def taps_over(padded, table_ref, store, tiles, reverse, block=64):
    pitch = TILE + 2 * REACH
    per = TILE // block
    lanes = padded.shape[0]
    for lane in range(lanes):
        weights = [
            jnp.broadcast_to(
                table_ref[TAP_ROW + k : TAP_ROW + k + 1, lane * 128 : lane * 128 + 128], (block, 128)
            )
            for k in range(TAPS)
        ]

        def run(at, _):
            tile, inner = at // per, at % per
            base = tile * pitch + inner * block
            total = jnp.zeros((block, 128), F32)
            for k in range(TAPS):
                shift = REACH + (TAPS // 2 - k if reverse else k - TAPS // 2)
                total = total + weights[k] * padded[lane, pl.ds(base + shift, block), :]
            store(lane, tile * TILE + inner * block, base, total)
            return 0

        lax.fori_loop(0, tiles * per, run, 0)


def small_exp(v):
    return 1.0 + v * (1.0 + v * (0.5 + v * (1.0 / 6 + v * (1.0 / 24 + v * (1.0 / 120)))))


def small_expm1_over(v):
    return 1.0 + v * (
        0.5 + v * (1.0 / 6 + v * (1.0 / 24 + v * (1.0 / 120 + v * (1.0 / 720 + v * (1.0 / 5040)))))
    )


def state_terms(table_ref):
    log_decay = -jnp.exp(table_ref[RATE : RATE + STATES, :])
    root = jnp.sqrt(-2.0 * log_decay * small_expm1_over(2.0 * log_decay))
    maps_in = table_ref[MAP_IN : MAP_IN + STATES, :]
    maps_out = table_ref[MAP_OUT : MAP_OUT + STATES, :]
    return log_decay, small_exp(log_decay), root, maps_in, maps_out


def ref_rows(ref):
    return ref.reshape((ref.shape[0] * ref.shape[1], ref.shape[2]))


PIECE = 16
WIDTH = 512


def cols_of(ref, first, at):
    per = WIDTH // CHUNK
    part = ref[:, first + lax.div(at, per), :, columns(lax.rem(at, per))]
    return part.reshape((ref.shape[0] * PIECE, CHUNK))


def rows_of(ref, first, at):
    groups = WIDTH // (4 * PIECE)
    part = ref[pl.ds(at * groups, groups), first : first + 4]
    return part.reshape((WIDTH, WIDTH))


def bias_of(ref, layer, at):
    row = 8 * layer + 2 * at
    return jnp.concatenate([ref[pl.ds(row, 1), :], ref[pl.ds(row + 1, 1), :]], axis=1)


def square_of(ref, at):
    return ref[:, at].reshape((ref.shape[0] * PIECE, WIDTH))


def store_wide(out, first, acc):
    def run(group, _):
        rows = pl.ds(pl.multiple_of(group * PIECE, PIECE), PIECE)
        for k in range(acc.shape[1] // WIDTH):
            out[group, first + k] = acc[rows, k * WIDTH : k * WIDTH + WIDTH].astype(BF16)
        return 0

    lax.fori_loop(0, acc.shape[0] // PIECE, run, 0)


def store_tall(out, first, acc):
    def run(group, _):
        rows = pl.ds(pl.multiple_of(group * 4 * PIECE, 4 * PIECE), 4 * PIECE)
        out[group, first : first + 4] = acc[rows, :].astype(BF16).reshape((4, PIECE, WIDTH))
        return 0

    lax.fori_loop(0, acc.shape[0] // (4 * PIECE), run, 0)


def flat_groups(ref):
    count = 1
    for n in ref.shape[:-3]:
        count *= n
    return ref.reshape((count,) + ref.shape[-3:])


def carries(offsets_ref, counts_ref, tiles):
    out = []
    for tile in range(tiles):
        begins = jnp.int32(0)
        for slot in range(offsets_ref.shape[1]):
            here = (offsets_ref[0, slot] == tile * TILE) & (slot < counts_ref[0])
            begins = jnp.maximum(begins, here.astype(jnp.int32))
        out.append((1 - begins).astype(F32))
    return out


STRETCH = 16
SPREAD = PIECE * STATES


def same_channel(rows, width, per, first=0):
    shape = (rows, width)
    row = lax.rem(lax.broadcasted_iota(jnp.int32, shape, 0), PIECE)
    col = lax.broadcasted_iota(jnp.int32, shape, 1)
    if per == 1:
        return row == lax.rem(col, PIECE)
    return row == lax.div(col, per)


def split_low(v):
    high = v.astype(BF16)
    return high, (v - high.astype(F32)).astype(BF16)


def spread_states(part):
    rows = part.shape[0]
    state = lax.broadcasted_iota(jnp.int32, (STATES, SPREAD), 0)
    col = lax.broadcasted_iota(jnp.int32, (STATES, SPREAD), 1)
    pick_state = (state == lax.rem(col, STATES)).astype(F32).astype(BF16)
    wide = dot_nn(part, pick_state)
    wide = jnp.where(same_channel(rows, SPREAD, STATES), wide, 0.0)
    return jnp.sum(wide.reshape((rows // PIECE, PIECE, SPREAD)), axis=1)


def gather_states(wide):
    groups = wide.shape[0]
    full = jnp.broadcast_to(wide[:, None, :], (groups, PIECE, SPREAD)).reshape((groups * PIECE, SPREAD))
    full = jnp.where(same_channel(groups * PIECE, SPREAD, STATES), full, 0.0)
    state = lax.broadcasted_iota(jnp.int32, (SPREAD, 128), 1)
    row = lax.broadcasted_iota(jnp.int32, (SPREAD, 128), 0)
    pick_state = (state == lax.rem(row, STATES)).astype(F32).astype(BF16)
    high, low = split_low(full)
    return (dot_nn(high, pick_state) + dot_nn(low, pick_state)).T[:STATES, :]


def prepare_states(small, power, shifted, weight):
    groups = small.shape[0]
    entries = lambda first: small[:, :, first : first + STATES].reshape((groups * PIECE, STATES))
    log_decay = -jnp.exp(spread_states(entries(RATE)))
    root = jnp.sqrt(-2.0 * log_decay * small_expm1_over(2.0 * log_decay))
    both = spread_states(entries(MAP_IN)) * root * spread_states(entries(MAP_OUT))
    weight[...] = both
    col = lax.broadcasted_iota(jnp.int32, (SPREAD, 128), 1)
    row = lax.broadcasted_iota(jnp.int32, (SPREAD, 128), 0)
    add_states = (col == lax.div(row, STATES)).astype(F32).astype(BF16)
    power[0] = jnp.ones_like(both)
    decay = small_exp(log_decay)
    for m in range(1, STRETCH):
        power[m] = power[m - 1] * decay
    halves = []
    for half in range(2):
        total = jnp.zeros((groups, 128), F32)
        for k in range(8):
            high, low = split_low(power[half * 8 + k] * both)
            lag = dot_nn(high, add_states) + dot_nn(low, add_states)
            total = total + (pltpu.roll(lag, k * PIECE, 1) if k else lag)
        halves.append(total)
    blank = jnp.zeros((groups, 256), F32)
    padded = jnp.concatenate([blank] + halves, axis=1)
    for m in range(STRETCH):
        shifted[m] = pltpu.roll(padded, 512 - (m + 1) * PIECE, 1)[:, :256]


def group_weights(power, shifted, group, decay_w, lag_w):
    mask = same_channel(PIECE, SPREAD, STATES)
    lag_mask = same_channel(PIECE, 256, 1)
    for m in range(STRETCH):
        rows = slice(m * PIECE, m * PIECE + PIECE)
        line = jnp.broadcast_to(power[m, pl.ds(group, 1), :], (PIECE, SPREAD))
        decay_w[rows, :] = jnp.where(mask, line, 0.0).astype(BF16)
        line = jnp.broadcast_to(shifted[m, pl.ds(group, 1), :], (PIECE, 256))
        lag_w[rows, :] = jnp.where(lag_mask, line, 0.0).astype(BF16)


def swap_blocks(parts):
    col = lax.div(lax.broadcasted_iota(jnp.int32, parts[0].shape, 1), PIECE)
    parts = list(parts)
    for distance in (1, 2, 4):
        low = lax.rem(lax.div(col, distance), 2) == 0
        shift = distance * PIECE
        for a in range(8):
            if a & distance:
                continue
            first, second = parts[a], parts[a + distance]
            parts[a] = jnp.where(low, first, pltpu.roll(second, shift, 1))
            parts[a + distance] = jnp.where(low, pltpu.roll(first, 128 - shift, 1), second)
    return parts


SLAB = 32
TOGETHER = 4


def to_blocks(load, out, blocks, backward):
    for slab in range(blocks // SLAB):
        rows = slice(slab * SLAB, slab * SLAB + SLAB)
        for half in range(2):
            parts = []
            for k in range(8):
                frame = half * 8 + k
                frame = STRETCH - 1 - frame if backward else frame
                parts.append(load(slab * SLAB * STRETCH + frame))
            for group, part in enumerate(swap_blocks(parts)):
                out[group, rows, half * 128 : half * 128 + 128] = part.astype(out.dtype)


def from_blocks(store, ref, blocks, backward):
    for slab in range(blocks // SLAB):
        rows = slice(slab * SLAB, slab * SLAB + SLAB)
        for half in range(2):
            parts = [ref[group, rows, half * 128 : half * 128 + 128] for group in range(8)]
            for k, part in enumerate(swap_blocks(parts)):
                frame = half * 8 + k
                frame = STRETCH - 1 - frame if backward else frame
                store(slab * SLAB * STRETCH + frame, part)


def block_powers(decay):
    q2 = decay * decay
    q4 = q2 * q2
    q8 = q4 * q4
    one = q8 * q8
    two = one * one
    four = two * two
    return one, two, four


def row_powers(one, count=8):
    rows = [one]
    for _ in range(count - 1):
        rows.append(rows[-1] * one)
    return rows


def scan_blocks(source, into, decay, keeps, per, reverse):
    blocks, width = source.shape
    one, two, four = block_powers(decay)
    row = lax.broadcasted_iota(jnp.int32, (8, width), 0)
    if reverse:
        row = 7 - row
    factors = []
    for distance, power in ((1, one), (2, two), (4, four)):
        line = jnp.broadcast_to(power, (8, width))
        factors.append((8 - distance if reverse else distance, jnp.where(row >= distance, line, 0.0)))
    entering = jnp.ones((8, width), F32)
    for bit, power in ((1, one), (2, two), (4, four)):
        line = jnp.broadcast_to(power, (8, width))
        entering = jnp.where(lax.rem(lax.div(row, bit), 2) == 1, entering * line, entering)
    eight = jnp.broadcast_to(four * four, (8, width))
    carry = jnp.zeros((8, width), F32)
    tiles = blocks // 8
    for k in range(tiles):
        tile = tiles - 1 - k if reverse else k
        edge = (tile + 1) * 8 if reverse else tile * 8
        if k and edge % per == 0:
            carry = carry * keeps[edge // per]
        x = source[tile * 8 : tile * 8 + 8, :]
        for shift, factor in factors:
            x = x + factor * pltpu.roll(x, shift, 0)
        moved = pltpu.roll(x, 7 if reverse else 1, 0)
        into[tile * 8 : tile * 8 + 8, :] = jnp.where(row >= 1, moved, 0.0) + entering * carry
        end = x[0:1, :] if reverse else x[7:8, :]
        carry = jnp.broadcast_to(end, (8, width)) + eight * carry


def mix_forward(u_ref, y_ref, power, shifted, weight, keeps, ub_out, state_out, blk_in, blk_out, decay_w, lag_w, t_scr, h_scr):
    lanes, frames, _ = u_ref.shape
    blocks = frames // STRETCH
    count = decay_w.shape[0]
    several = range(count)

    def lane_tile(lane, _):
        to_blocks(lambda at: u_ref[lane, pl.ds(at, SLAB, stride=STRETCH), :], blk_in, blocks, True)

        def some_groups(k, _):
            place = [k * count + n for n in several]
            groups = [lane * 8 + at for at in place]
            for n in several:
                group_weights(power, shifted, groups[n], decay_w.at[n], lag_w.at[n])
            for n in several:
                ub_out[groups[n]] = blk_in[place[n]]
                t_scr[n] = dot_nn(blk_in[place[n]], decay_w[n])
            for n in several:
                decay = power[1, pl.ds(groups[n], 1), :]
                scan_blocks(t_scr.at[n], h_scr.at[n], decay, keeps, TILE // STRETCH, False)
            for n in several:
                decay = power[1, pl.ds(groups[n], 1), :]
                state = h_scr[n]
                state_out[groups[n]] = state.astype(BF16)
                out = (state * (weight[pl.ds(groups[n], 1), :] * decay)).astype(BF16)
                blk_out[place[n]] = dot_nn(blk_in[place[n]], lag_w[n]) + dot_nt(out, decay_w[n])
            return 0

        lax.fori_loop(0, 8 // count, some_groups, 0)

        def store(at, values):
            y_ref[lane, pl.ds(at, SLAB, stride=STRETCH), :] = values

        from_blocks(store, blk_out, blocks, False)
        return 0

    lax.fori_loop(0, lanes, lane_tile, 0)


def mix_backward(
    lane, u_ref, grad, skip, u_tile, u_sem, power, shifted, weight, keeps, ub_ref, state_ref, lags, sums,
    frames_scr, blk_in, blk_out, decay_w, lag_w, stack_scr, e_scr, r_scr,
):
    blocks = frames_scr.shape[2]
    count = decay_w.shape[0]
    several = range(count)
    lanes = u_ref.shape[0]
    copy = lambda at: pltpu.make_async_copy(u_ref.at[at], u_tile, u_sem)
    copy(lane).wait()
    for at in range(STRETCH):
        for slab in range(blocks // SLAB):
            rows = slice(slab * SLAB, slab * SLAB + SLAB)
            first = pl.ds(slab * SLAB * STRETCH + at, SLAB, stride=STRETCH)
            frames_scr[0, at, rows, :] = u_tile[first, :]
            frames_scr[1, at, rows, :] = grad[lane, first, :]

    @pl.when(lane + 1 < lanes)
    def _():
        copy(lane + 1).start()

    def one_lag(lag, _):
        def one_frame(at, total):
            for slab in range(blocks // SLAB):
                rows = slice(slab * SLAB, slab * SLAB + SLAB)
                total = total + frames_scr[1, at, rows, :] * frames_scr[0, at - lag, rows, :]
            return total

        total = lax.fori_loop(lag, STRETCH, one_frame, jnp.zeros((SLAB, 128), F32))
        lags[lane, pl.ds(lag, 1), :] = jnp.sum(total, axis=0, keepdims=True)
        return 0

    lax.fori_loop(0, STRETCH, one_lag, 0)
    for slab in range(blocks // SLAB):
        rows = slice(slab * SLAB, slab * SLAB + SLAB)
        for half in range(2):
            parts = [frames_scr[1, half * 8 + k, rows, :] for k in range(8)]
            for group, part in enumerate(swap_blocks(parts)):
                blk_in[group, rows, half * 128 : half * 128 + 128] = part.astype(BF16)
    position = lax.div(lax.broadcasted_iota(jnp.int32, (1, 256), 1), PIECE).astype(F32)

    def some_groups(k, _):
        place = [k * count + n for n in several]
        groups = [lane * 8 + at for at in place]
        for n in several:
            group_weights(power, shifted, groups[n], decay_w.at[n], lag_w.at[n])
        for n in several:
            gy = blk_in[place[n]]
            stack_scr[n, 0:blocks, :] = gy
            stack_scr[n, blocks : 2 * blocks, :] = (gy.astype(F32) * (position + 1.0)).astype(BF16)
            stack_scr[n, 2 * blocks :, :] = (ub_ref[groups[n]].astype(F32) * position).astype(BF16)
        for n in several:
            e_scr[n] = dot_nn(stack_scr[n], decay_w[n])
        for n in several:
            decay = power[1, pl.ds(groups[n], 1), :]
            own = e_scr.at[n, pl.ds(0, blocks)]
            own[...] = own[...] * decay
            scan_blocks(own, r_scr.at[n], decay, keeps, TILE // STRETCH, True)
        for n in several:
            group = groups[n]
            inverse = 1.0 / power[1, pl.ds(group, 1), :]
            last = 16.0 * power[15, pl.ds(group, 1), :]
            first, second = jnp.zeros((8, SPREAD), F32), jnp.zeros((8, SPREAD), F32)
            for at in range(blocks // 8):
                rows = slice(at * 8, at * 8 + 8)
                state = state_ref[group, rows, :].astype(F32)
                turn = e_scr[n, 2 * blocks + at * 8 : 2 * blocks + at * 8 + 8, :]
                first = first + state * e_scr[n, rows, :]
                second = second + state * e_scr[n, blocks + at * 8 : blocks + at * 8 + 8, :]
                second = second + r_scr[n, rows, :] * (turn * inverse + last * state)
            sums[0, pl.ds(group, 1), :] = jnp.sum(first, axis=0, keepdims=True)
            sums[1, pl.ds(group, 1), :] = jnp.sum(second, axis=0, keepdims=True)
            out = (r_scr[n] * weight[pl.ds(group, 1), :]).astype(BF16)
            blk_out[place[n]] = dot_nt(blk_in[place[n]], lag_w[n]) + dot_nt(out, decay_w[n])
        return 0

    lax.fori_loop(0, 8 // count, some_groups, 0)

    def store(at, values):
        slab, frame = at // (SLAB * STRETCH), at % STRETCH
        through = frames_scr[1, frame, slab * SLAB : slab * SLAB + SLAB, :]
        grad[lane, pl.ds(at, SLAB, stride=STRETCH), :] = values + skip[pl.ds(lane, 1), :] * through

    from_blocks(store, blk_out, blocks, True)


def mix_gradients(lags, sums, table_ref):
    _, decay, root, maps_in, maps_out = state_terms(table_ref)
    coupling = maps_in * root * maps_out
    gmap = gather_states(sums[0])
    gdecay = gather_states(sums[1])
    power = jnp.ones_like(decay)
    for lag in range(STRETCH):
        line = jnp.concatenate([lags[k, lag : lag + 1, :] for k in range(lags.shape[0])], axis=1)
        if lag:
            gdecay = gdecay + float(lag) * power * line
            power = power * decay
        gmap = gmap + power * line
    return gmap, gdecay * coupling


def pack_small(out, scr, place, bias_ref, gains, shifts, conv_bias, taps, rate, maps):
    own = gains.shape[1]
    scr[...] = jnp.zeros_like(scr)
    scr[0:6, :own] = gains[...].astype(F32)
    scr[6:18, :own] = shifts[...].astype(F32)
    scr[18:19, :own] = conv_bias[...].astype(F32)
    scr[TAP_ROW : TAP_ROW + TAPS, :own] = taps[...].astype(F32)
    out[:, :CHUNK] = scr[...].T[:own, :].astype(BF16)
    out[:, RATE:MAP_IN] = rate[...]
    out[:, MAP_IN:MAP_OUT] = maps[0]
    out[:, MAP_OUT:TABLE] = maps[1]
    count = bias_ref.shape[1]
    row = lax.div(place * count, CHUNK)
    inner = place * count - row * CHUNK
    at_row = lax.broadcasted_iota(jnp.int32, (PIECE, CHUNK), 0)
    wide = jnp.zeros((PIECE, CHUNK), F32)
    for layer in range(2):
        line = jnp.broadcast_to(bias_ref[layer : layer + 1, :].astype(F32), (8, count))
        line = jnp.concatenate([line, jnp.zeros((8, CHUNK - count), F32)], axis=1)
        line = pltpu.roll(line, inner, 1)
        wide = wide + jnp.where(at_row == 8 * layer + row, jnp.broadcast_to(line[0:1], wide.shape), 0.0)
    out[:, CHUNK:] = wide.astype(BF16)


def front_kernel(mesh_size, *refs):
    fused = mesh_size is not None
    refs = list(refs)
    take = lambda count: [refs.pop(0) for _ in range(count)]
    offsets_ref, counts_ref, x_ref = take(3)
    if fused:
        n_dp, n_fs = mesh_size
        small_in = take(7)
        up_s, down_s, mixin_s, mixout_s, convin_s, convout_s = take(6)
    else:
        first_v, second_v, third_v, table_in, bias_in = take(5)
    (
        h_out,
        x1_out,
        v_out,
        y_out,
        gated_out,
        x2_out,
        p_out,
        u_out,
        w_out,
        stat_out,
        table_ref,
        bias_ref,
        ub_out,
        state_out,
        power,
        shifted,
        weight,
    ) = take(17)
    gathered = take(4) if fused else []
    x1_scr, low_all, low_scr, sum_scr, y_all, padded = take(6)
    mix_scr = take(6)
    step = pl.program_id(0)
    channels = x_ref.shape[1]
    frames = w_out.shape[0]
    tiles = frames // TILE
    lanes = channels // 128
    gain = lambda k: table_ref[k : k + 1, :]
    shift = lambda k: table_ref[6 + k : 7 + k, :]
    here = lambda rows, tile: pl.ds(pl.multiple_of(tile * TILE + rows.start, ROWS), ROWS)
    flags = carries(offsets_ref, counts_ref, tiles)
    if fused:
        first_c, second_c, third_c = take(3)
        sources = take(4)
        turn_scr = refs.pop(0)
        sems = take(3)
        load_sem = refs.pop(0)
        swap = take(4)
        dp, fs = lax.axis_index("dp"), lax.axis_index("fsdp")
        place = Place(dp, fs, n_dp, n_fs)
        landing = [first_c, second_c, third_c, gathered[3]]
        plans, sends = block_gather(place, sources, landing, *sems)
        first_v, second_v, third_v = [flat_groups(r) for r in landing[:3]]

        def keep_copy(chunk):
            return pltpu.make_async_copy(landing[chunk], gathered[chunk], load_sem.at[chunk])

        def run(*stages):
            for chunk, stage in stages:
                plans[chunk][stage]()

        @pl.when(step == 0)
        def _():
            pack_small(sources[0].at[0], turn_scr, dp * n_fs + fs, *small_in)
            for k in range(4):
                cols = slice(k * WIDTH, k * WIDTH + WIDTH)
                sources[0][1 + k] = up_s[0, :, cols]
                sources[3][1 + k] = up_s[1, :, cols]
                rows = slice(k * PIECE, k * PIECE + PIECE)
                sources[1][k] = down_s[0, rows, :]
                sources[3][5 + k] = down_s[1, rows, :]
            for k in range(2):
                cols = slice(k * WIDTH, k * WIDTH + WIDTH)
                sources[2][k] = mixin_s[:, cols]
                sources[2][3 + k] = convin_s[:, cols]
            sources[2][2] = mixout_s[...]
            sources[3][0] = convout_s[...]
            greet(dp, fs, n_dp, n_fs)
            run((0, 0), (1, 0), (0, 1), (1, 1), (2, 0), (0, 2), (1, 2), (0, 3), (2, 1), (1, 3), (0, 4))
            table_ref[...] = first_v[:, 0, :, :CHUNK].reshape((channels, CHUNK)).astype(F32).T[:TABLE, :]
            total = first_v[0, 0, :, CHUNK:].astype(F32)
            for k in range(1, n_dp * n_fs):
                total = total + first_v[k, 0, :, CHUNK:].astype(F32)
            bias_ref[...] = total
            run((1, 4))

        rest = {1: [(2, 2), (3, 0)], 2: [(2, 3)], tiles: [(2, 4), (3, 1)]}
        rest.update({tiles + 1: [(3, 2)], tiles + 2: [(3, 3)], 2 * tiles + 1: [(3, 4)]})
        for at, stages in rest.items():

            @pl.when(step == at)
            def _(at=at, stages=stages):
                run(*stages)
                if at == tiles:
                    for chunk in range(3):
                        keep_copy(chunk).start()
                if at == 2 * tiles + 1:
                    for chunk in range(3):
                        keep_copy(chunk).wait()
                    for wait in sends:
                        wait()

    else:

        @pl.when(step == 0)
        def _():
            table_ref[...] = table_in[...]
            bias_ref[...] = bias_in[...]

    @pl.when(step < tiles)
    def _():
        def first(rows):
            e, _ = norm_parts(x_ref[rows, :].astype(F32))
            low_scr[rows, :] = (e * gain(0) + shift(0)).astype(BF16)
            sum_scr[rows, :] = jnp.zeros((ROWS, channels), F32)

        by_rows(first)

        def hidden(c, _):
            cols = columns(c, WIDTH)
            h = dot_nn(low_scr[...], square_of(first_v, 1 + c)) + bias_of(bias_ref, 0, c)
            h_out[:, cols] = h.astype(BF16)
            active = (h * sigmoid(h)).astype(BF16)
            sum_scr[...] += dot_nn(active, rows_of(second_v, 0, c))
            return 0

        lax.fori_loop(0, h_out.shape[1] // WIDTH, hidden, 0)

        def second(rows):
            x1 = x_ref[rows, :].astype(F32) + 0.5 * (sum_scr[rows, :] + shift(6))
            x1_out[rows, :] = x1
            x1_scr[here(rows, step), :] = x1
            e, _ = norm_parts(x1)
            low_all[here(rows, step), :] = (e * gain(1) + shift(1)).astype(BF16)

        by_rows(second)

    @pl.when(step == tiles)
    def _():
        prepare_states(first_v[:, 0, :, :CHUNK], power, shifted, weight)

        def project(tile, _):
            rows = pl.ds(pl.multiple_of(tile * TILE, TILE), TILE)
            u = dot_nn(low_all[rows, :], square_of(third_v, 0))
            for lane in range(lanes):
                u_out[lane, rows, :] = u[:, lane * 128 : lane * 128 + 128]
            return 0

        lax.fori_loop(0, tiles, project, 0)
        mix_forward(u_out, y_all, power, shifted, weight, flags, ub_out, state_out, *mix_scr)

    @pl.when((step > tiles) & (step <= 2 * tiles))
    def _():
        at = step - tiles - 1
        whole_tile = pl.ds(pl.multiple_of(at * TILE, TILE), TILE)
        v_out[...] = dot_nn(low_all[whole_tile, :], square_of(third_v, 1)).astype(BF16)

        def gate(rows):
            join = lambda ref: jnp.concatenate([ref[lane, here(rows, at), :] for lane in range(lanes)], axis=1)
            y = join(y_all) + shift(11) * join(u_out)
            v = v_out[rows, :].astype(F32)
            y_out[rows, :] = y.astype(BF16)
            gated_out[rows, :] = (y * (v * sigmoid(v))).astype(BF16)

        by_rows(gate)
        sum_scr[...] = dot_nn(gated_out[...], square_of(third_v, 2))

        def third(rows):
            x2 = x1_scr[here(rows, at), :] + (sum_scr[rows, :] + shift(8))
            x2_out[rows, :] = x2
            e, _ = norm_parts(x2)
            low_scr[rows, :] = (e * gain(2) + shift(2)).astype(BF16)

        by_rows(third)
        pitch = TILE + 2 * REACH

        def widen(c, _):
            cols = columns(c)
            right = columns(c + channels // CHUNK)
            left_part = dot_nn(low_scr[...], cols_of(third_v, 3, c)) + table_ref[15:16, cols]
            right_part = dot_nn(low_scr[...], cols_of(third_v, 4, c)) + table_ref[16:17, cols]
            p_out[:, cols] = left_part.astype(BF16)
            p_out[:, right] = right_part.astype(BF16)
            g = left_part * sigmoid(right_part)
            place = pl.ds(pl.multiple_of(at * pitch + REACH, 8), TILE)
            for k in range(CHUNK // 128):
                padded[c * (CHUNK // 128) + k, place, :] = g[:, k * 128 : k * 128 + 128]
            return 0

        lax.fori_loop(0, channels // CHUNK, widen, 0)

    @pl.when(step == 2 * tiles + 1)
    def _():
        fill_halo(padded, flags, tiles)

        def store(lane, row, base, total):
            w_out[pl.ds(pl.multiple_of(row, 64), 64), lane * 128 : lane * 128 + 128] = total

        taps_over(padded, table_ref, store, tiles, False)
        stat_out[...] = jnp.zeros_like(stat_out)

        def total(at, _):
            rows = pl.ds(pl.multiple_of(at * ROWS, ROWS), ROWS)
            stat_out[...] += fold8(w_out[rows, :])
            return 0

        lax.fori_loop(0, frames // ROWS, total, 0)
        center = jnp.sum(stat_out[...], axis=0, keepdims=True) * (1.0 / frames)
        stat_out[...] = jnp.zeros_like(stat_out)

        def spread(at, _):
            rows = pl.ds(pl.multiple_of(at * ROWS, ROWS), ROWS)
            off = w_out[rows, :] - center
            stat_out[...] += fold8(off * off)
            return 0

        lax.fori_loop(0, frames // ROWS, spread, 0)
        around = jnp.sum(stat_out[...], axis=0, keepdims=True)
        if fused:
            center, around = pool_over(center, around, frames, dp, fs, n_dp, n_fs, *swap)
            around = lax.rsqrt(around * (1.0 / (frames * n_dp * n_fs)) + EPSILON)
        stat_out[...] = jnp.zeros_like(stat_out)
        stat_out[0:1, :] = center
        stat_out[1:2, :] = around


def whole(shape):
    zeros = (0,) * len(shape)
    return pl.BlockSpec(shape, lambda *_: zeros, pipeline_mode=pl.Buffered(1))


def params(collective_id=None):
    if collective_id is None:
        return pltpu.CompilerParams(
            dimension_semantics=("arbitrary",), vmem_limit_bytes=VMEM_LIMIT
        )
    return pltpu.CompilerParams(
        dimension_semantics=("arbitrary",),
        vmem_limit_bytes=VMEM_LIMIT,
        collective_id=collective_id,
        has_side_effects=True,
    )


SMEM_SPEC = pl.BlockSpec(memory_space=pltpu.SMEM)
HBM_SPEC = pl.BlockSpec(memory_space=pltpu.HBM)


def front(mesh_size, offsets, counts, x, small, weights, hidden, collective_id=None):
    fused = mesh_size is not None
    frames, channels = x.shape
    tiles = frames // TILE
    early = lambda width: pl.BlockSpec((TILE, width), lambda i: (jnp.minimum(i, tiles - 1), 0))
    place = lambda i: jnp.clip(i - tiles - 1, 0, tiles - 1)
    late = lambda width: pl.BlockSpec((TILE, width), lambda i: (place(i), 0))
    shape = lambda width, kind: jax.ShapeDtypeStruct((frames, width), kind)
    groups, blocks = channels // PIECE, frames // STRETCH
    out_shape = [
        shape(hidden, BF16),
        shape(channels, F32),
        shape(channels, BF16),
        shape(channels, BF16),
        shape(channels, BF16),
        shape(channels, F32),
        shape(2 * channels, BF16),
        jax.ShapeDtypeStruct((channels // 128, frames, 128), F32),
        shape(channels, F32),
        jax.ShapeDtypeStruct((8, channels), F32),
        jax.ShapeDtypeStruct((TABLE, channels), F32),
        jax.ShapeDtypeStruct((16, CHUNK), F32),
        jax.ShapeDtypeStruct((groups, blocks, STRETCH * PIECE), BF16),
        jax.ShapeDtypeStruct((groups, blocks, SPREAD), BF16),
        jax.ShapeDtypeStruct((STRETCH, groups, SPREAD), F32),
        jax.ShapeDtypeStruct((STRETCH, groups, STRETCH * PIECE), F32),
        jax.ShapeDtypeStruct((groups, SPREAD), F32),
    ]
    out_specs = [early(hidden), early(channels)] + [late(channels)] * 4 + [late(2 * channels)]
    out_specs += [whole(s.shape) for s in out_shape[7:]]
    scratch = [
        pltpu.VMEM((frames, channels), F32),
        pltpu.VMEM((frames, channels), BF16),
        pltpu.VMEM((TILE, channels), BF16),
        pltpu.VMEM((TILE, channels), F32),
        pltpu.VMEM((channels // 128, frames, 128), F32),
        pltpu.VMEM((channels // 128, tiles * (TILE + 2 * REACH), 128), F32),
        pltpu.VMEM((8, blocks, STRETCH * PIECE), BF16),
        pltpu.VMEM((8, blocks, STRETCH * PIECE), F32),
        pltpu.VMEM((TOGETHER, STRETCH * PIECE, SPREAD), BF16),
        pltpu.VMEM((TOGETHER, STRETCH * PIECE, STRETCH * PIECE), BF16),
        pltpu.VMEM((TOGETHER, blocks, SPREAD), F32),
        pltpu.VMEM((TOGETHER, blocks, SPREAD), F32),
    ]
    operands = (weights if not fused else small + weights) + (small if not fused else [])
    if fused:
        layout = block_layout(*mesh_size)
        blocks = (5, 4, 5, 9)
        chunks = [jax.ShapeDtypeStruct(layout + (k, PIECE, WIDTH), BF16) for k in blocks]
        out_shape += chunks
        out_specs += [HBM_SPEC] * len(chunks)
        scratch += [pltpu.VMEM(c.shape, BF16) for c in chunks[:3]]
        scratch += [pltpu.VMEM((k, PIECE, WIDTH), BF16) for k in blocks]
        scratch += [pltpu.VMEM((CHUNK, 128), F32)]
        scratch += block_sems(*mesh_size, len(chunks)) + [pltpu.SemaphoreType.DMA((3,))]
        scratch += swap_scratch(*mesh_size, channels)
    return pl.pallas_call(
        partial(front_kernel, mesh_size),
        grid=(2 * tiles + 2,),
        in_specs=[SMEM_SPEC, SMEM_SPEC, early(channels)] + [whole(a.shape) for a in operands],
        out_specs=out_specs,
        out_shape=out_shape,
        scratch_shapes=scratch,
        compiler_params=params(collective_id),
        name="front",
    )(offsets, counts, x, *operands)


def middle_kernel(
    mesh_size,
    x2_ref,
    w_ref,
    cot_ref,
    blocks_ref,
    bias_ref,
    vec_ref,
    stat_ref,
    out_ref,
    gx3_ref,
    gnb_ref,
    gblocks_out,
    gbias_out,
    gvec_out,
    stat_out,
    up_acc,
    down_acc,
    convout_acc,
    bias_acc,
    vec_acc,
    h_scr,
    low_scr,
    turn_scr,
    act_scr,
    grad_scr,
    sum_scr,
    x3_scr,
    *swap,
):
    at = pl.program_id(0)
    tiles = pl.num_programs(0)
    channels = x2_ref.shape[1]
    if mesh_size is not None:
        n_dp, n_fs = mesh_size
        dp, fs = lax.axis_index("dp"), lax.axis_index("fsdp")

        @pl.when(at == 0)
        def _():
            greet(dp, fs, n_dp, n_fs)

    hidden = up_acc.shape[1]
    gain = lambda k: vec_ref[k : k + 1, :]
    shift = lambda k: vec_ref[6 + k : 7 + k, :]
    center, scale = stat_ref[0:1, :], stat_ref[1:2, :]

    @pl.when(at == 0)
    def _():
        for ref in (up_acc, down_acc, convout_acc, bias_acc, vec_acc):
            ref[...] = jnp.zeros_like(ref)

    def normed(rows):
        e = (w_ref[rows, :] - center) * scale
        return e, e * gain(5) + shift(5)

    def first(rows):
        _, nb = normed(rows)
        act_scr[rows, :] = (nb * sigmoid(nb)).astype(BF16)

    by_rows(first)
    sum_scr[...] = dot_nn(act_scr[...], square_of(blocks_ref, 0))

    def second(rows):
        x3 = x2_ref[rows, :] + (sum_scr[rows, :] + vec_ref[18:19, :])
        x3_scr[rows, :] = x3
        e, _ = norm_parts(x3)
        low_scr[rows, :] = (e * gain(3) + shift(3)).astype(BF16)
        sum_scr[rows, :] = jnp.zeros((ROWS, channels), F32)

    by_rows(second)

    def forward(c, _):
        cols = columns(c, WIDTH)
        h = dot_nn(low_scr[...], square_of(blocks_ref, 1 + c)) + bias_of(bias_ref, 1, c)
        h_scr[:, cols] = h
        active = (h * sigmoid(h)).astype(BF16)
        sum_scr[...] += dot_nn(active, rows_of(blocks_ref, 5, c))
        return 0

    lax.fori_loop(0, hidden // WIDTH, forward, 0)
    turn_scr[...] = low_scr[...].T

    def last(rows):
        x4 = x3_scr[rows, :] + 0.5 * (sum_scr[rows, :] + shift(7))
        e, inv = norm_parts(x4)
        out_ref[rows, :] = (e * gain(4) + shift(4)).astype(BF16)
        cot = cot_ref[rows, :].astype(F32)
        vec_acc[0] += fold8(cot * e)
        vec_acc[1] += fold8(cot)
        gx4 = norm_back(cot, e, inv, gain(4))
        gx3_ref[rows, :] = gx4
        low = (0.5 * gx4).astype(BF16)
        grad_scr[rows, :] = low
        vec_acc[2] += fold8(low.astype(F32))
        sum_scr[rows, :] = jnp.zeros((ROWS, channels), F32)

    by_rows(last)

    def backward(c, _):
        cols = columns(c, WIDTH)
        h = h_scr[:, cols]
        sig = sigmoid(h)
        active = h * sig
        gate = dot_nt(grad_scr[...], rows_of(blocks_ref, 5, c))
        grad_h = (gate * (sig * (1.0 + h - active))).astype(BF16)
        bias_acc[:, cols] += fold8(grad_h.astype(F32))
        down_acc[cols, :] += dot_tn(active.astype(BF16), grad_scr[...])
        up_acc[:, cols] += dot_nn(turn_scr[...], grad_h)
        sum_scr[...] += dot_nt(grad_h, square_of(blocks_ref, 1 + c))
        return 0

    lax.fori_loop(0, hidden // WIDTH, backward, 0)

    def fourth(rows):
        e, inv = norm_parts(x3_scr[rows, :])
        grad = sum_scr[rows, :]
        vec_acc[3] += fold8(grad * e)
        vec_acc[4] += fold8(grad)
        gx3 = gx3_ref[rows, :] + norm_back(grad, e, inv, gain(3))
        gx3_ref[rows, :] = gx3
        low = gx3.astype(BF16)
        grad_scr[rows, :] = low
        vec_acc[5] += fold8(low.astype(F32))

    by_rows(fourth)
    convout_acc[...] += dot_tn(act_scr[...], grad_scr[...])
    sum_scr[...] = dot_nt(grad_scr[...], square_of(blocks_ref, 0))

    def fifth(rows):
        e, nb = normed(rows)
        sig = sigmoid(nb)
        gnb = sum_scr[rows, :] * (sig * (1.0 + nb * (1.0 - sig)))
        gnb_ref[rows, :] = gnb
        vec_acc[6] += fold8(gnb * e)
        vec_acc[7] += fold8(gnb)

    by_rows(fifth)

    @pl.when(at == tiles - 1)
    def _():
        for k in range(8):
            gvec_out[k : k + 1, :] = jnp.sum(vec_acc[k], axis=0, keepdims=True)

        def convert():
            store_wide(gblocks_out, 0, convout_acc)
            store_wide(gblocks_out, 1, up_acc)
            store_tall(gblocks_out, 5, down_acc)
            gbias_out[...] = jnp.broadcast_to(
                jnp.sum(bias_acc[...], axis=0, keepdims=True), gbias_out.shape
            )

        stat_out[...] = stat_ref[...]
        if mesh_size is None:
            convert()
        else:
            total = sum_over(gvec_out[...], dp, fs, n_dp, n_fs, *swap, between=convert)
            share = gain(5) * (1.0 / (TILE * tiles * n_dp * n_fs))
            stat_out[2:3, :] = total[7:8, :] * share
            stat_out[3:4, :] = total[6:7, :] * share


def middle(mesh_size, x2, w, cot, blocks, bias, vec, stat, hidden, collective_id=None):
    frames, channels = x2.shape
    tiles = frames // TILE
    row = lambda width: pl.BlockSpec((TILE, width), lambda i: (i, 0))
    shapes = [
        jax.ShapeDtypeStruct((frames, channels), BF16),
        jax.ShapeDtypeStruct((frames, channels), F32),
        jax.ShapeDtypeStruct((frames, channels), F32),
        jax.ShapeDtypeStruct(blocks.shape, BF16),
        jax.ShapeDtypeStruct((8, hidden), F32),
        jax.ShapeDtypeStruct((8, channels), F32),
        jax.ShapeDtypeStruct((8, channels), F32),
    ]
    swap = [] if mesh_size is None else swap_scratch(*mesh_size, channels)
    return pl.pallas_call(
        partial(middle_kernel, mesh_size),
        grid=(tiles,),
        in_specs=[row(channels)] * 3
        + [whole(a.shape) for a in (blocks, bias, vec, stat)],
        out_specs=[row(channels)] * 3 + [whole(s.shape) for s in shapes[3:]],
        out_shape=shapes,
        scratch_shapes=[
            pltpu.VMEM((channels, hidden), F32),
            pltpu.VMEM((hidden, channels), F32),
            pltpu.VMEM((channels, channels), F32),
            pltpu.VMEM((8, hidden), F32),
            pltpu.VMEM((8, 8, channels), F32),
            pltpu.VMEM((TILE, hidden), F32),
            pltpu.VMEM((TILE, channels), BF16),
            pltpu.VMEM((channels, TILE), BF16),
            pltpu.VMEM((TILE, channels), BF16),
            pltpu.VMEM((TILE, channels), BF16),
            pltpu.VMEM((TILE, channels), F32),
            pltpu.VMEM((TILE, channels), F32),
        ]
        + swap,
        compiler_params=params(collective_id),
        name="middle",
    )(x2, w, cot, blocks, bias, vec, stat)


def back_kernel(mesh_size, *refs):
    fused = mesh_size is not None
    refs = list(refs)
    take = lambda count: [refs.pop(0) for _ in range(count)]
    offsets_ref, counts_ref, w_ref, gnb_ref, p_ref = take(5)
    x2_ref, gx3_ref, gated_ref, y_ref, v_ref, x1_ref = take(6)
    u_ref, ub_ref, state_ref, power, shifted, weight, blocks_ref, vec_ref, stat_ref = take(9)
    sources = take(1) if fused else []
    gx1_ref, gin_out, gvec_out, gtaps_ref, gmap_out, gdecay_out = take(6)
    reduced = take(2) if fused else []
    mid_ref = None if fused else refs.pop(0)
    wide_acc, mixout_acc, vec_acc, low_scr, wide_scr, sum_scr = take(6)
    padded, gpad, gv_all, lags, sums, skip, u_tile, u_sem = take(8)
    mix_scr = take(8)
    step = pl.program_id(0)
    channels = x2_ref.shape[1]
    frames = u_ref.shape[1]
    tiles = frames // TILE
    lanes = channels // 128
    pitch = TILE + 2 * REACH
    conv_at, mix_at = tiles, 2 * tiles + 1
    last_step = 3 * tiles + 1
    gain = lambda k: vec_ref[k : k + 1, :]
    shift = lambda k: vec_ref[6 + k : 7 + k, :]
    left, right = slice(0, channels), slice(channels, 2 * channels)
    flags = carries(offsets_ref, counts_ref, tiles)
    schedule = {}
    if fused:
        n_dp, n_fs = mesh_size
        place = Place(lax.axis_index("dp"), lax.axis_index("fsdp"), n_dp, n_fs)
        mid_src = refs.pop(0)
        mid_ref = flat_groups(mid_src)
        scratch = take(2 * (2 + place.count))

        def emit(chunk, total):
            reduced[chunk][...] = total

        plans, sends = block_scatter(place, sources + [mid_src], emit, scratch, *take(3))
        first = [(0, 0), (conv_at, 1), (conv_at + 2, 0), (conv_at + 3, 0), (mix_at, 1)]
        second = [(mix_at, 0), (mix_at, 1), (mix_at + 1, 0), (mix_at + 2, 0), (last_step, 1)]
        for chunk, points in enumerate((first, second)):
            for stage, point in enumerate(points):
                schedule.setdefault(point, []).append((stage, chunk))

    def progress(at, part):
        for stage, chunk in sorted(schedule.get((at, part), [])):
            plans[chunk][stage]()

    @pl.when(step == 0)
    def _():
        for ref in (wide_acc, mixout_acc, vec_acc):
            ref[...] = jnp.zeros_like(ref)
        if fused:
            greet(place.dp, place.fs, n_dp, n_fs)

    for at in sorted({key[0] for key in schedule if key[1] == 0 and key[0] != mix_at}):

        @pl.when(step == at)
        def _(at=at):
            progress(at, 0)

    @pl.when(step < tiles)
    def _():
        center, scale = stat_ref[0:1, :], stat_ref[1:2, :]
        plain, cross = stat_ref[2:3, :], stat_ref[3:4, :]

        def fill(index, _):
            rows = pl.ds(pl.multiple_of(index * 64, 64), 64)
            spot = pl.ds(pl.multiple_of(step * pitch + REACH + index * 64, 8), 64)
            e = (w_ref[rows, :] - center) * scale
            d = gnb_ref[rows, :] * gain(5)
            gw = scale * (d - plain - e * cross)
            g = p_ref[rows, left].astype(F32) * sigmoid(p_ref[rows, right].astype(F32))
            for lane in range(lanes):
                cols = slice(lane * 128, lane * 128 + 128)
                padded[lane, spot, :] = gw[:, cols]
                gpad[lane, spot, :] = g[:, cols]
            return 0

        lax.fori_loop(0, TILE // 64, fill, 0)

    @pl.when(step == conv_at)
    def _():
        fill_halo(padded, flags, tiles)
        fill_halo(gpad, flags, tiles)
        block = 64
        per = TILE // block
        gtaps_ref[...] = jnp.zeros_like(gtaps_ref)
        for lane in range(lanes):

            def corr(index, sums, lane=lane):
                base = (index // per) * pitch + (index % per) * block
                here = padded[lane, pl.ds(pl.multiple_of(base + REACH, 8), block), :]
                return tuple(
                    s + fold8(here * gpad[lane, pl.ds(base + REACH + k - TAPS // 2, block), :])
                    for k, s in enumerate(sums)
                )

            found = lax.fori_loop(0, tiles * per, corr, (jnp.zeros((8, 128), F32),) * TAPS)
            for k in range(TAPS):
                gtaps_ref[k : k + 1, lane * 128 : lane * 128 + 128] = jnp.sum(
                    found[k], axis=0, keepdims=True
                )
        progress(conv_at, 1)

        def store(lane, row, base, total):
            gpad[lane, pl.ds(pl.multiple_of(base + REACH, 8), 64), :] = total

        taps_over(padded, vec_ref, store, tiles, True)

    @pl.when((step > conv_at) & (step < mix_at))
    def _():
        at = step - conv_at - 1

        def first(rows):
            spot = pl.ds(pl.multiple_of(at * pitch + REACH + rows.start, 8), ROWS)
            grad = jnp.concatenate([gpad[lane, spot, :] for lane in range(lanes)], axis=1)
            sig = sigmoid(p_ref[rows, right].astype(F32))
            gl = (grad * sig).astype(BF16)
            gr = (grad * p_ref[rows, left].astype(F32) * (sig * (1.0 - sig))).astype(BF16)
            wide_scr[rows, left] = gl
            wide_scr[rows, right] = gr
            vec_acc[0] += fold8(gl.astype(F32))
            vec_acc[1] += fold8(gr.astype(F32))
            e, _ = norm_parts(x2_ref[rows, :])
            low_scr[rows, :] = (e * gain(2) + shift(2)).astype(BF16)

        by_rows(first)
        turned = low_scr[...].T
        wide_acc[...] += dot_nn(turned, wide_scr[...])
        sum_scr[...] = dot_nt(wide_scr[:, left], square_of(blocks_ref, 3)) + dot_nt(
            wide_scr[:, right], square_of(blocks_ref, 4)
        )

        def second(rows):
            here = pl.ds(pl.multiple_of(at * TILE + rows.start, ROWS), ROWS)
            e, inv = norm_parts(x2_ref[rows, :])
            grad = sum_scr[rows, :]
            vec_acc[2] += fold8(grad * e)
            vec_acc[3] += fold8(grad)
            gx2 = gx3_ref[rows, :] + norm_back(grad, e, inv, gain(2))
            spot = pl.ds(pl.multiple_of(at * pitch + REACH + rows.start, 8), ROWS)
            for lane in range(lanes):
                gpad[lane, spot, :] = gx2[:, lane * 128 : lane * 128 + 128]
            low = gx2.astype(BF16)
            low_scr[rows, :] = low
            vec_acc[4] += fold8(low.astype(F32))

        by_rows(second)
        mixout_acc[...] += dot_tn(gated_ref[...], low_scr[...])
        sum_scr[...] = dot_nt(low_scr[...], square_of(blocks_ref, 2))

        def third(rows):
            here = pl.ds(pl.multiple_of(at * TILE + rows.start, ROWS), ROWS)
            grad = sum_scr[rows, :]
            v = v_ref[rows, :].astype(F32)
            sig = sigmoid(v)
            swish = v * sig
            gy = grad * swish
            for lane in range(lanes):
                padded[lane, here, :] = gy[:, lane * 128 : lane * 128 + 128]
            gv_all[here, :] = (
                grad * y_ref[rows, :].astype(F32) * (sig * (1.0 + v - swish))
            ).astype(BF16)


        by_rows(third)

    @pl.when(step == mix_at)
    def _():
        pltpu.make_async_copy(u_ref.at[0], u_tile, u_sem).start()
        store_wide(mid_ref, 0, mixout_acc)
        store_wide(mid_ref, 1, wide_acc)
        wide_acc[...] = jnp.zeros_like(wide_acc)
        for lane in range(lanes):
            skip[lane : lane + 1, :] = vec_ref[17:18, lane * 128 : lane * 128 + 128]
        progress(mix_at, 0)

        def one(lane, _):
            mix_backward(
                lane, u_ref, padded, skip, u_tile, u_sem, power, shifted, weight, flags, ub_ref, state_ref, lags, sums, *mix_scr
            )
            return 0

        lax.fori_loop(0, lanes // 2, one, 0)
        progress(mix_at, 1)
        lax.fori_loop(lanes // 2, lanes, one, 0)
        gmap, gdecay = mix_gradients(lags, sums, vec_ref)
        gmap_out[...] = gmap
        gdecay_out[...] = gdecay

    @pl.when(step > mix_at)
    def _():
        at = step - mix_at - 1

        def fourth(rows):
            here = pl.ds(pl.multiple_of(at * TILE + rows.start, ROWS), ROWS)
            gu = jnp.concatenate([padded[lane, here, :] for lane in range(lanes)], axis=1)
            wide_scr[rows, left] = gu.astype(BF16)
            wide_scr[rows, right] = gv_all[here, :]
            e, _ = norm_parts(x1_ref[rows, :])
            low_scr[rows, :] = (e * gain(1) + shift(1)).astype(BF16)

        by_rows(fourth)
        turned = low_scr[...].T
        wide_acc[...] += dot_nn(turned, wide_scr[...])
        sum_scr[...] = dot_nt(wide_scr[:, left], square_of(blocks_ref, 0)) + dot_nt(
            wide_scr[:, right], square_of(blocks_ref, 1)
        )

        def fifth(rows):
            e, inv = norm_parts(x1_ref[rows, :])
            grad = sum_scr[rows, :]
            vec_acc[6] += fold8(grad * e)
            vec_acc[7] += fold8(grad)
            spot = pl.ds(pl.multiple_of(at * pitch + REACH + rows.start, 8), ROWS)
            gx2 = jnp.concatenate([gpad[lane, spot, :] for lane in range(lanes)], axis=1)
            gx1_ref[rows, :] = gx2 + norm_back(grad, e, inv, gain(1))

        by_rows(fifth)

    @pl.when(step == last_step)
    def _():
        store_wide(gin_out, 0, wide_acc)
        for k in range(8):
            gvec_out[k : k + 1, :] = jnp.sum(vec_acc[k], axis=0, keepdims=True)
        gvec_out[5:6, :] = jnp.concatenate([lags[k, 0:1, :] for k in range(lanes)], axis=1)
        if fused:
            progress(last_step, 1)
            for wait in sends:
                wait()


def back(mesh_size, offsets, counts, tiled, wholes, grads=(), collective_id=None):
    fused = mesh_size is not None
    frames, channels = tiled[0].shape
    tiles = frames // TILE
    groups, blocks = channels // PIECE, frames // STRETCH
    late = lambda i, first: jnp.clip(i - first, 0, tiles - 1)
    filling = lambda i: (late(i, 0), 0)
    twice = lambda i: (jnp.where(i < tiles, i, late(i, tiles + 1)), 0)
    mixing = lambda i: (late(i, tiles + 1), 0)
    ending = lambda i: (late(i, 2 * tiles + 2), 0)
    maps = [filling, filling, twice] + [mixing] * 5 + [ending]
    state = jax.ShapeDtypeStruct((STATES, channels), F32)
    bf16 = lambda *shape: jax.ShapeDtypeStruct(shape, BF16)
    shapes = [
        jax.ShapeDtypeStruct((frames, channels), F32),
        bf16(groups, 2, PIECE, WIDTH),
        jax.ShapeDtypeStruct((8, channels), F32),
        jax.ShapeDtypeStruct((16, channels), F32),
        state,
        state,
    ]
    pad = pltpu.VMEM((channels // 128, tiles * (TILE + 2 * REACH), 128), F32)
    scratch = [
        pltpu.VMEM((channels, 2 * channels), F32),
        pltpu.VMEM((channels, channels), F32),
        pltpu.VMEM((8, 8, channels), F32),
        pltpu.VMEM((TILE, channels), BF16),
        pltpu.VMEM((TILE, 2 * channels), BF16),
        pltpu.VMEM((TILE, channels), F32),
        pad,
        pad,
        pltpu.VMEM((frames, channels), BF16),
        pltpu.VMEM((channels // 128, STRETCH, 128), F32),
        pltpu.VMEM((2, groups, SPREAD), F32),
        pltpu.VMEM((8, 128), F32),
        pltpu.VMEM((frames, 128), F32),
        pltpu.SemaphoreType.DMA(()),
        pltpu.VMEM((2, STRETCH, blocks, 128), F32),
        pltpu.VMEM((8, blocks, STRETCH * PIECE), BF16),
        pltpu.VMEM((8, blocks, STRETCH * PIECE), F32),
        pltpu.VMEM((2, STRETCH * PIECE, SPREAD), BF16),
        pltpu.VMEM((2, STRETCH * PIECE, STRETCH * PIECE), BF16),
        pltpu.VMEM((2, 3 * blocks, STRETCH * PIECE), BF16),
        pltpu.VMEM((2, 3 * blocks, SPREAD), F32),
        pltpu.VMEM((2, blocks, SPREAD), F32),
    ]
    if fused:
        counts_of = [grads[0].shape[-3], 3]
        shapes += [jax.ShapeDtypeStruct((k, PIECE, WIDTH), F32) for k in counts_of]
        scratch += [pltpu.VMEM(block_layout(*mesh_size) + (3, PIECE, WIDTH), BF16)]
        scratch += block_scratch(*mesh_size, counts_of, (PIECE, WIDTH))
        scratch += block_sems(*mesh_size, 2)
    else:
        shapes.append(bf16(groups, 3, PIECE, WIDTH))
    return pl.pallas_call(
        partial(back_kernel, mesh_size),
        grid=(3 * tiles + 2,),
        in_specs=[SMEM_SPEC, SMEM_SPEC]
        + [pl.BlockSpec((TILE, a.shape[1]), index) for a, index in zip(tiled, maps)]
        + [HBM_SPEC]
        + [whole(a.shape) for a in wholes[1:]]
        + [HBM_SPEC] * len(grads),
        out_specs=[pl.BlockSpec((TILE, channels), ending)] + [whole(s.shape) for s in shapes[1:]],
        out_shape=shapes,
        scratch_shapes=scratch,
        compiler_params=params(collective_id),
        name="back",
    )(offsets, counts, *tiled, *wholes, *grads)


def small_gradients(out, gvec1, gvec2, gvec3, gtaps, gmap, gdecay, table_ref):
    out[...] = jnp.zeros_like(out)
    gains = {1: (gvec2, 6), 2: (gvec2, 2), 3: (gvec1, 3), 4: (gvec1, 0), 5: (gvec1, 6)}
    shifts = {1: (gvec2, 7), 2: (gvec2, 3), 3: (gvec1, 4), 4: (gvec1, 1), 5: (gvec1, 7)}
    shifts.update({6: (gvec3, 0), 7: (gvec1, 2), 8: (gvec2, 4), 9: (gvec2, 0), 10: (gvec2, 1)})
    shifts.update({11: (gvec2, 5), 12: (gvec1, 5)})
    for at, (ref, row) in gains.items():
        out[at : at + 1, :] = ref[row : row + 1, :]
    for at, (ref, row) in shifts.items():
        out[6 + at : 7 + at, :] = ref[row : row + 1, :]
    out[TAP_ROW : TAP_ROW + TAPS, :] = gtaps[:TAPS, :]
    log_decay, decay, root, maps_in, maps_out = state_terms(table_ref)
    both = gmap[...] * root
    out[MAP_IN:MAP_OUT, :] = both * maps_out
    out[MAP_OUT:TABLE, :] = both * maps_in
    turn = (1.0 - root * root) / root
    out[RATE:MAP_IN, :] = log_decay * (
        gdecay[...] * decay - gmap[...] * maps_in * maps_out * turn
    )


def store_cols(out, at, value):
    groups = value.shape[0] // PIECE
    out[:, at] = value.reshape((groups, PIECE, WIDTH))


def tail_kernel(mesh_size, *refs):
    fused = mesh_size is not None
    refs = list(refs)
    take = lambda count: [refs.pop(0) for _ in range(count)]
    x_ref, h_ref, gx1_ref, up_ref, down_ref, table_ref = take(6)
    hidden = 4 * WIDTH
    if fused:
        gvec1, gvec2, gtaps, gmap, gdecay, gbias1 = take(6)
        sources = take(1)
        gx_ref, last_out = take(2)
        reduced = take(5)
    else:
        gx_ref, gvec_out, gbias_out, up_out, down_out = take(5)
    turn_scr, grad_scr, gh_scr, vec_acc, bias_scr = take(5)
    step = pl.program_id(0)
    frames, channels = x_ref.shape
    chunks = hidden // WIDTH
    tiles = frames // TILE
    first_b, first_c = 1 + chunks, 1 + 2 * chunks
    schedule = {}
    if fused:
        n_dp, n_fs = mesh_size
        down_src, left_src, right_src, small_src, small_scr, gvec3 = take(6)
        dp, fs = lax.axis_index("dp"), lax.axis_index("fsdp")
        place = Place(dp, fs, n_dp, n_fs)
        scratch = take(5 * (2 + place.count))
        sems = take(3)
        swap = take(4)
        down_out = flat_groups(down_src)
        halves = (flat_groups(left_src), flat_groups(right_src))

        def emit(chunk, total):
            reduced[chunk][...] = total

        plans, sends = block_scatter(
            place, sources + [down_src, left_src, right_src, small_src], emit, scratch, *sems
        )
        begins = [
            (0, 1, 2, 4, 6),
            (first_b, first_b + 1, first_b + 2, first_b + 3, first_c),
            (first_b + 2, first_b + 3, first_c, first_c + 1, first_c + 2),
            (first_c, first_c + 1, first_c + 2, first_c + tiles, first_c + tiles),
            (first_c, first_c + 1, first_c + 2, first_c + tiles, first_c + tiles),
        ]
        for chunk, steps in enumerate(begins):
            for stage, at in enumerate(steps):
                schedule.setdefault(at, []).append((stage, chunk))
    last_step = first_c + tiles - 1

    def progress(at):
        for stage, chunk in sorted(schedule.get(at, [])):
            plans[chunk][stage]()

    @pl.when(step == 0)
    def _():
        if fused:
            greet(dp, fs, n_dp, n_fs)
        progress(0)
        vec_acc[...] = jnp.zeros_like(vec_acc)

        def first(rows):
            e, _ = norm_parts(x_ref[rows, :].astype(F32))
            low = (e * table_ref[0:1, :] + table_ref[6:7, :]).astype(BF16)
            turn_scr[:, rows] = low.T
            grad = (0.5 * gx1_ref[rows, :]).astype(BF16)
            grad_scr[rows, :] = grad
            vec_acc[0] += fold8(grad.astype(F32))

        by_rows(first, frames)

    if fused:
        for at in range(1, last_step + 1):
            if at in schedule and at != first_c:

                @pl.when(step == at)
                def _(at=at):
                    progress(at)

    @pl.when((step >= 1) & (step < first_b))
    def _():
        h = h_ref[...].astype(F32)
        active = (h * sigmoid(h)).astype(BF16)
        value = dot_tn(active, grad_scr[...]).astype(BF16)
        groups = WIDTH // (4 * PIECE)
        down_out[pl.ds((step - 1) * groups, groups)] = value.reshape((groups, 4, PIECE, WIDTH))

    def second_half(c, store):
        cols = columns(c, WIDTH)
        h = h_ref[...].astype(F32)
        sig = sigmoid(h)
        gate = dot_nt(grad_scr[...], rows_of(down_ref, 0, c))
        grad_h = (gate * (sig * (1.0 + h * (1.0 - sig)))).astype(BF16)
        gh_scr[:, cols] = grad_h
        sums = jnp.sum(fold8(grad_h.astype(F32)), axis=0, keepdims=True)
        bias_scr[pl.ds(2 * c, 1), :] = sums[:, :CHUNK]
        bias_scr[pl.ds(2 * c + 1, 1), :] = sums[:, CHUNK:]
        store(dot_nn(turn_scr[...], grad_h).astype(BF16))

    if fused:
        for half in range(2):
            begin = first_b + half * (chunks // 2)

            @pl.when((step >= begin) & (step < begin + chunks // 2))
            def _(half=half, begin=begin):
                def store(value):
                    store_cols(halves[half], step - begin, value)

                second_half(step - first_b, store)

    else:

        @pl.when((step >= first_b) & (step < first_c))
        def _():
            def store(value):
                store_cols(up_out, step - first_b, value)

            second_half(step - first_b, store)

    if fused:

        @pl.when(step == first_c)
        def _():
            gvec3[0:1, :] = jnp.sum(vec_acc[0], axis=0, keepdims=True)
            small_gradients(small_scr, gvec1, gvec2, gvec3, gtaps, gmap, gdecay, table_ref)
            narrow = small_scr[...].T.astype(BF16)
            devices = n_dp * n_fs
            small_out = flat_groups(small_src)
            small_out[:, 0, :, :CHUNK] = narrow.reshape((devices, PIECE, CHUNK))
            for c in range(8):
                bias_scr[8 + c : 9 + c, :] = gbias1[0:1, c * CHUNK : c * CHUNK + CHUNK]
            bias = bias_scr[...].astype(BF16)
            small_out[:, 0, :, CHUNK:] = jnp.broadcast_to(bias[None], (devices, PIECE, CHUNK))
            progress(first_c)

    @pl.when(step >= first_c)
    def _():
        tile = step - first_c
        whole_tile = pl.ds(pl.multiple_of(tile * TILE, TILE), TILE)
        total = dot_nt(gh_scr[whole_tile, :WIDTH], square_of(up_ref, 1))
        for k in range(1, hidden // WIDTH):
            cols = slice(k * WIDTH, k * WIDTH + WIDTH)
            total = total + dot_nt(gh_scr[whole_tile, cols], square_of(up_ref, 1 + k))
        gx_ref[...] = total

        def second(rows):
            here = pl.ds(pl.multiple_of(tile * TILE + rows.start, ROWS), ROWS)
            e, inv = norm_parts(x_ref[here, :].astype(F32))
            grad = gx_ref[rows, :]
            vec_acc[1] += fold8(grad * e)
            vec_acc[2] += fold8(grad)
            gx_ref[rows, :] = gx1_ref[here, :] + norm_back(grad, e, inv, table_ref[0:1, :])

        by_rows(second)

    @pl.when(step == last_step)
    def _():
        if fused:
            last_out[...] = jnp.zeros_like(last_out)
            for k in range(2):
                last_out[k : k + 1, :] = jnp.sum(vec_acc[1 + k], axis=0, keepdims=True)
            ends = sorted(schedule.get(last_step + 1, []))

            def between():
                for stage, chunk in ends:
                    plans[chunk][stage]()

            last_out[...] = sum_over(last_out[...], dp, fs, n_dp, n_fs, *swap, between=between)
            for wait in sends:
                wait()
        else:
            gvec_out[...] = jnp.zeros_like(gvec_out)
            for k in range(3):
                gvec_out[k : k + 1, :] = jnp.sum(vec_acc[k], axis=0, keepdims=True)
            gbias_out[...] = bias_scr[...]


def tail(mesh_size, x, h, gx1, up, down, table, others=(), grads=(), collective_id=None):
    fused = mesh_size is not None
    frames, channels = x.shape
    hidden = h.shape[1]
    tiles, chunks = frames // TILE, hidden // WIDTH
    first_b, first_c = 1 + chunks, 1 + 2 * chunks
    place = lambda i: jnp.where(
        i < first_b, jnp.maximum(i - 1, 0), jnp.minimum(i - first_b, chunks - 1)
    )
    shapes = [jax.ShapeDtypeStruct((frames, channels), F32)]
    scratch = [
        pltpu.VMEM((channels, frames), BF16),
        pltpu.VMEM((frames, channels), BF16),
        pltpu.VMEM((frames, hidden), BF16),
        pltpu.VMEM((8, 8, channels), F32),
        pltpu.VMEM((16, CHUNK), F32),
    ]
    if fused:
        own = [4, 2, 2, 1]
        counts = [g.shape[-3] for g in grads] + own
        shapes.append(jax.ShapeDtypeStruct((8, channels), F32))
        shapes += [jax.ShapeDtypeStruct((k, PIECE, WIDTH), F32) for k in counts]
        layout = block_layout(*mesh_size)
        scratch += [pltpu.VMEM(layout + (k, PIECE, WIDTH), BF16) for k in own]
        scratch += [pltpu.VMEM((256, channels), F32), pltpu.VMEM((8, channels), F32)]
        scratch += block_scratch(*mesh_size, counts, (PIECE, WIDTH))
        scratch += block_sems(*mesh_size, len(counts))
        scratch += swap_scratch(*mesh_size, channels)
    else:
        shapes += [
            jax.ShapeDtypeStruct((8, channels), F32),
            jax.ShapeDtypeStruct((16, CHUNK), F32),
            jax.ShapeDtypeStruct((channels // PIECE, 4, PIECE, WIDTH), BF16),
            jax.ShapeDtypeStruct((channels // PIECE, 4, PIECE, WIDTH), BF16),
        ]
    return pl.pallas_call(
        partial(tail_kernel, mesh_size),
        grid=(first_c + tiles,),
        in_specs=[whole(x.shape), pl.BlockSpec((frames, WIDTH), lambda i: (0, place(i)))]
        + [whole(a.shape) for a in (gx1, up, down, table) + tuple(others)]
        + [pl.BlockSpec(memory_space=pltpu.HBM)] * len(grads),
        out_specs=[
            pl.BlockSpec((TILE, channels), lambda i: (jnp.maximum(i - first_c, 0), 0))
        ]
        + [whole(s.shape) for s in shapes[1:]],
        out_shape=shapes,
        scratch_shapes=scratch,
        compiler_params=params(collective_id),
        name="tail",
    )(x, h, gx1, up, down, table, *others, *grads)


def unpack_kernel(
    place_ref,
    second_ref,
    middle_ref,
    mixin_ref,
    down_ref,
    left_ref,
    right_ref,
    small_ref,
    last_ref,
    up_out,
    down_out,
    bias_out,
    mixin_out,
    mixout_out,
    convin_out,
    convout_out,
    convbias_out,
    rate_out,
    map_out,
    taps_out,
    gains_out,
    shifts_out,
):
    mine = place_ref[0]
    for k in range(4):
        cols = slice(k * WIDTH, k * WIDTH + WIDTH)
        rows = slice(k * PIECE, k * PIECE + PIECE)
        up_out[0, :, cols] = (left_ref if k < 2 else right_ref)[k % 2]
        up_out[1, :, cols] = second_ref[1 + k]
        down_out[0, rows, :] = down_ref[k]
        down_out[1, rows, :] = second_ref[5 + k]
    convout_out[...] = second_ref[0]
    mixout_out[...] = middle_ref[0]
    for k in range(2):
        cols = slice(k * WIDTH, k * WIDTH + WIDTH)
        mixin_out[:, cols] = mixin_ref[k]
        convin_out[:, cols] = middle_ref[1 + k]
    count = bias_out.shape[1]
    row = (mine * count) // CHUNK
    inner = mine * count - row * CHUNK
    for layer in range(2):
        line = small_ref[0, pl.ds(8 * layer + row, 1), CHUNK:]
        line = pltpu.roll(jnp.broadcast_to(line, (8, CHUNK)), CHUNK - inner, 1)
        bias_out[layer : layer + 1, :] = line[0:1, :count]
    channels = last_ref.shape[1]
    first = pltpu.roll(last_ref[...], channels - mine * PIECE, 1)[:, :PIECE]
    small = small_ref[0, :, :CHUNK]
    turned = small.T
    gains_out[...] = turned[0:6, :]
    gains_out[0:1, :] = first[0:1, :]
    shifts_out[...] = turned[6:18, :]
    shifts_out[0:1, :] = first[1:2, :]
    convbias_out[...] = turned[18:19, :]
    taps_out[...] = turned[TAP_ROW : TAP_ROW + TAPS, :]
    rate_out[...] = small[:, RATE:MAP_IN]
    map_out[0] = small[:, MAP_IN:MAP_OUT]
    map_out[1] = small[:, MAP_OUT:TABLE]


def unpack(mine, arrays, hidden):
    channels = arrays[-1].shape[1]
    devices = channels // PIECE
    f32 = lambda *shape: jax.ShapeDtypeStruct(shape, F32)
    vmem = pl.BlockSpec(memory_space=pltpu.VMEM)
    return pl.pallas_call(
        unpack_kernel,
        in_specs=[SMEM_SPEC] + [vmem] * len(arrays),
        out_specs=[vmem] * 13,
        out_shape=[
            f32(2, PIECE, hidden),
            f32(2, hidden // devices, channels),
            f32(2, hidden // devices),
            f32(PIECE, 2 * WIDTH),
            f32(PIECE, WIDTH),
            f32(PIECE, 2 * WIDTH),
            f32(PIECE, WIDTH),
            f32(1, PIECE),
            f32(PIECE, STATES),
            f32(2, PIECE, STATES),
            f32(TAPS, PIECE),
            f32(6, PIECE),
            f32(12, PIECE),
        ],
        name="unpack",
    )(mine, *arrays)


def pack_table(gains, shifts, conv_bias, taps, rate, maps):
    channels = gains.shape[1]
    blank = lambda rows: jnp.zeros((rows, channels), gains.dtype)
    parts = [gains, shifts, conv_bias[None], blank(TAP_ROW - 19), taps, blank(RATE - TAP_ROW - TAPS)]
    parts += [rate, maps[0], maps[1], blank(256 - TABLE)]
    return jnp.concatenate(parts, axis=0).T


def pack_bias(bias, place):
    layers, count = bias.shape
    hidden = 16 * CHUNK // layers
    wide = lax.dynamic_update_slice(
        jnp.zeros((layers, hidden), bias.dtype), bias, (0, place * count)
    )
    return wide.reshape((16, CHUNK))


def unpack_table(table):
    return (
        table[0:6],
        table[6:18],
        table[18],
        table[TAP_ROW : TAP_ROW + TAPS],
        table[RATE:MAP_IN],
        jnp.stack([table[MAP_IN:MAP_OUT], table[MAP_OUT:TABLE]]),
    )


def on_device(
    n_dp,
    n_fs,
    frames,
    seq_lengths,
    seq_offsets,
    seq_counts,
    ffn_up,
    ffn_down,
    ffn_bias_up,
    mix_in,
    mix_out,
    conv_in,
    conv_out,
    conv_out_bias,
    ssm_rate,
    ssm_map,
    conv_kernel,
    gains,
    shifts,
    cotangent,
):
    devices = n_dp * n_fs
    mine = lax.axis_index("dp") * n_fs + lax.axis_index("fsdp")
    frames_dev, channels = frames.shape
    hidden = ffn_up.shape[2]
    if channels // devices == PIECE:
        size = (n_dp, n_fs)
        small = [
            ffn_bias_up,
            gains,
            shifts,
            conv_out_bias[None],
            conv_kernel,
            ssm_rate.T,
            ssm_map.transpose((0, 2, 1)),
        ]
        weights = [ffn_up, ffn_down, mix_in, mix_out, conv_in, conv_out]
        made = front(size, seq_offsets, seq_counts, frames, small, weights, hidden, 1)
        h0, x1, v, y, gated, x2, p, u, w, stat, table, bias, *mixing = made[:17]
        groups = lambda g: g.reshape((devices,) + g.shape[-3:])
        places = lambda g: g.reshape(block_layout(n_dp, n_fs) + g.shape[1:])
        first, second, third, fourth = [groups(g) for g in made[17:]]
        result, gx3, gnb, grads, gbias1, gvec1, stat = middle(
            size, x2, w, cotangent, fourth, bias, table, stat, hidden, 2
        )
        gx1, grads2, gvec2, gtaps, gmap, gdecay, reduced, reduced2 = back(
            size,
            seq_offsets,
            seq_counts,
            [w, gnb, p, x2, gx3, gated, y, v, x1],
            [u] + mixing + [third, table, stat],
            (places(grads),),
            3,
        )
        others = (gvec1, gvec2, gtaps, gmap, gdecay, gbias1)
        gx, last, *late = tail(
            size, frames, h0, gx1, first, second, table, others, (places(grads2),), 4
        )
        made = unpack(mine.reshape((1,)), [reduced, reduced2] + late + [last], hidden)
        made = list(made)
        made[7] = made[7].reshape((-1,))
        made[8] = made[8].T
        made[9] = made[9].transpose((0, 2, 1))
        return (result, gx) + tuple(made)

    small = pack_table(gains, shifts, conv_out_bias, conv_kernel, ssm_rate, ssm_map)
    got = gather_all(
        n_dp,
        n_fs,
        [
            small[None],
            pack_bias(ffn_bias_up, mine)[None],
            ffn_up,
            ffn_down,
            mix_in[None],
            mix_out[None],
            conv_in[None],
            conv_out[None],
        ],
        1,
    )
    matrix = lambda g: g.reshape((-1, g.shape[-1]))
    table, _, up0, up1, down0, down1, mixin, mixout, convin, convout = [matrix(g) for g in got]
    table = table.astype(F32).T[:TABLE]
    bias = jnp.sum(got[1].astype(F32), axis=0)
    group_count = channels // PIECE
    cut = lambda g: g.reshape((group_count, PIECE, -1, WIDTH)).transpose((0, 2, 1, 3))
    tall = lambda g: g.reshape((group_count, -1, PIECE, WIDTH))
    join = lambda g: g.transpose((0, 2, 1, 3)).reshape((channels, -1))
    blank = jnp.pad(matrix(got[0]), ((0, 0), (0, WIDTH - 256))).reshape((group_count, 1, PIECE, WIDTH))
    first = jnp.concatenate([blank, cut(up0)], axis=1)
    third = jnp.concatenate([cut(mixin), cut(mixout), cut(convin)], axis=1)
    fourth = jnp.concatenate([cut(convout), cut(up1), tall(down1)], axis=1)
    made = front(
        None, seq_offsets, seq_counts, frames, [table, bias], [first, tall(down0), third], hidden
    )
    h0, x1, v, y, gated, x2, p, u, w, stat, table, bias, *mixing = made
    pool = exchange(n_dp, n_fs, stat, frames_dev, 2, pool_kernel)
    scale = lax.rsqrt(pool[1:2] / (frames_dev * devices) + EPSILON)
    stat = jnp.concatenate([pool[0:1], scale, jnp.zeros((6, channels), F32)])
    result, gx3, gnb, grads, gbias1, gvec1, stat = middle(
        None, x2, w, cotangent, fourth, bias, table, stat, hidden
    )
    sums = exchange(n_dp, n_fs, gvec1, 1, 4, total_kernel)[6:8]
    sums = sums * (table[5:6] / (frames_dev * devices))
    stat = jnp.concatenate([stat[0:2], sums[1:2], sums[0:1], stat[4:8]])
    gx1, grads2, gvec2, gtaps, gmap, gdecay, grads3 = back(
        None,
        seq_offsets,
        seq_counts,
        [w, gnb, p, x2, gx3, gated, y, v, x1],
        [u] + mixing + [third, table, stat],
    )
    gx, gvec3, gbias0, gup0, gdown0 = tail(None, frames, h0, gx1, first, tall(down0), table)

    def weights_of(log_rate, maps):
        log_decay = -jnp.exp(log_rate)
        root = jnp.sqrt(-jnp.expm1(2.0 * log_decay))
        return jnp.exp(log_decay), maps[0] * root * maps[1]

    rate, maps = unpack_table(table)[4:]
    rate_grad, map_grad = jax.vjp(weights_of, rate, maps)[1]((gdecay, gmap))
    gain_grad = jnp.stack([gvec3[1], gvec2[6], gvec2[2], gvec1[3], gvec1[0], gvec1[6]])
    rows = [gvec3[2], gvec2[7], gvec2[3], gvec1[4], gvec1[1], gvec1[7], gvec3[0], gvec1[2]]
    rows += [gvec2[4], gvec2[0], gvec2[1], gvec2[5]]
    small_grad = pack_table(
        gain_grad, jnp.stack(rows), gvec1[5], gtaps[:TAPS], rate_grad, map_grad
    )
    bias_grad = jnp.concatenate([gbias0[:8], gbias1[0].reshape((8, CHUNK))])
    wide = lambda g: g.reshape((devices, g.shape[0] // devices, g.shape[1]))
    reduced = scatter_all(
        n_dp,
        n_fs,
        [
            wide(join(grads[:, 1:5])),
            wide(matrix(grads[:, 5:9])),
            wide(join(grads[:, 0:1])),
            wide(join(grads3[:, 1:3])),
            wide(join(grads3[:, 0:1])),
            wide(join(grads2[:, 0:2])),
            wide(join(gup0)),
            wide(matrix(gdown0)),
            wide(small_grad.astype(BF16)),
            jnp.broadcast_to(bias_grad.astype(BF16), (devices, PIECE, CHUNK)),
        ],
        5,
    )
    gains_grad, shifts_grad, conv_bias_grad, taps_grad, rate_grad, map_grad = unpack_table(
        reduced[8].T
    )
    bias_grad = reduced[9].reshape((2, -1))
    count = bias_grad.shape[1] // devices
    bias_grad = lax.dynamic_slice(bias_grad, (0, mine * count), (2, count))
    return (
        result,
        gx,
        jnp.stack([reduced[6], reduced[0]]),
        jnp.stack([reduced[7], reduced[1]]),
        bias_grad,
        reduced[5],
        reduced[4],
        reduced[3],
        reduced[2],
        conv_bias_grad,
        rate_grad,
        map_grad,
        taps_grad,
        gains_grad,
        shifts_grad,
    )


def solution(mesh):
    both = ("dp", "fsdp")
    row, row1 = P(both, None), P(both)
    col, col3, mid = P(None, both), P(None, None, both), P(None, both, None)
    in_specs = (
        row,
        row,
        row,
        row1,
        mid,
        mid,
        col,
        row,
        row,
        row,
        row,
        row1,
        col,
        col3,
        col,
        col,
        col,
        row,
    )
    out_specs = (row, row, mid, mid, col, row, row, row, row, row1, col, col3, col, col, col)
    return jax.shard_map(
        partial(on_device, mesh.shape["dp"], mesh.shape["fsdp"]),
        mesh=mesh,
        in_specs=in_specs,
        out_specs=out_specs,
        check_vma=False,
    )
```

```python
import itertools
from functools import partial

import jax
import jax.numpy as jnp
from jax import lax
from jax.experimental import pallas as pl
from jax.experimental.pallas import tpu as pltpu
from jax.sharding import PartitionSpec as P

MESH = pl.DeviceIdType.MESH
BF16 = jnp.bfloat16
F32 = jnp.float32


def flip(index, bit):
    return index + bit * (1 - 2 * lax.rem(lax.div(index, bit), 2))


def flip_all(index, bits):
    for bit in bits:
        index = flip(index, bit)
    return index


def combos(bits):
    found = [()]
    for bit in bits:
        found = found + [entry + (bit,) for entry in found]
    return found


def plan_bits(n_dp):
    bits, bit = [], 2
    while bit < n_dp:
        bits.append(bit)
        bit *= 2
    return tuple(bits)


def greet(dp, fs, n_dp, n_fs):
    barrier = pltpu.get_barrier_semaphore()
    for step in range(1, n_dp):
        pl.semaphore_signal(
            barrier, inc=1, device_id=(lax.rem(dp + step, n_dp), fs), device_id_type=MESH
        )
    for step in range(1, n_fs):
        pl.semaphore_signal(
            barrier, inc=1, device_id=(dp, lax.rem(fs + step, n_fs)), device_id_type=MESH
        )
    pl.semaphore_wait(barrier, n_dp + n_fs - 2)


def gather_plan(dp, fs, n_dp, n_fs, sources, outs, send_sem, recv_sem, local_sem):
    bits = plan_bits(n_dp)
    orders = (bits, bits[::-1])
    half = n_fs // 2
    sends = []

    def stages(chunk):
        src, out = sources[chunk], outs[chunk]
        slots = itertools.count()

        def zone(where, part):
            if part is None:
                return out.at[pl.ds(where * n_fs, n_fs)]
            return out.at[pl.ds(where * n_fs + part * half, half)]

        def remote(slot, view_from, view_to, device):
            return pltpu.make_async_remote_copy(
                src_ref=view_from,
                dst_ref=view_to,
                send_sem=send_sem.at[chunk, slot],
                recv_sem=recv_sem.at[chunk, slot],
                device_id=device,
                device_id_type=MESH,
            )

        def launch(make):
            make().start()
            sends.append(lambda: make().wait_send())

        z_slots = [next(slots) for _ in range(1, n_fs)]

        def own_copy():
            return pltpu.make_async_copy(src, out.at[dp * n_fs + fs], local_sem.at[chunk])

        def start():
            own_copy().start()
            for step in range(1, n_fs):
                launch(
                    lambda step=step: remote(
                        z_slots[step - 1],
                        src,
                        out.at[dp * n_fs + fs],
                        (dp, lax.rem(fs + step, n_fs)),
                    )
                )

        def wait_z():
            own_copy().wait()
            for step in range(1, n_fs):
                origin = dp * n_fs + lax.rem(fs + n_fs - step, n_fs)
                remote(z_slots[step - 1], src, out.at[origin], (dp, fs)).wait_recv()

        steps, before = [start], wait_z
        for depth in range(len(bits)):
            plan = []
            for part, order in enumerate(orders):
                for entry in combos(order[:depth]):
                    plan.append((next(slots), part, order[depth], entry))

            def view(slot, part, bit, entry, arrived):
                where = flip_all(flip(dp, bit) if arrived else dp, entry)
                return remote(slot, zone(where, part), zone(where, part), (flip(dp, bit), fs))

            def go(plan=plan, before=before, view=view):
                before()
                for item in plan:
                    launch(lambda item=item: view(*item, False))

            def arrive(plan=plan, view=view):
                for item in plan:
                    view(*item, True).wait_recv()

            steps.append(go)
            before = arrive
        last = [(next(slots), entry) for entry in combos(bits)]

        def across(slot, entry, arrived):
            where = flip_all(flip(dp, 1) if arrived else dp, entry)
            return remote(slot, zone(where, None), zone(where, None), (flip(dp, 1), fs))

        def cross(before=before):
            before()
            for item in last:
                launch(lambda item=item: across(*item, False))

        def finish():
            for item in last:
                across(*item, True).wait_recv()

        return steps + [cross, finish]

    return [stages(chunk) for chunk in range(len(outs))], sends


def waves(plans):
    depth = len(plans[0])
    out = []
    for wave in range(len(plans) + depth - 1):
        out.append(
            [plans[c][wave - c] for c in range(len(plans)) if 0 <= wave - c < depth]
        )
    return out


def gather_kernel(n_dp, n_fs, layers, *refs):
    n_in = len(layers)
    n_out = sum(layers)
    ins, outs = refs[:n_in], refs[n_in : n_in + n_out]
    send_sem, recv_sem, local_sem = refs[n_in + n_out :]
    sources = []
    for ref, count in zip(ins, layers):
        sources += [ref.at[layer] for layer in range(count)]
    dp, fs = lax.axis_index("dp"), lax.axis_index("fsdp")
    greet(dp, fs, n_dp, n_fs)
    plans, sends = gather_plan(dp, fs, n_dp, n_fs, sources, outs, send_sem, recv_sem, local_sem)
    for wave in waves(plans):
        for stage in wave:
            stage()
    for wait in sends:
        wait()


def slot_count(n_dp, n_fs):
    nb = len(plan_bits(n_dp))
    return n_fs - 1 + 2 * (2**nb - 1) + 2**nb


def gather_all(n_dp, n_fs, arrays, collective_id):
    layers = tuple(a.shape[0] for a in arrays)
    outs = []
    for a in arrays:
        outs += [jax.ShapeDtypeStruct((n_dp * n_fs,) + a.shape[1:], a.dtype)] * a.shape[0]
    count = slot_count(n_dp, n_fs)
    return pl.pallas_call(
        partial(gather_kernel, n_dp, n_fs, layers),
        out_shape=outs,
        in_specs=[pl.BlockSpec(memory_space=pltpu.HBM)] * len(arrays),
        out_specs=[pl.BlockSpec(memory_space=pltpu.HBM)] * len(outs),
        scratch_shapes=[
            pltpu.SemaphoreType.DMA((len(outs), count)),
            pltpu.SemaphoreType.DMA((len(outs), count)),
            pltpu.SemaphoreType.DMA((len(outs),)),
        ],
        compiler_params=pltpu.CompilerParams(collective_id=collective_id, has_side_effects=True),
        name="gather_parameters",
    )(*arrays)


def scatter_plan(dp, fs, n_dp, n_fs, ins, emit, scratch, send_sem, recv_sem, local_sem, first=0):
    bits = plan_bits(n_dp)
    orders = (bits[::-1], bits)
    half = n_fs // 2
    index = {entry: at for at, entry in enumerate(combos(bits))}
    sends = []

    def add_into(kept, other):
        def body(at, _):
            kept[at] = (kept[at].astype(F32) + other[at].astype(F32)).astype(BF16)
            return 0

        lax.fori_loop(0, kept.shape[0], body, 0)

    def stages(chunk):
        src = ins[chunk]
        cross_in, own, later, last = scratch[4 * chunk : 4 * chunk + 4]
        slots = itertools.count()

        def remote(slot, view_from, view_to, device):
            return pltpu.make_async_remote_copy(
                src_ref=view_from,
                dst_ref=view_to,
                send_sem=send_sem.at[first + chunk, slot],
                recv_sem=recv_sem.at[first + chunk, slot],
                device_id=device,
                device_id_type=MESH,
            )

        def launch(make):
            make().start()
            sends.append(lambda: make().wait_send())

        def zone(entry, crossed):
            return src.at[pl.ds(flip_all(flip(dp, 1) if crossed else dp, entry) * n_fs, n_fs)]

        pieces = [(next(slots), entry, index[entry]) for entry in combos(bits)]

        def load(entry, at):
            return pltpu.make_async_copy(
                zone(entry, False), own.at[at], local_sem.at[first + chunk, at]
            )

        def across(slot, entry, at):
            return remote(slot, zone(entry, True), cross_in.at[at], (flip(dp, 1), fs))

        def start():
            for item in pieces:
                launch(lambda item=item: across(*item))
            for _, entry, at in pieces:
                load(entry, at).start()

        def fold_cross():
            for slot, entry, at in pieces:
                load(entry, at).wait()
                across(slot, entry, at).wait_recv()
                add_into(own.at[at], cross_in.at[at])

        steps, before = [start], fold_cross
        used = 0
        for depth in range(len(bits)):
            plan = []
            for part, order in enumerate(orders):
                bit, gone = order[depth], order[:depth]
                for entry in combos(bits):
                    if not (set(entry) & set(gone)) and bit not in entry:
                        away = tuple(sorted(entry + (bit,)))
                        plan.append((next(slots), part, bit, index[away], index[entry], used))
                        used += 1

            def move(slot, part, bit, away, kept, place):
                return remote(
                    slot,
                    own.at[away, pl.ds(part * half, half)],
                    later.at[place],
                    (flip(dp, bit), fs),
                )

            def go(plan=plan, before=before, move=move):
                before()
                for item in plan:
                    launch(lambda item=item: move(*item))

            def fold(plan=plan, move=move):
                for item in plan:
                    move(*item).wait_recv()
                    _, part, _, _, kept, place = item
                    add_into(own.at[kept, pl.ds(part * half, half)], later.at[place])

            steps.append(go)
            before = fold
        z_slots = [next(slots) for _ in range(1, n_fs)]

        def along(step):
            to = lax.rem(fs + step, n_fs)
            return remote(z_slots[step - 1], own.at[0, to], last.at[step - 1], (dp, to))

        def spread(before=before):
            before()
            for step in range(1, n_fs):
                launch(lambda step=step: along(step))

        def finish():
            total = own[0, fs].astype(F32)
            for step in range(1, n_fs):
                along(step).wait_recv()
                total = total + last[step - 1].astype(F32)
            emit(chunk, total)

        return steps + [spread, finish]

    return [stages(chunk) for chunk in range(len(ins))], sends


def scatter_scratch(n_dp, n_fs, tails):
    pieces = 2 ** len(plan_bits(n_dp))
    scratch = []
    for tail in tails:
        scratch += [
            pltpu.VMEM((pieces, n_fs) + tail, BF16),
            pltpu.VMEM((pieces, n_fs) + tail, BF16),
            pltpu.VMEM((2 * (pieces - 1), n_fs // 2) + tail, BF16),
            pltpu.VMEM((n_fs - 1,) + tail, BF16),
        ]
    return scratch


def scatter_sems(n_dp, n_fs, chunks):
    count = slot_count(n_dp, n_fs)
    return [
        pltpu.SemaphoreType.DMA((chunks, count)),
        pltpu.SemaphoreType.DMA((chunks, count)),
        pltpu.SemaphoreType.DMA((chunks, 2 ** len(plan_bits(n_dp)))),
    ]


def scatter_kernel(n_dp, n_fs, n_chunks, *refs):
    ins, outs = refs[:n_chunks], refs[n_chunks : 2 * n_chunks]
    scratch = refs[2 * n_chunks : 6 * n_chunks]
    dp, fs = lax.axis_index("dp"), lax.axis_index("fsdp")
    greet(dp, fs, n_dp, n_fs)

    def emit(chunk, total):
        outs[chunk][...] = total

    plans, sends = scatter_plan(dp, fs, n_dp, n_fs, ins, emit, scratch, *refs[6 * n_chunks :])
    for wave in waves(plans):
        for stage in wave:
            stage()
    for wait in sends:
        wait()


def scatter_all(n_dp, n_fs, arrays, collective_id):
    n = len(arrays)
    return pl.pallas_call(
        partial(scatter_kernel, n_dp, n_fs, n),
        out_shape=[jax.ShapeDtypeStruct(a.shape[1:], F32) for a in arrays],
        in_specs=[pl.BlockSpec(memory_space=pltpu.HBM)] * n,
        out_specs=[pl.BlockSpec(memory_space=pltpu.VMEM)] * n,
        scratch_shapes=scatter_scratch(n_dp, n_fs, [a.shape[1:] for a in arrays])
        + scatter_sems(n_dp, n_fs, n),
        compiler_params=pltpu.CompilerParams(
            collective_id=collective_id, has_side_effects=True, vmem_limit_bytes=48 << 20
        ),
        name="scatter_gradients",
    )(*arrays)


def swap_copy(axis, place, count, buffer, send_sem, recv_sem, step):
    return pltpu.make_async_remote_copy(
        src_ref=buffer.at[0],
        dst_ref=buffer.at[step],
        send_sem=send_sem.at[step],
        recv_sem=recv_sem.at[step],
        device_id={axis: lax.rem(place + step, count)},
        device_id_type=MESH,
    )


def swap_start(axis, place, count, *rest):
    for step in range(1, count):
        swap_copy(axis, place, count, *rest, step).start()


def swap_wait(axis, place, count, *rest):
    for step in range(1, count):
        swap_copy(axis, place, count, *rest, step).wait_recv()
    for step in range(1, count):
        swap_copy(axis, place, count, *rest, step).wait_send()


def swap_rows(*args):
    swap_start(*args)
    swap_wait(*args)


def sum_over(x, dp, fs, n_dp, n_fs, octet, line, send_sem, recv_sem, between=None):
    first = ("dp", dp, n_dp, octet, send_sem.at[0], recv_sem.at[0])
    octet[0] = x
    swap_start(*first)
    if between is not None:
        between()
    swap_wait(*first)
    total = octet[0]
    for step in range(1, n_dp):
        total = total + octet[step]
    line[0] = total
    swap_rows("fsdp", fs, n_fs, line, send_sem.at[1], recv_sem.at[1])
    total = line[0]
    for step in range(1, n_fs):
        total = total + line[step]
    return total


def pooled(buffer, count, weight):
    means = [buffer[k, 0:1, :] for k in range(count)]
    center = sum(means[1:], means[0]) * (1.0 / count)
    spread = buffer[0, 1:2, :]
    for k in range(1, count):
        spread = spread + buffer[k, 1:2, :]
    off = (means[0] - center) * (means[0] - center)
    for mean in means[1:]:
        off = off + (mean - center) * (mean - center)
    return center, spread + weight * off


def pool_over(center, spread, frames, dp, fs, n_dp, n_fs, octet, line, send_sem, recv_sem):
    octet[0] = jnp.zeros(octet.shape[1:], F32)
    line[0] = jnp.zeros(line.shape[1:], F32)
    octet[0, 0:1, :] = center
    octet[0, 1:2, :] = spread
    swap_rows("dp", dp, n_dp, octet, send_sem.at[0], recv_sem.at[0])
    center, spread = pooled(octet, n_dp, float(frames))
    line[0, 0:1, :] = center
    line[0, 1:2, :] = spread
    swap_rows("fsdp", fs, n_fs, line, send_sem.at[1], recv_sem.at[1])
    return pooled(line, n_fs, float(frames * n_dp))


def swap_scratch(n_dp, n_fs, channels):
    return [
        pltpu.VMEM((n_dp, 8, channels), F32),
        pltpu.VMEM((n_fs, 8, channels), F32),
        pltpu.SemaphoreType.DMA((2, max(n_dp, n_fs))),
        pltpu.SemaphoreType.DMA((2, max(n_dp, n_fs))),
    ]


def pool_kernel(n_dp, n_fs, frames, x_ref, out_ref, octet, line, send_sem, recv_sem):
    dp, fs = lax.axis_index("dp"), lax.axis_index("fsdp")
    greet(dp, fs, n_dp, n_fs)
    octet[0] = x_ref[...]
    center, spread = pool_over(
        x_ref[0:1, :], x_ref[1:2, :], frames, dp, fs, n_dp, n_fs, octet, line, send_sem, recv_sem
    )
    out_ref[...] = x_ref[...]
    out_ref[0:1, :] = center
    out_ref[1:2, :] = spread


def total_kernel(n_dp, n_fs, frames, x_ref, out_ref, octet, line, send_sem, recv_sem):
    dp, fs = lax.axis_index("dp"), lax.axis_index("fsdp")
    greet(dp, fs, n_dp, n_fs)
    out_ref[...] = sum_over(x_ref[...], dp, fs, n_dp, n_fs, octet, line, send_sem, recv_sem)


def exchange(n_dp, n_fs, x, frames, collective_id, kernel):
    return pl.pallas_call(
        partial(kernel, n_dp, n_fs, frames),
        out_shape=jax.ShapeDtypeStruct(x.shape, F32),
        in_specs=[pl.BlockSpec(memory_space=pltpu.VMEM)],
        out_specs=pl.BlockSpec(memory_space=pltpu.VMEM),
        scratch_shapes=swap_scratch(n_dp, n_fs, x.shape[1]),
        compiler_params=pltpu.CompilerParams(collective_id=collective_id, has_side_effects=True),
        name="exchange_rows",
    )(x)


class Place:
    def __init__(self, dp, fs, n_dp, n_fs):
        self.dp, self.fs, self.n_dp, self.n_fs = dp, fs, n_dp, n_fs
        self.count = (n_dp - 1).bit_length()
        self.bits = [lax.rem(lax.div(dp, 2**k), 2) for k in range(self.count)]
        self.half = n_fs // 2

    def peer(self, bit):
        return (flip(self.dp, 2**bit), self.fs)

    def view(self, ref, free=(), flipped=(), z=None, skip=()):
        index = []
        for bit in reversed(range(self.count)):
            if bit in skip:
                continue
            if bit in free:
                index.append(slice(None))
            else:
                index.append(1 - self.bits[bit] if bit in flipped else self.bits[bit])
        if z is not None:
            index.append(z)
        return ref.at[tuple(index)] if index else ref

    def part(self, which):
        return pl.ds(which * self.half, self.half)


def block_layout(n_dp, n_fs):
    return (2,) * ((n_dp - 1).bit_length()) + (n_fs,)


def hop_orders(place):
    bits = tuple(range(1, place.count))
    return (bits, bits[::-1])


def copy_count(n_dp, n_fs):
    return n_fs - 1 + 2 * ((n_dp - 1).bit_length() - 1) + 1


def block_gather(place, sources, outs, send_sem, recv_sem, local_sem):
    n_fs, fs = place.n_fs, place.fs
    sends = []

    def stages(chunk):
        src, out = sources[chunk], outs[chunk]

        def remote(slot, view_from, view_to, device):
            return pltpu.make_async_remote_copy(
                src_ref=view_from,
                dst_ref=view_to,
                send_sem=send_sem.at[chunk, slot],
                recv_sem=recv_sem.at[chunk, slot],
                device_id=device,
                device_id_type=MESH,
            )

        def launch(make):
            make().start()
            sends.append(lambda: make().wait_send())

        def own_copy():
            return pltpu.make_async_copy(src, place.view(out, z=fs), local_sem.at[chunk])

        def along(step):
            to = lax.rem(fs + step, n_fs)
            return remote(step - 1, src, place.view(out, z=fs), (place.dp, to))

        def start():
            own_copy().start()
            for step in range(1, n_fs):
                launch(lambda step=step: along(step))

        def wait_along():
            own_copy().wait()
            for step in range(1, n_fs):
                origin = lax.rem(fs + n_fs - step, n_fs)
                remote(
                    step - 1, src, place.view(out, z=origin), (place.dp, origin)
                ).wait_recv()

        steps, before = [start], wait_along
        slot = n_fs - 1
        orders = hop_orders(place)
        for depth in range(place.count - 1):
            plan = [(slot + part, part, order[depth], order[:depth]) for part, order in enumerate(orders)]
            slot += 2

            def hop(slot, part, bit, free, arrived):
                view = place.view(out, free, (bit,) if arrived else (), place.part(part))
                return remote(slot, view, view, place.peer(bit))

            def go(plan=plan, before=before, hop=hop):
                before()
                for item in plan:
                    launch(lambda item=item: hop(*item, False))

            def arrive(plan=plan, hop=hop):
                for item in plan:
                    hop(*item, True).wait_recv()

            steps.append(go)
            before = arrive

        def across(arrived, slot=slot):
            free = tuple(range(1, place.count))
            view = place.view(out, free, (0,) if arrived else ())
            return remote(slot, view, view, place.peer(0))

        def cross(before=before):
            before()
            launch(lambda: across(False))

        return steps + [cross, lambda: across(True).wait_recv()]

    return [stages(chunk) for chunk in range(len(outs))], sends


def block_scatter(place, sources, emit, scratch, send_sem, recv_sem, local_sem):
    n_fs, fs = place.n_fs, place.fs
    sends = []
    per = 3 + place.count - 1

    def add_into(kept, other):
        shape = kept.shape[:-3]
        for index in itertools.product(*[range(n) for n in shape]):
            kept[index] = (kept[index].astype(F32) + other[index].astype(F32)).astype(BF16)

    def stages(chunk):
        src = sources[chunk]
        own, cross_in, last, *later = scratch[per * chunk : per * chunk + per]

        def remote(slot, view_from, view_to, device):
            return pltpu.make_async_remote_copy(
                src_ref=view_from,
                dst_ref=view_to,
                send_sem=send_sem.at[chunk, slot],
                recv_sem=recv_sem.at[chunk, slot],
                device_id=device,
                device_id_type=MESH,
            )

        def launch(make):
            make().start()
            sends.append(lambda: make().wait_send())

        every = tuple(range(1, place.count))

        def load():
            return pltpu.make_async_copy(place.view(src, every), own, local_sem.at[chunk])

        def across():
            return remote(0, place.view(src, every, (0,)), cross_in, place.peer(0))

        def start():
            launch(across)
            load().start()

        def fold_cross():
            load().wait()
            across().wait_recv()
            add_into(own, cross_in)

        steps, before = [start], fold_cross
        slot = 1
        orders = [order[::-1] for order in hop_orders(place)]
        for depth in range(place.count - 1):
            plan = []
            for part, order in enumerate(orders):
                free = tuple(order[depth + 1 :])
                plan.append((slot + part, part, order[depth], free, later[depth]))
            slot += 2

            def hop(slot, part, bit, free, buffer):
                view = place.view(own, free, (bit,), place.part(part), skip=(0,))
                return remote(slot, view, buffer.at[part], place.peer(bit))

            def go(plan=plan, before=before, hop=hop):
                before()
                for item in plan:
                    launch(lambda item=item: hop(*item))

            def fold(plan=plan, hop=hop):
                for item in plan:
                    hop(*item).wait_recv()
                    _, part, _, free, buffer = item
                    kept = place.view(own, free, (), place.part(part), skip=(0,))
                    add_into(kept, buffer.at[part])

            steps.append(go)
            before = fold

        def along(step, slot=slot):
            to = lax.rem(fs + step, n_fs)
            view = place.view(own, z=to, skip=(0,))
            return remote(slot + step - 1, view, last.at[step - 1], (place.dp, to))

        def spread(before=before):
            before()
            for step in range(1, n_fs):
                launch(lambda step=step: along(step))

        def finish():
            total = place.view(own, z=fs, skip=(0,))[...].astype(F32)
            for step in range(1, n_fs):
                along(step).wait_recv()
                total = total + last[step - 1].astype(F32)
            emit(chunk, total)

        return steps + [spread, finish]

    return [stages(chunk) for chunk in range(len(sources))], sends


def block_scratch(n_dp, n_fs, blocks, tail):
    hops = (n_dp - 1).bit_length() - 1
    out = []
    for count in blocks:
        entry = (count,) + tail
        zone = (2,) * hops + (n_fs,) + entry
        out += [pltpu.VMEM(zone, BF16), pltpu.VMEM(zone, BF16), pltpu.VMEM((n_fs - 1,) + entry, BF16)]
        for depth in range(hops):
            out.append(pltpu.VMEM((2,) + (2,) * (hops - 1 - depth) + (n_fs // 2,) + entry, BF16))
    return out


def block_sems(n_dp, n_fs, chunks):
    count = copy_count(n_dp, n_fs)
    return [
        pltpu.SemaphoreType.DMA((chunks, count)),
        pltpu.SemaphoreType.DMA((chunks, count)),
        pltpu.SemaphoreType.DMA((chunks,)),
    ]


TILE = 512
STATES = 32
TAPS = 15
REACH = 8
EPSILON = 1e-05
CHUNK = 256
ROWS = 128
VMEM_LIMIT = 60 << 20
TAP_ROW = 24
RATE = 40
MAP_IN = 72
MAP_OUT = 104
TABLE = 136


def sigmoid(v):
    return 0.5 * jnp.tanh(0.5 * v) + 0.5


def dot_nn(a, b):
    return jnp.dot(a, b, preferred_element_type=F32)


def dot_nt(a, b):
    return lax.dot_general(a, b, (((1,), (1,)), ((), ())), preferred_element_type=F32)


def dot_tn(a, b):
    return lax.dot_general(a, b, (((0,), (0,)), ((), ())), preferred_element_type=F32)


def norm_parts(v):
    centered = v - jnp.mean(v, axis=-1, keepdims=True)
    inv = lax.rsqrt(jnp.mean(centered * centered, axis=-1, keepdims=True) + EPSILON)
    return centered * inv, inv


def norm_back(grad, e, inv, gain):
    d = grad * gain
    return (
        d - jnp.mean(d, axis=-1, keepdims=True) - e * jnp.mean(d * e, axis=-1, keepdims=True)
    ) * inv


def fold8(v):
    return jnp.sum(v.reshape((v.shape[0] // 8, 8, v.shape[1])), axis=0)


def by_rows(body, rows=TILE, step=ROWS):
    def run(at, _):
        body(pl.ds(pl.multiple_of(at * step, step), step))
        return 0

    lax.fori_loop(0, rows // step, run, 0)


def columns(at, width=CHUNK):
    return pl.ds(pl.multiple_of(at * width, width), width)


def fill_halo(padded, flags, tiles):
    pitch = TILE + 2 * REACH
    for at in range(tiles):
        base = at * pitch
        if at == 0:
            padded[:, base : base + REACH, :] = jnp.zeros_like(padded[:, base : base + REACH, :])
        if at == tiles - 1:
            end = base + REACH + TILE
            padded[:, end : end + REACH, :] = jnp.zeros_like(padded[:, end : end + REACH, :])
        else:
            keep = flags[at + 1]
            end = base + REACH + TILE
            padded[:, end : end + REACH, :] = (
                padded[:, base + pitch + REACH : base + pitch + 2 * REACH, :] * keep
            )
            padded[:, base + pitch : base + pitch + REACH, :] = (
                padded[:, end - REACH : end, :] * keep
            )


def taps_over(padded, table_ref, store, tiles, reverse, block=64):
    pitch = TILE + 2 * REACH
    per = TILE // block
    lanes = padded.shape[0]
    for lane in range(lanes):
        weights = [
            jnp.broadcast_to(
                table_ref[TAP_ROW + k : TAP_ROW + k + 1, lane * 128 : lane * 128 + 128], (block, 128)
            )
            for k in range(TAPS)
        ]

        def run(at, _):
            tile, inner = at // per, at % per
            base = tile * pitch + inner * block
            total = jnp.zeros((block, 128), F32)
            for k in range(TAPS):
                shift = REACH + (TAPS // 2 - k if reverse else k - TAPS // 2)
                total = total + weights[k] * padded[lane, pl.ds(base + shift, block), :]
            store(lane, tile * TILE + inner * block, base, total)
            return 0

        lax.fori_loop(0, tiles * per, run, 0)


def small_exp(v):
    return 1.0 + v * (1.0 + v * (0.5 + v * (1.0 / 6 + v * (1.0 / 24 + v * (1.0 / 120)))))


def small_expm1_over(v):
    return 1.0 + v * (
        0.5 + v * (1.0 / 6 + v * (1.0 / 24 + v * (1.0 / 120 + v * (1.0 / 720 + v * (1.0 / 5040)))))
    )


def state_terms(table_ref):
    log_decay = -jnp.exp(table_ref[RATE : RATE + STATES, :])
    root = jnp.sqrt(-2.0 * log_decay * small_expm1_over(2.0 * log_decay))
    maps_in = table_ref[MAP_IN : MAP_IN + STATES, :]
    maps_out = table_ref[MAP_OUT : MAP_OUT + STATES, :]
    return log_decay, small_exp(log_decay), root, maps_in, maps_out


def ref_rows(ref):
    return ref.reshape((ref.shape[0] * ref.shape[1], ref.shape[2]))


PIECE = 16
WIDTH = 512


def cols_of(ref, first, at):
    per = WIDTH // CHUNK
    part = ref[:, first + lax.div(at, per), :, columns(lax.rem(at, per))]
    return part.reshape((ref.shape[0] * PIECE, CHUNK))


def rows_of(ref, first, at):
    groups = WIDTH // (4 * PIECE)
    part = ref[pl.ds(at * groups, groups), first : first + 4]
    return part.reshape((WIDTH, WIDTH))


def bias_of(ref, layer, at):
    row = 8 * layer + 2 * at
    return jnp.concatenate([ref[pl.ds(row, 1), :], ref[pl.ds(row + 1, 1), :]], axis=1)


def square_of(ref, at):
    return ref[:, at].reshape((ref.shape[0] * PIECE, WIDTH))


def store_wide(out, first, acc):
    def run(group, _):
        rows = pl.ds(pl.multiple_of(group * PIECE, PIECE), PIECE)
        for k in range(acc.shape[1] // WIDTH):
            out[group, first + k] = acc[rows, k * WIDTH : k * WIDTH + WIDTH].astype(BF16)
        return 0

    lax.fori_loop(0, acc.shape[0] // PIECE, run, 0)


def store_tall(out, first, acc):
    def run(group, _):
        rows = pl.ds(pl.multiple_of(group * 4 * PIECE, 4 * PIECE), 4 * PIECE)
        out[group, first : first + 4] = acc[rows, :].astype(BF16).reshape((4, PIECE, WIDTH))
        return 0

    lax.fori_loop(0, acc.shape[0] // (4 * PIECE), run, 0)


def flat_groups(ref):
    count = 1
    for n in ref.shape[:-3]:
        count *= n
    return ref.reshape((count,) + ref.shape[-3:])


def carries(offsets_ref, counts_ref, tiles):
    out = []
    for tile in range(tiles):
        begins = jnp.int32(0)
        for slot in range(offsets_ref.shape[1]):
            here = (offsets_ref[0, slot] == tile * TILE) & (slot < counts_ref[0])
            begins = jnp.maximum(begins, here.astype(jnp.int32))
        out.append((1 - begins).astype(F32))
    return out


STRETCH = 16
SPREAD = PIECE * STATES


def same_channel(rows, width, per, first=0):
    shape = (rows, width)
    row = lax.rem(lax.broadcasted_iota(jnp.int32, shape, 0), PIECE)
    col = lax.broadcasted_iota(jnp.int32, shape, 1)
    if per == 1:
        return row == lax.rem(col, PIECE)
    return row == lax.div(col, per)


def split_low(v):
    high = v.astype(BF16)
    return high, (v - high.astype(F32)).astype(BF16)


def spread_states(part):
    rows = part.shape[0]
    state = lax.broadcasted_iota(jnp.int32, (STATES, SPREAD), 0)
    col = lax.broadcasted_iota(jnp.int32, (STATES, SPREAD), 1)
    pick_state = (state == lax.rem(col, STATES)).astype(F32).astype(BF16)
    wide = dot_nn(part, pick_state)
    wide = jnp.where(same_channel(rows, SPREAD, STATES), wide, 0.0)
    return jnp.sum(wide.reshape((rows // PIECE, PIECE, SPREAD)), axis=1)


def gather_states(wide):
    groups = wide.shape[0]
    full = jnp.broadcast_to(wide[:, None, :], (groups, PIECE, SPREAD)).reshape((groups * PIECE, SPREAD))
    full = jnp.where(same_channel(groups * PIECE, SPREAD, STATES), full, 0.0)
    state = lax.broadcasted_iota(jnp.int32, (SPREAD, 128), 1)
    row = lax.broadcasted_iota(jnp.int32, (SPREAD, 128), 0)
    pick_state = (state == lax.rem(row, STATES)).astype(F32).astype(BF16)
    high, low = split_low(full)
    return (dot_nn(high, pick_state) + dot_nn(low, pick_state)).T[:STATES, :]


def prepare_states(small, power, shifted, weight):
    groups = small.shape[0]
    entries = lambda first: small[:, :, first : first + STATES].reshape((groups * PIECE, STATES))
    log_decay = -jnp.exp(spread_states(entries(RATE)))
    root = jnp.sqrt(-2.0 * log_decay * small_expm1_over(2.0 * log_decay))
    both = spread_states(entries(MAP_IN)) * root * spread_states(entries(MAP_OUT))
    weight[...] = both
    col = lax.broadcasted_iota(jnp.int32, (SPREAD, 128), 1)
    row = lax.broadcasted_iota(jnp.int32, (SPREAD, 128), 0)
    add_states = (col == lax.div(row, STATES)).astype(F32).astype(BF16)
    power[0] = jnp.ones_like(both)
    decay = small_exp(log_decay)
    for m in range(1, STRETCH):
        power[m] = power[m - 1] * decay
    halves = []
    for half in range(2):
        total = jnp.zeros((groups, 128), F32)
        for k in range(8):
            high, low = split_low(power[half * 8 + k] * both)
            lag = dot_nn(high, add_states) + dot_nn(low, add_states)
            total = total + (pltpu.roll(lag, k * PIECE, 1) if k else lag)
        halves.append(total)
    blank = jnp.zeros((groups, 256), F32)
    padded = jnp.concatenate([blank] + halves, axis=1)
    for m in range(STRETCH):
        shifted[m] = pltpu.roll(padded, 512 - (m + 1) * PIECE, 1)[:, :256]


def group_weights(power, shifted, group, decay_w, lag_w):
    mask = same_channel(PIECE, SPREAD, STATES)
    lag_mask = same_channel(PIECE, 256, 1)
    for m in range(STRETCH):
        rows = slice(m * PIECE, m * PIECE + PIECE)
        line = jnp.broadcast_to(power[m, pl.ds(group, 1), :], (PIECE, SPREAD))
        decay_w[rows, :] = jnp.where(mask, line, 0.0).astype(BF16)
        line = jnp.broadcast_to(shifted[m, pl.ds(group, 1), :], (PIECE, 256))
        lag_w[rows, :] = jnp.where(lag_mask, line, 0.0).astype(BF16)


def swap_blocks(parts):
    col = lax.div(lax.broadcasted_iota(jnp.int32, parts[0].shape, 1), PIECE)
    parts = list(parts)
    for distance in (1, 2, 4):
        low = lax.rem(lax.div(col, distance), 2) == 0
        shift = distance * PIECE
        for a in range(8):
            if a & distance:
                continue
            first, second = parts[a], parts[a + distance]
            parts[a] = jnp.where(low, first, pltpu.roll(second, shift, 1))
            parts[a + distance] = jnp.where(low, pltpu.roll(first, 128 - shift, 1), second)
    return parts


SLAB = 32
TOGETHER = 4


def to_blocks(load, out, blocks, backward):
    for slab in range(blocks // SLAB):
        rows = slice(slab * SLAB, slab * SLAB + SLAB)
        for half in range(2):
            parts = []
            for k in range(8):
                frame = half * 8 + k
                frame = STRETCH - 1 - frame if backward else frame
                parts.append(load(slab * SLAB * STRETCH + frame))
            for group, part in enumerate(swap_blocks(parts)):
                out[group, rows, half * 128 : half * 128 + 128] = part.astype(out.dtype)


def from_blocks(store, ref, blocks, backward):
    for slab in range(blocks // SLAB):
        rows = slice(slab * SLAB, slab * SLAB + SLAB)
        for half in range(2):
            parts = [ref[group, rows, half * 128 : half * 128 + 128] for group in range(8)]
            for k, part in enumerate(swap_blocks(parts)):
                frame = half * 8 + k
                frame = STRETCH - 1 - frame if backward else frame
                store(slab * SLAB * STRETCH + frame, part)


def block_powers(decay):
    q2 = decay * decay
    q4 = q2 * q2
    q8 = q4 * q4
    one = q8 * q8
    two = one * one
    four = two * two
    return one, two, four


def row_powers(one, count=8):
    rows = [one]
    for _ in range(count - 1):
        rows.append(rows[-1] * one)
    return rows


def scan_blocks(source, into, decay, keeps, per, reverse):
    blocks, width = source.shape
    one, two, four = block_powers(decay)
    row = lax.broadcasted_iota(jnp.int32, (8, width), 0)
    if reverse:
        row = 7 - row
    factors = []
    for distance, power in ((1, one), (2, two), (4, four)):
        line = jnp.broadcast_to(power, (8, width))
        factors.append((8 - distance if reverse else distance, jnp.where(row >= distance, line, 0.0)))
    entering = jnp.ones((8, width), F32)
    for bit, power in ((1, one), (2, two), (4, four)):
        line = jnp.broadcast_to(power, (8, width))
        entering = jnp.where(lax.rem(lax.div(row, bit), 2) == 1, entering * line, entering)
    eight = jnp.broadcast_to(four * four, (8, width))
    carry = jnp.zeros((8, width), F32)
    tiles = blocks // 8
    for k in range(tiles):
        tile = tiles - 1 - k if reverse else k
        edge = (tile + 1) * 8 if reverse else tile * 8
        if k and edge % per == 0:
            carry = carry * keeps[edge // per]
        x = source[tile * 8 : tile * 8 + 8, :]
        for shift, factor in factors:
            x = x + factor * pltpu.roll(x, shift, 0)
        moved = pltpu.roll(x, 7 if reverse else 1, 0)
        into[tile * 8 : tile * 8 + 8, :] = jnp.where(row >= 1, moved, 0.0) + entering * carry
        end = x[0:1, :] if reverse else x[7:8, :]
        carry = jnp.broadcast_to(end, (8, width)) + eight * carry


def mix_forward(u_ref, y_ref, power, shifted, weight, keeps, ub_out, state_out, blk_in, blk_out, decay_w, lag_w, t_scr, h_scr):
    lanes, frames, _ = u_ref.shape
    blocks = frames // STRETCH
    count = decay_w.shape[0]
    several = range(count)

    def lane_tile(lane, _):
        to_blocks(lambda at: u_ref[lane, pl.ds(at, SLAB, stride=STRETCH), :], blk_in, blocks, True)

        def some_groups(k, _):
            place = [k * count + n for n in several]
            groups = [lane * 8 + at for at in place]
            for n in several:
                group_weights(power, shifted, groups[n], decay_w.at[n], lag_w.at[n])
            for n in several:
                ub_out[groups[n]] = blk_in[place[n]]
                t_scr[n] = dot_nn(blk_in[place[n]], decay_w[n])
            for n in several:
                decay = power[1, pl.ds(groups[n], 1), :]
                scan_blocks(t_scr.at[n], h_scr.at[n], decay, keeps, TILE // STRETCH, False)
            for n in several:
                decay = power[1, pl.ds(groups[n], 1), :]
                state = h_scr[n]
                state_out[groups[n]] = state.astype(BF16)
                out = (state * (weight[pl.ds(groups[n], 1), :] * decay)).astype(BF16)
                blk_out[place[n]] = dot_nn(blk_in[place[n]], lag_w[n]) + dot_nt(out, decay_w[n])
            return 0

        lax.fori_loop(0, 8 // count, some_groups, 0)

        def store(at, values):
            y_ref[lane, pl.ds(at, SLAB, stride=STRETCH), :] = values

        from_blocks(store, blk_out, blocks, False)
        return 0

    lax.fori_loop(0, lanes, lane_tile, 0)


def mix_backward(
    lane, u_ref, grad, skip, u_tile, u_sem, power, shifted, weight, keeps, ub_ref, state_ref, lags, sums,
    frames_scr, blk_in, blk_out, decay_w, lag_w, stack_scr, e_scr, r_scr,
):
    blocks = frames_scr.shape[2]
    count = decay_w.shape[0]
    several = range(count)
    lanes = u_ref.shape[0]
    copy = lambda at: pltpu.make_async_copy(u_ref.at[at], u_tile, u_sem)
    copy(lane).wait()
    for at in range(STRETCH):
        for slab in range(blocks // SLAB):
            rows = slice(slab * SLAB, slab * SLAB + SLAB)
            first = pl.ds(slab * SLAB * STRETCH + at, SLAB, stride=STRETCH)
            frames_scr[0, at, rows, :] = u_tile[first, :]
            frames_scr[1, at, rows, :] = grad[lane, first, :]

    @pl.when(lane + 1 < lanes)
    def _():
        copy(lane + 1).start()

    def one_lag(lag, _):
        def one_frame(at, total):
            for slab in range(blocks // SLAB):
                rows = slice(slab * SLAB, slab * SLAB + SLAB)
                total = total + frames_scr[1, at, rows, :] * frames_scr[0, at - lag, rows, :]
            return total

        total = lax.fori_loop(lag, STRETCH, one_frame, jnp.zeros((SLAB, 128), F32))
        lags[lane, pl.ds(lag, 1), :] = jnp.sum(total, axis=0, keepdims=True)
        return 0

    lax.fori_loop(0, STRETCH, one_lag, 0)
    for slab in range(blocks // SLAB):
        rows = slice(slab * SLAB, slab * SLAB + SLAB)
        for half in range(2):
            parts = [frames_scr[1, half * 8 + k, rows, :] for k in range(8)]
            for group, part in enumerate(swap_blocks(parts)):
                blk_in[group, rows, half * 128 : half * 128 + 128] = part.astype(BF16)
    position = lax.div(lax.broadcasted_iota(jnp.int32, (1, 256), 1), PIECE).astype(F32)

    def some_groups(k, _):
        place = [k * count + n for n in several]
        groups = [lane * 8 + at for at in place]
        for n in several:
            group_weights(power, shifted, groups[n], decay_w.at[n], lag_w.at[n])
        for n in several:
            gy = blk_in[place[n]]
            stack_scr[n, 0:blocks, :] = gy
            stack_scr[n, blocks : 2 * blocks, :] = (gy.astype(F32) * (position + 1.0)).astype(BF16)
            stack_scr[n, 2 * blocks :, :] = (ub_ref[groups[n]].astype(F32) * position).astype(BF16)
        for n in several:
            e_scr[n] = dot_nn(stack_scr[n], decay_w[n])
        for n in several:
            decay = power[1, pl.ds(groups[n], 1), :]
            own = e_scr.at[n, pl.ds(0, blocks)]
            own[...] = own[...] * decay
            scan_blocks(own, r_scr.at[n], decay, keeps, TILE // STRETCH, True)
        for n in several:
            group = groups[n]
            inverse = 1.0 / power[1, pl.ds(group, 1), :]
            last = 16.0 * power[15, pl.ds(group, 1), :]
            first, second = jnp.zeros((8, SPREAD), F32), jnp.zeros((8, SPREAD), F32)
            for at in range(blocks // 8):
                rows = slice(at * 8, at * 8 + 8)
                state = state_ref[group, rows, :].astype(F32)
                turn = e_scr[n, 2 * blocks + at * 8 : 2 * blocks + at * 8 + 8, :]
                first = first + state * e_scr[n, rows, :]
                second = second + state * e_scr[n, blocks + at * 8 : blocks + at * 8 + 8, :]
                second = second + r_scr[n, rows, :] * (turn * inverse + last * state)
            sums[0, pl.ds(group, 1), :] = jnp.sum(first, axis=0, keepdims=True)
            sums[1, pl.ds(group, 1), :] = jnp.sum(second, axis=0, keepdims=True)
            out = (r_scr[n] * weight[pl.ds(group, 1), :]).astype(BF16)
            blk_out[place[n]] = dot_nt(blk_in[place[n]], lag_w[n]) + dot_nt(out, decay_w[n])
        return 0

    lax.fori_loop(0, 8 // count, some_groups, 0)

    def store(at, values):
        slab, frame = at // (SLAB * STRETCH), at % STRETCH
        through = frames_scr[1, frame, slab * SLAB : slab * SLAB + SLAB, :]
        grad[lane, pl.ds(at, SLAB, stride=STRETCH), :] = values + skip[pl.ds(lane, 1), :] * through

    from_blocks(store, blk_out, blocks, True)


def mix_gradients(lags, sums, table_ref):
    _, decay, root, maps_in, maps_out = state_terms(table_ref)
    coupling = maps_in * root * maps_out
    gmap = gather_states(sums[0])
    gdecay = gather_states(sums[1])
    power = jnp.ones_like(decay)
    for lag in range(STRETCH):
        line = jnp.concatenate([lags[k, lag : lag + 1, :] for k in range(lags.shape[0])], axis=1)
        if lag:
            gdecay = gdecay + float(lag) * power * line
            power = power * decay
        gmap = gmap + power * line
    return gmap, gdecay * coupling


def pack_small(out, scr, place, bias_ref, gains, shifts, conv_bias, taps, rate, maps):
    own = gains.shape[1]
    scr[...] = jnp.zeros_like(scr)
    scr[0:6, :own] = gains[...].astype(F32)
    scr[6:18, :own] = shifts[...].astype(F32)
    scr[18:19, :own] = conv_bias[...].astype(F32)
    scr[TAP_ROW : TAP_ROW + TAPS, :own] = taps[...].astype(F32)
    out[:, :CHUNK] = scr[...].T[:own, :].astype(BF16)
    out[:, RATE:MAP_IN] = rate[...]
    out[:, MAP_IN:MAP_OUT] = maps[0]
    out[:, MAP_OUT:TABLE] = maps[1]
    count = bias_ref.shape[1]
    row = lax.div(place * count, CHUNK)
    inner = place * count - row * CHUNK
    at_row = lax.broadcasted_iota(jnp.int32, (PIECE, CHUNK), 0)
    wide = jnp.zeros((PIECE, CHUNK), F32)
    for layer in range(2):
        line = jnp.broadcast_to(bias_ref[layer : layer + 1, :].astype(F32), (8, count))
        line = jnp.concatenate([line, jnp.zeros((8, CHUNK - count), F32)], axis=1)
        line = pltpu.roll(line, inner, 1)
        wide = wide + jnp.where(at_row == 8 * layer + row, jnp.broadcast_to(line[0:1], wide.shape), 0.0)
    out[:, CHUNK:] = wide.astype(BF16)


def front_kernel(mesh_size, *refs):
    fused = mesh_size is not None
    refs = list(refs)
    take = lambda count: [refs.pop(0) for _ in range(count)]
    offsets_ref, counts_ref, x_ref = take(3)
    if fused:
        n_dp, n_fs = mesh_size
        small_in = take(7)
        up_s, down_s, mixin_s, mixout_s, convin_s, convout_s = take(6)
    else:
        first_v, extra_v, second_v, third_v, table_in, bias_in = take(6)
    (
        h_out,
        x1_out,
        v_out,
        y_out,
        gated_out,
        x2_out,
        p_out,
        u_out,
        w_out,
        stat_out,
        table_ref,
        bias_ref,
        ub_out,
        state_out,
        power,
        shifted,
        weight,
    ) = take(17)
    gathered = take(5) if fused else []
    x1_scr, low_all, low_scr, sum_scr, y_all, padded, act_all = take(7)
    mix_scr = take(6)
    step = pl.program_id(0)
    channels = x_ref.shape[1]
    frames = w_out.shape[0]
    tiles = frames // TILE
    lanes = channels // 128
    gain = lambda k: table_ref[k : k + 1, :]
    shift = lambda k: table_ref[6 + k : 7 + k, :]
    here = lambda rows, tile: pl.ds(pl.multiple_of(tile * TILE + rows.start, ROWS), ROWS)
    flags = carries(offsets_ref, counts_ref, tiles)
    mix_at, last_step = 3 * tiles, 4 * tiles + 1
    if fused:
        landing = take(4)
        sources = take(5)
        turn_scr = refs.pop(0)
        sems = take(3)
        load_sem = refs.pop(0)
        swap = take(4)
        dp, fs = lax.axis_index("dp"), lax.axis_index("fsdp")
        place = Place(dp, fs, n_dp, n_fs)
        landing.append(gathered[4])
        plans, sends = block_gather(place, sources, landing, *sems)
        first_v, extra_v, second_v, third_v = [flat_groups(r) for r in landing[:4]]

        def keep_copy(chunk):
            return pltpu.make_async_copy(landing[chunk], gathered[chunk], load_sem.at[chunk])

        def run(*stages):
            for chunk, stage in stages:
                plans[chunk][stage]()

        @pl.when(step == 0)
        def _():
            pack_small(sources[0].at[0], turn_scr, dp * n_fs + fs, *small_in)
            for k in range(4):
                cols = slice(k * WIDTH, k * WIDTH + WIDTH)
                if k < 2:
                    sources[0][1 + k] = up_s[0, :, cols]
                else:
                    sources[1][k - 2] = up_s[0, :, cols]
                sources[4][1 + k] = up_s[1, :, cols]
                rows = slice(k * PIECE, k * PIECE + PIECE)
                sources[2][k] = down_s[0, rows, :]
                sources[4][5 + k] = down_s[1, rows, :]
            for k in range(2):
                cols = slice(k * WIDTH, k * WIDTH + WIDTH)
                sources[3][k] = mixin_s[:, cols]
                sources[3][3 + k] = convin_s[:, cols]
            sources[3][2] = mixout_s[...]
            sources[4][0] = convout_s[...]
            greet(dp, fs, n_dp, n_fs)
            run((0, 0), (1, 0), (0, 1), (2, 0), (1, 1), (0, 2), (1, 2), (0, 3), (2, 1), (0, 4))
            table_ref[...] = first_v[:, 0, :, :CHUNK].reshape((channels, CHUNK)).astype(F32).T[:TABLE, :]
            total = first_v[0, 0, :, CHUNK:].astype(F32)
            for k in range(1, n_dp * n_fs):
                total = total + first_v[k, 0, :, CHUNK:].astype(F32)
            bias_ref[...] = total

        rest = {1: [(1, 3), (3, 0)], 2: [(2, 2)], tiles: [(1, 4), (4, 0)], tiles + 1: [(2, 3), (3, 1)]}
        rest.update({2 * tiles: [(2, 4), (3, 2)], 2 * tiles + 1: [(3, 3)]})
        rest.update({mix_at: [(3, 4), (4, 1)], mix_at + 1: [(4, 2)], mix_at + 2: [(4, 3)]})
        rest[last_step] = [(4, 4)]
        for at, stages in rest.items():

            @pl.when(step == at)
            def _(at=at, stages=stages):
                run(*stages)
                if at == mix_at:
                    for chunk in range(4):
                        keep_copy(chunk).start()
                if at == last_step:
                    for chunk in range(4):
                        keep_copy(chunk).wait()
                    for wait in sends:
                        wait()

    else:

        @pl.when(step == 0)
        def _():
            table_ref[...] = table_in[...]
            bias_ref[...] = bias_in[...]

    @pl.when(step < tiles)
    def _():
        def first(rows):
            e, _ = norm_parts(x_ref[rows, :].astype(F32))
            low_all[here(rows, step), :] = (e * gain(0) + shift(0)).astype(BF16)

        by_rows(first)

    for half, part in enumerate((first_v, extra_v)):

        @pl.when((step >= half * tiles) & (step < half * tiles + tiles))
        def _(half=half, part=part):
            tile_rows = pl.ds(pl.multiple_of((step - half * tiles) * TILE, TILE), TILE)
            for k in range(2):
                c = 2 * half + k
                h = dot_nn(low_all[tile_rows, :], square_of(part, 1 - half + k))
                h = h + bias_of(bias_ref, 0, c)
                h_out[:, k * WIDTH : k * WIDTH + WIDTH] = h.astype(BF16)
                active = (h * sigmoid(h)).astype(BF16)
                act_all[tile_rows, c * WIDTH : c * WIDTH + WIDTH] = active

    @pl.when((step >= 2 * tiles) & (step < mix_at))
    def _():
        at = step - 2 * tiles
        tile_rows = pl.ds(pl.multiple_of(at * TILE, TILE), TILE)
        total = dot_nn(act_all[tile_rows, :WIDTH], rows_of(second_v, 0, 0))
        for c in range(1, 4):
            cols = slice(c * WIDTH, c * WIDTH + WIDTH)
            total = total + dot_nn(act_all[tile_rows, cols], rows_of(second_v, 0, c))
        sum_scr[...] = total

        def second(rows):
            x1 = x_ref[rows, :].astype(F32) + 0.5 * (sum_scr[rows, :] + shift(6))
            x1_out[rows, :] = x1
            x1_scr[here(rows, at), :] = x1
            e, _ = norm_parts(x1)
            low_all[here(rows, at), :] = (e * gain(1) + shift(1)).astype(BF16)

        by_rows(second)

    @pl.when(step == mix_at)
    def _():
        prepare_states(first_v[:, 0, :, :CHUNK], power, shifted, weight)

        def project(tile, _):
            rows = pl.ds(pl.multiple_of(tile * TILE, TILE), TILE)
            u = dot_nn(low_all[rows, :], square_of(third_v, 0))
            for lane in range(lanes):
                u_out[lane, rows, :] = u[:, lane * 128 : lane * 128 + 128]
            return 0

        lax.fori_loop(0, tiles, project, 0)
        mix_forward(u_out, y_all, power, shifted, weight, flags, ub_out, state_out, *mix_scr)

    @pl.when((step > mix_at) & (step < last_step))
    def _():
        at = step - mix_at - 1
        whole_tile = pl.ds(pl.multiple_of(at * TILE, TILE), TILE)
        v_out[...] = dot_nn(low_all[whole_tile, :], square_of(third_v, 1)).astype(BF16)

        def gate(rows):
            join = lambda ref: jnp.concatenate([ref[lane, here(rows, at), :] for lane in range(lanes)], axis=1)
            y = join(y_all) + shift(11) * join(u_out)
            v = v_out[rows, :].astype(F32)
            y_out[rows, :] = y.astype(BF16)
            gated_out[rows, :] = (y * (v * sigmoid(v))).astype(BF16)

        by_rows(gate)
        sum_scr[...] = dot_nn(gated_out[...], square_of(third_v, 2))

        def third(rows):
            x2 = x1_scr[here(rows, at), :] + (sum_scr[rows, :] + shift(8))
            x2_out[rows, :] = x2
            e, _ = norm_parts(x2)
            low_scr[rows, :] = (e * gain(2) + shift(2)).astype(BF16)

        by_rows(third)
        pitch = TILE + 2 * REACH

        def widen(c, _):
            cols = columns(c)
            right = columns(c + channels // CHUNK)
            left_part = dot_nn(low_scr[...], cols_of(third_v, 3, c)) + table_ref[15:16, cols]
            right_part = dot_nn(low_scr[...], cols_of(third_v, 4, c)) + table_ref[16:17, cols]
            p_out[:, cols] = left_part.astype(BF16)
            p_out[:, right] = right_part.astype(BF16)
            g = left_part * sigmoid(right_part)
            place = pl.ds(pl.multiple_of(at * pitch + REACH, 8), TILE)
            for k in range(CHUNK // 128):
                padded[c * (CHUNK // 128) + k, place, :] = g[:, k * 128 : k * 128 + 128]
            return 0

        lax.fori_loop(0, channels // CHUNK, widen, 0)

    @pl.when(step == last_step)
    def _():
        fill_halo(padded, flags, tiles)

        def store(lane, row, base, total):
            w_out[pl.ds(pl.multiple_of(row, 64), 64), lane * 128 : lane * 128 + 128] = total

        taps_over(padded, table_ref, store, tiles, False)
        stat_out[...] = jnp.zeros_like(stat_out)

        def total(at, _):
            rows = pl.ds(pl.multiple_of(at * ROWS, ROWS), ROWS)
            stat_out[...] += fold8(w_out[rows, :])
            return 0

        lax.fori_loop(0, frames // ROWS, total, 0)
        center = jnp.sum(stat_out[...], axis=0, keepdims=True) * (1.0 / frames)
        stat_out[...] = jnp.zeros_like(stat_out)

        def spread(at, _):
            rows = pl.ds(pl.multiple_of(at * ROWS, ROWS), ROWS)
            off = w_out[rows, :] - center
            stat_out[...] += fold8(off * off)
            return 0

        lax.fori_loop(0, frames // ROWS, spread, 0)
        around = jnp.sum(stat_out[...], axis=0, keepdims=True)
        if fused:
            center, around = pool_over(center, around, frames, dp, fs, n_dp, n_fs, *swap)
            around = lax.rsqrt(around * (1.0 / (frames * n_dp * n_fs)) + EPSILON)
        stat_out[...] = jnp.zeros_like(stat_out)
        stat_out[0:1, :] = center
        stat_out[1:2, :] = around


def whole(shape):
    zeros = (0,) * len(shape)
    return pl.BlockSpec(shape, lambda *_: zeros, pipeline_mode=pl.Buffered(1))


def params(collective_id=None):
    if collective_id is None:
        return pltpu.CompilerParams(
            dimension_semantics=("arbitrary",), vmem_limit_bytes=VMEM_LIMIT
        )
    return pltpu.CompilerParams(
        dimension_semantics=("arbitrary",),
        vmem_limit_bytes=VMEM_LIMIT,
        collective_id=collective_id,
        has_side_effects=True,
    )


SMEM_SPEC = pl.BlockSpec(memory_space=pltpu.SMEM)
HBM_SPEC = pl.BlockSpec(memory_space=pltpu.HBM)


def front(mesh_size, offsets, counts, x, small, weights, hidden, collective_id=None):
    fused = mesh_size is not None
    frames, channels = x.shape
    tiles = frames // TILE
    clip = lambda i, first: jnp.clip(i - first, 0, tiles - 1)
    twice = lambda i: (jnp.where(i < tiles, i, jnp.where(i < 2 * tiles, tiles - 1, clip(i, 2 * tiles))), 0)
    halves = lambda i: (jnp.where(i < tiles, i, clip(i, tiles)), jnp.where(i < tiles, 0, 1))
    place = lambda i: clip(i, 3 * tiles + 1)
    late = lambda width: pl.BlockSpec((TILE, width), lambda i: (place(i), 0))
    shape = lambda width, kind: jax.ShapeDtypeStruct((frames, width), kind)
    groups, blocks = channels // PIECE, frames // STRETCH
    out_shape = [
        shape(hidden, BF16),
        shape(channels, F32),
        shape(channels, BF16),
        shape(channels, BF16),
        shape(channels, BF16),
        shape(channels, F32),
        shape(2 * channels, BF16),
        jax.ShapeDtypeStruct((channels // 128, frames, 128), F32),
        shape(channels, F32),
        jax.ShapeDtypeStruct((8, channels), F32),
        jax.ShapeDtypeStruct((TABLE, channels), F32),
        jax.ShapeDtypeStruct((16, CHUNK), F32),
        jax.ShapeDtypeStruct((groups, blocks, STRETCH * PIECE), BF16),
        jax.ShapeDtypeStruct((groups, blocks, SPREAD), BF16),
        jax.ShapeDtypeStruct((STRETCH, groups, SPREAD), F32),
        jax.ShapeDtypeStruct((STRETCH, groups, STRETCH * PIECE), F32),
        jax.ShapeDtypeStruct((groups, SPREAD), F32),
    ]
    out_specs = [
        pl.BlockSpec((TILE, hidden // 2), halves),
        pl.BlockSpec((TILE, channels), lambda i: (clip(i, 2 * tiles), 0)),
    ]
    out_specs += [late(channels)] * 4 + [late(2 * channels)]
    out_specs += [whole(s.shape) for s in out_shape[7:]]
    scratch = [
        pltpu.VMEM((frames, channels), F32),
        pltpu.VMEM((frames, channels), BF16),
        pltpu.VMEM((TILE, channels), BF16),
        pltpu.VMEM((TILE, channels), F32),
        pltpu.VMEM((channels // 128, frames, 128), F32),
        pltpu.VMEM((channels // 128, tiles * (TILE + 2 * REACH), 128), F32),
        pltpu.VMEM((frames, hidden), BF16),
        pltpu.VMEM((8, blocks, STRETCH * PIECE), BF16),
        pltpu.VMEM((8, blocks, STRETCH * PIECE), F32),
        pltpu.VMEM((TOGETHER, STRETCH * PIECE, SPREAD), BF16),
        pltpu.VMEM((TOGETHER, STRETCH * PIECE, STRETCH * PIECE), BF16),
        pltpu.VMEM((TOGETHER, blocks, SPREAD), F32),
        pltpu.VMEM((TOGETHER, blocks, SPREAD), F32),
    ]
    operands = (weights if not fused else small + weights) + (small if not fused else [])
    if fused:
        layout = block_layout(*mesh_size)
        blocks = (3, 2, 4, 5, 9)
        chunks = [jax.ShapeDtypeStruct(layout + (k, PIECE, WIDTH), BF16) for k in blocks]
        out_shape += chunks
        out_specs += [HBM_SPEC] * len(chunks)
        scratch += [pltpu.VMEM(c.shape, BF16) for c in chunks[:4]]
        scratch += [pltpu.VMEM((k, PIECE, WIDTH), BF16) for k in blocks]
        scratch += [pltpu.VMEM((CHUNK, 128), F32)]
        scratch += block_sems(*mesh_size, len(chunks)) + [pltpu.SemaphoreType.DMA((4,))]
        scratch += swap_scratch(*mesh_size, channels)
    return pl.pallas_call(
        partial(front_kernel, mesh_size),
        grid=(4 * tiles + 2,),
        in_specs=[SMEM_SPEC, SMEM_SPEC, pl.BlockSpec((TILE, channels), twice)] + [whole(a.shape) for a in operands],
        out_specs=out_specs,
        out_shape=out_shape,
        scratch_shapes=scratch,
        compiler_params=params(collective_id),
        name="front",
    )(offsets, counts, x, *operands)


def middle_kernel(
    mesh_size,
    x2_ref,
    w_ref,
    cot_ref,
    blocks_ref,
    bias_ref,
    vec_ref,
    stat_ref,
    out_ref,
    gx3_ref,
    gnb_ref,
    gblocks_out,
    gbias_out,
    gvec_out,
    stat_out,
    up_acc,
    down_acc,
    convout_acc,
    bias_acc,
    vec_acc,
    h_scr,
    low_scr,
    turn_scr,
    act_scr,
    grad_scr,
    sum_scr,
    x3_scr,
    *swap,
):
    at = pl.program_id(0)
    tiles = pl.num_programs(0)
    channels = x2_ref.shape[1]
    if mesh_size is not None:
        n_dp, n_fs = mesh_size
        dp, fs = lax.axis_index("dp"), lax.axis_index("fsdp")

        @pl.when(at == 0)
        def _():
            greet(dp, fs, n_dp, n_fs)

    hidden = up_acc.shape[1]
    gain = lambda k: vec_ref[k : k + 1, :]
    shift = lambda k: vec_ref[6 + k : 7 + k, :]
    center, scale = stat_ref[0:1, :], stat_ref[1:2, :]

    @pl.when(at == 0)
    def _():
        for ref in (up_acc, down_acc, convout_acc, bias_acc, vec_acc):
            ref[...] = jnp.zeros_like(ref)

    def normed(rows):
        e = (w_ref[rows, :] - center) * scale
        return e, e * gain(5) + shift(5)

    def first(rows):
        _, nb = normed(rows)
        act_scr[rows, :] = (nb * sigmoid(nb)).astype(BF16)

    by_rows(first)
    sum_scr[...] = dot_nn(act_scr[...], square_of(blocks_ref, 0))

    def second(rows):
        x3 = x2_ref[rows, :] + (sum_scr[rows, :] + vec_ref[18:19, :])
        x3_scr[rows, :] = x3
        e, _ = norm_parts(x3)
        low_scr[rows, :] = (e * gain(3) + shift(3)).astype(BF16)
        sum_scr[rows, :] = jnp.zeros((ROWS, channels), F32)

    by_rows(second)

    def forward(c, _):
        cols = columns(c, WIDTH)
        h = dot_nn(low_scr[...], square_of(blocks_ref, 1 + c)) + bias_of(bias_ref, 1, c)
        h_scr[:, cols] = h
        active = (h * sigmoid(h)).astype(BF16)
        sum_scr[...] += dot_nn(active, rows_of(blocks_ref, 5, c))
        return 0

    lax.fori_loop(0, hidden // WIDTH, forward, 0)
    turn_scr[...] = low_scr[...].T

    def last(rows):
        x4 = x3_scr[rows, :] + 0.5 * (sum_scr[rows, :] + shift(7))
        e, inv = norm_parts(x4)
        out_ref[rows, :] = (e * gain(4) + shift(4)).astype(BF16)
        cot = cot_ref[rows, :].astype(F32)
        vec_acc[0] += fold8(cot * e)
        vec_acc[1] += fold8(cot)
        gx4 = norm_back(cot, e, inv, gain(4))
        gx3_ref[rows, :] = gx4
        low = (0.5 * gx4).astype(BF16)
        grad_scr[rows, :] = low
        vec_acc[2] += fold8(low.astype(F32))
        sum_scr[rows, :] = jnp.zeros((ROWS, channels), F32)

    by_rows(last)

    def backward(c, _):
        cols = columns(c, WIDTH)
        h = h_scr[:, cols]
        sig = sigmoid(h)
        active = h * sig
        gate = dot_nt(grad_scr[...], rows_of(blocks_ref, 5, c))
        grad_h = (gate * (sig * (1.0 + h - active))).astype(BF16)
        bias_acc[:, cols] += fold8(grad_h.astype(F32))
        down_acc[cols, :] += dot_tn(active.astype(BF16), grad_scr[...])
        up_acc[:, cols] += dot_nn(turn_scr[...], grad_h)
        sum_scr[...] += dot_nt(grad_h, square_of(blocks_ref, 1 + c))
        return 0

    lax.fori_loop(0, hidden // WIDTH, backward, 0)

    def fourth(rows):
        e, inv = norm_parts(x3_scr[rows, :])
        grad = sum_scr[rows, :]
        vec_acc[3] += fold8(grad * e)
        vec_acc[4] += fold8(grad)
        gx3 = gx3_ref[rows, :] + norm_back(grad, e, inv, gain(3))
        gx3_ref[rows, :] = gx3
        low = gx3.astype(BF16)
        grad_scr[rows, :] = low
        vec_acc[5] += fold8(low.astype(F32))

    by_rows(fourth)
    convout_acc[...] += dot_tn(act_scr[...], grad_scr[...])
    sum_scr[...] = dot_nt(grad_scr[...], square_of(blocks_ref, 0))

    def fifth(rows):
        e, nb = normed(rows)
        sig = sigmoid(nb)
        gnb = sum_scr[rows, :] * (sig * (1.0 + nb * (1.0 - sig)))
        gnb_ref[rows, :] = gnb
        vec_acc[6] += fold8(gnb * e)
        vec_acc[7] += fold8(gnb)

    by_rows(fifth)

    @pl.when(at == tiles - 1)
    def _():
        for k in range(8):
            gvec_out[k : k + 1, :] = jnp.sum(vec_acc[k], axis=0, keepdims=True)

        def convert():
            store_wide(gblocks_out, 0, convout_acc)
            store_wide(gblocks_out, 1, up_acc)
            store_tall(gblocks_out, 5, down_acc)
            gbias_out[...] = jnp.broadcast_to(
                jnp.sum(bias_acc[...], axis=0, keepdims=True), gbias_out.shape
            )

        stat_out[...] = stat_ref[...]
        if mesh_size is None:
            convert()
        else:
            total = sum_over(gvec_out[...], dp, fs, n_dp, n_fs, *swap, between=convert)
            share = gain(5) * (1.0 / (TILE * tiles * n_dp * n_fs))
            stat_out[2:3, :] = total[7:8, :] * share
            stat_out[3:4, :] = total[6:7, :] * share


def middle(mesh_size, x2, w, cot, blocks, bias, vec, stat, hidden, collective_id=None):
    frames, channels = x2.shape
    tiles = frames // TILE
    row = lambda width: pl.BlockSpec((TILE, width), lambda i: (i, 0))
    shapes = [
        jax.ShapeDtypeStruct((frames, channels), BF16),
        jax.ShapeDtypeStruct((frames, channels), F32),
        jax.ShapeDtypeStruct((frames, channels), F32),
        jax.ShapeDtypeStruct(blocks.shape, BF16),
        jax.ShapeDtypeStruct((8, hidden), F32),
        jax.ShapeDtypeStruct((8, channels), F32),
        jax.ShapeDtypeStruct((8, channels), F32),
    ]
    swap = [] if mesh_size is None else swap_scratch(*mesh_size, channels)
    return pl.pallas_call(
        partial(middle_kernel, mesh_size),
        grid=(tiles,),
        in_specs=[row(channels)] * 3
        + [whole(a.shape) for a in (blocks, bias, vec, stat)],
        out_specs=[row(channels)] * 3 + [whole(s.shape) for s in shapes[3:]],
        out_shape=shapes,
        scratch_shapes=[
            pltpu.VMEM((channels, hidden), F32),
            pltpu.VMEM((hidden, channels), F32),
            pltpu.VMEM((channels, channels), F32),
            pltpu.VMEM((8, hidden), F32),
            pltpu.VMEM((8, 8, channels), F32),
            pltpu.VMEM((TILE, hidden), F32),
            pltpu.VMEM((TILE, channels), BF16),
            pltpu.VMEM((channels, TILE), BF16),
            pltpu.VMEM((TILE, channels), BF16),
            pltpu.VMEM((TILE, channels), BF16),
            pltpu.VMEM((TILE, channels), F32),
            pltpu.VMEM((TILE, channels), F32),
        ]
        + swap,
        compiler_params=params(collective_id),
        name="middle",
    )(x2, w, cot, blocks, bias, vec, stat)


def back_kernel(mesh_size, *refs):
    fused = mesh_size is not None
    refs = list(refs)
    take = lambda count: [refs.pop(0) for _ in range(count)]
    offsets_ref, counts_ref, w_ref, gnb_ref, p_ref = take(5)
    x2_ref, gx3_ref, gated_ref, y_ref, v_ref, x1_ref = take(6)
    u_ref, ub_ref, state_ref, power, shifted, weight, blocks_ref, vec_ref, stat_ref = take(9)
    sources = take(1) if fused else []
    gx1_ref, gin_out, gvec_out, gtaps_ref, gmap_out, gdecay_out = take(6)
    reduced = take(2) if fused else []
    mid_ref = None if fused else refs.pop(0)
    wide_acc, mixout_acc, vec_acc, low_scr, wide_scr, sum_scr = take(6)
    padded, gpad, gv_all, lags, sums, skip, u_tile, u_sem = take(8)
    mix_scr = take(8)
    step = pl.program_id(0)
    channels = x2_ref.shape[1]
    frames = u_ref.shape[1]
    tiles = frames // TILE
    lanes = channels // 128
    pitch = TILE + 2 * REACH
    conv_at, mix_at = tiles, 2 * tiles + 1
    last_step = 3 * tiles + 1
    gain = lambda k: vec_ref[k : k + 1, :]
    shift = lambda k: vec_ref[6 + k : 7 + k, :]
    left, right = slice(0, channels), slice(channels, 2 * channels)
    flags = carries(offsets_ref, counts_ref, tiles)
    schedule = {}
    if fused:
        n_dp, n_fs = mesh_size
        place = Place(lax.axis_index("dp"), lax.axis_index("fsdp"), n_dp, n_fs)
        mid_src = refs.pop(0)
        mid_ref = flat_groups(mid_src)
        scratch = take(2 * (2 + place.count))

        def emit(chunk, total):
            reduced[chunk][...] = total

        plans, sends = block_scatter(place, sources + [mid_src], emit, scratch, *take(3))
        first = [(0, 0), (conv_at, 1), (conv_at + 2, 0), (conv_at + 3, 0), (mix_at, 1)]
        second = [(mix_at, 0), (mix_at, 1), (mix_at + 1, 0), (mix_at + 2, 0), (last_step, 1)]
        for chunk, points in enumerate((first, second)):
            for stage, point in enumerate(points):
                schedule.setdefault(point, []).append((stage, chunk))

    def progress(at, part):
        for stage, chunk in sorted(schedule.get((at, part), [])):
            plans[chunk][stage]()

    @pl.when(step == 0)
    def _():
        for ref in (wide_acc, mixout_acc, vec_acc):
            ref[...] = jnp.zeros_like(ref)
        if fused:
            greet(place.dp, place.fs, n_dp, n_fs)

    for at in sorted({key[0] for key in schedule if key[1] == 0 and key[0] != mix_at}):

        @pl.when(step == at)
        def _(at=at):
            progress(at, 0)

    @pl.when(step < tiles)
    def _():
        center, scale = stat_ref[0:1, :], stat_ref[1:2, :]
        plain, cross = stat_ref[2:3, :], stat_ref[3:4, :]

        def fill(index, _):
            rows = pl.ds(pl.multiple_of(index * 64, 64), 64)
            spot = pl.ds(pl.multiple_of(step * pitch + REACH + index * 64, 8), 64)
            e = (w_ref[rows, :] - center) * scale
            d = gnb_ref[rows, :] * gain(5)
            gw = scale * (d - plain - e * cross)
            g = p_ref[rows, left].astype(F32) * sigmoid(p_ref[rows, right].astype(F32))
            for lane in range(lanes):
                cols = slice(lane * 128, lane * 128 + 128)
                padded[lane, spot, :] = gw[:, cols]
                gpad[lane, spot, :] = g[:, cols]
            return 0

        lax.fori_loop(0, TILE // 64, fill, 0)

    @pl.when(step == conv_at)
    def _():
        fill_halo(padded, flags, tiles)
        fill_halo(gpad, flags, tiles)
        block = 64
        per = TILE // block
        gtaps_ref[...] = jnp.zeros_like(gtaps_ref)
        for lane in range(lanes):

            def corr(index, sums, lane=lane):
                base = (index // per) * pitch + (index % per) * block
                here = padded[lane, pl.ds(pl.multiple_of(base + REACH, 8), block), :]
                return tuple(
                    s + fold8(here * gpad[lane, pl.ds(base + REACH + k - TAPS // 2, block), :])
                    for k, s in enumerate(sums)
                )

            found = lax.fori_loop(0, tiles * per, corr, (jnp.zeros((8, 128), F32),) * TAPS)
            for k in range(TAPS):
                gtaps_ref[k : k + 1, lane * 128 : lane * 128 + 128] = jnp.sum(
                    found[k], axis=0, keepdims=True
                )
        progress(conv_at, 1)

        def store(lane, row, base, total):
            gpad[lane, pl.ds(pl.multiple_of(base + REACH, 8), 64), :] = total

        taps_over(padded, vec_ref, store, tiles, True)

    @pl.when((step > conv_at) & (step < mix_at))
    def _():
        at = step - conv_at - 1

        def first(rows):
            spot = pl.ds(pl.multiple_of(at * pitch + REACH + rows.start, 8), ROWS)
            grad = jnp.concatenate([gpad[lane, spot, :] for lane in range(lanes)], axis=1)
            sig = sigmoid(p_ref[rows, right].astype(F32))
            gl = (grad * sig).astype(BF16)
            gr = (grad * p_ref[rows, left].astype(F32) * (sig * (1.0 - sig))).astype(BF16)
            wide_scr[rows, left] = gl
            wide_scr[rows, right] = gr
            vec_acc[0] += fold8(gl.astype(F32))
            vec_acc[1] += fold8(gr.astype(F32))
            e, _ = norm_parts(x2_ref[rows, :])
            low_scr[rows, :] = (e * gain(2) + shift(2)).astype(BF16)

        by_rows(first)
        turned = low_scr[...].T
        wide_acc[...] += dot_nn(turned, wide_scr[...])
        sum_scr[...] = dot_nt(wide_scr[:, left], square_of(blocks_ref, 3)) + dot_nt(
            wide_scr[:, right], square_of(blocks_ref, 4)
        )

        def second(rows):
            here = pl.ds(pl.multiple_of(at * TILE + rows.start, ROWS), ROWS)
            e, inv = norm_parts(x2_ref[rows, :])
            grad = sum_scr[rows, :]
            vec_acc[2] += fold8(grad * e)
            vec_acc[3] += fold8(grad)
            gx2 = gx3_ref[rows, :] + norm_back(grad, e, inv, gain(2))
            spot = pl.ds(pl.multiple_of(at * pitch + REACH + rows.start, 8), ROWS)
            for lane in range(lanes):
                gpad[lane, spot, :] = gx2[:, lane * 128 : lane * 128 + 128]
            low = gx2.astype(BF16)
            low_scr[rows, :] = low
            vec_acc[4] += fold8(low.astype(F32))

        by_rows(second)
        mixout_acc[...] += dot_tn(gated_ref[...], low_scr[...])
        sum_scr[...] = dot_nt(low_scr[...], square_of(blocks_ref, 2))

        def third(rows):
            here = pl.ds(pl.multiple_of(at * TILE + rows.start, ROWS), ROWS)
            grad = sum_scr[rows, :]
            v = v_ref[rows, :].astype(F32)
            sig = sigmoid(v)
            swish = v * sig
            gy = grad * swish
            for lane in range(lanes):
                padded[lane, here, :] = gy[:, lane * 128 : lane * 128 + 128]
            gv_all[here, :] = (
                grad * y_ref[rows, :].astype(F32) * (sig * (1.0 + v - swish))
            ).astype(BF16)


        by_rows(third)

    @pl.when(step == mix_at)
    def _():
        pltpu.make_async_copy(u_ref.at[0], u_tile, u_sem).start()
        store_wide(mid_ref, 0, mixout_acc)
        store_wide(mid_ref, 1, wide_acc)
        wide_acc[...] = jnp.zeros_like(wide_acc)
        for lane in range(lanes):
            skip[lane : lane + 1, :] = vec_ref[17:18, lane * 128 : lane * 128 + 128]
        progress(mix_at, 0)

        def one(lane, _):
            mix_backward(
                lane, u_ref, padded, skip, u_tile, u_sem, power, shifted, weight, flags, ub_ref, state_ref, lags, sums, *mix_scr
            )
            return 0

        lax.fori_loop(0, lanes // 2, one, 0)
        progress(mix_at, 1)
        lax.fori_loop(lanes // 2, lanes, one, 0)
        gmap, gdecay = mix_gradients(lags, sums, vec_ref)
        gmap_out[...] = gmap
        gdecay_out[...] = gdecay

    @pl.when(step > mix_at)
    def _():
        at = step - mix_at - 1

        def fourth(rows):
            here = pl.ds(pl.multiple_of(at * TILE + rows.start, ROWS), ROWS)
            gu = jnp.concatenate([padded[lane, here, :] for lane in range(lanes)], axis=1)
            wide_scr[rows, left] = gu.astype(BF16)
            wide_scr[rows, right] = gv_all[here, :]
            e, _ = norm_parts(x1_ref[rows, :])
            low_scr[rows, :] = (e * gain(1) + shift(1)).astype(BF16)

        by_rows(fourth)
        turned = low_scr[...].T
        wide_acc[...] += dot_nn(turned, wide_scr[...])
        sum_scr[...] = dot_nt(wide_scr[:, left], square_of(blocks_ref, 0)) + dot_nt(
            wide_scr[:, right], square_of(blocks_ref, 1)
        )

        def fifth(rows):
            e, inv = norm_parts(x1_ref[rows, :])
            grad = sum_scr[rows, :]
            vec_acc[6] += fold8(grad * e)
            vec_acc[7] += fold8(grad)
            spot = pl.ds(pl.multiple_of(at * pitch + REACH + rows.start, 8), ROWS)
            gx2 = jnp.concatenate([gpad[lane, spot, :] for lane in range(lanes)], axis=1)
            gx1_ref[rows, :] = gx2 + norm_back(grad, e, inv, gain(1))

        by_rows(fifth)

    @pl.when(step == last_step)
    def _():
        store_wide(gin_out, 0, wide_acc)
        for k in range(8):
            gvec_out[k : k + 1, :] = jnp.sum(vec_acc[k], axis=0, keepdims=True)
        gvec_out[5:6, :] = jnp.concatenate([lags[k, 0:1, :] for k in range(lanes)], axis=1)
        if fused:
            progress(last_step, 1)
            for wait in sends:
                wait()


def back(mesh_size, offsets, counts, tiled, wholes, grads=(), collective_id=None):
    fused = mesh_size is not None
    frames, channels = tiled[0].shape
    tiles = frames // TILE
    groups, blocks = channels // PIECE, frames // STRETCH
    late = lambda i, first: jnp.clip(i - first, 0, tiles - 1)
    filling = lambda i: (late(i, 0), 0)
    twice = lambda i: (jnp.where(i < tiles, i, late(i, tiles + 1)), 0)
    mixing = lambda i: (late(i, tiles + 1), 0)
    ending = lambda i: (late(i, 2 * tiles + 2), 0)
    maps = [filling, filling, twice] + [mixing] * 5 + [ending]
    state = jax.ShapeDtypeStruct((STATES, channels), F32)
    bf16 = lambda *shape: jax.ShapeDtypeStruct(shape, BF16)
    shapes = [
        jax.ShapeDtypeStruct((frames, channels), F32),
        bf16(groups, 2, PIECE, WIDTH),
        jax.ShapeDtypeStruct((8, channels), F32),
        jax.ShapeDtypeStruct((16, channels), F32),
        state,
        state,
    ]
    pad = pltpu.VMEM((channels // 128, tiles * (TILE + 2 * REACH), 128), F32)
    scratch = [
        pltpu.VMEM((channels, 2 * channels), F32),
        pltpu.VMEM((channels, channels), F32),
        pltpu.VMEM((8, 8, channels), F32),
        pltpu.VMEM((TILE, channels), BF16),
        pltpu.VMEM((TILE, 2 * channels), BF16),
        pltpu.VMEM((TILE, channels), F32),
        pad,
        pad,
        pltpu.VMEM((frames, channels), BF16),
        pltpu.VMEM((channels // 128, STRETCH, 128), F32),
        pltpu.VMEM((2, groups, SPREAD), F32),
        pltpu.VMEM((8, 128), F32),
        pltpu.VMEM((frames, 128), F32),
        pltpu.SemaphoreType.DMA(()),
        pltpu.VMEM((2, STRETCH, blocks, 128), F32),
        pltpu.VMEM((8, blocks, STRETCH * PIECE), BF16),
        pltpu.VMEM((8, blocks, STRETCH * PIECE), F32),
        pltpu.VMEM((2, STRETCH * PIECE, SPREAD), BF16),
        pltpu.VMEM((2, STRETCH * PIECE, STRETCH * PIECE), BF16),
        pltpu.VMEM((2, 3 * blocks, STRETCH * PIECE), BF16),
        pltpu.VMEM((2, 3 * blocks, SPREAD), F32),
        pltpu.VMEM((2, blocks, SPREAD), F32),
    ]
    if fused:
        counts_of = [grads[0].shape[-3], 3]
        shapes += [jax.ShapeDtypeStruct((k, PIECE, WIDTH), F32) for k in counts_of]
        scratch += [pltpu.VMEM(block_layout(*mesh_size) + (3, PIECE, WIDTH), BF16)]
        scratch += block_scratch(*mesh_size, counts_of, (PIECE, WIDTH))
        scratch += block_sems(*mesh_size, 2)
    else:
        shapes.append(bf16(groups, 3, PIECE, WIDTH))
    return pl.pallas_call(
        partial(back_kernel, mesh_size),
        grid=(3 * tiles + 2,),
        in_specs=[SMEM_SPEC, SMEM_SPEC]
        + [pl.BlockSpec((TILE, a.shape[1]), index) for a, index in zip(tiled, maps)]
        + [HBM_SPEC]
        + [whole(a.shape) for a in wholes[1:]]
        + [HBM_SPEC] * len(grads),
        out_specs=[pl.BlockSpec((TILE, channels), ending)] + [whole(s.shape) for s in shapes[1:]],
        out_shape=shapes,
        scratch_shapes=scratch,
        compiler_params=params(collective_id),
        name="back",
    )(offsets, counts, *tiled, *wholes, *grads)


def small_gradients(out, gvec1, gvec2, gvec3, gtaps, gmap, gdecay, table_ref):
    out[...] = jnp.zeros_like(out)
    gains = {1: (gvec2, 6), 2: (gvec2, 2), 3: (gvec1, 3), 4: (gvec1, 0), 5: (gvec1, 6)}
    shifts = {1: (gvec2, 7), 2: (gvec2, 3), 3: (gvec1, 4), 4: (gvec1, 1), 5: (gvec1, 7)}
    shifts.update({6: (gvec3, 0), 7: (gvec1, 2), 8: (gvec2, 4), 9: (gvec2, 0), 10: (gvec2, 1)})
    shifts.update({11: (gvec2, 5), 12: (gvec1, 5)})
    for at, (ref, row) in gains.items():
        out[at : at + 1, :] = ref[row : row + 1, :]
    for at, (ref, row) in shifts.items():
        out[6 + at : 7 + at, :] = ref[row : row + 1, :]
    out[TAP_ROW : TAP_ROW + TAPS, :] = gtaps[:TAPS, :]
    log_decay, decay, root, maps_in, maps_out = state_terms(table_ref)
    both = gmap[...] * root
    out[MAP_IN:MAP_OUT, :] = both * maps_out
    out[MAP_OUT:TABLE, :] = both * maps_in
    turn = (1.0 - root * root) / root
    out[RATE:MAP_IN, :] = log_decay * (
        gdecay[...] * decay - gmap[...] * maps_in * maps_out * turn
    )


def store_cols(out, at, value):
    groups = value.shape[0] // PIECE
    out[:, at] = value.reshape((groups, PIECE, WIDTH))


def tail_kernel(mesh_size, *refs):
    fused = mesh_size is not None
    refs = list(refs)
    take = lambda count: [refs.pop(0) for _ in range(count)]
    x_ref, h_ref, gx1_ref, up_ref, up2_ref, down_ref, table_ref = take(7)
    hidden = 4 * WIDTH
    if fused:
        gvec1, gvec2, gtaps, gmap, gdecay, gbias1 = take(6)
        sources = take(1)
        gx_ref, last_out = take(2)
        reduced = take(5)
    else:
        gx_ref, gvec_out, gbias_out, up_out, down_out = take(5)
    turn_scr, grad_scr, gh_scr, vec_acc, bias_scr = take(5)
    step = pl.program_id(0)
    frames, channels = x_ref.shape
    chunks = hidden // WIDTH
    tiles = frames // TILE
    first_b, first_c = 1 + chunks, 1 + 2 * chunks
    schedule = {}
    if fused:
        n_dp, n_fs = mesh_size
        down_src, left_src, right_src, small_src, small_scr, gvec3 = take(6)
        dp, fs = lax.axis_index("dp"), lax.axis_index("fsdp")
        place = Place(dp, fs, n_dp, n_fs)
        scratch = take(5 * (2 + place.count))
        sems = take(3)
        swap = take(4)
        down_out = flat_groups(down_src)
        halves = (flat_groups(left_src), flat_groups(right_src))

        def emit(chunk, total):
            reduced[chunk][...] = total

        plans, sends = block_scatter(
            place, sources + [down_src, left_src, right_src, small_src], emit, scratch, *sems
        )
        begins = [
            (0, 2, 4, 6, 8),
            (first_b, first_b + 2, first_c, first_c + 2, first_c + tiles),
            (first_b + 2, first_b + 3, first_c + 1, first_c + 2, first_c + tiles),
            (first_c, first_c + 1, first_c + 2, first_c + tiles, first_c + tiles),
            (first_c, first_c + 1, first_c + 2, first_c + tiles, first_c + tiles),
        ]
        for chunk, steps in enumerate(begins):
            for stage, at in enumerate(steps):
                schedule.setdefault(at, []).append((stage, chunk))
    last_step = first_c + tiles - 1

    def progress(at):
        for stage, chunk in sorted(schedule.get(at, [])):
            plans[chunk][stage]()

    @pl.when(step == 0)
    def _():
        if fused:
            greet(dp, fs, n_dp, n_fs)
        progress(0)
        vec_acc[...] = jnp.zeros_like(vec_acc)

        def first(rows):
            e, _ = norm_parts(x_ref[rows, :].astype(F32))
            low = (e * table_ref[0:1, :] + table_ref[6:7, :]).astype(BF16)
            turn_scr[:, rows] = low.T
            grad = (0.5 * gx1_ref[rows, :]).astype(BF16)
            grad_scr[rows, :] = grad
            vec_acc[0] += fold8(grad.astype(F32))

        by_rows(first, frames)

    if fused:
        for at in range(1, last_step + 1):
            if at in schedule and at != first_c:

                @pl.when(step == at)
                def _(at=at):
                    progress(at)

    @pl.when((step >= 1) & (step < first_b))
    def _():
        h = h_ref[...].astype(F32)
        active = (h * sigmoid(h)).astype(BF16)
        value = dot_tn(active, grad_scr[...]).astype(BF16)
        groups = WIDTH // (4 * PIECE)
        down_out[pl.ds((step - 1) * groups, groups)] = value.reshape((groups, 4, PIECE, WIDTH))

    def second_half(c, store):
        cols = columns(c, WIDTH)
        h = h_ref[...].astype(F32)
        sig = sigmoid(h)
        gate = dot_nt(grad_scr[...], rows_of(down_ref, 0, c))
        grad_h = (gate * (sig * (1.0 + h * (1.0 - sig)))).astype(BF16)
        gh_scr[:, cols] = grad_h
        sums = jnp.sum(fold8(grad_h.astype(F32)), axis=0, keepdims=True)
        bias_scr[pl.ds(2 * c, 1), :] = sums[:, :CHUNK]
        bias_scr[pl.ds(2 * c + 1, 1), :] = sums[:, CHUNK:]
        store(dot_nn(turn_scr[...], grad_h).astype(BF16))

    if fused:
        for half in range(2):
            begin = first_b + half * (chunks // 2)

            @pl.when((step >= begin) & (step < begin + chunks // 2))
            def _(half=half, begin=begin):
                def store(value):
                    store_cols(halves[half], step - begin, value)

                second_half(step - first_b, store)

    else:

        @pl.when((step >= first_b) & (step < first_c))
        def _():
            def store(value):
                store_cols(up_out, step - first_b, value)

            second_half(step - first_b, store)

    if fused:

        @pl.when(step == first_c)
        def _():
            gvec3[0:1, :] = jnp.sum(vec_acc[0], axis=0, keepdims=True)
            small_gradients(small_scr, gvec1, gvec2, gvec3, gtaps, gmap, gdecay, table_ref)
            narrow = small_scr[...].T.astype(BF16)
            devices = n_dp * n_fs
            small_out = flat_groups(small_src)
            small_out[:, 0, :, :CHUNK] = narrow.reshape((devices, PIECE, CHUNK))
            for c in range(8):
                bias_scr[8 + c : 9 + c, :] = gbias1[0:1, c * CHUNK : c * CHUNK + CHUNK]
            bias = bias_scr[...].astype(BF16)
            small_out[:, 0, :, CHUNK:] = jnp.broadcast_to(bias[None], (devices, PIECE, CHUNK))
            progress(first_c)

    @pl.when(step >= first_c)
    def _():
        tile = step - first_c
        whole_tile = pl.ds(pl.multiple_of(tile * TILE, TILE), TILE)
        total = dot_nt(gh_scr[whole_tile, :WIDTH], square_of(up_ref, 1))
        later = [square_of(up_ref, 2), square_of(up2_ref, 0), square_of(up2_ref, 1)]
        for k in range(1, hidden // WIDTH):
            cols = slice(k * WIDTH, k * WIDTH + WIDTH)
            total = total + dot_nt(gh_scr[whole_tile, cols], later[k - 1])
        gx_ref[...] = total

        def second(rows):
            here = pl.ds(pl.multiple_of(tile * TILE + rows.start, ROWS), ROWS)
            e, inv = norm_parts(x_ref[here, :].astype(F32))
            grad = gx_ref[rows, :]
            vec_acc[1] += fold8(grad * e)
            vec_acc[2] += fold8(grad)
            gx_ref[rows, :] = gx1_ref[here, :] + norm_back(grad, e, inv, table_ref[0:1, :])

        by_rows(second)

    @pl.when(step == last_step)
    def _():
        if fused:
            last_out[...] = jnp.zeros_like(last_out)
            for k in range(2):
                last_out[k : k + 1, :] = jnp.sum(vec_acc[1 + k], axis=0, keepdims=True)
            ends = sorted(schedule.get(last_step + 1, []))

            def between():
                for stage, chunk in ends:
                    plans[chunk][stage]()

            last_out[...] = sum_over(last_out[...], dp, fs, n_dp, n_fs, *swap, between=between)
            for wait in sends:
                wait()
        else:
            gvec_out[...] = jnp.zeros_like(gvec_out)
            for k in range(3):
                gvec_out[k : k + 1, :] = jnp.sum(vec_acc[k], axis=0, keepdims=True)
            gbias_out[...] = bias_scr[...]


def tail(mesh_size, x, h, gx1, up, up2, down, table, others=(), grads=(), collective_id=None):
    fused = mesh_size is not None
    frames, channels = x.shape
    hidden = h.shape[1]
    tiles, chunks = frames // TILE, hidden // WIDTH
    first_b, first_c = 1 + chunks, 1 + 2 * chunks
    place = lambda i: jnp.where(
        i < first_b, jnp.maximum(i - 1, 0), jnp.minimum(i - first_b, chunks - 1)
    )
    shapes = [jax.ShapeDtypeStruct((frames, channels), F32)]
    scratch = [
        pltpu.VMEM((channels, frames), BF16),
        pltpu.VMEM((frames, channels), BF16),
        pltpu.VMEM((frames, hidden), BF16),
        pltpu.VMEM((8, 8, channels), F32),
        pltpu.VMEM((16, CHUNK), F32),
    ]
    if fused:
        own = [4, 2, 2, 1]
        counts = [g.shape[-3] for g in grads] + own
        shapes.append(jax.ShapeDtypeStruct((8, channels), F32))
        shapes += [jax.ShapeDtypeStruct((k, PIECE, WIDTH), F32) for k in counts]
        layout = block_layout(*mesh_size)
        scratch += [pltpu.VMEM(layout + (k, PIECE, WIDTH), BF16) for k in own]
        scratch += [pltpu.VMEM((256, channels), F32), pltpu.VMEM((8, channels), F32)]
        scratch += block_scratch(*mesh_size, counts, (PIECE, WIDTH))
        scratch += block_sems(*mesh_size, len(counts))
        scratch += swap_scratch(*mesh_size, channels)
    else:
        shapes += [
            jax.ShapeDtypeStruct((8, channels), F32),
            jax.ShapeDtypeStruct((16, CHUNK), F32),
            jax.ShapeDtypeStruct((channels // PIECE, 4, PIECE, WIDTH), BF16),
            jax.ShapeDtypeStruct((channels // PIECE, 4, PIECE, WIDTH), BF16),
        ]
    return pl.pallas_call(
        partial(tail_kernel, mesh_size),
        grid=(first_c + tiles,),
        in_specs=[whole(x.shape), pl.BlockSpec((frames, WIDTH), lambda i: (0, place(i)))]
        + [whole(a.shape) for a in (gx1, up, up2, down, table) + tuple(others)]
        + [pl.BlockSpec(memory_space=pltpu.HBM)] * len(grads),
        out_specs=[
            pl.BlockSpec((TILE, channels), lambda i: (jnp.maximum(i - first_c, 0), 0))
        ]
        + [whole(s.shape) for s in shapes[1:]],
        out_shape=shapes,
        scratch_shapes=scratch,
        compiler_params=params(collective_id),
        name="tail",
    )(x, h, gx1, up, up2, down, table, *others, *grads)


def unpack_kernel(
    place_ref,
    second_ref,
    middle_ref,
    mixin_ref,
    down_ref,
    left_ref,
    right_ref,
    small_ref,
    last_ref,
    result_in,
    grad_in,
    result_out,
    grad_out,
    up_out,
    down_out,
    bias_out,
    mixin_out,
    mixout_out,
    convin_out,
    convout_out,
    convbias_out,
    rate_out,
    map_out,
    taps_out,
    gains_out,
    shifts_out,
    sem,
):
    mine = place_ref[0]
    copies = []
    for at, (source, target) in enumerate(((result_in, result_out), (grad_in, grad_out))):
        rows = source.shape[0] // 4
        for k in range(4):
            part = pl.ds(k * rows, rows)
            copies.append(pltpu.make_async_copy(source.at[part], target.at[part], sem.at[at, k]))
    for copy in copies:
        copy.start()
    for k in range(4):
        cols = slice(k * WIDTH, k * WIDTH + WIDTH)
        rows = slice(k * PIECE, k * PIECE + PIECE)
        up_out[0, :, cols] = (left_ref if k < 2 else right_ref)[k % 2]
        up_out[1, :, cols] = second_ref[1 + k]
        down_out[0, rows, :] = down_ref[k]
        down_out[1, rows, :] = second_ref[5 + k]
    convout_out[...] = second_ref[0]
    mixout_out[...] = middle_ref[0]
    for k in range(2):
        cols = slice(k * WIDTH, k * WIDTH + WIDTH)
        mixin_out[:, cols] = mixin_ref[k]
        convin_out[:, cols] = middle_ref[1 + k]
    count = bias_out.shape[1]
    row = (mine * count) // CHUNK
    inner = mine * count - row * CHUNK
    for layer in range(2):
        line = small_ref[0, pl.ds(8 * layer + row, 1), CHUNK:]
        line = pltpu.roll(jnp.broadcast_to(line, (8, CHUNK)), CHUNK - inner, 1)
        bias_out[layer : layer + 1, :] = line[0:1, :count]
    channels = last_ref.shape[1]
    first = pltpu.roll(last_ref[...], channels - mine * PIECE, 1)[:, :PIECE]
    small = small_ref[0, :, :CHUNK]
    turned = small.T
    gains_out[...] = turned[0:6, :]
    gains_out[0:1, :] = first[0:1, :]
    shifts_out[...] = turned[6:18, :]
    shifts_out[0:1, :] = first[1:2, :]
    convbias_out[...] = turned[18:19, :]
    taps_out[...] = turned[TAP_ROW : TAP_ROW + TAPS, :]
    rate_out[...] = small[:, RATE:MAP_IN]
    map_out[0] = small[:, MAP_IN:MAP_OUT]
    map_out[1] = small[:, MAP_OUT:TABLE]
    for copy in copies:
        copy.wait()


def unpack(mine, arrays, passed, hidden):
    channels = arrays[-1].shape[1]
    devices = channels // PIECE
    f32 = lambda *shape: jax.ShapeDtypeStruct(shape, F32)
    vmem = pl.BlockSpec(memory_space=pltpu.VMEM)
    return pl.pallas_call(
        unpack_kernel,
        in_specs=[SMEM_SPEC] + [vmem] * len(arrays) + [HBM_SPEC] * 2,
        out_specs=[HBM_SPEC] * 2 + [vmem] * 13,
        scratch_shapes=[pltpu.SemaphoreType.DMA((2, 4))],
        out_shape=[jax.ShapeDtypeStruct(a.shape, a.dtype) for a in passed]
        + [
            f32(2, PIECE, hidden),
            f32(2, hidden // devices, channels),
            f32(2, hidden // devices),
            f32(PIECE, 2 * WIDTH),
            f32(PIECE, WIDTH),
            f32(PIECE, 2 * WIDTH),
            f32(PIECE, WIDTH),
            f32(1, PIECE),
            f32(PIECE, STATES),
            f32(2, PIECE, STATES),
            f32(TAPS, PIECE),
            f32(6, PIECE),
            f32(12, PIECE),
        ],
        name="unpack",
    )(mine, *arrays, *passed)


def pack_table(gains, shifts, conv_bias, taps, rate, maps):
    channels = gains.shape[1]
    blank = lambda rows: jnp.zeros((rows, channels), gains.dtype)
    parts = [gains, shifts, conv_bias[None], blank(TAP_ROW - 19), taps, blank(RATE - TAP_ROW - TAPS)]
    parts += [rate, maps[0], maps[1], blank(256 - TABLE)]
    return jnp.concatenate(parts, axis=0).T


def pack_bias(bias, place):
    layers, count = bias.shape
    hidden = 16 * CHUNK // layers
    wide = lax.dynamic_update_slice(
        jnp.zeros((layers, hidden), bias.dtype), bias, (0, place * count)
    )
    return wide.reshape((16, CHUNK))


def unpack_table(table):
    return (
        table[0:6],
        table[6:18],
        table[18],
        table[TAP_ROW : TAP_ROW + TAPS],
        table[RATE:MAP_IN],
        jnp.stack([table[MAP_IN:MAP_OUT], table[MAP_OUT:TABLE]]),
    )


def on_device(
    n_dp,
    n_fs,
    frames,
    seq_lengths,
    seq_offsets,
    seq_counts,
    ffn_up,
    ffn_down,
    ffn_bias_up,
    mix_in,
    mix_out,
    conv_in,
    conv_out,
    conv_out_bias,
    ssm_rate,
    ssm_map,
    conv_kernel,
    gains,
    shifts,
    cotangent,
):
    devices = n_dp * n_fs
    mine = lax.axis_index("dp") * n_fs + lax.axis_index("fsdp")
    frames_dev, channels = frames.shape
    hidden = ffn_up.shape[2]
    if channels // devices == PIECE:
        size = (n_dp, n_fs)
        small = [
            ffn_bias_up,
            gains,
            shifts,
            conv_out_bias[None],
            conv_kernel,
            ssm_rate.T,
            ssm_map.transpose((0, 2, 1)),
        ]
        weights = [ffn_up, ffn_down, mix_in, mix_out, conv_in, conv_out]
        made = front(size, seq_offsets, seq_counts, frames, small, weights, hidden, 1)
        h0, x1, v, y, gated, x2, p, u, w, stat, table, bias, *mixing = made[:17]
        groups = lambda g: g.reshape((devices,) + g.shape[-3:])
        places = lambda g: g.reshape(block_layout(n_dp, n_fs) + g.shape[1:])
        first, extra, second, third, fourth = [groups(g) for g in made[17:]]
        result, gx3, gnb, grads, gbias1, gvec1, stat = middle(
            size, x2, w, cotangent, fourth, bias, table, stat, hidden, 2
        )
        gx1, grads2, gvec2, gtaps, gmap, gdecay, reduced, reduced2 = back(
            size,
            seq_offsets,
            seq_counts,
            [w, gnb, p, x2, gx3, gated, y, v, x1],
            [u] + mixing + [third, table, stat],
            (places(grads),),
            3,
        )
        others = (gvec1, gvec2, gtaps, gmap, gdecay, gbias1)
        gx, last, *late = tail(
            size, frames, h0, gx1, first, extra, second, table, others, (places(grads2),), 4
        )
        made = unpack(mine.reshape((1,)), [reduced, reduced2] + late + [last], (result, gx), hidden)
        made = list(made)
        made[9] = made[9].reshape((-1,))
        made[10] = made[10].T
        made[11] = made[11].transpose((0, 2, 1))
        return tuple(made)

    small = pack_table(gains, shifts, conv_out_bias, conv_kernel, ssm_rate, ssm_map)
    got = gather_all(
        n_dp,
        n_fs,
        [
            small[None],
            pack_bias(ffn_bias_up, mine)[None],
            ffn_up,
            ffn_down,
            mix_in[None],
            mix_out[None],
            conv_in[None],
            conv_out[None],
        ],
        1,
    )
    matrix = lambda g: g.reshape((-1, g.shape[-1]))
    table, _, up0, up1, down0, down1, mixin, mixout, convin, convout = [matrix(g) for g in got]
    table = table.astype(F32).T[:TABLE]
    bias = jnp.sum(got[1].astype(F32), axis=0)
    group_count = channels // PIECE
    cut = lambda g: g.reshape((group_count, PIECE, -1, WIDTH)).transpose((0, 2, 1, 3))
    tall = lambda g: g.reshape((group_count, -1, PIECE, WIDTH))
    join = lambda g: g.transpose((0, 2, 1, 3)).reshape((channels, -1))
    blank = jnp.pad(matrix(got[0]), ((0, 0), (0, WIDTH - 256))).reshape((group_count, 1, PIECE, WIDTH))
    extra = cut(up0)
    first, extra = jnp.concatenate([blank, extra[:, :2]], axis=1), extra[:, 2:]
    third = jnp.concatenate([cut(mixin), cut(mixout), cut(convin)], axis=1)
    fourth = jnp.concatenate([cut(convout), cut(up1), tall(down1)], axis=1)
    made = front(
        None, seq_offsets, seq_counts, frames, [table, bias], [first, extra, tall(down0), third], hidden
    )
    h0, x1, v, y, gated, x2, p, u, w, stat, table, bias, *mixing = made
    pool = exchange(n_dp, n_fs, stat, frames_dev, 2, pool_kernel)
    scale = lax.rsqrt(pool[1:2] / (frames_dev * devices) + EPSILON)
    stat = jnp.concatenate([pool[0:1], scale, jnp.zeros((6, channels), F32)])
    result, gx3, gnb, grads, gbias1, gvec1, stat = middle(
        None, x2, w, cotangent, fourth, bias, table, stat, hidden
    )
    sums = exchange(n_dp, n_fs, gvec1, 1, 4, total_kernel)[6:8]
    sums = sums * (table[5:6] / (frames_dev * devices))
    stat = jnp.concatenate([stat[0:2], sums[1:2], sums[0:1], stat[4:8]])
    gx1, grads2, gvec2, gtaps, gmap, gdecay, grads3 = back(
        None,
        seq_offsets,
        seq_counts,
        [w, gnb, p, x2, gx3, gated, y, v, x1],
        [u] + mixing + [third, table, stat],
    )
    gx, gvec3, gbias0, gup0, gdown0 = tail(None, frames, h0, gx1, first, extra, tall(down0), table)

    def weights_of(log_rate, maps):
        log_decay = -jnp.exp(log_rate)
        root = jnp.sqrt(-jnp.expm1(2.0 * log_decay))
        return jnp.exp(log_decay), maps[0] * root * maps[1]

    rate, maps = unpack_table(table)[4:]
    rate_grad, map_grad = jax.vjp(weights_of, rate, maps)[1]((gdecay, gmap))
    gain_grad = jnp.stack([gvec3[1], gvec2[6], gvec2[2], gvec1[3], gvec1[0], gvec1[6]])
    rows = [gvec3[2], gvec2[7], gvec2[3], gvec1[4], gvec1[1], gvec1[7], gvec3[0], gvec1[2]]
    rows += [gvec2[4], gvec2[0], gvec2[1], gvec2[5]]
    small_grad = pack_table(
        gain_grad, jnp.stack(rows), gvec1[5], gtaps[:TAPS], rate_grad, map_grad
    )
    bias_grad = jnp.concatenate([gbias0[:8], gbias1[0].reshape((8, CHUNK))])
    wide = lambda g: g.reshape((devices, g.shape[0] // devices, g.shape[1]))
    reduced = scatter_all(
        n_dp,
        n_fs,
        [
            wide(join(grads[:, 1:5])),
            wide(matrix(grads[:, 5:9])),
            wide(join(grads[:, 0:1])),
            wide(join(grads3[:, 1:3])),
            wide(join(grads3[:, 0:1])),
            wide(join(grads2[:, 0:2])),
            wide(join(gup0)),
            wide(matrix(gdown0)),
            wide(small_grad.astype(BF16)),
            jnp.broadcast_to(bias_grad.astype(BF16), (devices, PIECE, CHUNK)),
        ],
        5,
    )
    gains_grad, shifts_grad, conv_bias_grad, taps_grad, rate_grad, map_grad = unpack_table(
        reduced[8].T
    )
    bias_grad = reduced[9].reshape((2, -1))
    count = bias_grad.shape[1] // devices
    bias_grad = lax.dynamic_slice(bias_grad, (0, mine * count), (2, count))
    return (
        result,
        gx,
        jnp.stack([reduced[6], reduced[0]]),
        jnp.stack([reduced[7], reduced[1]]),
        bias_grad,
        reduced[5],
        reduced[4],
        reduced[3],
        reduced[2],
        conv_bias_grad,
        rate_grad,
        map_grad,
        taps_grad,
        gains_grad,
        shifts_grad,
    )


def solution(mesh):
    both = ("dp", "fsdp")
    row, row1 = P(both, None), P(both)
    col, col3, mid = P(None, both), P(None, None, both), P(None, both, None)
    in_specs = (
        row,
        row,
        row,
        row1,
        mid,
        mid,
        col,
        row,
        row,
        row,
        row,
        row1,
        col,
        col3,
        col,
        col,
        col,
        row,
    )
    out_specs = (row, row, mid, mid, col, row, row, row, row, row1, col, col3, col, col, col)
    return jax.shard_map(
        partial(on_device, mesh.shape["dp"], mesh.shape["fsdp"]),
        mesh=mesh,
        in_specs=in_specs,
        out_specs=out_specs,
        check_vma=False,
    )
```

```python
import itertools
from functools import partial

import jax
import jax.numpy as jnp
from jax import lax
from jax.experimental import pallas as pl
from jax.experimental.pallas import tpu as pltpu
from jax.sharding import PartitionSpec as P

MESH = pl.DeviceIdType.MESH
BF16 = jnp.bfloat16
F32 = jnp.float32


def flip(index, bit):
    return index + bit * (1 - 2 * lax.rem(lax.div(index, bit), 2))


def flip_all(index, bits):
    for bit in bits:
        index = flip(index, bit)
    return index


def combos(bits):
    found = [()]
    for bit in bits:
        found = found + [entry + (bit,) for entry in found]
    return found


def plan_bits(n_dp):
    bits, bit = [], 2
    while bit < n_dp:
        bits.append(bit)
        bit *= 2
    return tuple(bits)


def greet(dp, fs, n_dp, n_fs):
    barrier = pltpu.get_barrier_semaphore()
    for step in range(1, n_dp):
        pl.semaphore_signal(
            barrier, inc=1, device_id=(lax.rem(dp + step, n_dp), fs), device_id_type=MESH
        )
    for step in range(1, n_fs):
        pl.semaphore_signal(
            barrier, inc=1, device_id=(dp, lax.rem(fs + step, n_fs)), device_id_type=MESH
        )
    pl.semaphore_wait(barrier, n_dp + n_fs - 2)


def gather_plan(dp, fs, n_dp, n_fs, sources, outs, send_sem, recv_sem, local_sem):
    bits = plan_bits(n_dp)
    orders = (bits, bits[::-1])
    half = n_fs // 2
    sends = []

    def stages(chunk):
        src, out = sources[chunk], outs[chunk]
        slots = itertools.count()

        def zone(where, part):
            if part is None:
                return out.at[pl.ds(where * n_fs, n_fs)]
            return out.at[pl.ds(where * n_fs + part * half, half)]

        def remote(slot, view_from, view_to, device):
            return pltpu.make_async_remote_copy(
                src_ref=view_from,
                dst_ref=view_to,
                send_sem=send_sem.at[chunk, slot],
                recv_sem=recv_sem.at[chunk, slot],
                device_id=device,
                device_id_type=MESH,
            )

        def launch(make):
            make().start()
            sends.append(lambda: make().wait_send())

        z_slots = [next(slots) for _ in range(1, n_fs)]

        def own_copy():
            return pltpu.make_async_copy(src, out.at[dp * n_fs + fs], local_sem.at[chunk])

        def start():
            own_copy().start()
            for step in range(1, n_fs):
                launch(
                    lambda step=step: remote(
                        z_slots[step - 1],
                        src,
                        out.at[dp * n_fs + fs],
                        (dp, lax.rem(fs + step, n_fs)),
                    )
                )

        def wait_z():
            own_copy().wait()
            for step in range(1, n_fs):
                origin = dp * n_fs + lax.rem(fs + n_fs - step, n_fs)
                remote(z_slots[step - 1], src, out.at[origin], (dp, fs)).wait_recv()

        steps, before = [start], wait_z
        for depth in range(len(bits)):
            plan = []
            for part, order in enumerate(orders):
                for entry in combos(order[:depth]):
                    plan.append((next(slots), part, order[depth], entry))

            def view(slot, part, bit, entry, arrived):
                where = flip_all(flip(dp, bit) if arrived else dp, entry)
                return remote(slot, zone(where, part), zone(where, part), (flip(dp, bit), fs))

            def go(plan=plan, before=before, view=view):
                before()
                for item in plan:
                    launch(lambda item=item: view(*item, False))

            def arrive(plan=plan, view=view):
                for item in plan:
                    view(*item, True).wait_recv()

            steps.append(go)
            before = arrive
        last = [(next(slots), entry) for entry in combos(bits)]

        def across(slot, entry, arrived):
            where = flip_all(flip(dp, 1) if arrived else dp, entry)
            return remote(slot, zone(where, None), zone(where, None), (flip(dp, 1), fs))

        def cross(before=before):
            before()
            for item in last:
                launch(lambda item=item: across(*item, False))

        def finish():
            for item in last:
                across(*item, True).wait_recv()

        return steps + [cross, finish]

    return [stages(chunk) for chunk in range(len(outs))], sends


def waves(plans):
    depth = len(plans[0])
    out = []
    for wave in range(len(plans) + depth - 1):
        out.append(
            [plans[c][wave - c] for c in range(len(plans)) if 0 <= wave - c < depth]
        )
    return out


def gather_kernel(n_dp, n_fs, layers, *refs):
    n_in = len(layers)
    n_out = sum(layers)
    ins, outs = refs[:n_in], refs[n_in : n_in + n_out]
    send_sem, recv_sem, local_sem = refs[n_in + n_out :]
    sources = []
    for ref, count in zip(ins, layers):
        sources += [ref.at[layer] for layer in range(count)]
    dp, fs = lax.axis_index("dp"), lax.axis_index("fsdp")
    greet(dp, fs, n_dp, n_fs)
    plans, sends = gather_plan(dp, fs, n_dp, n_fs, sources, outs, send_sem, recv_sem, local_sem)
    for wave in waves(plans):
        for stage in wave:
            stage()
    for wait in sends:
        wait()


def slot_count(n_dp, n_fs):
    nb = len(plan_bits(n_dp))
    return n_fs - 1 + 2 * (2**nb - 1) + 2**nb


def gather_all(n_dp, n_fs, arrays, collective_id):
    layers = tuple(a.shape[0] for a in arrays)
    outs = []
    for a in arrays:
        outs += [jax.ShapeDtypeStruct((n_dp * n_fs,) + a.shape[1:], a.dtype)] * a.shape[0]
    count = slot_count(n_dp, n_fs)
    return pl.pallas_call(
        partial(gather_kernel, n_dp, n_fs, layers),
        out_shape=outs,
        in_specs=[pl.BlockSpec(memory_space=pltpu.HBM)] * len(arrays),
        out_specs=[pl.BlockSpec(memory_space=pltpu.HBM)] * len(outs),
        scratch_shapes=[
            pltpu.SemaphoreType.DMA((len(outs), count)),
            pltpu.SemaphoreType.DMA((len(outs), count)),
            pltpu.SemaphoreType.DMA((len(outs),)),
        ],
        compiler_params=pltpu.CompilerParams(collective_id=collective_id, has_side_effects=True),
        name="gather_parameters",
    )(*arrays)


def scatter_plan(dp, fs, n_dp, n_fs, ins, emit, scratch, send_sem, recv_sem, local_sem, first=0):
    bits = plan_bits(n_dp)
    orders = (bits[::-1], bits)
    half = n_fs // 2
    index = {entry: at for at, entry in enumerate(combos(bits))}
    sends = []

    def add_into(kept, other):
        def body(at, _):
            kept[at] = (kept[at].astype(F32) + other[at].astype(F32)).astype(BF16)
            return 0

        lax.fori_loop(0, kept.shape[0], body, 0)

    def stages(chunk):
        src = ins[chunk]
        cross_in, own, later, last = scratch[4 * chunk : 4 * chunk + 4]
        slots = itertools.count()

        def remote(slot, view_from, view_to, device):
            return pltpu.make_async_remote_copy(
                src_ref=view_from,
                dst_ref=view_to,
                send_sem=send_sem.at[first + chunk, slot],
                recv_sem=recv_sem.at[first + chunk, slot],
                device_id=device,
                device_id_type=MESH,
            )

        def launch(make):
            make().start()
            sends.append(lambda: make().wait_send())

        def zone(entry, crossed):
            return src.at[pl.ds(flip_all(flip(dp, 1) if crossed else dp, entry) * n_fs, n_fs)]

        pieces = [(next(slots), entry, index[entry]) for entry in combos(bits)]

        def load(entry, at):
            return pltpu.make_async_copy(
                zone(entry, False), own.at[at], local_sem.at[first + chunk, at]
            )

        def across(slot, entry, at):
            return remote(slot, zone(entry, True), cross_in.at[at], (flip(dp, 1), fs))

        def start():
            for item in pieces:
                launch(lambda item=item: across(*item))
            for _, entry, at in pieces:
                load(entry, at).start()

        def fold_cross():
            for slot, entry, at in pieces:
                load(entry, at).wait()
                across(slot, entry, at).wait_recv()
                add_into(own.at[at], cross_in.at[at])

        steps, before = [start], fold_cross
        used = 0
        for depth in range(len(bits)):
            plan = []
            for part, order in enumerate(orders):
                bit, gone = order[depth], order[:depth]
                for entry in combos(bits):
                    if not (set(entry) & set(gone)) and bit not in entry:
                        away = tuple(sorted(entry + (bit,)))
                        plan.append((next(slots), part, bit, index[away], index[entry], used))
                        used += 1

            def move(slot, part, bit, away, kept, place):
                return remote(
                    slot,
                    own.at[away, pl.ds(part * half, half)],
                    later.at[place],
                    (flip(dp, bit), fs),
                )

            def go(plan=plan, before=before, move=move):
                before()
                for item in plan:
                    launch(lambda item=item: move(*item))

            def fold(plan=plan, move=move):
                for item in plan:
                    move(*item).wait_recv()
                    _, part, _, _, kept, place = item
                    add_into(own.at[kept, pl.ds(part * half, half)], later.at[place])

            steps.append(go)
            before = fold
        z_slots = [next(slots) for _ in range(1, n_fs)]

        def along(step):
            to = lax.rem(fs + step, n_fs)
            return remote(z_slots[step - 1], own.at[0, to], last.at[step - 1], (dp, to))

        def spread(before=before):
            before()
            for step in range(1, n_fs):
                launch(lambda step=step: along(step))

        def finish():
            total = own[0, fs].astype(F32)
            for step in range(1, n_fs):
                along(step).wait_recv()
                total = total + last[step - 1].astype(F32)
            emit(chunk, total)

        return steps + [spread, finish]

    return [stages(chunk) for chunk in range(len(ins))], sends


def scatter_scratch(n_dp, n_fs, tails):
    pieces = 2 ** len(plan_bits(n_dp))
    scratch = []
    for tail in tails:
        scratch += [
            pltpu.VMEM((pieces, n_fs) + tail, BF16),
            pltpu.VMEM((pieces, n_fs) + tail, BF16),
            pltpu.VMEM((2 * (pieces - 1), n_fs // 2) + tail, BF16),
            pltpu.VMEM((n_fs - 1,) + tail, BF16),
        ]
    return scratch


def scatter_sems(n_dp, n_fs, chunks):
    count = slot_count(n_dp, n_fs)
    return [
        pltpu.SemaphoreType.DMA((chunks, count)),
        pltpu.SemaphoreType.DMA((chunks, count)),
        pltpu.SemaphoreType.DMA((chunks, 2 ** len(plan_bits(n_dp)))),
    ]


def scatter_kernel(n_dp, n_fs, n_chunks, *refs):
    ins, outs = refs[:n_chunks], refs[n_chunks : 2 * n_chunks]
    scratch = refs[2 * n_chunks : 6 * n_chunks]
    dp, fs = lax.axis_index("dp"), lax.axis_index("fsdp")
    greet(dp, fs, n_dp, n_fs)

    def emit(chunk, total):
        outs[chunk][...] = total

    plans, sends = scatter_plan(dp, fs, n_dp, n_fs, ins, emit, scratch, *refs[6 * n_chunks :])
    for wave in waves(plans):
        for stage in wave:
            stage()
    for wait in sends:
        wait()


def scatter_all(n_dp, n_fs, arrays, collective_id):
    n = len(arrays)
    return pl.pallas_call(
        partial(scatter_kernel, n_dp, n_fs, n),
        out_shape=[jax.ShapeDtypeStruct(a.shape[1:], F32) for a in arrays],
        in_specs=[pl.BlockSpec(memory_space=pltpu.HBM)] * n,
        out_specs=[pl.BlockSpec(memory_space=pltpu.VMEM)] * n,
        scratch_shapes=scatter_scratch(n_dp, n_fs, [a.shape[1:] for a in arrays])
        + scatter_sems(n_dp, n_fs, n),
        compiler_params=pltpu.CompilerParams(
            collective_id=collective_id, has_side_effects=True, vmem_limit_bytes=48 << 20
        ),
        name="scatter_gradients",
    )(*arrays)


def swap_copy(axis, place, count, buffer, send_sem, recv_sem, step):
    return pltpu.make_async_remote_copy(
        src_ref=buffer.at[0],
        dst_ref=buffer.at[step],
        send_sem=send_sem.at[step],
        recv_sem=recv_sem.at[step],
        device_id={axis: lax.rem(place + step, count)},
        device_id_type=MESH,
    )


def swap_start(axis, place, count, *rest):
    for step in range(1, count):
        swap_copy(axis, place, count, *rest, step).start()


def swap_wait(axis, place, count, *rest):
    for step in range(1, count):
        swap_copy(axis, place, count, *rest, step).wait_recv()
    for step in range(1, count):
        swap_copy(axis, place, count, *rest, step).wait_send()


def swap_rows(*args):
    swap_start(*args)
    swap_wait(*args)


def sum_over(x, dp, fs, n_dp, n_fs, octet, line, send_sem, recv_sem, between=None):
    first = ("dp", dp, n_dp, octet, send_sem.at[0], recv_sem.at[0])
    octet[0] = x
    swap_start(*first)
    if between is not None:
        between()
    swap_wait(*first)
    total = octet[0]
    for step in range(1, n_dp):
        total = total + octet[step]
    line[0] = total
    swap_rows("fsdp", fs, n_fs, line, send_sem.at[1], recv_sem.at[1])
    total = line[0]
    for step in range(1, n_fs):
        total = total + line[step]
    return total


def pooled(buffer, count, weight):
    means = [buffer[k, 0:1, :] for k in range(count)]
    center = sum(means[1:], means[0]) * (1.0 / count)
    spread = buffer[0, 1:2, :]
    for k in range(1, count):
        spread = spread + buffer[k, 1:2, :]
    off = (means[0] - center) * (means[0] - center)
    for mean in means[1:]:
        off = off + (mean - center) * (mean - center)
    return center, spread + weight * off


def pool_over(center, spread, frames, dp, fs, n_dp, n_fs, octet, line, send_sem, recv_sem):
    octet[0] = jnp.zeros(octet.shape[1:], F32)
    line[0] = jnp.zeros(line.shape[1:], F32)
    octet[0, 0:1, :] = center
    octet[0, 1:2, :] = spread
    swap_rows("dp", dp, n_dp, octet, send_sem.at[0], recv_sem.at[0])
    center, spread = pooled(octet, n_dp, float(frames))
    line[0, 0:1, :] = center
    line[0, 1:2, :] = spread
    swap_rows("fsdp", fs, n_fs, line, send_sem.at[1], recv_sem.at[1])
    return pooled(line, n_fs, float(frames * n_dp))


def swap_scratch(n_dp, n_fs, channels):
    return [
        pltpu.VMEM((n_dp, 8, channels), F32),
        pltpu.VMEM((n_fs, 8, channels), F32),
        pltpu.SemaphoreType.DMA((2, max(n_dp, n_fs))),
        pltpu.SemaphoreType.DMA((2, max(n_dp, n_fs))),
    ]


def pool_kernel(n_dp, n_fs, frames, x_ref, out_ref, octet, line, send_sem, recv_sem):
    dp, fs = lax.axis_index("dp"), lax.axis_index("fsdp")
    greet(dp, fs, n_dp, n_fs)
    octet[0] = x_ref[...]
    center, spread = pool_over(
        x_ref[0:1, :], x_ref[1:2, :], frames, dp, fs, n_dp, n_fs, octet, line, send_sem, recv_sem
    )
    out_ref[...] = x_ref[...]
    out_ref[0:1, :] = center
    out_ref[1:2, :] = spread


def total_kernel(n_dp, n_fs, frames, x_ref, out_ref, octet, line, send_sem, recv_sem):
    dp, fs = lax.axis_index("dp"), lax.axis_index("fsdp")
    greet(dp, fs, n_dp, n_fs)
    out_ref[...] = sum_over(x_ref[...], dp, fs, n_dp, n_fs, octet, line, send_sem, recv_sem)


def exchange(n_dp, n_fs, x, frames, collective_id, kernel):
    return pl.pallas_call(
        partial(kernel, n_dp, n_fs, frames),
        out_shape=jax.ShapeDtypeStruct(x.shape, F32),
        in_specs=[pl.BlockSpec(memory_space=pltpu.VMEM)],
        out_specs=pl.BlockSpec(memory_space=pltpu.VMEM),
        scratch_shapes=swap_scratch(n_dp, n_fs, x.shape[1]),
        compiler_params=pltpu.CompilerParams(collective_id=collective_id, has_side_effects=True),
        name="exchange_rows",
    )(x)


class Place:
    def __init__(self, dp, fs, n_dp, n_fs):
        self.dp, self.fs, self.n_dp, self.n_fs = dp, fs, n_dp, n_fs
        self.count = (n_dp - 1).bit_length()
        self.bits = [lax.rem(lax.div(dp, 2**k), 2) for k in range(self.count)]
        self.half = n_fs // 2

    def peer(self, bit):
        return (flip(self.dp, 2**bit), self.fs)

    def view(self, ref, free=(), flipped=(), z=None, skip=()):
        index = []
        for bit in reversed(range(self.count)):
            if bit in skip:
                continue
            if bit in free:
                index.append(slice(None))
            else:
                index.append(1 - self.bits[bit] if bit in flipped else self.bits[bit])
        if z is not None:
            index.append(z)
        return ref.at[tuple(index)] if index else ref

    def part(self, which):
        return pl.ds(which * self.half, self.half)


def block_layout(n_dp, n_fs):
    return (2,) * ((n_dp - 1).bit_length()) + (n_fs,)


def hop_orders(place):
    bits = tuple(range(1, place.count))
    return (bits, bits[::-1])


def copy_count(n_dp, n_fs):
    return n_fs - 1 + 2 * ((n_dp - 1).bit_length() - 1) + 1


def block_gather(place, sources, outs, send_sem, recv_sem, local_sem):
    n_fs, fs = place.n_fs, place.fs
    sends = []

    def stages(chunk):
        src, out = sources[chunk], outs[chunk]

        def remote(slot, view_from, view_to, device):
            return pltpu.make_async_remote_copy(
                src_ref=view_from,
                dst_ref=view_to,
                send_sem=send_sem.at[chunk, slot],
                recv_sem=recv_sem.at[chunk, slot],
                device_id=device,
                device_id_type=MESH,
            )

        def launch(make):
            make().start()
            sends.append(lambda: make().wait_send())

        def own_copy():
            return pltpu.make_async_copy(src, place.view(out, z=fs), local_sem.at[chunk])

        def along(step):
            to = lax.rem(fs + step, n_fs)
            return remote(step - 1, src, place.view(out, z=fs), (place.dp, to))

        def start():
            own_copy().start()
            for step in range(1, n_fs):
                launch(lambda step=step: along(step))

        def wait_along():
            own_copy().wait()
            for step in range(1, n_fs):
                origin = lax.rem(fs + n_fs - step, n_fs)
                remote(
                    step - 1, src, place.view(out, z=origin), (place.dp, origin)
                ).wait_recv()

        steps, before = [start], wait_along
        slot = n_fs - 1
        orders = hop_orders(place)
        for depth in range(place.count - 1):
            plan = [(slot + part, part, order[depth], order[:depth]) for part, order in enumerate(orders)]
            slot += 2

            def hop(slot, part, bit, free, arrived):
                view = place.view(out, free, (bit,) if arrived else (), place.part(part))
                return remote(slot, view, view, place.peer(bit))

            def go(plan=plan, before=before, hop=hop):
                before()
                for item in plan:
                    launch(lambda item=item: hop(*item, False))

            def arrive(plan=plan, hop=hop):
                for item in plan:
                    hop(*item, True).wait_recv()

            steps.append(go)
            before = arrive

        def across(arrived, slot=slot):
            free = tuple(range(1, place.count))
            view = place.view(out, free, (0,) if arrived else ())
            return remote(slot, view, view, place.peer(0))

        def cross(before=before):
            before()
            launch(lambda: across(False))

        return steps + [cross, lambda: across(True).wait_recv()]

    return [stages(chunk) for chunk in range(len(outs))], sends


def block_scatter(place, sources, emit, scratch, send_sem, recv_sem, local_sem):
    n_fs, fs = place.n_fs, place.fs
    sends = []
    per = 3 + place.count - 1

    def add_into(kept, other):
        shape = kept.shape[:-3]
        for index in itertools.product(*[range(n) for n in shape]):
            kept[index] = (kept[index].astype(F32) + other[index].astype(F32)).astype(BF16)

    def stages(chunk):
        src = sources[chunk]
        own, cross_in, last, *later = scratch[per * chunk : per * chunk + per]

        def remote(slot, view_from, view_to, device):
            return pltpu.make_async_remote_copy(
                src_ref=view_from,
                dst_ref=view_to,
                send_sem=send_sem.at[chunk, slot],
                recv_sem=recv_sem.at[chunk, slot],
                device_id=device,
                device_id_type=MESH,
            )

        def launch(make):
            make().start()
            sends.append(lambda: make().wait_send())

        every = tuple(range(1, place.count))

        def load():
            return pltpu.make_async_copy(place.view(src, every), own, local_sem.at[chunk])

        def across():
            return remote(0, place.view(src, every, (0,)), cross_in, place.peer(0))

        def start():
            launch(across)
            load().start()

        def fold_cross():
            load().wait()
            across().wait_recv()
            add_into(own, cross_in)

        steps, before = [start], fold_cross
        slot = 1
        orders = [order[::-1] for order in hop_orders(place)]
        for depth in range(place.count - 1):
            plan = []
            for part, order in enumerate(orders):
                free = tuple(order[depth + 1 :])
                plan.append((slot + part, part, order[depth], free, later[depth]))
            slot += 2

            def hop(slot, part, bit, free, buffer):
                view = place.view(own, free, (bit,), place.part(part), skip=(0,))
                return remote(slot, view, buffer.at[part], place.peer(bit))

            def go(plan=plan, before=before, hop=hop):
                before()
                for item in plan:
                    launch(lambda item=item: hop(*item))

            def fold(plan=plan, hop=hop):
                for item in plan:
                    hop(*item).wait_recv()
                    _, part, _, free, buffer = item
                    kept = place.view(own, free, (), place.part(part), skip=(0,))
                    add_into(kept, buffer.at[part])

            steps.append(go)
            before = fold

        def along(step, slot=slot):
            to = lax.rem(fs + step, n_fs)
            view = place.view(own, z=to, skip=(0,))
            return remote(slot + step - 1, view, last.at[step - 1], (place.dp, to))

        def spread(before=before):
            before()
            for step in range(1, n_fs):
                launch(lambda step=step: along(step))

        def finish():
            total = place.view(own, z=fs, skip=(0,))[...].astype(F32)
            for step in range(1, n_fs):
                along(step).wait_recv()
                total = total + last[step - 1].astype(F32)
            emit(chunk, total)

        return steps + [spread, finish]

    return [stages(chunk) for chunk in range(len(sources))], sends


def block_scratch(n_dp, n_fs, blocks, tail):
    hops = (n_dp - 1).bit_length() - 1
    out = []
    for count in blocks:
        entry = (count,) + tail
        zone = (2,) * hops + (n_fs,) + entry
        out += [pltpu.VMEM(zone, BF16), pltpu.VMEM(zone, BF16), pltpu.VMEM((n_fs - 1,) + entry, BF16)]
        for depth in range(hops):
            out.append(pltpu.VMEM((2,) + (2,) * (hops - 1 - depth) + (n_fs // 2,) + entry, BF16))
    return out


def block_sems(n_dp, n_fs, chunks):
    count = copy_count(n_dp, n_fs)
    return [
        pltpu.SemaphoreType.DMA((chunks, count)),
        pltpu.SemaphoreType.DMA((chunks, count)),
        pltpu.SemaphoreType.DMA((chunks,)),
    ]


TILE = 512
STATES = 32
TAPS = 15
REACH = 8
EPSILON = 1e-05
CHUNK = 256
ROWS = 128
VMEM_LIMIT = 60 << 20
TAP_ROW = 24
RATE = 40
MAP_IN = 72
MAP_OUT = 104
TABLE = 136


def sigmoid(v):
    return 0.5 * jnp.tanh(0.5 * v) + 0.5


def dot_nn(a, b):
    return jnp.dot(a, b, preferred_element_type=F32)


def dot_nt(a, b):
    return lax.dot_general(a, b, (((1,), (1,)), ((), ())), preferred_element_type=F32)


def dot_tn(a, b):
    return lax.dot_general(a, b, (((0,), (0,)), ((), ())), preferred_element_type=F32)


def norm_parts(v):
    centered = v - jnp.mean(v, axis=-1, keepdims=True)
    inv = lax.rsqrt(jnp.mean(centered * centered, axis=-1, keepdims=True) + EPSILON)
    return centered * inv, inv


def norm_back(grad, e, inv, gain):
    d = grad * gain
    return (
        d - jnp.mean(d, axis=-1, keepdims=True) - e * jnp.mean(d * e, axis=-1, keepdims=True)
    ) * inv


def fold8(v):
    return jnp.sum(v.reshape((v.shape[0] // 8, 8, v.shape[1])), axis=0)


def by_rows(body, rows=TILE, step=ROWS):
    def run(at, _):
        body(pl.ds(pl.multiple_of(at * step, step), step))
        return 0

    lax.fori_loop(0, rows // step, run, 0)


def columns(at, width=CHUNK):
    return pl.ds(pl.multiple_of(at * width, width), width)


def fill_halo(padded, flags, tiles):
    pitch = TILE + 2 * REACH
    for at in range(tiles):
        base = at * pitch
        if at == 0:
            padded[:, base : base + REACH, :] = jnp.zeros_like(padded[:, base : base + REACH, :])
        if at == tiles - 1:
            end = base + REACH + TILE
            padded[:, end : end + REACH, :] = jnp.zeros_like(padded[:, end : end + REACH, :])
        else:
            keep = flags[at + 1]
            end = base + REACH + TILE
            padded[:, end : end + REACH, :] = (
                padded[:, base + pitch + REACH : base + pitch + 2 * REACH, :] * keep
            )
            padded[:, base + pitch : base + pitch + REACH, :] = (
                padded[:, end - REACH : end, :] * keep
            )


def taps_over(padded, table_ref, store, tiles, reverse, block=64):
    pitch = TILE + 2 * REACH
    per = TILE // block
    lanes = padded.shape[0]
    for lane in range(lanes):
        weights = [
            jnp.broadcast_to(
                table_ref[TAP_ROW + k : TAP_ROW + k + 1, lane * 128 : lane * 128 + 128], (block, 128)
            )
            for k in range(TAPS)
        ]

        def run(at, _):
            tile, inner = at // per, at % per
            base = tile * pitch + inner * block
            total = jnp.zeros((block, 128), F32)
            for k in range(TAPS):
                shift = REACH + (TAPS // 2 - k if reverse else k - TAPS // 2)
                total = total + weights[k] * padded[lane, pl.ds(base + shift, block), :]
            store(lane, tile * TILE + inner * block, base, total)
            return 0

        lax.fori_loop(0, tiles * per, run, 0)


def small_exp(v):
    return 1.0 + v * (1.0 + v * (0.5 + v * (1.0 / 6 + v * (1.0 / 24 + v * (1.0 / 120)))))


def small_expm1_over(v):
    return 1.0 + v * (
        0.5 + v * (1.0 / 6 + v * (1.0 / 24 + v * (1.0 / 120 + v * (1.0 / 720 + v * (1.0 / 5040)))))
    )


def state_terms(table_ref):
    log_decay = -jnp.exp(table_ref[RATE : RATE + STATES, :])
    root = jnp.sqrt(-2.0 * log_decay * small_expm1_over(2.0 * log_decay))
    maps_in = table_ref[MAP_IN : MAP_IN + STATES, :]
    maps_out = table_ref[MAP_OUT : MAP_OUT + STATES, :]
    return log_decay, small_exp(log_decay), root, maps_in, maps_out


def ref_rows(ref):
    return ref.reshape((ref.shape[0] * ref.shape[1], ref.shape[2]))


PIECE = 16
WIDTH = 512


def cols_of(ref, first, at):
    per = WIDTH // CHUNK
    part = ref[:, first + lax.div(at, per), :, columns(lax.rem(at, per))]
    return part.reshape((ref.shape[0] * PIECE, CHUNK))


def rows_of(ref, first, at):
    groups = WIDTH // (4 * PIECE)
    part = ref[pl.ds(at * groups, groups), first : first + 4]
    return part.reshape((WIDTH, WIDTH))


def bias_of(ref, layer, at):
    row = 8 * layer + 2 * at
    return jnp.concatenate([ref[pl.ds(row, 1), :], ref[pl.ds(row + 1, 1), :]], axis=1)


def square_of(ref, at):
    return ref[:, at].reshape((ref.shape[0] * PIECE, WIDTH))


def store_wide(out, first, acc):
    def run(group, _):
        rows = pl.ds(pl.multiple_of(group * PIECE, PIECE), PIECE)
        for k in range(acc.shape[1] // WIDTH):
            out[group, first + k] = acc[rows, k * WIDTH : k * WIDTH + WIDTH].astype(BF16)
        return 0

    lax.fori_loop(0, acc.shape[0] // PIECE, run, 0)


def store_tall(out, first, acc):
    def run(group, _):
        rows = pl.ds(pl.multiple_of(group * 4 * PIECE, 4 * PIECE), 4 * PIECE)
        out[group, first : first + 4] = acc[rows, :].astype(BF16).reshape((4, PIECE, WIDTH))
        return 0

    lax.fori_loop(0, acc.shape[0] // (4 * PIECE), run, 0)


def flat_groups(ref):
    count = 1
    for n in ref.shape[:-3]:
        count *= n
    return ref.reshape((count,) + ref.shape[-3:])


def carries(offsets_ref, counts_ref, tiles):
    out = []
    for tile in range(tiles):
        begins = jnp.int32(0)
        for slot in range(offsets_ref.shape[1]):
            here = (offsets_ref[0, slot] == tile * TILE) & (slot < counts_ref[0])
            begins = jnp.maximum(begins, here.astype(jnp.int32))
        out.append((1 - begins).astype(F32))
    return out


STRETCH = 16
SPREAD = PIECE * STATES


def same_channel(rows, width, per, first=0):
    shape = (rows, width)
    row = lax.rem(lax.broadcasted_iota(jnp.int32, shape, 0), PIECE)
    col = lax.broadcasted_iota(jnp.int32, shape, 1)
    if per == 1:
        return row == lax.rem(col, PIECE)
    return row == lax.div(col, per)


def split_low(v):
    high = v.astype(BF16)
    return high, (v - high.astype(F32)).astype(BF16)


def spread_states(part):
    rows = part.shape[0]
    state = lax.broadcasted_iota(jnp.int32, (STATES, SPREAD), 0)
    col = lax.broadcasted_iota(jnp.int32, (STATES, SPREAD), 1)
    pick_state = (state == lax.rem(col, STATES)).astype(F32).astype(BF16)
    wide = dot_nn(part, pick_state)
    wide = jnp.where(same_channel(rows, SPREAD, STATES), wide, 0.0)
    return jnp.sum(wide.reshape((rows // PIECE, PIECE, SPREAD)), axis=1)


def gather_states(wide):
    groups = wide.shape[0]
    full = jnp.broadcast_to(wide[:, None, :], (groups, PIECE, SPREAD)).reshape((groups * PIECE, SPREAD))
    full = jnp.where(same_channel(groups * PIECE, SPREAD, STATES), full, 0.0)
    state = lax.broadcasted_iota(jnp.int32, (SPREAD, 128), 1)
    row = lax.broadcasted_iota(jnp.int32, (SPREAD, 128), 0)
    pick_state = (state == lax.rem(row, STATES)).astype(F32).astype(BF16)
    high, low = split_low(full)
    return (dot_nn(high, pick_state) + dot_nn(low, pick_state)).T[:STATES, :]


def prepare_states(small, power, shifted, weight):
    groups = small.shape[0]
    entries = lambda first: small[:, :, first : first + STATES].reshape((groups * PIECE, STATES))
    log_decay = -jnp.exp(spread_states(entries(RATE)))
    root = jnp.sqrt(-2.0 * log_decay * small_expm1_over(2.0 * log_decay))
    both = spread_states(entries(MAP_IN)) * root * spread_states(entries(MAP_OUT))
    weight[...] = both
    col = lax.broadcasted_iota(jnp.int32, (SPREAD, 128), 1)
    row = lax.broadcasted_iota(jnp.int32, (SPREAD, 128), 0)
    add_states = (col == lax.div(row, STATES)).astype(F32).astype(BF16)
    power[0] = jnp.ones_like(both)
    decay = small_exp(log_decay)
    for m in range(1, STRETCH):
        power[m] = power[m - 1] * decay
    halves = []
    for half in range(2):
        total = jnp.zeros((groups, 128), F32)
        for k in range(8):
            high, low = split_low(power[half * 8 + k] * both)
            lag = dot_nn(high, add_states) + dot_nn(low, add_states)
            total = total + (pltpu.roll(lag, k * PIECE, 1) if k else lag)
        halves.append(total)
    blank = jnp.zeros((groups, 256), F32)
    padded = jnp.concatenate([blank] + halves, axis=1)
    for m in range(STRETCH):
        shifted[m] = pltpu.roll(padded, 512 - (m + 1) * PIECE, 1)[:, :256]


def group_weights(power, shifted, group, decay_w, lag_w):
    mask = same_channel(PIECE, SPREAD, STATES)
    lag_mask = same_channel(PIECE, 256, 1)
    for m in range(STRETCH):
        rows = slice(m * PIECE, m * PIECE + PIECE)
        line = jnp.broadcast_to(power[m, pl.ds(group, 1), :], (PIECE, SPREAD))
        decay_w[rows, :] = jnp.where(mask, line, 0.0).astype(BF16)
        line = jnp.broadcast_to(shifted[m, pl.ds(group, 1), :], (PIECE, 256))
        lag_w[rows, :] = jnp.where(lag_mask, line, 0.0).astype(BF16)


def swap_blocks(parts):
    col = lax.div(lax.broadcasted_iota(jnp.int32, parts[0].shape, 1), PIECE)
    parts = list(parts)
    for distance in (1, 2, 4):
        low = lax.rem(lax.div(col, distance), 2) == 0
        shift = distance * PIECE
        for a in range(8):
            if a & distance:
                continue
            first, second = parts[a], parts[a + distance]
            parts[a] = jnp.where(low, first, pltpu.roll(second, shift, 1))
            parts[a + distance] = jnp.where(low, pltpu.roll(first, 128 - shift, 1), second)
    return parts


SLAB = 32
TOGETHER = 4


def to_blocks(load, out, blocks, backward):
    for slab in range(blocks // SLAB):
        rows = slice(slab * SLAB, slab * SLAB + SLAB)
        for half in range(2):
            parts = []
            for k in range(8):
                frame = half * 8 + k
                frame = STRETCH - 1 - frame if backward else frame
                parts.append(load(slab * SLAB * STRETCH + frame))
            for group, part in enumerate(swap_blocks(parts)):
                out[group, rows, half * 128 : half * 128 + 128] = part.astype(out.dtype)


def from_blocks(store, ref, blocks, backward):
    for slab in range(blocks // SLAB):
        rows = slice(slab * SLAB, slab * SLAB + SLAB)
        for half in range(2):
            parts = [ref[group, rows, half * 128 : half * 128 + 128] for group in range(8)]
            for k, part in enumerate(swap_blocks(parts)):
                frame = half * 8 + k
                frame = STRETCH - 1 - frame if backward else frame
                store(slab * SLAB * STRETCH + frame, part)


def block_powers(decay):
    q2 = decay * decay
    q4 = q2 * q2
    q8 = q4 * q4
    one = q8 * q8
    two = one * one
    four = two * two
    return one, two, four


def row_powers(one, count=8):
    rows = [one]
    for _ in range(count - 1):
        rows.append(rows[-1] * one)
    return rows


def scan_blocks(source, into, decay, keeps, per, reverse):
    blocks, width = source.shape
    one, two, four = block_powers(decay)
    row = lax.broadcasted_iota(jnp.int32, (8, width), 0)
    if reverse:
        row = 7 - row
    factors = []
    for distance, power in ((1, one), (2, two), (4, four)):
        line = jnp.broadcast_to(power, (8, width))
        factors.append((8 - distance if reverse else distance, jnp.where(row >= distance, line, 0.0)))
    entering = jnp.ones((8, width), F32)
    for bit, power in ((1, one), (2, two), (4, four)):
        line = jnp.broadcast_to(power, (8, width))
        entering = jnp.where(lax.rem(lax.div(row, bit), 2) == 1, entering * line, entering)
    eight = jnp.broadcast_to(four * four, (8, width))
    carry = jnp.zeros((8, width), F32)
    tiles = blocks // 8
    for k in range(tiles):
        tile = tiles - 1 - k if reverse else k
        edge = (tile + 1) * 8 if reverse else tile * 8
        if k and edge % per == 0:
            carry = carry * keeps[edge // per]
        x = source[tile * 8 : tile * 8 + 8, :]
        for shift, factor in factors:
            x = x + factor * pltpu.roll(x, shift, 0)
        moved = pltpu.roll(x, 7 if reverse else 1, 0)
        into[tile * 8 : tile * 8 + 8, :] = jnp.where(row >= 1, moved, 0.0) + entering * carry
        end = x[0:1, :] if reverse else x[7:8, :]
        carry = jnp.broadcast_to(end, (8, width)) + eight * carry


def mix_forward(begin, end, u_ref, y_ref, power, shifted, weight, keeps, ub_out, state_out, blk_in, blk_out, decay_w, lag_w, t_scr, h_scr):
    frames = u_ref.shape[1]
    blocks = frames // STRETCH
    count = decay_w.shape[0]
    several = range(count)

    def lane_tile(lane, _):
        to_blocks(lambda at: u_ref[lane, pl.ds(at, SLAB, stride=STRETCH), :], blk_in, blocks, True)

        def some_groups(k, _):
            place = [k * count + n for n in several]
            groups = [lane * 8 + at for at in place]
            for n in several:
                group_weights(power, shifted, groups[n], decay_w.at[n], lag_w.at[n])
            for n in several:
                ub_out[groups[n]] = blk_in[place[n]]
                t_scr[n] = dot_nn(blk_in[place[n]], decay_w[n])
            for n in several:
                decay = power[1, pl.ds(groups[n], 1), :]
                scan_blocks(t_scr.at[n], h_scr.at[n], decay, keeps, TILE // STRETCH, False)
            for n in several:
                decay = power[1, pl.ds(groups[n], 1), :]
                state = h_scr[n]
                state_out[groups[n]] = state.astype(BF16)
                out = (state * (weight[pl.ds(groups[n], 1), :] * decay)).astype(BF16)
                blk_out[place[n]] = dot_nn(blk_in[place[n]], lag_w[n]) + dot_nt(out, decay_w[n])
            return 0

        lax.fori_loop(0, 8 // count, some_groups, 0)

        def store(at, values):
            y_ref[lane, pl.ds(at, SLAB, stride=STRETCH), :] = values

        from_blocks(store, blk_out, blocks, False)
        return 0

    lax.fori_loop(begin, end, lane_tile, 0)


def mix_backward(
    lane, u_ref, grad, skip, u_tile, u_sem, power, shifted, weight, keeps, ub_ref, state_ref, lags, sums,
    frames_scr, blk_in, blk_out, decay_w, lag_w, stack_scr, e_scr, r_scr,
):
    blocks = frames_scr.shape[2]
    count = decay_w.shape[0]
    several = range(count)
    lanes = u_ref.shape[0]
    copy = lambda at: pltpu.make_async_copy(u_ref.at[at], u_tile, u_sem)
    copy(lane).wait()
    for at in range(STRETCH):
        for slab in range(blocks // SLAB):
            rows = slice(slab * SLAB, slab * SLAB + SLAB)
            first = pl.ds(slab * SLAB * STRETCH + at, SLAB, stride=STRETCH)
            frames_scr[0, at, rows, :] = u_tile[first, :]
            frames_scr[1, at, rows, :] = grad[lane, first, :]

    @pl.when(lane + 1 < lanes)
    def _():
        copy(lane + 1).start()

    def one_lag(lag, _):
        def one_frame(at, total):
            for slab in range(blocks // SLAB):
                rows = slice(slab * SLAB, slab * SLAB + SLAB)
                total = total + frames_scr[1, at, rows, :] * frames_scr[0, at - lag, rows, :]
            return total

        total = lax.fori_loop(lag, STRETCH, one_frame, jnp.zeros((SLAB, 128), F32))
        lags[lane, pl.ds(lag, 1), :] = jnp.sum(total, axis=0, keepdims=True)
        return 0

    lax.fori_loop(0, STRETCH, one_lag, 0)
    for slab in range(blocks // SLAB):
        rows = slice(slab * SLAB, slab * SLAB + SLAB)
        for half in range(2):
            parts = [frames_scr[1, half * 8 + k, rows, :] for k in range(8)]
            for group, part in enumerate(swap_blocks(parts)):
                blk_in[group, rows, half * 128 : half * 128 + 128] = part.astype(BF16)
    position = lax.div(lax.broadcasted_iota(jnp.int32, (1, 256), 1), PIECE).astype(F32)

    def some_groups(k, _):
        place = [k * count + n for n in several]
        groups = [lane * 8 + at for at in place]
        for n in several:
            group_weights(power, shifted, groups[n], decay_w.at[n], lag_w.at[n])
        for n in several:
            gy = blk_in[place[n]]
            stack_scr[n, 0:blocks, :] = gy
            stack_scr[n, blocks : 2 * blocks, :] = (gy.astype(F32) * (position + 1.0)).astype(BF16)
            stack_scr[n, 2 * blocks :, :] = (ub_ref[groups[n]].astype(F32) * position).astype(BF16)
        for n in several:
            e_scr[n] = dot_nn(stack_scr[n], decay_w[n])
        for n in several:
            decay = power[1, pl.ds(groups[n], 1), :]
            own = e_scr.at[n, pl.ds(0, blocks)]
            own[...] = own[...] * decay
            scan_blocks(own, r_scr.at[n], decay, keeps, TILE // STRETCH, True)
        for n in several:
            group = groups[n]
            inverse = 1.0 / power[1, pl.ds(group, 1), :]
            last = 16.0 * power[15, pl.ds(group, 1), :]
            first, second = jnp.zeros((8, SPREAD), F32), jnp.zeros((8, SPREAD), F32)
            for at in range(blocks // 8):
                rows = slice(at * 8, at * 8 + 8)
                state = state_ref[group, rows, :].astype(F32)
                turn = e_scr[n, 2 * blocks + at * 8 : 2 * blocks + at * 8 + 8, :]
                first = first + state * e_scr[n, rows, :]
                second = second + state * e_scr[n, blocks + at * 8 : blocks + at * 8 + 8, :]
                second = second + r_scr[n, rows, :] * (turn * inverse + last * state)
            sums[0, pl.ds(group, 1), :] = jnp.sum(first, axis=0, keepdims=True)
            sums[1, pl.ds(group, 1), :] = jnp.sum(second, axis=0, keepdims=True)
            out = (r_scr[n] * weight[pl.ds(group, 1), :]).astype(BF16)
            blk_out[place[n]] = dot_nt(blk_in[place[n]], lag_w[n]) + dot_nt(out, decay_w[n])
        return 0

    lax.fori_loop(0, 8 // count, some_groups, 0)

    def store(at, values):
        slab, frame = at // (SLAB * STRETCH), at % STRETCH
        through = frames_scr[1, frame, slab * SLAB : slab * SLAB + SLAB, :]
        grad[lane, pl.ds(at, SLAB, stride=STRETCH), :] = values + skip[pl.ds(lane, 1), :] * through

    from_blocks(store, blk_out, blocks, True)


def mix_gradients(lags, sums, table_ref):
    _, decay, root, maps_in, maps_out = state_terms(table_ref)
    coupling = maps_in * root * maps_out
    gmap = gather_states(sums[0])
    gdecay = gather_states(sums[1])
    power = jnp.ones_like(decay)
    for lag in range(STRETCH):
        line = jnp.concatenate([lags[k, lag : lag + 1, :] for k in range(lags.shape[0])], axis=1)
        if lag:
            gdecay = gdecay + float(lag) * power * line
            power = power * decay
        gmap = gmap + power * line
    return gmap, gdecay * coupling


def pack_small(out, scr, place, bias_ref, gains, shifts, conv_bias, taps, rate, maps):
    own = gains.shape[1]
    scr[...] = jnp.zeros_like(scr)
    scr[0:6, :own] = gains[...].astype(F32)
    scr[6:18, :own] = shifts[...].astype(F32)
    scr[18:19, :own] = conv_bias[...].astype(F32)
    scr[TAP_ROW : TAP_ROW + TAPS, :own] = taps[...].astype(F32)
    out[:, :CHUNK] = scr[...].T[:own, :].astype(BF16)
    out[:, RATE:MAP_IN] = rate[...]
    out[:, MAP_IN:MAP_OUT] = maps[0]
    out[:, MAP_OUT:TABLE] = maps[1]
    count = bias_ref.shape[1]
    row = lax.div(place * count, CHUNK)
    inner = place * count - row * CHUNK
    at_row = lax.broadcasted_iota(jnp.int32, (PIECE, CHUNK), 0)
    wide = jnp.zeros((PIECE, CHUNK), F32)
    for layer in range(2):
        line = jnp.broadcast_to(bias_ref[layer : layer + 1, :].astype(F32), (8, count))
        line = jnp.concatenate([line, jnp.zeros((8, CHUNK - count), F32)], axis=1)
        line = pltpu.roll(line, inner, 1)
        wide = wide + jnp.where(at_row == 8 * layer + row, jnp.broadcast_to(line[0:1], wide.shape), 0.0)
    out[:, CHUNK:] = wide.astype(BF16)


def front_kernel(mesh_size, *refs):
    fused = mesh_size is not None
    refs = list(refs)
    take = lambda count: [refs.pop(0) for _ in range(count)]
    offsets_ref, counts_ref, x_ref = take(3)
    if fused:
        n_dp, n_fs = mesh_size
        small_in = take(7)
        up_s, down_s, mixin_s, mixout_s, convin_s, convout_s = take(6)
    else:
        first_v, extra_v, second_v, third_v, fourth_v, table_in, bias_in = take(7)
    (
        h_out,
        x1_out,
        v_out,
        y_out,
        gated_out,
        x2_out,
        p_out,
        u_out,
        w_out,
        stat_out,
        table_ref,
        bias_ref,
        ub_out,
        state_out,
        power,
        shifted,
        weight,
    ) = take(17)
    gathered = take(6) if fused else []
    x1_scr, low_all, low_scr, sum_scr, y_all, padded, act_all = take(7)
    mix_scr = take(6)
    step = pl.program_id(0)
    channels = x_ref.shape[1]
    frames = w_out.shape[0]
    tiles = frames // TILE
    lanes = channels // 128
    gain = lambda k: table_ref[k : k + 1, :]
    shift = lambda k: table_ref[6 + k : 7 + k, :]
    here = lambda rows, tile: pl.ds(pl.multiple_of(tile * TILE + rows.start, ROWS), ROWS)
    flags = carries(offsets_ref, counts_ref, tiles)
    mix_at, last_step = 3 * tiles, 4 * tiles + 1
    if fused:
        landing = take(5)
        sources = take(6)
        turn_scr = refs.pop(0)
        sems = take(3)
        load_sem = refs.pop(0)
        swap = take(4)
        dp, fs = lax.axis_index("dp"), lax.axis_index("fsdp")
        place = Place(dp, fs, n_dp, n_fs)
        landing.append(gathered[5])
        plans, sends = block_gather(place, sources, landing, *sems)
        first_v, extra_v, second_v, third_v, fourth_v = [flat_groups(r) for r in landing[:5]]

        def keep_copy(chunk):
            return pltpu.make_async_copy(landing[chunk], gathered[chunk], load_sem.at[chunk])

        def run(*stages):
            for chunk, stage in stages:
                plans[chunk][stage]()

        @pl.when(step == 0)
        def _():
            pack_small(sources[0].at[0], turn_scr, dp * n_fs + fs, *small_in)
            for k in range(4):
                cols = slice(k * WIDTH, k * WIDTH + WIDTH)
                if k < 2:
                    sources[0][1 + k] = up_s[0, :, cols]
                else:
                    sources[1][k - 2] = up_s[0, :, cols]
                sources[5][1 + k] = up_s[1, :, cols]
                rows = slice(k * PIECE, k * PIECE + PIECE)
                sources[2][k] = down_s[0, rows, :]
                sources[5][5 + k] = down_s[1, rows, :]
            for k in range(2):
                cols = slice(k * WIDTH, k * WIDTH + WIDTH)
                sources[3][k] = mixin_s[:, cols]
                sources[4][1 + k] = convin_s[:, cols]
            sources[4][0] = mixout_s[...]
            sources[5][0] = convout_s[...]
            greet(dp, fs, n_dp, n_fs)
            run((0, 0), (1, 0), (0, 1), (2, 0), (1, 1), (0, 2), (1, 2), (0, 3), (2, 1), (3, 0), (0, 4))
            table_ref[...] = first_v[:, 0, :, :CHUNK].reshape((channels, CHUNK)).astype(F32).T[:TABLE, :]
            total = first_v[0, 0, :, CHUNK:].astype(F32)
            for k in range(1, n_dp * n_fs):
                total = total + first_v[k, 0, :, CHUNK:].astype(F32)
            bias_ref[...] = total

        rest = {1: [(1, 3), (2, 2)], 2: [(3, 1)], tiles: [(1, 4), (4, 0)], tiles + 1: [(2, 3), (3, 2)]}
        rest.update({2 * tiles: [(2, 4), (3, 3), (4, 1)], 2 * tiles + 1: [(5, 0)]})
        rest.update({2 * tiles + 2: [(4, 2)], mix_at: [(3, 4)]})
        rest.update({mix_at + 1: [(4, 4), (5, 2)], last_step: [(5, 3)]})
        for at, stages in rest.items():

            @pl.when(step == at)
            def _(at=at, stages=stages):
                run(*stages)
                saved = {2 * tiles: (0, 1, 2), mix_at: (3,), mix_at + 1: (4,)}
                for chunk in saved.get(at, ()):
                    keep_copy(chunk).start()

    else:

        @pl.when(step == 0)
        def _():
            table_ref[...] = table_in[...]
            bias_ref[...] = bias_in[...]

    @pl.when(step < tiles)
    def _():
        def first(rows):
            e, _ = norm_parts(x_ref[rows, :].astype(F32))
            low_all[here(rows, step), :] = (e * gain(0) + shift(0)).astype(BF16)

        by_rows(first)

    for half, part in enumerate((first_v, extra_v)):

        @pl.when((step >= half * tiles) & (step < half * tiles + tiles))
        def _(half=half, part=part):
            tile_rows = pl.ds(pl.multiple_of((step - half * tiles) * TILE, TILE), TILE)
            for k in range(2):
                c = 2 * half + k
                h = dot_nn(low_all[tile_rows, :], square_of(part, 1 - half + k))
                h = h + bias_of(bias_ref, 0, c)
                h_out[:, k * WIDTH : k * WIDTH + WIDTH] = h.astype(BF16)
                active = (h * sigmoid(h)).astype(BF16)
                act_all[tile_rows, c * WIDTH : c * WIDTH + WIDTH] = active

    @pl.when((step >= 2 * tiles) & (step < mix_at))
    def _():
        at = step - 2 * tiles
        tile_rows = pl.ds(pl.multiple_of(at * TILE, TILE), TILE)
        total = dot_nn(act_all[tile_rows, :WIDTH], rows_of(second_v, 0, 0))
        for c in range(1, 4):
            cols = slice(c * WIDTH, c * WIDTH + WIDTH)
            total = total + dot_nn(act_all[tile_rows, cols], rows_of(second_v, 0, c))
        sum_scr[...] = total

        def second(rows):
            x1 = x_ref[rows, :].astype(F32) + 0.5 * (sum_scr[rows, :] + shift(6))
            x1_out[rows, :] = x1
            x1_scr[here(rows, at), :] = x1
            e, _ = norm_parts(x1)
            low_all[here(rows, at), :] = (e * gain(1) + shift(1)).astype(BF16)

        by_rows(second)

    @pl.when(step == mix_at)
    def _():
        prepare_states(first_v[:, 0, :, :CHUNK], power, shifted, weight)

        def project(tile, _):
            rows = pl.ds(pl.multiple_of(tile * TILE, TILE), TILE)
            u = dot_nn(low_all[rows, :], square_of(third_v, 0))
            for lane in range(lanes):
                u_out[lane, rows, :] = u[:, lane * 128 : lane * 128 + 128]
            return 0

        lax.fori_loop(0, tiles, project, 0)
        if fused:
            run((4, 3))
        mixing = (u_out, y_all, power, shifted, weight, flags, ub_out, state_out) + tuple(mix_scr)
        mix_forward(0, lanes // 2, *mixing)
        if fused:
            run((5, 1))
        mix_forward(lanes // 2, lanes, *mixing)

    @pl.when((step > mix_at) & (step < last_step))
    def _():
        at = step - mix_at - 1
        whole_tile = pl.ds(pl.multiple_of(at * TILE, TILE), TILE)
        v_out[...] = dot_nn(low_all[whole_tile, :], square_of(third_v, 1)).astype(BF16)

        def gate(rows):
            join = lambda ref: jnp.concatenate([ref[lane, here(rows, at), :] for lane in range(lanes)], axis=1)
            y = join(y_all) + shift(11) * join(u_out)
            v = v_out[rows, :].astype(F32)
            y_out[rows, :] = y.astype(BF16)
            gated_out[rows, :] = (y * (v * sigmoid(v))).astype(BF16)

        by_rows(gate)
        sum_scr[...] = dot_nn(gated_out[...], square_of(fourth_v, 0))

        def third(rows):
            x2 = x1_scr[here(rows, at), :] + (sum_scr[rows, :] + shift(8))
            x2_out[rows, :] = x2
            e, _ = norm_parts(x2)
            low_scr[rows, :] = (e * gain(2) + shift(2)).astype(BF16)

        by_rows(third)
        pitch = TILE + 2 * REACH

        def widen(c, _):
            cols = columns(c)
            right = columns(c + channels // CHUNK)
            left_part = dot_nn(low_scr[...], cols_of(fourth_v, 1, c)) + table_ref[15:16, cols]
            right_part = dot_nn(low_scr[...], cols_of(fourth_v, 2, c)) + table_ref[16:17, cols]
            p_out[:, cols] = left_part.astype(BF16)
            p_out[:, right] = right_part.astype(BF16)
            g = left_part * sigmoid(right_part)
            place = pl.ds(pl.multiple_of(at * pitch + REACH, 8), TILE)
            for k in range(CHUNK // 128):
                padded[c * (CHUNK // 128) + k, place, :] = g[:, k * 128 : k * 128 + 128]
            return 0

        lax.fori_loop(0, channels // CHUNK, widen, 0)

    @pl.when(step == last_step)
    def _():
        fill_halo(padded, flags, tiles)

        def store(lane, row, base, total):
            w_out[pl.ds(pl.multiple_of(row, 64), 64), lane * 128 : lane * 128 + 128] = total

        taps_over(padded, table_ref, store, tiles, False)
        stat_out[...] = jnp.zeros_like(stat_out)

        def total(at, _):
            rows = pl.ds(pl.multiple_of(at * ROWS, ROWS), ROWS)
            stat_out[...] += fold8(w_out[rows, :])
            return 0

        lax.fori_loop(0, frames // ROWS, total, 0)
        center = jnp.sum(stat_out[...], axis=0, keepdims=True) * (1.0 / frames)
        stat_out[...] = jnp.zeros_like(stat_out)

        def spread(at, _):
            rows = pl.ds(pl.multiple_of(at * ROWS, ROWS), ROWS)
            off = w_out[rows, :] - center
            stat_out[...] += fold8(off * off)
            return 0

        lax.fori_loop(0, frames // ROWS, spread, 0)
        around = jnp.sum(stat_out[...], axis=0, keepdims=True)
        if fused:
            center, around = pool_over(center, around, frames, dp, fs, n_dp, n_fs, *swap)
            around = lax.rsqrt(around * (1.0 / (frames * n_dp * n_fs)) + EPSILON)
        stat_out[...] = jnp.zeros_like(stat_out)
        stat_out[0:1, :] = center
        stat_out[1:2, :] = around
        if fused:
            run((5, 4))
            for chunk in range(5):
                keep_copy(chunk).wait()
            for wait in sends:
                wait()


def whole(shape):
    zeros = (0,) * len(shape)
    return pl.BlockSpec(shape, lambda *_: zeros, pipeline_mode=pl.Buffered(1))


def params(collective_id=None):
    if collective_id is None:
        return pltpu.CompilerParams(
            dimension_semantics=("arbitrary",), vmem_limit_bytes=VMEM_LIMIT
        )
    return pltpu.CompilerParams(
        dimension_semantics=("arbitrary",),
        vmem_limit_bytes=VMEM_LIMIT,
        collective_id=collective_id,
        has_side_effects=True,
    )


SMEM_SPEC = pl.BlockSpec(memory_space=pltpu.SMEM)
HBM_SPEC = pl.BlockSpec(memory_space=pltpu.HBM)


def front(mesh_size, offsets, counts, x, small, weights, hidden, collective_id=None):
    fused = mesh_size is not None
    frames, channels = x.shape
    tiles = frames // TILE
    clip = lambda i, first: jnp.clip(i - first, 0, tiles - 1)
    twice = lambda i: (jnp.where(i < tiles, i, jnp.where(i < 2 * tiles, tiles - 1, clip(i, 2 * tiles))), 0)
    halves = lambda i: (jnp.where(i < tiles, i, clip(i, tiles)), jnp.where(i < tiles, 0, 1))
    place = lambda i: clip(i, 3 * tiles + 1)
    late = lambda width: pl.BlockSpec((TILE, width), lambda i: (place(i), 0))
    shape = lambda width, kind: jax.ShapeDtypeStruct((frames, width), kind)
    groups, blocks = channels // PIECE, frames // STRETCH
    out_shape = [
        shape(hidden, BF16),
        shape(channels, F32),
        shape(channels, BF16),
        shape(channels, BF16),
        shape(channels, BF16),
        shape(channels, F32),
        shape(2 * channels, BF16),
        jax.ShapeDtypeStruct((channels // 128, frames, 128), F32),
        shape(channels, F32),
        jax.ShapeDtypeStruct((8, channels), F32),
        jax.ShapeDtypeStruct((TABLE, channels), F32),
        jax.ShapeDtypeStruct((16, CHUNK), F32),
        jax.ShapeDtypeStruct((groups, blocks, STRETCH * PIECE), BF16),
        jax.ShapeDtypeStruct((groups, blocks, SPREAD), BF16),
        jax.ShapeDtypeStruct((STRETCH, groups, SPREAD), F32),
        jax.ShapeDtypeStruct((STRETCH, groups, STRETCH * PIECE), F32),
        jax.ShapeDtypeStruct((groups, SPREAD), F32),
    ]
    out_specs = [
        pl.BlockSpec((TILE, hidden // 2), halves),
        pl.BlockSpec((TILE, channels), lambda i: (clip(i, 2 * tiles), 0)),
    ]
    out_specs += [late(channels)] * 4 + [late(2 * channels)]
    out_specs += [whole(s.shape) for s in out_shape[7:]]
    scratch = [
        pltpu.VMEM((frames, channels), F32),
        pltpu.VMEM((frames, channels), BF16),
        pltpu.VMEM((TILE, channels), BF16),
        pltpu.VMEM((TILE, channels), F32),
        pltpu.VMEM((channels // 128, frames, 128), F32),
        pltpu.VMEM((channels // 128, tiles * (TILE + 2 * REACH), 128), F32),
        pltpu.VMEM((frames, hidden), BF16),
        pltpu.VMEM((8, blocks, STRETCH * PIECE), BF16),
        pltpu.VMEM((8, blocks, STRETCH * PIECE), F32),
        pltpu.VMEM((TOGETHER, STRETCH * PIECE, SPREAD), BF16),
        pltpu.VMEM((TOGETHER, STRETCH * PIECE, STRETCH * PIECE), BF16),
        pltpu.VMEM((TOGETHER, blocks, SPREAD), F32),
        pltpu.VMEM((TOGETHER, blocks, SPREAD), F32),
    ]
    operands = (weights if not fused else small + weights) + (small if not fused else [])
    if fused:
        layout = block_layout(*mesh_size)
        blocks = (3, 2, 4, 2, 3, 9)
        chunks = [jax.ShapeDtypeStruct(layout + (k, PIECE, WIDTH), BF16) for k in blocks]
        out_shape += chunks
        out_specs += [HBM_SPEC] * len(chunks)
        scratch += [pltpu.VMEM(c.shape, BF16) for c in chunks[:5]]
        scratch += [pltpu.VMEM((k, PIECE, WIDTH), BF16) for k in blocks]
        scratch += [pltpu.VMEM((CHUNK, 128), F32)]
        scratch += block_sems(*mesh_size, len(chunks)) + [pltpu.SemaphoreType.DMA((5,))]
        scratch += swap_scratch(*mesh_size, channels)
    return pl.pallas_call(
        partial(front_kernel, mesh_size),
        grid=(4 * tiles + 2,),
        in_specs=[SMEM_SPEC, SMEM_SPEC, pl.BlockSpec((TILE, channels), twice)] + [whole(a.shape) for a in operands],
        out_specs=out_specs,
        out_shape=out_shape,
        scratch_shapes=scratch,
        compiler_params=params(collective_id),
        name="front",
    )(offsets, counts, x, *operands)


def middle_kernel(
    mesh_size,
    x2_ref,
    w_ref,
    cot_ref,
    blocks_ref,
    bias_ref,
    vec_ref,
    stat_ref,
    out_ref,
    gx3_ref,
    gnb_ref,
    gblocks_out,
    gbias_out,
    gvec_out,
    stat_out,
    up_acc,
    down_acc,
    convout_acc,
    bias_acc,
    vec_acc,
    h_scr,
    low_scr,
    turn_scr,
    act_scr,
    grad_scr,
    sum_scr,
    x3_scr,
    *swap,
):
    at = pl.program_id(0)
    tiles = pl.num_programs(0)
    channels = x2_ref.shape[1]
    if mesh_size is not None:
        n_dp, n_fs = mesh_size
        dp, fs = lax.axis_index("dp"), lax.axis_index("fsdp")

        @pl.when(at == 0)
        def _():
            greet(dp, fs, n_dp, n_fs)

    hidden = up_acc.shape[1]
    gain = lambda k: vec_ref[k : k + 1, :]
    shift = lambda k: vec_ref[6 + k : 7 + k, :]
    center, scale = stat_ref[0:1, :], stat_ref[1:2, :]

    @pl.when(at == 0)
    def _():
        for ref in (up_acc, down_acc, convout_acc, bias_acc, vec_acc):
            ref[...] = jnp.zeros_like(ref)

    def normed(rows):
        e = (w_ref[rows, :] - center) * scale
        return e, e * gain(5) + shift(5)

    def first(rows):
        _, nb = normed(rows)
        act_scr[rows, :] = (nb * sigmoid(nb)).astype(BF16)

    by_rows(first)
    sum_scr[...] = dot_nn(act_scr[...], square_of(blocks_ref, 0))

    def second(rows):
        x3 = x2_ref[rows, :] + (sum_scr[rows, :] + vec_ref[18:19, :])
        x3_scr[rows, :] = x3
        e, _ = norm_parts(x3)
        low_scr[rows, :] = (e * gain(3) + shift(3)).astype(BF16)
        sum_scr[rows, :] = jnp.zeros((ROWS, channels), F32)

    by_rows(second)

    def forward(c, _):
        cols = columns(c, WIDTH)
        h = dot_nn(low_scr[...], square_of(blocks_ref, 1 + c)) + bias_of(bias_ref, 1, c)
        h_scr[:, cols] = h
        active = (h * sigmoid(h)).astype(BF16)
        sum_scr[...] += dot_nn(active, rows_of(blocks_ref, 5, c))
        return 0

    lax.fori_loop(0, hidden // WIDTH, forward, 0)
    turn_scr[...] = low_scr[...].T

    def last(rows):
        x4 = x3_scr[rows, :] + 0.5 * (sum_scr[rows, :] + shift(7))
        e, inv = norm_parts(x4)
        out_ref[rows, :] = (e * gain(4) + shift(4)).astype(BF16)
        cot = cot_ref[rows, :].astype(F32)
        vec_acc[0] += fold8(cot * e)
        vec_acc[1] += fold8(cot)
        gx4 = norm_back(cot, e, inv, gain(4))
        gx3_ref[rows, :] = gx4
        low = (0.5 * gx4).astype(BF16)
        grad_scr[rows, :] = low
        vec_acc[2] += fold8(low.astype(F32))
        sum_scr[rows, :] = jnp.zeros((ROWS, channels), F32)

    by_rows(last)

    def backward(c, _):
        cols = columns(c, WIDTH)
        h = h_scr[:, cols]
        sig = sigmoid(h)
        active = h * sig
        gate = dot_nt(grad_scr[...], rows_of(blocks_ref, 5, c))
        grad_h = (gate * (sig * (1.0 + h - active))).astype(BF16)
        bias_acc[:, cols] += fold8(grad_h.astype(F32))
        down_acc[cols, :] += dot_tn(active.astype(BF16), grad_scr[...])
        up_acc[:, cols] += dot_nn(turn_scr[...], grad_h)
        sum_scr[...] += dot_nt(grad_h, square_of(blocks_ref, 1 + c))
        return 0

    lax.fori_loop(0, hidden // WIDTH, backward, 0)

    def fourth(rows):
        e, inv = norm_parts(x3_scr[rows, :])
        grad = sum_scr[rows, :]
        vec_acc[3] += fold8(grad * e)
        vec_acc[4] += fold8(grad)
        gx3 = gx3_ref[rows, :] + norm_back(grad, e, inv, gain(3))
        gx3_ref[rows, :] = gx3
        low = gx3.astype(BF16)
        grad_scr[rows, :] = low
        vec_acc[5] += fold8(low.astype(F32))

    by_rows(fourth)
    convout_acc[...] += dot_tn(act_scr[...], grad_scr[...])
    sum_scr[...] = dot_nt(grad_scr[...], square_of(blocks_ref, 0))

    def fifth(rows):
        e, nb = normed(rows)
        sig = sigmoid(nb)
        gnb = sum_scr[rows, :] * (sig * (1.0 + nb * (1.0 - sig)))
        gnb_ref[rows, :] = gnb
        vec_acc[6] += fold8(gnb * e)
        vec_acc[7] += fold8(gnb)

    by_rows(fifth)

    @pl.when(at == tiles - 1)
    def _():
        for k in range(8):
            gvec_out[k : k + 1, :] = jnp.sum(vec_acc[k], axis=0, keepdims=True)

        def convert():
            store_wide(gblocks_out, 0, convout_acc)
            store_wide(gblocks_out, 1, up_acc)
            store_tall(gblocks_out, 5, down_acc)
            gbias_out[...] = jnp.broadcast_to(
                jnp.sum(bias_acc[...], axis=0, keepdims=True), gbias_out.shape
            )

        stat_out[...] = stat_ref[...]
        if mesh_size is None:
            convert()
        else:
            total = sum_over(gvec_out[...], dp, fs, n_dp, n_fs, *swap, between=convert)
            share = gain(5) * (1.0 / (TILE * tiles * n_dp * n_fs))
            stat_out[2:3, :] = total[7:8, :] * share
            stat_out[3:4, :] = total[6:7, :] * share


def middle(mesh_size, x2, w, cot, blocks, bias, vec, stat, hidden, collective_id=None):
    frames, channels = x2.shape
    tiles = frames // TILE
    row = lambda width: pl.BlockSpec((TILE, width), lambda i: (i, 0))
    shapes = [
        jax.ShapeDtypeStruct((frames, channels), BF16),
        jax.ShapeDtypeStruct((frames, channels), F32),
        jax.ShapeDtypeStruct((frames, channels), F32),
        jax.ShapeDtypeStruct(blocks.shape, BF16),
        jax.ShapeDtypeStruct((8, hidden), F32),
        jax.ShapeDtypeStruct((8, channels), F32),
        jax.ShapeDtypeStruct((8, channels), F32),
    ]
    swap = [] if mesh_size is None else swap_scratch(*mesh_size, channels)
    return pl.pallas_call(
        partial(middle_kernel, mesh_size),
        grid=(tiles,),
        in_specs=[row(channels)] * 3
        + [whole(a.shape) for a in (blocks, bias, vec, stat)],
        out_specs=[row(channels)] * 3 + [whole(s.shape) for s in shapes[3:]],
        out_shape=shapes,
        scratch_shapes=[
            pltpu.VMEM((channels, hidden), F32),
            pltpu.VMEM((hidden, channels), F32),
            pltpu.VMEM((channels, channels), F32),
            pltpu.VMEM((8, hidden), F32),
            pltpu.VMEM((8, 8, channels), F32),
            pltpu.VMEM((TILE, hidden), F32),
            pltpu.VMEM((TILE, channels), BF16),
            pltpu.VMEM((channels, TILE), BF16),
            pltpu.VMEM((TILE, channels), BF16),
            pltpu.VMEM((TILE, channels), BF16),
            pltpu.VMEM((TILE, channels), F32),
            pltpu.VMEM((TILE, channels), F32),
        ]
        + swap,
        compiler_params=params(collective_id),
        name="middle",
    )(x2, w, cot, blocks, bias, vec, stat)


def back_kernel(mesh_size, *refs):
    fused = mesh_size is not None
    refs = list(refs)
    take = lambda count: [refs.pop(0) for _ in range(count)]
    offsets_ref, counts_ref, w_ref, gnb_ref, p_ref = take(5)
    x2_ref, gx3_ref, gated_ref, y_ref, v_ref, x1_ref = take(6)
    u_ref, ub_ref, state_ref, power, shifted, weight, mixin_ref, middle_ref, vec_ref, stat_ref = take(10)
    sources = take(1) if fused else []
    gx1_ref, gin_out, gvec_out, gtaps_ref, gmap_out, gdecay_out = take(6)
    reduced = take(2) if fused else []
    mid_ref = None if fused else refs.pop(0)
    wide_acc, mixout_acc, vec_acc, low_scr, wide_scr, sum_scr = take(6)
    padded, gpad, gv_all, lags, sums, skip, u_tile, u_sem = take(8)
    mix_scr = take(8)
    step = pl.program_id(0)
    channels = x2_ref.shape[1]
    frames = u_ref.shape[1]
    tiles = frames // TILE
    lanes = channels // 128
    pitch = TILE + 2 * REACH
    conv_at, mix_at = tiles, 2 * tiles + 1
    last_step = 3 * tiles + 1
    gain = lambda k: vec_ref[k : k + 1, :]
    shift = lambda k: vec_ref[6 + k : 7 + k, :]
    left, right = slice(0, channels), slice(channels, 2 * channels)
    flags = carries(offsets_ref, counts_ref, tiles)
    schedule = {}
    if fused:
        n_dp, n_fs = mesh_size
        place = Place(lax.axis_index("dp"), lax.axis_index("fsdp"), n_dp, n_fs)
        mid_src = refs.pop(0)
        mid_ref = flat_groups(mid_src)
        scratch = take(2 * (2 + place.count))

        def emit(chunk, total):
            reduced[chunk][...] = total

        plans, sends = block_scatter(place, sources + [mid_src], emit, scratch, *take(3))
        first = [(0, 0), (conv_at, 1), (conv_at + 2, 0), (conv_at + 3, 0), (mix_at, 1)]
        second = [(mix_at, 0), (mix_at, 1), (mix_at + 1, 0), (mix_at + 2, 0), (last_step, 1)]
        for chunk, points in enumerate((first, second)):
            for stage, point in enumerate(points):
                schedule.setdefault(point, []).append((stage, chunk))

    def progress(at, part):
        for stage, chunk in sorted(schedule.get((at, part), [])):
            plans[chunk][stage]()

    @pl.when(step == 0)
    def _():
        for ref in (wide_acc, mixout_acc, vec_acc):
            ref[...] = jnp.zeros_like(ref)
        if fused:
            greet(place.dp, place.fs, n_dp, n_fs)

    for at in sorted({key[0] for key in schedule if key[1] == 0 and key[0] != mix_at}):

        @pl.when(step == at)
        def _(at=at):
            progress(at, 0)

    @pl.when(step < tiles)
    def _():
        center, scale = stat_ref[0:1, :], stat_ref[1:2, :]
        plain, cross = stat_ref[2:3, :], stat_ref[3:4, :]

        def fill(index, _):
            rows = pl.ds(pl.multiple_of(index * 64, 64), 64)
            spot = pl.ds(pl.multiple_of(step * pitch + REACH + index * 64, 8), 64)
            e = (w_ref[rows, :] - center) * scale
            d = gnb_ref[rows, :] * gain(5)
            gw = scale * (d - plain - e * cross)
            g = p_ref[rows, left].astype(F32) * sigmoid(p_ref[rows, right].astype(F32))
            for lane in range(lanes):
                cols = slice(lane * 128, lane * 128 + 128)
                padded[lane, spot, :] = gw[:, cols]
                gpad[lane, spot, :] = g[:, cols]
            return 0

        lax.fori_loop(0, TILE // 64, fill, 0)

    @pl.when(step == conv_at)
    def _():
        fill_halo(padded, flags, tiles)
        fill_halo(gpad, flags, tiles)
        block = 64
        per = TILE // block
        gtaps_ref[...] = jnp.zeros_like(gtaps_ref)
        for lane in range(lanes):

            def corr(index, sums, lane=lane):
                base = (index // per) * pitch + (index % per) * block
                here = padded[lane, pl.ds(pl.multiple_of(base + REACH, 8), block), :]
                return tuple(
                    s + fold8(here * gpad[lane, pl.ds(base + REACH + k - TAPS // 2, block), :])
                    for k, s in enumerate(sums)
                )

            found = lax.fori_loop(0, tiles * per, corr, (jnp.zeros((8, 128), F32),) * TAPS)
            for k in range(TAPS):
                gtaps_ref[k : k + 1, lane * 128 : lane * 128 + 128] = jnp.sum(
                    found[k], axis=0, keepdims=True
                )
        progress(conv_at, 1)

        def store(lane, row, base, total):
            gpad[lane, pl.ds(pl.multiple_of(base + REACH, 8), 64), :] = total

        taps_over(padded, vec_ref, store, tiles, True)

    @pl.when((step > conv_at) & (step < mix_at))
    def _():
        at = step - conv_at - 1

        def first(rows):
            spot = pl.ds(pl.multiple_of(at * pitch + REACH + rows.start, 8), ROWS)
            grad = jnp.concatenate([gpad[lane, spot, :] for lane in range(lanes)], axis=1)
            sig = sigmoid(p_ref[rows, right].astype(F32))
            gl = (grad * sig).astype(BF16)
            gr = (grad * p_ref[rows, left].astype(F32) * (sig * (1.0 - sig))).astype(BF16)
            wide_scr[rows, left] = gl
            wide_scr[rows, right] = gr
            vec_acc[0] += fold8(gl.astype(F32))
            vec_acc[1] += fold8(gr.astype(F32))
            e, _ = norm_parts(x2_ref[rows, :])
            low_scr[rows, :] = (e * gain(2) + shift(2)).astype(BF16)

        by_rows(first)
        turned = low_scr[...].T
        wide_acc[...] += dot_nn(turned, wide_scr[...])
        sum_scr[...] = dot_nt(wide_scr[:, left], square_of(middle_ref, 1)) + dot_nt(
            wide_scr[:, right], square_of(middle_ref, 2)
        )

        def second(rows):
            here = pl.ds(pl.multiple_of(at * TILE + rows.start, ROWS), ROWS)
            e, inv = norm_parts(x2_ref[rows, :])
            grad = sum_scr[rows, :]
            vec_acc[2] += fold8(grad * e)
            vec_acc[3] += fold8(grad)
            gx2 = gx3_ref[rows, :] + norm_back(grad, e, inv, gain(2))
            spot = pl.ds(pl.multiple_of(at * pitch + REACH + rows.start, 8), ROWS)
            for lane in range(lanes):
                gpad[lane, spot, :] = gx2[:, lane * 128 : lane * 128 + 128]
            low = gx2.astype(BF16)
            low_scr[rows, :] = low
            vec_acc[4] += fold8(low.astype(F32))

        by_rows(second)
        mixout_acc[...] += dot_tn(gated_ref[...], low_scr[...])
        sum_scr[...] = dot_nt(low_scr[...], square_of(middle_ref, 0))

        def third(rows):
            here = pl.ds(pl.multiple_of(at * TILE + rows.start, ROWS), ROWS)
            grad = sum_scr[rows, :]
            v = v_ref[rows, :].astype(F32)
            sig = sigmoid(v)
            swish = v * sig
            gy = grad * swish
            for lane in range(lanes):
                padded[lane, here, :] = gy[:, lane * 128 : lane * 128 + 128]
            gv_all[here, :] = (
                grad * y_ref[rows, :].astype(F32) * (sig * (1.0 + v - swish))
            ).astype(BF16)


        by_rows(third)

    @pl.when(step == mix_at)
    def _():
        pltpu.make_async_copy(u_ref.at[0], u_tile, u_sem).start()
        store_wide(mid_ref, 0, mixout_acc)
        store_wide(mid_ref, 1, wide_acc)
        wide_acc[...] = jnp.zeros_like(wide_acc)
        for lane in range(lanes):
            skip[lane : lane + 1, :] = vec_ref[17:18, lane * 128 : lane * 128 + 128]
        progress(mix_at, 0)

        def one(lane, _):
            mix_backward(
                lane, u_ref, padded, skip, u_tile, u_sem, power, shifted, weight, flags, ub_ref, state_ref, lags, sums, *mix_scr
            )
            return 0

        lax.fori_loop(0, lanes // 2, one, 0)
        progress(mix_at, 1)
        lax.fori_loop(lanes // 2, lanes, one, 0)
        gmap, gdecay = mix_gradients(lags, sums, vec_ref)
        gmap_out[...] = gmap
        gdecay_out[...] = gdecay

    @pl.when(step > mix_at)
    def _():
        at = step - mix_at - 1

        def fourth(rows):
            here = pl.ds(pl.multiple_of(at * TILE + rows.start, ROWS), ROWS)
            gu = jnp.concatenate([padded[lane, here, :] for lane in range(lanes)], axis=1)
            wide_scr[rows, left] = gu.astype(BF16)
            wide_scr[rows, right] = gv_all[here, :]
            e, _ = norm_parts(x1_ref[rows, :])
            low_scr[rows, :] = (e * gain(1) + shift(1)).astype(BF16)

        by_rows(fourth)
        turned = low_scr[...].T
        wide_acc[...] += dot_nn(turned, wide_scr[...])
        sum_scr[...] = dot_nt(wide_scr[:, left], square_of(mixin_ref, 0)) + dot_nt(
            wide_scr[:, right], square_of(mixin_ref, 1)
        )

        def fifth(rows):
            e, inv = norm_parts(x1_ref[rows, :])
            grad = sum_scr[rows, :]
            vec_acc[6] += fold8(grad * e)
            vec_acc[7] += fold8(grad)
            spot = pl.ds(pl.multiple_of(at * pitch + REACH + rows.start, 8), ROWS)
            gx2 = jnp.concatenate([gpad[lane, spot, :] for lane in range(lanes)], axis=1)
            gx1_ref[rows, :] = gx2 + norm_back(grad, e, inv, gain(1))

        by_rows(fifth)

    @pl.when(step == last_step)
    def _():
        store_wide(gin_out, 0, wide_acc)
        for k in range(8):
            gvec_out[k : k + 1, :] = jnp.sum(vec_acc[k], axis=0, keepdims=True)
        gvec_out[5:6, :] = jnp.concatenate([lags[k, 0:1, :] for k in range(lanes)], axis=1)
        if fused:
            progress(last_step, 1)
            for wait in sends:
                wait()


def back(mesh_size, offsets, counts, tiled, wholes, grads=(), collective_id=None):
    fused = mesh_size is not None
    frames, channels = tiled[0].shape
    tiles = frames // TILE
    groups, blocks = channels // PIECE, frames // STRETCH
    late = lambda i, first: jnp.clip(i - first, 0, tiles - 1)
    filling = lambda i: (late(i, 0), 0)
    twice = lambda i: (jnp.where(i < tiles, i, late(i, tiles + 1)), 0)
    mixing = lambda i: (late(i, tiles + 1), 0)
    ending = lambda i: (late(i, 2 * tiles + 2), 0)
    maps = [filling, filling, twice] + [mixing] * 5 + [ending]
    state = jax.ShapeDtypeStruct((STATES, channels), F32)
    bf16 = lambda *shape: jax.ShapeDtypeStruct(shape, BF16)
    shapes = [
        jax.ShapeDtypeStruct((frames, channels), F32),
        bf16(groups, 2, PIECE, WIDTH),
        jax.ShapeDtypeStruct((8, channels), F32),
        jax.ShapeDtypeStruct((16, channels), F32),
        state,
        state,
    ]
    pad = pltpu.VMEM((channels // 128, tiles * (TILE + 2 * REACH), 128), F32)
    scratch = [
        pltpu.VMEM((channels, 2 * channels), F32),
        pltpu.VMEM((channels, channels), F32),
        pltpu.VMEM((8, 8, channels), F32),
        pltpu.VMEM((TILE, channels), BF16),
        pltpu.VMEM((TILE, 2 * channels), BF16),
        pltpu.VMEM((TILE, channels), F32),
        pad,
        pad,
        pltpu.VMEM((frames, channels), BF16),
        pltpu.VMEM((channels // 128, STRETCH, 128), F32),
        pltpu.VMEM((2, groups, SPREAD), F32),
        pltpu.VMEM((8, 128), F32),
        pltpu.VMEM((frames, 128), F32),
        pltpu.SemaphoreType.DMA(()),
        pltpu.VMEM((2, STRETCH, blocks, 128), F32),
        pltpu.VMEM((8, blocks, STRETCH * PIECE), BF16),
        pltpu.VMEM((8, blocks, STRETCH * PIECE), F32),
        pltpu.VMEM((2, STRETCH * PIECE, SPREAD), BF16),
        pltpu.VMEM((2, STRETCH * PIECE, STRETCH * PIECE), BF16),
        pltpu.VMEM((2, 3 * blocks, STRETCH * PIECE), BF16),
        pltpu.VMEM((2, 3 * blocks, SPREAD), F32),
        pltpu.VMEM((2, blocks, SPREAD), F32),
    ]
    if fused:
        counts_of = [grads[0].shape[-3], 3]
        shapes += [jax.ShapeDtypeStruct((k, PIECE, WIDTH), F32) for k in counts_of]
        scratch += [pltpu.VMEM(block_layout(*mesh_size) + (3, PIECE, WIDTH), BF16)]
        scratch += block_scratch(*mesh_size, counts_of, (PIECE, WIDTH))
        scratch += block_sems(*mesh_size, 2)
    else:
        shapes.append(bf16(groups, 3, PIECE, WIDTH))
    return pl.pallas_call(
        partial(back_kernel, mesh_size),
        grid=(3 * tiles + 2,),
        in_specs=[SMEM_SPEC, SMEM_SPEC]
        + [pl.BlockSpec((TILE, a.shape[1]), index) for a, index in zip(tiled, maps)]
        + [HBM_SPEC]
        + [whole(a.shape) for a in wholes[1:]]
        + [HBM_SPEC] * len(grads),
        out_specs=[pl.BlockSpec((TILE, channels), ending)] + [whole(s.shape) for s in shapes[1:]],
        out_shape=shapes,
        scratch_shapes=scratch,
        compiler_params=params(collective_id),
        name="back",
    )(offsets, counts, *tiled, *wholes, *grads)


def small_gradients(out, gvec1, gvec2, gvec3, gtaps, gmap, gdecay, table_ref):
    out[...] = jnp.zeros_like(out)
    gains = {1: (gvec2, 6), 2: (gvec2, 2), 3: (gvec1, 3), 4: (gvec1, 0), 5: (gvec1, 6)}
    shifts = {1: (gvec2, 7), 2: (gvec2, 3), 3: (gvec1, 4), 4: (gvec1, 1), 5: (gvec1, 7)}
    shifts.update({6: (gvec3, 0), 7: (gvec1, 2), 8: (gvec2, 4), 9: (gvec2, 0), 10: (gvec2, 1)})
    shifts.update({11: (gvec2, 5), 12: (gvec1, 5)})
    for at, (ref, row) in gains.items():
        out[at : at + 1, :] = ref[row : row + 1, :]
    for at, (ref, row) in shifts.items():
        out[6 + at : 7 + at, :] = ref[row : row + 1, :]
    out[TAP_ROW : TAP_ROW + TAPS, :] = gtaps[:TAPS, :]
    log_decay, decay, root, maps_in, maps_out = state_terms(table_ref)
    both = gmap[...] * root
    out[MAP_IN:MAP_OUT, :] = both * maps_out
    out[MAP_OUT:TABLE, :] = both * maps_in
    turn = (1.0 - root * root) / root
    out[RATE:MAP_IN, :] = log_decay * (
        gdecay[...] * decay - gmap[...] * maps_in * maps_out * turn
    )


def store_cols(out, at, value):
    groups = value.shape[0] // PIECE
    out[:, at] = value.reshape((groups, PIECE, WIDTH))


def tail_kernel(mesh_size, *refs):
    fused = mesh_size is not None
    refs = list(refs)
    take = lambda count: [refs.pop(0) for _ in range(count)]
    x_ref, h_ref, gx1_ref, up_ref, up2_ref, down_ref, table_ref = take(7)
    hidden = 4 * WIDTH
    if fused:
        gvec1, gvec2, gtaps, gmap, gdecay, gbias1 = take(6)
        sources = take(1)
        gx_ref, last_out = take(2)
        reduced = take(4)
    else:
        gx_ref, gvec_out, gbias_out, up_out, down_out = take(5)
    turn_scr, grad_scr, gh_scr, vec_acc, bias_scr = take(5)
    step = pl.program_id(0)
    frames, channels = x_ref.shape
    chunks = hidden // WIDTH
    tiles = frames // TILE
    first_b, first_c = 1 + chunks, 1 + 2 * chunks
    schedule = {}
    if fused:
        n_dp, n_fs = mesh_size
        down_src, left_src, right_src, small_scr, gvec3 = take(5)
        dp, fs = lax.axis_index("dp"), lax.axis_index("fsdp")
        place = Place(dp, fs, n_dp, n_fs)
        scratch = take(4 * (2 + place.count))
        sems = take(3)
        swap = take(4)
        down_out = flat_groups(down_src)
        halves = (flat_groups(left_src), flat_groups(right_src))

        def emit(chunk, total):
            reduced[chunk][...] = total

        plans, sends = block_scatter(
            place, sources + [down_src, left_src, right_src], emit, scratch, *sems
        )
        begins = [
            (0, 2, 4, 7, first_c),
            (first_b, first_b + 1, first_b + 3, first_c + 1, first_c + tiles),
            (first_b + 2, first_c, first_c + 1, first_c + 2, first_c + tiles),
            (first_c, first_c + 1, first_c + 2, first_c + tiles, first_c + tiles),
        ]
        for chunk, steps in enumerate(begins):
            for stage, at in enumerate(steps):
                schedule.setdefault(at, []).append((stage, chunk))
    last_step = first_c + tiles - 1

    def progress(at):
        for stage, chunk in sorted(schedule.get(at, [])):
            plans[chunk][stage]()

    @pl.when(step == 0)
    def _():
        if fused:
            greet(dp, fs, n_dp, n_fs)
        progress(0)
        vec_acc[...] = jnp.zeros_like(vec_acc)

        def first(rows):
            e, _ = norm_parts(x_ref[rows, :].astype(F32))
            low = (e * table_ref[0:1, :] + table_ref[6:7, :]).astype(BF16)
            turn_scr[:, rows] = low.T
            grad = (0.5 * gx1_ref[rows, :]).astype(BF16)
            grad_scr[rows, :] = grad
            vec_acc[0] += fold8(grad.astype(F32))

        by_rows(first, frames)

    if fused:
        for at in range(1, last_step + 1):
            if at in schedule and at != first_c:

                @pl.when(step == at)
                def _(at=at):
                    progress(at)

    @pl.when((step >= 1) & (step < first_b))
    def _():
        h = h_ref[...].astype(F32)
        active = (h * sigmoid(h)).astype(BF16)
        value = dot_tn(active, grad_scr[...]).astype(BF16)
        groups = WIDTH // (4 * PIECE)
        down_out[pl.ds((step - 1) * groups, groups)] = value.reshape((groups, 4, PIECE, WIDTH))

    def second_half(c, store):
        cols = columns(c, WIDTH)
        h = h_ref[...].astype(F32)
        sig = sigmoid(h)
        gate = dot_nt(grad_scr[...], rows_of(down_ref, 0, c))
        grad_h = (gate * (sig * (1.0 + h * (1.0 - sig)))).astype(BF16)
        gh_scr[:, cols] = grad_h
        sums = jnp.sum(fold8(grad_h.astype(F32)), axis=0, keepdims=True)
        bias_scr[pl.ds(2 * c, 1), :] = sums[:, :CHUNK]
        bias_scr[pl.ds(2 * c + 1, 1), :] = sums[:, CHUNK:]
        store(dot_nn(turn_scr[...], grad_h).astype(BF16))

    if fused:
        for half in range(2):
            begin = first_b + half * (chunks // 2)

            @pl.when((step >= begin) & (step < begin + chunks // 2))
            def _(half=half, begin=begin):
                def store(value):
                    store_cols(halves[half], step - begin, value)

                second_half(step - first_b, store)

    else:

        @pl.when((step >= first_b) & (step < first_c))
        def _():
            def store(value):
                store_cols(up_out, step - first_b, value)

            second_half(step - first_b, store)

    if fused:

        @pl.when(step == first_c)
        def _():
            gvec3[0:1, :] = jnp.sum(vec_acc[0], axis=0, keepdims=True)
            small_gradients(small_scr, gvec1, gvec2, gvec3, gtaps, gmap, gdecay, table_ref)
            narrow = small_scr[...].T.astype(BF16)
            devices = n_dp * n_fs
            small_out = halves[1]
            small_out[:, 2, :, :CHUNK] = narrow.reshape((devices, PIECE, CHUNK))
            for c in range(8):
                bias_scr[8 + c : 9 + c, :] = gbias1[0:1, c * CHUNK : c * CHUNK + CHUNK]
            bias = bias_scr[...].astype(BF16)
            small_out[:, 2, :, CHUNK:] = jnp.broadcast_to(bias[None], (devices, PIECE, CHUNK))
            progress(first_c)

    @pl.when(step >= first_c)
    def _():
        tile = step - first_c
        whole_tile = pl.ds(pl.multiple_of(tile * TILE, TILE), TILE)
        total = dot_nt(gh_scr[whole_tile, :WIDTH], square_of(up_ref, 1))
        later = [square_of(up_ref, 2), square_of(up2_ref, 0), square_of(up2_ref, 1)]
        for k in range(1, hidden // WIDTH):
            cols = slice(k * WIDTH, k * WIDTH + WIDTH)
            total = total + dot_nt(gh_scr[whole_tile, cols], later[k - 1])
        gx_ref[...] = total

        def second(rows):
            here = pl.ds(pl.multiple_of(tile * TILE + rows.start, ROWS), ROWS)
            e, inv = norm_parts(x_ref[here, :].astype(F32))
            grad = gx_ref[rows, :]
            vec_acc[1] += fold8(grad * e)
            vec_acc[2] += fold8(grad)
            gx_ref[rows, :] = gx1_ref[here, :] + norm_back(grad, e, inv, table_ref[0:1, :])

        by_rows(second)

    @pl.when(step == last_step)
    def _():
        if fused:
            last_out[...] = jnp.zeros_like(last_out)
            for k in range(2):
                last_out[k : k + 1, :] = jnp.sum(vec_acc[1 + k], axis=0, keepdims=True)
            ends = sorted(schedule.get(last_step + 1, []))

            def between():
                for stage, chunk in ends:
                    plans[chunk][stage]()

            last_out[...] = sum_over(last_out[...], dp, fs, n_dp, n_fs, *swap, between=between)
            for wait in sends:
                wait()
        else:
            gvec_out[...] = jnp.zeros_like(gvec_out)
            for k in range(3):
                gvec_out[k : k + 1, :] = jnp.sum(vec_acc[k], axis=0, keepdims=True)
            gbias_out[...] = bias_scr[...]


def tail(mesh_size, x, h, gx1, up, up2, down, table, others=(), grads=(), collective_id=None):
    fused = mesh_size is not None
    frames, channels = x.shape
    hidden = h.shape[1]
    tiles, chunks = frames // TILE, hidden // WIDTH
    first_b, first_c = 1 + chunks, 1 + 2 * chunks
    place = lambda i: jnp.where(
        i < first_b, jnp.maximum(i - 1, 0), jnp.minimum(i - first_b, chunks - 1)
    )
    shapes = [jax.ShapeDtypeStruct((frames, channels), F32)]
    scratch = [
        pltpu.VMEM((channels, frames), BF16),
        pltpu.VMEM((frames, channels), BF16),
        pltpu.VMEM((frames, hidden), BF16),
        pltpu.VMEM((8, 8, channels), F32),
        pltpu.VMEM((16, CHUNK), F32),
    ]
    if fused:
        own = [4, 2, 3]
        counts = [g.shape[-3] for g in grads] + own
        shapes.append(jax.ShapeDtypeStruct((8, channels), F32))
        shapes += [jax.ShapeDtypeStruct((k, PIECE, WIDTH), F32) for k in counts]
        layout = block_layout(*mesh_size)
        scratch += [pltpu.VMEM(layout + (k, PIECE, WIDTH), BF16) for k in own]
        scratch += [pltpu.VMEM((256, channels), F32), pltpu.VMEM((8, channels), F32)]
        scratch += block_scratch(*mesh_size, counts, (PIECE, WIDTH))
        scratch += block_sems(*mesh_size, len(counts))
        scratch += swap_scratch(*mesh_size, channels)
    else:
        shapes += [
            jax.ShapeDtypeStruct((8, channels), F32),
            jax.ShapeDtypeStruct((16, CHUNK), F32),
            jax.ShapeDtypeStruct((channels // PIECE, 4, PIECE, WIDTH), BF16),
            jax.ShapeDtypeStruct((channels // PIECE, 4, PIECE, WIDTH), BF16),
        ]
    return pl.pallas_call(
        partial(tail_kernel, mesh_size),
        grid=(first_c + tiles,),
        in_specs=[whole(x.shape), pl.BlockSpec((frames, WIDTH), lambda i: (0, place(i)))]
        + [whole(a.shape) for a in (gx1, up, up2, down, table) + tuple(others)]
        + [pl.BlockSpec(memory_space=pltpu.HBM)] * len(grads),
        out_specs=[
            pl.BlockSpec((TILE, channels), lambda i: (jnp.maximum(i - first_c, 0), 0))
        ]
        + [whole(s.shape) for s in shapes[1:]],
        out_shape=shapes,
        scratch_shapes=scratch,
        compiler_params=params(collective_id),
        name="tail",
    )(x, h, gx1, up, up2, down, table, *others, *grads)


def unpack_kernel(
    place_ref,
    second_ref,
    middle_ref,
    mixin_ref,
    down_ref,
    left_ref,
    right_ref,
    last_ref,
    up_out,
    down_out,
    bias_out,
    mixin_out,
    mixout_out,
    convin_out,
    convout_out,
    convbias_out,
    rate_out,
    map_out,
    taps_out,
    gains_out,
    shifts_out,
):
    mine = place_ref[0]
    for k in range(4):
        cols = slice(k * WIDTH, k * WIDTH + WIDTH)
        rows = slice(k * PIECE, k * PIECE + PIECE)
        up_out[0, :, cols] = (left_ref if k < 2 else right_ref)[k % 2]
        up_out[1, :, cols] = second_ref[1 + k]
        down_out[0, rows, :] = down_ref[k]
        down_out[1, rows, :] = second_ref[5 + k]
    convout_out[...] = second_ref[0]
    mixout_out[...] = middle_ref[0]
    for k in range(2):
        cols = slice(k * WIDTH, k * WIDTH + WIDTH)
        mixin_out[:, cols] = mixin_ref[k]
        convin_out[:, cols] = middle_ref[1 + k]
    count = bias_out.shape[1]
    row = (mine * count) // CHUNK
    inner = mine * count - row * CHUNK
    for layer in range(2):
        line = right_ref[2, pl.ds(8 * layer + row, 1), CHUNK:]
        line = pltpu.roll(jnp.broadcast_to(line, (8, CHUNK)), CHUNK - inner, 1)
        bias_out[layer : layer + 1, :] = line[0:1, :count]
    channels = last_ref.shape[1]
    first = pltpu.roll(last_ref[...], channels - mine * PIECE, 1)[:, :PIECE]
    small = right_ref[2, :, :CHUNK]
    turned = small.T
    gains_out[...] = turned[0:6, :]
    gains_out[0:1, :] = first[0:1, :]
    shifts_out[...] = turned[6:18, :]
    shifts_out[0:1, :] = first[1:2, :]
    convbias_out[...] = turned[18:19, :]
    taps_out[...] = turned[TAP_ROW : TAP_ROW + TAPS, :]
    rate_out[...] = small[:, RATE:MAP_IN]
    map_out[0] = small[:, MAP_IN:MAP_OUT]
    map_out[1] = small[:, MAP_OUT:TABLE]


def unpack(mine, arrays, hidden):
    channels = arrays[-1].shape[1]
    devices = channels // PIECE
    f32 = lambda *shape: jax.ShapeDtypeStruct(shape, F32)
    vmem = pl.BlockSpec(memory_space=pltpu.VMEM)
    return pl.pallas_call(
        unpack_kernel,
        in_specs=[SMEM_SPEC] + [vmem] * len(arrays),
        out_specs=[vmem] * 13,
        out_shape=[
            f32(2, PIECE, hidden),
            f32(2, hidden // devices, channels),
            f32(2, hidden // devices),
            f32(PIECE, 2 * WIDTH),
            f32(PIECE, WIDTH),
            f32(PIECE, 2 * WIDTH),
            f32(PIECE, WIDTH),
            f32(1, PIECE),
            f32(PIECE, STATES),
            f32(2, PIECE, STATES),
            f32(TAPS, PIECE),
            f32(6, PIECE),
            f32(12, PIECE),
        ],
        name="unpack",
    )(mine, *arrays)


def pack_table(gains, shifts, conv_bias, taps, rate, maps):
    channels = gains.shape[1]
    blank = lambda rows: jnp.zeros((rows, channels), gains.dtype)
    parts = [gains, shifts, conv_bias[None], blank(TAP_ROW - 19), taps, blank(RATE - TAP_ROW - TAPS)]
    parts += [rate, maps[0], maps[1], blank(256 - TABLE)]
    return jnp.concatenate(parts, axis=0).T


def pack_bias(bias, place):
    layers, count = bias.shape
    hidden = 16 * CHUNK // layers
    wide = lax.dynamic_update_slice(
        jnp.zeros((layers, hidden), bias.dtype), bias, (0, place * count)
    )
    return wide.reshape((16, CHUNK))


def unpack_table(table):
    return (
        table[0:6],
        table[6:18],
        table[18],
        table[TAP_ROW : TAP_ROW + TAPS],
        table[RATE:MAP_IN],
        jnp.stack([table[MAP_IN:MAP_OUT], table[MAP_OUT:TABLE]]),
    )


def on_device(
    n_dp,
    n_fs,
    frames,
    seq_lengths,
    seq_offsets,
    seq_counts,
    ffn_up,
    ffn_down,
    ffn_bias_up,
    mix_in,
    mix_out,
    conv_in,
    conv_out,
    conv_out_bias,
    ssm_rate,
    ssm_map,
    conv_kernel,
    gains,
    shifts,
    cotangent,
):
    devices = n_dp * n_fs
    mine = lax.axis_index("dp") * n_fs + lax.axis_index("fsdp")
    frames_dev, channels = frames.shape
    hidden = ffn_up.shape[2]
    if channels // devices == PIECE:
        size = (n_dp, n_fs)
        small = [
            ffn_bias_up,
            gains,
            shifts,
            conv_out_bias[None],
            conv_kernel,
            ssm_rate.T,
            ssm_map.transpose((0, 2, 1)),
        ]
        weights = [ffn_up, ffn_down, mix_in, mix_out, conv_in, conv_out]
        made = front(size, seq_offsets, seq_counts, frames, small, weights, hidden, 1)
        h0, x1, v, y, gated, x2, p, u, w, stat, table, bias, *mixing = made[:17]
        groups = lambda g: g.reshape((devices,) + g.shape[-3:])
        places = lambda g: g.reshape(block_layout(n_dp, n_fs) + g.shape[1:])
        first, extra, second, third, mixed, fourth = [groups(g) for g in made[17:]]
        result, gx3, gnb, grads, gbias1, gvec1, stat = middle(
            size, x2, w, cotangent, fourth, bias, table, stat, hidden, 2
        )
        gx1, grads2, gvec2, gtaps, gmap, gdecay, reduced, reduced2 = back(
            size,
            seq_offsets,
            seq_counts,
            [w, gnb, p, x2, gx3, gated, y, v, x1],
            [u] + mixing + [third, mixed, table, stat],
            (places(grads),),
            3,
        )
        others = (gvec1, gvec2, gtaps, gmap, gdecay, gbias1)
        gx, last, *late = tail(
            size, frames, h0, gx1, first, extra, second, table, others, (places(grads2),), 4
        )
        made = unpack(mine.reshape((1,)), [reduced, reduced2] + late + [last], hidden)
        made = list(made)
        made[7] = made[7].reshape((-1,))
        made[8] = made[8].T
        made[9] = made[9].transpose((0, 2, 1))
        return (result, gx) + tuple(made)

    small = pack_table(gains, shifts, conv_out_bias, conv_kernel, ssm_rate, ssm_map)
    got = gather_all(
        n_dp,
        n_fs,
        [
            small[None],
            pack_bias(ffn_bias_up, mine)[None],
            ffn_up,
            ffn_down,
            mix_in[None],
            mix_out[None],
            conv_in[None],
            conv_out[None],
        ],
        1,
    )
    matrix = lambda g: g.reshape((-1, g.shape[-1]))
    table, _, up0, up1, down0, down1, mixin, mixout, convin, convout = [matrix(g) for g in got]
    table = table.astype(F32).T[:TABLE]
    bias = jnp.sum(got[1].astype(F32), axis=0)
    group_count = channels // PIECE
    cut = lambda g: g.reshape((group_count, PIECE, -1, WIDTH)).transpose((0, 2, 1, 3))
    tall = lambda g: g.reshape((group_count, -1, PIECE, WIDTH))
    join = lambda g: g.transpose((0, 2, 1, 3)).reshape((channels, -1))
    blank = jnp.pad(matrix(got[0]), ((0, 0), (0, WIDTH - 256))).reshape((group_count, 1, PIECE, WIDTH))
    extra = cut(up0)
    first, extra = jnp.concatenate([blank, extra[:, :2]], axis=1), extra[:, 2:]
    third = cut(mixin)
    mixed = jnp.concatenate([cut(mixout), cut(convin)], axis=1)
    fourth = jnp.concatenate([cut(convout), cut(up1), tall(down1)], axis=1)
    made = front(
        None, seq_offsets, seq_counts, frames, [table, bias], [first, extra, tall(down0), third, mixed], hidden
    )
    h0, x1, v, y, gated, x2, p, u, w, stat, table, bias, *mixing = made
    pool = exchange(n_dp, n_fs, stat, frames_dev, 2, pool_kernel)
    scale = lax.rsqrt(pool[1:2] / (frames_dev * devices) + EPSILON)
    stat = jnp.concatenate([pool[0:1], scale, jnp.zeros((6, channels), F32)])
    result, gx3, gnb, grads, gbias1, gvec1, stat = middle(
        None, x2, w, cotangent, fourth, bias, table, stat, hidden
    )
    sums = exchange(n_dp, n_fs, gvec1, 1, 4, total_kernel)[6:8]
    sums = sums * (table[5:6] / (frames_dev * devices))
    stat = jnp.concatenate([stat[0:2], sums[1:2], sums[0:1], stat[4:8]])
    gx1, grads2, gvec2, gtaps, gmap, gdecay, grads3 = back(
        None,
        seq_offsets,
        seq_counts,
        [w, gnb, p, x2, gx3, gated, y, v, x1],
        [u] + mixing + [third, mixed, table, stat],
    )
    gx, gvec3, gbias0, gup0, gdown0 = tail(None, frames, h0, gx1, first, extra, tall(down0), table)

    def weights_of(log_rate, maps):
        log_decay = -jnp.exp(log_rate)
        root = jnp.sqrt(-jnp.expm1(2.0 * log_decay))
        return jnp.exp(log_decay), maps[0] * root * maps[1]

    rate, maps = unpack_table(table)[4:]
    rate_grad, map_grad = jax.vjp(weights_of, rate, maps)[1]((gdecay, gmap))
    gain_grad = jnp.stack([gvec3[1], gvec2[6], gvec2[2], gvec1[3], gvec1[0], gvec1[6]])
    rows = [gvec3[2], gvec2[7], gvec2[3], gvec1[4], gvec1[1], gvec1[7], gvec3[0], gvec1[2]]
    rows += [gvec2[4], gvec2[0], gvec2[1], gvec2[5]]
    small_grad = pack_table(
        gain_grad, jnp.stack(rows), gvec1[5], gtaps[:TAPS], rate_grad, map_grad
    )
    bias_grad = jnp.concatenate([gbias0[:8], gbias1[0].reshape((8, CHUNK))])
    wide = lambda g: g.reshape((devices, g.shape[0] // devices, g.shape[1]))
    reduced = scatter_all(
        n_dp,
        n_fs,
        [
            wide(join(grads[:, 1:5])),
            wide(matrix(grads[:, 5:9])),
            wide(join(grads[:, 0:1])),
            wide(join(grads3[:, 1:3])),
            wide(join(grads3[:, 0:1])),
            wide(join(grads2[:, 0:2])),
            wide(join(gup0)),
            wide(matrix(gdown0)),
            wide(small_grad.astype(BF16)),
            jnp.broadcast_to(bias_grad.astype(BF16), (devices, PIECE, CHUNK)),
        ],
        5,
    )
    gains_grad, shifts_grad, conv_bias_grad, taps_grad, rate_grad, map_grad = unpack_table(
        reduced[8].T
    )
    bias_grad = reduced[9].reshape((2, -1))
    count = bias_grad.shape[1] // devices
    bias_grad = lax.dynamic_slice(bias_grad, (0, mine * count), (2, count))
    return (
        result,
        gx,
        jnp.stack([reduced[6], reduced[0]]),
        jnp.stack([reduced[7], reduced[1]]),
        bias_grad,
        reduced[5],
        reduced[4],
        reduced[3],
        reduced[2],
        conv_bias_grad,
        rate_grad,
        map_grad,
        taps_grad,
        gains_grad,
        shifts_grad,
    )


def solution(mesh):
    both = ("dp", "fsdp")
    row, row1 = P(both, None), P(both)
    col, col3, mid = P(None, both), P(None, None, both), P(None, both, None)
    in_specs = (
        row,
        row,
        row,
        row1,
        mid,
        mid,
        col,
        row,
        row,
        row,
        row,
        row1,
        col,
        col3,
        col,
        col,
        col,
        row,
    )
    out_specs = (row, row, mid, mid, col, row, row, row, row, row1, col, col3, col, col, col)
    return jax.shard_map(
        partial(on_device, mesh.shape["dp"], mesh.shape["fsdp"]),
        mesh=mesh,
        in_specs=in_specs,
        out_specs=out_specs,
        check_vma=False,
    )
```

```python
import itertools
from functools import partial

import jax
import jax.numpy as jnp
from jax import lax
from jax.experimental import pallas as pl
from jax.experimental.pallas import tpu as pltpu
from jax.sharding import PartitionSpec as P

MESH = pl.DeviceIdType.MESH
BF16 = jnp.bfloat16
F32 = jnp.float32


def flip(index, bit):
    return index + bit * (1 - 2 * lax.rem(lax.div(index, bit), 2))


def flip_all(index, bits):
    for bit in bits:
        index = flip(index, bit)
    return index


def combos(bits):
    found = [()]
    for bit in bits:
        found = found + [entry + (bit,) for entry in found]
    return found


def plan_bits(n_dp):
    bits, bit = [], 2
    while bit < n_dp:
        bits.append(bit)
        bit *= 2
    return tuple(bits)


def greet(dp, fs, n_dp, n_fs):
    barrier = pltpu.get_barrier_semaphore()
    for step in range(1, n_dp):
        pl.semaphore_signal(
            barrier, inc=1, device_id=(lax.rem(dp + step, n_dp), fs), device_id_type=MESH
        )
    for step in range(1, n_fs):
        pl.semaphore_signal(
            barrier, inc=1, device_id=(dp, lax.rem(fs + step, n_fs)), device_id_type=MESH
        )
    pl.semaphore_wait(barrier, n_dp + n_fs - 2)


def gather_plan(dp, fs, n_dp, n_fs, sources, outs, send_sem, recv_sem, local_sem):
    bits = plan_bits(n_dp)
    orders = (bits, bits[::-1])
    half = n_fs // 2
    sends = []

    def stages(chunk):
        src, out = sources[chunk], outs[chunk]
        slots = itertools.count()

        def zone(where, part):
            if part is None:
                return out.at[pl.ds(where * n_fs, n_fs)]
            return out.at[pl.ds(where * n_fs + part * half, half)]

        def remote(slot, view_from, view_to, device):
            return pltpu.make_async_remote_copy(
                src_ref=view_from,
                dst_ref=view_to,
                send_sem=send_sem.at[chunk, slot],
                recv_sem=recv_sem.at[chunk, slot],
                device_id=device,
                device_id_type=MESH,
            )

        def launch(make):
            make().start()
            sends.append(lambda: make().wait_send())

        z_slots = [next(slots) for _ in range(1, n_fs)]

        def own_copy():
            return pltpu.make_async_copy(src, out.at[dp * n_fs + fs], local_sem.at[chunk])

        def start():
            own_copy().start()
            for step in range(1, n_fs):
                launch(
                    lambda step=step: remote(
                        z_slots[step - 1],
                        src,
                        out.at[dp * n_fs + fs],
                        (dp, lax.rem(fs + step, n_fs)),
                    )
                )

        def wait_z():
            own_copy().wait()
            for step in range(1, n_fs):
                origin = dp * n_fs + lax.rem(fs + n_fs - step, n_fs)
                remote(z_slots[step - 1], src, out.at[origin], (dp, fs)).wait_recv()

        steps, before = [start], wait_z
        for depth in range(len(bits)):
            plan = []
            for part, order in enumerate(orders):
                for entry in combos(order[:depth]):
                    plan.append((next(slots), part, order[depth], entry))

            def view(slot, part, bit, entry, arrived):
                where = flip_all(flip(dp, bit) if arrived else dp, entry)
                return remote(slot, zone(where, part), zone(where, part), (flip(dp, bit), fs))

            def go(plan=plan, before=before, view=view):
                before()
                for item in plan:
                    launch(lambda item=item: view(*item, False))

            def arrive(plan=plan, view=view):
                for item in plan:
                    view(*item, True).wait_recv()

            steps.append(go)
            before = arrive
        last = [(next(slots), entry) for entry in combos(bits)]

        def across(slot, entry, arrived):
            where = flip_all(flip(dp, 1) if arrived else dp, entry)
            return remote(slot, zone(where, None), zone(where, None), (flip(dp, 1), fs))

        def cross(before=before):
            before()
            for item in last:
                launch(lambda item=item: across(*item, False))

        def finish():
            for item in last:
                across(*item, True).wait_recv()

        return steps + [cross, finish]

    return [stages(chunk) for chunk in range(len(outs))], sends


def waves(plans):
    depth = len(plans[0])
    out = []
    for wave in range(len(plans) + depth - 1):
        out.append(
            [plans[c][wave - c] for c in range(len(plans)) if 0 <= wave - c < depth]
        )
    return out


def gather_kernel(n_dp, n_fs, layers, *refs):
    n_in = len(layers)
    n_out = sum(layers)
    ins, outs = refs[:n_in], refs[n_in : n_in + n_out]
    send_sem, recv_sem, local_sem = refs[n_in + n_out :]
    sources = []
    for ref, count in zip(ins, layers):
        sources += [ref.at[layer] for layer in range(count)]
    dp, fs = lax.axis_index("dp"), lax.axis_index("fsdp")
    greet(dp, fs, n_dp, n_fs)
    plans, sends = gather_plan(dp, fs, n_dp, n_fs, sources, outs, send_sem, recv_sem, local_sem)
    for wave in waves(plans):
        for stage in wave:
            stage()
    for wait in sends:
        wait()


def slot_count(n_dp, n_fs):
    nb = len(plan_bits(n_dp))
    return n_fs - 1 + 2 * (2**nb - 1) + 2**nb


def gather_all(n_dp, n_fs, arrays, collective_id):
    layers = tuple(a.shape[0] for a in arrays)
    outs = []
    for a in arrays:
        outs += [jax.ShapeDtypeStruct((n_dp * n_fs,) + a.shape[1:], a.dtype)] * a.shape[0]
    count = slot_count(n_dp, n_fs)
    return pl.pallas_call(
        partial(gather_kernel, n_dp, n_fs, layers),
        out_shape=outs,
        in_specs=[pl.BlockSpec(memory_space=pltpu.HBM)] * len(arrays),
        out_specs=[pl.BlockSpec(memory_space=pltpu.HBM)] * len(outs),
        scratch_shapes=[
            pltpu.SemaphoreType.DMA((len(outs), count)),
            pltpu.SemaphoreType.DMA((len(outs), count)),
            pltpu.SemaphoreType.DMA((len(outs),)),
        ],
        compiler_params=pltpu.CompilerParams(collective_id=collective_id, has_side_effects=True),
        name="gather_parameters",
    )(*arrays)


def scatter_plan(dp, fs, n_dp, n_fs, ins, emit, scratch, send_sem, recv_sem, local_sem, first=0):
    bits = plan_bits(n_dp)
    orders = (bits[::-1], bits)
    half = n_fs // 2
    index = {entry: at for at, entry in enumerate(combos(bits))}
    sends = []

    def add_into(kept, other):
        def body(at, _):
            kept[at] = (kept[at].astype(F32) + other[at].astype(F32)).astype(BF16)
            return 0

        lax.fori_loop(0, kept.shape[0], body, 0)

    def stages(chunk):
        src = ins[chunk]
        cross_in, own, later, last = scratch[4 * chunk : 4 * chunk + 4]
        slots = itertools.count()

        def remote(slot, view_from, view_to, device):
            return pltpu.make_async_remote_copy(
                src_ref=view_from,
                dst_ref=view_to,
                send_sem=send_sem.at[first + chunk, slot],
                recv_sem=recv_sem.at[first + chunk, slot],
                device_id=device,
                device_id_type=MESH,
            )

        def launch(make):
            make().start()
            sends.append(lambda: make().wait_send())

        def zone(entry, crossed):
            return src.at[pl.ds(flip_all(flip(dp, 1) if crossed else dp, entry) * n_fs, n_fs)]

        pieces = [(next(slots), entry, index[entry]) for entry in combos(bits)]

        def load(entry, at):
            return pltpu.make_async_copy(
                zone(entry, False), own.at[at], local_sem.at[first + chunk, at]
            )

        def across(slot, entry, at):
            return remote(slot, zone(entry, True), cross_in.at[at], (flip(dp, 1), fs))

        def start():
            for item in pieces:
                launch(lambda item=item: across(*item))
            for _, entry, at in pieces:
                load(entry, at).start()

        def fold_cross():
            for slot, entry, at in pieces:
                load(entry, at).wait()
                across(slot, entry, at).wait_recv()
                add_into(own.at[at], cross_in.at[at])

        steps, before = [start], fold_cross
        used = 0
        for depth in range(len(bits)):
            plan = []
            for part, order in enumerate(orders):
                bit, gone = order[depth], order[:depth]
                for entry in combos(bits):
                    if not (set(entry) & set(gone)) and bit not in entry:
                        away = tuple(sorted(entry + (bit,)))
                        plan.append((next(slots), part, bit, index[away], index[entry], used))
                        used += 1

            def move(slot, part, bit, away, kept, place):
                return remote(
                    slot,
                    own.at[away, pl.ds(part * half, half)],
                    later.at[place],
                    (flip(dp, bit), fs),
                )

            def go(plan=plan, before=before, move=move):
                before()
                for item in plan:
                    launch(lambda item=item: move(*item))

            def fold(plan=plan, move=move):
                for item in plan:
                    move(*item).wait_recv()
                    _, part, _, _, kept, place = item
                    add_into(own.at[kept, pl.ds(part * half, half)], later.at[place])

            steps.append(go)
            before = fold
        z_slots = [next(slots) for _ in range(1, n_fs)]

        def along(step):
            to = lax.rem(fs + step, n_fs)
            return remote(z_slots[step - 1], own.at[0, to], last.at[step - 1], (dp, to))

        def spread(before=before):
            before()
            for step in range(1, n_fs):
                launch(lambda step=step: along(step))

        def finish():
            total = own[0, fs].astype(F32)
            for step in range(1, n_fs):
                along(step).wait_recv()
                total = total + last[step - 1].astype(F32)
            emit(chunk, total)

        return steps + [spread, finish]

    return [stages(chunk) for chunk in range(len(ins))], sends


def scatter_scratch(n_dp, n_fs, tails):
    pieces = 2 ** len(plan_bits(n_dp))
    scratch = []
    for tail in tails:
        scratch += [
            pltpu.VMEM((pieces, n_fs) + tail, BF16),
            pltpu.VMEM((pieces, n_fs) + tail, BF16),
            pltpu.VMEM((2 * (pieces - 1), n_fs // 2) + tail, BF16),
            pltpu.VMEM((n_fs - 1,) + tail, BF16),
        ]
    return scratch


def scatter_sems(n_dp, n_fs, chunks):
    count = slot_count(n_dp, n_fs)
    return [
        pltpu.SemaphoreType.DMA((chunks, count)),
        pltpu.SemaphoreType.DMA((chunks, count)),
        pltpu.SemaphoreType.DMA((chunks, 2 ** len(plan_bits(n_dp)))),
    ]


def scatter_kernel(n_dp, n_fs, n_chunks, *refs):
    ins, outs = refs[:n_chunks], refs[n_chunks : 2 * n_chunks]
    scratch = refs[2 * n_chunks : 6 * n_chunks]
    dp, fs = lax.axis_index("dp"), lax.axis_index("fsdp")
    greet(dp, fs, n_dp, n_fs)

    def emit(chunk, total):
        outs[chunk][...] = total

    plans, sends = scatter_plan(dp, fs, n_dp, n_fs, ins, emit, scratch, *refs[6 * n_chunks :])
    for wave in waves(plans):
        for stage in wave:
            stage()
    for wait in sends:
        wait()


def scatter_all(n_dp, n_fs, arrays, collective_id):
    n = len(arrays)
    return pl.pallas_call(
        partial(scatter_kernel, n_dp, n_fs, n),
        out_shape=[jax.ShapeDtypeStruct(a.shape[1:], F32) for a in arrays],
        in_specs=[pl.BlockSpec(memory_space=pltpu.HBM)] * n,
        out_specs=[pl.BlockSpec(memory_space=pltpu.VMEM)] * n,
        scratch_shapes=scatter_scratch(n_dp, n_fs, [a.shape[1:] for a in arrays])
        + scatter_sems(n_dp, n_fs, n),
        compiler_params=pltpu.CompilerParams(
            collective_id=collective_id, has_side_effects=True, vmem_limit_bytes=48 << 20
        ),
        name="scatter_gradients",
    )(*arrays)


def swap_copy(axis, place, count, buffer, send_sem, recv_sem, step):
    return pltpu.make_async_remote_copy(
        src_ref=buffer.at[0],
        dst_ref=buffer.at[step],
        send_sem=send_sem.at[step],
        recv_sem=recv_sem.at[step],
        device_id={axis: lax.rem(place + step, count)},
        device_id_type=MESH,
    )


def swap_start(axis, place, count, *rest):
    for step in range(1, count):
        swap_copy(axis, place, count, *rest, step).start()


def swap_wait(axis, place, count, *rest):
    for step in range(1, count):
        swap_copy(axis, place, count, *rest, step).wait_recv()
    for step in range(1, count):
        swap_copy(axis, place, count, *rest, step).wait_send()


def swap_rows(*args):
    swap_start(*args)
    swap_wait(*args)


def sum_over(x, dp, fs, n_dp, n_fs, octet, line, send_sem, recv_sem, between=None):
    first = ("dp", dp, n_dp, octet, send_sem.at[0], recv_sem.at[0])
    octet[0] = x
    swap_start(*first)
    if between is not None:
        between()
    swap_wait(*first)
    total = octet[0]
    for step in range(1, n_dp):
        total = total + octet[step]
    line[0] = total
    swap_rows("fsdp", fs, n_fs, line, send_sem.at[1], recv_sem.at[1])
    total = line[0]
    for step in range(1, n_fs):
        total = total + line[step]
    return total


def pooled(buffer, count, weight):
    means = [buffer[k, 0:1, :] for k in range(count)]
    center = sum(means[1:], means[0]) * (1.0 / count)
    spread = buffer[0, 1:2, :]
    for k in range(1, count):
        spread = spread + buffer[k, 1:2, :]
    off = (means[0] - center) * (means[0] - center)
    for mean in means[1:]:
        off = off + (mean - center) * (mean - center)
    return center, spread + weight * off


def pool_over(center, spread, frames, dp, fs, n_dp, n_fs, octet, line, send_sem, recv_sem):
    octet[0] = jnp.zeros(octet.shape[1:], F32)
    line[0] = jnp.zeros(line.shape[1:], F32)
    octet[0, 0:1, :] = center
    octet[0, 1:2, :] = spread
    swap_rows("dp", dp, n_dp, octet, send_sem.at[0], recv_sem.at[0])
    center, spread = pooled(octet, n_dp, float(frames))
    line[0, 0:1, :] = center
    line[0, 1:2, :] = spread
    swap_rows("fsdp", fs, n_fs, line, send_sem.at[1], recv_sem.at[1])
    return pooled(line, n_fs, float(frames * n_dp))


def swap_scratch(n_dp, n_fs, channels):
    return [
        pltpu.VMEM((n_dp, 8, channels), F32),
        pltpu.VMEM((n_fs, 8, channels), F32),
        pltpu.SemaphoreType.DMA((2, max(n_dp, n_fs))),
        pltpu.SemaphoreType.DMA((2, max(n_dp, n_fs))),
    ]


def pool_kernel(n_dp, n_fs, frames, x_ref, out_ref, octet, line, send_sem, recv_sem):
    dp, fs = lax.axis_index("dp"), lax.axis_index("fsdp")
    greet(dp, fs, n_dp, n_fs)
    octet[0] = x_ref[...]
    center, spread = pool_over(
        x_ref[0:1, :], x_ref[1:2, :], frames, dp, fs, n_dp, n_fs, octet, line, send_sem, recv_sem
    )
    out_ref[...] = x_ref[...]
    out_ref[0:1, :] = center
    out_ref[1:2, :] = spread


def total_kernel(n_dp, n_fs, frames, x_ref, out_ref, octet, line, send_sem, recv_sem):
    dp, fs = lax.axis_index("dp"), lax.axis_index("fsdp")
    greet(dp, fs, n_dp, n_fs)
    out_ref[...] = sum_over(x_ref[...], dp, fs, n_dp, n_fs, octet, line, send_sem, recv_sem)


def exchange(n_dp, n_fs, x, frames, collective_id, kernel):
    return pl.pallas_call(
        partial(kernel, n_dp, n_fs, frames),
        out_shape=jax.ShapeDtypeStruct(x.shape, F32),
        in_specs=[pl.BlockSpec(memory_space=pltpu.VMEM)],
        out_specs=pl.BlockSpec(memory_space=pltpu.VMEM),
        scratch_shapes=swap_scratch(n_dp, n_fs, x.shape[1]),
        compiler_params=pltpu.CompilerParams(collective_id=collective_id, has_side_effects=True),
        name="exchange_rows",
    )(x)


class Place:
    def __init__(self, dp, fs, n_dp, n_fs):
        self.dp, self.fs, self.n_dp, self.n_fs = dp, fs, n_dp, n_fs
        self.count = (n_dp - 1).bit_length()
        self.bits = [lax.rem(lax.div(dp, 2**k), 2) for k in range(self.count)]
        self.half = n_fs // 2

    def peer(self, bit):
        return (flip(self.dp, 2**bit), self.fs)

    def view(self, ref, free=(), flipped=(), z=None, skip=()):
        index = []
        for bit in reversed(range(self.count)):
            if bit in skip:
                continue
            if bit in free:
                index.append(slice(None))
            else:
                index.append(1 - self.bits[bit] if bit in flipped else self.bits[bit])
        if z is not None:
            index.append(z)
        return ref.at[tuple(index)] if index else ref

    def part(self, which):
        return pl.ds(which * self.half, self.half)


def block_layout(n_dp, n_fs):
    return (2,) * ((n_dp - 1).bit_length()) + (n_fs,)


def hop_orders(place):
    bits = tuple(range(1, place.count))
    return (bits, bits[::-1])


def copy_count(n_dp, n_fs):
    return n_fs - 1 + 2 * ((n_dp - 1).bit_length() - 1) + 1


def block_gather(place, sources, outs, send_sem, recv_sem, local_sem):
    n_fs, fs = place.n_fs, place.fs
    sends = []

    def stages(chunk):
        src, out = sources[chunk], outs[chunk]

        def remote(slot, view_from, view_to, device):
            return pltpu.make_async_remote_copy(
                src_ref=view_from,
                dst_ref=view_to,
                send_sem=send_sem.at[chunk, slot],
                recv_sem=recv_sem.at[chunk, slot],
                device_id=device,
                device_id_type=MESH,
            )

        def launch(make):
            make().start()
            sends.append(lambda: make().wait_send())

        def own_copy():
            return pltpu.make_async_copy(src, place.view(out, z=fs), local_sem.at[chunk])

        def along(step):
            to = lax.rem(fs + step, n_fs)
            return remote(step - 1, src, place.view(out, z=fs), (place.dp, to))

        def start():
            own_copy().start()
            for step in range(1, n_fs):
                launch(lambda step=step: along(step))

        def wait_along():
            own_copy().wait()
            for step in range(1, n_fs):
                origin = lax.rem(fs + n_fs - step, n_fs)
                remote(
                    step - 1, src, place.view(out, z=origin), (place.dp, origin)
                ).wait_recv()

        steps, before = [start], wait_along
        slot = n_fs - 1
        orders = hop_orders(place)
        for depth in range(place.count - 1):
            plan = [(slot + part, part, order[depth], order[:depth]) for part, order in enumerate(orders)]
            slot += 2

            def hop(slot, part, bit, free, arrived):
                view = place.view(out, free, (bit,) if arrived else (), place.part(part))
                return remote(slot, view, view, place.peer(bit))

            def go(plan=plan, before=before, hop=hop):
                before()
                for item in plan:
                    launch(lambda item=item: hop(*item, False))

            def arrive(plan=plan, hop=hop):
                for item in plan:
                    hop(*item, True).wait_recv()

            steps.append(go)
            before = arrive

        def across(arrived, slot=slot):
            free = tuple(range(1, place.count))
            view = place.view(out, free, (0,) if arrived else ())
            return remote(slot, view, view, place.peer(0))

        def cross(before=before):
            before()
            launch(lambda: across(False))

        return steps + [cross, lambda: across(True).wait_recv()]

    return [stages(chunk) for chunk in range(len(outs))], sends


def block_scatter(place, sources, emit, scratch, send_sem, recv_sem, local_sem):
    n_fs, fs = place.n_fs, place.fs
    sends = []
    per = 3 + place.count - 1

    def add_into(kept, other):
        shape = kept.shape[:-3]
        for index in itertools.product(*[range(n) for n in shape]):
            kept[index] = (kept[index].astype(F32) + other[index].astype(F32)).astype(BF16)

    def stages(chunk):
        src = sources[chunk]
        own, cross_in, last, *later = scratch[per * chunk : per * chunk + per]

        def remote(slot, view_from, view_to, device):
            return pltpu.make_async_remote_copy(
                src_ref=view_from,
                dst_ref=view_to,
                send_sem=send_sem.at[chunk, slot],
                recv_sem=recv_sem.at[chunk, slot],
                device_id=device,
                device_id_type=MESH,
            )

        def launch(make):
            make().start()
            sends.append(lambda: make().wait_send())

        every = tuple(range(1, place.count))

        def load():
            return pltpu.make_async_copy(place.view(src, every), own, local_sem.at[chunk])

        def across():
            return remote(0, place.view(src, every, (0,)), cross_in, place.peer(0))

        def start():
            launch(across)
            load().start()

        def fold_cross():
            load().wait()
            across().wait_recv()
            add_into(own, cross_in)

        steps, before = [start], fold_cross
        slot = 1
        orders = [order[::-1] for order in hop_orders(place)]
        for depth in range(place.count - 1):
            plan = []
            for part, order in enumerate(orders):
                free = tuple(order[depth + 1 :])
                plan.append((slot + part, part, order[depth], free, later[depth]))
            slot += 2

            def hop(slot, part, bit, free, buffer):
                view = place.view(own, free, (bit,), place.part(part), skip=(0,))
                return remote(slot, view, buffer.at[part], place.peer(bit))

            def go(plan=plan, before=before, hop=hop):
                before()
                for item in plan:
                    launch(lambda item=item: hop(*item))

            def fold(plan=plan, hop=hop):
                for item in plan:
                    hop(*item).wait_recv()
                    _, part, _, free, buffer = item
                    kept = place.view(own, free, (), place.part(part), skip=(0,))
                    add_into(kept, buffer.at[part])

            steps.append(go)
            before = fold

        def along(step, slot=slot):
            to = lax.rem(fs + step, n_fs)
            view = place.view(own, z=to, skip=(0,))
            return remote(slot + step - 1, view, last.at[step - 1], (place.dp, to))

        def spread(before=before):
            before()
            for step in range(1, n_fs):
                launch(lambda step=step: along(step))

        def finish():
            total = place.view(own, z=fs, skip=(0,))[...].astype(F32)
            for step in range(1, n_fs):
                along(step).wait_recv()
                total = total + last[step - 1].astype(F32)
            emit(chunk, total)

        return steps + [spread, finish]

    return [stages(chunk) for chunk in range(len(sources))], sends


def block_scratch(n_dp, n_fs, blocks, tail):
    hops = (n_dp - 1).bit_length() - 1
    out = []
    for count in blocks:
        entry = (count,) + tail
        zone = (2,) * hops + (n_fs,) + entry
        out += [pltpu.VMEM(zone, BF16), pltpu.VMEM(zone, BF16), pltpu.VMEM((n_fs - 1,) + entry, BF16)]
        for depth in range(hops):
            out.append(pltpu.VMEM((2,) + (2,) * (hops - 1 - depth) + (n_fs // 2,) + entry, BF16))
    return out


def block_sems(n_dp, n_fs, chunks):
    count = copy_count(n_dp, n_fs)
    return [
        pltpu.SemaphoreType.DMA((chunks, count)),
        pltpu.SemaphoreType.DMA((chunks, count)),
        pltpu.SemaphoreType.DMA((chunks,)),
    ]


TILE = 512
STATES = 32
TAPS = 15
REACH = 8
EPSILON = 1e-05
CHUNK = 256
ROWS = 128
VMEM_LIMIT = 60 << 20
TAP_ROW = 24
RATE = 40
MAP_IN = 72
MAP_OUT = 104
TABLE = 136


def sigmoid(v):
    return 0.5 * jnp.tanh(0.5 * v) + 0.5


def dot_nn(a, b):
    return jnp.dot(a, b, preferred_element_type=F32)


def dot_nt(a, b):
    return lax.dot_general(a, b, (((1,), (1,)), ((), ())), preferred_element_type=F32)


def dot_tn(a, b):
    return lax.dot_general(a, b, (((0,), (0,)), ((), ())), preferred_element_type=F32)


def norm_parts(v):
    centered = v - jnp.mean(v, axis=-1, keepdims=True)
    inv = lax.rsqrt(jnp.mean(centered * centered, axis=-1, keepdims=True) + EPSILON)
    return centered * inv, inv


def norm_back(grad, e, inv, gain):
    d = grad * gain
    return (
        d - jnp.mean(d, axis=-1, keepdims=True) - e * jnp.mean(d * e, axis=-1, keepdims=True)
    ) * inv


def fold8(v):
    return jnp.sum(v.reshape((v.shape[0] // 8, 8, v.shape[1])), axis=0)


def by_rows(body, rows=TILE, step=ROWS):
    def run(at, _):
        body(pl.ds(pl.multiple_of(at * step, step), step))
        return 0

    lax.fori_loop(0, rows // step, run, 0)


def columns(at, width=CHUNK):
    return pl.ds(pl.multiple_of(at * width, width), width)


def fill_halo(padded, flags, tiles):
    pitch = TILE + 2 * REACH
    for at in range(tiles):
        base = at * pitch
        if at == 0:
            padded[:, base : base + REACH, :] = jnp.zeros_like(padded[:, base : base + REACH, :])
        if at == tiles - 1:
            end = base + REACH + TILE
            padded[:, end : end + REACH, :] = jnp.zeros_like(padded[:, end : end + REACH, :])
        else:
            keep = flags[at + 1]
            end = base + REACH + TILE
            padded[:, end : end + REACH, :] = (
                padded[:, base + pitch + REACH : base + pitch + 2 * REACH, :] * keep
            )
            padded[:, base + pitch : base + pitch + REACH, :] = (
                padded[:, end - REACH : end, :] * keep
            )


def taps_over(padded, table_ref, store, tiles, reverse, block=64):
    pitch = TILE + 2 * REACH
    per = TILE // block
    lanes = padded.shape[0]
    for lane in range(lanes):
        weights = [
            jnp.broadcast_to(
                table_ref[TAP_ROW + k : TAP_ROW + k + 1, lane * 128 : lane * 128 + 128], (block, 128)
            )
            for k in range(TAPS)
        ]

        def run(at, _):
            tile, inner = at // per, at % per
            base = tile * pitch + inner * block
            total = jnp.zeros((block, 128), F32)
            for k in range(TAPS):
                shift = REACH + (TAPS // 2 - k if reverse else k - TAPS // 2)
                total = total + weights[k] * padded[lane, pl.ds(base + shift, block), :]
            store(lane, tile * TILE + inner * block, base, total)
            return 0

        lax.fori_loop(0, tiles * per, run, 0)


def small_exp(v):
    return 1.0 + v * (1.0 + v * (0.5 + v * (1.0 / 6 + v * (1.0 / 24 + v * (1.0 / 120)))))


def small_expm1_over(v):
    return 1.0 + v * (
        0.5 + v * (1.0 / 6 + v * (1.0 / 24 + v * (1.0 / 120 + v * (1.0 / 720 + v * (1.0 / 5040)))))
    )


def state_terms(table_ref):
    log_decay = -jnp.exp(table_ref[RATE : RATE + STATES, :])
    root = jnp.sqrt(-2.0 * log_decay * small_expm1_over(2.0 * log_decay))
    maps_in = table_ref[MAP_IN : MAP_IN + STATES, :]
    maps_out = table_ref[MAP_OUT : MAP_OUT + STATES, :]
    return log_decay, small_exp(log_decay), root, maps_in, maps_out


def ref_rows(ref):
    return ref.reshape((ref.shape[0] * ref.shape[1], ref.shape[2]))


PIECE = 16
WIDTH = 512


def cols_of(ref, first, at):
    per = WIDTH // CHUNK
    part = ref[:, first + lax.div(at, per), :, columns(lax.rem(at, per))]
    return part.reshape((ref.shape[0] * PIECE, CHUNK))


def rows_of(ref, first, at):
    groups = WIDTH // (4 * PIECE)
    part = ref[pl.ds(at * groups, groups), first : first + 4]
    return part.reshape((WIDTH, WIDTH))


def bias_of(ref, layer, at):
    row = 8 * layer + 2 * at
    return jnp.concatenate([ref[pl.ds(row, 1), :], ref[pl.ds(row + 1, 1), :]], axis=1)


def square_of(ref, at):
    return ref[:, at].reshape((ref.shape[0] * PIECE, WIDTH))


def store_wide(out, first, acc):
    def run(group, _):
        rows = pl.ds(pl.multiple_of(group * PIECE, PIECE), PIECE)
        for k in range(acc.shape[1] // WIDTH):
            out[group, first + k] = acc[rows, k * WIDTH : k * WIDTH + WIDTH].astype(BF16)
        return 0

    lax.fori_loop(0, acc.shape[0] // PIECE, run, 0)


def store_tall(out, first, acc):
    def run(group, _):
        rows = pl.ds(pl.multiple_of(group * 4 * PIECE, 4 * PIECE), 4 * PIECE)
        out[group, first : first + 4] = acc[rows, :].astype(BF16).reshape((4, PIECE, WIDTH))
        return 0

    lax.fori_loop(0, acc.shape[0] // (4 * PIECE), run, 0)


def flat_groups(ref):
    count = 1
    for n in ref.shape[:-3]:
        count *= n
    return ref.reshape((count,) + ref.shape[-3:])


def carries(offsets_ref, counts_ref, tiles):
    out = []
    for tile in range(tiles):
        begins = jnp.int32(0)
        for slot in range(offsets_ref.shape[1]):
            here = (offsets_ref[0, slot] == tile * TILE) & (slot < counts_ref[0])
            begins = jnp.maximum(begins, here.astype(jnp.int32))
        out.append((1 - begins).astype(F32))
    return out


STRETCH = 16
SPREAD = PIECE * STATES


def same_channel(rows, width, per, first=0):
    shape = (rows, width)
    row = lax.rem(lax.broadcasted_iota(jnp.int32, shape, 0), PIECE)
    col = lax.broadcasted_iota(jnp.int32, shape, 1)
    if per == 1:
        return row == lax.rem(col, PIECE)
    return row == lax.div(col, per)


def split_low(v):
    high = v.astype(BF16)
    return high, (v - high.astype(F32)).astype(BF16)


def spread_states(part):
    rows = part.shape[0]
    state = lax.broadcasted_iota(jnp.int32, (STATES, SPREAD), 0)
    col = lax.broadcasted_iota(jnp.int32, (STATES, SPREAD), 1)
    pick_state = (state == lax.rem(col, STATES)).astype(F32).astype(BF16)
    wide = dot_nn(part, pick_state)
    wide = jnp.where(same_channel(rows, SPREAD, STATES), wide, 0.0)
    return jnp.sum(wide.reshape((rows // PIECE, PIECE, SPREAD)), axis=1)


def gather_states(wide):
    groups = wide.shape[0]
    full = jnp.broadcast_to(wide[:, None, :], (groups, PIECE, SPREAD)).reshape((groups * PIECE, SPREAD))
    full = jnp.where(same_channel(groups * PIECE, SPREAD, STATES), full, 0.0)
    state = lax.broadcasted_iota(jnp.int32, (SPREAD, 128), 1)
    row = lax.broadcasted_iota(jnp.int32, (SPREAD, 128), 0)
    pick_state = (state == lax.rem(row, STATES)).astype(F32).astype(BF16)
    high, low = split_low(full)
    return (dot_nn(high, pick_state) + dot_nn(low, pick_state)).T[:STATES, :]


def prepare_states(small, power, shifted, weight):
    groups = small.shape[0]
    entries = lambda first: small[:, :, first : first + STATES].reshape((groups * PIECE, STATES))
    log_decay = -jnp.exp(spread_states(entries(RATE)))
    root = jnp.sqrt(-2.0 * log_decay * small_expm1_over(2.0 * log_decay))
    both = spread_states(entries(MAP_IN)) * root * spread_states(entries(MAP_OUT))
    weight[...] = both
    col = lax.broadcasted_iota(jnp.int32, (SPREAD, 128), 1)
    row = lax.broadcasted_iota(jnp.int32, (SPREAD, 128), 0)
    add_states = (col == lax.div(row, STATES)).astype(F32).astype(BF16)
    power[0] = jnp.ones_like(both)
    decay = small_exp(log_decay)
    for m in range(1, STRETCH):
        power[m] = power[m - 1] * decay
    halves = []
    for half in range(2):
        total = jnp.zeros((groups, 128), F32)
        for k in range(8):
            high, low = split_low(power[half * 8 + k] * both)
            lag = dot_nn(high, add_states) + dot_nn(low, add_states)
            total = total + (pltpu.roll(lag, k * PIECE, 1) if k else lag)
        halves.append(total)
    blank = jnp.zeros((groups, 256), F32)
    padded = jnp.concatenate([blank] + halves, axis=1)
    for m in range(STRETCH):
        shifted[m] = pltpu.roll(padded, 512 - (m + 1) * PIECE, 1)[:, :256]


def group_weights(power, shifted, group, decay_w, lag_w):
    mask = same_channel(PIECE, SPREAD, STATES)
    lag_mask = same_channel(PIECE, 256, 1)
    for m in range(STRETCH):
        rows = slice(m * PIECE, m * PIECE + PIECE)
        line = jnp.broadcast_to(power[m, pl.ds(group, 1), :], (PIECE, SPREAD))
        decay_w[rows, :] = jnp.where(mask, line, 0.0).astype(BF16)
        line = jnp.broadcast_to(shifted[m, pl.ds(group, 1), :], (PIECE, 256))
        lag_w[rows, :] = jnp.where(lag_mask, line, 0.0).astype(BF16)


def swap_blocks(parts):
    col = lax.div(lax.broadcasted_iota(jnp.int32, parts[0].shape, 1), PIECE)
    parts = list(parts)
    for distance in (1, 2, 4):
        low = lax.rem(lax.div(col, distance), 2) == 0
        shift = distance * PIECE
        for a in range(8):
            if a & distance:
                continue
            first, second = parts[a], parts[a + distance]
            parts[a] = jnp.where(low, first, pltpu.roll(second, shift, 1))
            parts[a + distance] = jnp.where(low, pltpu.roll(first, 128 - shift, 1), second)
    return parts


SLAB = 32
TOGETHER = 4


def to_blocks(load, out, blocks, backward):
    for slab in range(blocks // SLAB):
        rows = slice(slab * SLAB, slab * SLAB + SLAB)
        for half in range(2):
            parts = []
            for k in range(8):
                frame = half * 8 + k
                frame = STRETCH - 1 - frame if backward else frame
                parts.append(load(slab * SLAB * STRETCH + frame))
            for group, part in enumerate(swap_blocks(parts)):
                out[group, rows, half * 128 : half * 128 + 128] = part.astype(out.dtype)


def from_blocks(store, ref, blocks, backward):
    for slab in range(blocks // SLAB):
        rows = slice(slab * SLAB, slab * SLAB + SLAB)
        for half in range(2):
            parts = [ref[group, rows, half * 128 : half * 128 + 128] for group in range(8)]
            for k, part in enumerate(swap_blocks(parts)):
                frame = half * 8 + k
                frame = STRETCH - 1 - frame if backward else frame
                store(slab * SLAB * STRETCH + frame, part)


def block_powers(decay):
    q2 = decay * decay
    q4 = q2 * q2
    q8 = q4 * q4
    one = q8 * q8
    two = one * one
    four = two * two
    return one, two, four


def row_powers(one, count=8):
    rows = [one]
    for _ in range(count - 1):
        rows.append(rows[-1] * one)
    return rows


def scan_blocks(source, into, decay, keeps, per, reverse):
    blocks, width = source.shape
    one, two, four = block_powers(decay)
    row = lax.broadcasted_iota(jnp.int32, (8, width), 0)
    if reverse:
        row = 7 - row
    factors = []
    for distance, power in ((1, one), (2, two), (4, four)):
        line = jnp.broadcast_to(power, (8, width))
        factors.append((8 - distance if reverse else distance, jnp.where(row >= distance, line, 0.0)))
    entering = jnp.ones((8, width), F32)
    for bit, power in ((1, one), (2, two), (4, four)):
        line = jnp.broadcast_to(power, (8, width))
        entering = jnp.where(lax.rem(lax.div(row, bit), 2) == 1, entering * line, entering)
    eight = jnp.broadcast_to(four * four, (8, width))
    carry = jnp.zeros((8, width), F32)
    tiles = blocks // 8
    for k in range(tiles):
        tile = tiles - 1 - k if reverse else k
        edge = (tile + 1) * 8 if reverse else tile * 8
        if k and edge % per == 0:
            carry = carry * keeps[edge // per]
        x = source[tile * 8 : tile * 8 + 8, :]
        for shift, factor in factors:
            x = x + factor * pltpu.roll(x, shift, 0)
        moved = pltpu.roll(x, 7 if reverse else 1, 0)
        into[tile * 8 : tile * 8 + 8, :] = jnp.where(row >= 1, moved, 0.0) + entering * carry
        end = x[0:1, :] if reverse else x[7:8, :]
        carry = jnp.broadcast_to(end, (8, width)) + eight * carry


def mix_forward(midway, u_ref, y_ref, power, shifted, weight, keeps, ub_out, state_out, blk_in, blk_out, decay_w, lag_w, t_scr, h_scr):
    frames = u_ref.shape[1]
    blocks = frames // STRETCH
    count = decay_w.shape[0]
    several = range(count)

    def lane_tile(lane, _):
        if midway is not None:
            pl.when(lane == u_ref.shape[0] // 2)(midway)
        to_blocks(lambda at: u_ref[lane, pl.ds(at, SLAB, stride=STRETCH), :], blk_in, blocks, True)

        def some_groups(k, _):
            place = [k * count + n for n in several]
            groups = [lane * 8 + at for at in place]
            for n in several:
                group_weights(power, shifted, groups[n], decay_w.at[n], lag_w.at[n])
            for n in several:
                ub_out[groups[n]] = blk_in[place[n]]
                t_scr[n] = dot_nn(blk_in[place[n]], decay_w[n])
            for n in several:
                decay = power[1, pl.ds(groups[n], 1), :]
                scan_blocks(t_scr.at[n], h_scr.at[n], decay, keeps, TILE // STRETCH, False)
            for n in several:
                decay = power[1, pl.ds(groups[n], 1), :]
                state = h_scr[n]
                state_out[groups[n]] = state.astype(BF16)
                out = (state * (weight[pl.ds(groups[n], 1), :] * decay)).astype(BF16)
                blk_out[place[n]] = dot_nn(blk_in[place[n]], lag_w[n]) + dot_nt(out, decay_w[n])
            return 0

        lax.fori_loop(0, 8 // count, some_groups, 0)

        def store(at, values):
            y_ref[lane, pl.ds(at, SLAB, stride=STRETCH), :] = values

        from_blocks(store, blk_out, blocks, False)
        return 0

    lax.fori_loop(0, u_ref.shape[0], lane_tile, 0)


def mix_backward(
    lane, u_ref, grad, skip, u_tile, u_sem, power, shifted, weight, keeps, ub_ref, state_ref, lags, sums,
    frames_scr, blk_in, blk_out, decay_w, lag_w, stack_scr, e_scr, r_scr,
):
    blocks = frames_scr.shape[2]
    count = decay_w.shape[0]
    several = range(count)
    lanes = u_ref.shape[0]
    copy = lambda at: pltpu.make_async_copy(u_ref.at[at], u_tile, u_sem)
    copy(lane).wait()
    for at in range(STRETCH):
        for slab in range(blocks // SLAB):
            rows = slice(slab * SLAB, slab * SLAB + SLAB)
            first = pl.ds(slab * SLAB * STRETCH + at, SLAB, stride=STRETCH)
            frames_scr[0, at, rows, :] = u_tile[first, :]
            frames_scr[1, at, rows, :] = grad[lane, first, :]

    @pl.when(lane + 1 < lanes)
    def _():
        copy(lane + 1).start()

    def one_lag(lag, _):
        def one_frame(at, total):
            for slab in range(blocks // SLAB):
                rows = slice(slab * SLAB, slab * SLAB + SLAB)
                total = total + frames_scr[1, at, rows, :] * frames_scr[0, at - lag, rows, :]
            return total

        total = lax.fori_loop(lag, STRETCH, one_frame, jnp.zeros((SLAB, 128), F32))
        lags[lane, pl.ds(lag, 1), :] = jnp.sum(total, axis=0, keepdims=True)
        return 0

    lax.fori_loop(0, STRETCH, one_lag, 0)
    for slab in range(blocks // SLAB):
        rows = slice(slab * SLAB, slab * SLAB + SLAB)
        for half in range(2):
            parts = [frames_scr[1, half * 8 + k, rows, :] for k in range(8)]
            for group, part in enumerate(swap_blocks(parts)):
                blk_in[group, rows, half * 128 : half * 128 + 128] = part.astype(BF16)
    position = lax.div(lax.broadcasted_iota(jnp.int32, (1, 256), 1), PIECE).astype(F32)

    def some_groups(k, _):
        place = [k * count + n for n in several]
        groups = [lane * 8 + at for at in place]
        for n in several:
            group_weights(power, shifted, groups[n], decay_w.at[n], lag_w.at[n])
        for n in several:
            gy = blk_in[place[n]]
            stack_scr[n, 0:blocks, :] = gy
            stack_scr[n, blocks : 2 * blocks, :] = (gy.astype(F32) * (position + 1.0)).astype(BF16)
            stack_scr[n, 2 * blocks :, :] = (ub_ref[groups[n]].astype(F32) * position).astype(BF16)
        for n in several:
            e_scr[n] = dot_nn(stack_scr[n], decay_w[n])
        for n in several:
            decay = power[1, pl.ds(groups[n], 1), :]
            own = e_scr.at[n, pl.ds(0, blocks)]
            own[...] = own[...] * decay
            scan_blocks(own, r_scr.at[n], decay, keeps, TILE // STRETCH, True)
        for n in several:
            group = groups[n]
            inverse = 1.0 / power[1, pl.ds(group, 1), :]
            last = 16.0 * power[15, pl.ds(group, 1), :]
            first, second = jnp.zeros((8, SPREAD), F32), jnp.zeros((8, SPREAD), F32)
            for at in range(blocks // 8):
                rows = slice(at * 8, at * 8 + 8)
                state = state_ref[group, rows, :].astype(F32)
                turn = e_scr[n, 2 * blocks + at * 8 : 2 * blocks + at * 8 + 8, :]
                first = first + state * e_scr[n, rows, :]
                second = second + state * e_scr[n, blocks + at * 8 : blocks + at * 8 + 8, :]
                second = second + r_scr[n, rows, :] * (turn * inverse + last * state)
            sums[0, pl.ds(group, 1), :] = jnp.sum(first, axis=0, keepdims=True)
            sums[1, pl.ds(group, 1), :] = jnp.sum(second, axis=0, keepdims=True)
            out = (r_scr[n] * weight[pl.ds(group, 1), :]).astype(BF16)
            blk_out[place[n]] = dot_nt(blk_in[place[n]], lag_w[n]) + dot_nt(out, decay_w[n])
        return 0

    lax.fori_loop(0, 8 // count, some_groups, 0)

    def store(at, values):
        slab, frame = at // (SLAB * STRETCH), at % STRETCH
        through = frames_scr[1, frame, slab * SLAB : slab * SLAB + SLAB, :]
        grad[lane, pl.ds(at, SLAB, stride=STRETCH), :] = values + skip[pl.ds(lane, 1), :] * through

    from_blocks(store, blk_out, blocks, True)


def mix_gradients(lags, sums, table_ref):
    _, decay, root, maps_in, maps_out = state_terms(table_ref)
    coupling = maps_in * root * maps_out
    gmap = gather_states(sums[0])
    gdecay = gather_states(sums[1])
    power = jnp.ones_like(decay)
    for lag in range(STRETCH):
        line = jnp.concatenate([lags[k, lag : lag + 1, :] for k in range(lags.shape[0])], axis=1)
        if lag:
            gdecay = gdecay + float(lag) * power * line
            power = power * decay
        gmap = gmap + power * line
    return gmap, gdecay * coupling


def pack_small(out, scr, place, bias_ref, gains, shifts, conv_bias, taps, rate, maps):
    own = gains.shape[1]
    scr[...] = jnp.zeros_like(scr)
    scr[0:6, :own] = gains[...].astype(F32)
    scr[6:18, :own] = shifts[...].astype(F32)
    scr[18:19, :own] = conv_bias[...].astype(F32)
    scr[TAP_ROW : TAP_ROW + TAPS, :own] = taps[...].astype(F32)
    out[:, :CHUNK] = scr[...].T[:own, :].astype(BF16)
    out[:, RATE:MAP_IN] = rate[...]
    out[:, MAP_IN:MAP_OUT] = maps[0]
    out[:, MAP_OUT:TABLE] = maps[1]
    count = bias_ref.shape[1]
    row = lax.div(place * count, CHUNK)
    inner = place * count - row * CHUNK
    at_row = lax.broadcasted_iota(jnp.int32, (PIECE, CHUNK), 0)
    wide = jnp.zeros((PIECE, CHUNK), F32)
    for layer in range(2):
        line = jnp.broadcast_to(bias_ref[layer : layer + 1, :].astype(F32), (8, count))
        line = jnp.concatenate([line, jnp.zeros((8, CHUNK - count), F32)], axis=1)
        line = pltpu.roll(line, inner, 1)
        wide = wide + jnp.where(at_row == 8 * layer + row, jnp.broadcast_to(line[0:1], wide.shape), 0.0)
    out[:, CHUNK:] = wide.astype(BF16)


def front_kernel(mesh_size, *refs):
    fused = mesh_size is not None
    refs = list(refs)
    take = lambda count: [refs.pop(0) for _ in range(count)]
    offsets_ref, counts_ref, x_ref = take(3)
    if fused:
        n_dp, n_fs = mesh_size
        small_in = take(7)
        up_s, down_s, mixin_s, mixout_s, convin_s, convout_s = take(6)
    else:
        first_v, extra_v, second_v, third_v, fourth_v, table_in, bias_in = take(7)
    (
        h_out,
        x1_out,
        v_out,
        y_out,
        gated_out,
        x2_out,
        p_out,
        u_out,
        w_out,
        stat_out,
        table_ref,
        bias_ref,
        ub_out,
        state_out,
        power,
        shifted,
        weight,
    ) = take(17)
    gathered = take(6) if fused else []
    x1_scr, low_all, low_scr, sum_scr, y_all, padded, act_all = take(7)
    mix_scr = take(6)
    step = pl.program_id(0)
    channels = x_ref.shape[1]
    frames = w_out.shape[0]
    tiles = frames // TILE
    lanes = channels // 128
    gain = lambda k: table_ref[k : k + 1, :]
    shift = lambda k: table_ref[6 + k : 7 + k, :]
    here = lambda rows, tile: pl.ds(pl.multiple_of(tile * TILE + rows.start, ROWS), ROWS)
    flags = carries(offsets_ref, counts_ref, tiles)
    mix_at, last_step = 3 * tiles, 4 * tiles + 1
    if fused:
        landing = take(5)
        sources = take(6)
        turn_scr = refs.pop(0)
        sems = take(3)
        load_sem = refs.pop(0)
        swap = take(4)
        dp, fs = lax.axis_index("dp"), lax.axis_index("fsdp")
        place = Place(dp, fs, n_dp, n_fs)
        landing.append(gathered[5])
        plans, sends = block_gather(place, sources, landing, *sems)
        first_v, extra_v, second_v, third_v, fourth_v = [flat_groups(r) for r in landing[:5]]

        def keep_copy(chunk):
            return pltpu.make_async_copy(landing[chunk], gathered[chunk], load_sem.at[chunk])

        def run(*stages):
            for chunk, stage in stages:
                plans[chunk][stage]()

        @pl.when(step == 0)
        def _():
            pack_small(sources[0].at[0], turn_scr, dp * n_fs + fs, *small_in)
            for k in range(4):
                cols = slice(k * WIDTH, k * WIDTH + WIDTH)
                if k < 2:
                    sources[0][1 + k] = up_s[0, :, cols]
                else:
                    sources[1][k - 2] = up_s[0, :, cols]
                sources[5][1 + k] = up_s[1, :, cols]
                rows = slice(k * PIECE, k * PIECE + PIECE)
                sources[2][k] = down_s[0, rows, :]
                sources[5][5 + k] = down_s[1, rows, :]
            for k in range(2):
                cols = slice(k * WIDTH, k * WIDTH + WIDTH)
                sources[3][k] = mixin_s[:, cols]
                sources[4][1 + k] = convin_s[:, cols]
            sources[4][0] = mixout_s[...]
            sources[5][0] = convout_s[...]
            greet(dp, fs, n_dp, n_fs)
            run((0, 0), (1, 0), (0, 1), (2, 0), (1, 1), (0, 2), (1, 2), (0, 3), (2, 1), (3, 0), (0, 4))
            table_ref[...] = first_v[:, 0, :, :CHUNK].reshape((channels, CHUNK)).astype(F32).T[:TABLE, :]
            total = first_v[0, 0, :, CHUNK:].astype(F32)
            for k in range(1, n_dp * n_fs):
                total = total + first_v[k, 0, :, CHUNK:].astype(F32)
            bias_ref[...] = total

        rest = {1: [(1, 3), (2, 2)], 2: [(3, 1)], tiles: [(1, 4), (4, 0)], tiles + 1: [(2, 3), (3, 2)]}
        rest.update({2 * tiles: [(2, 4), (3, 3), (4, 1)], 2 * tiles + 1: [(5, 0)]})
        rest.update({2 * tiles + 2: [(4, 2)], mix_at: [(3, 4)]})
        rest.update({mix_at + 1: [(4, 4), (5, 2)], last_step: [(5, 3)]})
        for at, stages in rest.items():

            @pl.when(step == at)
            def _(at=at, stages=stages):
                run(*stages)
                saved = {2 * tiles: (0, 1, 2), mix_at: (3,), mix_at + 1: (4,)}
                for chunk in saved.get(at, ()):
                    keep_copy(chunk).start()

    else:

        @pl.when(step == 0)
        def _():
            table_ref[...] = table_in[...]
            bias_ref[...] = bias_in[...]

    @pl.when(step < tiles)
    def _():
        def first(rows):
            e, _ = norm_parts(x_ref[rows, :].astype(F32))
            low_all[here(rows, step), :] = (e * gain(0) + shift(0)).astype(BF16)

        by_rows(first)

    for half, part in enumerate((first_v, extra_v)):

        @pl.when((step >= half * tiles) & (step < half * tiles + tiles))
        def _(half=half, part=part):
            tile_rows = pl.ds(pl.multiple_of((step - half * tiles) * TILE, TILE), TILE)
            for k in range(2):
                c = 2 * half + k
                h = dot_nn(low_all[tile_rows, :], square_of(part, 1 - half + k))
                h = h + bias_of(bias_ref, 0, c)
                h_out[:, k * WIDTH : k * WIDTH + WIDTH] = h.astype(BF16)
                active = (h * sigmoid(h)).astype(BF16)
                act_all[tile_rows, c * WIDTH : c * WIDTH + WIDTH] = active

    @pl.when((step >= 2 * tiles) & (step < mix_at))
    def _():
        at = step - 2 * tiles
        tile_rows = pl.ds(pl.multiple_of(at * TILE, TILE), TILE)
        total = dot_nn(act_all[tile_rows, :WIDTH], rows_of(second_v, 0, 0))
        for c in range(1, 4):
            cols = slice(c * WIDTH, c * WIDTH + WIDTH)
            total = total + dot_nn(act_all[tile_rows, cols], rows_of(second_v, 0, c))
        sum_scr[...] = total

        def second(rows):
            x1 = x_ref[rows, :].astype(F32) + 0.5 * (sum_scr[rows, :] + shift(6))
            x1_out[rows, :] = x1
            x1_scr[here(rows, at), :] = x1
            e, _ = norm_parts(x1)
            low_all[here(rows, at), :] = (e * gain(1) + shift(1)).astype(BF16)

        by_rows(second)

    @pl.when(step == mix_at)
    def _():
        prepare_states(first_v[:, 0, :, :CHUNK], power, shifted, weight)

        def project(tile, _):
            rows = pl.ds(pl.multiple_of(tile * TILE, TILE), TILE)
            u = dot_nn(low_all[rows, :], square_of(third_v, 0))
            for lane in range(lanes):
                u_out[lane, rows, :] = u[:, lane * 128 : lane * 128 + 128]
            return 0

        lax.fori_loop(0, tiles, project, 0)
        if fused:
            run((4, 3))
        mixing = (u_out, y_all, power, shifted, weight, flags, ub_out, state_out) + tuple(mix_scr)
        mix_forward((lambda: run((5, 1))) if fused else None, *mixing)

    @pl.when((step > mix_at) & (step < last_step))
    def _():
        at = step - mix_at - 1
        whole_tile = pl.ds(pl.multiple_of(at * TILE, TILE), TILE)
        v_out[...] = dot_nn(low_all[whole_tile, :], square_of(third_v, 1)).astype(BF16)

        def gate(rows):
            join = lambda ref: jnp.concatenate([ref[lane, here(rows, at), :] for lane in range(lanes)], axis=1)
            y = join(y_all) + shift(11) * join(u_out)
            v = v_out[rows, :].astype(F32)
            y_out[rows, :] = y.astype(BF16)
            gated_out[rows, :] = (y * (v * sigmoid(v))).astype(BF16)

        by_rows(gate)
        sum_scr[...] = dot_nn(gated_out[...], square_of(fourth_v, 0))

        def third(rows):
            x2 = x1_scr[here(rows, at), :] + (sum_scr[rows, :] + shift(8))
            x2_out[rows, :] = x2
            e, _ = norm_parts(x2)
            low_scr[rows, :] = (e * gain(2) + shift(2)).astype(BF16)

        by_rows(third)
        pitch = TILE + 2 * REACH

        def widen(c, _):
            cols = columns(c)
            right = columns(c + channels // CHUNK)
            left_part = dot_nn(low_scr[...], cols_of(fourth_v, 1, c)) + table_ref[15:16, cols]
            right_part = dot_nn(low_scr[...], cols_of(fourth_v, 2, c)) + table_ref[16:17, cols]
            p_out[:, cols] = left_part.astype(BF16)
            p_out[:, right] = right_part.astype(BF16)
            g = left_part * sigmoid(right_part)
            place = pl.ds(pl.multiple_of(at * pitch + REACH, 8), TILE)
            for k in range(CHUNK // 128):
                padded[c * (CHUNK // 128) + k, place, :] = g[:, k * 128 : k * 128 + 128]
            return 0

        lax.fori_loop(0, channels // CHUNK, widen, 0)

    @pl.when(step == last_step)
    def _():
        fill_halo(padded, flags, tiles)

        def store(lane, row, base, total):
            w_out[pl.ds(pl.multiple_of(row, 64), 64), lane * 128 : lane * 128 + 128] = total

        taps_over(padded, table_ref, store, tiles, False)
        stat_out[...] = jnp.zeros_like(stat_out)

        def total(at, _):
            rows = pl.ds(pl.multiple_of(at * ROWS, ROWS), ROWS)
            stat_out[...] += fold8(w_out[rows, :])
            return 0

        lax.fori_loop(0, frames // ROWS, total, 0)
        center = jnp.sum(stat_out[...], axis=0, keepdims=True) * (1.0 / frames)
        stat_out[...] = jnp.zeros_like(stat_out)

        def spread(at, _):
            rows = pl.ds(pl.multiple_of(at * ROWS, ROWS), ROWS)
            off = w_out[rows, :] - center
            stat_out[...] += fold8(off * off)
            return 0

        lax.fori_loop(0, frames // ROWS, spread, 0)
        around = jnp.sum(stat_out[...], axis=0, keepdims=True)
        if fused:
            center, around = pool_over(center, around, frames, dp, fs, n_dp, n_fs, *swap)
            around = lax.rsqrt(around * (1.0 / (frames * n_dp * n_fs)) + EPSILON)
        stat_out[...] = jnp.zeros_like(stat_out)
        stat_out[0:1, :] = center
        stat_out[1:2, :] = around
        if fused:
            run((5, 4))
            for chunk in range(5):
                keep_copy(chunk).wait()
            for wait in sends:
                wait()


def whole(shape):
    zeros = (0,) * len(shape)
    return pl.BlockSpec(shape, lambda *_: zeros, pipeline_mode=pl.Buffered(1))


def params(collective_id=None):
    if collective_id is None:
        return pltpu.CompilerParams(
            dimension_semantics=("arbitrary",), vmem_limit_bytes=VMEM_LIMIT
        )
    return pltpu.CompilerParams(
        dimension_semantics=("arbitrary",),
        vmem_limit_bytes=VMEM_LIMIT,
        collective_id=collective_id,
        has_side_effects=True,
    )


SMEM_SPEC = pl.BlockSpec(memory_space=pltpu.SMEM)
HBM_SPEC = pl.BlockSpec(memory_space=pltpu.HBM)


def front(mesh_size, offsets, counts, x, small, weights, hidden, collective_id=None):
    fused = mesh_size is not None
    frames, channels = x.shape
    tiles = frames // TILE
    clip = lambda i, first: jnp.clip(i - first, 0, tiles - 1)
    twice = lambda i: (jnp.where(i < tiles, i, jnp.where(i < 2 * tiles, tiles - 1, clip(i, 2 * tiles))), 0)
    halves = lambda i: (jnp.where(i < tiles, i, clip(i, tiles)), jnp.where(i < tiles, 0, 1))
    place = lambda i: clip(i, 3 * tiles + 1)
    late = lambda width: pl.BlockSpec((TILE, width), lambda i: (place(i), 0))
    shape = lambda width, kind: jax.ShapeDtypeStruct((frames, width), kind)
    groups, blocks = channels // PIECE, frames // STRETCH
    out_shape = [
        shape(hidden, BF16),
        shape(channels, F32),
        shape(channels, BF16),
        shape(channels, BF16),
        shape(channels, BF16),
        shape(channels, F32),
        shape(2 * channels, BF16),
        jax.ShapeDtypeStruct((channels // 128, frames, 128), F32),
        shape(channels, F32),
        jax.ShapeDtypeStruct((8, channels), F32),
        jax.ShapeDtypeStruct((TABLE, channels), F32),
        jax.ShapeDtypeStruct((16, CHUNK), F32),
        jax.ShapeDtypeStruct((groups, blocks, STRETCH * PIECE), BF16),
        jax.ShapeDtypeStruct((groups, blocks, SPREAD), BF16),
        jax.ShapeDtypeStruct((STRETCH, groups, SPREAD), F32),
        jax.ShapeDtypeStruct((STRETCH, groups, STRETCH * PIECE), F32),
        jax.ShapeDtypeStruct((groups, SPREAD), F32),
    ]
    out_specs = [
        pl.BlockSpec((TILE, hidden // 2), halves),
        pl.BlockSpec((TILE, channels), lambda i: (clip(i, 2 * tiles), 0)),
    ]
    out_specs += [late(channels)] * 4 + [late(2 * channels)]
    out_specs += [whole(s.shape) for s in out_shape[7:]]
    scratch = [
        pltpu.VMEM((frames, channels), F32),
        pltpu.VMEM((frames, channels), BF16),
        pltpu.VMEM((TILE, channels), BF16),
        pltpu.VMEM((TILE, channels), F32),
        pltpu.VMEM((channels // 128, frames, 128), F32),
        pltpu.VMEM((channels // 128, tiles * (TILE + 2 * REACH), 128), F32),
        pltpu.VMEM((frames, hidden), BF16),
        pltpu.VMEM((8, blocks, STRETCH * PIECE), BF16),
        pltpu.VMEM((8, blocks, STRETCH * PIECE), F32),
        pltpu.VMEM((TOGETHER, STRETCH * PIECE, SPREAD), BF16),
        pltpu.VMEM((TOGETHER, STRETCH * PIECE, STRETCH * PIECE), BF16),
        pltpu.VMEM((TOGETHER, blocks, SPREAD), F32),
        pltpu.VMEM((TOGETHER, blocks, SPREAD), F32),
    ]
    operands = (weights if not fused else small + weights) + (small if not fused else [])
    if fused:
        layout = block_layout(*mesh_size)
        blocks = (3, 2, 4, 2, 3, 9)
        chunks = [jax.ShapeDtypeStruct(layout + (k, PIECE, WIDTH), BF16) for k in blocks]
        out_shape += chunks
        out_specs += [HBM_SPEC] * len(chunks)
        scratch += [pltpu.VMEM(c.shape, BF16) for c in chunks[:5]]
        scratch += [pltpu.VMEM((k, PIECE, WIDTH), BF16) for k in blocks]
        scratch += [pltpu.VMEM((CHUNK, 128), F32)]
        scratch += block_sems(*mesh_size, len(chunks)) + [pltpu.SemaphoreType.DMA((5,))]
        scratch += swap_scratch(*mesh_size, channels)
    return pl.pallas_call(
        partial(front_kernel, mesh_size),
        grid=(4 * tiles + 2,),
        in_specs=[SMEM_SPEC, SMEM_SPEC, pl.BlockSpec((TILE, channels), twice)] + [whole(a.shape) for a in operands],
        out_specs=out_specs,
        out_shape=out_shape,
        scratch_shapes=scratch,
        compiler_params=params(collective_id),
        name="front",
    )(offsets, counts, x, *operands)


def middle_kernel(
    mesh_size,
    x2_ref,
    w_ref,
    cot_ref,
    blocks_ref,
    bias_ref,
    vec_ref,
    stat_ref,
    out_ref,
    gx3_ref,
    gnb_ref,
    gblocks_out,
    gbias_out,
    gvec_out,
    stat_out,
    up_acc,
    down_acc,
    convout_acc,
    bias_acc,
    vec_acc,
    h_scr,
    low_scr,
    turn_scr,
    act_scr,
    grad_scr,
    sum_scr,
    x3_scr,
    *swap,
):
    at = pl.program_id(0)
    tiles = pl.num_programs(0)
    channels = x2_ref.shape[1]
    if mesh_size is not None:
        n_dp, n_fs = mesh_size
        dp, fs = lax.axis_index("dp"), lax.axis_index("fsdp")

        @pl.when(at == 0)
        def _():
            greet(dp, fs, n_dp, n_fs)

    hidden = up_acc.shape[1]
    gain = lambda k: vec_ref[k : k + 1, :]
    shift = lambda k: vec_ref[6 + k : 7 + k, :]
    center, scale = stat_ref[0:1, :], stat_ref[1:2, :]

    @pl.when(at == 0)
    def _():
        for ref in (up_acc, down_acc, convout_acc, bias_acc, vec_acc):
            ref[...] = jnp.zeros_like(ref)

    def normed(rows):
        e = (w_ref[rows, :] - center) * scale
        return e, e * gain(5) + shift(5)

    def first(rows):
        _, nb = normed(rows)
        act_scr[rows, :] = (nb * sigmoid(nb)).astype(BF16)

    by_rows(first)
    sum_scr[...] = dot_nn(act_scr[...], square_of(blocks_ref, 0))

    def second(rows):
        x3 = x2_ref[rows, :] + (sum_scr[rows, :] + vec_ref[18:19, :])
        x3_scr[rows, :] = x3
        e, _ = norm_parts(x3)
        low_scr[rows, :] = (e * gain(3) + shift(3)).astype(BF16)
        sum_scr[rows, :] = jnp.zeros((ROWS, channels), F32)

    by_rows(second)

    def forward(c, _):
        cols = columns(c, WIDTH)
        h = dot_nn(low_scr[...], square_of(blocks_ref, 1 + c)) + bias_of(bias_ref, 1, c)
        h_scr[:, cols] = h
        active = (h * sigmoid(h)).astype(BF16)
        sum_scr[...] += dot_nn(active, rows_of(blocks_ref, 5, c))
        return 0

    lax.fori_loop(0, hidden // WIDTH, forward, 0)
    turn_scr[...] = low_scr[...].T

    def last(rows):
        x4 = x3_scr[rows, :] + 0.5 * (sum_scr[rows, :] + shift(7))
        e, inv = norm_parts(x4)
        out_ref[rows, :] = (e * gain(4) + shift(4)).astype(BF16)
        cot = cot_ref[rows, :].astype(F32)
        vec_acc[0] += fold8(cot * e)
        vec_acc[1] += fold8(cot)
        gx4 = norm_back(cot, e, inv, gain(4))
        gx3_ref[rows, :] = gx4
        low = (0.5 * gx4).astype(BF16)
        grad_scr[rows, :] = low
        vec_acc[2] += fold8(low.astype(F32))
        sum_scr[rows, :] = jnp.zeros((ROWS, channels), F32)

    by_rows(last)

    def backward(c, _):
        cols = columns(c, WIDTH)
        h = h_scr[:, cols]
        sig = sigmoid(h)
        active = h * sig
        gate = dot_nt(grad_scr[...], rows_of(blocks_ref, 5, c))
        grad_h = (gate * (sig * (1.0 + h - active))).astype(BF16)
        bias_acc[:, cols] += fold8(grad_h.astype(F32))
        down_acc[cols, :] += dot_tn(active.astype(BF16), grad_scr[...])
        up_acc[:, cols] += dot_nn(turn_scr[...], grad_h)
        sum_scr[...] += dot_nt(grad_h, square_of(blocks_ref, 1 + c))
        return 0

    lax.fori_loop(0, hidden // WIDTH, backward, 0)

    def fourth(rows):
        e, inv = norm_parts(x3_scr[rows, :])
        grad = sum_scr[rows, :]
        vec_acc[3] += fold8(grad * e)
        vec_acc[4] += fold8(grad)
        gx3 = gx3_ref[rows, :] + norm_back(grad, e, inv, gain(3))
        gx3_ref[rows, :] = gx3
        low = gx3.astype(BF16)
        grad_scr[rows, :] = low
        vec_acc[5] += fold8(low.astype(F32))

    by_rows(fourth)
    convout_acc[...] += dot_tn(act_scr[...], grad_scr[...])
    sum_scr[...] = dot_nt(grad_scr[...], square_of(blocks_ref, 0))

    def fifth(rows):
        e, nb = normed(rows)
        sig = sigmoid(nb)
        gnb = sum_scr[rows, :] * (sig * (1.0 + nb * (1.0 - sig)))
        gnb_ref[rows, :] = gnb
        vec_acc[6] += fold8(gnb * e)
        vec_acc[7] += fold8(gnb)

    by_rows(fifth)

    @pl.when(at == tiles - 1)
    def _():
        for k in range(8):
            gvec_out[k : k + 1, :] = jnp.sum(vec_acc[k], axis=0, keepdims=True)

        def convert():
            store_wide(gblocks_out, 0, convout_acc)
            store_wide(gblocks_out, 1, up_acc)
            store_tall(gblocks_out, 5, down_acc)
            gbias_out[...] = jnp.broadcast_to(
                jnp.sum(bias_acc[...], axis=0, keepdims=True), gbias_out.shape
            )

        stat_out[...] = stat_ref[...]
        if mesh_size is None:
            convert()
        else:
            total = sum_over(gvec_out[...], dp, fs, n_dp, n_fs, *swap, between=convert)
            share = gain(5) * (1.0 / (TILE * tiles * n_dp * n_fs))
            stat_out[2:3, :] = total[7:8, :] * share
            stat_out[3:4, :] = total[6:7, :] * share


def middle(mesh_size, x2, w, cot, blocks, bias, vec, stat, hidden, collective_id=None):
    frames, channels = x2.shape
    tiles = frames // TILE
    row = lambda width: pl.BlockSpec((TILE, width), lambda i: (i, 0))
    shapes = [
        jax.ShapeDtypeStruct((frames, channels), BF16),
        jax.ShapeDtypeStruct((frames, channels), F32),
        jax.ShapeDtypeStruct((frames, channels), F32),
        jax.ShapeDtypeStruct(blocks.shape, BF16),
        jax.ShapeDtypeStruct((8, hidden), F32),
        jax.ShapeDtypeStruct((8, channels), F32),
        jax.ShapeDtypeStruct((8, channels), F32),
    ]
    swap = [] if mesh_size is None else swap_scratch(*mesh_size, channels)
    return pl.pallas_call(
        partial(middle_kernel, mesh_size),
        grid=(tiles,),
        in_specs=[row(channels)] * 3
        + [whole(a.shape) for a in (blocks, bias, vec, stat)],
        out_specs=[row(channels)] * 3 + [whole(s.shape) for s in shapes[3:]],
        out_shape=shapes,
        scratch_shapes=[
            pltpu.VMEM((channels, hidden), F32),
            pltpu.VMEM((hidden, channels), F32),
            pltpu.VMEM((channels, channels), F32),
            pltpu.VMEM((8, hidden), F32),
            pltpu.VMEM((8, 8, channels), F32),
            pltpu.VMEM((TILE, hidden), F32),
            pltpu.VMEM((TILE, channels), BF16),
            pltpu.VMEM((channels, TILE), BF16),
            pltpu.VMEM((TILE, channels), BF16),
            pltpu.VMEM((TILE, channels), BF16),
            pltpu.VMEM((TILE, channels), F32),
            pltpu.VMEM((TILE, channels), F32),
        ]
        + swap,
        compiler_params=params(collective_id),
        name="middle",
    )(x2, w, cot, blocks, bias, vec, stat)


def back_kernel(mesh_size, *refs):
    fused = mesh_size is not None
    refs = list(refs)
    take = lambda count: [refs.pop(0) for _ in range(count)]
    offsets_ref, counts_ref, w_ref, gnb_ref, p_ref = take(5)
    x2_ref, gx3_ref, gated_ref, y_ref, v_ref, x1_ref = take(6)
    u_ref, ub_ref, state_ref, power, shifted, weight, mixin_ref, middle_ref, vec_ref, stat_ref = take(10)
    sources = take(1) if fused else []
    gx1_ref, gin_out, gvec_out, gtaps_ref, gmap_out, gdecay_out = take(6)
    reduced = take(2) if fused else []
    mid_ref = None if fused else refs.pop(0)
    wide_acc, mixout_acc, vec_acc, low_scr, wide_scr, sum_scr = take(6)
    padded, gpad, gv_all, lags, sums, skip, u_tile, u_sem = take(8)
    mix_scr = take(8)
    step = pl.program_id(0)
    channels = x2_ref.shape[1]
    frames = u_ref.shape[1]
    tiles = frames // TILE
    lanes = channels // 128
    pitch = TILE + 2 * REACH
    conv_at, mix_at = tiles, 2 * tiles + 1
    last_step = 3 * tiles + 1
    gain = lambda k: vec_ref[k : k + 1, :]
    shift = lambda k: vec_ref[6 + k : 7 + k, :]
    left, right = slice(0, channels), slice(channels, 2 * channels)
    flags = carries(offsets_ref, counts_ref, tiles)
    schedule = {}
    if fused:
        n_dp, n_fs = mesh_size
        place = Place(lax.axis_index("dp"), lax.axis_index("fsdp"), n_dp, n_fs)
        mid_src = refs.pop(0)
        mid_ref = flat_groups(mid_src)
        scratch = take(2 * (2 + place.count))

        def emit(chunk, total):
            reduced[chunk][...] = total

        plans, sends = block_scatter(place, sources + [mid_src], emit, scratch, *take(3))
        first = [(0, 0), (conv_at, 1), (conv_at + 2, 0), (conv_at + 3, 0), (mix_at, 1)]
        second = [(mix_at, 0), (mix_at, 1), (mix_at + 1, 0), (mix_at + 2, 0), (last_step, 1)]
        for chunk, points in enumerate((first, second)):
            for stage, point in enumerate(points):
                schedule.setdefault(point, []).append((stage, chunk))

    def progress(at, part):
        for stage, chunk in sorted(schedule.get((at, part), [])):
            plans[chunk][stage]()

    @pl.when(step == 0)
    def _():
        for ref in (wide_acc, mixout_acc, vec_acc):
            ref[...] = jnp.zeros_like(ref)
        if fused:
            greet(place.dp, place.fs, n_dp, n_fs)

    for at in sorted({key[0] for key in schedule if key[1] == 0 and key[0] != mix_at}):

        @pl.when(step == at)
        def _(at=at):
            progress(at, 0)

    @pl.when(step < tiles)
    def _():
        center, scale = stat_ref[0:1, :], stat_ref[1:2, :]
        plain, cross = stat_ref[2:3, :], stat_ref[3:4, :]

        def fill(index, _):
            rows = pl.ds(pl.multiple_of(index * 64, 64), 64)
            spot = pl.ds(pl.multiple_of(step * pitch + REACH + index * 64, 8), 64)
            e = (w_ref[rows, :] - center) * scale
            d = gnb_ref[rows, :] * gain(5)
            gw = scale * (d - plain - e * cross)
            g = p_ref[rows, left].astype(F32) * sigmoid(p_ref[rows, right].astype(F32))
            for lane in range(lanes):
                cols = slice(lane * 128, lane * 128 + 128)
                padded[lane, spot, :] = gw[:, cols]
                gpad[lane, spot, :] = g[:, cols]
            return 0

        lax.fori_loop(0, TILE // 64, fill, 0)

    @pl.when(step == conv_at)
    def _():
        fill_halo(padded, flags, tiles)
        fill_halo(gpad, flags, tiles)
        block = 64
        per = TILE // block
        gtaps_ref[...] = jnp.zeros_like(gtaps_ref)
        for lane in range(lanes):

            def corr(index, sums, lane=lane):
                base = (index // per) * pitch + (index % per) * block
                here = padded[lane, pl.ds(pl.multiple_of(base + REACH, 8), block), :]
                return tuple(
                    s + fold8(here * gpad[lane, pl.ds(base + REACH + k - TAPS // 2, block), :])
                    for k, s in enumerate(sums)
                )

            found = lax.fori_loop(0, tiles * per, corr, (jnp.zeros((8, 128), F32),) * TAPS)
            for k in range(TAPS):
                gtaps_ref[k : k + 1, lane * 128 : lane * 128 + 128] = jnp.sum(
                    found[k], axis=0, keepdims=True
                )
        progress(conv_at, 1)

        def store(lane, row, base, total):
            gpad[lane, pl.ds(pl.multiple_of(base + REACH, 8), 64), :] = total

        taps_over(padded, vec_ref, store, tiles, True)

    @pl.when((step > conv_at) & (step < mix_at))
    def _():
        at = step - conv_at - 1

        def first(rows):
            spot = pl.ds(pl.multiple_of(at * pitch + REACH + rows.start, 8), ROWS)
            grad = jnp.concatenate([gpad[lane, spot, :] for lane in range(lanes)], axis=1)
            sig = sigmoid(p_ref[rows, right].astype(F32))
            gl = (grad * sig).astype(BF16)
            gr = (grad * p_ref[rows, left].astype(F32) * (sig * (1.0 - sig))).astype(BF16)
            wide_scr[rows, left] = gl
            wide_scr[rows, right] = gr
            vec_acc[0] += fold8(gl.astype(F32))
            vec_acc[1] += fold8(gr.astype(F32))
            e, _ = norm_parts(x2_ref[rows, :])
            low_scr[rows, :] = (e * gain(2) + shift(2)).astype(BF16)

        by_rows(first)
        turned = low_scr[...].T
        wide_acc[...] += dot_nn(turned, wide_scr[...])
        sum_scr[...] = dot_nt(wide_scr[:, left], square_of(middle_ref, 1)) + dot_nt(
            wide_scr[:, right], square_of(middle_ref, 2)
        )

        def second(rows):
            here = pl.ds(pl.multiple_of(at * TILE + rows.start, ROWS), ROWS)
            e, inv = norm_parts(x2_ref[rows, :])
            grad = sum_scr[rows, :]
            vec_acc[2] += fold8(grad * e)
            vec_acc[3] += fold8(grad)
            gx2 = gx3_ref[rows, :] + norm_back(grad, e, inv, gain(2))
            spot = pl.ds(pl.multiple_of(at * pitch + REACH + rows.start, 8), ROWS)
            for lane in range(lanes):
                gpad[lane, spot, :] = gx2[:, lane * 128 : lane * 128 + 128]
            low = gx2.astype(BF16)
            low_scr[rows, :] = low
            vec_acc[4] += fold8(low.astype(F32))

        by_rows(second)
        mixout_acc[...] += dot_tn(gated_ref[...], low_scr[...])
        sum_scr[...] = dot_nt(low_scr[...], square_of(middle_ref, 0))

        def third(rows):
            here = pl.ds(pl.multiple_of(at * TILE + rows.start, ROWS), ROWS)
            grad = sum_scr[rows, :]
            v = v_ref[rows, :].astype(F32)
            sig = sigmoid(v)
            swish = v * sig
            gy = grad * swish
            for lane in range(lanes):
                padded[lane, here, :] = gy[:, lane * 128 : lane * 128 + 128]
            gv_all[here, :] = (
                grad * y_ref[rows, :].astype(F32) * (sig * (1.0 + v - swish))
            ).astype(BF16)


        by_rows(third)

    @pl.when(step == mix_at)
    def _():
        pltpu.make_async_copy(u_ref.at[0], u_tile, u_sem).start()
        store_wide(mid_ref, 0, mixout_acc)
        store_wide(mid_ref, 1, wide_acc)
        wide_acc[...] = jnp.zeros_like(wide_acc)
        for lane in range(lanes):
            skip[lane : lane + 1, :] = vec_ref[17:18, lane * 128 : lane * 128 + 128]
        progress(mix_at, 0)

        def one(lane, _):
            if fused:
                pl.when(lane == lanes // 2)(lambda: progress(mix_at, 1))
            mix_backward(
                lane, u_ref, padded, skip, u_tile, u_sem, power, shifted, weight, flags, ub_ref, state_ref, lags, sums, *mix_scr
            )
            return 0

        lax.fori_loop(0, lanes, one, 0)
        gmap, gdecay = mix_gradients(lags, sums, vec_ref)
        gmap_out[...] = gmap
        gdecay_out[...] = gdecay

    @pl.when(step > mix_at)
    def _():
        at = step - mix_at - 1

        def fourth(rows):
            here = pl.ds(pl.multiple_of(at * TILE + rows.start, ROWS), ROWS)
            gu = jnp.concatenate([padded[lane, here, :] for lane in range(lanes)], axis=1)
            wide_scr[rows, left] = gu.astype(BF16)
            wide_scr[rows, right] = gv_all[here, :]
            e, _ = norm_parts(x1_ref[rows, :])
            low_scr[rows, :] = (e * gain(1) + shift(1)).astype(BF16)

        by_rows(fourth)
        turned = low_scr[...].T
        wide_acc[...] += dot_nn(turned, wide_scr[...])
        sum_scr[...] = dot_nt(wide_scr[:, left], square_of(mixin_ref, 0)) + dot_nt(
            wide_scr[:, right], square_of(mixin_ref, 1)
        )

        def fifth(rows):
            e, inv = norm_parts(x1_ref[rows, :])
            grad = sum_scr[rows, :]
            vec_acc[6] += fold8(grad * e)
            vec_acc[7] += fold8(grad)
            spot = pl.ds(pl.multiple_of(at * pitch + REACH + rows.start, 8), ROWS)
            gx2 = jnp.concatenate([gpad[lane, spot, :] for lane in range(lanes)], axis=1)
            gx1_ref[rows, :] = gx2 + norm_back(grad, e, inv, gain(1))

        by_rows(fifth)

    @pl.when(step == last_step)
    def _():
        store_wide(gin_out, 0, wide_acc)
        for k in range(8):
            gvec_out[k : k + 1, :] = jnp.sum(vec_acc[k], axis=0, keepdims=True)
        gvec_out[5:6, :] = jnp.concatenate([lags[k, 0:1, :] for k in range(lanes)], axis=1)
        if fused:
            progress(last_step, 1)
            for wait in sends:
                wait()


def back(mesh_size, offsets, counts, tiled, wholes, grads=(), collective_id=None):
    fused = mesh_size is not None
    frames, channels = tiled[0].shape
    tiles = frames // TILE
    groups, blocks = channels // PIECE, frames // STRETCH
    late = lambda i, first: jnp.clip(i - first, 0, tiles - 1)
    filling = lambda i: (late(i, 0), 0)
    twice = lambda i: (jnp.where(i < tiles, i, late(i, tiles + 1)), 0)
    mixing = lambda i: (late(i, tiles + 1), 0)
    ending = lambda i: (late(i, 2 * tiles + 2), 0)
    maps = [filling, filling, twice] + [mixing] * 5 + [ending]
    state = jax.ShapeDtypeStruct((STATES, channels), F32)
    bf16 = lambda *shape: jax.ShapeDtypeStruct(shape, BF16)
    shapes = [
        jax.ShapeDtypeStruct((frames, channels), F32),
        bf16(groups, 2, PIECE, WIDTH),
        jax.ShapeDtypeStruct((8, channels), F32),
        jax.ShapeDtypeStruct((16, channels), F32),
        state,
        state,
    ]
    pad = pltpu.VMEM((channels // 128, tiles * (TILE + 2 * REACH), 128), F32)
    scratch = [
        pltpu.VMEM((channels, 2 * channels), F32),
        pltpu.VMEM((channels, channels), F32),
        pltpu.VMEM((8, 8, channels), F32),
        pltpu.VMEM((TILE, channels), BF16),
        pltpu.VMEM((TILE, 2 * channels), BF16),
        pltpu.VMEM((TILE, channels), F32),
        pad,
        pad,
        pltpu.VMEM((frames, channels), BF16),
        pltpu.VMEM((channels // 128, STRETCH, 128), F32),
        pltpu.VMEM((2, groups, SPREAD), F32),
        pltpu.VMEM((8, 128), F32),
        pltpu.VMEM((frames, 128), F32),
        pltpu.SemaphoreType.DMA(()),
        pltpu.VMEM((2, STRETCH, blocks, 128), F32),
        pltpu.VMEM((8, blocks, STRETCH * PIECE), BF16),
        pltpu.VMEM((8, blocks, STRETCH * PIECE), F32),
        pltpu.VMEM((2, STRETCH * PIECE, SPREAD), BF16),
        pltpu.VMEM((2, STRETCH * PIECE, STRETCH * PIECE), BF16),
        pltpu.VMEM((2, 3 * blocks, STRETCH * PIECE), BF16),
        pltpu.VMEM((2, 3 * blocks, SPREAD), F32),
        pltpu.VMEM((2, blocks, SPREAD), F32),
    ]
    if fused:
        counts_of = [grads[0].shape[-3], 3]
        shapes += [jax.ShapeDtypeStruct((k, PIECE, WIDTH), F32) for k in counts_of]
        scratch += [pltpu.VMEM(block_layout(*mesh_size) + (3, PIECE, WIDTH), BF16)]
        scratch += block_scratch(*mesh_size, counts_of, (PIECE, WIDTH))
        scratch += block_sems(*mesh_size, 2)
    else:
        shapes.append(bf16(groups, 3, PIECE, WIDTH))
    return pl.pallas_call(
        partial(back_kernel, mesh_size),
        grid=(3 * tiles + 2,),
        in_specs=[SMEM_SPEC, SMEM_SPEC]
        + [pl.BlockSpec((TILE, a.shape[1]), index) for a, index in zip(tiled, maps)]
        + [HBM_SPEC]
        + [whole(a.shape) for a in wholes[1:]]
        + [HBM_SPEC] * len(grads),
        out_specs=[pl.BlockSpec((TILE, channels), ending)] + [whole(s.shape) for s in shapes[1:]],
        out_shape=shapes,
        scratch_shapes=scratch,
        compiler_params=params(collective_id),
        name="back",
    )(offsets, counts, *tiled, *wholes, *grads)


def small_gradients(out, gvec1, gvec2, gvec3, gtaps, gmap, gdecay, table_ref):
    out[...] = jnp.zeros_like(out)
    gains = {1: (gvec2, 6), 2: (gvec2, 2), 3: (gvec1, 3), 4: (gvec1, 0), 5: (gvec1, 6)}
    shifts = {1: (gvec2, 7), 2: (gvec2, 3), 3: (gvec1, 4), 4: (gvec1, 1), 5: (gvec1, 7)}
    shifts.update({6: (gvec3, 0), 7: (gvec1, 2), 8: (gvec2, 4), 9: (gvec2, 0), 10: (gvec2, 1)})
    shifts.update({11: (gvec2, 5), 12: (gvec1, 5)})
    for at, (ref, row) in gains.items():
        out[at : at + 1, :] = ref[row : row + 1, :]
    for at, (ref, row) in shifts.items():
        out[6 + at : 7 + at, :] = ref[row : row + 1, :]
    out[TAP_ROW : TAP_ROW + TAPS, :] = gtaps[:TAPS, :]
    log_decay, decay, root, maps_in, maps_out = state_terms(table_ref)
    both = gmap[...] * root
    out[MAP_IN:MAP_OUT, :] = both * maps_out
    out[MAP_OUT:TABLE, :] = both * maps_in
    turn = (1.0 - root * root) / root
    out[RATE:MAP_IN, :] = log_decay * (
        gdecay[...] * decay - gmap[...] * maps_in * maps_out * turn
    )


def store_cols(out, at, value):
    groups = value.shape[0] // PIECE
    out[:, at] = value.reshape((groups, PIECE, WIDTH))


def tail_kernel(mesh_size, *refs):
    fused = mesh_size is not None
    refs = list(refs)
    take = lambda count: [refs.pop(0) for _ in range(count)]
    x_ref, h_ref, gx1_ref, up_ref, up2_ref, down_ref, table_ref = take(7)
    hidden = 4 * WIDTH
    if fused:
        gvec1, gvec2, gtaps, gmap, gdecay, gbias1 = take(6)
        sources = take(1)
        gx_ref, last_out = take(2)
        reduced = take(4)
    else:
        gx_ref, gvec_out, gbias_out, up_out, down_out = take(5)
    turn_scr, grad_scr, gh_scr, vec_acc, bias_scr = take(5)
    step = pl.program_id(0)
    frames, channels = x_ref.shape
    chunks = hidden // WIDTH
    tiles = frames // TILE
    first_b, first_c = 1 + chunks, 1 + 2 * chunks
    schedule = {}
    if fused:
        n_dp, n_fs = mesh_size
        down_src, left_src, right_src, small_scr, gvec3 = take(5)
        dp, fs = lax.axis_index("dp"), lax.axis_index("fsdp")
        place = Place(dp, fs, n_dp, n_fs)
        scratch = take(4 * (2 + place.count))
        sems = take(3)
        swap = take(4)
        down_out = flat_groups(down_src)
        halves = (flat_groups(left_src), flat_groups(right_src))

        def emit(chunk, total):
            reduced[chunk][...] = total

        plans, sends = block_scatter(
            place, sources + [down_src, left_src, right_src], emit, scratch, *sems
        )
        begins = [
            (0, 2, 4, 7, first_c),
            (first_b, first_b + 1, first_b + 3, first_c + 1, first_c + tiles),
            (first_b + 2, first_c, first_c + 1, first_c + 2, first_c + tiles),
            (first_c, first_c + 1, first_c + 2, first_c + tiles, first_c + tiles),
        ]
        for chunk, steps in enumerate(begins):
            for stage, at in enumerate(steps):
                schedule.setdefault(at, []).append((stage, chunk))
    last_step = first_c + tiles - 1

    def progress(at):
        for stage, chunk in sorted(schedule.get(at, [])):
            plans[chunk][stage]()

    @pl.when(step == 0)
    def _():
        if fused:
            greet(dp, fs, n_dp, n_fs)
        progress(0)
        vec_acc[...] = jnp.zeros_like(vec_acc)

        def first(rows):
            e, _ = norm_parts(x_ref[rows, :].astype(F32))
            low = (e * table_ref[0:1, :] + table_ref[6:7, :]).astype(BF16)
            turn_scr[:, rows] = low.T
            grad = (0.5 * gx1_ref[rows, :]).astype(BF16)
            grad_scr[rows, :] = grad
            vec_acc[0] += fold8(grad.astype(F32))

        by_rows(first, frames)

    if fused:
        for at in range(1, last_step + 1):
            if at in schedule and at != first_c:

                @pl.when(step == at)
                def _(at=at):
                    progress(at)

    @pl.when((step >= 1) & (step < first_b))
    def _():
        h = h_ref[...].astype(F32)
        active = (h * sigmoid(h)).astype(BF16)
        value = dot_tn(active, grad_scr[...]).astype(BF16)
        groups = WIDTH // (4 * PIECE)
        down_out[pl.ds((step - 1) * groups, groups)] = value.reshape((groups, 4, PIECE, WIDTH))

    def second_half(c, store):
        cols = columns(c, WIDTH)
        h = h_ref[...].astype(F32)
        sig = sigmoid(h)
        gate = dot_nt(grad_scr[...], rows_of(down_ref, 0, c))
        grad_h = (gate * (sig * (1.0 + h * (1.0 - sig)))).astype(BF16)
        gh_scr[:, cols] = grad_h
        sums = jnp.sum(fold8(grad_h.astype(F32)), axis=0, keepdims=True)
        bias_scr[pl.ds(2 * c, 1), :] = sums[:, :CHUNK]
        bias_scr[pl.ds(2 * c + 1, 1), :] = sums[:, CHUNK:]
        store(dot_nn(turn_scr[...], grad_h).astype(BF16))

    if fused:
        for half in range(2):
            begin = first_b + half * (chunks // 2)

            @pl.when((step >= begin) & (step < begin + chunks // 2))
            def _(half=half, begin=begin):
                def store(value):
                    store_cols(halves[half], step - begin, value)

                second_half(step - first_b, store)

    else:

        @pl.when((step >= first_b) & (step < first_c))
        def _():
            def store(value):
                store_cols(up_out, step - first_b, value)

            second_half(step - first_b, store)

    if fused:

        @pl.when(step == first_c)
        def _():
            gvec3[0:1, :] = jnp.sum(vec_acc[0], axis=0, keepdims=True)
            small_gradients(small_scr, gvec1, gvec2, gvec3, gtaps, gmap, gdecay, table_ref)
            narrow = small_scr[...].T.astype(BF16)
            devices = n_dp * n_fs
            small_out = halves[1]
            small_out[:, 2, :, :CHUNK] = narrow.reshape((devices, PIECE, CHUNK))
            for c in range(8):
                bias_scr[8 + c : 9 + c, :] = gbias1[0:1, c * CHUNK : c * CHUNK + CHUNK]
            bias = bias_scr[...].astype(BF16)
            small_out[:, 2, :, CHUNK:] = jnp.broadcast_to(bias[None], (devices, PIECE, CHUNK))
            progress(first_c)

    @pl.when(step >= first_c)
    def _():
        tile = step - first_c
        whole_tile = pl.ds(pl.multiple_of(tile * TILE, TILE), TILE)
        total = dot_nt(gh_scr[whole_tile, :WIDTH], square_of(up_ref, 1))
        later = [square_of(up_ref, 2), square_of(up2_ref, 0), square_of(up2_ref, 1)]
        for k in range(1, hidden // WIDTH):
            cols = slice(k * WIDTH, k * WIDTH + WIDTH)
            total = total + dot_nt(gh_scr[whole_tile, cols], later[k - 1])
        gx_ref[...] = total

        def second(rows):
            here = pl.ds(pl.multiple_of(tile * TILE + rows.start, ROWS), ROWS)
            e, inv = norm_parts(x_ref[here, :].astype(F32))
            grad = gx_ref[rows, :]
            vec_acc[1] += fold8(grad * e)
            vec_acc[2] += fold8(grad)
            gx_ref[rows, :] = gx1_ref[here, :] + norm_back(grad, e, inv, table_ref[0:1, :])

        by_rows(second)

    @pl.when(step == last_step)
    def _():
        if fused:
            last_out[...] = jnp.zeros_like(last_out)
            for k in range(2):
                last_out[k : k + 1, :] = jnp.sum(vec_acc[1 + k], axis=0, keepdims=True)
            ends = sorted(schedule.get(last_step + 1, []))

            def between():
                for stage, chunk in ends:
                    plans[chunk][stage]()

            last_out[...] = sum_over(last_out[...], dp, fs, n_dp, n_fs, *swap, between=between)
            for wait in sends:
                wait()
        else:
            gvec_out[...] = jnp.zeros_like(gvec_out)
            for k in range(3):
                gvec_out[k : k + 1, :] = jnp.sum(vec_acc[k], axis=0, keepdims=True)
            gbias_out[...] = bias_scr[...]


def tail(mesh_size, x, h, gx1, up, up2, down, table, others=(), grads=(), collective_id=None):
    fused = mesh_size is not None
    frames, channels = x.shape
    hidden = h.shape[1]
    tiles, chunks = frames // TILE, hidden // WIDTH
    first_b, first_c = 1 + chunks, 1 + 2 * chunks
    place = lambda i: jnp.where(
        i < first_b, jnp.maximum(i - 1, 0), jnp.minimum(i - first_b, chunks - 1)
    )
    shapes = [jax.ShapeDtypeStruct((frames, channels), F32)]
    scratch = [
        pltpu.VMEM((channels, frames), BF16),
        pltpu.VMEM((frames, channels), BF16),
        pltpu.VMEM((frames, hidden), BF16),
        pltpu.VMEM((8, 8, channels), F32),
        pltpu.VMEM((16, CHUNK), F32),
    ]
    if fused:
        own = [4, 2, 3]
        counts = [g.shape[-3] for g in grads] + own
        shapes.append(jax.ShapeDtypeStruct((8, channels), F32))
        shapes += [jax.ShapeDtypeStruct((k, PIECE, WIDTH), F32) for k in counts]
        layout = block_layout(*mesh_size)
        scratch += [pltpu.VMEM(layout + (k, PIECE, WIDTH), BF16) for k in own]
        scratch += [pltpu.VMEM((256, channels), F32), pltpu.VMEM((8, channels), F32)]
        scratch += block_scratch(*mesh_size, counts, (PIECE, WIDTH))
        scratch += block_sems(*mesh_size, len(counts))
        scratch += swap_scratch(*mesh_size, channels)
    else:
        shapes += [
            jax.ShapeDtypeStruct((8, channels), F32),
            jax.ShapeDtypeStruct((16, CHUNK), F32),
            jax.ShapeDtypeStruct((channels // PIECE, 4, PIECE, WIDTH), BF16),
            jax.ShapeDtypeStruct((channels // PIECE, 4, PIECE, WIDTH), BF16),
        ]
    return pl.pallas_call(
        partial(tail_kernel, mesh_size),
        grid=(first_c + tiles,),
        in_specs=[whole(x.shape), pl.BlockSpec((frames, WIDTH), lambda i: (0, place(i)))]
        + [whole(a.shape) for a in (gx1, up, up2, down, table) + tuple(others)]
        + [pl.BlockSpec(memory_space=pltpu.HBM)] * len(grads),
        out_specs=[
            pl.BlockSpec((TILE, channels), lambda i: (jnp.maximum(i - first_c, 0), 0))
        ]
        + [whole(s.shape) for s in shapes[1:]],
        out_shape=shapes,
        scratch_shapes=scratch,
        compiler_params=params(collective_id),
        name="tail",
    )(x, h, gx1, up, up2, down, table, *others, *grads)


def unpack_kernel(
    place_ref,
    second_ref,
    middle_ref,
    mixin_ref,
    down_ref,
    left_ref,
    right_ref,
    last_ref,
    up_out,
    down_out,
    bias_out,
    mixin_out,
    mixout_out,
    convin_out,
    convout_out,
    convbias_out,
    rate_out,
    map_out,
    taps_out,
    gains_out,
    shifts_out,
):
    mine = place_ref[0]
    for k in range(4):
        cols = slice(k * WIDTH, k * WIDTH + WIDTH)
        rows = slice(k * PIECE, k * PIECE + PIECE)
        up_out[0, :, cols] = (left_ref if k < 2 else right_ref)[k % 2]
        up_out[1, :, cols] = second_ref[1 + k]
        down_out[0, rows, :] = down_ref[k]
        down_out[1, rows, :] = second_ref[5 + k]
    convout_out[...] = second_ref[0]
    mixout_out[...] = middle_ref[0]
    for k in range(2):
        cols = slice(k * WIDTH, k * WIDTH + WIDTH)
        mixin_out[:, cols] = mixin_ref[k]
        convin_out[:, cols] = middle_ref[1 + k]
    count = bias_out.shape[1]
    row = (mine * count) // CHUNK
    inner = mine * count - row * CHUNK
    for layer in range(2):
        line = right_ref[2, pl.ds(8 * layer + row, 1), CHUNK:]
        line = pltpu.roll(jnp.broadcast_to(line, (8, CHUNK)), CHUNK - inner, 1)
        bias_out[layer : layer + 1, :] = line[0:1, :count]
    channels = last_ref.shape[1]
    first = pltpu.roll(last_ref[...], channels - mine * PIECE, 1)[:, :PIECE]
    small = right_ref[2, :, :CHUNK]
    turned = small.T
    gains_out[...] = turned[0:6, :]
    gains_out[0:1, :] = first[0:1, :]
    shifts_out[...] = turned[6:18, :]
    shifts_out[0:1, :] = first[1:2, :]
    convbias_out[...] = turned[18:19, :]
    taps_out[...] = turned[TAP_ROW : TAP_ROW + TAPS, :]
    rate_out[...] = small[:, RATE:MAP_IN]
    map_out[0] = small[:, MAP_IN:MAP_OUT]
    map_out[1] = small[:, MAP_OUT:TABLE]


def unpack(mine, arrays, hidden):
    channels = arrays[-1].shape[1]
    devices = channels // PIECE
    f32 = lambda *shape: jax.ShapeDtypeStruct(shape, F32)
    vmem = pl.BlockSpec(memory_space=pltpu.VMEM)
    return pl.pallas_call(
        unpack_kernel,
        in_specs=[SMEM_SPEC] + [vmem] * len(arrays),
        out_specs=[vmem] * 13,
        out_shape=[
            f32(2, PIECE, hidden),
            f32(2, hidden // devices, channels),
            f32(2, hidden // devices),
            f32(PIECE, 2 * WIDTH),
            f32(PIECE, WIDTH),
            f32(PIECE, 2 * WIDTH),
            f32(PIECE, WIDTH),
            f32(1, PIECE),
            f32(PIECE, STATES),
            f32(2, PIECE, STATES),
            f32(TAPS, PIECE),
            f32(6, PIECE),
            f32(12, PIECE),
        ],
        name="unpack",
    )(mine, *arrays)


def pack_table(gains, shifts, conv_bias, taps, rate, maps):
    channels = gains.shape[1]
    blank = lambda rows: jnp.zeros((rows, channels), gains.dtype)
    parts = [gains, shifts, conv_bias[None], blank(TAP_ROW - 19), taps, blank(RATE - TAP_ROW - TAPS)]
    parts += [rate, maps[0], maps[1], blank(256 - TABLE)]
    return jnp.concatenate(parts, axis=0).T


def pack_bias(bias, place):
    layers, count = bias.shape
    hidden = 16 * CHUNK // layers
    wide = lax.dynamic_update_slice(
        jnp.zeros((layers, hidden), bias.dtype), bias, (0, place * count)
    )
    return wide.reshape((16, CHUNK))


def unpack_table(table):
    return (
        table[0:6],
        table[6:18],
        table[18],
        table[TAP_ROW : TAP_ROW + TAPS],
        table[RATE:MAP_IN],
        jnp.stack([table[MAP_IN:MAP_OUT], table[MAP_OUT:TABLE]]),
    )


def on_device(
    n_dp,
    n_fs,
    frames,
    seq_lengths,
    seq_offsets,
    seq_counts,
    ffn_up,
    ffn_down,
    ffn_bias_up,
    mix_in,
    mix_out,
    conv_in,
    conv_out,
    conv_out_bias,
    ssm_rate,
    ssm_map,
    conv_kernel,
    gains,
    shifts,
    cotangent,
):
    devices = n_dp * n_fs
    mine = lax.axis_index("dp") * n_fs + lax.axis_index("fsdp")
    frames_dev, channels = frames.shape
    hidden = ffn_up.shape[2]
    if channels // devices == PIECE:
        size = (n_dp, n_fs)
        small = [
            ffn_bias_up,
            gains,
            shifts,
            conv_out_bias[None],
            conv_kernel,
            ssm_rate.T,
            ssm_map.transpose((0, 2, 1)),
        ]
        weights = [ffn_up, ffn_down, mix_in, mix_out, conv_in, conv_out]
        made = front(size, seq_offsets, seq_counts, frames, small, weights, hidden, 1)
        h0, x1, v, y, gated, x2, p, u, w, stat, table, bias, *mixing = made[:17]
        groups = lambda g: g.reshape((devices,) + g.shape[-3:])
        places = lambda g: g.reshape(block_layout(n_dp, n_fs) + g.shape[1:])
        first, extra, second, third, mixed, fourth = [groups(g) for g in made[17:]]
        result, gx3, gnb, grads, gbias1, gvec1, stat = middle(
            size, x2, w, cotangent, fourth, bias, table, stat, hidden, 2
        )
        gx1, grads2, gvec2, gtaps, gmap, gdecay, reduced, reduced2 = back(
            size,
            seq_offsets,
            seq_counts,
            [w, gnb, p, x2, gx3, gated, y, v, x1],
            [u] + mixing + [third, mixed, table, stat],
            (places(grads),),
            3,
        )
        others = (gvec1, gvec2, gtaps, gmap, gdecay, gbias1)
        gx, last, *late = tail(
            size, frames, h0, gx1, first, extra, second, table, others, (places(grads2),), 4
        )
        made = unpack(mine.reshape((1,)), [reduced, reduced2] + late + [last], hidden)
        made = list(made)
        made[7] = made[7].reshape((-1,))
        made[8] = made[8].T
        made[9] = made[9].transpose((0, 2, 1))
        return (result, gx) + tuple(made)

    small = pack_table(gains, shifts, conv_out_bias, conv_kernel, ssm_rate, ssm_map)
    got = gather_all(
        n_dp,
        n_fs,
        [
            small[None],
            pack_bias(ffn_bias_up, mine)[None],
            ffn_up,
            ffn_down,
            mix_in[None],
            mix_out[None],
            conv_in[None],
            conv_out[None],
        ],
        1,
    )
    matrix = lambda g: g.reshape((-1, g.shape[-1]))
    table, _, up0, up1, down0, down1, mixin, mixout, convin, convout = [matrix(g) for g in got]
    table = table.astype(F32).T[:TABLE]
    bias = jnp.sum(got[1].astype(F32), axis=0)
    group_count = channels // PIECE
    cut = lambda g: g.reshape((group_count, PIECE, -1, WIDTH)).transpose((0, 2, 1, 3))
    tall = lambda g: g.reshape((group_count, -1, PIECE, WIDTH))
    join = lambda g: g.transpose((0, 2, 1, 3)).reshape((channels, -1))
    blank = jnp.pad(matrix(got[0]), ((0, 0), (0, WIDTH - 256))).reshape((group_count, 1, PIECE, WIDTH))
    extra = cut(up0)
    first, extra = jnp.concatenate([blank, extra[:, :2]], axis=1), extra[:, 2:]
    third = cut(mixin)
    mixed = jnp.concatenate([cut(mixout), cut(convin)], axis=1)
    fourth = jnp.concatenate([cut(convout), cut(up1), tall(down1)], axis=1)
    made = front(
        None, seq_offsets, seq_counts, frames, [table, bias], [first, extra, tall(down0), third, mixed], hidden
    )
    h0, x1, v, y, gated, x2, p, u, w, stat, table, bias, *mixing = made
    pool = exchange(n_dp, n_fs, stat, frames_dev, 2, pool_kernel)
    scale = lax.rsqrt(pool[1:2] / (frames_dev * devices) + EPSILON)
    stat = jnp.concatenate([pool[0:1], scale, jnp.zeros((6, channels), F32)])
    result, gx3, gnb, grads, gbias1, gvec1, stat = middle(
        None, x2, w, cotangent, fourth, bias, table, stat, hidden
    )
    sums = exchange(n_dp, n_fs, gvec1, 1, 4, total_kernel)[6:8]
    sums = sums * (table[5:6] / (frames_dev * devices))
    stat = jnp.concatenate([stat[0:2], sums[1:2], sums[0:1], stat[4:8]])
    gx1, grads2, gvec2, gtaps, gmap, gdecay, grads3 = back(
        None,
        seq_offsets,
        seq_counts,
        [w, gnb, p, x2, gx3, gated, y, v, x1],
        [u] + mixing + [third, mixed, table, stat],
    )
    gx, gvec3, gbias0, gup0, gdown0 = tail(None, frames, h0, gx1, first, extra, tall(down0), table)

    def weights_of(log_rate, maps):
        log_decay = -jnp.exp(log_rate)
        root = jnp.sqrt(-jnp.expm1(2.0 * log_decay))
        return jnp.exp(log_decay), maps[0] * root * maps[1]

    rate, maps = unpack_table(table)[4:]
    rate_grad, map_grad = jax.vjp(weights_of, rate, maps)[1]((gdecay, gmap))
    gain_grad = jnp.stack([gvec3[1], gvec2[6], gvec2[2], gvec1[3], gvec1[0], gvec1[6]])
    rows = [gvec3[2], gvec2[7], gvec2[3], gvec1[4], gvec1[1], gvec1[7], gvec3[0], gvec1[2]]
    rows += [gvec2[4], gvec2[0], gvec2[1], gvec2[5]]
    small_grad = pack_table(
        gain_grad, jnp.stack(rows), gvec1[5], gtaps[:TAPS], rate_grad, map_grad
    )
    bias_grad = jnp.concatenate([gbias0[:8], gbias1[0].reshape((8, CHUNK))])
    wide = lambda g: g.reshape((devices, g.shape[0] // devices, g.shape[1]))
    reduced = scatter_all(
        n_dp,
        n_fs,
        [
            wide(join(grads[:, 1:5])),
            wide(matrix(grads[:, 5:9])),
            wide(join(grads[:, 0:1])),
            wide(join(grads3[:, 1:3])),
            wide(join(grads3[:, 0:1])),
            wide(join(grads2[:, 0:2])),
            wide(join(gup0)),
            wide(matrix(gdown0)),
            wide(small_grad.astype(BF16)),
            jnp.broadcast_to(bias_grad.astype(BF16), (devices, PIECE, CHUNK)),
        ],
        5,
    )
    gains_grad, shifts_grad, conv_bias_grad, taps_grad, rate_grad, map_grad = unpack_table(
        reduced[8].T
    )
    bias_grad = reduced[9].reshape((2, -1))
    count = bias_grad.shape[1] // devices
    bias_grad = lax.dynamic_slice(bias_grad, (0, mine * count), (2, count))
    return (
        result,
        gx,
        jnp.stack([reduced[6], reduced[0]]),
        jnp.stack([reduced[7], reduced[1]]),
        bias_grad,
        reduced[5],
        reduced[4],
        reduced[3],
        reduced[2],
        conv_bias_grad,
        rate_grad,
        map_grad,
        taps_grad,
        gains_grad,
        shifts_grad,
    )


def solution(mesh):
    both = ("dp", "fsdp")
    row, row1 = P(both, None), P(both)
    col, col3, mid = P(None, both), P(None, None, both), P(None, both, None)
    in_specs = (
        row,
        row,
        row,
        row1,
        mid,
        mid,
        col,
        row,
        row,
        row,
        row,
        row1,
        col,
        col3,
        col,
        col,
        col,
        row,
    )
    out_specs = (row, row, mid, mid, col, row, row, row, row, row1, col, col3, col, col, col)
    return jax.shard_map(
        partial(on_device, mesh.shape["dp"], mesh.shape["fsdp"]),
        mesh=mesh,
        in_specs=in_specs,
        out_specs=out_specs,
        check_vma=False,
    )
```

```python
import itertools
from functools import partial

import jax
import jax.numpy as jnp
from jax import lax
from jax.experimental import pallas as pl
from jax.experimental.pallas import tpu as pltpu
from jax.sharding import PartitionSpec as P

MESH = pl.DeviceIdType.MESH
BF16 = jnp.bfloat16
F32 = jnp.float32


def flip(index, bit):
    return index + bit * (1 - 2 * lax.rem(lax.div(index, bit), 2))


def flip_all(index, bits):
    for bit in bits:
        index = flip(index, bit)
    return index


def combos(bits):
    found = [()]
    for bit in bits:
        found = found + [entry + (bit,) for entry in found]
    return found


def plan_bits(n_dp):
    bits, bit = [], 2
    while bit < n_dp:
        bits.append(bit)
        bit *= 2
    return tuple(bits)


def greet(dp, fs, n_dp, n_fs):
    barrier = pltpu.get_barrier_semaphore()
    for step in range(1, n_dp):
        pl.semaphore_signal(
            barrier, inc=1, device_id=(lax.rem(dp + step, n_dp), fs), device_id_type=MESH
        )
    for step in range(1, n_fs):
        pl.semaphore_signal(
            barrier, inc=1, device_id=(dp, lax.rem(fs + step, n_fs)), device_id_type=MESH
        )
    pl.semaphore_wait(barrier, n_dp + n_fs - 2)


def gather_plan(dp, fs, n_dp, n_fs, sources, outs, send_sem, recv_sem, local_sem):
    bits = plan_bits(n_dp)
    orders = (bits, bits[::-1])
    half = n_fs // 2
    sends = []

    def stages(chunk):
        src, out = sources[chunk], outs[chunk]
        slots = itertools.count()

        def zone(where, part):
            if part is None:
                return out.at[pl.ds(where * n_fs, n_fs)]
            return out.at[pl.ds(where * n_fs + part * half, half)]

        def remote(slot, view_from, view_to, device):
            return pltpu.make_async_remote_copy(
                src_ref=view_from,
                dst_ref=view_to,
                send_sem=send_sem.at[chunk, slot],
                recv_sem=recv_sem.at[chunk, slot],
                device_id=device,
                device_id_type=MESH,
            )

        def launch(make):
            make().start()
            sends.append(lambda: make().wait_send())

        z_slots = [next(slots) for _ in range(1, n_fs)]

        def own_copy():
            return pltpu.make_async_copy(src, out.at[dp * n_fs + fs], local_sem.at[chunk])

        def start():
            own_copy().start()
            for step in range(1, n_fs):
                launch(
                    lambda step=step: remote(
                        z_slots[step - 1],
                        src,
                        out.at[dp * n_fs + fs],
                        (dp, lax.rem(fs + step, n_fs)),
                    )
                )

        def wait_z():
            own_copy().wait()
            for step in range(1, n_fs):
                origin = dp * n_fs + lax.rem(fs + n_fs - step, n_fs)
                remote(z_slots[step - 1], src, out.at[origin], (dp, fs)).wait_recv()

        steps, before = [start], wait_z
        for depth in range(len(bits)):
            plan = []
            for part, order in enumerate(orders):
                for entry in combos(order[:depth]):
                    plan.append((next(slots), part, order[depth], entry))

            def view(slot, part, bit, entry, arrived):
                where = flip_all(flip(dp, bit) if arrived else dp, entry)
                return remote(slot, zone(where, part), zone(where, part), (flip(dp, bit), fs))

            def go(plan=plan, before=before, view=view):
                before()
                for item in plan:
                    launch(lambda item=item: view(*item, False))

            def arrive(plan=plan, view=view):
                for item in plan:
                    view(*item, True).wait_recv()

            steps.append(go)
            before = arrive
        last = [(next(slots), entry) for entry in combos(bits)]

        def across(slot, entry, arrived):
            where = flip_all(flip(dp, 1) if arrived else dp, entry)
            return remote(slot, zone(where, None), zone(where, None), (flip(dp, 1), fs))

        def cross(before=before):
            before()
            for item in last:
                launch(lambda item=item: across(*item, False))

        def finish():
            for item in last:
                across(*item, True).wait_recv()

        return steps + [cross, finish]

    return [stages(chunk) for chunk in range(len(outs))], sends


def waves(plans):
    depth = len(plans[0])
    out = []
    for wave in range(len(plans) + depth - 1):
        out.append(
            [plans[c][wave - c] for c in range(len(plans)) if 0 <= wave - c < depth]
        )
    return out


def gather_kernel(n_dp, n_fs, layers, *refs):
    n_in = len(layers)
    n_out = sum(layers)
    ins, outs = refs[:n_in], refs[n_in : n_in + n_out]
    send_sem, recv_sem, local_sem = refs[n_in + n_out :]
    sources = []
    for ref, count in zip(ins, layers):
        sources += [ref.at[layer] for layer in range(count)]
    dp, fs = lax.axis_index("dp"), lax.axis_index("fsdp")
    greet(dp, fs, n_dp, n_fs)
    plans, sends = gather_plan(dp, fs, n_dp, n_fs, sources, outs, send_sem, recv_sem, local_sem)
    for wave in waves(plans):
        for stage in wave:
            stage()
    for wait in sends:
        wait()


def slot_count(n_dp, n_fs):
    nb = len(plan_bits(n_dp))
    return n_fs - 1 + 2 * (2**nb - 1) + 2**nb


def gather_all(n_dp, n_fs, arrays, collective_id):
    layers = tuple(a.shape[0] for a in arrays)
    outs = []
    for a in arrays:
        outs += [jax.ShapeDtypeStruct((n_dp * n_fs,) + a.shape[1:], a.dtype)] * a.shape[0]
    count = slot_count(n_dp, n_fs)
    return pl.pallas_call(
        partial(gather_kernel, n_dp, n_fs, layers),
        out_shape=outs,
        in_specs=[pl.BlockSpec(memory_space=pltpu.HBM)] * len(arrays),
        out_specs=[pl.BlockSpec(memory_space=pltpu.HBM)] * len(outs),
        scratch_shapes=[
            pltpu.SemaphoreType.DMA((len(outs), count)),
            pltpu.SemaphoreType.DMA((len(outs), count)),
            pltpu.SemaphoreType.DMA((len(outs),)),
        ],
        compiler_params=pltpu.CompilerParams(collective_id=collective_id, has_side_effects=True),
        name="gather_parameters",
    )(*arrays)


def scatter_plan(dp, fs, n_dp, n_fs, ins, emit, scratch, send_sem, recv_sem, local_sem, first=0):
    bits = plan_bits(n_dp)
    orders = (bits[::-1], bits)
    half = n_fs // 2
    index = {entry: at for at, entry in enumerate(combos(bits))}
    sends = []

    def add_into(kept, other):
        def body(at, _):
            kept[at] = (kept[at].astype(F32) + other[at].astype(F32)).astype(BF16)
            return 0

        lax.fori_loop(0, kept.shape[0], body, 0)

    def stages(chunk):
        src = ins[chunk]
        cross_in, own, later, last = scratch[4 * chunk : 4 * chunk + 4]
        slots = itertools.count()

        def remote(slot, view_from, view_to, device):
            return pltpu.make_async_remote_copy(
                src_ref=view_from,
                dst_ref=view_to,
                send_sem=send_sem.at[first + chunk, slot],
                recv_sem=recv_sem.at[first + chunk, slot],
                device_id=device,
                device_id_type=MESH,
            )

        def launch(make):
            make().start()
            sends.append(lambda: make().wait_send())

        def zone(entry, crossed):
            return src.at[pl.ds(flip_all(flip(dp, 1) if crossed else dp, entry) * n_fs, n_fs)]

        pieces = [(next(slots), entry, index[entry]) for entry in combos(bits)]

        def load(entry, at):
            return pltpu.make_async_copy(
                zone(entry, False), own.at[at], local_sem.at[first + chunk, at]
            )

        def across(slot, entry, at):
            return remote(slot, zone(entry, True), cross_in.at[at], (flip(dp, 1), fs))

        def start():
            for item in pieces:
                launch(lambda item=item: across(*item))
            for _, entry, at in pieces:
                load(entry, at).start()

        def fold_cross():
            for slot, entry, at in pieces:
                load(entry, at).wait()
                across(slot, entry, at).wait_recv()
                add_into(own.at[at], cross_in.at[at])

        steps, before = [start], fold_cross
        used = 0
        for depth in range(len(bits)):
            plan = []
            for part, order in enumerate(orders):
                bit, gone = order[depth], order[:depth]
                for entry in combos(bits):
                    if not (set(entry) & set(gone)) and bit not in entry:
                        away = tuple(sorted(entry + (bit,)))
                        plan.append((next(slots), part, bit, index[away], index[entry], used))
                        used += 1

            def move(slot, part, bit, away, kept, place):
                return remote(
                    slot,
                    own.at[away, pl.ds(part * half, half)],
                    later.at[place],
                    (flip(dp, bit), fs),
                )

            def go(plan=plan, before=before, move=move):
                before()
                for item in plan:
                    launch(lambda item=item: move(*item))

            def fold(plan=plan, move=move):
                for item in plan:
                    move(*item).wait_recv()
                    _, part, _, _, kept, place = item
                    add_into(own.at[kept, pl.ds(part * half, half)], later.at[place])

            steps.append(go)
            before = fold
        z_slots = [next(slots) for _ in range(1, n_fs)]

        def along(step):
            to = lax.rem(fs + step, n_fs)
            return remote(z_slots[step - 1], own.at[0, to], last.at[step - 1], (dp, to))

        def spread(before=before):
            before()
            for step in range(1, n_fs):
                launch(lambda step=step: along(step))

        def finish():
            total = own[0, fs].astype(F32)
            for step in range(1, n_fs):
                along(step).wait_recv()
                total = total + last[step - 1].astype(F32)
            emit(chunk, total)

        return steps + [spread, finish]

    return [stages(chunk) for chunk in range(len(ins))], sends


def scatter_scratch(n_dp, n_fs, tails):
    pieces = 2 ** len(plan_bits(n_dp))
    scratch = []
    for tail in tails:
        scratch += [
            pltpu.VMEM((pieces, n_fs) + tail, BF16),
            pltpu.VMEM((pieces, n_fs) + tail, BF16),
            pltpu.VMEM((2 * (pieces - 1), n_fs // 2) + tail, BF16),
            pltpu.VMEM((n_fs - 1,) + tail, BF16),
        ]
    return scratch


def scatter_sems(n_dp, n_fs, chunks):
    count = slot_count(n_dp, n_fs)
    return [
        pltpu.SemaphoreType.DMA((chunks, count)),
        pltpu.SemaphoreType.DMA((chunks, count)),
        pltpu.SemaphoreType.DMA((chunks, 2 ** len(plan_bits(n_dp)))),
    ]


def scatter_kernel(n_dp, n_fs, n_chunks, *refs):
    ins, outs = refs[:n_chunks], refs[n_chunks : 2 * n_chunks]
    scratch = refs[2 * n_chunks : 6 * n_chunks]
    dp, fs = lax.axis_index("dp"), lax.axis_index("fsdp")
    greet(dp, fs, n_dp, n_fs)

    def emit(chunk, total):
        outs[chunk][...] = total

    plans, sends = scatter_plan(dp, fs, n_dp, n_fs, ins, emit, scratch, *refs[6 * n_chunks :])
    for wave in waves(plans):
        for stage in wave:
            stage()
    for wait in sends:
        wait()


def scatter_all(n_dp, n_fs, arrays, collective_id):
    n = len(arrays)
    return pl.pallas_call(
        partial(scatter_kernel, n_dp, n_fs, n),
        out_shape=[jax.ShapeDtypeStruct(a.shape[1:], F32) for a in arrays],
        in_specs=[pl.BlockSpec(memory_space=pltpu.HBM)] * n,
        out_specs=[pl.BlockSpec(memory_space=pltpu.VMEM)] * n,
        scratch_shapes=scatter_scratch(n_dp, n_fs, [a.shape[1:] for a in arrays])
        + scatter_sems(n_dp, n_fs, n),
        compiler_params=pltpu.CompilerParams(
            collective_id=collective_id, has_side_effects=True, vmem_limit_bytes=48 << 20
        ),
        name="scatter_gradients",
    )(*arrays)


def swap_copy(axis, place, count, buffer, send_sem, recv_sem, step):
    return pltpu.make_async_remote_copy(
        src_ref=buffer.at[0],
        dst_ref=buffer.at[step],
        send_sem=send_sem.at[step],
        recv_sem=recv_sem.at[step],
        device_id={axis: lax.rem(place + step, count)},
        device_id_type=MESH,
    )


def swap_start(axis, place, count, *rest):
    for step in range(1, count):
        swap_copy(axis, place, count, *rest, step).start()


def swap_wait(axis, place, count, *rest):
    for step in range(1, count):
        swap_copy(axis, place, count, *rest, step).wait_recv()
    for step in range(1, count):
        swap_copy(axis, place, count, *rest, step).wait_send()


def swap_rows(*args):
    swap_start(*args)
    swap_wait(*args)


def sum_over(x, dp, fs, n_dp, n_fs, octet, line, send_sem, recv_sem, between=None):
    first = ("dp", dp, n_dp, octet, send_sem.at[0], recv_sem.at[0])
    octet[0] = x
    swap_start(*first)
    if between is not None:
        between()
    swap_wait(*first)
    total = octet[0]
    for step in range(1, n_dp):
        total = total + octet[step]
    line[0] = total
    swap_rows("fsdp", fs, n_fs, line, send_sem.at[1], recv_sem.at[1])
    total = line[0]
    for step in range(1, n_fs):
        total = total + line[step]
    return total


def pooled(buffer, count, weight):
    means = [buffer[k, 0:1, :] for k in range(count)]
    center = sum(means[1:], means[0]) * (1.0 / count)
    spread = buffer[0, 1:2, :]
    for k in range(1, count):
        spread = spread + buffer[k, 1:2, :]
    off = (means[0] - center) * (means[0] - center)
    for mean in means[1:]:
        off = off + (mean - center) * (mean - center)
    return center, spread + weight * off


def pool_over(center, spread, frames, dp, fs, n_dp, n_fs, octet, line, send_sem, recv_sem):
    octet[0] = jnp.zeros(octet.shape[1:], F32)
    line[0] = jnp.zeros(line.shape[1:], F32)
    octet[0, 0:1, :] = center
    octet[0, 1:2, :] = spread
    swap_rows("dp", dp, n_dp, octet, send_sem.at[0], recv_sem.at[0])
    center, spread = pooled(octet, n_dp, float(frames))
    line[0, 0:1, :] = center
    line[0, 1:2, :] = spread
    swap_rows("fsdp", fs, n_fs, line, send_sem.at[1], recv_sem.at[1])
    return pooled(line, n_fs, float(frames * n_dp))


def swap_scratch(n_dp, n_fs, channels):
    return [
        pltpu.VMEM((n_dp, 8, channels), F32),
        pltpu.VMEM((n_fs, 8, channels), F32),
        pltpu.SemaphoreType.DMA((2, max(n_dp, n_fs))),
        pltpu.SemaphoreType.DMA((2, max(n_dp, n_fs))),
    ]


def pool_kernel(n_dp, n_fs, frames, x_ref, out_ref, octet, line, send_sem, recv_sem):
    dp, fs = lax.axis_index("dp"), lax.axis_index("fsdp")
    greet(dp, fs, n_dp, n_fs)
    octet[0] = x_ref[...]
    center, spread = pool_over(
        x_ref[0:1, :], x_ref[1:2, :], frames, dp, fs, n_dp, n_fs, octet, line, send_sem, recv_sem
    )
    out_ref[...] = x_ref[...]
    out_ref[0:1, :] = center
    out_ref[1:2, :] = spread


def total_kernel(n_dp, n_fs, frames, x_ref, out_ref, octet, line, send_sem, recv_sem):
    dp, fs = lax.axis_index("dp"), lax.axis_index("fsdp")
    greet(dp, fs, n_dp, n_fs)
    out_ref[...] = sum_over(x_ref[...], dp, fs, n_dp, n_fs, octet, line, send_sem, recv_sem)


def exchange(n_dp, n_fs, x, frames, collective_id, kernel):
    return pl.pallas_call(
        partial(kernel, n_dp, n_fs, frames),
        out_shape=jax.ShapeDtypeStruct(x.shape, F32),
        in_specs=[pl.BlockSpec(memory_space=pltpu.VMEM)],
        out_specs=pl.BlockSpec(memory_space=pltpu.VMEM),
        scratch_shapes=swap_scratch(n_dp, n_fs, x.shape[1]),
        compiler_params=pltpu.CompilerParams(collective_id=collective_id, has_side_effects=True),
        name="exchange_rows",
    )(x)


class Place:
    def __init__(self, dp, fs, n_dp, n_fs):
        self.dp, self.fs, self.n_dp, self.n_fs = dp, fs, n_dp, n_fs
        self.count = (n_dp - 1).bit_length()
        self.bits = [lax.rem(lax.div(dp, 2**k), 2) for k in range(self.count)]
        self.half = n_fs // 2

    def peer(self, bit):
        return (flip(self.dp, 2**bit), self.fs)

    def view(self, ref, free=(), flipped=(), z=None, skip=()):
        index = []
        for bit in reversed(range(self.count)):
            if bit in skip:
                continue
            if bit in free:
                index.append(slice(None))
            else:
                index.append(1 - self.bits[bit] if bit in flipped else self.bits[bit])
        if z is not None:
            index.append(z)
        return ref.at[tuple(index)] if index else ref

    def part(self, which):
        return pl.ds(which * self.half, self.half)


def block_layout(n_dp, n_fs):
    return (2,) * ((n_dp - 1).bit_length()) + (n_fs,)


def hop_orders(place):
    bits = tuple(range(1, place.count))
    return (bits, bits[::-1])


def copy_count(n_dp, n_fs):
    return n_fs - 1 + 2 * ((n_dp - 1).bit_length() - 1) + 1


def block_gather(place, sources, outs, send_sem, recv_sem, local_sem):
    n_fs, fs = place.n_fs, place.fs
    sends = []

    def stages(chunk):
        src, out = sources[chunk], outs[chunk]

        def remote(slot, view_from, view_to, device):
            return pltpu.make_async_remote_copy(
                src_ref=view_from,
                dst_ref=view_to,
                send_sem=send_sem.at[chunk, slot],
                recv_sem=recv_sem.at[chunk, slot],
                device_id=device,
                device_id_type=MESH,
            )

        def launch(make):
            make().start()
            sends.append(lambda: make().wait_send())

        def own_copy():
            return pltpu.make_async_copy(src, place.view(out, z=fs), local_sem.at[chunk])

        def along(step):
            to = lax.rem(fs + step, n_fs)
            return remote(step - 1, src, place.view(out, z=fs), (place.dp, to))

        def start():
            own_copy().start()
            for step in range(1, n_fs):
                launch(lambda step=step: along(step))

        def wait_along():
            own_copy().wait()
            for step in range(1, n_fs):
                origin = lax.rem(fs + n_fs - step, n_fs)
                remote(
                    step - 1, src, place.view(out, z=origin), (place.dp, origin)
                ).wait_recv()

        steps, before = [start], wait_along
        slot = n_fs - 1
        orders = hop_orders(place)
        for depth in range(place.count - 1):
            plan = [(slot + part, part, order[depth], order[:depth]) for part, order in enumerate(orders)]
            slot += 2

            def hop(slot, part, bit, free, arrived):
                view = place.view(out, free, (bit,) if arrived else (), place.part(part))
                return remote(slot, view, view, place.peer(bit))

            def go(plan=plan, before=before, hop=hop):
                before()
                for item in plan:
                    launch(lambda item=item: hop(*item, False))

            def arrive(plan=plan, hop=hop):
                for item in plan:
                    hop(*item, True).wait_recv()

            steps.append(go)
            before = arrive

        def across(arrived, slot=slot):
            free = tuple(range(1, place.count))
            view = place.view(out, free, (0,) if arrived else ())
            return remote(slot, view, view, place.peer(0))

        def cross(before=before):
            before()
            launch(lambda: across(False))

        return steps + [cross, lambda: across(True).wait_recv()]

    return [stages(chunk) for chunk in range(len(outs))], sends


def block_scatter(place, sources, emit, scratch, send_sem, recv_sem, local_sem):
    n_fs, fs = place.n_fs, place.fs
    sends = []
    per = 3 + place.count - 1

    def add_into(kept, other):
        shape = kept.shape[:-3]
        for index in itertools.product(*[range(n) for n in shape]):
            kept[index] = (kept[index].astype(F32) + other[index].astype(F32)).astype(BF16)

    def stages(chunk):
        src = sources[chunk]
        own, cross_in, last, *later = scratch[per * chunk : per * chunk + per]

        def remote(slot, view_from, view_to, device):
            return pltpu.make_async_remote_copy(
                src_ref=view_from,
                dst_ref=view_to,
                send_sem=send_sem.at[chunk, slot],
                recv_sem=recv_sem.at[chunk, slot],
                device_id=device,
                device_id_type=MESH,
            )

        def launch(make):
            make().start()
            sends.append(lambda: make().wait_send())

        every = tuple(range(1, place.count))

        def load():
            return pltpu.make_async_copy(place.view(src, every), own, local_sem.at[chunk])

        def across():
            return remote(0, place.view(src, every, (0,)), cross_in, place.peer(0))

        def start():
            launch(across)
            load().start()

        def fold_cross():
            load().wait()
            across().wait_recv()
            add_into(own, cross_in)

        steps, before = [start], fold_cross
        slot = 1
        orders = [order[::-1] for order in hop_orders(place)]
        for depth in range(place.count - 1):
            plan = []
            for part, order in enumerate(orders):
                free = tuple(order[depth + 1 :])
                plan.append((slot + part, part, order[depth], free, later[depth]))
            slot += 2

            def hop(slot, part, bit, free, buffer):
                view = place.view(own, free, (bit,), place.part(part), skip=(0,))
                return remote(slot, view, buffer.at[part], place.peer(bit))

            def go(plan=plan, before=before, hop=hop):
                before()
                for item in plan:
                    launch(lambda item=item: hop(*item))

            def fold(plan=plan, hop=hop):
                for item in plan:
                    hop(*item).wait_recv()
                    _, part, _, free, buffer = item
                    kept = place.view(own, free, (), place.part(part), skip=(0,))
                    add_into(kept, buffer.at[part])

            steps.append(go)
            before = fold

        def along(step, slot=slot):
            to = lax.rem(fs + step, n_fs)
            view = place.view(own, z=to, skip=(0,))
            return remote(slot + step - 1, view, last.at[step - 1], (place.dp, to))

        def spread(before=before):
            before()
            for step in range(1, n_fs):
                launch(lambda step=step: along(step))

        def finish():
            total = place.view(own, z=fs, skip=(0,))[...].astype(F32)
            for step in range(1, n_fs):
                along(step).wait_recv()
                total = total + last[step - 1].astype(F32)
            emit(chunk, total)

        return steps + [spread, finish]

    return [stages(chunk) for chunk in range(len(sources))], sends


def block_scratch(n_dp, n_fs, blocks, tail):
    hops = (n_dp - 1).bit_length() - 1
    out = []
    for count in blocks:
        entry = (count,) + tail
        zone = (2,) * hops + (n_fs,) + entry
        out += [pltpu.VMEM(zone, BF16), pltpu.VMEM(zone, BF16), pltpu.VMEM((n_fs - 1,) + entry, BF16)]
        for depth in range(hops):
            out.append(pltpu.VMEM((2,) + (2,) * (hops - 1 - depth) + (n_fs // 2,) + entry, BF16))
    return out


def block_sems(n_dp, n_fs, chunks):
    count = copy_count(n_dp, n_fs)
    return [
        pltpu.SemaphoreType.DMA((chunks, count)),
        pltpu.SemaphoreType.DMA((chunks, count)),
        pltpu.SemaphoreType.DMA((chunks,)),
    ]


TILE = 512
STATES = 32
TAPS = 15
REACH = 8
EPSILON = 1e-05
CHUNK = 256
ROWS = 512
VMEM_LIMIT = 60 << 20
TAP_ROW = 24
RATE = 40
MAP_IN = 72
MAP_OUT = 104
TABLE = 136


def sigmoid(v):
    return 0.5 * jnp.tanh(0.5 * v) + 0.5


def dot_nn(a, b):
    return jnp.dot(a, b, preferred_element_type=F32)


def dot_nt(a, b):
    return lax.dot_general(a, b, (((1,), (1,)), ((), ())), preferred_element_type=F32)


def dot_tn(a, b):
    return lax.dot_general(a, b, (((0,), (0,)), ((), ())), preferred_element_type=F32)


def norm_parts(v):
    centered = v - jnp.mean(v, axis=-1, keepdims=True)
    inv = lax.rsqrt(jnp.mean(centered * centered, axis=-1, keepdims=True) + EPSILON)
    return centered * inv, inv


def norm_back(grad, e, inv, gain):
    d = grad * gain
    return (
        d - jnp.mean(d, axis=-1, keepdims=True) - e * jnp.mean(d * e, axis=-1, keepdims=True)
    ) * inv


def fold8(v):
    return jnp.sum(v.reshape((v.shape[0] // 8, 8, v.shape[1])), axis=0)


def by_rows(body, rows=TILE, step=ROWS):
    def run(at, _):
        body(pl.ds(pl.multiple_of(at * step, step), step))
        return 0

    lax.fori_loop(0, rows // step, run, 0)


def columns(at, width=CHUNK):
    return pl.ds(pl.multiple_of(at * width, width), width)


def fill_halo(padded, flags, tiles):
    pitch = TILE + 2 * REACH
    for at in range(tiles):
        base = at * pitch
        if at == 0:
            padded[:, base : base + REACH, :] = jnp.zeros_like(padded[:, base : base + REACH, :])
        if at == tiles - 1:
            end = base + REACH + TILE
            padded[:, end : end + REACH, :] = jnp.zeros_like(padded[:, end : end + REACH, :])
        else:
            keep = flags[at + 1]
            end = base + REACH + TILE
            padded[:, end : end + REACH, :] = (
                padded[:, base + pitch + REACH : base + pitch + 2 * REACH, :] * keep
            )
            padded[:, base + pitch : base + pitch + REACH, :] = (
                padded[:, end - REACH : end, :] * keep
            )


def taps_over(padded, table_ref, store, tiles, reverse, block=64):
    pitch = TILE + 2 * REACH
    per = TILE // block
    lanes = padded.shape[0]
    for lane in range(lanes):
        weights = [
            jnp.broadcast_to(
                table_ref[TAP_ROW + k : TAP_ROW + k + 1, lane * 128 : lane * 128 + 128], (block, 128)
            )
            for k in range(TAPS)
        ]

        def run(at, _):
            tile, inner = at // per, at % per
            base = tile * pitch + inner * block
            total = jnp.zeros((block, 128), F32)
            for k in range(TAPS):
                shift = REACH + (TAPS // 2 - k if reverse else k - TAPS // 2)
                total = total + weights[k] * padded[lane, pl.ds(base + shift, block), :]
            store(lane, tile * TILE + inner * block, base, total)
            return 0

        lax.fori_loop(0, tiles * per, run, 0)


def small_exp(v):
    return 1.0 + v * (1.0 + v * (0.5 + v * (1.0 / 6 + v * (1.0 / 24 + v * (1.0 / 120)))))


def small_expm1_over(v):
    return 1.0 + v * (
        0.5 + v * (1.0 / 6 + v * (1.0 / 24 + v * (1.0 / 120 + v * (1.0 / 720 + v * (1.0 / 5040)))))
    )


def state_terms(table_ref):
    log_decay = -jnp.exp(table_ref[RATE : RATE + STATES, :])
    root = jnp.sqrt(-2.0 * log_decay * small_expm1_over(2.0 * log_decay))
    maps_in = table_ref[MAP_IN : MAP_IN + STATES, :]
    maps_out = table_ref[MAP_OUT : MAP_OUT + STATES, :]
    return log_decay, small_exp(log_decay), root, maps_in, maps_out


def ref_rows(ref):
    return ref.reshape((ref.shape[0] * ref.shape[1], ref.shape[2]))


PIECE = 16
WIDTH = 512


def cols_of(ref, first, at):
    per = WIDTH // CHUNK
    part = ref[:, first + lax.div(at, per), :, columns(lax.rem(at, per))]
    return part.reshape((ref.shape[0] * PIECE, CHUNK))


def rows_of(ref, first, at):
    groups = WIDTH // (4 * PIECE)
    part = ref[pl.ds(at * groups, groups), first : first + 4]
    return part.reshape((WIDTH, WIDTH))


def bias_of(ref, layer, at):
    row = 8 * layer + 2 * at
    return jnp.concatenate([ref[pl.ds(row, 1), :], ref[pl.ds(row + 1, 1), :]], axis=1)


def square_of(ref, at):
    return ref[:, at].reshape((ref.shape[0] * PIECE, WIDTH))


def store_wide(out, first, acc):
    def run(group, _):
        rows = pl.ds(pl.multiple_of(group * PIECE, PIECE), PIECE)
        for k in range(acc.shape[1] // WIDTH):
            out[group, first + k] = acc[rows, k * WIDTH : k * WIDTH + WIDTH].astype(BF16)
        return 0

    lax.fori_loop(0, acc.shape[0] // PIECE, run, 0)


def store_tall(out, first, acc):
    def run(group, _):
        rows = pl.ds(pl.multiple_of(group * 4 * PIECE, 4 * PIECE), 4 * PIECE)
        out[group, first : first + 4] = acc[rows, :].astype(BF16).reshape((4, PIECE, WIDTH))
        return 0

    lax.fori_loop(0, acc.shape[0] // (4 * PIECE), run, 0)


def flat_groups(ref):
    count = 1
    for n in ref.shape[:-3]:
        count *= n
    return ref.reshape((count,) + ref.shape[-3:])


def carries(offsets_ref, counts_ref, tiles):
    out = []
    for tile in range(tiles):
        begins = jnp.int32(0)
        for slot in range(offsets_ref.shape[1]):
            here = (offsets_ref[0, slot] == tile * TILE) & (slot < counts_ref[0])
            begins = jnp.maximum(begins, here.astype(jnp.int32))
        out.append((1 - begins).astype(F32))
    return out


STRETCH = 16
SPREAD = PIECE * STATES


def same_channel(rows, width, per, first=0):
    shape = (rows, width)
    row = lax.rem(lax.broadcasted_iota(jnp.int32, shape, 0), PIECE)
    col = lax.broadcasted_iota(jnp.int32, shape, 1)
    if per == 1:
        return row == lax.rem(col, PIECE)
    return row == lax.div(col, per)


def split_low(v):
    high = v.astype(BF16)
    return high, (v - high.astype(F32)).astype(BF16)


def spread_states(part):
    rows = part.shape[0]
    state = lax.broadcasted_iota(jnp.int32, (STATES, SPREAD), 0)
    col = lax.broadcasted_iota(jnp.int32, (STATES, SPREAD), 1)
    pick_state = (state == lax.rem(col, STATES)).astype(F32).astype(BF16)
    wide = dot_nn(part, pick_state)
    wide = jnp.where(same_channel(rows, SPREAD, STATES), wide, 0.0)
    return jnp.sum(wide.reshape((rows // PIECE, PIECE, SPREAD)), axis=1)


def gather_states(wide):
    groups = wide.shape[0]
    full = jnp.broadcast_to(wide[:, None, :], (groups, PIECE, SPREAD)).reshape((groups * PIECE, SPREAD))
    full = jnp.where(same_channel(groups * PIECE, SPREAD, STATES), full, 0.0)
    state = lax.broadcasted_iota(jnp.int32, (SPREAD, 128), 1)
    row = lax.broadcasted_iota(jnp.int32, (SPREAD, 128), 0)
    pick_state = (state == lax.rem(row, STATES)).astype(F32).astype(BF16)
    high, low = split_low(full)
    return (dot_nn(high, pick_state) + dot_nn(low, pick_state)).T[:STATES, :]


def prepare_states(small, power, shifted, weight):
    groups = small.shape[0]
    entries = lambda first: small[:, :, first : first + STATES].reshape((groups * PIECE, STATES))
    log_decay = -jnp.exp(spread_states(entries(RATE)))
    root = jnp.sqrt(-2.0 * log_decay * small_expm1_over(2.0 * log_decay))
    both = spread_states(entries(MAP_IN)) * root * spread_states(entries(MAP_OUT))
    weight[...] = both
    col = lax.broadcasted_iota(jnp.int32, (SPREAD, 128), 1)
    row = lax.broadcasted_iota(jnp.int32, (SPREAD, 128), 0)
    add_states = (col == lax.div(row, STATES)).astype(F32).astype(BF16)
    power[0] = jnp.ones_like(both)
    decay = small_exp(log_decay)
    for m in range(1, STRETCH):
        power[m] = power[m - 1] * decay
    halves = []
    for half in range(2):
        total = jnp.zeros((groups, 128), F32)
        for k in range(8):
            high, low = split_low(power[half * 8 + k] * both)
            lag = dot_nn(high, add_states) + dot_nn(low, add_states)
            total = total + (pltpu.roll(lag, k * PIECE, 1) if k else lag)
        halves.append(total)
    blank = jnp.zeros((groups, 256), F32)
    padded = jnp.concatenate([blank] + halves, axis=1)
    for m in range(STRETCH):
        shifted[m] = pltpu.roll(padded, 512 - (m + 1) * PIECE, 1)[:, :256]


def group_weights(power, shifted, group, decay_w, lag_w):
    mask = same_channel(PIECE, SPREAD, STATES)
    lag_mask = same_channel(PIECE, 256, 1)
    for m in range(STRETCH):
        rows = slice(m * PIECE, m * PIECE + PIECE)
        line = jnp.broadcast_to(power[m, pl.ds(group, 1), :], (PIECE, SPREAD))
        decay_w[rows, :] = jnp.where(mask, line, 0.0).astype(BF16)
        line = jnp.broadcast_to(shifted[m, pl.ds(group, 1), :], (PIECE, 256))
        lag_w[rows, :] = jnp.where(lag_mask, line, 0.0).astype(BF16)


def swap_blocks(parts):
    col = lax.div(lax.broadcasted_iota(jnp.int32, parts[0].shape, 1), PIECE)
    parts = list(parts)
    for distance in (1, 2, 4):
        low = lax.rem(lax.div(col, distance), 2) == 0
        shift = distance * PIECE
        for a in range(8):
            if a & distance:
                continue
            first, second = parts[a], parts[a + distance]
            parts[a] = jnp.where(low, first, pltpu.roll(second, shift, 1))
            parts[a + distance] = jnp.where(low, pltpu.roll(first, 128 - shift, 1), second)
    return parts


SLAB = 32
TOGETHER = 4


def to_blocks(load, out, blocks, backward):
    for slab in range(blocks // SLAB):
        rows = slice(slab * SLAB, slab * SLAB + SLAB)
        for half in range(2):
            parts = []
            for k in range(8):
                frame = half * 8 + k
                frame = STRETCH - 1 - frame if backward else frame
                parts.append(load(slab * SLAB * STRETCH + frame))
            for group, part in enumerate(swap_blocks(parts)):
                out[group, rows, half * 128 : half * 128 + 128] = part.astype(out.dtype)


def from_blocks(store, ref, blocks, backward):
    for slab in range(blocks // SLAB):
        rows = slice(slab * SLAB, slab * SLAB + SLAB)
        for half in range(2):
            parts = [ref[group, rows, half * 128 : half * 128 + 128] for group in range(8)]
            for k, part in enumerate(swap_blocks(parts)):
                frame = half * 8 + k
                frame = STRETCH - 1 - frame if backward else frame
                store(slab * SLAB * STRETCH + frame, part)


def block_powers(decay):
    q2 = decay * decay
    q4 = q2 * q2
    q8 = q4 * q4
    one = q8 * q8
    two = one * one
    four = two * two
    return one, two, four


def row_powers(one, count=8):
    rows = [one]
    for _ in range(count - 1):
        rows.append(rows[-1] * one)
    return rows


def scan_blocks(source, into, decay, keeps, per, reverse):
    blocks, width = source.shape
    one, two, four = block_powers(decay)
    row = lax.broadcasted_iota(jnp.int32, (8, width), 0)
    if reverse:
        row = 7 - row
    factors = []
    for distance, power in ((1, one), (2, two), (4, four)):
        line = jnp.broadcast_to(power, (8, width))
        factors.append((8 - distance if reverse else distance, jnp.where(row >= distance, line, 0.0)))
    entering = jnp.ones((8, width), F32)
    for bit, power in ((1, one), (2, two), (4, four)):
        line = jnp.broadcast_to(power, (8, width))
        entering = jnp.where(lax.rem(lax.div(row, bit), 2) == 1, entering * line, entering)
    eight = jnp.broadcast_to(four * four, (8, width))
    carry = jnp.zeros((8, width), F32)
    tiles = blocks // 8
    for k in range(tiles):
        tile = tiles - 1 - k if reverse else k
        edge = (tile + 1) * 8 if reverse else tile * 8
        if k and edge % per == 0:
            carry = carry * keeps[edge // per]
        x = source[tile * 8 : tile * 8 + 8, :]
        for shift, factor in factors:
            x = x + factor * pltpu.roll(x, shift, 0)
        moved = pltpu.roll(x, 7 if reverse else 1, 0)
        into[tile * 8 : tile * 8 + 8, :] = jnp.where(row >= 1, moved, 0.0) + entering * carry
        end = x[0:1, :] if reverse else x[7:8, :]
        carry = jnp.broadcast_to(end, (8, width)) + eight * carry


def mix_forward(midway, u_ref, y_ref, power, shifted, weight, keeps, ub_out, state_out, blk_in, blk_out, decay_w, lag_w, t_scr, h_scr):
    frames = u_ref.shape[1]
    blocks = frames // STRETCH
    count = decay_w.shape[0]
    several = range(count)

    def lane_tile(lane, _):
        if midway is not None:
            pl.when(lane == u_ref.shape[0] // 2)(midway)
        to_blocks(lambda at: u_ref[lane, pl.ds(at, SLAB, stride=STRETCH), :], blk_in, blocks, True)

        def some_groups(k, _):
            place = [k * count + n for n in several]
            groups = [lane * 8 + at for at in place]
            for n in several:
                group_weights(power, shifted, groups[n], decay_w.at[n], lag_w.at[n])
            for n in several:
                ub_out[groups[n]] = blk_in[place[n]]
                t_scr[n] = dot_nn(blk_in[place[n]], decay_w[n])
            for n in several:
                decay = power[1, pl.ds(groups[n], 1), :]
                scan_blocks(t_scr.at[n], h_scr.at[n], decay, keeps, TILE // STRETCH, False)
            for n in several:
                decay = power[1, pl.ds(groups[n], 1), :]
                state = h_scr[n]
                state_out[groups[n]] = state.astype(BF16)
                out = (state * (weight[pl.ds(groups[n], 1), :] * decay)).astype(BF16)
                blk_out[place[n]] = dot_nn(blk_in[place[n]], lag_w[n]) + dot_nt(out, decay_w[n])
            return 0

        lax.fori_loop(0, 8 // count, some_groups, 0)

        def store(at, values):
            y_ref[lane, pl.ds(at, SLAB, stride=STRETCH), :] = values

        from_blocks(store, blk_out, blocks, False)
        return 0

    lax.fori_loop(0, u_ref.shape[0], lane_tile, 0)


def mix_backward(
    lane, u_ref, grad, skip, u_tile, u_sem, power, shifted, weight, keeps, ub_ref, state_ref, lags, sums,
    frames_scr, blk_in, blk_out, decay_w, lag_w, stack_scr, e_scr, r_scr,
):
    blocks = frames_scr.shape[2]
    count = decay_w.shape[0]
    several = range(count)
    lanes = u_ref.shape[0]
    copy = lambda at: pltpu.make_async_copy(u_ref.at[at], u_tile, u_sem)
    copy(lane).wait()
    for at in range(STRETCH):
        for slab in range(blocks // SLAB):
            rows = slice(slab * SLAB, slab * SLAB + SLAB)
            first = pl.ds(slab * SLAB * STRETCH + at, SLAB, stride=STRETCH)
            frames_scr[0, at, rows, :] = u_tile[first, :]
            frames_scr[1, at, rows, :] = grad[lane, first, :]

    @pl.when(lane + 1 < lanes)
    def _():
        copy(lane + 1).start()

    def one_lag(lag, _):
        def one_frame(at, total):
            for slab in range(blocks // SLAB):
                rows = slice(slab * SLAB, slab * SLAB + SLAB)
                total = total + frames_scr[1, at, rows, :] * frames_scr[0, at - lag, rows, :]
            return total

        total = lax.fori_loop(lag, STRETCH, one_frame, jnp.zeros((SLAB, 128), F32))
        lags[lane, pl.ds(lag, 1), :] = jnp.sum(total, axis=0, keepdims=True)
        return 0

    lax.fori_loop(0, STRETCH, one_lag, 0)
    for slab in range(blocks // SLAB):
        rows = slice(slab * SLAB, slab * SLAB + SLAB)
        for half in range(2):
            parts = [frames_scr[1, half * 8 + k, rows, :] for k in range(8)]
            for group, part in enumerate(swap_blocks(parts)):
                blk_in[group, rows, half * 128 : half * 128 + 128] = part.astype(BF16)
    position = lax.div(lax.broadcasted_iota(jnp.int32, (1, 256), 1), PIECE).astype(F32)

    def some_groups(k, _):
        place = [k * count + n for n in several]
        groups = [lane * 8 + at for at in place]
        for n in several:
            group_weights(power, shifted, groups[n], decay_w.at[n], lag_w.at[n])
        for n in several:
            gy = blk_in[place[n]]
            stack_scr[n, 0:blocks, :] = gy
            stack_scr[n, blocks : 2 * blocks, :] = (gy.astype(F32) * (position + 1.0)).astype(BF16)
            stack_scr[n, 2 * blocks :, :] = (ub_ref[groups[n]].astype(F32) * position).astype(BF16)
        for n in several:
            e_scr[n] = dot_nn(stack_scr[n], decay_w[n])
        for n in several:
            decay = power[1, pl.ds(groups[n], 1), :]
            own = e_scr.at[n, pl.ds(0, blocks)]
            own[...] = own[...] * decay
            scan_blocks(own, r_scr.at[n], decay, keeps, TILE // STRETCH, True)
        for n in several:
            group = groups[n]
            inverse = 1.0 / power[1, pl.ds(group, 1), :]
            last = 16.0 * power[15, pl.ds(group, 1), :]
            first, second = jnp.zeros((8, SPREAD), F32), jnp.zeros((8, SPREAD), F32)
            for at in range(blocks // 8):
                rows = slice(at * 8, at * 8 + 8)
                state = state_ref[group, rows, :].astype(F32)
                turn = e_scr[n, 2 * blocks + at * 8 : 2 * blocks + at * 8 + 8, :]
                first = first + state * e_scr[n, rows, :]
                second = second + state * e_scr[n, blocks + at * 8 : blocks + at * 8 + 8, :]
                second = second + r_scr[n, rows, :] * (turn * inverse + last * state)
            sums[0, pl.ds(group, 1), :] = jnp.sum(first, axis=0, keepdims=True)
            sums[1, pl.ds(group, 1), :] = jnp.sum(second, axis=0, keepdims=True)
            out = (r_scr[n] * weight[pl.ds(group, 1), :]).astype(BF16)
            blk_out[place[n]] = dot_nt(blk_in[place[n]], lag_w[n]) + dot_nt(out, decay_w[n])
        return 0

    lax.fori_loop(0, 8 // count, some_groups, 0)

    def store(at, values):
        slab, frame = at // (SLAB * STRETCH), at % STRETCH
        through = frames_scr[1, frame, slab * SLAB : slab * SLAB + SLAB, :]
        grad[lane, pl.ds(at, SLAB, stride=STRETCH), :] = values + skip[pl.ds(lane, 1), :] * through

    from_blocks(store, blk_out, blocks, True)


def mix_gradients(lags, sums, table_ref):
    _, decay, root, maps_in, maps_out = state_terms(table_ref)
    coupling = maps_in * root * maps_out
    gmap = gather_states(sums[0])
    gdecay = gather_states(sums[1])
    power = jnp.ones_like(decay)
    for lag in range(STRETCH):
        line = jnp.concatenate([lags[k, lag : lag + 1, :] for k in range(lags.shape[0])], axis=1)
        if lag:
            gdecay = gdecay + float(lag) * power * line
            power = power * decay
        gmap = gmap + power * line
    return gmap, gdecay * coupling


def pack_small(out, scr, place, bias_ref, gains, shifts, conv_bias, taps, rate, maps):
    own = gains.shape[1]
    scr[...] = jnp.zeros_like(scr)
    scr[0:6, :own] = gains[...].astype(F32)
    scr[6:18, :own] = shifts[...].astype(F32)
    scr[18:19, :own] = conv_bias[...].astype(F32)
    scr[TAP_ROW : TAP_ROW + TAPS, :own] = taps[...].astype(F32)
    out[:, :CHUNK] = scr[...].T[:own, :].astype(BF16)
    out[:, RATE:MAP_IN] = rate[...]
    out[:, MAP_IN:MAP_OUT] = maps[0]
    out[:, MAP_OUT:TABLE] = maps[1]
    count = bias_ref.shape[1]
    row = lax.div(place * count, CHUNK)
    inner = place * count - row * CHUNK
    at_row = lax.broadcasted_iota(jnp.int32, (PIECE, CHUNK), 0)
    wide = jnp.zeros((PIECE, CHUNK), F32)
    for layer in range(2):
        line = jnp.broadcast_to(bias_ref[layer : layer + 1, :].astype(F32), (8, count))
        line = jnp.concatenate([line, jnp.zeros((8, CHUNK - count), F32)], axis=1)
        line = pltpu.roll(line, inner, 1)
        wide = wide + jnp.where(at_row == 8 * layer + row, jnp.broadcast_to(line[0:1], wide.shape), 0.0)
    out[:, CHUNK:] = wide.astype(BF16)


def front_kernel(mesh_size, *refs):
    fused = mesh_size is not None
    refs = list(refs)
    take = lambda count: [refs.pop(0) for _ in range(count)]
    offsets_ref, counts_ref, x_ref = take(3)
    if fused:
        n_dp, n_fs = mesh_size
        small_in = take(7)
        up_s, down_s, mixin_s, mixout_s, convin_s, convout_s = take(6)
    else:
        first_v, extra_v, second_v, third_v, fourth_v, table_in, bias_in = take(7)
    (
        h_out,
        x1_out,
        v_out,
        y_out,
        gated_out,
        x2_out,
        p_out,
        u_out,
        w_out,
        stat_out,
        table_ref,
        bias_ref,
        ub_out,
        state_out,
        power,
        shifted,
        weight,
    ) = take(17)
    gathered = take(6) if fused else []
    x1_scr, low_all, low_scr, sum_scr, y_all, padded, act_all = take(7)
    mix_scr = take(6)
    step = pl.program_id(0)
    channels = x_ref.shape[1]
    frames = w_out.shape[0]
    tiles = frames // TILE
    lanes = channels // 128
    gain = lambda k: table_ref[k : k + 1, :]
    shift = lambda k: table_ref[6 + k : 7 + k, :]
    here = lambda rows, tile: pl.ds(pl.multiple_of(tile * TILE + rows.start, ROWS), ROWS)
    flags = carries(offsets_ref, counts_ref, tiles)
    mix_at, last_step = 3 * tiles, 4 * tiles + 1
    if fused:
        landing = take(5)
        sources = take(6)
        turn_scr = refs.pop(0)
        sems = take(3)
        load_sem = refs.pop(0)
        swap = take(4)
        dp, fs = lax.axis_index("dp"), lax.axis_index("fsdp")
        place = Place(dp, fs, n_dp, n_fs)
        landing.append(gathered[5])
        plans, sends = block_gather(place, sources, landing, *sems)
        first_v, extra_v, second_v, third_v, fourth_v = [flat_groups(r) for r in landing[:5]]

        def keep_copy(chunk):
            return pltpu.make_async_copy(landing[chunk], gathered[chunk], load_sem.at[chunk])

        def run(*stages):
            for chunk, stage in stages:
                plans[chunk][stage]()

        @pl.when(step == 0)
        def _():
            pack_small(sources[0].at[0], turn_scr, dp * n_fs + fs, *small_in)
            for k in range(4):
                cols = slice(k * WIDTH, k * WIDTH + WIDTH)
                if k < 2:
                    sources[0][1 + k] = up_s[0, :, cols]
                else:
                    sources[1][k - 2] = up_s[0, :, cols]
                sources[5][1 + k] = up_s[1, :, cols]
                rows = slice(k * PIECE, k * PIECE + PIECE)
                sources[2][k] = down_s[0, rows, :]
                sources[5][5 + k] = down_s[1, rows, :]
            for k in range(2):
                cols = slice(k * WIDTH, k * WIDTH + WIDTH)
                sources[3][k] = mixin_s[:, cols]
                sources[4][1 + k] = convin_s[:, cols]
            sources[4][0] = mixout_s[...]
            sources[5][0] = convout_s[...]
            greet(dp, fs, n_dp, n_fs)
            run((0, 0), (1, 0), (0, 1), (2, 0), (1, 1), (0, 2), (1, 2), (0, 3), (2, 1), (3, 0), (0, 4))
            table_ref[...] = first_v[:, 0, :, :CHUNK].reshape((channels, CHUNK)).astype(F32).T[:TABLE, :]
            total = first_v[0, 0, :, CHUNK:].astype(F32)
            for k in range(1, n_dp * n_fs):
                total = total + first_v[k, 0, :, CHUNK:].astype(F32)
            bias_ref[...] = total

        rest = {1: [(1, 3), (2, 2)], 2: [(3, 1)], tiles: [(1, 4), (4, 0)], tiles + 1: [(2, 3), (3, 2)]}
        rest.update({2 * tiles: [(2, 4), (3, 3), (4, 1)], 2 * tiles + 1: [(5, 0)]})
        rest.update({2 * tiles + 2: [(4, 2)], mix_at: [(3, 4)]})
        rest.update({mix_at + 1: [(4, 4), (5, 2)], last_step: [(5, 3)]})
        for at, stages in rest.items():

            @pl.when(step == at)
            def _(at=at, stages=stages):
                run(*stages)
                saved = {2 * tiles: (0, 1, 2), mix_at: (3,), mix_at + 1: (4,)}
                for chunk in saved.get(at, ()):
                    keep_copy(chunk).start()

    else:

        @pl.when(step == 0)
        def _():
            table_ref[...] = table_in[...]
            bias_ref[...] = bias_in[...]

    @pl.when(step < tiles)
    def _():
        def first(rows):
            e, _ = norm_parts(x_ref[rows, :].astype(F32))
            low_all[here(rows, step), :] = (e * gain(0) + shift(0)).astype(BF16)

        by_rows(first)

    for half, part in enumerate((first_v, extra_v)):

        @pl.when((step >= half * tiles) & (step < half * tiles + tiles))
        def _(half=half, part=part):
            tile_rows = pl.ds(pl.multiple_of((step - half * tiles) * TILE, TILE), TILE)
            for k in range(2):
                c = 2 * half + k
                h = dot_nn(low_all[tile_rows, :], square_of(part, 1 - half + k))
                h = h + bias_of(bias_ref, 0, c)
                h_out[:, k * WIDTH : k * WIDTH + WIDTH] = h.astype(BF16)
                active = (h * sigmoid(h)).astype(BF16)
                act_all[tile_rows, c * WIDTH : c * WIDTH + WIDTH] = active

    @pl.when((step >= 2 * tiles) & (step < mix_at))
    def _():
        at = step - 2 * tiles
        tile_rows = pl.ds(pl.multiple_of(at * TILE, TILE), TILE)
        total = dot_nn(act_all[tile_rows, :WIDTH], rows_of(second_v, 0, 0))
        for c in range(1, 4):
            cols = slice(c * WIDTH, c * WIDTH + WIDTH)
            total = total + dot_nn(act_all[tile_rows, cols], rows_of(second_v, 0, c))
        sum_scr[...] = total

        def second(rows):
            x1 = x_ref[rows, :].astype(F32) + 0.5 * (sum_scr[rows, :] + shift(6))
            x1_out[rows, :] = x1
            x1_scr[here(rows, at), :] = x1
            e, _ = norm_parts(x1)
            low_all[here(rows, at), :] = (e * gain(1) + shift(1)).astype(BF16)

        by_rows(second)

    @pl.when(step == mix_at)
    def _():
        prepare_states(first_v[:, 0, :, :CHUNK], power, shifted, weight)

        def project(tile, _):
            rows = pl.ds(pl.multiple_of(tile * TILE, TILE), TILE)
            u = dot_nn(low_all[rows, :], square_of(third_v, 0))
            for lane in range(lanes):
                u_out[lane, rows, :] = u[:, lane * 128 : lane * 128 + 128]
            return 0

        lax.fori_loop(0, tiles, project, 0)
        if fused:
            run((4, 3))
        mixing = (u_out, y_all, power, shifted, weight, flags, ub_out, state_out) + tuple(mix_scr)
        mix_forward((lambda: run((5, 1))) if fused else None, *mixing)

    @pl.when((step > mix_at) & (step < last_step))
    def _():
        at = step - mix_at - 1
        whole_tile = pl.ds(pl.multiple_of(at * TILE, TILE), TILE)
        v_out[...] = dot_nn(low_all[whole_tile, :], square_of(third_v, 1)).astype(BF16)

        def gate(rows):
            join = lambda ref: jnp.concatenate([ref[lane, here(rows, at), :] for lane in range(lanes)], axis=1)
            y = join(y_all) + shift(11) * join(u_out)
            v = v_out[rows, :].astype(F32)
            y_out[rows, :] = y.astype(BF16)
            gated_out[rows, :] = (y * (v * sigmoid(v))).astype(BF16)

        by_rows(gate)
        sum_scr[...] = dot_nn(gated_out[...], square_of(fourth_v, 0))

        def third(rows):
            x2 = x1_scr[here(rows, at), :] + (sum_scr[rows, :] + shift(8))
            x2_out[rows, :] = x2
            e, _ = norm_parts(x2)
            low_scr[rows, :] = (e * gain(2) + shift(2)).astype(BF16)

        by_rows(third)
        pitch = TILE + 2 * REACH

        def widen(c, _):
            cols = columns(c)
            right = columns(c + channels // CHUNK)
            left_part = dot_nn(low_scr[...], cols_of(fourth_v, 1, c)) + table_ref[15:16, cols]
            right_part = dot_nn(low_scr[...], cols_of(fourth_v, 2, c)) + table_ref[16:17, cols]
            p_out[:, cols] = left_part.astype(BF16)
            p_out[:, right] = right_part.astype(BF16)
            g = left_part * sigmoid(right_part)
            place = pl.ds(pl.multiple_of(at * pitch + REACH, 8), TILE)
            for k in range(CHUNK // 128):
                padded[c * (CHUNK // 128) + k, place, :] = g[:, k * 128 : k * 128 + 128]
            return 0

        lax.fori_loop(0, channels // CHUNK, widen, 0)

    @pl.when(step == last_step)
    def _():
        fill_halo(padded, flags, tiles)

        def store(lane, row, base, total):
            w_out[pl.ds(pl.multiple_of(row, 64), 64), lane * 128 : lane * 128 + 128] = total

        taps_over(padded, table_ref, store, tiles, False)
        stat_out[...] = jnp.zeros_like(stat_out)

        def total(at, _):
            rows = pl.ds(pl.multiple_of(at * ROWS, ROWS), ROWS)
            stat_out[...] += fold8(w_out[rows, :])
            return 0

        lax.fori_loop(0, frames // ROWS, total, 0)
        center = jnp.sum(stat_out[...], axis=0, keepdims=True) * (1.0 / frames)
        stat_out[...] = jnp.zeros_like(stat_out)

        def spread(at, _):
            rows = pl.ds(pl.multiple_of(at * ROWS, ROWS), ROWS)
            off = w_out[rows, :] - center
            stat_out[...] += fold8(off * off)
            return 0

        lax.fori_loop(0, frames // ROWS, spread, 0)
        around = jnp.sum(stat_out[...], axis=0, keepdims=True)
        if fused:
            center, around = pool_over(center, around, frames, dp, fs, n_dp, n_fs, *swap)
            around = lax.rsqrt(around * (1.0 / (frames * n_dp * n_fs)) + EPSILON)
        stat_out[...] = jnp.zeros_like(stat_out)
        stat_out[0:1, :] = center
        stat_out[1:2, :] = around
        if fused:
            run((5, 4))
            for chunk in range(5):
                keep_copy(chunk).wait()
            for wait in sends:
                wait()


def whole(shape):
    zeros = (0,) * len(shape)
    return pl.BlockSpec(shape, lambda *_: zeros, pipeline_mode=pl.Buffered(1))


def params(collective_id=None):
    if collective_id is None:
        return pltpu.CompilerParams(
            dimension_semantics=("arbitrary",), vmem_limit_bytes=VMEM_LIMIT
        )
    return pltpu.CompilerParams(
        dimension_semantics=("arbitrary",),
        vmem_limit_bytes=VMEM_LIMIT,
        collective_id=collective_id,
        has_side_effects=True,
    )


SMEM_SPEC = pl.BlockSpec(memory_space=pltpu.SMEM)
HBM_SPEC = pl.BlockSpec(memory_space=pltpu.HBM)


def front(mesh_size, offsets, counts, x, small, weights, hidden, collective_id=None):
    fused = mesh_size is not None
    frames, channels = x.shape
    tiles = frames // TILE
    clip = lambda i, first: jnp.clip(i - first, 0, tiles - 1)
    twice = lambda i: (jnp.where(i < tiles, i, jnp.where(i < 2 * tiles, tiles - 1, clip(i, 2 * tiles))), 0)
    halves = lambda i: (jnp.where(i < tiles, i, clip(i, tiles)), jnp.where(i < tiles, 0, 1))
    place = lambda i: clip(i, 3 * tiles + 1)
    late = lambda width: pl.BlockSpec((TILE, width), lambda i: (place(i), 0))
    shape = lambda width, kind: jax.ShapeDtypeStruct((frames, width), kind)
    groups, blocks = channels // PIECE, frames // STRETCH
    out_shape = [
        shape(hidden, BF16),
        shape(channels, F32),
        shape(channels, BF16),
        shape(channels, BF16),
        shape(channels, BF16),
        shape(channels, F32),
        shape(2 * channels, BF16),
        jax.ShapeDtypeStruct((channels // 128, frames, 128), F32),
        shape(channels, F32),
        jax.ShapeDtypeStruct((8, channels), F32),
        jax.ShapeDtypeStruct((TABLE, channels), F32),
        jax.ShapeDtypeStruct((16, CHUNK), F32),
        jax.ShapeDtypeStruct((groups, blocks, STRETCH * PIECE), BF16),
        jax.ShapeDtypeStruct((groups, blocks, SPREAD), BF16),
        jax.ShapeDtypeStruct((STRETCH, groups, SPREAD), F32),
        jax.ShapeDtypeStruct((STRETCH, groups, STRETCH * PIECE), F32),
        jax.ShapeDtypeStruct((groups, SPREAD), F32),
    ]
    out_specs = [
        pl.BlockSpec((TILE, hidden // 2), halves),
        pl.BlockSpec((TILE, channels), lambda i: (clip(i, 2 * tiles), 0)),
    ]
    out_specs += [late(channels)] * 4 + [late(2 * channels)]
    out_specs += [whole(s.shape) for s in out_shape[7:]]
    scratch = [
        pltpu.VMEM((frames, channels), F32),
        pltpu.VMEM((frames, channels), BF16),
        pltpu.VMEM((TILE, channels), BF16),
        pltpu.VMEM((TILE, channels), F32),
        pltpu.VMEM((channels // 128, frames, 128), F32),
        pltpu.VMEM((channels // 128, tiles * (TILE + 2 * REACH), 128), F32),
        pltpu.VMEM((frames, hidden), BF16),
        pltpu.VMEM((8, blocks, STRETCH * PIECE), BF16),
        pltpu.VMEM((8, blocks, STRETCH * PIECE), F32),
        pltpu.VMEM((TOGETHER, STRETCH * PIECE, SPREAD), BF16),
        pltpu.VMEM((TOGETHER, STRETCH * PIECE, STRETCH * PIECE), BF16),
        pltpu.VMEM((TOGETHER, blocks, SPREAD), F32),
        pltpu.VMEM((TOGETHER, blocks, SPREAD), F32),
    ]
    operands = (weights if not fused else small + weights) + (small if not fused else [])
    if fused:
        layout = block_layout(*mesh_size)
        blocks = (3, 2, 4, 2, 3, 9)
        chunks = [jax.ShapeDtypeStruct(layout + (k, PIECE, WIDTH), BF16) for k in blocks]
        out_shape += chunks
        out_specs += [HBM_SPEC] * len(chunks)
        scratch += [pltpu.VMEM(c.shape, BF16) for c in chunks[:5]]
        scratch += [pltpu.VMEM((k, PIECE, WIDTH), BF16) for k in blocks]
        scratch += [pltpu.VMEM((CHUNK, 128), F32)]
        scratch += block_sems(*mesh_size, len(chunks)) + [pltpu.SemaphoreType.DMA((5,))]
        scratch += swap_scratch(*mesh_size, channels)
    return pl.pallas_call(
        partial(front_kernel, mesh_size),
        grid=(4 * tiles + 2,),
        in_specs=[SMEM_SPEC, SMEM_SPEC, pl.BlockSpec((TILE, channels), twice)] + [whole(a.shape) for a in operands],
        out_specs=out_specs,
        out_shape=out_shape,
        scratch_shapes=scratch,
        compiler_params=params(collective_id),
        name="front",
    )(offsets, counts, x, *operands)


def middle_kernel(
    mesh_size,
    x2_ref,
    w_ref,
    cot_ref,
    blocks_ref,
    bias_ref,
    vec_ref,
    stat_ref,
    out_ref,
    gx3_ref,
    gnb_ref,
    gblocks_out,
    gbias_out,
    gvec_out,
    stat_out,
    up_acc,
    down_acc,
    convout_acc,
    bias_acc,
    vec_acc,
    h_scr,
    low_scr,
    turn_scr,
    act_scr,
    grad_scr,
    sum_scr,
    x3_scr,
    *swap,
):
    at = pl.program_id(0)
    tiles = pl.num_programs(0)
    channels = x2_ref.shape[1]
    if mesh_size is not None:
        n_dp, n_fs = mesh_size
        dp, fs = lax.axis_index("dp"), lax.axis_index("fsdp")

        @pl.when(at == 0)
        def _():
            greet(dp, fs, n_dp, n_fs)

    hidden = up_acc.shape[1]
    gain = lambda k: vec_ref[k : k + 1, :]
    shift = lambda k: vec_ref[6 + k : 7 + k, :]
    center, scale = stat_ref[0:1, :], stat_ref[1:2, :]

    @pl.when(at == 0)
    def _():
        for ref in (up_acc, down_acc, convout_acc, bias_acc, vec_acc):
            ref[...] = jnp.zeros_like(ref)

    def normed(rows):
        e = (w_ref[rows, :] - center) * scale
        return e, e * gain(5) + shift(5)

    def first(rows):
        _, nb = normed(rows)
        act_scr[rows, :] = (nb * sigmoid(nb)).astype(BF16)

    by_rows(first)
    sum_scr[...] = dot_nn(act_scr[...], square_of(blocks_ref, 0))

    def second(rows):
        x3 = x2_ref[rows, :] + (sum_scr[rows, :] + vec_ref[18:19, :])
        x3_scr[rows, :] = x3
        e, _ = norm_parts(x3)
        low_scr[rows, :] = (e * gain(3) + shift(3)).astype(BF16)
        sum_scr[rows, :] = jnp.zeros((ROWS, channels), F32)

    by_rows(second)

    def forward(c, _):
        cols = columns(c, WIDTH)
        h = dot_nn(low_scr[...], square_of(blocks_ref, 1 + c)) + bias_of(bias_ref, 1, c)
        h_scr[:, cols] = h
        active = (h * sigmoid(h)).astype(BF16)
        sum_scr[...] += dot_nn(active, rows_of(blocks_ref, 5, c))
        return 0

    lax.fori_loop(0, hidden // WIDTH, forward, 0)
    turn_scr[...] = low_scr[...].T

    def last(rows):
        x4 = x3_scr[rows, :] + 0.5 * (sum_scr[rows, :] + shift(7))
        e, inv = norm_parts(x4)
        out_ref[rows, :] = (e * gain(4) + shift(4)).astype(BF16)
        cot = cot_ref[rows, :].astype(F32)
        vec_acc[0] += fold8(cot * e)
        vec_acc[1] += fold8(cot)
        gx4 = norm_back(cot, e, inv, gain(4))
        gx3_ref[rows, :] = gx4
        low = (0.5 * gx4).astype(BF16)
        grad_scr[rows, :] = low
        vec_acc[2] += fold8(low.astype(F32))
        sum_scr[rows, :] = jnp.zeros((ROWS, channels), F32)

    by_rows(last)

    def backward(c, _):
        cols = columns(c, WIDTH)
        h = h_scr[:, cols]
        sig = sigmoid(h)
        active = h * sig
        gate = dot_nt(grad_scr[...], rows_of(blocks_ref, 5, c))
        grad_h = (gate * (sig * (1.0 + h - active))).astype(BF16)
        bias_acc[:, cols] += fold8(grad_h.astype(F32))
        down_acc[cols, :] += dot_tn(active.astype(BF16), grad_scr[...])
        up_acc[:, cols] += dot_nn(turn_scr[...], grad_h)
        sum_scr[...] += dot_nt(grad_h, square_of(blocks_ref, 1 + c))
        return 0

    lax.fori_loop(0, hidden // WIDTH, backward, 0)

    def fourth(rows):
        e, inv = norm_parts(x3_scr[rows, :])
        grad = sum_scr[rows, :]
        vec_acc[3] += fold8(grad * e)
        vec_acc[4] += fold8(grad)
        gx3 = gx3_ref[rows, :] + norm_back(grad, e, inv, gain(3))
        gx3_ref[rows, :] = gx3
        low = gx3.astype(BF16)
        grad_scr[rows, :] = low
        vec_acc[5] += fold8(low.astype(F32))

    by_rows(fourth)
    convout_acc[...] += dot_tn(act_scr[...], grad_scr[...])
    sum_scr[...] = dot_nt(grad_scr[...], square_of(blocks_ref, 0))

    def fifth(rows):
        e, nb = normed(rows)
        sig = sigmoid(nb)
        gnb = sum_scr[rows, :] * (sig * (1.0 + nb * (1.0 - sig)))
        gnb_ref[rows, :] = gnb
        vec_acc[6] += fold8(gnb * e)
        vec_acc[7] += fold8(gnb)

    by_rows(fifth)

    @pl.when(at == tiles - 1)
    def _():
        for k in range(8):
            gvec_out[k : k + 1, :] = jnp.sum(vec_acc[k], axis=0, keepdims=True)

        def convert():
            store_wide(gblocks_out, 0, convout_acc)
            store_wide(gblocks_out, 1, up_acc)
            store_tall(gblocks_out, 5, down_acc)
            gbias_out[...] = jnp.broadcast_to(
                jnp.sum(bias_acc[...], axis=0, keepdims=True), gbias_out.shape
            )

        stat_out[...] = stat_ref[...]
        if mesh_size is None:
            convert()
        else:
            total = sum_over(gvec_out[...], dp, fs, n_dp, n_fs, *swap, between=convert)
            share = gain(5) * (1.0 / (TILE * tiles * n_dp * n_fs))
            stat_out[2:3, :] = total[7:8, :] * share
            stat_out[3:4, :] = total[6:7, :] * share


def middle(mesh_size, x2, w, cot, blocks, bias, vec, stat, hidden, collective_id=None):
    frames, channels = x2.shape
    tiles = frames // TILE
    row = lambda width: pl.BlockSpec((TILE, width), lambda i: (i, 0))
    shapes = [
        jax.ShapeDtypeStruct((frames, channels), BF16),
        jax.ShapeDtypeStruct((frames, channels), F32),
        jax.ShapeDtypeStruct((frames, channels), F32),
        jax.ShapeDtypeStruct(blocks.shape, BF16),
        jax.ShapeDtypeStruct((8, hidden), F32),
        jax.ShapeDtypeStruct((8, channels), F32),
        jax.ShapeDtypeStruct((8, channels), F32),
    ]
    swap = [] if mesh_size is None else swap_scratch(*mesh_size, channels)
    return pl.pallas_call(
        partial(middle_kernel, mesh_size),
        grid=(tiles,),
        in_specs=[row(channels)] * 3
        + [whole(a.shape) for a in (blocks, bias, vec, stat)],
        out_specs=[row(channels)] * 3 + [whole(s.shape) for s in shapes[3:]],
        out_shape=shapes,
        scratch_shapes=[
            pltpu.VMEM((channels, hidden), F32),
            pltpu.VMEM((hidden, channels), F32),
            pltpu.VMEM((channels, channels), F32),
            pltpu.VMEM((8, hidden), F32),
            pltpu.VMEM((8, 8, channels), F32),
            pltpu.VMEM((TILE, hidden), F32),
            pltpu.VMEM((TILE, channels), BF16),
            pltpu.VMEM((channels, TILE), BF16),
            pltpu.VMEM((TILE, channels), BF16),
            pltpu.VMEM((TILE, channels), BF16),
            pltpu.VMEM((TILE, channels), F32),
            pltpu.VMEM((TILE, channels), F32),
        ]
        + swap,
        compiler_params=params(collective_id),
        name="middle",
    )(x2, w, cot, blocks, bias, vec, stat)


def back_kernel(mesh_size, *refs):
    fused = mesh_size is not None
    refs = list(refs)
    take = lambda count: [refs.pop(0) for _ in range(count)]
    offsets_ref, counts_ref, w_ref, gnb_ref, p_ref = take(5)
    x2_ref, gx3_ref, gated_ref, y_ref, v_ref, x1_ref = take(6)
    u_ref, ub_ref, state_ref, power, shifted, weight, mixin_ref, middle_ref, vec_ref, stat_ref = take(10)
    sources = take(1) if fused else []
    gx1_ref, gin_out, gvec_out, gtaps_ref, gmap_out, gdecay_out = take(6)
    reduced = take(2) if fused else []
    mid_ref = None if fused else refs.pop(0)
    wide_acc, mixout_acc, vec_acc, low_scr, wide_scr, sum_scr = take(6)
    padded, gpad, gv_all, lags, sums, skip, u_tile, u_sem = take(8)
    mix_scr = take(8)
    step = pl.program_id(0)
    channels = x2_ref.shape[1]
    frames = u_ref.shape[1]
    tiles = frames // TILE
    lanes = channels // 128
    pitch = TILE + 2 * REACH
    conv_at, mix_at = tiles, 2 * tiles + 1
    last_step = 3 * tiles + 1
    gain = lambda k: vec_ref[k : k + 1, :]
    shift = lambda k: vec_ref[6 + k : 7 + k, :]
    left, right = slice(0, channels), slice(channels, 2 * channels)
    flags = carries(offsets_ref, counts_ref, tiles)
    schedule = {}
    if fused:
        n_dp, n_fs = mesh_size
        place = Place(lax.axis_index("dp"), lax.axis_index("fsdp"), n_dp, n_fs)
        mid_src = refs.pop(0)
        mid_ref = flat_groups(mid_src)
        scratch = take(2 * (2 + place.count))

        def emit(chunk, total):
            reduced[chunk][...] = total

        plans, sends = block_scatter(place, sources + [mid_src], emit, scratch, *take(3))
        first = [(0, 0), (conv_at, 1), (conv_at + 2, 0), (mix_at, 0), (mix_at, 1)]
        second = [(mix_at, 0), (mix_at, 1), (mix_at + 1, 0), (mix_at + 2, 0), (last_step, 1)]
        for chunk, points in enumerate((first, second)):
            for stage, point in enumerate(points):
                schedule.setdefault(point, []).append((stage, chunk))

    def progress(at, part):
        for stage, chunk in sorted(schedule.get((at, part), [])):
            plans[chunk][stage]()

    @pl.when(step == 0)
    def _():
        for ref in (wide_acc, mixout_acc, vec_acc):
            ref[...] = jnp.zeros_like(ref)
        if fused:
            greet(place.dp, place.fs, n_dp, n_fs)

    for at in sorted({key[0] for key in schedule if key[1] == 0 and key[0] != mix_at}):

        @pl.when(step == at)
        def _(at=at):
            progress(at, 0)

    @pl.when(step < tiles)
    def _():
        center, scale = stat_ref[0:1, :], stat_ref[1:2, :]
        plain, cross = stat_ref[2:3, :], stat_ref[3:4, :]

        def fill(index, _):
            rows = pl.ds(pl.multiple_of(index * 64, 64), 64)
            spot = pl.ds(pl.multiple_of(step * pitch + REACH + index * 64, 8), 64)
            e = (w_ref[rows, :] - center) * scale
            d = gnb_ref[rows, :] * gain(5)
            gw = scale * (d - plain - e * cross)
            g = p_ref[rows, left].astype(F32) * sigmoid(p_ref[rows, right].astype(F32))
            for lane in range(lanes):
                cols = slice(lane * 128, lane * 128 + 128)
                padded[lane, spot, :] = gw[:, cols]
                gpad[lane, spot, :] = g[:, cols]
            return 0

        lax.fori_loop(0, TILE // 64, fill, 0)

    @pl.when(step == conv_at)
    def _():
        fill_halo(padded, flags, tiles)
        fill_halo(gpad, flags, tiles)
        block = 64
        per = TILE // block
        gtaps_ref[...] = jnp.zeros_like(gtaps_ref)
        for lane in range(lanes):

            def corr(index, sums, lane=lane):
                base = (index // per) * pitch + (index % per) * block
                here = padded[lane, pl.ds(pl.multiple_of(base + REACH, 8), block), :]
                return tuple(
                    s + fold8(here * gpad[lane, pl.ds(base + REACH + k - TAPS // 2, block), :])
                    for k, s in enumerate(sums)
                )

            found = lax.fori_loop(0, tiles * per, corr, (jnp.zeros((8, 128), F32),) * TAPS)
            for k in range(TAPS):
                gtaps_ref[k : k + 1, lane * 128 : lane * 128 + 128] = jnp.sum(
                    found[k], axis=0, keepdims=True
                )
        progress(conv_at, 1)

        def store(lane, row, base, total):
            gpad[lane, pl.ds(pl.multiple_of(base + REACH, 8), 64), :] = total

        taps_over(padded, vec_ref, store, tiles, True)

    @pl.when((step > conv_at) & (step < mix_at))
    def _():
        at = step - conv_at - 1

        def first(rows):
            spot = pl.ds(pl.multiple_of(at * pitch + REACH + rows.start, 8), ROWS)
            grad = jnp.concatenate([gpad[lane, spot, :] for lane in range(lanes)], axis=1)
            sig = sigmoid(p_ref[rows, right].astype(F32))
            gl = (grad * sig).astype(BF16)
            gr = (grad * p_ref[rows, left].astype(F32) * (sig * (1.0 - sig))).astype(BF16)
            wide_scr[rows, left] = gl
            wide_scr[rows, right] = gr
            vec_acc[0] += fold8(gl.astype(F32))
            vec_acc[1] += fold8(gr.astype(F32))
            e, _ = norm_parts(x2_ref[rows, :])
            low_scr[rows, :] = (e * gain(2) + shift(2)).astype(BF16)

        by_rows(first)
        turned = low_scr[...].T
        wide_acc[...] += dot_nn(turned, wide_scr[...])
        sum_scr[...] = dot_nt(wide_scr[:, left], square_of(middle_ref, 1)) + dot_nt(
            wide_scr[:, right], square_of(middle_ref, 2)
        )

        def second(rows):
            here = pl.ds(pl.multiple_of(at * TILE + rows.start, ROWS), ROWS)
            e, inv = norm_parts(x2_ref[rows, :])
            grad = sum_scr[rows, :]
            vec_acc[2] += fold8(grad * e)
            vec_acc[3] += fold8(grad)
            gx2 = gx3_ref[rows, :] + norm_back(grad, e, inv, gain(2))
            spot = pl.ds(pl.multiple_of(at * pitch + REACH + rows.start, 8), ROWS)
            for lane in range(lanes):
                gpad[lane, spot, :] = gx2[:, lane * 128 : lane * 128 + 128]
            low = gx2.astype(BF16)
            low_scr[rows, :] = low
            vec_acc[4] += fold8(low.astype(F32))

        by_rows(second)
        mixout_acc[...] += dot_tn(gated_ref[...], low_scr[...])
        sum_scr[...] = dot_nt(low_scr[...], square_of(middle_ref, 0))

        def third(rows):
            here = pl.ds(pl.multiple_of(at * TILE + rows.start, ROWS), ROWS)
            grad = sum_scr[rows, :]
            v = v_ref[rows, :].astype(F32)
            sig = sigmoid(v)
            swish = v * sig
            gy = grad * swish
            for lane in range(lanes):
                padded[lane, here, :] = gy[:, lane * 128 : lane * 128 + 128]
            gv_all[here, :] = (
                grad * y_ref[rows, :].astype(F32) * (sig * (1.0 + v - swish))
            ).astype(BF16)


        by_rows(third)

    @pl.when(step == mix_at)
    def _():
        pltpu.make_async_copy(u_ref.at[0], u_tile, u_sem).start()
        store_wide(mid_ref, 0, mixout_acc)
        store_wide(mid_ref, 1, wide_acc)
        wide_acc[...] = jnp.zeros_like(wide_acc)
        for lane in range(lanes):
            skip[lane : lane + 1, :] = vec_ref[17:18, lane * 128 : lane * 128 + 128]
        progress(mix_at, 0)

        def one(lane, _):
            if fused:
                pl.when(lane == lanes // 2)(lambda: progress(mix_at, 1))
            mix_backward(
                lane, u_ref, padded, skip, u_tile, u_sem, power, shifted, weight, flags, ub_ref, state_ref, lags, sums, *mix_scr
            )
            return 0

        lax.fori_loop(0, lanes, one, 0)
        gmap, gdecay = mix_gradients(lags, sums, vec_ref)
        gmap_out[...] = gmap
        gdecay_out[...] = gdecay

    @pl.when(step > mix_at)
    def _():
        at = step - mix_at - 1

        def fourth(rows):
            here = pl.ds(pl.multiple_of(at * TILE + rows.start, ROWS), ROWS)
            gu = jnp.concatenate([padded[lane, here, :] for lane in range(lanes)], axis=1)
            wide_scr[rows, left] = gu.astype(BF16)
            wide_scr[rows, right] = gv_all[here, :]
            e, _ = norm_parts(x1_ref[rows, :])
            low_scr[rows, :] = (e * gain(1) + shift(1)).astype(BF16)

        by_rows(fourth)
        turned = low_scr[...].T
        wide_acc[...] += dot_nn(turned, wide_scr[...])
        sum_scr[...] = dot_nt(wide_scr[:, left], square_of(mixin_ref, 0)) + dot_nt(
            wide_scr[:, right], square_of(mixin_ref, 1)
        )

        def fifth(rows):
            e, inv = norm_parts(x1_ref[rows, :])
            grad = sum_scr[rows, :]
            vec_acc[6] += fold8(grad * e)
            vec_acc[7] += fold8(grad)
            spot = pl.ds(pl.multiple_of(at * pitch + REACH + rows.start, 8), ROWS)
            gx2 = jnp.concatenate([gpad[lane, spot, :] for lane in range(lanes)], axis=1)
            gx1_ref[rows, :] = gx2 + norm_back(grad, e, inv, gain(1))

        by_rows(fifth)

    @pl.when(step == last_step)
    def _():
        store_wide(gin_out, 0, wide_acc)
        for k in range(8):
            gvec_out[k : k + 1, :] = jnp.sum(vec_acc[k], axis=0, keepdims=True)
        gvec_out[5:6, :] = jnp.concatenate([lags[k, 0:1, :] for k in range(lanes)], axis=1)
        if fused:
            progress(last_step, 1)
            for wait in sends:
                wait()


def back(mesh_size, offsets, counts, tiled, wholes, grads=(), collective_id=None):
    fused = mesh_size is not None
    frames, channels = tiled[0].shape
    tiles = frames // TILE
    groups, blocks = channels // PIECE, frames // STRETCH
    late = lambda i, first: jnp.clip(i - first, 0, tiles - 1)
    filling = lambda i: (late(i, 0), 0)
    twice = lambda i: (jnp.where(i < tiles, i, late(i, tiles + 1)), 0)
    mixing = lambda i: (late(i, tiles + 1), 0)
    ending = lambda i: (late(i, 2 * tiles + 2), 0)
    maps = [filling, filling, twice] + [mixing] * 5 + [ending]
    state = jax.ShapeDtypeStruct((STATES, channels), F32)
    bf16 = lambda *shape: jax.ShapeDtypeStruct(shape, BF16)
    shapes = [
        jax.ShapeDtypeStruct((frames, channels), F32),
        bf16(groups, 2, PIECE, WIDTH),
        jax.ShapeDtypeStruct((8, channels), F32),
        jax.ShapeDtypeStruct((16, channels), F32),
        state,
        state,
    ]
    pad = pltpu.VMEM((channels // 128, tiles * (TILE + 2 * REACH), 128), F32)
    scratch = [
        pltpu.VMEM((channels, 2 * channels), F32),
        pltpu.VMEM((channels, channels), F32),
        pltpu.VMEM((8, 8, channels), F32),
        pltpu.VMEM((TILE, channels), BF16),
        pltpu.VMEM((TILE, 2 * channels), BF16),
        pltpu.VMEM((TILE, channels), F32),
        pad,
        pad,
        pltpu.VMEM((frames, channels), BF16),
        pltpu.VMEM((channels // 128, STRETCH, 128), F32),
        pltpu.VMEM((2, groups, SPREAD), F32),
        pltpu.VMEM((8, 128), F32),
        pltpu.VMEM((frames, 128), F32),
        pltpu.SemaphoreType.DMA(()),
        pltpu.VMEM((2, STRETCH, blocks, 128), F32),
        pltpu.VMEM((8, blocks, STRETCH * PIECE), BF16),
        pltpu.VMEM((8, blocks, STRETCH * PIECE), F32),
        pltpu.VMEM((2, STRETCH * PIECE, SPREAD), BF16),
        pltpu.VMEM((2, STRETCH * PIECE, STRETCH * PIECE), BF16),
        pltpu.VMEM((2, 3 * blocks, STRETCH * PIECE), BF16),
        pltpu.VMEM((2, 3 * blocks, SPREAD), F32),
        pltpu.VMEM((2, blocks, SPREAD), F32),
    ]
    if fused:
        counts_of = [grads[0].shape[-3], 3]
        shapes += [jax.ShapeDtypeStruct((k, PIECE, WIDTH), F32) for k in counts_of]
        scratch += [pltpu.VMEM(block_layout(*mesh_size) + (3, PIECE, WIDTH), BF16)]
        scratch += block_scratch(*mesh_size, counts_of, (PIECE, WIDTH))
        scratch += block_sems(*mesh_size, 2)
    else:
        shapes.append(bf16(groups, 3, PIECE, WIDTH))
    return pl.pallas_call(
        partial(back_kernel, mesh_size),
        grid=(3 * tiles + 2,),
        in_specs=[SMEM_SPEC, SMEM_SPEC]
        + [pl.BlockSpec((TILE, a.shape[1]), index) for a, index in zip(tiled, maps)]
        + [HBM_SPEC]
        + [whole(a.shape) for a in wholes[1:]]
        + [HBM_SPEC] * len(grads),
        out_specs=[pl.BlockSpec((TILE, channels), ending)] + [whole(s.shape) for s in shapes[1:]],
        out_shape=shapes,
        scratch_shapes=scratch,
        compiler_params=params(collective_id),
        name="back",
    )(offsets, counts, *tiled, *wholes, *grads)


def small_gradients(out, gvec1, gvec2, gvec3, gtaps, gmap, gdecay, table_ref):
    out[...] = jnp.zeros_like(out)
    gains = {1: (gvec2, 6), 2: (gvec2, 2), 3: (gvec1, 3), 4: (gvec1, 0), 5: (gvec1, 6)}
    shifts = {1: (gvec2, 7), 2: (gvec2, 3), 3: (gvec1, 4), 4: (gvec1, 1), 5: (gvec1, 7)}
    shifts.update({6: (gvec3, 0), 7: (gvec1, 2), 8: (gvec2, 4), 9: (gvec2, 0), 10: (gvec2, 1)})
    shifts.update({11: (gvec2, 5), 12: (gvec1, 5)})
    for at, (ref, row) in gains.items():
        out[at : at + 1, :] = ref[row : row + 1, :]
    for at, (ref, row) in shifts.items():
        out[6 + at : 7 + at, :] = ref[row : row + 1, :]
    out[TAP_ROW : TAP_ROW + TAPS, :] = gtaps[:TAPS, :]
    log_decay, decay, root, maps_in, maps_out = state_terms(table_ref)
    both = gmap[...] * root
    out[MAP_IN:MAP_OUT, :] = both * maps_out
    out[MAP_OUT:TABLE, :] = both * maps_in
    turn = (1.0 - root * root) / root
    out[RATE:MAP_IN, :] = log_decay * (
        gdecay[...] * decay - gmap[...] * maps_in * maps_out * turn
    )


def store_cols(out, at, value):
    groups = value.shape[0] // PIECE
    out[:, at] = value.reshape((groups, PIECE, WIDTH))


def tail_kernel(mesh_size, *refs):
    fused = mesh_size is not None
    refs = list(refs)
    take = lambda count: [refs.pop(0) for _ in range(count)]
    x_ref, h_ref, gx1_ref, up_ref, up2_ref, down_ref, table_ref = take(7)
    hidden = 4 * WIDTH
    if fused:
        gvec1, gvec2, gtaps, gmap, gdecay, gbias1 = take(6)
        sources = take(1)
        gx_ref, last_out = take(2)
        reduced = take(4)
    else:
        gx_ref, gvec_out, gbias_out, up_out, down_out = take(5)
    turn_scr, grad_scr, gh_scr, vec_acc, bias_scr = take(5)
    step = pl.program_id(0)
    frames, channels = x_ref.shape
    chunks = hidden // WIDTH
    tiles = frames // TILE
    first_b, first_c = 1 + chunks, 1 + 2 * chunks
    schedule = {}
    if fused:
        n_dp, n_fs = mesh_size
        down_src, left_src, right_src, small_scr, gvec3 = take(5)
        dp, fs = lax.axis_index("dp"), lax.axis_index("fsdp")
        place = Place(dp, fs, n_dp, n_fs)
        scratch = take(4 * (2 + place.count))
        sems = take(3)
        swap = take(4)
        down_out = flat_groups(down_src)
        halves = (flat_groups(left_src), flat_groups(right_src))

        def emit(chunk, total):
            reduced[chunk][...] = total

        plans, sends = block_scatter(
            place, sources + [down_src, left_src, right_src], emit, scratch, *sems
        )
        begins = [
            (0, 2, 4, 7, first_c),
            (first_b, first_b + 1, first_b + 3, first_c + 1, first_c + tiles),
            (first_b + 2, first_c, first_c + 1, first_c + 2, first_c + tiles),
            (first_c, first_c + 1, first_c + 2, first_c + tiles, first_c + tiles),
        ]
        for chunk, steps in enumerate(begins):
            for stage, at in enumerate(steps):
                schedule.setdefault(at, []).append((stage, chunk))
    last_step = first_c + tiles - 1

    def progress(at):
        for stage, chunk in sorted(schedule.get(at, [])):
            plans[chunk][stage]()

    @pl.when(step == 0)
    def _():
        if fused:
            greet(dp, fs, n_dp, n_fs)
        progress(0)
        vec_acc[...] = jnp.zeros_like(vec_acc)

        def first(rows):
            e, _ = norm_parts(x_ref[rows, :].astype(F32))
            low = (e * table_ref[0:1, :] + table_ref[6:7, :]).astype(BF16)
            turn_scr[:, rows] = low.T
            grad = (0.5 * gx1_ref[rows, :]).astype(BF16)
            grad_scr[rows, :] = grad
            vec_acc[0] += fold8(grad.astype(F32))

        by_rows(first, frames)

    if fused:
        for at in range(1, last_step + 1):
            if at in schedule and at != first_c:

                @pl.when(step == at)
                def _(at=at):
                    progress(at)

    @pl.when((step >= 1) & (step < first_b))
    def _():
        h = h_ref[...].astype(F32)
        active = (h * sigmoid(h)).astype(BF16)
        value = dot_tn(active, grad_scr[...]).astype(BF16)
        groups = WIDTH // (4 * PIECE)
        down_out[pl.ds((step - 1) * groups, groups)] = value.reshape((groups, 4, PIECE, WIDTH))

    def second_half(c, store):
        cols = columns(c, WIDTH)
        h = h_ref[...].astype(F32)
        sig = sigmoid(h)
        gate = dot_nt(grad_scr[...], rows_of(down_ref, 0, c))
        grad_h = (gate * (sig * (1.0 + h * (1.0 - sig)))).astype(BF16)
        gh_scr[:, cols] = grad_h
        sums = jnp.sum(fold8(grad_h.astype(F32)), axis=0, keepdims=True)
        bias_scr[pl.ds(2 * c, 1), :] = sums[:, :CHUNK]
        bias_scr[pl.ds(2 * c + 1, 1), :] = sums[:, CHUNK:]
        store(dot_nn(turn_scr[...], grad_h).astype(BF16))

    if fused:
        for half in range(2):
            begin = first_b + half * (chunks // 2)

            @pl.when((step >= begin) & (step < begin + chunks // 2))
            def _(half=half, begin=begin):
                def store(value):
                    store_cols(halves[half], step - begin, value)

                second_half(step - first_b, store)

    else:

        @pl.when((step >= first_b) & (step < first_c))
        def _():
            def store(value):
                store_cols(up_out, step - first_b, value)

            second_half(step - first_b, store)

    if fused:

        @pl.when(step == first_c)
        def _():
            gvec3[0:1, :] = jnp.sum(vec_acc[0], axis=0, keepdims=True)
            small_gradients(small_scr, gvec1, gvec2, gvec3, gtaps, gmap, gdecay, table_ref)
            narrow = small_scr[...].T.astype(BF16)
            devices = n_dp * n_fs
            small_out = halves[1]
            small_out[:, 2, :, :CHUNK] = narrow.reshape((devices, PIECE, CHUNK))
            for c in range(8):
                bias_scr[8 + c : 9 + c, :] = gbias1[0:1, c * CHUNK : c * CHUNK + CHUNK]
            bias = bias_scr[...].astype(BF16)
            small_out[:, 2, :, CHUNK:] = jnp.broadcast_to(bias[None], (devices, PIECE, CHUNK))
            progress(first_c)

    @pl.when(step >= first_c)
    def _():
        tile = step - first_c
        whole_tile = pl.ds(pl.multiple_of(tile * TILE, TILE), TILE)
        total = dot_nt(gh_scr[whole_tile, :WIDTH], square_of(up_ref, 1))
        later = [square_of(up_ref, 2), square_of(up2_ref, 0), square_of(up2_ref, 1)]
        for k in range(1, hidden // WIDTH):
            cols = slice(k * WIDTH, k * WIDTH + WIDTH)
            total = total + dot_nt(gh_scr[whole_tile, cols], later[k - 1])
        gx_ref[...] = total

        def second(rows):
            here = pl.ds(pl.multiple_of(tile * TILE + rows.start, ROWS), ROWS)
            e, inv = norm_parts(x_ref[here, :].astype(F32))
            grad = gx_ref[rows, :]
            vec_acc[1] += fold8(grad * e)
            vec_acc[2] += fold8(grad)
            gx_ref[rows, :] = gx1_ref[here, :] + norm_back(grad, e, inv, table_ref[0:1, :])

        by_rows(second)

    @pl.when(step == last_step)
    def _():
        if fused:
            last_out[...] = jnp.zeros_like(last_out)
            for k in range(2):
                last_out[k : k + 1, :] = jnp.sum(vec_acc[1 + k], axis=0, keepdims=True)
            ends = sorted(schedule.get(last_step + 1, []))

            def between():
                for stage, chunk in ends:
                    plans[chunk][stage]()

            last_out[...] = sum_over(last_out[...], dp, fs, n_dp, n_fs, *swap, between=between)
            for wait in sends:
                wait()
        else:
            gvec_out[...] = jnp.zeros_like(gvec_out)
            for k in range(3):
                gvec_out[k : k + 1, :] = jnp.sum(vec_acc[k], axis=0, keepdims=True)
            gbias_out[...] = bias_scr[...]


def tail(mesh_size, x, h, gx1, up, up2, down, table, others=(), grads=(), collective_id=None):
    fused = mesh_size is not None
    frames, channels = x.shape
    hidden = h.shape[1]
    tiles, chunks = frames // TILE, hidden // WIDTH
    first_b, first_c = 1 + chunks, 1 + 2 * chunks
    place = lambda i: jnp.where(
        i < first_b, jnp.maximum(i - 1, 0), jnp.minimum(i - first_b, chunks - 1)
    )
    shapes = [jax.ShapeDtypeStruct((frames, channels), F32)]
    scratch = [
        pltpu.VMEM((channels, frames), BF16),
        pltpu.VMEM((frames, channels), BF16),
        pltpu.VMEM((frames, hidden), BF16),
        pltpu.VMEM((8, 8, channels), F32),
        pltpu.VMEM((16, CHUNK), F32),
    ]
    if fused:
        own = [4, 2, 3]
        counts = [g.shape[-3] for g in grads] + own
        shapes.append(jax.ShapeDtypeStruct((8, channels), F32))
        shapes += [jax.ShapeDtypeStruct((k, PIECE, WIDTH), F32) for k in counts]
        layout = block_layout(*mesh_size)
        scratch += [pltpu.VMEM(layout + (k, PIECE, WIDTH), BF16) for k in own]
        scratch += [pltpu.VMEM((256, channels), F32), pltpu.VMEM((8, channels), F32)]
        scratch += block_scratch(*mesh_size, counts, (PIECE, WIDTH))
        scratch += block_sems(*mesh_size, len(counts))
        scratch += swap_scratch(*mesh_size, channels)
    else:
        shapes += [
            jax.ShapeDtypeStruct((8, channels), F32),
            jax.ShapeDtypeStruct((16, CHUNK), F32),
            jax.ShapeDtypeStruct((channels // PIECE, 4, PIECE, WIDTH), BF16),
            jax.ShapeDtypeStruct((channels // PIECE, 4, PIECE, WIDTH), BF16),
        ]
    return pl.pallas_call(
        partial(tail_kernel, mesh_size),
        grid=(first_c + tiles,),
        in_specs=[whole(x.shape), pl.BlockSpec((frames, WIDTH), lambda i: (0, place(i)))]
        + [whole(a.shape) for a in (gx1, up, up2, down, table) + tuple(others)]
        + [pl.BlockSpec(memory_space=pltpu.HBM)] * len(grads),
        out_specs=[
            pl.BlockSpec((TILE, channels), lambda i: (jnp.maximum(i - first_c, 0), 0))
        ]
        + [whole(s.shape) for s in shapes[1:]],
        out_shape=shapes,
        scratch_shapes=scratch,
        compiler_params=params(collective_id),
        name="tail",
    )(x, h, gx1, up, up2, down, table, *others, *grads)


def unpack_kernel(
    place_ref,
    second_ref,
    middle_ref,
    mixin_ref,
    down_ref,
    left_ref,
    right_ref,
    last_ref,
    up_out,
    down_out,
    bias_out,
    mixin_out,
    mixout_out,
    convin_out,
    convout_out,
    convbias_out,
    rate_out,
    map_out,
    taps_out,
    gains_out,
    shifts_out,
):
    mine = place_ref[0]
    for k in range(4):
        cols = slice(k * WIDTH, k * WIDTH + WIDTH)
        rows = slice(k * PIECE, k * PIECE + PIECE)
        up_out[0, :, cols] = (left_ref if k < 2 else right_ref)[k % 2]
        up_out[1, :, cols] = second_ref[1 + k]
        down_out[0, rows, :] = down_ref[k]
        down_out[1, rows, :] = second_ref[5 + k]
    convout_out[...] = second_ref[0]
    mixout_out[...] = middle_ref[0]
    for k in range(2):
        cols = slice(k * WIDTH, k * WIDTH + WIDTH)
        mixin_out[:, cols] = mixin_ref[k]
        convin_out[:, cols] = middle_ref[1 + k]
    count = bias_out.shape[1]
    row = (mine * count) // CHUNK
    inner = mine * count - row * CHUNK
    for layer in range(2):
        line = right_ref[2, pl.ds(8 * layer + row, 1), CHUNK:]
        line = pltpu.roll(jnp.broadcast_to(line, (8, CHUNK)), CHUNK - inner, 1)
        bias_out[layer : layer + 1, :] = line[0:1, :count]
    channels = last_ref.shape[1]
    first = pltpu.roll(last_ref[...], channels - mine * PIECE, 1)[:, :PIECE]
    small = right_ref[2, :, :CHUNK]
    turned = small.T
    gains_out[...] = turned[0:6, :]
    gains_out[0:1, :] = first[0:1, :]
    shifts_out[...] = turned[6:18, :]
    shifts_out[0:1, :] = first[1:2, :]
    convbias_out[...] = turned[18:19, :]
    taps_out[...] = turned[TAP_ROW : TAP_ROW + TAPS, :]
    rate_out[...] = small[:, RATE:MAP_IN]
    map_out[0] = small[:, MAP_IN:MAP_OUT]
    map_out[1] = small[:, MAP_OUT:TABLE]


def unpack(mine, arrays, hidden):
    channels = arrays[-1].shape[1]
    devices = channels // PIECE
    f32 = lambda *shape: jax.ShapeDtypeStruct(shape, F32)
    vmem = pl.BlockSpec(memory_space=pltpu.VMEM)
    return pl.pallas_call(
        unpack_kernel,
        in_specs=[SMEM_SPEC] + [vmem] * len(arrays),
        out_specs=[vmem] * 13,
        out_shape=[
            f32(2, PIECE, hidden),
            f32(2, hidden // devices, channels),
            f32(2, hidden // devices),
            f32(PIECE, 2 * WIDTH),
            f32(PIECE, WIDTH),
            f32(PIECE, 2 * WIDTH),
            f32(PIECE, WIDTH),
            f32(1, PIECE),
            f32(PIECE, STATES),
            f32(2, PIECE, STATES),
            f32(TAPS, PIECE),
            f32(6, PIECE),
            f32(12, PIECE),
        ],
        name="unpack",
    )(mine, *arrays)


def pack_table(gains, shifts, conv_bias, taps, rate, maps):
    channels = gains.shape[1]
    blank = lambda rows: jnp.zeros((rows, channels), gains.dtype)
    parts = [gains, shifts, conv_bias[None], blank(TAP_ROW - 19), taps, blank(RATE - TAP_ROW - TAPS)]
    parts += [rate, maps[0], maps[1], blank(256 - TABLE)]
    return jnp.concatenate(parts, axis=0).T


def pack_bias(bias, place):
    layers, count = bias.shape
    hidden = 16 * CHUNK // layers
    wide = lax.dynamic_update_slice(
        jnp.zeros((layers, hidden), bias.dtype), bias, (0, place * count)
    )
    return wide.reshape((16, CHUNK))


def unpack_table(table):
    return (
        table[0:6],
        table[6:18],
        table[18],
        table[TAP_ROW : TAP_ROW + TAPS],
        table[RATE:MAP_IN],
        jnp.stack([table[MAP_IN:MAP_OUT], table[MAP_OUT:TABLE]]),
    )


def on_device(
    n_dp,
    n_fs,
    frames,
    seq_lengths,
    seq_offsets,
    seq_counts,
    ffn_up,
    ffn_down,
    ffn_bias_up,
    mix_in,
    mix_out,
    conv_in,
    conv_out,
    conv_out_bias,
    ssm_rate,
    ssm_map,
    conv_kernel,
    gains,
    shifts,
    cotangent,
):
    devices = n_dp * n_fs
    mine = lax.axis_index("dp") * n_fs + lax.axis_index("fsdp")
    frames_dev, channels = frames.shape
    hidden = ffn_up.shape[2]
    if channels // devices == PIECE:
        size = (n_dp, n_fs)
        small = [
            ffn_bias_up,
            gains,
            shifts,
            conv_out_bias[None],
            conv_kernel,
            ssm_rate.T,
            ssm_map.transpose((0, 2, 1)),
        ]
        weights = [ffn_up, ffn_down, mix_in, mix_out, conv_in, conv_out]
        made = front(size, seq_offsets, seq_counts, frames, small, weights, hidden, 1)
        h0, x1, v, y, gated, x2, p, u, w, stat, table, bias, *mixing = made[:17]
        groups = lambda g: g.reshape((devices,) + g.shape[-3:])
        places = lambda g: g.reshape(block_layout(n_dp, n_fs) + g.shape[1:])
        first, extra, second, third, mixed, fourth = [groups(g) for g in made[17:]]
        result, gx3, gnb, grads, gbias1, gvec1, stat = middle(
            size, x2, w, cotangent, fourth, bias, table, stat, hidden, 2
        )
        gx1, grads2, gvec2, gtaps, gmap, gdecay, reduced, reduced2 = back(
            size,
            seq_offsets,
            seq_counts,
            [w, gnb, p, x2, gx3, gated, y, v, x1],
            [u] + mixing + [third, mixed, table, stat],
            (places(grads),),
            3,
        )
        others = (gvec1, gvec2, gtaps, gmap, gdecay, gbias1)
        gx, last, *late = tail(
            size, frames, h0, gx1, first, extra, second, table, others, (places(grads2),), 4
        )
        made = unpack(mine.reshape((1,)), [reduced, reduced2] + late + [last], hidden)
        made = list(made)
        made[7] = made[7].reshape((-1,))
        made[8] = made[8].T
        made[9] = made[9].transpose((0, 2, 1))
        return (result, gx) + tuple(made)

    small = pack_table(gains, shifts, conv_out_bias, conv_kernel, ssm_rate, ssm_map)
    got = gather_all(
        n_dp,
        n_fs,
        [
            small[None],
            pack_bias(ffn_bias_up, mine)[None],
            ffn_up,
            ffn_down,
            mix_in[None],
            mix_out[None],
            conv_in[None],
            conv_out[None],
        ],
        1,
    )
    matrix = lambda g: g.reshape((-1, g.shape[-1]))
    table, _, up0, up1, down0, down1, mixin, mixout, convin, convout = [matrix(g) for g in got]
    table = table.astype(F32).T[:TABLE]
    bias = jnp.sum(got[1].astype(F32), axis=0)
    group_count = channels // PIECE
    cut = lambda g: g.reshape((group_count, PIECE, -1, WIDTH)).transpose((0, 2, 1, 3))
    tall = lambda g: g.reshape((group_count, -1, PIECE, WIDTH))
    join = lambda g: g.transpose((0, 2, 1, 3)).reshape((channels, -1))
    blank = jnp.pad(matrix(got[0]), ((0, 0), (0, WIDTH - 256))).reshape((group_count, 1, PIECE, WIDTH))
    extra = cut(up0)
    first, extra = jnp.concatenate([blank, extra[:, :2]], axis=1), extra[:, 2:]
    third = cut(mixin)
    mixed = jnp.concatenate([cut(mixout), cut(convin)], axis=1)
    fourth = jnp.concatenate([cut(convout), cut(up1), tall(down1)], axis=1)
    made = front(
        None, seq_offsets, seq_counts, frames, [table, bias], [first, extra, tall(down0), third, mixed], hidden
    )
    h0, x1, v, y, gated, x2, p, u, w, stat, table, bias, *mixing = made
    pool = exchange(n_dp, n_fs, stat, frames_dev, 2, pool_kernel)
    scale = lax.rsqrt(pool[1:2] / (frames_dev * devices) + EPSILON)
    stat = jnp.concatenate([pool[0:1], scale, jnp.zeros((6, channels), F32)])
    result, gx3, gnb, grads, gbias1, gvec1, stat = middle(
        None, x2, w, cotangent, fourth, bias, table, stat, hidden
    )
    sums = exchange(n_dp, n_fs, gvec1, 1, 4, total_kernel)[6:8]
    sums = sums * (table[5:6] / (frames_dev * devices))
    stat = jnp.concatenate([stat[0:2], sums[1:2], sums[0:1], stat[4:8]])
    gx1, grads2, gvec2, gtaps, gmap, gdecay, grads3 = back(
        None,
        seq_offsets,
        seq_counts,
        [w, gnb, p, x2, gx3, gated, y, v, x1],
        [u] + mixing + [third, mixed, table, stat],
    )
    gx, gvec3, gbias0, gup0, gdown0 = tail(None, frames, h0, gx1, first, extra, tall(down0), table)

    def weights_of(log_rate, maps):
        log_decay = -jnp.exp(log_rate)
        root = jnp.sqrt(-jnp.expm1(2.0 * log_decay))
        return jnp.exp(log_decay), maps[0] * root * maps[1]

    rate, maps = unpack_table(table)[4:]
    rate_grad, map_grad = jax.vjp(weights_of, rate, maps)[1]((gdecay, gmap))
    gain_grad = jnp.stack([gvec3[1], gvec2[6], gvec2[2], gvec1[3], gvec1[0], gvec1[6]])
    rows = [gvec3[2], gvec2[7], gvec2[3], gvec1[4], gvec1[1], gvec1[7], gvec3[0], gvec1[2]]
    rows += [gvec2[4], gvec2[0], gvec2[1], gvec2[5]]
    small_grad = pack_table(
        gain_grad, jnp.stack(rows), gvec1[5], gtaps[:TAPS], rate_grad, map_grad
    )
    bias_grad = jnp.concatenate([gbias0[:8], gbias1[0].reshape((8, CHUNK))])
    wide = lambda g: g.reshape((devices, g.shape[0] // devices, g.shape[1]))
    reduced = scatter_all(
        n_dp,
        n_fs,
        [
            wide(join(grads[:, 1:5])),
            wide(matrix(grads[:, 5:9])),
            wide(join(grads[:, 0:1])),
            wide(join(grads3[:, 1:3])),
            wide(join(grads3[:, 0:1])),
            wide(join(grads2[:, 0:2])),
            wide(join(gup0)),
            wide(matrix(gdown0)),
            wide(small_grad.astype(BF16)),
            jnp.broadcast_to(bias_grad.astype(BF16), (devices, PIECE, CHUNK)),
        ],
        5,
    )
    gains_grad, shifts_grad, conv_bias_grad, taps_grad, rate_grad, map_grad = unpack_table(
        reduced[8].T
    )
    bias_grad = reduced[9].reshape((2, -1))
    count = bias_grad.shape[1] // devices
    bias_grad = lax.dynamic_slice(bias_grad, (0, mine * count), (2, count))
    return (
        result,
        gx,
        jnp.stack([reduced[6], reduced[0]]),
        jnp.stack([reduced[7], reduced[1]]),
        bias_grad,
        reduced[5],
        reduced[4],
        reduced[3],
        reduced[2],
        conv_bias_grad,
        rate_grad,
        map_grad,
        taps_grad,
        gains_grad,
        shifts_grad,
    )


def solution(mesh):
    both = ("dp", "fsdp")
    row, row1 = P(both, None), P(both)
    col, col3, mid = P(None, both), P(None, None, both), P(None, both, None)
    in_specs = (
        row,
        row,
        row,
        row1,
        mid,
        mid,
        col,
        row,
        row,
        row,
        row,
        row1,
        col,
        col3,
        col,
        col,
        col,
        row,
    )
    out_specs = (row, row, mid, mid, col, row, row, row, row, row1, col, col3, col, col, col)
    return jax.shard_map(
        partial(on_device, mesh.shape["dp"], mesh.shape["fsdp"]),
        mesh=mesh,
        in_specs=in_specs,
        out_specs=out_specs,
        check_vma=False,
    )
```

```python
import itertools
from functools import partial

import jax
import jax.numpy as jnp
from jax import lax
from jax.experimental import pallas as pl
from jax.experimental.pallas import tpu as pltpu
from jax.sharding import PartitionSpec as P

MESH = pl.DeviceIdType.MESH
BF16 = jnp.bfloat16
F32 = jnp.float32


def flip(index, bit):
    return index + bit * (1 - 2 * lax.rem(lax.div(index, bit), 2))


def flip_all(index, bits):
    for bit in bits:
        index = flip(index, bit)
    return index


def combos(bits):
    found = [()]
    for bit in bits:
        found = found + [entry + (bit,) for entry in found]
    return found


def plan_bits(n_dp):
    bits, bit = [], 2
    while bit < n_dp:
        bits.append(bit)
        bit *= 2
    return tuple(bits)


def greet(dp, fs, n_dp, n_fs):
    barrier = pltpu.get_barrier_semaphore()
    for step in range(1, n_dp):
        pl.semaphore_signal(
            barrier, inc=1, device_id=(lax.rem(dp + step, n_dp), fs), device_id_type=MESH
        )
    for step in range(1, n_fs):
        pl.semaphore_signal(
            barrier, inc=1, device_id=(dp, lax.rem(fs + step, n_fs)), device_id_type=MESH
        )
    pl.semaphore_wait(barrier, n_dp + n_fs - 2)


def gather_plan(dp, fs, n_dp, n_fs, sources, outs, send_sem, recv_sem, local_sem):
    bits = plan_bits(n_dp)
    orders = (bits, bits[::-1])
    half = n_fs // 2
    sends = []

    def stages(chunk):
        src, out = sources[chunk], outs[chunk]
        slots = itertools.count()

        def zone(where, part):
            if part is None:
                return out.at[pl.ds(where * n_fs, n_fs)]
            return out.at[pl.ds(where * n_fs + part * half, half)]

        def remote(slot, view_from, view_to, device):
            return pltpu.make_async_remote_copy(
                src_ref=view_from,
                dst_ref=view_to,
                send_sem=send_sem.at[chunk, slot],
                recv_sem=recv_sem.at[chunk, slot],
                device_id=device,
                device_id_type=MESH,
            )

        def launch(make):
            make().start()
            sends.append(lambda: make().wait_send())

        z_slots = [next(slots) for _ in range(1, n_fs)]

        def own_copy():
            return pltpu.make_async_copy(src, out.at[dp * n_fs + fs], local_sem.at[chunk])

        def start():
            own_copy().start()
            for step in range(1, n_fs):
                launch(
                    lambda step=step: remote(
                        z_slots[step - 1],
                        src,
                        out.at[dp * n_fs + fs],
                        (dp, lax.rem(fs + step, n_fs)),
                    )
                )

        def wait_z():
            own_copy().wait()
            for step in range(1, n_fs):
                origin = dp * n_fs + lax.rem(fs + n_fs - step, n_fs)
                remote(z_slots[step - 1], src, out.at[origin], (dp, fs)).wait_recv()

        steps, before = [start], wait_z
        for depth in range(len(bits)):
            plan = []
            for part, order in enumerate(orders):
                for entry in combos(order[:depth]):
                    plan.append((next(slots), part, order[depth], entry))

            def view(slot, part, bit, entry, arrived):
                where = flip_all(flip(dp, bit) if arrived else dp, entry)
                return remote(slot, zone(where, part), zone(where, part), (flip(dp, bit), fs))

            def go(plan=plan, before=before, view=view):
                before()
                for item in plan:
                    launch(lambda item=item: view(*item, False))

            def arrive(plan=plan, view=view):
                for item in plan:
                    view(*item, True).wait_recv()

            steps.append(go)
            before = arrive
        last = [(next(slots), entry) for entry in combos(bits)]

        def across(slot, entry, arrived):
            where = flip_all(flip(dp, 1) if arrived else dp, entry)
            return remote(slot, zone(where, None), zone(where, None), (flip(dp, 1), fs))

        def cross(before=before):
            before()
            for item in last:
                launch(lambda item=item: across(*item, False))

        def finish():
            for item in last:
                across(*item, True).wait_recv()

        return steps + [cross, finish]

    return [stages(chunk) for chunk in range(len(outs))], sends


def waves(plans):
    depth = len(plans[0])
    out = []
    for wave in range(len(plans) + depth - 1):
        out.append(
            [plans[c][wave - c] for c in range(len(plans)) if 0 <= wave - c < depth]
        )
    return out


def gather_kernel(n_dp, n_fs, layers, *refs):
    n_in = len(layers)
    n_out = sum(layers)
    ins, outs = refs[:n_in], refs[n_in : n_in + n_out]
    send_sem, recv_sem, local_sem = refs[n_in + n_out :]
    sources = []
    for ref, count in zip(ins, layers):
        sources += [ref.at[layer] for layer in range(count)]
    dp, fs = lax.axis_index("dp"), lax.axis_index("fsdp")
    greet(dp, fs, n_dp, n_fs)
    plans, sends = gather_plan(dp, fs, n_dp, n_fs, sources, outs, send_sem, recv_sem, local_sem)
    for wave in waves(plans):
        for stage in wave:
            stage()
    for wait in sends:
        wait()


def slot_count(n_dp, n_fs):
    nb = len(plan_bits(n_dp))
    return n_fs - 1 + 2 * (2**nb - 1) + 2**nb


def gather_all(n_dp, n_fs, arrays, collective_id):
    layers = tuple(a.shape[0] for a in arrays)
    outs = []
    for a in arrays:
        outs += [jax.ShapeDtypeStruct((n_dp * n_fs,) + a.shape[1:], a.dtype)] * a.shape[0]
    count = slot_count(n_dp, n_fs)
    return pl.pallas_call(
        partial(gather_kernel, n_dp, n_fs, layers),
        out_shape=outs,
        in_specs=[pl.BlockSpec(memory_space=pltpu.HBM)] * len(arrays),
        out_specs=[pl.BlockSpec(memory_space=pltpu.HBM)] * len(outs),
        scratch_shapes=[
            pltpu.SemaphoreType.DMA((len(outs), count)),
            pltpu.SemaphoreType.DMA((len(outs), count)),
            pltpu.SemaphoreType.DMA((len(outs),)),
        ],
        compiler_params=pltpu.CompilerParams(collective_id=collective_id, has_side_effects=True),
        name="gather_parameters",
    )(*arrays)


def scatter_plan(dp, fs, n_dp, n_fs, ins, emit, scratch, send_sem, recv_sem, local_sem, first=0):
    bits = plan_bits(n_dp)
    orders = (bits[::-1], bits)
    half = n_fs // 2
    index = {entry: at for at, entry in enumerate(combos(bits))}
    sends = []

    def add_into(kept, other):
        def body(at, _):
            kept[at] = (kept[at].astype(F32) + other[at].astype(F32)).astype(BF16)
            return 0

        lax.fori_loop(0, kept.shape[0], body, 0)

    def stages(chunk):
        src = ins[chunk]
        cross_in, own, later, last = scratch[4 * chunk : 4 * chunk + 4]
        slots = itertools.count()

        def remote(slot, view_from, view_to, device):
            return pltpu.make_async_remote_copy(
                src_ref=view_from,
                dst_ref=view_to,
                send_sem=send_sem.at[first + chunk, slot],
                recv_sem=recv_sem.at[first + chunk, slot],
                device_id=device,
                device_id_type=MESH,
            )

        def launch(make):
            make().start()
            sends.append(lambda: make().wait_send())

        def zone(entry, crossed):
            return src.at[pl.ds(flip_all(flip(dp, 1) if crossed else dp, entry) * n_fs, n_fs)]

        pieces = [(next(slots), entry, index[entry]) for entry in combos(bits)]

        def load(entry, at):
            return pltpu.make_async_copy(
                zone(entry, False), own.at[at], local_sem.at[first + chunk, at]
            )

        def across(slot, entry, at):
            return remote(slot, zone(entry, True), cross_in.at[at], (flip(dp, 1), fs))

        def start():
            for item in pieces:
                launch(lambda item=item: across(*item))
            for _, entry, at in pieces:
                load(entry, at).start()

        def fold_cross():
            for slot, entry, at in pieces:
                load(entry, at).wait()
                across(slot, entry, at).wait_recv()
                add_into(own.at[at], cross_in.at[at])

        steps, before = [start], fold_cross
        used = 0
        for depth in range(len(bits)):
            plan = []
            for part, order in enumerate(orders):
                bit, gone = order[depth], order[:depth]
                for entry in combos(bits):
                    if not (set(entry) & set(gone)) and bit not in entry:
                        away = tuple(sorted(entry + (bit,)))
                        plan.append((next(slots), part, bit, index[away], index[entry], used))
                        used += 1

            def move(slot, part, bit, away, kept, place):
                return remote(
                    slot,
                    own.at[away, pl.ds(part * half, half)],
                    later.at[place],
                    (flip(dp, bit), fs),
                )

            def go(plan=plan, before=before, move=move):
                before()
                for item in plan:
                    launch(lambda item=item: move(*item))

            def fold(plan=plan, move=move):
                for item in plan:
                    move(*item).wait_recv()
                    _, part, _, _, kept, place = item
                    add_into(own.at[kept, pl.ds(part * half, half)], later.at[place])

            steps.append(go)
            before = fold
        z_slots = [next(slots) for _ in range(1, n_fs)]

        def along(step):
            to = lax.rem(fs + step, n_fs)
            return remote(z_slots[step - 1], own.at[0, to], last.at[step - 1], (dp, to))

        def spread(before=before):
            before()
            for step in range(1, n_fs):
                launch(lambda step=step: along(step))

        def finish():
            total = own[0, fs].astype(F32)
            for step in range(1, n_fs):
                along(step).wait_recv()
                total = total + last[step - 1].astype(F32)
            emit(chunk, total)

        return steps + [spread, finish]

    return [stages(chunk) for chunk in range(len(ins))], sends


def scatter_scratch(n_dp, n_fs, tails):
    pieces = 2 ** len(plan_bits(n_dp))
    scratch = []
    for tail in tails:
        scratch += [
            pltpu.VMEM((pieces, n_fs) + tail, BF16),
            pltpu.VMEM((pieces, n_fs) + tail, BF16),
            pltpu.VMEM((2 * (pieces - 1), n_fs // 2) + tail, BF16),
            pltpu.VMEM((n_fs - 1,) + tail, BF16),
        ]
    return scratch


def scatter_sems(n_dp, n_fs, chunks):
    count = slot_count(n_dp, n_fs)
    return [
        pltpu.SemaphoreType.DMA((chunks, count)),
        pltpu.SemaphoreType.DMA((chunks, count)),
        pltpu.SemaphoreType.DMA((chunks, 2 ** len(plan_bits(n_dp)))),
    ]


def scatter_kernel(n_dp, n_fs, n_chunks, *refs):
    ins, outs = refs[:n_chunks], refs[n_chunks : 2 * n_chunks]
    scratch = refs[2 * n_chunks : 6 * n_chunks]
    dp, fs = lax.axis_index("dp"), lax.axis_index("fsdp")
    greet(dp, fs, n_dp, n_fs)

    def emit(chunk, total):
        outs[chunk][...] = total

    plans, sends = scatter_plan(dp, fs, n_dp, n_fs, ins, emit, scratch, *refs[6 * n_chunks :])
    for wave in waves(plans):
        for stage in wave:
            stage()
    for wait in sends:
        wait()


def scatter_all(n_dp, n_fs, arrays, collective_id):
    n = len(arrays)
    return pl.pallas_call(
        partial(scatter_kernel, n_dp, n_fs, n),
        out_shape=[jax.ShapeDtypeStruct(a.shape[1:], F32) for a in arrays],
        in_specs=[pl.BlockSpec(memory_space=pltpu.HBM)] * n,
        out_specs=[pl.BlockSpec(memory_space=pltpu.VMEM)] * n,
        scratch_shapes=scatter_scratch(n_dp, n_fs, [a.shape[1:] for a in arrays])
        + scatter_sems(n_dp, n_fs, n),
        compiler_params=pltpu.CompilerParams(
            collective_id=collective_id, has_side_effects=True, vmem_limit_bytes=48 << 20
        ),
        name="scatter_gradients",
    )(*arrays)


def swap_copy(axis, place, count, buffer, send_sem, recv_sem, step):
    return pltpu.make_async_remote_copy(
        src_ref=buffer.at[0],
        dst_ref=buffer.at[step],
        send_sem=send_sem.at[step],
        recv_sem=recv_sem.at[step],
        device_id={axis: lax.rem(place + step, count)},
        device_id_type=MESH,
    )


def swap_start(axis, place, count, *rest):
    for step in range(1, count):
        swap_copy(axis, place, count, *rest, step).start()


def swap_wait(axis, place, count, *rest):
    for step in range(1, count):
        swap_copy(axis, place, count, *rest, step).wait_recv()
    for step in range(1, count):
        swap_copy(axis, place, count, *rest, step).wait_send()


def swap_rows(*args):
    swap_start(*args)
    swap_wait(*args)


def sum_over(x, dp, fs, n_dp, n_fs, octet, line, send_sem, recv_sem, between=None):
    first = ("dp", dp, n_dp, octet, send_sem.at[0], recv_sem.at[0])
    octet[0] = x
    swap_start(*first)
    if between is not None:
        between()
    swap_wait(*first)
    total = octet[0]
    for step in range(1, n_dp):
        total = total + octet[step]
    line[0] = total
    swap_rows("fsdp", fs, n_fs, line, send_sem.at[1], recv_sem.at[1])
    total = line[0]
    for step in range(1, n_fs):
        total = total + line[step]
    return total


def pooled(buffer, count, weight):
    means = [buffer[k, 0:1, :] for k in range(count)]
    center = sum(means[1:], means[0]) * (1.0 / count)
    spread = buffer[0, 1:2, :]
    for k in range(1, count):
        spread = spread + buffer[k, 1:2, :]
    off = (means[0] - center) * (means[0] - center)
    for mean in means[1:]:
        off = off + (mean - center) * (mean - center)
    return center, spread + weight * off


def pool_over(center, spread, frames, dp, fs, n_dp, n_fs, octet, line, send_sem, recv_sem):
    octet[0] = jnp.zeros(octet.shape[1:], F32)
    line[0] = jnp.zeros(line.shape[1:], F32)
    octet[0, 0:1, :] = center
    octet[0, 1:2, :] = spread
    swap_rows("dp", dp, n_dp, octet, send_sem.at[0], recv_sem.at[0])
    center, spread = pooled(octet, n_dp, float(frames))
    line[0, 0:1, :] = center
    line[0, 1:2, :] = spread
    swap_rows("fsdp", fs, n_fs, line, send_sem.at[1], recv_sem.at[1])
    return pooled(line, n_fs, float(frames * n_dp))


def swap_scratch(n_dp, n_fs, channels):
    return [
        pltpu.VMEM((n_dp, 8, channels), F32),
        pltpu.VMEM((n_fs, 8, channels), F32),
        pltpu.SemaphoreType.DMA((2, max(n_dp, n_fs))),
        pltpu.SemaphoreType.DMA((2, max(n_dp, n_fs))),
    ]


def pool_kernel(n_dp, n_fs, frames, x_ref, out_ref, octet, line, send_sem, recv_sem):
    dp, fs = lax.axis_index("dp"), lax.axis_index("fsdp")
    greet(dp, fs, n_dp, n_fs)
    octet[0] = x_ref[...]
    center, spread = pool_over(
        x_ref[0:1, :], x_ref[1:2, :], frames, dp, fs, n_dp, n_fs, octet, line, send_sem, recv_sem
    )
    out_ref[...] = x_ref[...]
    out_ref[0:1, :] = center
    out_ref[1:2, :] = spread


def total_kernel(n_dp, n_fs, frames, x_ref, out_ref, octet, line, send_sem, recv_sem):
    dp, fs = lax.axis_index("dp"), lax.axis_index("fsdp")
    greet(dp, fs, n_dp, n_fs)
    out_ref[...] = sum_over(x_ref[...], dp, fs, n_dp, n_fs, octet, line, send_sem, recv_sem)


def exchange(n_dp, n_fs, x, frames, collective_id, kernel):
    return pl.pallas_call(
        partial(kernel, n_dp, n_fs, frames),
        out_shape=jax.ShapeDtypeStruct(x.shape, F32),
        in_specs=[pl.BlockSpec(memory_space=pltpu.VMEM)],
        out_specs=pl.BlockSpec(memory_space=pltpu.VMEM),
        scratch_shapes=swap_scratch(n_dp, n_fs, x.shape[1]),
        compiler_params=pltpu.CompilerParams(collective_id=collective_id, has_side_effects=True),
        name="exchange_rows",
    )(x)


class Place:
    def __init__(self, dp, fs, n_dp, n_fs):
        self.dp, self.fs, self.n_dp, self.n_fs = dp, fs, n_dp, n_fs
        self.count = (n_dp - 1).bit_length()
        self.bits = [lax.rem(lax.div(dp, 2**k), 2) for k in range(self.count)]
        self.half = n_fs // 2

    def peer(self, bit):
        return (flip(self.dp, 2**bit), self.fs)

    def view(self, ref, free=(), flipped=(), z=None, skip=()):
        index = []
        for bit in reversed(range(self.count)):
            if bit in skip:
                continue
            if bit in free:
                index.append(slice(None))
            else:
                index.append(1 - self.bits[bit] if bit in flipped else self.bits[bit])
        if z is not None:
            index.append(z)
        return ref.at[tuple(index)] if index else ref

    def part(self, which):
        return pl.ds(which * self.half, self.half)


def block_layout(n_dp, n_fs):
    return (2,) * ((n_dp - 1).bit_length()) + (n_fs,)


def hop_orders(place):
    bits = tuple(range(1, place.count))
    return (bits, bits[::-1])


def copy_count(n_dp, n_fs):
    return n_fs - 1 + 2 * ((n_dp - 1).bit_length() - 1) + 1


def block_gather(place, sources, outs, send_sem, recv_sem, local_sem):
    n_fs, fs = place.n_fs, place.fs
    sends = []

    def stages(chunk):
        src, out = sources[chunk], outs[chunk]

        def remote(slot, view_from, view_to, device):
            return pltpu.make_async_remote_copy(
                src_ref=view_from,
                dst_ref=view_to,
                send_sem=send_sem.at[chunk, slot],
                recv_sem=recv_sem.at[chunk, slot],
                device_id=device,
                device_id_type=MESH,
            )

        def launch(make):
            make().start()
            sends.append(lambda: make().wait_send())

        def own_copy():
            return pltpu.make_async_copy(src, place.view(out, z=fs), local_sem.at[chunk])

        def along(step):
            to = lax.rem(fs + step, n_fs)
            return remote(step - 1, src, place.view(out, z=fs), (place.dp, to))

        def start():
            own_copy().start()
            for step in range(1, n_fs):
                launch(lambda step=step: along(step))

        def wait_along():
            own_copy().wait()
            for step in range(1, n_fs):
                origin = lax.rem(fs + n_fs - step, n_fs)
                remote(
                    step - 1, src, place.view(out, z=origin), (place.dp, origin)
                ).wait_recv()

        steps, before = [start], wait_along
        slot = n_fs - 1
        orders = hop_orders(place)
        for depth in range(place.count - 1):
            plan = [(slot + part, part, order[depth], order[:depth]) for part, order in enumerate(orders)]
            slot += 2

            def hop(slot, part, bit, free, arrived):
                view = place.view(out, free, (bit,) if arrived else (), place.part(part))
                return remote(slot, view, view, place.peer(bit))

            def go(plan=plan, before=before, hop=hop):
                before()
                for item in plan:
                    launch(lambda item=item: hop(*item, False))

            def arrive(plan=plan, hop=hop):
                for item in plan:
                    hop(*item, True).wait_recv()

            steps.append(go)
            before = arrive

        def across(arrived, slot=slot):
            free = tuple(range(1, place.count))
            view = place.view(out, free, (0,) if arrived else ())
            return remote(slot, view, view, place.peer(0))

        def cross(before=before):
            before()
            launch(lambda: across(False))

        return steps + [cross, lambda: across(True).wait_recv()]

    return [stages(chunk) for chunk in range(len(outs))], sends


def block_scatter(place, sources, emit, scratch, send_sem, recv_sem, local_sem):
    n_fs, fs = place.n_fs, place.fs
    sends = []
    per = 3 + place.count - 1

    def add_into(kept, other):
        shape = kept.shape[:-3]
        for index in itertools.product(*[range(n) for n in shape]):
            kept[index] = (kept[index].astype(F32) + other[index].astype(F32)).astype(BF16)

    def stages(chunk):
        src = sources[chunk]
        own, cross_in, last, *later = scratch[per * chunk : per * chunk + per]

        def remote(slot, view_from, view_to, device):
            return pltpu.make_async_remote_copy(
                src_ref=view_from,
                dst_ref=view_to,
                send_sem=send_sem.at[chunk, slot],
                recv_sem=recv_sem.at[chunk, slot],
                device_id=device,
                device_id_type=MESH,
            )

        def launch(make):
            make().start()
            sends.append(lambda: make().wait_send())

        every = tuple(range(1, place.count))

        def load():
            return pltpu.make_async_copy(place.view(src, every), own, local_sem.at[chunk])

        def across():
            return remote(0, place.view(src, every, (0,)), cross_in, place.peer(0))

        def start():
            launch(across)
            load().start()

        def fold_cross():
            load().wait()
            across().wait_recv()
            add_into(own, cross_in)

        steps, before = [start], fold_cross
        slot = 1
        orders = [order[::-1] for order in hop_orders(place)]
        for depth in range(place.count - 1):
            plan = []
            for part, order in enumerate(orders):
                free = tuple(order[depth + 1 :])
                plan.append((slot + part, part, order[depth], free, later[depth]))
            slot += 2

            def hop(slot, part, bit, free, buffer):
                view = place.view(own, free, (bit,), place.part(part), skip=(0,))
                return remote(slot, view, buffer.at[part], place.peer(bit))

            def go(plan=plan, before=before, hop=hop):
                before()
                for item in plan:
                    launch(lambda item=item: hop(*item))

            def fold(plan=plan, hop=hop):
                for item in plan:
                    hop(*item).wait_recv()
                    _, part, _, free, buffer = item
                    kept = place.view(own, free, (), place.part(part), skip=(0,))
                    add_into(kept, buffer.at[part])

            steps.append(go)
            before = fold

        def along(step, slot=slot):
            to = lax.rem(fs + step, n_fs)
            view = place.view(own, z=to, skip=(0,))
            return remote(slot + step - 1, view, last.at[step - 1], (place.dp, to))

        def spread(before=before):
            before()
            for step in range(1, n_fs):
                launch(lambda step=step: along(step))

        def finish():
            total = place.view(own, z=fs, skip=(0,))[...].astype(F32)
            for step in range(1, n_fs):
                along(step).wait_recv()
                total = total + last[step - 1].astype(F32)
            emit(chunk, total)

        return steps + [spread, finish]

    return [stages(chunk) for chunk in range(len(sources))], sends


def block_scratch(n_dp, n_fs, blocks, tail):
    hops = (n_dp - 1).bit_length() - 1
    out = []
    for count in blocks:
        entry = (count,) + tail
        zone = (2,) * hops + (n_fs,) + entry
        out += [pltpu.VMEM(zone, BF16), pltpu.VMEM(zone, BF16), pltpu.VMEM((n_fs - 1,) + entry, BF16)]
        for depth in range(hops):
            out.append(pltpu.VMEM((2,) + (2,) * (hops - 1 - depth) + (n_fs // 2,) + entry, BF16))
    return out


def block_sems(n_dp, n_fs, chunks):
    count = copy_count(n_dp, n_fs)
    return [
        pltpu.SemaphoreType.DMA((chunks, count)),
        pltpu.SemaphoreType.DMA((chunks, count)),
        pltpu.SemaphoreType.DMA((chunks,)),
    ]


TILE = 512
STATES = 32
TAPS = 15
REACH = 8
EPSILON = 1e-05
CHUNK = 256
ROWS = 256
VMEM_LIMIT = 60 << 20
TAP_ROW = 24
RATE = 40
MAP_IN = 72
MAP_OUT = 104
TABLE = 136


def sigmoid(v):
    return 0.5 * jnp.tanh(0.5 * v) + 0.5


def dot_nn(a, b):
    return jnp.dot(a, b, preferred_element_type=F32)


def dot_nt(a, b):
    return lax.dot_general(a, b, (((1,), (1,)), ((), ())), preferred_element_type=F32)


def dot_tn(a, b):
    return lax.dot_general(a, b, (((0,), (0,)), ((), ())), preferred_element_type=F32)


def norm_parts(v):
    centered = v - jnp.mean(v, axis=-1, keepdims=True)
    inv = lax.rsqrt(jnp.mean(centered * centered, axis=-1, keepdims=True) + EPSILON)
    return centered * inv, inv


def norm_back(grad, e, inv, gain):
    d = grad * gain
    return (
        d - jnp.mean(d, axis=-1, keepdims=True) - e * jnp.mean(d * e, axis=-1, keepdims=True)
    ) * inv


def fold8(v):
    return jnp.sum(v.reshape((v.shape[0] // 8, 8, v.shape[1])), axis=0)


def by_rows(body, rows=TILE, step=ROWS):
    def run(at, _):
        body(pl.ds(pl.multiple_of(at * step, step), step))
        return 0

    lax.fori_loop(0, rows // step, run, 0)


def columns(at, width=CHUNK):
    return pl.ds(pl.multiple_of(at * width, width), width)


def fill_halo(padded, flags, tiles):
    pitch = TILE + 2 * REACH
    for at in range(tiles):
        base = at * pitch
        if at == 0:
            padded[:, base : base + REACH, :] = jnp.zeros_like(padded[:, base : base + REACH, :])
        if at == tiles - 1:
            end = base + REACH + TILE
            padded[:, end : end + REACH, :] = jnp.zeros_like(padded[:, end : end + REACH, :])
        else:
            keep = flags[at + 1]
            end = base + REACH + TILE
            padded[:, end : end + REACH, :] = (
                padded[:, base + pitch + REACH : base + pitch + 2 * REACH, :] * keep
            )
            padded[:, base + pitch : base + pitch + REACH, :] = (
                padded[:, end - REACH : end, :] * keep
            )


def taps_over(padded, table_ref, store, tiles, reverse, block=64):
    pitch = TILE + 2 * REACH
    per = TILE // block
    lanes = padded.shape[0]
    for lane in range(lanes):
        weights = [
            jnp.broadcast_to(
                table_ref[TAP_ROW + k : TAP_ROW + k + 1, lane * 128 : lane * 128 + 128], (block, 128)
            )
            for k in range(TAPS)
        ]

        def run(at, _):
            tile, inner = at // per, at % per
            base = tile * pitch + inner * block
            total = jnp.zeros((block, 128), F32)
            for k in range(TAPS):
                shift = REACH + (TAPS // 2 - k if reverse else k - TAPS // 2)
                total = total + weights[k] * padded[lane, pl.ds(base + shift, block), :]
            store(lane, tile * TILE + inner * block, base, total)
            return 0

        lax.fori_loop(0, tiles * per, run, 0)


def small_exp(v):
    return 1.0 + v * (1.0 + v * (0.5 + v * (1.0 / 6 + v * (1.0 / 24 + v * (1.0 / 120)))))


def small_expm1_over(v):
    return 1.0 + v * (
        0.5 + v * (1.0 / 6 + v * (1.0 / 24 + v * (1.0 / 120 + v * (1.0 / 720 + v * (1.0 / 5040)))))
    )


def state_terms(table_ref):
    log_decay = -jnp.exp(table_ref[RATE : RATE + STATES, :])
    root = jnp.sqrt(-2.0 * log_decay * small_expm1_over(2.0 * log_decay))
    maps_in = table_ref[MAP_IN : MAP_IN + STATES, :]
    maps_out = table_ref[MAP_OUT : MAP_OUT + STATES, :]
    return log_decay, small_exp(log_decay), root, maps_in, maps_out


def ref_rows(ref):
    return ref.reshape((ref.shape[0] * ref.shape[1], ref.shape[2]))


PIECE = 16
WIDTH = 512


def cols_of(ref, first, at):
    per = WIDTH // CHUNK
    part = ref[:, first + lax.div(at, per), :, columns(lax.rem(at, per))]
    return part.reshape((ref.shape[0] * PIECE, CHUNK))


def rows_of(ref, first, at):
    groups = WIDTH // (4 * PIECE)
    part = ref[pl.ds(at * groups, groups), first : first + 4]
    return part.reshape((WIDTH, WIDTH))


def bias_of(ref, layer, at):
    row = 8 * layer + 2 * at
    return jnp.concatenate([ref[pl.ds(row, 1), :], ref[pl.ds(row + 1, 1), :]], axis=1)


def square_of(ref, at):
    return ref[:, at].reshape((ref.shape[0] * PIECE, WIDTH))


def store_wide(out, first, acc):
    def run(group, _):
        rows = pl.ds(pl.multiple_of(group * PIECE, PIECE), PIECE)
        for k in range(acc.shape[1] // WIDTH):
            out[group, first + k] = acc[rows, k * WIDTH : k * WIDTH + WIDTH].astype(BF16)
        return 0

    lax.fori_loop(0, acc.shape[0] // PIECE, run, 0)


def store_tall(out, first, acc):
    def run(group, _):
        rows = pl.ds(pl.multiple_of(group * 4 * PIECE, 4 * PIECE), 4 * PIECE)
        out[group, first : first + 4] = acc[rows, :].astype(BF16).reshape((4, PIECE, WIDTH))
        return 0

    lax.fori_loop(0, acc.shape[0] // (4 * PIECE), run, 0)


def flat_groups(ref):
    count = 1
    for n in ref.shape[:-3]:
        count *= n
    return ref.reshape((count,) + ref.shape[-3:])


def carries(offsets_ref, counts_ref, tiles):
    out = []
    for tile in range(tiles):
        begins = jnp.int32(0)
        for slot in range(offsets_ref.shape[1]):
            here = (offsets_ref[0, slot] == tile * TILE) & (slot < counts_ref[0])
            begins = jnp.maximum(begins, here.astype(jnp.int32))
        out.append((1 - begins).astype(F32))
    return out


STRETCH = 16
SPREAD = PIECE * STATES


def same_channel(rows, width, per, first=0):
    shape = (rows, width)
    row = lax.rem(lax.broadcasted_iota(jnp.int32, shape, 0), PIECE)
    col = lax.broadcasted_iota(jnp.int32, shape, 1)
    if per == 1:
        return row == lax.rem(col, PIECE)
    return row == lax.div(col, per)


def split_low(v):
    high = v.astype(BF16)
    return high, (v - high.astype(F32)).astype(BF16)


def spread_states(part):
    rows = part.shape[0]
    state = lax.broadcasted_iota(jnp.int32, (STATES, SPREAD), 0)
    col = lax.broadcasted_iota(jnp.int32, (STATES, SPREAD), 1)
    pick_state = (state == lax.rem(col, STATES)).astype(F32).astype(BF16)
    wide = dot_nn(part, pick_state)
    wide = jnp.where(same_channel(rows, SPREAD, STATES), wide, 0.0)
    return jnp.sum(wide.reshape((rows // PIECE, PIECE, SPREAD)), axis=1)


def gather_states(wide):
    groups = wide.shape[0]
    full = jnp.broadcast_to(wide[:, None, :], (groups, PIECE, SPREAD)).reshape((groups * PIECE, SPREAD))
    full = jnp.where(same_channel(groups * PIECE, SPREAD, STATES), full, 0.0)
    state = lax.broadcasted_iota(jnp.int32, (SPREAD, 128), 1)
    row = lax.broadcasted_iota(jnp.int32, (SPREAD, 128), 0)
    pick_state = (state == lax.rem(row, STATES)).astype(F32).astype(BF16)
    high, low = split_low(full)
    return (dot_nn(high, pick_state) + dot_nn(low, pick_state)).T[:STATES, :]


def prepare_states(small, power, shifted, weight):
    groups = small.shape[0]
    entries = lambda first: small[:, :, first : first + STATES].reshape((groups * PIECE, STATES))
    log_decay = -jnp.exp(spread_states(entries(RATE)))
    root = jnp.sqrt(-2.0 * log_decay * small_expm1_over(2.0 * log_decay))
    both = spread_states(entries(MAP_IN)) * root * spread_states(entries(MAP_OUT))
    weight[...] = both
    col = lax.broadcasted_iota(jnp.int32, (SPREAD, 128), 1)
    row = lax.broadcasted_iota(jnp.int32, (SPREAD, 128), 0)
    add_states = (col == lax.div(row, STATES)).astype(F32).astype(BF16)
    power[0] = jnp.ones_like(both)
    decay = small_exp(log_decay)
    for m in range(1, STRETCH):
        power[m] = power[m - 1] * decay
    halves = []
    for half in range(2):
        total = jnp.zeros((groups, 128), F32)
        for k in range(8):
            high, low = split_low(power[half * 8 + k] * both)
            lag = dot_nn(high, add_states) + dot_nn(low, add_states)
            total = total + (pltpu.roll(lag, k * PIECE, 1) if k else lag)
        halves.append(total)
    blank = jnp.zeros((groups, 256), F32)
    padded = jnp.concatenate([blank] + halves, axis=1)
    for m in range(STRETCH):
        shifted[m] = pltpu.roll(padded, 512 - (m + 1) * PIECE, 1)[:, :256]


def group_weights(power, shifted, group, decay_w, lag_w):
    mask = same_channel(PIECE, SPREAD, STATES)
    lag_mask = same_channel(PIECE, 256, 1)
    for m in range(STRETCH):
        rows = slice(m * PIECE, m * PIECE + PIECE)
        line = jnp.broadcast_to(power[m, pl.ds(group, 1), :], (PIECE, SPREAD))
        decay_w[rows, :] = jnp.where(mask, line, 0.0).astype(BF16)
        line = jnp.broadcast_to(shifted[m, pl.ds(group, 1), :], (PIECE, 256))
        lag_w[rows, :] = jnp.where(lag_mask, line, 0.0).astype(BF16)


def swap_blocks(parts):
    col = lax.div(lax.broadcasted_iota(jnp.int32, parts[0].shape, 1), PIECE)
    parts = list(parts)
    for distance in (1, 2, 4):
        low = lax.rem(lax.div(col, distance), 2) == 0
        shift = distance * PIECE
        for a in range(8):
            if a & distance:
                continue
            first, second = parts[a], parts[a + distance]
            parts[a] = jnp.where(low, first, pltpu.roll(second, shift, 1))
            parts[a + distance] = jnp.where(low, pltpu.roll(first, 128 - shift, 1), second)
    return parts


SLAB = 32
TOGETHER = 4


def to_blocks(load, out, blocks, backward):
    for slab in range(blocks // SLAB):
        rows = slice(slab * SLAB, slab * SLAB + SLAB)
        for half in range(2):
            parts = []
            for k in range(8):
                frame = half * 8 + k
                frame = STRETCH - 1 - frame if backward else frame
                parts.append(load(slab * SLAB * STRETCH + frame))
            for group, part in enumerate(swap_blocks(parts)):
                out[group, rows, half * 128 : half * 128 + 128] = part.astype(out.dtype)


def from_blocks(store, ref, blocks, backward):
    for slab in range(blocks // SLAB):
        rows = slice(slab * SLAB, slab * SLAB + SLAB)
        for half in range(2):
            parts = [ref[group, rows, half * 128 : half * 128 + 128] for group in range(8)]
            for k, part in enumerate(swap_blocks(parts)):
                frame = half * 8 + k
                frame = STRETCH - 1 - frame if backward else frame
                store(slab * SLAB * STRETCH + frame, part)


def block_powers(decay):
    q2 = decay * decay
    q4 = q2 * q2
    q8 = q4 * q4
    one = q8 * q8
    two = one * one
    four = two * two
    return one, two, four


def row_powers(one, count=8):
    rows = [one]
    for _ in range(count - 1):
        rows.append(rows[-1] * one)
    return rows


def scan_blocks(source, into, decay, keeps, per, reverse):
    blocks, width = source.shape
    one, two, four = block_powers(decay)
    row = lax.broadcasted_iota(jnp.int32, (8, width), 0)
    if reverse:
        row = 7 - row
    factors = []
    for distance, power in ((1, one), (2, two), (4, four)):
        line = jnp.broadcast_to(power, (8, width))
        factors.append((8 - distance if reverse else distance, jnp.where(row >= distance, line, 0.0)))
    entering = jnp.ones((8, width), F32)
    for bit, power in ((1, one), (2, two), (4, four)):
        line = jnp.broadcast_to(power, (8, width))
        entering = jnp.where(lax.rem(lax.div(row, bit), 2) == 1, entering * line, entering)
    eight = jnp.broadcast_to(four * four, (8, width))
    carry = jnp.zeros((8, width), F32)
    tiles = blocks // 8
    for k in range(tiles):
        tile = tiles - 1 - k if reverse else k
        edge = (tile + 1) * 8 if reverse else tile * 8
        if k and edge % per == 0:
            carry = carry * keeps[edge // per]
        x = source[tile * 8 : tile * 8 + 8, :]
        for shift, factor in factors:
            x = x + factor * pltpu.roll(x, shift, 0)
        moved = pltpu.roll(x, 7 if reverse else 1, 0)
        into[tile * 8 : tile * 8 + 8, :] = jnp.where(row >= 1, moved, 0.0) + entering * carry
        end = x[0:1, :] if reverse else x[7:8, :]
        carry = jnp.broadcast_to(end, (8, width)) + eight * carry


def mix_forward(midway, u_ref, y_ref, power, shifted, weight, keeps, ub_out, state_out, blk_in, blk_out, decay_w, lag_w, t_scr, h_scr):
    frames = u_ref.shape[1]
    blocks = frames // STRETCH
    count = decay_w.shape[0]
    several = range(count)

    def lane_tile(lane, _):
        if midway is not None:
            pl.when(lane == u_ref.shape[0] // 2)(midway)
        to_blocks(lambda at: u_ref[lane, pl.ds(at, SLAB, stride=STRETCH), :], blk_in, blocks, True)

        def some_groups(k, _):
            place = [k * count + n for n in several]
            groups = [lane * 8 + at for at in place]
            for n in several:
                group_weights(power, shifted, groups[n], decay_w.at[n], lag_w.at[n])
            for n in several:
                ub_out[groups[n]] = blk_in[place[n]]
                t_scr[n] = dot_nn(blk_in[place[n]], decay_w[n])
            for n in several:
                decay = power[1, pl.ds(groups[n], 1), :]
                scan_blocks(t_scr.at[n], h_scr.at[n], decay, keeps, TILE // STRETCH, False)
            for n in several:
                decay = power[1, pl.ds(groups[n], 1), :]
                state = h_scr[n]
                state_out[groups[n]] = state.astype(BF16)
                out = (state * (weight[pl.ds(groups[n], 1), :] * decay)).astype(BF16)
                blk_out[place[n]] = dot_nn(blk_in[place[n]], lag_w[n]) + dot_nt(out, decay_w[n])
            return 0

        lax.fori_loop(0, 8 // count, some_groups, 0)

        def store(at, values):
            y_ref[lane, pl.ds(at, SLAB, stride=STRETCH), :] = values

        from_blocks(store, blk_out, blocks, False)
        return 0

    lax.fori_loop(0, u_ref.shape[0], lane_tile, 0)


def mix_backward(
    lane, u_ref, grad, skip, u_tile, u_sem, power, shifted, weight, keeps, ub_ref, state_ref, lags, sums,
    frames_scr, blk_in, blk_out, decay_w, lag_w, stack_scr, e_scr, r_scr,
):
    blocks = frames_scr.shape[2]
    count = decay_w.shape[0]
    several = range(count)
    lanes = u_ref.shape[0]
    copy = lambda at: pltpu.make_async_copy(u_ref.at[at], u_tile, u_sem)
    copy(lane).wait()
    for at in range(STRETCH):
        for slab in range(blocks // SLAB):
            rows = slice(slab * SLAB, slab * SLAB + SLAB)
            first = pl.ds(slab * SLAB * STRETCH + at, SLAB, stride=STRETCH)
            frames_scr[0, at, rows, :] = u_tile[first, :]
            frames_scr[1, at, rows, :] = grad[lane, first, :]

    @pl.when(lane + 1 < lanes)
    def _():
        copy(lane + 1).start()

    def one_lag(lag, _):
        def one_frame(at, total):
            for slab in range(blocks // SLAB):
                rows = slice(slab * SLAB, slab * SLAB + SLAB)
                total = total + frames_scr[1, at, rows, :] * frames_scr[0, at - lag, rows, :]
            return total

        total = lax.fori_loop(lag, STRETCH, one_frame, jnp.zeros((SLAB, 128), F32))
        lags[lane, pl.ds(lag, 1), :] = jnp.sum(total, axis=0, keepdims=True)
        return 0

    lax.fori_loop(0, STRETCH, one_lag, 0)
    for slab in range(blocks // SLAB):
        rows = slice(slab * SLAB, slab * SLAB + SLAB)
        for half in range(2):
            parts = [frames_scr[1, half * 8 + k, rows, :] for k in range(8)]
            for group, part in enumerate(swap_blocks(parts)):
                blk_in[group, rows, half * 128 : half * 128 + 128] = part.astype(BF16)
    position = lax.div(lax.broadcasted_iota(jnp.int32, (1, 256), 1), PIECE).astype(F32)

    def some_groups(k, _):
        place = [k * count + n for n in several]
        groups = [lane * 8 + at for at in place]
        for n in several:
            group_weights(power, shifted, groups[n], decay_w.at[n], lag_w.at[n])
        for n in several:
            gy = blk_in[place[n]]
            stack_scr[n, 0:blocks, :] = gy
            stack_scr[n, blocks : 2 * blocks, :] = (gy.astype(F32) * (position + 1.0)).astype(BF16)
            stack_scr[n, 2 * blocks :, :] = (ub_ref[groups[n]].astype(F32) * position).astype(BF16)
        for n in several:
            e_scr[n] = dot_nn(stack_scr[n], decay_w[n])
        for n in several:
            decay = power[1, pl.ds(groups[n], 1), :]
            own = e_scr.at[n, pl.ds(0, blocks)]
            own[...] = own[...] * decay
            scan_blocks(own, r_scr.at[n], decay, keeps, TILE // STRETCH, True)
        for n in several:
            group = groups[n]
            inverse = 1.0 / power[1, pl.ds(group, 1), :]
            last = 16.0 * power[15, pl.ds(group, 1), :]
            first, second = jnp.zeros((8, SPREAD), F32), jnp.zeros((8, SPREAD), F32)
            for at in range(blocks // 8):
                rows = slice(at * 8, at * 8 + 8)
                state = state_ref[group, rows, :].astype(F32)
                turn = e_scr[n, 2 * blocks + at * 8 : 2 * blocks + at * 8 + 8, :]
                first = first + state * e_scr[n, rows, :]
                second = second + state * e_scr[n, blocks + at * 8 : blocks + at * 8 + 8, :]
                second = second + r_scr[n, rows, :] * (turn * inverse + last * state)
            sums[0, pl.ds(group, 1), :] = jnp.sum(first, axis=0, keepdims=True)
            sums[1, pl.ds(group, 1), :] = jnp.sum(second, axis=0, keepdims=True)
            out = (r_scr[n] * weight[pl.ds(group, 1), :]).astype(BF16)
            blk_out[place[n]] = dot_nt(blk_in[place[n]], lag_w[n]) + dot_nt(out, decay_w[n])
        return 0

    lax.fori_loop(0, 8 // count, some_groups, 0)

    def store(at, values):
        slab, frame = at // (SLAB * STRETCH), at % STRETCH
        through = frames_scr[1, frame, slab * SLAB : slab * SLAB + SLAB, :]
        grad[lane, pl.ds(at, SLAB, stride=STRETCH), :] = values + skip[pl.ds(lane, 1), :] * through

    from_blocks(store, blk_out, blocks, True)


def mix_gradients(lags, sums, table_ref):
    _, decay, root, maps_in, maps_out = state_terms(table_ref)
    coupling = maps_in * root * maps_out
    gmap = gather_states(sums[0])
    gdecay = gather_states(sums[1])
    power = jnp.ones_like(decay)
    for lag in range(STRETCH):
        line = jnp.concatenate([lags[k, lag : lag + 1, :] for k in range(lags.shape[0])], axis=1)
        if lag:
            gdecay = gdecay + float(lag) * power * line
            power = power * decay
        gmap = gmap + power * line
    return gmap, gdecay * coupling


def pack_small(out, scr, place, bias_ref, gains, shifts, conv_bias, taps, rate, maps):
    own = gains.shape[1]
    scr[...] = jnp.zeros_like(scr)
    scr[0:6, :own] = gains[...].astype(F32)
    scr[6:18, :own] = shifts[...].astype(F32)
    scr[18:19, :own] = conv_bias[...].astype(F32)
    scr[TAP_ROW : TAP_ROW + TAPS, :own] = taps[...].astype(F32)
    out[:, :CHUNK] = scr[...].T[:own, :].astype(BF16)
    out[:, RATE:MAP_IN] = rate[...]
    out[:, MAP_IN:MAP_OUT] = maps[0]
    out[:, MAP_OUT:TABLE] = maps[1]
    count = bias_ref.shape[1]
    row = lax.div(place * count, CHUNK)
    inner = place * count - row * CHUNK
    at_row = lax.broadcasted_iota(jnp.int32, (PIECE, CHUNK), 0)
    wide = jnp.zeros((PIECE, CHUNK), F32)
    for layer in range(2):
        line = jnp.broadcast_to(bias_ref[layer : layer + 1, :].astype(F32), (8, count))
        line = jnp.concatenate([line, jnp.zeros((8, CHUNK - count), F32)], axis=1)
        line = pltpu.roll(line, inner, 1)
        wide = wide + jnp.where(at_row == 8 * layer + row, jnp.broadcast_to(line[0:1], wide.shape), 0.0)
    out[:, CHUNK:] = wide.astype(BF16)


def front_kernel(mesh_size, *refs):
    fused = mesh_size is not None
    refs = list(refs)
    take = lambda count: [refs.pop(0) for _ in range(count)]
    offsets_ref, counts_ref, x_ref = take(3)
    if fused:
        n_dp, n_fs = mesh_size
        small_in = take(7)
        up_s, down_s, mixin_s, mixout_s, convin_s, convout_s = take(6)
    else:
        first_v, extra_v, second_v, third_v, fourth_v, table_in, bias_in = take(7)
    (
        h_out,
        x1_out,
        v_out,
        y_out,
        gated_out,
        x2_out,
        p_out,
        u_out,
        w_out,
        stat_out,
        table_ref,
        bias_ref,
        ub_out,
        state_out,
        power,
        shifted,
        weight,
    ) = take(17)
    gathered = take(6) if fused else []
    x1_scr, low_all, low_scr, sum_scr, y_all, padded, act_all = take(7)
    mix_scr = take(6)
    step = pl.program_id(0)
    channels = x_ref.shape[1]
    frames = w_out.shape[0]
    tiles = frames // TILE
    lanes = channels // 128
    gain = lambda k: table_ref[k : k + 1, :]
    shift = lambda k: table_ref[6 + k : 7 + k, :]
    here = lambda rows, tile: pl.ds(pl.multiple_of(tile * TILE + rows.start, ROWS), ROWS)
    flags = carries(offsets_ref, counts_ref, tiles)
    mix_at, last_step = 3 * tiles, 4 * tiles + 1
    if fused:
        landing = take(5)
        sources = take(6)
        turn_scr = refs.pop(0)
        sems = take(3)
        load_sem = refs.pop(0)
        swap = take(4)
        dp, fs = lax.axis_index("dp"), lax.axis_index("fsdp")
        place = Place(dp, fs, n_dp, n_fs)
        landing.append(gathered[5])
        plans, sends = block_gather(place, sources, landing, *sems)
        first_v, extra_v, second_v, third_v, fourth_v = [flat_groups(r) for r in landing[:5]]

        def keep_copy(chunk):
            return pltpu.make_async_copy(landing[chunk], gathered[chunk], load_sem.at[chunk])

        def run(*stages):
            for chunk, stage in stages:
                plans[chunk][stage]()

        @pl.when(step == 0)
        def _():
            pack_small(sources[0].at[0], turn_scr, dp * n_fs + fs, *small_in)
            for k in range(4):
                cols = slice(k * WIDTH, k * WIDTH + WIDTH)
                if k < 2:
                    sources[0][1 + k] = up_s[0, :, cols]
                else:
                    sources[1][k - 2] = up_s[0, :, cols]
                sources[5][1 + k] = up_s[1, :, cols]
                rows = slice(k * PIECE, k * PIECE + PIECE)
                sources[2][k] = down_s[0, rows, :]
                sources[5][5 + k] = down_s[1, rows, :]
            for k in range(2):
                cols = slice(k * WIDTH, k * WIDTH + WIDTH)
                sources[3][k] = mixin_s[:, cols]
                sources[4][1 + k] = convin_s[:, cols]
            sources[4][0] = mixout_s[...]
            sources[5][0] = convout_s[...]
            greet(dp, fs, n_dp, n_fs)
            run((0, 0), (1, 0), (0, 1), (2, 0), (1, 1), (0, 2), (1, 2), (0, 3), (2, 1), (3, 0), (0, 4))
            table_ref[...] = first_v[:, 0, :, :CHUNK].reshape((channels, CHUNK)).astype(F32).T[:TABLE, :]
            total = first_v[0, 0, :, CHUNK:].astype(F32)
            for k in range(1, n_dp * n_fs):
                total = total + first_v[k, 0, :, CHUNK:].astype(F32)
            bias_ref[...] = total

        rest = {1: [(1, 3), (2, 2)], 2: [(3, 1)], tiles: [(1, 4), (4, 0)], tiles + 1: [(2, 3), (3, 2)]}
        rest.update({2 * tiles: [(2, 4), (3, 3), (4, 1)], 2 * tiles + 1: [(5, 0)]})
        rest.update({2 * tiles + 2: [(4, 2)], mix_at: [(3, 4)]})
        rest.update({mix_at + 1: [(4, 4), (5, 2)], last_step: [(5, 3)]})
        for at, stages in rest.items():

            @pl.when(step == at)
            def _(at=at, stages=stages):
                run(*stages)
                saved = {2 * tiles: (0, 1, 2), mix_at: (3,), mix_at + 1: (4,)}
                for chunk in saved.get(at, ()):
                    keep_copy(chunk).start()

    else:

        @pl.when(step == 0)
        def _():
            table_ref[...] = table_in[...]
            bias_ref[...] = bias_in[...]

    @pl.when(step < tiles)
    def _():
        def first(rows):
            e, _ = norm_parts(x_ref[rows, :].astype(F32))
            low_all[here(rows, step), :] = (e * gain(0) + shift(0)).astype(BF16)

        by_rows(first)

    for half, part in enumerate((first_v, extra_v)):

        @pl.when((step >= half * tiles) & (step < half * tiles + tiles))
        def _(half=half, part=part):
            tile_rows = pl.ds(pl.multiple_of((step - half * tiles) * TILE, TILE), TILE)
            for k in range(2):
                c = 2 * half + k
                h = dot_nn(low_all[tile_rows, :], square_of(part, 1 - half + k))
                h = h + bias_of(bias_ref, 0, c)
                h_out[:, k * WIDTH : k * WIDTH + WIDTH] = h.astype(BF16)
                active = (h * sigmoid(h)).astype(BF16)
                act_all[tile_rows, c * WIDTH : c * WIDTH + WIDTH] = active

    @pl.when((step >= 2 * tiles) & (step < mix_at))
    def _():
        at = step - 2 * tiles
        tile_rows = pl.ds(pl.multiple_of(at * TILE, TILE), TILE)
        total = dot_nn(act_all[tile_rows, :WIDTH], rows_of(second_v, 0, 0))
        for c in range(1, 4):
            cols = slice(c * WIDTH, c * WIDTH + WIDTH)
            total = total + dot_nn(act_all[tile_rows, cols], rows_of(second_v, 0, c))
        sum_scr[...] = total

        def second(rows):
            x1 = x_ref[rows, :].astype(F32) + 0.5 * (sum_scr[rows, :] + shift(6))
            x1_out[rows, :] = x1
            x1_scr[here(rows, at), :] = x1
            e, _ = norm_parts(x1)
            low_all[here(rows, at), :] = (e * gain(1) + shift(1)).astype(BF16)

        by_rows(second)

    @pl.when(step == mix_at)
    def _():
        prepare_states(first_v[:, 0, :, :CHUNK], power, shifted, weight)

        def project(tile, _):
            rows = pl.ds(pl.multiple_of(tile * TILE, TILE), TILE)
            u = dot_nn(low_all[rows, :], square_of(third_v, 0))
            for lane in range(lanes):
                u_out[lane, rows, :] = u[:, lane * 128 : lane * 128 + 128]
            return 0

        lax.fori_loop(0, tiles, project, 0)
        if fused:
            run((4, 3))
        mixing = (u_out, y_all, power, shifted, weight, flags, ub_out, state_out) + tuple(mix_scr)
        mix_forward((lambda: run((5, 1))) if fused else None, *mixing)

    @pl.when((step > mix_at) & (step < last_step))
    def _():
        at = step - mix_at - 1
        whole_tile = pl.ds(pl.multiple_of(at * TILE, TILE), TILE)
        v_out[...] = dot_nn(low_all[whole_tile, :], square_of(third_v, 1)).astype(BF16)

        def gate(rows):
            join = lambda ref: jnp.concatenate([ref[lane, here(rows, at), :] for lane in range(lanes)], axis=1)
            y = join(y_all) + shift(11) * join(u_out)
            v = v_out[rows, :].astype(F32)
            y_out[rows, :] = y.astype(BF16)
            gated_out[rows, :] = (y * (v * sigmoid(v))).astype(BF16)

        by_rows(gate)
        sum_scr[...] = dot_nn(gated_out[...], square_of(fourth_v, 0))

        def third(rows):
            x2 = x1_scr[here(rows, at), :] + (sum_scr[rows, :] + shift(8))
            x2_out[rows, :] = x2
            e, _ = norm_parts(x2)
            low_scr[rows, :] = (e * gain(2) + shift(2)).astype(BF16)

        by_rows(third)
        pitch = TILE + 2 * REACH

        def widen(c, _):
            cols = columns(c)
            right = columns(c + channels // CHUNK)
            left_part = dot_nn(low_scr[...], cols_of(fourth_v, 1, c)) + table_ref[15:16, cols]
            right_part = dot_nn(low_scr[...], cols_of(fourth_v, 2, c)) + table_ref[16:17, cols]
            p_out[:, cols] = left_part.astype(BF16)
            p_out[:, right] = right_part.astype(BF16)
            g = left_part * sigmoid(right_part)
            place = pl.ds(pl.multiple_of(at * pitch + REACH, 8), TILE)
            for k in range(CHUNK // 128):
                padded[c * (CHUNK // 128) + k, place, :] = g[:, k * 128 : k * 128 + 128]
            return 0

        lax.fori_loop(0, channels // CHUNK, widen, 0)

    @pl.when(step == last_step)
    def _():
        fill_halo(padded, flags, tiles)

        def store(lane, row, base, total):
            w_out[pl.ds(pl.multiple_of(row, 64), 64), lane * 128 : lane * 128 + 128] = total

        taps_over(padded, table_ref, store, tiles, False)
        stat_out[...] = jnp.zeros_like(stat_out)

        def total(at, _):
            rows = pl.ds(pl.multiple_of(at * ROWS, ROWS), ROWS)
            stat_out[...] += fold8(w_out[rows, :])
            return 0

        lax.fori_loop(0, frames // ROWS, total, 0)
        center = jnp.sum(stat_out[...], axis=0, keepdims=True) * (1.0 / frames)
        stat_out[...] = jnp.zeros_like(stat_out)

        def spread(at, _):
            rows = pl.ds(pl.multiple_of(at * ROWS, ROWS), ROWS)
            off = w_out[rows, :] - center
            stat_out[...] += fold8(off * off)
            return 0

        lax.fori_loop(0, frames // ROWS, spread, 0)
        around = jnp.sum(stat_out[...], axis=0, keepdims=True)
        if fused:
            center, around = pool_over(center, around, frames, dp, fs, n_dp, n_fs, *swap)
            around = lax.rsqrt(around * (1.0 / (frames * n_dp * n_fs)) + EPSILON)
        stat_out[...] = jnp.zeros_like(stat_out)
        stat_out[0:1, :] = center
        stat_out[1:2, :] = around
        if fused:
            run((5, 4))
            for chunk in range(5):
                keep_copy(chunk).wait()
            for wait in sends:
                wait()


def whole(shape):
    zeros = (0,) * len(shape)
    return pl.BlockSpec(shape, lambda *_: zeros, pipeline_mode=pl.Buffered(1))


def params(collective_id=None):
    if collective_id is None:
        return pltpu.CompilerParams(
            dimension_semantics=("arbitrary",), vmem_limit_bytes=VMEM_LIMIT
        )
    return pltpu.CompilerParams(
        dimension_semantics=("arbitrary",),
        vmem_limit_bytes=VMEM_LIMIT,
        collective_id=collective_id,
        has_side_effects=True,
    )


SMEM_SPEC = pl.BlockSpec(memory_space=pltpu.SMEM)
HBM_SPEC = pl.BlockSpec(memory_space=pltpu.HBM)


def front(mesh_size, offsets, counts, x, small, weights, hidden, collective_id=None):
    fused = mesh_size is not None
    frames, channels = x.shape
    tiles = frames // TILE
    clip = lambda i, first: jnp.clip(i - first, 0, tiles - 1)
    twice = lambda i: (jnp.where(i < tiles, i, jnp.where(i < 2 * tiles, tiles - 1, clip(i, 2 * tiles))), 0)
    halves = lambda i: (jnp.where(i < tiles, i, clip(i, tiles)), jnp.where(i < tiles, 0, 1))
    place = lambda i: clip(i, 3 * tiles + 1)
    late = lambda width: pl.BlockSpec((TILE, width), lambda i: (place(i), 0))
    shape = lambda width, kind: jax.ShapeDtypeStruct((frames, width), kind)
    groups, blocks = channels // PIECE, frames // STRETCH
    out_shape = [
        shape(hidden, BF16),
        shape(channels, F32),
        shape(channels, BF16),
        shape(channels, BF16),
        shape(channels, BF16),
        shape(channels, F32),
        shape(2 * channels, BF16),
        jax.ShapeDtypeStruct((channels // 128, frames, 128), F32),
        shape(channels, F32),
        jax.ShapeDtypeStruct((8, channels), F32),
        jax.ShapeDtypeStruct((TABLE, channels), F32),
        jax.ShapeDtypeStruct((16, CHUNK), F32),
        jax.ShapeDtypeStruct((groups, blocks, STRETCH * PIECE), BF16),
        jax.ShapeDtypeStruct((groups, blocks, SPREAD), BF16),
        jax.ShapeDtypeStruct((STRETCH, groups, SPREAD), F32),
        jax.ShapeDtypeStruct((STRETCH, groups, STRETCH * PIECE), F32),
        jax.ShapeDtypeStruct((groups, SPREAD), F32),
    ]
    out_specs = [
        pl.BlockSpec((TILE, hidden // 2), halves),
        pl.BlockSpec((TILE, channels), lambda i: (clip(i, 2 * tiles), 0)),
    ]
    out_specs += [late(channels)] * 4 + [late(2 * channels)]
    out_specs += [whole(s.shape) for s in out_shape[7:]]
    scratch = [
        pltpu.VMEM((frames, channels), F32),
        pltpu.VMEM((frames, channels), BF16),
        pltpu.VMEM((TILE, channels), BF16),
        pltpu.VMEM((TILE, channels), F32),
        pltpu.VMEM((channels // 128, frames, 128), F32),
        pltpu.VMEM((channels // 128, tiles * (TILE + 2 * REACH), 128), F32),
        pltpu.VMEM((frames, hidden), BF16),
        pltpu.VMEM((8, blocks, STRETCH * PIECE), BF16),
        pltpu.VMEM((8, blocks, STRETCH * PIECE), F32),
        pltpu.VMEM((TOGETHER, STRETCH * PIECE, SPREAD), BF16),
        pltpu.VMEM((TOGETHER, STRETCH * PIECE, STRETCH * PIECE), BF16),
        pltpu.VMEM((TOGETHER, blocks, SPREAD), F32),
        pltpu.VMEM((TOGETHER, blocks, SPREAD), F32),
    ]
    operands = (weights if not fused else small + weights) + (small if not fused else [])
    if fused:
        layout = block_layout(*mesh_size)
        blocks = (3, 2, 4, 2, 3, 9)
        chunks = [jax.ShapeDtypeStruct(layout + (k, PIECE, WIDTH), BF16) for k in blocks]
        out_shape += chunks
        out_specs += [HBM_SPEC] * len(chunks)
        scratch += [pltpu.VMEM(c.shape, BF16) for c in chunks[:5]]
        scratch += [pltpu.VMEM((k, PIECE, WIDTH), BF16) for k in blocks]
        scratch += [pltpu.VMEM((CHUNK, 128), F32)]
        scratch += block_sems(*mesh_size, len(chunks)) + [pltpu.SemaphoreType.DMA((5,))]
        scratch += swap_scratch(*mesh_size, channels)
    return pl.pallas_call(
        partial(front_kernel, mesh_size),
        grid=(4 * tiles + 2,),
        in_specs=[SMEM_SPEC, SMEM_SPEC, pl.BlockSpec((TILE, channels), twice)] + [whole(a.shape) for a in operands],
        out_specs=out_specs,
        out_shape=out_shape,
        scratch_shapes=scratch,
        compiler_params=params(collective_id),
        name="front",
    )(offsets, counts, x, *operands)


def middle_kernel(
    mesh_size,
    x2_ref,
    w_ref,
    cot_ref,
    blocks_ref,
    bias_ref,
    vec_ref,
    stat_ref,
    out_ref,
    gx3_ref,
    gnb_ref,
    gblocks_out,
    gbias_out,
    gvec_out,
    stat_out,
    up_acc,
    down_acc,
    convout_acc,
    bias_acc,
    vec_acc,
    h_scr,
    low_scr,
    turn_scr,
    act_scr,
    grad_scr,
    sum_scr,
    x3_scr,
    *swap,
):
    at = pl.program_id(0)
    tiles = pl.num_programs(0)
    channels = x2_ref.shape[1]
    if mesh_size is not None:
        n_dp, n_fs = mesh_size
        dp, fs = lax.axis_index("dp"), lax.axis_index("fsdp")

        @pl.when(at == 0)
        def _():
            greet(dp, fs, n_dp, n_fs)

    hidden = up_acc.shape[1]
    gain = lambda k: vec_ref[k : k + 1, :]
    shift = lambda k: vec_ref[6 + k : 7 + k, :]
    center, scale = stat_ref[0:1, :], stat_ref[1:2, :]

    @pl.when(at == 0)
    def _():
        for ref in (up_acc, down_acc, convout_acc, bias_acc, vec_acc):
            ref[...] = jnp.zeros_like(ref)

    def normed(rows):
        e = (w_ref[rows, :] - center) * scale
        return e, e * gain(5) + shift(5)

    def first(rows):
        _, nb = normed(rows)
        act_scr[rows, :] = (nb * sigmoid(nb)).astype(BF16)

    by_rows(first)
    sum_scr[...] = dot_nn(act_scr[...], square_of(blocks_ref, 0))

    def second(rows):
        x3 = x2_ref[rows, :] + (sum_scr[rows, :] + vec_ref[18:19, :])
        x3_scr[rows, :] = x3
        e, _ = norm_parts(x3)
        low_scr[rows, :] = (e * gain(3) + shift(3)).astype(BF16)
        sum_scr[rows, :] = jnp.zeros((ROWS, channels), F32)

    by_rows(second)

    def forward(c, _):
        cols = columns(c, WIDTH)
        h = dot_nn(low_scr[...], square_of(blocks_ref, 1 + c)) + bias_of(bias_ref, 1, c)
        h_scr[:, cols] = h
        active = (h * sigmoid(h)).astype(BF16)
        sum_scr[...] += dot_nn(active, rows_of(blocks_ref, 5, c))
        return 0

    lax.fori_loop(0, hidden // WIDTH, forward, 0)
    turn_scr[...] = low_scr[...].T

    def last(rows):
        x4 = x3_scr[rows, :] + 0.5 * (sum_scr[rows, :] + shift(7))
        e, inv = norm_parts(x4)
        out_ref[rows, :] = (e * gain(4) + shift(4)).astype(BF16)
        cot = cot_ref[rows, :].astype(F32)
        vec_acc[0] += fold8(cot * e)
        vec_acc[1] += fold8(cot)
        gx4 = norm_back(cot, e, inv, gain(4))
        gx3_ref[rows, :] = gx4
        low = (0.5 * gx4).astype(BF16)
        grad_scr[rows, :] = low
        vec_acc[2] += fold8(low.astype(F32))
        sum_scr[rows, :] = jnp.zeros((ROWS, channels), F32)

    by_rows(last)

    def backward(c, _):
        cols = columns(c, WIDTH)
        h = h_scr[:, cols]
        sig = sigmoid(h)
        active = h * sig
        gate = dot_nt(grad_scr[...], rows_of(blocks_ref, 5, c))
        grad_h = (gate * (sig * (1.0 + h - active))).astype(BF16)
        bias_acc[:, cols] += fold8(grad_h.astype(F32))
        down_acc[cols, :] += dot_tn(active.astype(BF16), grad_scr[...])
        up_acc[:, cols] += dot_nn(turn_scr[...], grad_h)
        sum_scr[...] += dot_nt(grad_h, square_of(blocks_ref, 1 + c))
        return 0

    lax.fori_loop(0, hidden // WIDTH, backward, 0)

    def fourth(rows):
        e, inv = norm_parts(x3_scr[rows, :])
        grad = sum_scr[rows, :]
        vec_acc[3] += fold8(grad * e)
        vec_acc[4] += fold8(grad)
        gx3 = gx3_ref[rows, :] + norm_back(grad, e, inv, gain(3))
        gx3_ref[rows, :] = gx3
        low = gx3.astype(BF16)
        grad_scr[rows, :] = low
        vec_acc[5] += fold8(low.astype(F32))

    by_rows(fourth)
    convout_acc[...] += dot_tn(act_scr[...], grad_scr[...])
    sum_scr[...] = dot_nt(grad_scr[...], square_of(blocks_ref, 0))

    def fifth(rows):
        e, nb = normed(rows)
        sig = sigmoid(nb)
        gnb = sum_scr[rows, :] * (sig * (1.0 + nb * (1.0 - sig)))
        gnb_ref[rows, :] = gnb
        vec_acc[6] += fold8(gnb * e)
        vec_acc[7] += fold8(gnb)

    by_rows(fifth)

    @pl.when(at == tiles - 1)
    def _():
        for k in range(8):
            gvec_out[k : k + 1, :] = jnp.sum(vec_acc[k], axis=0, keepdims=True)

        def convert():
            store_wide(gblocks_out, 0, convout_acc)
            store_wide(gblocks_out, 1, up_acc)
            store_tall(gblocks_out, 5, down_acc)
            gbias_out[...] = jnp.broadcast_to(
                jnp.sum(bias_acc[...], axis=0, keepdims=True), gbias_out.shape
            )

        stat_out[...] = stat_ref[...]
        if mesh_size is None:
            convert()
        else:
            total = sum_over(gvec_out[...], dp, fs, n_dp, n_fs, *swap, between=convert)
            share = gain(5) * (1.0 / (TILE * tiles * n_dp * n_fs))
            stat_out[2:3, :] = total[7:8, :] * share
            stat_out[3:4, :] = total[6:7, :] * share


def middle(mesh_size, x2, w, cot, blocks, bias, vec, stat, hidden, collective_id=None):
    frames, channels = x2.shape
    tiles = frames // TILE
    row = lambda width: pl.BlockSpec((TILE, width), lambda i: (i, 0))
    shapes = [
        jax.ShapeDtypeStruct((frames, channels), BF16),
        jax.ShapeDtypeStruct((frames, channels), F32),
        jax.ShapeDtypeStruct((frames, channels), F32),
        jax.ShapeDtypeStruct(blocks.shape, BF16),
        jax.ShapeDtypeStruct((8, hidden), F32),
        jax.ShapeDtypeStruct((8, channels), F32),
        jax.ShapeDtypeStruct((8, channels), F32),
    ]
    swap = [] if mesh_size is None else swap_scratch(*mesh_size, channels)
    return pl.pallas_call(
        partial(middle_kernel, mesh_size),
        grid=(tiles,),
        in_specs=[row(channels)] * 3
        + [whole(a.shape) for a in (blocks, bias, vec, stat)],
        out_specs=[row(channels)] * 3 + [whole(s.shape) for s in shapes[3:]],
        out_shape=shapes,
        scratch_shapes=[
            pltpu.VMEM((channels, hidden), F32),
            pltpu.VMEM((hidden, channels), F32),
            pltpu.VMEM((channels, channels), F32),
            pltpu.VMEM((8, hidden), F32),
            pltpu.VMEM((8, 8, channels), F32),
            pltpu.VMEM((TILE, hidden), F32),
            pltpu.VMEM((TILE, channels), BF16),
            pltpu.VMEM((channels, TILE), BF16),
            pltpu.VMEM((TILE, channels), BF16),
            pltpu.VMEM((TILE, channels), BF16),
            pltpu.VMEM((TILE, channels), F32),
            pltpu.VMEM((TILE, channels), F32),
        ]
        + swap,
        compiler_params=params(collective_id),
        name="middle",
    )(x2, w, cot, blocks, bias, vec, stat)


def back_kernel(mesh_size, *refs):
    fused = mesh_size is not None
    refs = list(refs)
    take = lambda count: [refs.pop(0) for _ in range(count)]
    offsets_ref, counts_ref, w_ref, gnb_ref, p_ref = take(5)
    x2_ref, gx3_ref, gated_ref, y_ref, v_ref, x1_ref = take(6)
    u_ref, ub_ref, state_ref, power, shifted, weight, mixin_ref, middle_ref, vec_ref, stat_ref = take(10)
    sources = take(1) if fused else []
    gx1_ref, gin_out, gvec_out, gtaps_ref, gmap_out, gdecay_out = take(6)
    reduced = take(2) if fused else []
    mid_ref = None if fused else refs.pop(0)
    wide_acc, mixout_acc, vec_acc, low_scr, wide_scr, sum_scr = take(6)
    padded, gpad, gv_all, lags, sums, skip, u_tile, u_sem = take(8)
    mix_scr = take(8)
    step = pl.program_id(0)
    channels = x2_ref.shape[1]
    frames = u_ref.shape[1]
    tiles = frames // TILE
    lanes = channels // 128
    pitch = TILE + 2 * REACH
    conv_at, mix_at = tiles, 2 * tiles + 1
    last_step = 3 * tiles + 1
    gain = lambda k: vec_ref[k : k + 1, :]
    shift = lambda k: vec_ref[6 + k : 7 + k, :]
    left, right = slice(0, channels), slice(channels, 2 * channels)
    flags = carries(offsets_ref, counts_ref, tiles)
    schedule = {}
    if fused:
        n_dp, n_fs = mesh_size
        place = Place(lax.axis_index("dp"), lax.axis_index("fsdp"), n_dp, n_fs)
        mid_src = refs.pop(0)
        mid_ref = flat_groups(mid_src)
        scratch = take(2 * (2 + place.count))

        def emit(chunk, total):
            reduced[chunk][...] = total

        plans, sends = block_scatter(place, sources + [mid_src], emit, scratch, *take(3))
        first = [(0, 0), (conv_at, 1), (conv_at + 2, 0), (mix_at, 0), (mix_at, 1)]
        second = [(mix_at, 0), (mix_at, 1), (mix_at + 1, 0), (mix_at + 2, 0), (last_step, 1)]
        for chunk, points in enumerate((first, second)):
            for stage, point in enumerate(points):
                schedule.setdefault(point, []).append((stage, chunk))

    def progress(at, part):
        for stage, chunk in sorted(schedule.get((at, part), [])):
            plans[chunk][stage]()

    @pl.when(step == 0)
    def _():
        for ref in (wide_acc, mixout_acc, vec_acc):
            ref[...] = jnp.zeros_like(ref)
        if fused:
            greet(place.dp, place.fs, n_dp, n_fs)

    for at in sorted({key[0] for key in schedule if key[1] == 0 and key[0] != mix_at}):

        @pl.when(step == at)
        def _(at=at):
            progress(at, 0)

    @pl.when(step < tiles)
    def _():
        center, scale = stat_ref[0:1, :], stat_ref[1:2, :]
        plain, cross = stat_ref[2:3, :], stat_ref[3:4, :]

        def fill(index, _):
            rows = pl.ds(pl.multiple_of(index * 64, 64), 64)
            spot = pl.ds(pl.multiple_of(step * pitch + REACH + index * 64, 8), 64)
            e = (w_ref[rows, :] - center) * scale
            d = gnb_ref[rows, :] * gain(5)
            gw = scale * (d - plain - e * cross)
            g = p_ref[rows, left].astype(F32) * sigmoid(p_ref[rows, right].astype(F32))
            for lane in range(lanes):
                cols = slice(lane * 128, lane * 128 + 128)
                padded[lane, spot, :] = gw[:, cols]
                gpad[lane, spot, :] = g[:, cols]
            return 0

        lax.fori_loop(0, TILE // 64, fill, 0)

    @pl.when(step == conv_at)
    def _():
        fill_halo(padded, flags, tiles)
        fill_halo(gpad, flags, tiles)
        block = 64
        per = TILE // block
        gtaps_ref[...] = jnp.zeros_like(gtaps_ref)
        for lane in range(lanes):

            def corr(index, sums, lane=lane):
                base = (index // per) * pitch + (index % per) * block
                here = padded[lane, pl.ds(pl.multiple_of(base + REACH, 8), block), :]
                return tuple(
                    s + fold8(here * gpad[lane, pl.ds(base + REACH + k - TAPS // 2, block), :])
                    for k, s in enumerate(sums)
                )

            found = lax.fori_loop(0, tiles * per, corr, (jnp.zeros((8, 128), F32),) * TAPS)
            for k in range(TAPS):
                gtaps_ref[k : k + 1, lane * 128 : lane * 128 + 128] = jnp.sum(
                    found[k], axis=0, keepdims=True
                )
        progress(conv_at, 1)

        def store(lane, row, base, total):
            gpad[lane, pl.ds(pl.multiple_of(base + REACH, 8), 64), :] = total

        taps_over(padded, vec_ref, store, tiles, True)

    @pl.when((step > conv_at) & (step < mix_at))
    def _():
        at = step - conv_at - 1

        def first(rows):
            spot = pl.ds(pl.multiple_of(at * pitch + REACH + rows.start, 8), ROWS)
            grad = jnp.concatenate([gpad[lane, spot, :] for lane in range(lanes)], axis=1)
            sig = sigmoid(p_ref[rows, right].astype(F32))
            gl = (grad * sig).astype(BF16)
            gr = (grad * p_ref[rows, left].astype(F32) * (sig * (1.0 - sig))).astype(BF16)
            wide_scr[rows, left] = gl
            wide_scr[rows, right] = gr
            vec_acc[0] += fold8(gl.astype(F32))
            vec_acc[1] += fold8(gr.astype(F32))
            e, _ = norm_parts(x2_ref[rows, :])
            low_scr[rows, :] = (e * gain(2) + shift(2)).astype(BF16)

        by_rows(first)
        turned = low_scr[...].T
        wide_acc[...] += dot_nn(turned, wide_scr[...])
        sum_scr[...] = dot_nt(wide_scr[:, left], square_of(middle_ref, 1)) + dot_nt(
            wide_scr[:, right], square_of(middle_ref, 2)
        )

        def second(rows):
            here = pl.ds(pl.multiple_of(at * TILE + rows.start, ROWS), ROWS)
            e, inv = norm_parts(x2_ref[rows, :])
            grad = sum_scr[rows, :]
            vec_acc[2] += fold8(grad * e)
            vec_acc[3] += fold8(grad)
            gx2 = gx3_ref[rows, :] + norm_back(grad, e, inv, gain(2))
            spot = pl.ds(pl.multiple_of(at * pitch + REACH + rows.start, 8), ROWS)
            for lane in range(lanes):
                gpad[lane, spot, :] = gx2[:, lane * 128 : lane * 128 + 128]
            low = gx2.astype(BF16)
            low_scr[rows, :] = low
            vec_acc[4] += fold8(low.astype(F32))

        by_rows(second)
        mixout_acc[...] += dot_tn(gated_ref[...], low_scr[...])
        sum_scr[...] = dot_nt(low_scr[...], square_of(middle_ref, 0))

        def third(rows):
            here = pl.ds(pl.multiple_of(at * TILE + rows.start, ROWS), ROWS)
            grad = sum_scr[rows, :]
            v = v_ref[rows, :].astype(F32)
            sig = sigmoid(v)
            swish = v * sig
            gy = grad * swish
            for lane in range(lanes):
                padded[lane, here, :] = gy[:, lane * 128 : lane * 128 + 128]
            gv_all[here, :] = (
                grad * y_ref[rows, :].astype(F32) * (sig * (1.0 + v - swish))
            ).astype(BF16)


        by_rows(third)

    @pl.when(step == mix_at)
    def _():
        pltpu.make_async_copy(u_ref.at[0], u_tile, u_sem).start()
        store_wide(mid_ref, 0, mixout_acc)
        store_wide(mid_ref, 1, wide_acc)
        wide_acc[...] = jnp.zeros_like(wide_acc)
        for lane in range(lanes):
            skip[lane : lane + 1, :] = vec_ref[17:18, lane * 128 : lane * 128 + 128]
        progress(mix_at, 0)

        def one(lane, _):
            if fused:
                pl.when(lane == lanes // 2)(lambda: progress(mix_at, 1))
            mix_backward(
                lane, u_ref, padded, skip, u_tile, u_sem, power, shifted, weight, flags, ub_ref, state_ref, lags, sums, *mix_scr
            )
            return 0

        lax.fori_loop(0, lanes, one, 0)
        gmap, gdecay = mix_gradients(lags, sums, vec_ref)
        gmap_out[...] = gmap
        gdecay_out[...] = gdecay

    @pl.when(step > mix_at)
    def _():
        at = step - mix_at - 1

        def fourth(rows):
            here = pl.ds(pl.multiple_of(at * TILE + rows.start, ROWS), ROWS)
            gu = jnp.concatenate([padded[lane, here, :] for lane in range(lanes)], axis=1)
            wide_scr[rows, left] = gu.astype(BF16)
            wide_scr[rows, right] = gv_all[here, :]
            e, _ = norm_parts(x1_ref[rows, :])
            low_scr[rows, :] = (e * gain(1) + shift(1)).astype(BF16)

        by_rows(fourth)
        turned = low_scr[...].T
        wide_acc[...] += dot_nn(turned, wide_scr[...])
        sum_scr[...] = dot_nt(wide_scr[:, left], square_of(mixin_ref, 0)) + dot_nt(
            wide_scr[:, right], square_of(mixin_ref, 1)
        )

        def fifth(rows):
            e, inv = norm_parts(x1_ref[rows, :])
            grad = sum_scr[rows, :]
            vec_acc[6] += fold8(grad * e)
            vec_acc[7] += fold8(grad)
            spot = pl.ds(pl.multiple_of(at * pitch + REACH + rows.start, 8), ROWS)
            gx2 = jnp.concatenate([gpad[lane, spot, :] for lane in range(lanes)], axis=1)
            gx1_ref[rows, :] = gx2 + norm_back(grad, e, inv, gain(1))

        by_rows(fifth)

    @pl.when(step == last_step)
    def _():
        store_wide(gin_out, 0, wide_acc)
        for k in range(8):
            gvec_out[k : k + 1, :] = jnp.sum(vec_acc[k], axis=0, keepdims=True)
        gvec_out[5:6, :] = jnp.concatenate([lags[k, 0:1, :] for k in range(lanes)], axis=1)
        if fused:
            progress(last_step, 1)
            for wait in sends:
                wait()


def back(mesh_size, offsets, counts, tiled, wholes, grads=(), collective_id=None):
    fused = mesh_size is not None
    frames, channels = tiled[0].shape
    tiles = frames // TILE
    groups, blocks = channels // PIECE, frames // STRETCH
    late = lambda i, first: jnp.clip(i - first, 0, tiles - 1)
    filling = lambda i: (late(i, 0), 0)
    twice = lambda i: (jnp.where(i < tiles, i, late(i, tiles + 1)), 0)
    mixing = lambda i: (late(i, tiles + 1), 0)
    ending = lambda i: (late(i, 2 * tiles + 2), 0)
    maps = [filling, filling, twice] + [mixing] * 5 + [ending]
    state = jax.ShapeDtypeStruct((STATES, channels), F32)
    bf16 = lambda *shape: jax.ShapeDtypeStruct(shape, BF16)
    shapes = [
        jax.ShapeDtypeStruct((frames, channels), F32),
        bf16(groups, 2, PIECE, WIDTH),
        jax.ShapeDtypeStruct((8, channels), F32),
        jax.ShapeDtypeStruct((16, channels), F32),
        state,
        state,
    ]
    pad = pltpu.VMEM((channels // 128, tiles * (TILE + 2 * REACH), 128), F32)
    scratch = [
        pltpu.VMEM((channels, 2 * channels), F32),
        pltpu.VMEM((channels, channels), F32),
        pltpu.VMEM((8, 8, channels), F32),
        pltpu.VMEM((TILE, channels), BF16),
        pltpu.VMEM((TILE, 2 * channels), BF16),
        pltpu.VMEM((TILE, channels), F32),
        pad,
        pad,
        pltpu.VMEM((frames, channels), BF16),
        pltpu.VMEM((channels // 128, STRETCH, 128), F32),
        pltpu.VMEM((2, groups, SPREAD), F32),
        pltpu.VMEM((8, 128), F32),
        pltpu.VMEM((frames, 128), F32),
        pltpu.SemaphoreType.DMA(()),
        pltpu.VMEM((2, STRETCH, blocks, 128), F32),
        pltpu.VMEM((8, blocks, STRETCH * PIECE), BF16),
        pltpu.VMEM((8, blocks, STRETCH * PIECE), F32),
        pltpu.VMEM((2, STRETCH * PIECE, SPREAD), BF16),
        pltpu.VMEM((2, STRETCH * PIECE, STRETCH * PIECE), BF16),
        pltpu.VMEM((2, 3 * blocks, STRETCH * PIECE), BF16),
        pltpu.VMEM((2, 3 * blocks, SPREAD), F32),
        pltpu.VMEM((2, blocks, SPREAD), F32),
    ]
    if fused:
        counts_of = [grads[0].shape[-3], 3]
        shapes += [jax.ShapeDtypeStruct((k, PIECE, WIDTH), F32) for k in counts_of]
        scratch += [pltpu.VMEM(block_layout(*mesh_size) + (3, PIECE, WIDTH), BF16)]
        scratch += block_scratch(*mesh_size, counts_of, (PIECE, WIDTH))
        scratch += block_sems(*mesh_size, 2)
    else:
        shapes.append(bf16(groups, 3, PIECE, WIDTH))
    return pl.pallas_call(
        partial(back_kernel, mesh_size),
        grid=(3 * tiles + 2,),
        in_specs=[SMEM_SPEC, SMEM_SPEC]
        + [pl.BlockSpec((TILE, a.shape[1]), index) for a, index in zip(tiled, maps)]
        + [HBM_SPEC]
        + [whole(a.shape) for a in wholes[1:]]
        + [HBM_SPEC] * len(grads),
        out_specs=[pl.BlockSpec((TILE, channels), ending)] + [whole(s.shape) for s in shapes[1:]],
        out_shape=shapes,
        scratch_shapes=scratch,
        compiler_params=params(collective_id),
        name="back",
    )(offsets, counts, *tiled, *wholes, *grads)


def small_gradients(out, gvec1, gvec2, gvec3, gtaps, gmap, gdecay, table_ref):
    out[...] = jnp.zeros_like(out)
    gains = {1: (gvec2, 6), 2: (gvec2, 2), 3: (gvec1, 3), 4: (gvec1, 0), 5: (gvec1, 6)}
    shifts = {1: (gvec2, 7), 2: (gvec2, 3), 3: (gvec1, 4), 4: (gvec1, 1), 5: (gvec1, 7)}
    shifts.update({6: (gvec3, 0), 7: (gvec1, 2), 8: (gvec2, 4), 9: (gvec2, 0), 10: (gvec2, 1)})
    shifts.update({11: (gvec2, 5), 12: (gvec1, 5)})
    for at, (ref, row) in gains.items():
        out[at : at + 1, :] = ref[row : row + 1, :]
    for at, (ref, row) in shifts.items():
        out[6 + at : 7 + at, :] = ref[row : row + 1, :]
    out[TAP_ROW : TAP_ROW + TAPS, :] = gtaps[:TAPS, :]
    log_decay, decay, root, maps_in, maps_out = state_terms(table_ref)
    both = gmap[...] * root
    out[MAP_IN:MAP_OUT, :] = both * maps_out
    out[MAP_OUT:TABLE, :] = both * maps_in
    turn = (1.0 - root * root) / root
    out[RATE:MAP_IN, :] = log_decay * (
        gdecay[...] * decay - gmap[...] * maps_in * maps_out * turn
    )


def store_cols(out, at, value):
    groups = value.shape[0] // PIECE
    out[:, at] = value.reshape((groups, PIECE, WIDTH))


def tail_kernel(mesh_size, *refs):
    fused = mesh_size is not None
    refs = list(refs)
    take = lambda count: [refs.pop(0) for _ in range(count)]
    x_ref, h_ref, gx1_ref, up_ref, up2_ref, down_ref, table_ref = take(7)
    hidden = 4 * WIDTH
    if fused:
        gvec1, gvec2, gtaps, gmap, gdecay, gbias1 = take(6)
        sources = take(1)
        gx_ref, last_out = take(2)
        reduced = take(4)
    else:
        gx_ref, gvec_out, gbias_out, up_out, down_out = take(5)
    turn_scr, grad_scr, gh_scr, vec_acc, bias_scr = take(5)
    step = pl.program_id(0)
    frames, channels = x_ref.shape
    chunks = hidden // WIDTH
    tiles = frames // TILE
    first_b, first_c = 1 + chunks, 1 + 2 * chunks
    schedule = {}
    if fused:
        n_dp, n_fs = mesh_size
        down_src, left_src, right_src, small_scr, gvec3 = take(5)
        dp, fs = lax.axis_index("dp"), lax.axis_index("fsdp")
        place = Place(dp, fs, n_dp, n_fs)
        scratch = take(4 * (2 + place.count))
        sems = take(3)
        swap = take(4)
        down_out = flat_groups(down_src)
        halves = (flat_groups(left_src), flat_groups(right_src))

        def emit(chunk, total):
            reduced[chunk][...] = total

        plans, sends = block_scatter(
            place, sources + [down_src, left_src, right_src], emit, scratch, *sems
        )
        begins = [
            (0, 2, 4, 7, first_c),
            (first_b, first_b + 1, first_b + 3, first_c + 1, first_c + tiles),
            (first_b + 2, first_c, first_c + 1, first_c + 2, first_c + tiles),
            (first_c, first_c + 1, first_c + 2, first_c + tiles, first_c + tiles),
        ]
        for chunk, steps in enumerate(begins):
            for stage, at in enumerate(steps):
                schedule.setdefault(at, []).append((stage, chunk))
    last_step = first_c + tiles - 1

    def progress(at):
        for stage, chunk in sorted(schedule.get(at, [])):
            plans[chunk][stage]()

    @pl.when(step == 0)
    def _():
        if fused:
            greet(dp, fs, n_dp, n_fs)
        progress(0)
        vec_acc[...] = jnp.zeros_like(vec_acc)

        def first(rows):
            e, _ = norm_parts(x_ref[rows, :].astype(F32))
            low = (e * table_ref[0:1, :] + table_ref[6:7, :]).astype(BF16)
            turn_scr[:, rows] = low.T
            grad = (0.5 * gx1_ref[rows, :]).astype(BF16)
            grad_scr[rows, :] = grad
            vec_acc[0] += fold8(grad.astype(F32))

        by_rows(first, frames)

    if fused:
        for at in range(1, last_step + 1):
            if at in schedule and at != first_c:

                @pl.when(step == at)
                def _(at=at):
                    progress(at)

    @pl.when((step >= 1) & (step < first_b))
    def _():
        h = h_ref[...].astype(F32)
        active = (h * sigmoid(h)).astype(BF16)
        value = dot_tn(active, grad_scr[...]).astype(BF16)
        groups = WIDTH // (4 * PIECE)
        down_out[pl.ds((step - 1) * groups, groups)] = value.reshape((groups, 4, PIECE, WIDTH))

    def second_half(c, store):
        cols = columns(c, WIDTH)
        h = h_ref[...].astype(F32)
        sig = sigmoid(h)
        gate = dot_nt(grad_scr[...], rows_of(down_ref, 0, c))
        grad_h = (gate * (sig * (1.0 + h * (1.0 - sig)))).astype(BF16)
        gh_scr[:, cols] = grad_h
        sums = jnp.sum(fold8(grad_h.astype(F32)), axis=0, keepdims=True)
        bias_scr[pl.ds(2 * c, 1), :] = sums[:, :CHUNK]
        bias_scr[pl.ds(2 * c + 1, 1), :] = sums[:, CHUNK:]
        store(dot_nn(turn_scr[...], grad_h).astype(BF16))

    if fused:
        for half in range(2):
            begin = first_b + half * (chunks // 2)

            @pl.when((step >= begin) & (step < begin + chunks // 2))
            def _(half=half, begin=begin):
                def store(value):
                    store_cols(halves[half], step - begin, value)

                second_half(step - first_b, store)

    else:

        @pl.when((step >= first_b) & (step < first_c))
        def _():
            def store(value):
                store_cols(up_out, step - first_b, value)

            second_half(step - first_b, store)

    if fused:

        @pl.when(step == first_c)
        def _():
            gvec3[0:1, :] = jnp.sum(vec_acc[0], axis=0, keepdims=True)
            small_gradients(small_scr, gvec1, gvec2, gvec3, gtaps, gmap, gdecay, table_ref)
            narrow = small_scr[...].T.astype(BF16)
            devices = n_dp * n_fs
            small_out = halves[1]
            small_out[:, 2, :, :CHUNK] = narrow.reshape((devices, PIECE, CHUNK))
            for c in range(8):
                bias_scr[8 + c : 9 + c, :] = gbias1[0:1, c * CHUNK : c * CHUNK + CHUNK]
            bias = bias_scr[...].astype(BF16)
            small_out[:, 2, :, CHUNK:] = jnp.broadcast_to(bias[None], (devices, PIECE, CHUNK))
            progress(first_c)

    @pl.when(step >= first_c)
    def _():
        tile = step - first_c
        whole_tile = pl.ds(pl.multiple_of(tile * TILE, TILE), TILE)
        total = dot_nt(gh_scr[whole_tile, :WIDTH], square_of(up_ref, 1))
        later = [square_of(up_ref, 2), square_of(up2_ref, 0), square_of(up2_ref, 1)]
        for k in range(1, hidden // WIDTH):
            cols = slice(k * WIDTH, k * WIDTH + WIDTH)
            total = total + dot_nt(gh_scr[whole_tile, cols], later[k - 1])
        gx_ref[...] = total

        def second(rows):
            here = pl.ds(pl.multiple_of(tile * TILE + rows.start, ROWS), ROWS)
            e, inv = norm_parts(x_ref[here, :].astype(F32))
            grad = gx_ref[rows, :]
            vec_acc[1] += fold8(grad * e)
            vec_acc[2] += fold8(grad)
            gx_ref[rows, :] = gx1_ref[here, :] + norm_back(grad, e, inv, table_ref[0:1, :])

        by_rows(second)

    @pl.when(step == last_step)
    def _():
        if fused:
            last_out[...] = jnp.zeros_like(last_out)
            for k in range(2):
                last_out[k : k + 1, :] = jnp.sum(vec_acc[1 + k], axis=0, keepdims=True)
            ends = sorted(schedule.get(last_step + 1, []))

            def between():
                for stage, chunk in ends:
                    plans[chunk][stage]()

            last_out[...] = sum_over(last_out[...], dp, fs, n_dp, n_fs, *swap, between=between)
            for wait in sends:
                wait()
        else:
            gvec_out[...] = jnp.zeros_like(gvec_out)
            for k in range(3):
                gvec_out[k : k + 1, :] = jnp.sum(vec_acc[k], axis=0, keepdims=True)
            gbias_out[...] = bias_scr[...]


def tail(mesh_size, x, h, gx1, up, up2, down, table, others=(), grads=(), collective_id=None):
    fused = mesh_size is not None
    frames, channels = x.shape
    hidden = h.shape[1]
    tiles, chunks = frames // TILE, hidden // WIDTH
    first_b, first_c = 1 + chunks, 1 + 2 * chunks
    place = lambda i: jnp.where(
        i < first_b, jnp.maximum(i - 1, 0), jnp.minimum(i - first_b, chunks - 1)
    )
    shapes = [jax.ShapeDtypeStruct((frames, channels), F32)]
    scratch = [
        pltpu.VMEM((channels, frames), BF16),
        pltpu.VMEM((frames, channels), BF16),
        pltpu.VMEM((frames, hidden), BF16),
        pltpu.VMEM((8, 8, channels), F32),
        pltpu.VMEM((16, CHUNK), F32),
    ]
    if fused:
        own = [4, 2, 3]
        counts = [g.shape[-3] for g in grads] + own
        shapes.append(jax.ShapeDtypeStruct((8, channels), F32))
        shapes += [jax.ShapeDtypeStruct((k, PIECE, WIDTH), F32) for k in counts]
        layout = block_layout(*mesh_size)
        scratch += [pltpu.VMEM(layout + (k, PIECE, WIDTH), BF16) for k in own]
        scratch += [pltpu.VMEM((256, channels), F32), pltpu.VMEM((8, channels), F32)]
        scratch += block_scratch(*mesh_size, counts, (PIECE, WIDTH))
        scratch += block_sems(*mesh_size, len(counts))
        scratch += swap_scratch(*mesh_size, channels)
    else:
        shapes += [
            jax.ShapeDtypeStruct((8, channels), F32),
            jax.ShapeDtypeStruct((16, CHUNK), F32),
            jax.ShapeDtypeStruct((channels // PIECE, 4, PIECE, WIDTH), BF16),
            jax.ShapeDtypeStruct((channels // PIECE, 4, PIECE, WIDTH), BF16),
        ]
    return pl.pallas_call(
        partial(tail_kernel, mesh_size),
        grid=(first_c + tiles,),
        in_specs=[whole(x.shape), pl.BlockSpec((frames, WIDTH), lambda i: (0, place(i)))]
        + [whole(a.shape) for a in (gx1, up, up2, down, table) + tuple(others)]
        + [pl.BlockSpec(memory_space=pltpu.HBM)] * len(grads),
        out_specs=[
            pl.BlockSpec((TILE, channels), lambda i: (jnp.maximum(i - first_c, 0), 0))
        ]
        + [whole(s.shape) for s in shapes[1:]],
        out_shape=shapes,
        scratch_shapes=scratch,
        compiler_params=params(collective_id),
        name="tail",
    )(x, h, gx1, up, up2, down, table, *others, *grads)


def unpack_kernel(
    place_ref,
    second_ref,
    middle_ref,
    mixin_ref,
    down_ref,
    left_ref,
    right_ref,
    last_ref,
    up_out,
    down_out,
    bias_out,
    mixin_out,
    mixout_out,
    convin_out,
    convout_out,
    convbias_out,
    rate_out,
    map_out,
    taps_out,
    gains_out,
    shifts_out,
):
    mine = place_ref[0]
    for k in range(4):
        cols = slice(k * WIDTH, k * WIDTH + WIDTH)
        rows = slice(k * PIECE, k * PIECE + PIECE)
        up_out[0, :, cols] = (left_ref if k < 2 else right_ref)[k % 2]
        up_out[1, :, cols] = second_ref[1 + k]
        down_out[0, rows, :] = down_ref[k]
        down_out[1, rows, :] = second_ref[5 + k]
    convout_out[...] = second_ref[0]
    mixout_out[...] = middle_ref[0]
    for k in range(2):
        cols = slice(k * WIDTH, k * WIDTH + WIDTH)
        mixin_out[:, cols] = mixin_ref[k]
        convin_out[:, cols] = middle_ref[1 + k]
    count = bias_out.shape[1]
    row = (mine * count) // CHUNK
    inner = mine * count - row * CHUNK
    for layer in range(2):
        line = right_ref[2, pl.ds(8 * layer + row, 1), CHUNK:]
        line = pltpu.roll(jnp.broadcast_to(line, (8, CHUNK)), CHUNK - inner, 1)
        bias_out[layer : layer + 1, :] = line[0:1, :count]
    channels = last_ref.shape[1]
    first = pltpu.roll(last_ref[...], channels - mine * PIECE, 1)[:, :PIECE]
    small = right_ref[2, :, :CHUNK]
    turned = small.T
    gains_out[...] = turned[0:6, :]
    gains_out[0:1, :] = first[0:1, :]
    shifts_out[...] = turned[6:18, :]
    shifts_out[0:1, :] = first[1:2, :]
    convbias_out[...] = turned[18:19, :]
    taps_out[...] = turned[TAP_ROW : TAP_ROW + TAPS, :]
    rate_out[...] = small[:, RATE:MAP_IN]
    map_out[0] = small[:, MAP_IN:MAP_OUT]
    map_out[1] = small[:, MAP_OUT:TABLE]


def unpack(mine, arrays, hidden):
    channels = arrays[-1].shape[1]
    devices = channels // PIECE
    f32 = lambda *shape: jax.ShapeDtypeStruct(shape, F32)
    vmem = pl.BlockSpec(memory_space=pltpu.VMEM)
    return pl.pallas_call(
        unpack_kernel,
        in_specs=[SMEM_SPEC] + [vmem] * len(arrays),
        out_specs=[vmem] * 13,
        out_shape=[
            f32(2, PIECE, hidden),
            f32(2, hidden // devices, channels),
            f32(2, hidden // devices),
            f32(PIECE, 2 * WIDTH),
            f32(PIECE, WIDTH),
            f32(PIECE, 2 * WIDTH),
            f32(PIECE, WIDTH),
            f32(1, PIECE),
            f32(PIECE, STATES),
            f32(2, PIECE, STATES),
            f32(TAPS, PIECE),
            f32(6, PIECE),
            f32(12, PIECE),
        ],
        name="unpack",
    )(mine, *arrays)


def pack_table(gains, shifts, conv_bias, taps, rate, maps):
    channels = gains.shape[1]
    blank = lambda rows: jnp.zeros((rows, channels), gains.dtype)
    parts = [gains, shifts, conv_bias[None], blank(TAP_ROW - 19), taps, blank(RATE - TAP_ROW - TAPS)]
    parts += [rate, maps[0], maps[1], blank(256 - TABLE)]
    return jnp.concatenate(parts, axis=0).T


def pack_bias(bias, place):
    layers, count = bias.shape
    hidden = 16 * CHUNK // layers
    wide = lax.dynamic_update_slice(
        jnp.zeros((layers, hidden), bias.dtype), bias, (0, place * count)
    )
    return wide.reshape((16, CHUNK))


def unpack_table(table):
    return (
        table[0:6],
        table[6:18],
        table[18],
        table[TAP_ROW : TAP_ROW + TAPS],
        table[RATE:MAP_IN],
        jnp.stack([table[MAP_IN:MAP_OUT], table[MAP_OUT:TABLE]]),
    )


def on_device(
    n_dp,
    n_fs,
    frames,
    seq_lengths,
    seq_offsets,
    seq_counts,
    ffn_up,
    ffn_down,
    ffn_bias_up,
    mix_in,
    mix_out,
    conv_in,
    conv_out,
    conv_out_bias,
    ssm_rate,
    ssm_map,
    conv_kernel,
    gains,
    shifts,
    cotangent,
):
    devices = n_dp * n_fs
    mine = lax.axis_index("dp") * n_fs + lax.axis_index("fsdp")
    frames_dev, channels = frames.shape
    hidden = ffn_up.shape[2]
    if channels // devices == PIECE:
        size = (n_dp, n_fs)
        small = [
            ffn_bias_up,
            gains,
            shifts,
            conv_out_bias[None],
            conv_kernel,
            ssm_rate.T,
            ssm_map.transpose((0, 2, 1)),
        ]
        weights = [ffn_up, ffn_down, mix_in, mix_out, conv_in, conv_out]
        made = front(size, seq_offsets, seq_counts, frames, small, weights, hidden, 1)
        h0, x1, v, y, gated, x2, p, u, w, stat, table, bias, *mixing = made[:17]
        groups = lambda g: g.reshape((devices,) + g.shape[-3:])
        places = lambda g: g.reshape(block_layout(n_dp, n_fs) + g.shape[1:])
        first, extra, second, third, mixed, fourth = [groups(g) for g in made[17:]]
        result, gx3, gnb, grads, gbias1, gvec1, stat = middle(
            size, x2, w, cotangent, fourth, bias, table, stat, hidden, 2
        )
        gx1, grads2, gvec2, gtaps, gmap, gdecay, reduced, reduced2 = back(
            size,
            seq_offsets,
            seq_counts,
            [w, gnb, p, x2, gx3, gated, y, v, x1],
            [u] + mixing + [third, mixed, table, stat],
            (places(grads),),
            3,
        )
        others = (gvec1, gvec2, gtaps, gmap, gdecay, gbias1)
        gx, last, *late = tail(
            size, frames, h0, gx1, first, extra, second, table, others, (places(grads2),), 4
        )
        made = unpack(mine.reshape((1,)), [reduced, reduced2] + late + [last], hidden)
        made = list(made)
        made[7] = made[7].reshape((-1,))
        made[8] = made[8].T
        made[9] = made[9].transpose((0, 2, 1))
        return (result, gx) + tuple(made)

    small = pack_table(gains, shifts, conv_out_bias, conv_kernel, ssm_rate, ssm_map)
    got = gather_all(
        n_dp,
        n_fs,
        [
            small[None],
            pack_bias(ffn_bias_up, mine)[None],
            ffn_up,
            ffn_down,
            mix_in[None],
            mix_out[None],
            conv_in[None],
            conv_out[None],
        ],
        1,
    )
    matrix = lambda g: g.reshape((-1, g.shape[-1]))
    table, _, up0, up1, down0, down1, mixin, mixout, convin, convout = [matrix(g) for g in got]
    table = table.astype(F32).T[:TABLE]
    bias = jnp.sum(got[1].astype(F32), axis=0)
    group_count = channels // PIECE
    cut = lambda g: g.reshape((group_count, PIECE, -1, WIDTH)).transpose((0, 2, 1, 3))
    tall = lambda g: g.reshape((group_count, -1, PIECE, WIDTH))
    join = lambda g: g.transpose((0, 2, 1, 3)).reshape((channels, -1))
    blank = jnp.pad(matrix(got[0]), ((0, 0), (0, WIDTH - 256))).reshape((group_count, 1, PIECE, WIDTH))
    extra = cut(up0)
    first, extra = jnp.concatenate([blank, extra[:, :2]], axis=1), extra[:, 2:]
    third = cut(mixin)
    mixed = jnp.concatenate([cut(mixout), cut(convin)], axis=1)
    fourth = jnp.concatenate([cut(convout), cut(up1), tall(down1)], axis=1)
    made = front(
        None, seq_offsets, seq_counts, frames, [table, bias], [first, extra, tall(down0), third, mixed], hidden
    )
    h0, x1, v, y, gated, x2, p, u, w, stat, table, bias, *mixing = made
    pool = exchange(n_dp, n_fs, stat, frames_dev, 2, pool_kernel)
    scale = lax.rsqrt(pool[1:2] / (frames_dev * devices) + EPSILON)
    stat = jnp.concatenate([pool[0:1], scale, jnp.zeros((6, channels), F32)])
    result, gx3, gnb, grads, gbias1, gvec1, stat = middle(
        None, x2, w, cotangent, fourth, bias, table, stat, hidden
    )
    sums = exchange(n_dp, n_fs, gvec1, 1, 4, total_kernel)[6:8]
    sums = sums * (table[5:6] / (frames_dev * devices))
    stat = jnp.concatenate([stat[0:2], sums[1:2], sums[0:1], stat[4:8]])
    gx1, grads2, gvec2, gtaps, gmap, gdecay, grads3 = back(
        None,
        seq_offsets,
        seq_counts,
        [w, gnb, p, x2, gx3, gated, y, v, x1],
        [u] + mixing + [third, mixed, table, stat],
    )
    gx, gvec3, gbias0, gup0, gdown0 = tail(None, frames, h0, gx1, first, extra, tall(down0), table)

    def weights_of(log_rate, maps):
        log_decay = -jnp.exp(log_rate)
        root = jnp.sqrt(-jnp.expm1(2.0 * log_decay))
        return jnp.exp(log_decay), maps[0] * root * maps[1]

    rate, maps = unpack_table(table)[4:]
    rate_grad, map_grad = jax.vjp(weights_of, rate, maps)[1]((gdecay, gmap))
    gain_grad = jnp.stack([gvec3[1], gvec2[6], gvec2[2], gvec1[3], gvec1[0], gvec1[6]])
    rows = [gvec3[2], gvec2[7], gvec2[3], gvec1[4], gvec1[1], gvec1[7], gvec3[0], gvec1[2]]
    rows += [gvec2[4], gvec2[0], gvec2[1], gvec2[5]]
    small_grad = pack_table(
        gain_grad, jnp.stack(rows), gvec1[5], gtaps[:TAPS], rate_grad, map_grad
    )
    bias_grad = jnp.concatenate([gbias0[:8], gbias1[0].reshape((8, CHUNK))])
    wide = lambda g: g.reshape((devices, g.shape[0] // devices, g.shape[1]))
    reduced = scatter_all(
        n_dp,
        n_fs,
        [
            wide(join(grads[:, 1:5])),
            wide(matrix(grads[:, 5:9])),
            wide(join(grads[:, 0:1])),
            wide(join(grads3[:, 1:3])),
            wide(join(grads3[:, 0:1])),
            wide(join(grads2[:, 0:2])),
            wide(join(gup0)),
            wide(matrix(gdown0)),
            wide(small_grad.astype(BF16)),
            jnp.broadcast_to(bias_grad.astype(BF16), (devices, PIECE, CHUNK)),
        ],
        5,
    )
    gains_grad, shifts_grad, conv_bias_grad, taps_grad, rate_grad, map_grad = unpack_table(
        reduced[8].T
    )
    bias_grad = reduced[9].reshape((2, -1))
    count = bias_grad.shape[1] // devices
    bias_grad = lax.dynamic_slice(bias_grad, (0, mine * count), (2, count))
    return (
        result,
        gx,
        jnp.stack([reduced[6], reduced[0]]),
        jnp.stack([reduced[7], reduced[1]]),
        bias_grad,
        reduced[5],
        reduced[4],
        reduced[3],
        reduced[2],
        conv_bias_grad,
        rate_grad,
        map_grad,
        taps_grad,
        gains_grad,
        shifts_grad,
    )


def solution(mesh):
    both = ("dp", "fsdp")
    row, row1 = P(both, None), P(both)
    col, col3, mid = P(None, both), P(None, None, both), P(None, both, None)
    in_specs = (
        row,
        row,
        row,
        row1,
        mid,
        mid,
        col,
        row,
        row,
        row,
        row,
        row1,
        col,
        col3,
        col,
        col,
        col,
        row,
    )
    out_specs = (row, row, mid, mid, col, row, row, row, row, row1, col, col3, col, col, col)
    return jax.shard_map(
        partial(on_device, mesh.shape["dp"], mesh.shape["fsdp"]),
        mesh=mesh,
        in_specs=in_specs,
        out_specs=out_specs,
        check_vma=False,
    )
```
